32 devices in a mesh: tile: 8 (over z, x), zslab: 4 (over y, core).
Axes of the slice: x: 2, y: 2, z: 4, core: 2. Of those that a mesh axis runs over, the one named last changes fastest.
Arguments:
- band: bfloat16 [8, 4, 128, 64, 512], P('tile', None, 'zslab'), may hold values from -6 to 6
- pairs: int32 [16, 4], replicated, may hold values from 0 to 7, as said below
- extents: int32 [16, 2], replicated, may hold values from 32 to 512, as said below
Outputs:
- maps: float32 [16, 128, 32, 256], P('tile', 'zslab')
The draws below stay inside these ranges and needn't reach their ends.
Inputs may be any that keep to these rules, and one draw needn't show every extreme that they name: `pairs`: every slot (tile, face) with tile < 8 and face < 4 is named by exactly one pair, and a pair names two different slots. `extents`: column 0 lies in 32 to 64, column 1 in 256 to 512; some pair has both at their most.
All inputs are finite; a program needn't handle non-finite values.
Results may differ from the reference program's by a relative error of at most 0.012.
The reference program's roundings to bfloat16 on the way count: a program that leaves them out, or rounds other values in their place, can miss the bound.
Values may be sent and summed in bfloat16 or wider, within the bound.
No kernel may reach another device: no remote copies, remote signals or barrier semaphores. Data moves between devices by JAX's collectives and lax.ppermute only.
A program may use at most 64 MiB of HBM per device.

```python
import math
import jax
import jax.numpy as jnp
from jax import lax

GX = 32
GY = 256
GZ = 128
FACES = 4
TILES = 8
PAIRS = 16


def draw_pairs(key, part):
    grid_cols = 4
    grid_rows = TILES // grid_cols
    tile_order = jax.random.permutation(jax.random.fold_in(key, 11), TILES).astype(jnp.int32)
    places = jnp.arange(TILES, dtype=jnp.int32)
    grid_row = places // grid_cols
    grid_col = places % grid_cols
    eastern = grid_row * grid_cols + (grid_col + 1) % grid_cols
    southern = (grid_row + 1) % grid_rows * grid_cols + grid_col
    blank = jnp.zeros((TILES,), jnp.int32)
    first_rows = jnp.stack([tile_order, blank, tile_order[eastern], blank + 1], axis=1)
    second_tile_rows = jnp.stack([tile_order, blank + 2, tile_order[southern], blank + 3], axis=1)
    listing = jnp.concatenate([first_rows, second_tile_rows], axis=0)
    shuffle = jax.random.permutation(jax.random.fold_in(key, 12), PAIRS)
    return listing[shuffle].astype(jnp.int32)


def draw_extents(key, part):
    across = jax.random.randint(jax.random.fold_in(key, 21), (PAIRS,), GX, 2 * GX + 1).astype(jnp.int32)
    along = jax.random.randint(jax.random.fold_in(key, 22), (PAIRS,), GY, 2 * GY + 1).astype(jnp.int32)
    across = across.at[0].set(2 * GX).at[1].set(GX)
    along = along.at[0].set(2 * GY).at[1].set(GY)
    return jnp.stack([across, along], axis=1).astype(jnp.int32)


def block_levels(key, extent, shards, low, high):
    def one(axis_at, parts):
        draws = jax.random.uniform(jax.random.fold_in(jax.random.fold_in(key, 6), axis_at), (parts,), jnp.float32, low / len(shards), high / len(shards))
        return jnp.repeat(jnp.exp(draws), extent[axis_at] // parts).reshape((-1,) + (1,) * (len(extent) - axis_at - 1))

    factor_of = one(*shards[0])
    for cut in shards[1:]:
        factor_of = factor_of * one(*cut)
    return factor_of


def noise(own_key, shape, scale, bound, cuts=(), kind=jnp.bfloat16):
    factor_of = block_levels(own_key, shape, cuts, -0.22, 0.18) if cuts else 1.0
    result = jax.random.normal(own_key, shape, jnp.float32) * scale * factor_of
    return jnp.minimum(jnp.maximum(result, -bound), bound).astype(kind)


def setup_inputs(seed: int = 0) -> dict:
    key_of = jax.random.split(jax.random.key(seed), 4)
    return {
        "band": noise(key_of[0], (TILES, FACES, GZ, 2 * GX, 2 * GY), 1.0, 6.0, ((0, 8), (2, 4))),
        "pairs": draw_pairs(jax.random.fold_in(key_of[3], 71), 0),
        "extents": draw_extents(jax.random.fold_in(key_of[3], 71), 0),
    }


def dft_tables(length):
    indices = jnp.arange(length, dtype=jnp.int32)
    modular = indices[:, None] * indices[None, :] % length
    angles = modular.astype(jnp.float32) * (2.0 * math.pi / length)
    factor = 1.0 / math.sqrt(length)
    return ((jnp.cos(angles) * factor).astype(jnp.bfloat16), (jnp.sin(angles) * factor).astype(jnp.bfloat16))

def contract(form, left, right):
    return jnp.einsum(form, left.astype(jnp.float32), right.astype(jnp.float32))

def reduce_resolution(image_volume, crop_bounds):
    row_mask = (jnp.arange(image_volume.shape[2], dtype=jnp.int32)[None, :] < crop_bounds[:, 0:1]).astype(jnp.float32)
    col_mask = (jnp.arange(image_volume.shape[3], dtype=jnp.int32)[None, :] < crop_bounds[:, 1:2]).astype(jnp.float32)
    masked = image_volume.astype(jnp.float32) * row_mask[:, None, :, None] * col_mask[:, None, None, :]
    shaped = masked.reshape(image_volume.shape[0], image_volume.shape[1], GX, 2, GY, 2)
    return (0.5 * lax.optimization_barrier(jnp.sum(shaped, axis=(3, 5)))).astype(jnp.bfloat16)

def reference(band, pairs, extents):
    tables_x = dft_tables(GX)
    tables_y = dft_tables(GY)
    tables_z = dft_tables(GZ)
    first_slot = pairs[:, 0] * FACES + pairs[:, 1]
    second_slot = pairs[:, 2] * FACES + pairs[:, 3]
    slot_ext = jnp.zeros((TILES * FACES, 2), jnp.int32).at[first_slot].set(extents).at[second_slot].set(extents)
    slot_ext = slot_ext.reshape(TILES, FACES, 2)

    def forward(einsum_inputs):
        reduced_volume = reduce_resolution(einsum_inputs[0], einsum_inputs[1])
        y_re = contract('fzxy,yk->fzxk', reduced_volume, tables_y[0]).astype(jnp.bfloat16)
        y_im = (-contract('fzxy,yk->fzxk', reduced_volume, tables_y[1])).astype(jnp.bfloat16)
        x_re = (contract('fzxk,xj->fzjk', y_re, tables_x[0]) + contract('fzxk,xj->fzjk', y_im, tables_x[1])).astype(jnp.bfloat16)
        x_im = (contract('fzxk,xj->fzjk', y_im, tables_x[0]) - contract('fzxk,xj->fzjk', y_re, tables_x[1])).astype(jnp.bfloat16)
        z_re = (contract('fzjk,zm->fmjk', x_re, tables_z[0]) + contract('fzjk,zm->fmjk', x_im, tables_z[1])).astype(jnp.bfloat16)
        z_im = (contract('fzjk,zm->fmjk', x_im, tables_z[0]) - contract('fzjk,zm->fmjk', x_re, tables_z[1])).astype(jnp.bfloat16)
        return (z_re, z_im)
    spec_re, spec_im = lax.map(forward, (band, slot_ext))

    def correlate(entry):
        first_re = spec_re[entry[0], entry[1]].astype(jnp.float32)
        first_im = spec_im[entry[0], entry[1]].astype(jnp.float32)
        second_re = spec_re[entry[2], entry[3]].astype(jnp.float32)
        second_im = spec_im[entry[2], entry[3]].astype(jnp.float32)
        cross_re = first_re * second_re + first_im * second_im
        cross_im = first_im * second_re - first_re * second_im
        scaled = jnp.sqrt(cross_re * cross_re + cross_im * cross_im + 1.0)
        phase_real_part = (cross_re / scaled).astype(jnp.bfloat16)
        phase_im = (cross_im / scaled).astype(jnp.bfloat16)
        w_re = (contract('mjk,mz->zjk', phase_real_part, tables_z[0]) - contract('mjk,mz->zjk', phase_im, tables_z[1])).astype(jnp.bfloat16)
        w_im = (contract('mjk,mz->zjk', phase_im, tables_z[0]) + contract('mjk,mz->zjk', phase_real_part, tables_z[1])).astype(jnp.bfloat16)
        v_re = (contract('zjk,jx->zxk', w_re, tables_x[0]) - contract('zjk,jx->zxk', w_im, tables_x[1])).astype(jnp.bfloat16)
        v_im = (contract('zjk,jx->zxk', w_im, tables_x[0]) + contract('zjk,jx->zxk', w_re, tables_x[1])).astype(jnp.bfloat16)
        return contract('zxk,ky->zxy', v_re, tables_y[0]) - contract('zxk,ky->zxy', v_im, tables_y[1])
    return lax.map(correlate, pairs)
```

```python
import functools
import math


import jax
import jax.numpy as jnp
import numpy as np
from jax import lax
from jax.experimental import pallas as pl
from jax.experimental.pallas import tpu as pltpu
from jax.sharding import PartitionSpec as P

GX = 32
GY = 256
GZ = 128
FACES = 4


def dft_tables(length):
    indices = jnp.arange(length, dtype=jnp.int32)
    modular = indices[:, None] * indices[None, :] % length
    angles = modular.astype(jnp.float32) * (2.0 * math.pi / length)
    factor = 1.0 / math.sqrt(length)
    return (
        (jnp.cos(angles) * factor).astype(jnp.bfloat16),
        (jnp.sin(angles) * factor).astype(jnp.bfloat16),
    )


def product(form, left, right):
    return jnp.einsum(form, left, right, preferred_element_type=jnp.float32)


def reduce_resolution(image_volume, crop_bounds):
    row_mask = (
        jnp.arange(image_volume.shape[2], dtype=jnp.int32)[None, :] < crop_bounds[:, 0:1]
    ).astype(jnp.bfloat16)
    col_mask = (
        jnp.arange(image_volume.shape[3], dtype=jnp.int32)[None, :] < crop_bounds[:, 1:2]
    ).astype(jnp.bfloat16)
    masked = image_volume * row_mask[:, None, :, None] * col_mask[:, None, None, :]
    raw_cols = jnp.arange(image_volume.shape[3], dtype=jnp.int32)
    pooled_cols = jnp.arange(GY, dtype=jnp.int32)
    pooling = jnp.where(raw_cols[:, None] // 2 == pooled_cols[None, :], 0.5, 0.0).astype(
        jnp.bfloat16
    )
    along_pooled = product("szxy,yk->szxk", masked, pooling)
    shaped = along_pooled.reshape(image_volume.shape[0], image_volume.shape[1], GX, 2, GY)
    return (shaped[:, :, :, 0, :] + shaped[:, :, :, 1, :]).astype(jnp.bfloat16)


def cross_phase(owner_re, owner_im, pairs, tiles_here):
    first_dev = pairs[:, 0] // tiles_here
    first_pos = pairs[:, 0] % tiles_here * FACES + pairs[:, 1]
    second_tile_device = pairs[:, 2] // tiles_here
    second_pos = pairs[:, 2] % tiles_here * FACES + pairs[:, 3]
    first_re = owner_re[first_dev, :, first_pos].astype(jnp.float32)
    first_im = owner_im[first_dev, :, first_pos].astype(jnp.float32)
    second_re = owner_re[second_tile_device, :, second_pos].astype(jnp.float32)
    second_im = owner_im[second_tile_device, :, second_pos].astype(jnp.float32)
    cross_re = first_re * second_re + first_im * second_im
    cross_im = first_im * second_re - first_re * second_im
    scaled = jnp.sqrt(cross_re * cross_re + cross_im * cross_im + 1.0)
    return ((cross_re / scaled).astype(jnp.bfloat16), (cross_im / scaled).astype(jnp.bfloat16))


def inverse_z(phase_real_part, phase_im, tables_z):
    w_re = (
        product("pmjk,mz->pzjk", phase_real_part, tables_z[0])
        - product("pmjk,mz->pzjk", phase_im, tables_z[1])
    ).astype(jnp.bfloat16)
    w_im = (
        product("pmjk,mz->pzjk", phase_im, tables_z[0])
        + product("pmjk,mz->pzjk", phase_real_part, tables_z[1])
    ).astype(jnp.bfloat16)
    return (w_re, w_im)


def inverse_x(w_re, w_im, tables_x):
    v_re = (
        product("pzjk,jx->pzxk", w_re, tables_x[0]) - product("pzjk,jx->pzxk", w_im, tables_x[1])
    ).astype(jnp.bfloat16)
    v_im = (
        product("pzjk,jx->pzxk", w_im, tables_x[0]) + product("pzjk,jx->pzxk", w_re, tables_x[1])
    ).astype(jnp.bfloat16)
    return (v_re, v_im)


def general_shards(band, pairs, extents):
    tables_x = dft_tables(GX)
    tables_y = dft_tables(GY)
    tables_z = dft_tables(GZ)
    tiles_here = band.shape[0]
    slots = tiles_here * FACES
    zrows = band.shape[2]
    tile_pos = lax.axis_index("tile")
    global_slot = tile_pos * slots + jnp.arange(slots, dtype=jnp.int32)
    first_slot = pairs[:, 0] * FACES + pairs[:, 1]
    second_slot = pairs[:, 2] * FACES + pairs[:, 3]
    matches = (
        (first_slot[None, :] == global_slot[:, None])
        | (second_slot[None, :] == global_slot[:, None])
    ).astype(jnp.int32)
    crop_bounds = jnp.sum(matches[:, :, None] * extents[None, :, :], axis=1)
    image_volume = band.reshape(slots, zrows, 2 * GX, 2 * GY)
    reduced_volume = reduce_resolution(image_volume, crop_bounds)
    y_re = product("szxy,yk->szxk", reduced_volume, tables_y[0]).astype(jnp.bfloat16)
    y_im = (-product("szxy,yk->szxk", reduced_volume, tables_y[1])).astype(jnp.bfloat16)
    x_re = (
        product("szxk,xj->szjk", y_re, tables_x[0]) + product("szxk,xj->szjk", y_im, tables_x[1])
    ).astype(jnp.bfloat16)
    x_im = (
        product("szxk,xj->szjk", y_im, tables_x[0]) - product("szxk,xj->szjk", y_re, tables_x[1])
    ).astype(jnp.bfloat16)
    kx_part = GX // lax.axis_size("zslab")
    re_in = lax.all_to_all(x_re, "zslab", split_axis=2, concat_axis=1, tiled=True)
    im_in = lax.all_to_all(x_im, "zslab", split_axis=2, concat_axis=1, tiled=True)
    out_re = (
        product("szjk,zm->msjk", re_in, tables_z[0]) + product("szjk,zm->msjk", im_in, tables_z[1])
    ).astype(jnp.bfloat16)
    out_im = (
        product("szjk,zm->msjk", im_in, tables_z[0]) - product("szjk,zm->msjk", re_in, tables_z[1])
    ).astype(jnp.bfloat16)
    tile_count = lax.axis_size("tile")
    kz_part = GZ // tile_count
    spectra = (
        lax.all_to_all(out_re, "tile", split_axis=0, concat_axis=0, tiled=True),
        lax.all_to_all(out_im, "tile", split_axis=0, concat_axis=0, tiled=True),
    )
    owner_re = spectra[0].reshape(tile_count, kz_part, slots, kx_part, GY)
    owner_im = spectra[1].reshape(tile_count, kz_part, slots, kx_part, GY)
    phase_real_part, phase_im = cross_phase(owner_re, owner_im, pairs, tiles_here)
    returned = (
        lax.all_to_all(phase_real_part, "tile", split_axis=0, concat_axis=1, tiled=True),
        lax.all_to_all(phase_im, "tile", split_axis=0, concat_axis=1, tiled=True),
    )
    w_re, w_im = inverse_z(returned[0], returned[1], tables_z)
    v_re, v_im = inverse_x(
        lax.all_to_all(w_re, "zslab", split_axis=1, concat_axis=2, tiled=True),
        lax.all_to_all(w_im, "zslab", split_axis=1, concat_axis=2, tiled=True),
        tables_x,
    )
    return product("pzxk,ky->pzxy", v_re, tables_y[0]) - product("pzxk,ky->pzxy", v_im, tables_y[1])


HALF = GY // 2
ZTILE = 16
VMEM_BYTES = 56 * 1024 * 1024


def host_tables(length):
    indices = np.arange(length, dtype=np.int32)
    modular = indices[:, None] * indices[None, :] % length
    angles = modular.astype(np.float32) * np.float32(2.0 * math.pi / length)
    factor = np.float32(1.0 / math.sqrt(length))
    return (
        (np.cos(angles) * factor).astype(jnp.bfloat16),
        (np.sin(angles) * factor).astype(jnp.bfloat16),
    )


def pooling_table():
    raw = np.arange(2 * GY)[:, None] // 2
    return np.where(raw == np.arange(GY)[None, :], 0.5, 0.0).astype(jnp.bfloat16)


def half_y_table():
    cosine, sine = host_tables(GY)
    imag = -sine[:, :HALF]
    imag[:, 0] = cosine[:, HALF]
    return np.concatenate([cosine[:, :HALF], imag], axis=1)


def half_y_inverse():
    cosine, sine = host_tables(GY)
    two = np.array(2.0, jnp.bfloat16)
    real = cosine[:HALF, :] * two
    real[0] = cosine[0]
    imag = -sine[:HALF, :] * two
    imag[0] = cosine[HALF]
    return np.concatenate([real, imag], axis=0)


def spread_x(table):
    planes = np.eye(ZTILE, dtype=np.float32)
    grid = np.einsum("jx,az->jazx", table.astype(np.float32), planes)
    return grid.reshape(GX * ZTILE, ZTILE * GX).astype(jnp.bfloat16)


def forward_x_table():
    cosine, sine = (spread_x(table) for table in host_tables(GX))
    return np.block([[cosine, sine], [-sine, cosine]])


def inverse_x_table():
    return np.ascontiguousarray(forward_x_table().T)


def forward_z_table():
    cosine, sine = host_tables(GZ)
    return np.block([[cosine, sine], [-sine, cosine]])


def inverse_z_table():
    cosine, sine = host_tables(GZ)
    return np.block([[cosine, -sine], [sine, cosine]])


def dot(left, right):
    return jnp.dot(left, right, preferred_element_type=jnp.float32)


def analyse_kernel(
    slots, zrows, pairs_ref, extents_ref, where_ref, band_ref, pool_ref, wy_ref, wx_ref, out_ref, pooled_ref
):
    slot = where_ref[0] * slots + pl.program_id(0)
    across, along = jnp.int32(0), jnp.int32(0)
    for p in range(pairs_ref.shape[0]):
        first = pairs_ref[p, 0] * FACES + pairs_ref[p, 1]
        second = pairs_ref[p, 2] * FACES + pairs_ref[p, 3]
        named = (first == slot) | (second == slot)
        across = jnp.where(named, extents_ref[p, 0], across)
        along = jnp.where(named, extents_ref[p, 1], along)
    raw_col = lax.broadcasted_iota(jnp.int32, (2 * GY, GY), 0)
    pool = jnp.where(raw_col < along, pool_ref[...].astype(jnp.float32), 0.0).astype(jnp.bfloat16)
    rows = ZTILE * GX
    cell = lax.broadcasted_iota(jnp.int32, (rows, 128), 0) % GX
    even_live = 2 * cell < across
    odd_live = 2 * cell + 1 < across
    columns = []
    for part in range(zrows // ZTILE):
        raw = band_ref[0, 0, part * ZTILE : (part + 1) * ZTILE].reshape(2 * rows, 2 * GY)
        pooled = dot(raw, pool)
        halves = []
        for lane in range(GY // 128):
            pooled_ref[...] = pooled[:, lane * 128 : (lane + 1) * 128]
            even = jnp.where(even_live, pooled_ref[pl.ds(0, rows, stride=2), :], 0.0)
            odd = jnp.where(odd_live, pooled_ref[pl.ds(1, rows, stride=2), :], 0.0)
            halves.append((even + odd).astype(jnp.bfloat16))
        down = jnp.concatenate(halves, axis=1)
        columns.append(dot(down, wy_ref[...]).astype(jnp.bfloat16))
    stacked = jnp.concatenate(
        [
            jnp.concatenate([c[:, :HALF] for c in columns], axis=1),
            jnp.concatenate([c[:, HALF:] for c in columns], axis=1),
        ],
        axis=0,
    )
    real = dot(wx_ref[:rows, :], stacked)
    imag = dot(wx_ref[rows:, :], stacked)
    lane0 = lax.broadcasted_iota(jnp.int32, (ZTILE, HALF), 1) == 0
    for part in range(zrows // ZTILE):
        lanes = slice(part * HALF, (part + 1) * HALF)
        zs = slice(part * ZTILE, (part + 1) * ZTILE)

        def put(j, re, im):
            out_ref[j, 0, zs, 0:HALF] = re.astype(jnp.bfloat16)
            out_ref[j, 0, zs, HALF:] = im.astype(jnp.bfloat16)

        def at(j):
            block = slice(j * ZTILE, (j + 1) * ZTILE)
            return real[block, lanes], imag[block, lanes]

        for j in (0, GX // 2):
            put(j, *at(j))
        for j in range(1, GX // 2):
            re, im = at(j)
            re_m, im_m = at(GX - j)
            put(j, jnp.where(lane0, 0.5 * (re + re_m), re), jnp.where(lane0, 0.5 * (im - im_m), im))
            put(
                GX - j,
                jnp.where(lane0, 0.5 * (im + im_m), re_m),
                jnp.where(lane0, 0.5 * (re - re_m), im_m),
            )


def analyse(band, pairs, extents, place):
    slots, zrows = band.shape[0] * FACES, band.shape[2]
    tables = (pooling_table(), half_y_table(), forward_x_table())
    whole = [pl.BlockSpec(t.shape, lambda i, *_: (0, 0)) for t in tables]
    return pl.pallas_call(
        functools.partial(analyse_kernel, slots, zrows),
        grid_spec=pltpu.PrefetchScalarGridSpec(
            num_scalar_prefetch=3,
            grid=(slots,),
            in_specs=[
                pl.BlockSpec(
                    (1, 1, zrows, 2 * GX, 2 * GY), lambda i, *_: (i // FACES, i % FACES, 0, 0, 0)
                )
            ]
            + whole,
            out_specs=pl.BlockSpec((GX, 1, zrows, GY), lambda i, *_: (0, i, 0, 0)),
            scratch_shapes=[pltpu.VMEM((2 * ZTILE * GX, 128), jnp.float32)],
        ),
        out_shape=jax.ShapeDtypeStruct((GX, slots, zrows, GY), jnp.bfloat16),
        compiler_params=pltpu.CompilerParams(vmem_limit_bytes=VMEM_BYTES),
        name="analyse",
    )(pairs, extents, place, band, *(jnp.asarray(t) for t in tables))


def normalised(a_re, a_im, b_re, b_im):
    cross_re = a_re * b_re + a_im * b_im
    cross_im = a_im * b_re - a_re * b_im
    scale = lax.rsqrt(cross_re * cross_re + cross_im * cross_im + 1.0)
    return (cross_re * scale).astype(jnp.bfloat16), (cross_im * scale).astype(jnp.bfloat16)


def correlate_kernel(
    slabs, tiles_here, pairs_ref, place_ref, in_ref, wz_ref, wzi_ref, out_ref
):
    total = pairs_ref.shape[0]
    pairs_here = out_ref.shape[1]
    zrows = GZ // slabs
    both_real = (place_ref[0] == 0) | (place_ref[0] == GX // 2)
    lane = lax.broadcasted_iota(jnp.int32, (GZ, HALF), 1)
    lane0 = lane == 0

    def load(p, end, half):
        tile = pairs_ref[p, 2 * end]
        row = tile // tiles_here * slabs
        pos = tile % tiles_here * FACES + pairs_ref[p, 2 * end + 1]
        lanes = slice(half * HALF, (half + 1) * HALF)
        return jnp.concatenate([in_ref[row + s, pos, :, lanes] for s in range(slabs)], axis=0)

    def forward(re, im):
        spec = dot(wz_ref[...], jnp.concatenate([re, im], axis=0))
        return spec.astype(jnp.bfloat16).astype(jnp.float32)

    def phase_of(spec):
        return normalised(spec[:GZ, :HALF], spec[GZ:, :HALF], spec[:GZ, HALF:], spec[GZ:, HALF:])

    drop = lane0 & both_real
    for p in range(0, total, 2):
        phases = []
        for q in (p, p + 1):
            re = jnp.concatenate([load(q, 0, 0), load(q, 1, 0)], axis=1)
            im = jnp.concatenate(
                [
                    jnp.where(drop, 0.0, load(q, end, 1).astype(jnp.float32)).astype(jnp.bfloat16)
                    for end in (0, 1)
                ],
                axis=1,
            )
            phases.append(phase_of(forward(re, im)))
        stacked = jnp.concatenate(
            [
                jnp.concatenate([phases[0][0], phases[1][0]], axis=1),
                jnp.concatenate([phases[0][1], phases[1][1]], axis=1),
            ],
            axis=0,
        )
        w = dot(wzi_ref[...], stacked).astype(jnp.bfloat16)
        for k, q in enumerate((p, p + 1)):
            for half in (0, 1):
                plane = w[half * GZ : (half + 1) * GZ, k * HALF : (k + 1) * HALF]
                for s in range(slabs):
                    out_ref[
                        q // pairs_here * slabs + s,
                        q % pairs_here,
                        :,
                        half * HALF : (half + 1) * HALF,
                    ] = plane[s * zrows : (s + 1) * zrows]

    @pl.when(both_real)
    def _():
        first = jnp.zeros((GZ, HALF), jnp.float32)
        second = jnp.zeros((GZ, HALF), jnp.float32)
        for p in range(total):
            a = load(p, 0, 1).astype(jnp.float32)[:, 0:1]
            b = load(p, 1, 1).astype(jnp.float32)[:, 0:1]
            first = jnp.where(lane == p, a, first)
            second = jnp.where(lane == p, b, second)
        re = jnp.concatenate([first, second], axis=1).astype(jnp.bfloat16)
        phase = phase_of(forward(re, jnp.zeros_like(re)))
        w = dot(wzi_ref[...], jnp.concatenate(phase, axis=0))[:GZ]
        for p in range(total):
            column = w[:, p : p + 1]
            for s in range(slabs):
                at = (p // pairs_here * slabs + s, p % pairs_here, slice(None), slice(HALF, 2 * HALF))
                old = out_ref[at].astype(jnp.float32)
                rows = slice(s * zrows, (s + 1) * zrows)
                out_ref[at] = jnp.where(lane0[rows], column[rows], old).astype(jnp.bfloat16)


def correlate(spread, pairs, place, slabs, tiles_here):
    devices, _, zrows, _ = spread.shape
    pairs_here = pairs.shape[0] * slabs // devices
    tables = (forward_z_table(), inverse_z_table())
    vmem = pl.BlockSpec(memory_space=pltpu.VMEM)
    smem = pl.BlockSpec(memory_space=pltpu.SMEM)
    return pl.pallas_call(
        functools.partial(correlate_kernel, slabs, tiles_here),
        in_specs=[smem, smem, vmem, vmem, vmem],
        out_specs=vmem,
        out_shape=jax.ShapeDtypeStruct((devices, pairs_here, zrows, GY), jnp.bfloat16),
        compiler_params=pltpu.CompilerParams(vmem_limit_bytes=VMEM_BYTES),
        name="correlate",
    )(pairs, place, spread, *(jnp.asarray(t) for t in tables))


def synthesise_kernel(zrows, in_ref, wx_ref, wy_ref, out_ref):
    rows = ZTILE * GX
    parts = zrows // ZTILE
    lane0 = lax.broadcasted_iota(jnp.int32, (ZTILE, HALF), 1) == 0
    real, imag = [], []
    for part in range(parts):
        zs = slice(part * ZTILE, (part + 1) * ZTILE)

        def at(j):
            return (
                in_ref[j, 0, zs, 0:HALF].astype(jnp.float32),
                in_ref[j, 0, zs, HALF:].astype(jnp.float32),
            )

        blocks = [None] * GX
        for j in (0, GX // 2):
            blocks[j] = at(j)
        for j in range(1, GX // 2):
            re, im = at(j)
            re_m, im_m = at(GX - j)
            blocks[j] = (
                jnp.where(lane0, re + im_m, re),
                jnp.where(lane0, im + re_m, im),
            )
            blocks[GX - j] = (
                jnp.where(lane0, re - im_m, re_m),
                jnp.where(lane0, re_m - im, im_m),
            )
        real.append(jnp.concatenate([b[0].astype(jnp.bfloat16) for b in blocks], axis=0))
        imag.append(jnp.concatenate([b[1].astype(jnp.bfloat16) for b in blocks], axis=0))
    stacked = jnp.concatenate(
        [jnp.concatenate(real, axis=1), jnp.concatenate(imag, axis=1)], axis=0
    )
    v_re = dot(wx_ref[:rows, :], stacked).astype(jnp.bfloat16)
    v_im = dot(wx_ref[rows:, :], stacked).astype(jnp.bfloat16)
    for part in range(parts):
        lanes = slice(part * HALF, (part + 1) * HALF)
        v = jnp.concatenate([v_re[:, lanes], v_im[:, lanes]], axis=1)
        out_ref[0, part * ZTILE : (part + 1) * ZTILE] = dot(v, wy_ref[...]).reshape(ZTILE, GX, GY)


def synthesise(returned):
    _, pairs_here, zrows, _ = returned.shape
    tables = (inverse_x_table(), half_y_inverse())
    return pl.pallas_call(
        functools.partial(synthesise_kernel, zrows),
        grid=(pairs_here,),
        in_specs=[pl.BlockSpec((GX, 1, zrows, GY), lambda i: (0, i, 0, 0))]
        + [pl.BlockSpec(t.shape, lambda i: (0, 0)) for t in tables],
        out_specs=pl.BlockSpec((1, zrows, GX, GY), lambda i: (i, 0, 0, 0)),
        out_shape=jax.ShapeDtypeStruct((pairs_here, zrows, GX, GY), jnp.float32),
        compiler_params=pltpu.CompilerParams(vmem_limit_bytes=VMEM_BYTES),
        name="synthesise",
    )(returned, *(jnp.asarray(t) for t in tables))


def shards(band, pairs, extents):
    tiles, slabs = lax.axis_size("tile"), lax.axis_size("zslab")
    zrows = band.shape[2]
    if tiles * slabs != GX or zrows % ZTILE or pairs.shape[0] % (2 * tiles):
        return general_shards(band, pairs, extents)
    tile = lax.axis_index("tile").astype(jnp.int32)
    device = tile * slabs + lax.axis_index("zslab").astype(jnp.int32)
    spectra = analyse(band, pairs, extents, tile[None])
    spread = lax.all_to_all(spectra, ("tile", "zslab"), split_axis=0, concat_axis=0, tiled=True)
    w = correlate(spread, pairs, device[None], slabs, band.shape[0])
    returned = lax.all_to_all(w, ("tile", "zslab"), split_axis=0, concat_axis=0, tiled=True)
    return synthesise(returned)


def solution(mesh):
    placed = (P("tile", None, "zslab", None, None), P(), P())
    return jax.shard_map(
        shards,
        mesh=mesh,
        in_specs=placed,
        out_specs=P("tile", "zslab", None, None),
        check_vma=False,
    )
```

```python
import functools
import math


import jax
import jax.numpy as jnp
import numpy as np
from jax import lax
from jax.experimental import pallas as pl
from jax.experimental.pallas import tpu as pltpu
from jax.sharding import PartitionSpec as P

GX = 32
GY = 256
GZ = 128
FACES = 4


def dft_tables(length):
    indices = jnp.arange(length, dtype=jnp.int32)
    modular = indices[:, None] * indices[None, :] % length
    angles = modular.astype(jnp.float32) * (2.0 * math.pi / length)
    factor = 1.0 / math.sqrt(length)
    return (
        (jnp.cos(angles) * factor).astype(jnp.bfloat16),
        (jnp.sin(angles) * factor).astype(jnp.bfloat16),
    )


def product(form, left, right):
    return jnp.einsum(form, left, right, preferred_element_type=jnp.float32)


def reduce_resolution(image_volume, crop_bounds):
    row_mask = (
        jnp.arange(image_volume.shape[2], dtype=jnp.int32)[None, :] < crop_bounds[:, 0:1]
    ).astype(jnp.bfloat16)
    col_mask = (
        jnp.arange(image_volume.shape[3], dtype=jnp.int32)[None, :] < crop_bounds[:, 1:2]
    ).astype(jnp.bfloat16)
    masked = image_volume * row_mask[:, None, :, None] * col_mask[:, None, None, :]
    raw_cols = jnp.arange(image_volume.shape[3], dtype=jnp.int32)
    pooled_cols = jnp.arange(GY, dtype=jnp.int32)
    pooling = jnp.where(raw_cols[:, None] // 2 == pooled_cols[None, :], 0.5, 0.0).astype(
        jnp.bfloat16
    )
    along_pooled = product("szxy,yk->szxk", masked, pooling)
    shaped = along_pooled.reshape(image_volume.shape[0], image_volume.shape[1], GX, 2, GY)
    return (shaped[:, :, :, 0, :] + shaped[:, :, :, 1, :]).astype(jnp.bfloat16)


def cross_phase(owner_re, owner_im, pairs, tiles_here):
    first_dev = pairs[:, 0] // tiles_here
    first_pos = pairs[:, 0] % tiles_here * FACES + pairs[:, 1]
    second_tile_device = pairs[:, 2] // tiles_here
    second_pos = pairs[:, 2] % tiles_here * FACES + pairs[:, 3]
    first_re = owner_re[first_dev, :, first_pos].astype(jnp.float32)
    first_im = owner_im[first_dev, :, first_pos].astype(jnp.float32)
    second_re = owner_re[second_tile_device, :, second_pos].astype(jnp.float32)
    second_im = owner_im[second_tile_device, :, second_pos].astype(jnp.float32)
    cross_re = first_re * second_re + first_im * second_im
    cross_im = first_im * second_re - first_re * second_im
    scaled = jnp.sqrt(cross_re * cross_re + cross_im * cross_im + 1.0)
    return ((cross_re / scaled).astype(jnp.bfloat16), (cross_im / scaled).astype(jnp.bfloat16))


def inverse_z(phase_real_part, phase_im, tables_z):
    w_re = (
        product("pmjk,mz->pzjk", phase_real_part, tables_z[0])
        - product("pmjk,mz->pzjk", phase_im, tables_z[1])
    ).astype(jnp.bfloat16)
    w_im = (
        product("pmjk,mz->pzjk", phase_im, tables_z[0])
        + product("pmjk,mz->pzjk", phase_real_part, tables_z[1])
    ).astype(jnp.bfloat16)
    return (w_re, w_im)


def inverse_x(w_re, w_im, tables_x):
    v_re = (
        product("pzjk,jx->pzxk", w_re, tables_x[0]) - product("pzjk,jx->pzxk", w_im, tables_x[1])
    ).astype(jnp.bfloat16)
    v_im = (
        product("pzjk,jx->pzxk", w_im, tables_x[0]) + product("pzjk,jx->pzxk", w_re, tables_x[1])
    ).astype(jnp.bfloat16)
    return (v_re, v_im)


def general_shards(band, pairs, extents):
    tables_x = dft_tables(GX)
    tables_y = dft_tables(GY)
    tables_z = dft_tables(GZ)
    tiles_here = band.shape[0]
    slots = tiles_here * FACES
    zrows = band.shape[2]
    tile_pos = lax.axis_index("tile")
    global_slot = tile_pos * slots + jnp.arange(slots, dtype=jnp.int32)
    first_slot = pairs[:, 0] * FACES + pairs[:, 1]
    second_slot = pairs[:, 2] * FACES + pairs[:, 3]
    matches = (
        (first_slot[None, :] == global_slot[:, None])
        | (second_slot[None, :] == global_slot[:, None])
    ).astype(jnp.int32)
    crop_bounds = jnp.sum(matches[:, :, None] * extents[None, :, :], axis=1)
    image_volume = band.reshape(slots, zrows, 2 * GX, 2 * GY)
    reduced_volume = reduce_resolution(image_volume, crop_bounds)
    y_re = product("szxy,yk->szxk", reduced_volume, tables_y[0]).astype(jnp.bfloat16)
    y_im = (-product("szxy,yk->szxk", reduced_volume, tables_y[1])).astype(jnp.bfloat16)
    x_re = (
        product("szxk,xj->szjk", y_re, tables_x[0]) + product("szxk,xj->szjk", y_im, tables_x[1])
    ).astype(jnp.bfloat16)
    x_im = (
        product("szxk,xj->szjk", y_im, tables_x[0]) - product("szxk,xj->szjk", y_re, tables_x[1])
    ).astype(jnp.bfloat16)
    kx_part = GX // lax.axis_size("zslab")
    re_in = lax.all_to_all(x_re, "zslab", split_axis=2, concat_axis=1, tiled=True)
    im_in = lax.all_to_all(x_im, "zslab", split_axis=2, concat_axis=1, tiled=True)
    out_re = (
        product("szjk,zm->msjk", re_in, tables_z[0]) + product("szjk,zm->msjk", im_in, tables_z[1])
    ).astype(jnp.bfloat16)
    out_im = (
        product("szjk,zm->msjk", im_in, tables_z[0]) - product("szjk,zm->msjk", re_in, tables_z[1])
    ).astype(jnp.bfloat16)
    tile_count = lax.axis_size("tile")
    kz_part = GZ // tile_count
    spectra = (
        lax.all_to_all(out_re, "tile", split_axis=0, concat_axis=0, tiled=True),
        lax.all_to_all(out_im, "tile", split_axis=0, concat_axis=0, tiled=True),
    )
    owner_re = spectra[0].reshape(tile_count, kz_part, slots, kx_part, GY)
    owner_im = spectra[1].reshape(tile_count, kz_part, slots, kx_part, GY)
    phase_real_part, phase_im = cross_phase(owner_re, owner_im, pairs, tiles_here)
    returned = (
        lax.all_to_all(phase_real_part, "tile", split_axis=0, concat_axis=1, tiled=True),
        lax.all_to_all(phase_im, "tile", split_axis=0, concat_axis=1, tiled=True),
    )
    w_re, w_im = inverse_z(returned[0], returned[1], tables_z)
    v_re, v_im = inverse_x(
        lax.all_to_all(w_re, "zslab", split_axis=1, concat_axis=2, tiled=True),
        lax.all_to_all(w_im, "zslab", split_axis=1, concat_axis=2, tiled=True),
        tables_x,
    )
    return product("pzxk,ky->pzxy", v_re, tables_y[0]) - product("pzxk,ky->pzxy", v_im, tables_y[1])


HALF = GY // 2
ZTILE = 16
VMEM_BYTES = 56 * 1024 * 1024


def host_tables(length):
    indices = np.arange(length, dtype=np.int32)
    modular = indices[:, None] * indices[None, :] % length
    angles = modular.astype(np.float32) * np.float32(2.0 * math.pi / length)
    factor = np.float32(1.0 / math.sqrt(length))
    return (
        (np.cos(angles) * factor).astype(jnp.bfloat16),
        (np.sin(angles) * factor).astype(jnp.bfloat16),
    )


def pooling_table():
    raw = np.arange(2 * GY)[:, None] // 2
    return np.where(raw == np.arange(GY)[None, :], 0.5, 0.0).astype(jnp.bfloat16)


def half_y_table():
    cosine, sine = host_tables(GY)
    imag = -sine[:, :HALF]
    imag[:, 0] = cosine[:, HALF]
    return np.concatenate([cosine[:, :HALF], imag], axis=1)


def half_y_inverse():
    cosine, sine = host_tables(GY)
    two = np.array(2.0, jnp.bfloat16)
    real = cosine[:HALF, :] * two
    real[0] = cosine[0]
    imag = -sine[:HALF, :] * two
    imag[0] = cosine[HALF]
    return np.concatenate([real, imag], axis=0)


def spread_x(table):
    planes = np.eye(ZTILE, dtype=np.float32)
    grid = np.einsum("jx,az->jazx", table.astype(np.float32), planes)
    return grid.reshape(GX * ZTILE, ZTILE * GX).astype(jnp.bfloat16)


def forward_x_table():
    cosine, sine = (spread_x(table) for table in host_tables(GX))
    return np.block([[cosine, sine], [-sine, cosine]])


def inverse_x_table():
    return np.ascontiguousarray(forward_x_table().T)


def forward_z_table():
    cosine, sine = host_tables(GZ)
    return np.block([[cosine, sine], [-sine, cosine]])


def inverse_z_table():
    cosine, sine = host_tables(GZ)
    return np.block([[cosine, -sine], [sine, cosine]])


def dot(left, right):
    return jnp.dot(left, right, preferred_element_type=jnp.float32)


def analyse_kernel(
    slots, slabs, pairs_ref, extents_ref, where_ref, band_ref, pool_ref, wy_ref, wx_ref, *rest
):
    out_refs, (pooled_ref, spec_ref) = rest[:GX], rest[GX:]
    zrows = band_ref.shape[2]
    slot = where_ref[0] // slabs * slots + pl.program_id(0)
    across, along = jnp.int32(0), jnp.int32(0)
    for p in range(pairs_ref.shape[1]):
        first = pairs_ref[0, p] * FACES + pairs_ref[1, p]
        second = pairs_ref[2, p] * FACES + pairs_ref[3, p]
        named = (first == slot) | (second == slot)
        across = jnp.where(named, extents_ref[0, p], across)
        along = jnp.where(named, extents_ref[1, p], along)
    raw_col = lax.broadcasted_iota(jnp.int32, (2 * GY, GY), 0)
    pool = jnp.where(raw_col < along, pool_ref[...].astype(jnp.float32), 0.0).astype(jnp.bfloat16)
    rows = ZTILE * GX
    cell = lax.broadcasted_iota(jnp.int32, (rows, 128), 0) % GX
    even_live = 2 * cell < across
    odd_live = 2 * cell + 1 < across
    columns = []
    for part in range(zrows // ZTILE):
        raw = band_ref[0, 0, part * ZTILE : (part + 1) * ZTILE].reshape(2 * rows, 2 * GY)
        pooled = dot(raw, pool)
        halves = []
        for lane in range(GY // 128):
            pooled_ref[...] = pooled[:, lane * 128 : (lane + 1) * 128]
            even = jnp.where(even_live, pooled_ref[pl.ds(0, rows, stride=2), :], 0.0)
            odd = jnp.where(odd_live, pooled_ref[pl.ds(1, rows, stride=2), :], 0.0)
            halves.append((even + odd).astype(jnp.bfloat16))
        down = jnp.concatenate(halves, axis=1)
        columns.append(dot(down, wy_ref[...]).astype(jnp.bfloat16))
    stacked = jnp.concatenate(
        [
            jnp.concatenate([c[:, :HALF] for c in columns], axis=1),
            jnp.concatenate([c[:, HALF:] for c in columns], axis=1),
        ],
        axis=0,
    )
    real = dot(wx_ref[:rows, :], stacked)
    imag = dot(wx_ref[rows:, :], stacked)
    lane0 = lax.broadcasted_iota(jnp.int32, (ZTILE, HALF), 1) == 0
    for part in range(zrows // ZTILE):
        lanes = slice(part * HALF, (part + 1) * HALF)
        zs = slice(part * ZTILE, (part + 1) * ZTILE)

        def put(j, re, im):
            spec_ref[j, zs, 0:HALF] = re.astype(jnp.bfloat16)
            spec_ref[j, zs, HALF:] = im.astype(jnp.bfloat16)

        def at(j):
            block = slice(j * ZTILE, (j + 1) * ZTILE)
            return real[block, lanes], imag[block, lanes]

        for j in (0, GX // 2):
            put(j, *at(j))
        for j in range(1, GX // 2):
            re, im = at(j)
            re_m, im_m = at(GX - j)
            put(j, jnp.where(lane0, 0.5 * (re + re_m), re), jnp.where(lane0, 0.5 * (im - im_m), im))
            put(
                GX - j,
                jnp.where(lane0, 0.5 * (im + im_m), re_m),
                jnp.where(lane0, 0.5 * (re - re_m), im_m),
            )
    for i in range(GX):
        out_refs[i][0] = spec_ref[where_ref[0] ^ i]


def analyse(band, pairs, extents, place, slabs):
    slots, zrows = band.shape[0] * FACES, band.shape[2]
    tables = (pooling_table(), half_y_table(), forward_x_table())
    whole = [pl.BlockSpec(t.shape, lambda i, *_: (0, 0)) for t in tables]
    return pl.pallas_call(
        functools.partial(analyse_kernel, slots, slabs),
        grid_spec=pltpu.PrefetchScalarGridSpec(
            num_scalar_prefetch=3,
            grid=(slots,),
            in_specs=[
                pl.BlockSpec(
                    (1, 1, zrows, 2 * GX, 2 * GY), lambda i, *_: (i // FACES, i % FACES, 0, 0, 0)
                )
            ]
            + whole,
            out_specs=[pl.BlockSpec((1, zrows, GY), lambda i, *_: (i, 0, 0))] * GX,
            scratch_shapes=[
                pltpu.VMEM((2 * ZTILE * GX, 128), jnp.float32),
                pltpu.VMEM((GX, zrows, GY), jnp.bfloat16),
            ],
        ),
        out_shape=[jax.ShapeDtypeStruct((slots, zrows, GY), jnp.bfloat16)] * GX,
        compiler_params=pltpu.CompilerParams(vmem_limit_bytes=VMEM_BYTES),
        name="analyse",
    )(pairs, extents, place, band, *(jnp.asarray(t) for t in tables))


def normalised(a_re, a_im, b_re, b_im):
    cross_re = a_re * b_re + a_im * b_im
    cross_im = a_im * b_re - a_re * b_im
    scale = lax.rsqrt(cross_re * cross_re + cross_im * cross_im + 1.0)
    return (cross_re * scale).astype(jnp.bfloat16), (cross_im * scale).astype(jnp.bfloat16)


def correlate_kernel(
    slabs, tiles_here, pairs_here, pairs_ref, place_ref, wz_ref, wzi_ref, *rest
):
    in_refs, out_refs = rest[:GX], rest[GX : 2 * GX]
    in_ref, out_ref, sems = rest[2 * GX :]
    copies = [
        pltpu.make_async_copy(in_refs[i], in_ref.at[place_ref[0] ^ i], sems.at[i])
        for i in range(GX)
    ]
    for copy in copies:
        copy.start()
    for copy in copies:
        copy.wait()
    total = pairs_ref.shape[1]
    zrows = GZ // slabs
    both_real = (place_ref[0] == 0) | (place_ref[0] == GX // 2)
    lane = lax.broadcasted_iota(jnp.int32, (GZ, HALF), 1)
    lane0 = lane == 0

    def load(p, end, half):
        tile = pairs_ref[2 * end, p]
        row = tile // tiles_here * slabs
        pos = tile % tiles_here * FACES + pairs_ref[2 * end + 1, p]
        lanes = slice(half * HALF, (half + 1) * HALF)
        return jnp.concatenate([in_ref[row + s, pos, :, lanes] for s in range(slabs)], axis=0)

    def forward(re, im):
        spec = dot(wz_ref[...], jnp.concatenate([re, im], axis=0))
        return spec.astype(jnp.bfloat16).astype(jnp.float32)

    def phase_of(spec):
        return normalised(spec[:GZ, :HALF], spec[GZ:, :HALF], spec[:GZ, HALF:], spec[GZ:, HALF:])

    drop = lane0 & both_real
    for p in range(0, total, 2):
        phases = []
        for q in (p, p + 1):
            re = jnp.concatenate([load(q, 0, 0), load(q, 1, 0)], axis=1)
            im = jnp.concatenate(
                [
                    jnp.where(drop, 0.0, load(q, end, 1).astype(jnp.float32)).astype(jnp.bfloat16)
                    for end in (0, 1)
                ],
                axis=1,
            )
            phases.append(phase_of(forward(re, im)))
        stacked = jnp.concatenate(
            [
                jnp.concatenate([phases[0][0], phases[1][0]], axis=1),
                jnp.concatenate([phases[0][1], phases[1][1]], axis=1),
            ],
            axis=0,
        )
        w = dot(wzi_ref[...], stacked).astype(jnp.bfloat16)
        for k, q in enumerate((p, p + 1)):
            for half in (0, 1):
                plane = w[half * GZ : (half + 1) * GZ, k * HALF : (k + 1) * HALF]
                for s in range(slabs):
                    out_ref[
                        q // pairs_here * slabs + s,
                        q % pairs_here,
                        :,
                        half * HALF : (half + 1) * HALF,
                    ] = plane[s * zrows : (s + 1) * zrows]

    @pl.when(both_real)
    def _():
        first = jnp.zeros((GZ, HALF), jnp.float32)
        second = jnp.zeros((GZ, HALF), jnp.float32)
        for p in range(total):
            a = load(p, 0, 1).astype(jnp.float32)[:, 0:1]
            b = load(p, 1, 1).astype(jnp.float32)[:, 0:1]
            first = jnp.where(lane == p, a, first)
            second = jnp.where(lane == p, b, second)
        re = jnp.concatenate([first, second], axis=1).astype(jnp.bfloat16)
        phase = phase_of(forward(re, jnp.zeros_like(re)))
        w = dot(wzi_ref[...], jnp.concatenate(phase, axis=0))[:GZ]
        for p in range(total):
            column = w[:, p : p + 1]
            for s in range(slabs):
                at = (p // pairs_here * slabs + s, p % pairs_here, slice(None), slice(HALF, 2 * HALF))
                old = out_ref[at].astype(jnp.float32)
                rows = slice(s * zrows, (s + 1) * zrows)
                out_ref[at] = jnp.where(lane0[rows], column[rows], old).astype(jnp.bfloat16)

    for i in range(GX):
        out_refs[i][...] = out_ref[place_ref[0] ^ i]


def correlate(spread, pairs, place, slabs, tiles_here):
    slots, zrows, _ = spread[0].shape
    pairs_here = slots // 2
    tables = (forward_z_table(), inverse_z_table())
    vmem = pl.BlockSpec(memory_space=pltpu.VMEM)
    smem = pl.BlockSpec(memory_space=pltpu.SMEM)
    return pl.pallas_call(
        functools.partial(correlate_kernel, slabs, tiles_here, pairs_here),
        in_specs=[smem, smem, vmem, vmem] + [pl.BlockSpec(memory_space=pl.ANY)] * GX,
        out_specs=[vmem] * GX,
        out_shape=[jax.ShapeDtypeStruct((pairs_here, zrows, GY), jnp.bfloat16)] * GX,
        scratch_shapes=[
            pltpu.VMEM((GX, slots, zrows, GY), jnp.bfloat16),
            pltpu.VMEM((GX, pairs_here, zrows, GY), jnp.bfloat16),
            pltpu.SemaphoreType.DMA((GX,)),
        ],
        compiler_params=pltpu.CompilerParams(vmem_limit_bytes=VMEM_BYTES),
        name="correlate",
    )(pairs, place, *(jnp.asarray(t) for t in tables), *spread)


def synthesise_kernel(place_ref, wx_ref, wy_ref, *rest):
    in_refs, out_ref, in_ref = rest[:GX], rest[GX], rest[GX + 1]
    zrows = out_ref.shape[1]
    for i in range(GX):
        in_ref[place_ref[0] ^ i] = in_refs[i][...]
    rows = ZTILE * GX
    parts = zrows // ZTILE
    lane0 = lax.broadcasted_iota(jnp.int32, (ZTILE, HALF), 1) == 0
    real, imag = [], []
    for part in range(parts):
        zs = slice(part * ZTILE, (part + 1) * ZTILE)

        def at(j):
            return (
                in_ref[j, 0, zs, 0:HALF].astype(jnp.float32),
                in_ref[j, 0, zs, HALF:].astype(jnp.float32),
            )

        blocks = [None] * GX
        for j in (0, GX // 2):
            blocks[j] = at(j)
        for j in range(1, GX // 2):
            re, im = at(j)
            re_m, im_m = at(GX - j)
            blocks[j] = (
                jnp.where(lane0, re + im_m, re),
                jnp.where(lane0, im + re_m, im),
            )
            blocks[GX - j] = (
                jnp.where(lane0, re - im_m, re_m),
                jnp.where(lane0, re_m - im, im_m),
            )
        real.append(jnp.concatenate([b[0].astype(jnp.bfloat16) for b in blocks], axis=0))
        imag.append(jnp.concatenate([b[1].astype(jnp.bfloat16) for b in blocks], axis=0))
    stacked = jnp.concatenate(
        [jnp.concatenate(real, axis=1), jnp.concatenate(imag, axis=1)], axis=0
    )
    v_re = dot(wx_ref[:rows, :], stacked).astype(jnp.bfloat16)
    v_im = dot(wx_ref[rows:, :], stacked).astype(jnp.bfloat16)
    for part in range(parts):
        lanes = slice(part * HALF, (part + 1) * HALF)
        v = jnp.concatenate([v_re[:, lanes], v_im[:, lanes]], axis=1)
        out_ref[0, part * ZTILE : (part + 1) * ZTILE] = dot(v, wy_ref[...]).reshape(ZTILE, GX, GY)


def synthesise(returned, place):
    pairs_here, zrows, _ = returned[0].shape
    tables = (inverse_x_table(), half_y_inverse())
    return pl.pallas_call(
        synthesise_kernel,
        grid_spec=pltpu.PrefetchScalarGridSpec(
            num_scalar_prefetch=1,
            grid=(pairs_here,),
            in_specs=[pl.BlockSpec(t.shape, lambda i, *_: (0, 0)) for t in tables]
            + [pl.BlockSpec((1, zrows, GY), lambda i, *_: (i, 0, 0))] * GX,
            out_specs=pl.BlockSpec((1, zrows, GX, GY), lambda i, *_: (i, 0, 0, 0)),
            scratch_shapes=[pltpu.VMEM((GX, 1, zrows, GY), jnp.bfloat16)],
        ),
        out_shape=jax.ShapeDtypeStruct((pairs_here, zrows, GX, GY), jnp.float32),
        compiler_params=pltpu.CompilerParams(vmem_limit_bytes=VMEM_BYTES),
        name="synthesise",
    )(place, *(jnp.asarray(t) for t in tables), *returned)


def exchange(blocks):
    count = len(blocks)
    return [blocks[0]] + [
        lax.ppermute(blocks[i], ("tile", "zslab"), [(s, s ^ i) for s in range(count)])
        for i in range(1, count)
    ]


def shards(band, pairs, extents):
    tiles, slabs = lax.axis_size("tile"), lax.axis_size("zslab")
    zrows = band.shape[2]
    if tiles * slabs != GX or zrows % ZTILE or pairs.shape[0] % (2 * tiles):
        return general_shards(band, pairs, extents)
    place = (lax.axis_index("tile") * slabs + lax.axis_index("zslab")).astype(jnp.int32)[None]
    spectra = analyse(band, pairs.T, extents.T, place, slabs)
    w = correlate(exchange(spectra), pairs.T, place, slabs, band.shape[0])
    return synthesise(exchange(w), place)


def solution(mesh):
    placed = (P("tile", None, "zslab", None, None), P(), P())
    return jax.shard_map(
        shards,
        mesh=mesh,
        in_specs=placed,
        out_specs=P("tile", "zslab", None, None),
        check_vma=False,
    )
```

```python
import functools
import math


import jax
import jax.numpy as jnp
import numpy as np
from jax import lax
from jax.experimental import pallas as pl
from jax.experimental.pallas import tpu as pltpu
from jax.sharding import PartitionSpec as P

GX = 32
GY = 256
GZ = 128
FACES = 4


def dft_tables(length):
    indices = jnp.arange(length, dtype=jnp.int32)
    modular = indices[:, None] * indices[None, :] % length
    angles = modular.astype(jnp.float32) * (2.0 * math.pi / length)
    factor = 1.0 / math.sqrt(length)
    return (
        (jnp.cos(angles) * factor).astype(jnp.bfloat16),
        (jnp.sin(angles) * factor).astype(jnp.bfloat16),
    )


def product(form, left, right):
    return jnp.einsum(form, left, right, preferred_element_type=jnp.float32)


def reduce_resolution(image_volume, crop_bounds):
    row_mask = (
        jnp.arange(image_volume.shape[2], dtype=jnp.int32)[None, :] < crop_bounds[:, 0:1]
    ).astype(jnp.bfloat16)
    col_mask = (
        jnp.arange(image_volume.shape[3], dtype=jnp.int32)[None, :] < crop_bounds[:, 1:2]
    ).astype(jnp.bfloat16)
    masked = image_volume * row_mask[:, None, :, None] * col_mask[:, None, None, :]
    raw_cols = jnp.arange(image_volume.shape[3], dtype=jnp.int32)
    pooled_cols = jnp.arange(GY, dtype=jnp.int32)
    pooling = jnp.where(raw_cols[:, None] // 2 == pooled_cols[None, :], 0.5, 0.0).astype(
        jnp.bfloat16
    )
    along_pooled = product("szxy,yk->szxk", masked, pooling)
    shaped = along_pooled.reshape(image_volume.shape[0], image_volume.shape[1], GX, 2, GY)
    return (shaped[:, :, :, 0, :] + shaped[:, :, :, 1, :]).astype(jnp.bfloat16)


def cross_phase(owner_re, owner_im, pairs, tiles_here):
    first_dev = pairs[:, 0] // tiles_here
    first_pos = pairs[:, 0] % tiles_here * FACES + pairs[:, 1]
    second_tile_device = pairs[:, 2] // tiles_here
    second_pos = pairs[:, 2] % tiles_here * FACES + pairs[:, 3]
    first_re = owner_re[first_dev, :, first_pos].astype(jnp.float32)
    first_im = owner_im[first_dev, :, first_pos].astype(jnp.float32)
    second_re = owner_re[second_tile_device, :, second_pos].astype(jnp.float32)
    second_im = owner_im[second_tile_device, :, second_pos].astype(jnp.float32)
    cross_re = first_re * second_re + first_im * second_im
    cross_im = first_im * second_re - first_re * second_im
    scaled = jnp.sqrt(cross_re * cross_re + cross_im * cross_im + 1.0)
    return ((cross_re / scaled).astype(jnp.bfloat16), (cross_im / scaled).astype(jnp.bfloat16))


def inverse_z(phase_real_part, phase_im, tables_z):
    w_re = (
        product("pmjk,mz->pzjk", phase_real_part, tables_z[0])
        - product("pmjk,mz->pzjk", phase_im, tables_z[1])
    ).astype(jnp.bfloat16)
    w_im = (
        product("pmjk,mz->pzjk", phase_im, tables_z[0])
        + product("pmjk,mz->pzjk", phase_real_part, tables_z[1])
    ).astype(jnp.bfloat16)
    return (w_re, w_im)


def inverse_x(w_re, w_im, tables_x):
    v_re = (
        product("pzjk,jx->pzxk", w_re, tables_x[0]) - product("pzjk,jx->pzxk", w_im, tables_x[1])
    ).astype(jnp.bfloat16)
    v_im = (
        product("pzjk,jx->pzxk", w_im, tables_x[0]) + product("pzjk,jx->pzxk", w_re, tables_x[1])
    ).astype(jnp.bfloat16)
    return (v_re, v_im)


def general_shards(band, pairs, extents):
    tables_x = dft_tables(GX)
    tables_y = dft_tables(GY)
    tables_z = dft_tables(GZ)
    tiles_here = band.shape[0]
    slots = tiles_here * FACES
    zrows = band.shape[2]
    tile_pos = lax.axis_index("tile")
    global_slot = tile_pos * slots + jnp.arange(slots, dtype=jnp.int32)
    first_slot = pairs[:, 0] * FACES + pairs[:, 1]
    second_slot = pairs[:, 2] * FACES + pairs[:, 3]
    matches = (
        (first_slot[None, :] == global_slot[:, None])
        | (second_slot[None, :] == global_slot[:, None])
    ).astype(jnp.int32)
    crop_bounds = jnp.sum(matches[:, :, None] * extents[None, :, :], axis=1)
    image_volume = band.reshape(slots, zrows, 2 * GX, 2 * GY)
    reduced_volume = reduce_resolution(image_volume, crop_bounds)
    y_re = product("szxy,yk->szxk", reduced_volume, tables_y[0]).astype(jnp.bfloat16)
    y_im = (-product("szxy,yk->szxk", reduced_volume, tables_y[1])).astype(jnp.bfloat16)
    x_re = (
        product("szxk,xj->szjk", y_re, tables_x[0]) + product("szxk,xj->szjk", y_im, tables_x[1])
    ).astype(jnp.bfloat16)
    x_im = (
        product("szxk,xj->szjk", y_im, tables_x[0]) - product("szxk,xj->szjk", y_re, tables_x[1])
    ).astype(jnp.bfloat16)
    kx_part = GX // lax.axis_size("zslab")
    re_in = lax.all_to_all(x_re, "zslab", split_axis=2, concat_axis=1, tiled=True)
    im_in = lax.all_to_all(x_im, "zslab", split_axis=2, concat_axis=1, tiled=True)
    out_re = (
        product("szjk,zm->msjk", re_in, tables_z[0]) + product("szjk,zm->msjk", im_in, tables_z[1])
    ).astype(jnp.bfloat16)
    out_im = (
        product("szjk,zm->msjk", im_in, tables_z[0]) - product("szjk,zm->msjk", re_in, tables_z[1])
    ).astype(jnp.bfloat16)
    tile_count = lax.axis_size("tile")
    kz_part = GZ // tile_count
    spectra = (
        lax.all_to_all(out_re, "tile", split_axis=0, concat_axis=0, tiled=True),
        lax.all_to_all(out_im, "tile", split_axis=0, concat_axis=0, tiled=True),
    )
    owner_re = spectra[0].reshape(tile_count, kz_part, slots, kx_part, GY)
    owner_im = spectra[1].reshape(tile_count, kz_part, slots, kx_part, GY)
    phase_real_part, phase_im = cross_phase(owner_re, owner_im, pairs, tiles_here)
    returned = (
        lax.all_to_all(phase_real_part, "tile", split_axis=0, concat_axis=1, tiled=True),
        lax.all_to_all(phase_im, "tile", split_axis=0, concat_axis=1, tiled=True),
    )
    w_re, w_im = inverse_z(returned[0], returned[1], tables_z)
    v_re, v_im = inverse_x(
        lax.all_to_all(w_re, "zslab", split_axis=1, concat_axis=2, tiled=True),
        lax.all_to_all(w_im, "zslab", split_axis=1, concat_axis=2, tiled=True),
        tables_x,
    )
    return product("pzxk,ky->pzxy", v_re, tables_y[0]) - product("pzxk,ky->pzxy", v_im, tables_y[1])


HALF = GY // 2
ZTILE = 16
VMEM_BYTES = 56 * 1024 * 1024


def host_tables(length):
    indices = np.arange(length, dtype=np.int32)
    modular = indices[:, None] * indices[None, :] % length
    angles = modular.astype(np.float32) * np.float32(2.0 * math.pi / length)
    factor = np.float32(1.0 / math.sqrt(length))
    return (
        (np.cos(angles) * factor).astype(jnp.bfloat16),
        (np.sin(angles) * factor).astype(jnp.bfloat16),
    )


def pooling_table():
    raw = np.arange(2 * GY)[:, None] // 2
    return np.where(raw == np.arange(GY)[None, :], 0.5, 0.0).astype(jnp.bfloat16)


def half_y_table():
    cosine, sine = host_tables(GY)
    imag = -sine[:, :HALF]
    imag[:, 0] = cosine[:, HALF]
    return np.concatenate([cosine[:, :HALF], imag], axis=1)


def half_y_inverse():
    cosine, sine = host_tables(GY)
    two = np.array(2.0, jnp.bfloat16)
    real = cosine[:HALF, :] * two
    real[0] = cosine[0]
    imag = -sine[:HALF, :] * two
    imag[0] = cosine[HALF]
    return np.concatenate([real, imag], axis=0)


def spread_x(table):
    planes = np.eye(ZTILE, dtype=np.float32)
    grid = np.einsum("jx,az->jazx", table.astype(np.float32), planes)
    return grid.reshape(GX * ZTILE, ZTILE * GX).astype(jnp.bfloat16)


def forward_x_table():
    cosine, sine = (spread_x(table) for table in host_tables(GX))
    return np.block([[cosine, sine], [-sine, cosine]])


def inverse_x_table():
    return np.ascontiguousarray(forward_x_table().T)


def forward_z_table():
    cosine, sine = host_tables(GZ)
    return np.block([[cosine, sine], [-sine, cosine]])


def inverse_z_table():
    cosine, sine = host_tables(GZ)
    return np.block([[cosine, -sine], [sine, cosine]])


def dot(left, right):
    return jnp.dot(left, right, preferred_element_type=jnp.float32)


def analyse_kernel(
    slots, zrows, pairs_ref, extents_ref, where_ref, band_ref, pool_ref, wy_ref, wx_ref, out_ref, pooled_ref
):
    slot = where_ref[0] * slots + pl.program_id(0)
    across, along = jnp.int32(0), jnp.int32(0)
    for p in range(pairs_ref.shape[1]):
        first = pairs_ref[0, p] * FACES + pairs_ref[1, p]
        second = pairs_ref[2, p] * FACES + pairs_ref[3, p]
        named = (first == slot) | (second == slot)
        across = jnp.where(named, extents_ref[0, p], across)
        along = jnp.where(named, extents_ref[1, p], along)
    raw_col = lax.broadcasted_iota(jnp.int32, (2 * GY, GY), 0)
    pool = jnp.where(raw_col < along, pool_ref[...].astype(jnp.float32), 0.0).astype(jnp.bfloat16)
    rows = ZTILE * GX
    cell = lax.broadcasted_iota(jnp.int32, (rows, 128), 0) % GX
    even_live = 2 * cell < across
    odd_live = 2 * cell + 1 < across
    columns = []
    for part in range(zrows // ZTILE):
        raw = band_ref[0, 0, part * ZTILE : (part + 1) * ZTILE].reshape(2 * rows, 2 * GY)
        pooled = dot(raw, pool)
        halves = []
        for lane in range(GY // 128):
            pooled_ref[...] = pooled[:, lane * 128 : (lane + 1) * 128]
            even = jnp.where(even_live, pooled_ref[pl.ds(0, rows, stride=2), :], 0.0)
            odd = jnp.where(odd_live, pooled_ref[pl.ds(1, rows, stride=2), :], 0.0)
            halves.append((even + odd).astype(jnp.bfloat16))
        down = jnp.concatenate(halves, axis=1)
        columns.append(dot(down, wy_ref[...]).astype(jnp.bfloat16))
    stacked = jnp.concatenate(
        [
            jnp.concatenate([c[:, :HALF] for c in columns], axis=1),
            jnp.concatenate([c[:, HALF:] for c in columns], axis=1),
        ],
        axis=0,
    )
    real = dot(wx_ref[:rows, :], stacked)
    imag = dot(wx_ref[rows:, :], stacked)
    lane0 = lax.broadcasted_iota(jnp.int32, (ZTILE, HALF), 1) == 0
    for part in range(zrows // ZTILE):
        lanes = slice(part * HALF, (part + 1) * HALF)
        zs = slice(part * ZTILE, (part + 1) * ZTILE)

        def put(j, re, im):
            out_ref[j, 0, zs, 0:HALF] = re.astype(jnp.bfloat16)
            out_ref[j, 0, zs, HALF:] = im.astype(jnp.bfloat16)

        def at(j):
            block = slice(j * ZTILE, (j + 1) * ZTILE)
            return real[block, lanes], imag[block, lanes]

        for j in (0, GX // 2):
            put(j, *at(j))
        for j in range(1, GX // 2):
            re, im = at(j)
            re_m, im_m = at(GX - j)
            put(j, jnp.where(lane0, 0.5 * (re + re_m), re), jnp.where(lane0, 0.5 * (im - im_m), im))
            put(
                GX - j,
                jnp.where(lane0, 0.5 * (im + im_m), re_m),
                jnp.where(lane0, 0.5 * (re - re_m), im_m),
            )


def analyse(band, pairs, extents, place):
    slots, zrows = band.shape[0] * FACES, band.shape[2]
    tables = (pooling_table(), half_y_table(), forward_x_table())
    whole = [pl.BlockSpec(t.shape, lambda i, *_: (0, 0)) for t in tables]
    return pl.pallas_call(
        functools.partial(analyse_kernel, slots, zrows),
        grid_spec=pltpu.PrefetchScalarGridSpec(
            num_scalar_prefetch=3,
            grid=(slots,),
            in_specs=[
                pl.BlockSpec(
                    (1, 1, zrows, 2 * GX, 2 * GY), lambda i, *_: (i // FACES, i % FACES, 0, 0, 0)
                )
            ]
            + whole,
            out_specs=pl.BlockSpec((GX, 1, zrows, GY), lambda i, *_: (0, i, 0, 0)),
            scratch_shapes=[pltpu.VMEM((2 * ZTILE * GX, 128), jnp.float32)],
        ),
        out_shape=jax.ShapeDtypeStruct((GX, slots, zrows, GY), jnp.bfloat16),
        compiler_params=pltpu.CompilerParams(vmem_limit_bytes=VMEM_BYTES),
        name="analyse",
    )(pairs, extents, place, band, *(jnp.asarray(t) for t in tables))


def normalised(a_re, a_im, b_re, b_im):
    cross_re = a_re * b_re + a_im * b_im
    cross_im = a_im * b_re - a_re * b_im
    scale = lax.rsqrt(cross_re * cross_re + cross_im * cross_im + 1.0)
    return (cross_re * scale).astype(jnp.bfloat16), (cross_im * scale).astype(jnp.bfloat16)


def correlate_kernel(
    slabs, tiles_here, pairs_ref, place_ref, in_ref, wz_ref, wzi_ref, out_ref
):
    tiles = in_ref.shape[0] // slabs
    total = pairs_ref.shape[1]
    pairs_here = out_ref.shape[1]
    zrows = GZ // slabs
    both_real = (place_ref[0] == 0) | (place_ref[0] == GX // 2)
    lane = lax.broadcasted_iota(jnp.int32, (GZ, HALF), 1)
    lane0 = lane == 0

    def load(p, end, half):
        tile = pairs_ref[2 * end, p]
        row = tile // tiles_here
        pos = tile % tiles_here * FACES + pairs_ref[2 * end + 1, p]
        lanes = slice(half * HALF, (half + 1) * HALF)
        return jnp.concatenate([in_ref[row + s * tiles, pos, :, lanes] for s in range(slabs)], axis=0)

    def forward(re, im):
        spec = dot(wz_ref[...], jnp.concatenate([re, im], axis=0))
        return spec.astype(jnp.bfloat16).astype(jnp.float32)

    def phase_of(spec):
        return normalised(spec[:GZ, :HALF], spec[GZ:, :HALF], spec[:GZ, HALF:], spec[GZ:, HALF:])

    drop = lane0 & both_real
    for p in range(0, total, 2):
        phases = []
        for q in (p, p + 1):
            re = jnp.concatenate([load(q, 0, 0), load(q, 1, 0)], axis=1)
            im = jnp.concatenate(
                [
                    jnp.where(drop, 0.0, load(q, end, 1).astype(jnp.float32)).astype(jnp.bfloat16)
                    for end in (0, 1)
                ],
                axis=1,
            )
            phases.append(phase_of(forward(re, im)))
        stacked = jnp.concatenate(
            [
                jnp.concatenate([phases[0][0], phases[1][0]], axis=1),
                jnp.concatenate([phases[0][1], phases[1][1]], axis=1),
            ],
            axis=0,
        )
        w = dot(wzi_ref[...], stacked).astype(jnp.bfloat16)
        for k, q in enumerate((p, p + 1)):
            for half in (0, 1):
                plane = w[half * GZ : (half + 1) * GZ, k * HALF : (k + 1) * HALF]
                for s in range(slabs):
                    out_ref[
                        q // pairs_here + s * tiles,
                        q % pairs_here,
                        :,
                        half * HALF : (half + 1) * HALF,
                    ] = plane[s * zrows : (s + 1) * zrows]

    @pl.when(both_real)
    def _():
        first = jnp.zeros((GZ, HALF), jnp.float32)
        second = jnp.zeros((GZ, HALF), jnp.float32)
        for p in range(total):
            a = load(p, 0, 1).astype(jnp.float32)[:, 0:1]
            b = load(p, 1, 1).astype(jnp.float32)[:, 0:1]
            first = jnp.where(lane == p, a, first)
            second = jnp.where(lane == p, b, second)
        re = jnp.concatenate([first, second], axis=1).astype(jnp.bfloat16)
        phase = phase_of(forward(re, jnp.zeros_like(re)))
        w = dot(wzi_ref[...], jnp.concatenate(phase, axis=0))[:GZ]
        for p in range(total):
            column = w[:, p : p + 1]
            for s in range(slabs):
                at = (p // pairs_here + s * tiles, p % pairs_here, slice(None), slice(HALF, 2 * HALF))
                old = out_ref[at].astype(jnp.float32)
                rows = slice(s * zrows, (s + 1) * zrows)
                out_ref[at] = jnp.where(lane0[rows], column[rows], old).astype(jnp.bfloat16)


def correlate(spread, pairs, place, slabs, tiles_here):
    devices, _, zrows, _ = spread.shape
    pairs_here = pairs.shape[1] * slabs // devices
    tables = (forward_z_table(), inverse_z_table())
    vmem = pl.BlockSpec(memory_space=pltpu.VMEM)
    smem = pl.BlockSpec(memory_space=pltpu.SMEM)
    return pl.pallas_call(
        functools.partial(correlate_kernel, slabs, tiles_here),
        in_specs=[smem, smem, vmem, vmem, vmem],
        out_specs=vmem,
        out_shape=jax.ShapeDtypeStruct((devices, pairs_here, zrows, GY), jnp.bfloat16),
        compiler_params=pltpu.CompilerParams(vmem_limit_bytes=VMEM_BYTES // 2),
        name="correlate",
    )(pairs, place, spread, *(jnp.asarray(t) for t in tables))


def synthesise_kernel(zrows, in_ref, wx_ref, wy_ref, out_ref):
    rows = ZTILE * GX
    parts = zrows // ZTILE
    lane0 = lax.broadcasted_iota(jnp.int32, (ZTILE, HALF), 1) == 0
    real, imag = [], []
    for part in range(parts):
        zs = slice(part * ZTILE, (part + 1) * ZTILE)

        def at(j):
            return (
                in_ref[j, 0, zs, 0:HALF].astype(jnp.float32),
                in_ref[j, 0, zs, HALF:].astype(jnp.float32),
            )

        blocks = [None] * GX
        for j in (0, GX // 2):
            blocks[j] = at(j)
        for j in range(1, GX // 2):
            re, im = at(j)
            re_m, im_m = at(GX - j)
            blocks[j] = (
                jnp.where(lane0, re + im_m, re),
                jnp.where(lane0, im + re_m, im),
            )
            blocks[GX - j] = (
                jnp.where(lane0, re - im_m, re_m),
                jnp.where(lane0, re_m - im, im_m),
            )
        real.append(jnp.concatenate([b[0].astype(jnp.bfloat16) for b in blocks], axis=0))
        imag.append(jnp.concatenate([b[1].astype(jnp.bfloat16) for b in blocks], axis=0))
    stacked = jnp.concatenate(
        [jnp.concatenate(real, axis=1), jnp.concatenate(imag, axis=1)], axis=0
    )
    v_re = dot(wx_ref[:rows, :], stacked).astype(jnp.bfloat16)
    v_im = dot(wx_ref[rows:, :], stacked).astype(jnp.bfloat16)
    for part in range(parts):
        lanes = slice(part * HALF, (part + 1) * HALF)
        v = jnp.concatenate([v_re[:, lanes], v_im[:, lanes]], axis=1)
        out_ref[0, part * ZTILE : (part + 1) * ZTILE] = dot(v, wy_ref[...]).reshape(ZTILE, GX, GY)


def synthesise(returned):
    _, pairs_here, zrows, _ = returned.shape
    tables = (inverse_x_table(), half_y_inverse())
    return pl.pallas_call(
        functools.partial(synthesise_kernel, zrows),
        grid=(pairs_here,),
        in_specs=[pl.BlockSpec((GX, 1, zrows, GY), lambda i: (0, i, 0, 0))]
        + [pl.BlockSpec(t.shape, lambda i: (0, 0)) for t in tables],
        out_specs=pl.BlockSpec((1, zrows, GX, GY), lambda i: (i, 0, 0, 0)),
        out_shape=jax.ShapeDtypeStruct((pairs_here, zrows, GX, GY), jnp.float32),
        compiler_params=pltpu.CompilerParams(vmem_limit_bytes=VMEM_BYTES),
        name="synthesise",
    )(returned, *(jnp.asarray(t) for t in tables))


def shards(band, pairs, extents):
    tiles, slabs = lax.axis_size("tile"), lax.axis_size("zslab")
    zrows = band.shape[2]
    if tiles * slabs != GX or zrows % ZTILE or pairs.shape[0] % (2 * tiles):
        return general_shards(band, pairs, extents)
    pairs, extents = pairs.T, extents.T
    tile = lax.axis_index("tile").astype(jnp.int32)
    device = lax.axis_index("zslab").astype(jnp.int32) * tiles + tile
    spectra = analyse(band, pairs, extents, tile[None])
    spread = lax.all_to_all(spectra, ("zslab", "tile"), split_axis=0, concat_axis=0, tiled=True)
    w = correlate(spread, pairs, device[None], slabs, band.shape[0])
    returned = lax.all_to_all(w, ("zslab", "tile"), split_axis=0, concat_axis=0, tiled=True)
    return synthesise(returned)


def solution(mesh):
    placed = (P("tile", None, "zslab", None, None), P(), P())
    return jax.shard_map(
        shards,
        mesh=mesh,
        in_specs=placed,
        out_specs=P("tile", "zslab", None, None),
        check_vma=False,
    )
```

```python
import functools
import math


import jax
import jax.numpy as jnp
import numpy as np
from jax import lax
from jax.experimental import pallas as pl
from jax.experimental.pallas import tpu as pltpu
from jax.sharding import PartitionSpec as P

GX = 32
GY = 256
GZ = 128
FACES = 4


def dft_tables(length):
    indices = jnp.arange(length, dtype=jnp.int32)
    modular = indices[:, None] * indices[None, :] % length
    angles = modular.astype(jnp.float32) * (2.0 * math.pi / length)
    factor = 1.0 / math.sqrt(length)
    return (
        (jnp.cos(angles) * factor).astype(jnp.bfloat16),
        (jnp.sin(angles) * factor).astype(jnp.bfloat16),
    )


def product(form, left, right):
    return jnp.einsum(form, left, right, preferred_element_type=jnp.float32)


def reduce_resolution(image_volume, crop_bounds):
    row_mask = (
        jnp.arange(image_volume.shape[2], dtype=jnp.int32)[None, :] < crop_bounds[:, 0:1]
    ).astype(jnp.bfloat16)
    col_mask = (
        jnp.arange(image_volume.shape[3], dtype=jnp.int32)[None, :] < crop_bounds[:, 1:2]
    ).astype(jnp.bfloat16)
    masked = image_volume * row_mask[:, None, :, None] * col_mask[:, None, None, :]
    raw_cols = jnp.arange(image_volume.shape[3], dtype=jnp.int32)
    pooled_cols = jnp.arange(GY, dtype=jnp.int32)
    pooling = jnp.where(raw_cols[:, None] // 2 == pooled_cols[None, :], 0.5, 0.0).astype(
        jnp.bfloat16
    )
    along_pooled = product("szxy,yk->szxk", masked, pooling)
    shaped = along_pooled.reshape(image_volume.shape[0], image_volume.shape[1], GX, 2, GY)
    return (shaped[:, :, :, 0, :] + shaped[:, :, :, 1, :]).astype(jnp.bfloat16)


def cross_phase(owner_re, owner_im, pairs, tiles_here):
    first_dev = pairs[:, 0] // tiles_here
    first_pos = pairs[:, 0] % tiles_here * FACES + pairs[:, 1]
    second_tile_device = pairs[:, 2] // tiles_here
    second_pos = pairs[:, 2] % tiles_here * FACES + pairs[:, 3]
    first_re = owner_re[first_dev, :, first_pos].astype(jnp.float32)
    first_im = owner_im[first_dev, :, first_pos].astype(jnp.float32)
    second_re = owner_re[second_tile_device, :, second_pos].astype(jnp.float32)
    second_im = owner_im[second_tile_device, :, second_pos].astype(jnp.float32)
    cross_re = first_re * second_re + first_im * second_im
    cross_im = first_im * second_re - first_re * second_im
    scaled = jnp.sqrt(cross_re * cross_re + cross_im * cross_im + 1.0)
    return ((cross_re / scaled).astype(jnp.bfloat16), (cross_im / scaled).astype(jnp.bfloat16))


def inverse_z(phase_real_part, phase_im, tables_z):
    w_re = (
        product("pmjk,mz->pzjk", phase_real_part, tables_z[0])
        - product("pmjk,mz->pzjk", phase_im, tables_z[1])
    ).astype(jnp.bfloat16)
    w_im = (
        product("pmjk,mz->pzjk", phase_im, tables_z[0])
        + product("pmjk,mz->pzjk", phase_real_part, tables_z[1])
    ).astype(jnp.bfloat16)
    return (w_re, w_im)


def inverse_x(w_re, w_im, tables_x):
    v_re = (
        product("pzjk,jx->pzxk", w_re, tables_x[0]) - product("pzjk,jx->pzxk", w_im, tables_x[1])
    ).astype(jnp.bfloat16)
    v_im = (
        product("pzjk,jx->pzxk", w_im, tables_x[0]) + product("pzjk,jx->pzxk", w_re, tables_x[1])
    ).astype(jnp.bfloat16)
    return (v_re, v_im)


def general_shards(band, pairs, extents):
    tables_x = dft_tables(GX)
    tables_y = dft_tables(GY)
    tables_z = dft_tables(GZ)
    tiles_here = band.shape[0]
    slots = tiles_here * FACES
    zrows = band.shape[2]
    tile_pos = lax.axis_index("tile")
    global_slot = tile_pos * slots + jnp.arange(slots, dtype=jnp.int32)
    first_slot = pairs[:, 0] * FACES + pairs[:, 1]
    second_slot = pairs[:, 2] * FACES + pairs[:, 3]
    matches = (
        (first_slot[None, :] == global_slot[:, None])
        | (second_slot[None, :] == global_slot[:, None])
    ).astype(jnp.int32)
    crop_bounds = jnp.sum(matches[:, :, None] * extents[None, :, :], axis=1)
    image_volume = band.reshape(slots, zrows, 2 * GX, 2 * GY)
    reduced_volume = reduce_resolution(image_volume, crop_bounds)
    y_re = product("szxy,yk->szxk", reduced_volume, tables_y[0]).astype(jnp.bfloat16)
    y_im = (-product("szxy,yk->szxk", reduced_volume, tables_y[1])).astype(jnp.bfloat16)
    x_re = (
        product("szxk,xj->szjk", y_re, tables_x[0]) + product("szxk,xj->szjk", y_im, tables_x[1])
    ).astype(jnp.bfloat16)
    x_im = (
        product("szxk,xj->szjk", y_im, tables_x[0]) - product("szxk,xj->szjk", y_re, tables_x[1])
    ).astype(jnp.bfloat16)
    kx_part = GX // lax.axis_size("zslab")
    re_in = lax.all_to_all(x_re, "zslab", split_axis=2, concat_axis=1, tiled=True)
    im_in = lax.all_to_all(x_im, "zslab", split_axis=2, concat_axis=1, tiled=True)
    out_re = (
        product("szjk,zm->msjk", re_in, tables_z[0]) + product("szjk,zm->msjk", im_in, tables_z[1])
    ).astype(jnp.bfloat16)
    out_im = (
        product("szjk,zm->msjk", im_in, tables_z[0]) - product("szjk,zm->msjk", re_in, tables_z[1])
    ).astype(jnp.bfloat16)
    tile_count = lax.axis_size("tile")
    kz_part = GZ // tile_count
    spectra = (
        lax.all_to_all(out_re, "tile", split_axis=0, concat_axis=0, tiled=True),
        lax.all_to_all(out_im, "tile", split_axis=0, concat_axis=0, tiled=True),
    )
    owner_re = spectra[0].reshape(tile_count, kz_part, slots, kx_part, GY)
    owner_im = spectra[1].reshape(tile_count, kz_part, slots, kx_part, GY)
    phase_real_part, phase_im = cross_phase(owner_re, owner_im, pairs, tiles_here)
    returned = (
        lax.all_to_all(phase_real_part, "tile", split_axis=0, concat_axis=1, tiled=True),
        lax.all_to_all(phase_im, "tile", split_axis=0, concat_axis=1, tiled=True),
    )
    w_re, w_im = inverse_z(returned[0], returned[1], tables_z)
    v_re, v_im = inverse_x(
        lax.all_to_all(w_re, "zslab", split_axis=1, concat_axis=2, tiled=True),
        lax.all_to_all(w_im, "zslab", split_axis=1, concat_axis=2, tiled=True),
        tables_x,
    )
    return product("pzxk,ky->pzxy", v_re, tables_y[0]) - product("pzxk,ky->pzxy", v_im, tables_y[1])


HALF = GY // 2
ZTILE = 16
ZHALF = ZTILE // 2
VMEM_BYTES = 32 * 1024 * 1024


def host_tables(length):
    indices = np.arange(length, dtype=np.int32)
    modular = indices[:, None] * indices[None, :] % length
    angles = modular.astype(np.float32) * np.float32(2.0 * math.pi / length)
    factor = np.float32(1.0 / math.sqrt(length))
    return (
        (np.cos(angles) * factor).astype(jnp.bfloat16),
        (np.sin(angles) * factor).astype(jnp.bfloat16),
    )


def pooling_table():
    raw = np.arange(2 * GY)[:, None] // 2
    return np.where(raw == np.arange(GY)[None, :], 0.5, 0.0).astype(jnp.bfloat16)


def half_y_table():
    cosine, sine = host_tables(GY)
    imag = -sine[:, :HALF]
    imag[:, 0] = cosine[:, HALF]
    return np.concatenate([cosine[:, :HALF], imag], axis=1)


def half_y_inverse():
    cosine, sine = host_tables(GY)
    two = np.array(2.0, jnp.bfloat16)
    real = cosine[:HALF, :] * two
    real[0] = cosine[0]
    imag = -sine[:HALF, :] * two
    imag[0] = cosine[HALF]
    return np.concatenate([real, imag], axis=0)


def spread_x(table):
    planes = np.eye(ZHALF, dtype=np.float32)
    grid = np.einsum("jx,az->jazx", table.astype(np.float32), planes)
    return grid.reshape(GX * ZHALF, ZHALF * GX).astype(jnp.bfloat16)


def forward_x_table():
    cosine, sine = (spread_x(table) for table in host_tables(GX))
    return np.block([[cosine, sine], [-sine, cosine]])


def inverse_x_table():
    return np.ascontiguousarray(forward_x_table().T)


def forward_z_table():
    cosine, sine = host_tables(GZ)
    return np.block([[cosine, sine], [-sine, cosine]])


def inverse_z_table():
    cosine, sine = host_tables(GZ)
    return np.block([[cosine, -sine], [sine, cosine]])


def dot(left, right):
    return jnp.dot(left, right, preferred_element_type=jnp.float32)


def analyse_kernel(
    slots, pairs_ref, extents_ref, tile_ref, band_ref, pool_ref, wy_ref, wx_ref, out_ref, live_pool_ref, pooled_ref
):
    slot = tile_ref[0] * slots + pl.program_id(0)
    across, along = jnp.int32(0), jnp.int32(0)
    for p in range(pairs_ref.shape[1]):
        first = pairs_ref[0, p] * FACES + pairs_ref[1, p]
        second = pairs_ref[2, p] * FACES + pairs_ref[3, p]
        named = (first == slot) | (second == slot)
        across = jnp.where(named, extents_ref[0, p], across)
        along = jnp.where(named, extents_ref[1, p], along)

    @pl.when(pl.program_id(1) == 0)
    def _():
        raw_col = lax.broadcasted_iota(jnp.int32, (2 * GY, GY), 0)
        pool = jnp.where(raw_col < along, pool_ref[...].astype(jnp.float32), 0.0)
        live_pool_ref[...] = pool.astype(jnp.bfloat16)

    rows = ZHALF * GX
    cell = lax.broadcasted_iota(jnp.int32, (ZHALF, GX, 128), 1)
    even_live = 2 * cell < across
    odd_live = 2 * cell + 1 < across
    real, imag = [], []
    for half in range(2):
        raw = band_ref[0, 0, half * ZHALF : (half + 1) * ZHALF].reshape(2 * rows, 2 * GY)
        pooled = dot(raw, live_pool_ref[...])
        cells = []
        for lane in range(GY // 128):
            part_ref = pooled_ref.at[half, lane]
            part_ref[...] = pooled[:, lane * 128 : (lane + 1) * 128]
            even = part_ref[pl.ds(0, rows, stride=2), :].reshape(ZHALF, GX, 128)
            odd = part_ref[pl.ds(1, rows, stride=2), :].reshape(ZHALF, GX, 128)
            both = jnp.where(even_live, even, 0.0) + jnp.where(odd_live, odd, 0.0)
            cells.append(both.reshape(rows, 128).astype(jnp.bfloat16))
        y = dot(jnp.concatenate(cells, axis=1), wy_ref[...]).astype(jnp.bfloat16)
        real.append(y[:, :HALF])
        imag.append(y[:, HALF:])
    stacked = jnp.concatenate(
        [jnp.concatenate(real, axis=1), jnp.concatenate(imag, axis=1)], axis=0
    )
    real = dot(wx_ref[:rows, :], stacked)
    imag = dot(wx_ref[rows:, :], stacked)
    lane0 = lax.broadcasted_iota(jnp.int32, (ZTILE, HALF), 1) == 0

    def at(j):
        block = slice(j * ZHALF, (j + 1) * ZHALF)
        return tuple(
            jnp.concatenate([part[block, :HALF], part[block, HALF:]], axis=0) for part in (real, imag)
        )

    def put(j, re, im):
        out_ref[j, 0, :, 0:HALF] = re.astype(jnp.bfloat16)
        out_ref[j, 0, :, HALF:] = im.astype(jnp.bfloat16)

    for j in (0, GX // 2):
        put(j, *at(j))
    for j in range(1, GX // 2):
        re, im = at(j)
        re_m, im_m = at(GX - j)
        put(j, jnp.where(lane0, 0.5 * (re + re_m), re), jnp.where(lane0, 0.5 * (im - im_m), im))
        put(
            GX - j,
            jnp.where(lane0, 0.5 * (im + im_m), re_m),
            jnp.where(lane0, 0.5 * (re - re_m), im_m),
        )


def analyse(band, pairs, extents, tile):
    slots, zrows = band.shape[0] * FACES, band.shape[2]
    tables = (pooling_table(), half_y_table(), forward_x_table())
    whole = [pl.BlockSpec(t.shape, lambda i, z, *_: (0, 0)) for t in tables]
    return pl.pallas_call(
        functools.partial(analyse_kernel, slots),
        grid_spec=pltpu.PrefetchScalarGridSpec(
            num_scalar_prefetch=3,
            grid=(slots, zrows // ZTILE),
            in_specs=[
                pl.BlockSpec(
                    (1, 1, ZTILE, 2 * GX, 2 * GY), lambda i, z, *_: (i // FACES, i % FACES, z, 0, 0)
                )
            ]
            + whole,
            out_specs=pl.BlockSpec((GX, 1, ZTILE, GY), lambda i, z, *_: (0, i, z, 0)),
            scratch_shapes=[
                pltpu.VMEM((2 * GY, GY), jnp.bfloat16),
                pltpu.VMEM((2, GY // 128, 2 * ZHALF * GX, 128), jnp.float32),
            ],
        ),
        out_shape=jax.ShapeDtypeStruct((GX, slots, zrows, GY), jnp.bfloat16),
        compiler_params=pltpu.CompilerParams(vmem_limit_bytes=VMEM_BYTES),
        name="analyse",
    )(pairs, extents, tile, band, *(jnp.asarray(t) for t in tables))


def normalised(a_re, a_im, b_re, b_im):
    cross_re = a_re * b_re + a_im * b_im
    cross_im = a_im * b_re - a_re * b_im
    scale = lax.rsqrt(cross_re * cross_re + cross_im * cross_im + 1.0)
    return (cross_re * scale).astype(jnp.bfloat16), (cross_im * scale).astype(jnp.bfloat16)


def correlate_kernel(
    slabs, tiles_here, pairs_ref, place_ref, in_ref, wz_ref, wzi_ref, out_ref
):
    tiles = in_ref.shape[0] // slabs
    total = pairs_ref.shape[1]
    pairs_here = out_ref.shape[1]
    zrows = GZ // slabs
    both_real = (place_ref[0] == 0) | (place_ref[0] == GX // 2)
    lane = lax.broadcasted_iota(jnp.int32, (GZ, HALF), 1)
    lane0 = lane == 0

    def load(p, end, half):
        tile = pairs_ref[2 * end, p]
        row = tile // tiles_here
        pos = tile % tiles_here * FACES + pairs_ref[2 * end + 1, p]
        lanes = slice(half * HALF, (half + 1) * HALF)
        return jnp.concatenate([in_ref[row + s * tiles, pos, :, lanes] for s in range(slabs)], axis=0)

    def forward(re, im):
        spec = dot(wz_ref[...], jnp.concatenate([re, im], axis=0))
        return spec.astype(jnp.bfloat16).astype(jnp.float32)

    def phase_of(spec):
        return normalised(spec[:GZ, :HALF], spec[GZ:, :HALF], spec[:GZ, HALF:], spec[GZ:, HALF:])

    keep = jnp.where(lane0 & both_real, 0.0, 1.0).astype(jnp.bfloat16)
    for p in range(0, total, 2):
        phases = []
        for q in (p, p + 1):
            re = jnp.concatenate([load(q, 0, 0), load(q, 1, 0)], axis=1)
            im = jnp.concatenate([load(q, 0, 1) * keep, load(q, 1, 1) * keep], axis=1)
            phases.append(phase_of(forward(re, im)))
        stacked = jnp.concatenate(
            [
                jnp.concatenate([phases[0][0], phases[1][0]], axis=1),
                jnp.concatenate([phases[0][1], phases[1][1]], axis=1),
            ],
            axis=0,
        )
        w = dot(wzi_ref[...], stacked).astype(jnp.bfloat16)
        for k, q in enumerate((p, p + 1)):
            for half in (0, 1):
                plane = w[half * GZ : (half + 1) * GZ, k * HALF : (k + 1) * HALF]
                for s in range(slabs):
                    out_ref[
                        q // pairs_here + s * tiles,
                        q % pairs_here,
                        :,
                        half * HALF : (half + 1) * HALF,
                    ] = plane[s * zrows : (s + 1) * zrows]

    @pl.when(both_real)
    def _():
        first = jnp.zeros((GZ, HALF), jnp.float32)
        second = jnp.zeros((GZ, HALF), jnp.float32)
        for p in range(total):
            a = load(p, 0, 1).astype(jnp.float32)[:, 0:1]
            b = load(p, 1, 1).astype(jnp.float32)[:, 0:1]
            first = jnp.where(lane == p, a, first)
            second = jnp.where(lane == p, b, second)
        re = jnp.concatenate([first, second], axis=1).astype(jnp.bfloat16)
        phase = phase_of(forward(re, jnp.zeros_like(re)))
        w = dot(wzi_ref[...], jnp.concatenate(phase, axis=0))[:GZ]
        for p in range(total):
            column = w[:, p : p + 1]
            for s in range(slabs):
                at = (p // pairs_here + s * tiles, p % pairs_here, slice(None), slice(HALF, 2 * HALF))
                old = out_ref[at].astype(jnp.float32)
                rows = slice(s * zrows, (s + 1) * zrows)
                out_ref[at] = jnp.where(lane0[rows], column[rows], old).astype(jnp.bfloat16)


def correlate(spread, pairs, place, slabs, tiles_here):
    devices, _, zrows, _ = spread.shape
    pairs_here = pairs.shape[1] * slabs // devices
    tables = (forward_z_table(), inverse_z_table())
    vmem = pl.BlockSpec(memory_space=pltpu.VMEM)
    smem = pl.BlockSpec(memory_space=pltpu.SMEM)
    return pl.pallas_call(
        functools.partial(correlate_kernel, slabs, tiles_here),
        in_specs=[smem, smem, vmem, vmem, vmem],
        out_specs=vmem,
        out_shape=jax.ShapeDtypeStruct((devices, pairs_here, zrows, GY), jnp.bfloat16),
        compiler_params=pltpu.CompilerParams(vmem_limit_bytes=VMEM_BYTES),
        name="correlate",
    )(pairs, place, spread, *(jnp.asarray(t) for t in tables))


def synthesise_kernel(in_ref, wx_ref, wy_ref, out_ref):
    rows = ZHALF * GX
    lane0 = lax.broadcasted_iota(jnp.int32, (ZTILE, HALF), 1) == 0

    def at(j):
        return in_ref[j, 0, :, 0:HALF].astype(jnp.float32), in_ref[j, 0, :, HALF:].astype(jnp.float32)

    blocks = [None] * GX
    for j in (0, GX // 2):
        blocks[j] = at(j)
    for j in range(1, GX // 2):
        re, im = at(j)
        re_m, im_m = at(GX - j)
        blocks[j] = (jnp.where(lane0, re + im_m, re), jnp.where(lane0, im + re_m, im))
        blocks[GX - j] = (jnp.where(lane0, re - im_m, re_m), jnp.where(lane0, re_m - im, im_m))
    stacked = jnp.concatenate(
        [
            jnp.concatenate(
                [
                    jnp.concatenate([b[part][half * ZHALF : (half + 1) * ZHALF] for b in blocks], axis=0)
                    for half in range(2)
                ],
                axis=1,
            )
            for part in range(2)
        ],
        axis=0,
    ).astype(jnp.bfloat16)
    v_re = dot(wx_ref[:rows, :], stacked).astype(jnp.bfloat16)
    v_im = dot(wx_ref[rows:, :], stacked).astype(jnp.bfloat16)
    for half in range(2):
        lanes = slice(half * HALF, (half + 1) * HALF)
        v = jnp.concatenate([v_re[:, lanes], v_im[:, lanes]], axis=1)
        out_ref[0, half * ZHALF : (half + 1) * ZHALF] = dot(v, wy_ref[...]).reshape(ZHALF, GX, GY)


def synthesise(returned):
    _, pairs_here, zrows, _ = returned.shape
    tables = (inverse_x_table(), half_y_inverse())
    return pl.pallas_call(
        synthesise_kernel,
        grid=(pairs_here, zrows // ZTILE),
        in_specs=[pl.BlockSpec((GX, 1, ZTILE, GY), lambda i, z: (0, i, z, 0))]
        + [pl.BlockSpec(t.shape, lambda i, z: (0, 0)) for t in tables],
        out_specs=pl.BlockSpec((1, ZTILE, GX, GY), lambda i, z: (i, z, 0, 0)),
        out_shape=jax.ShapeDtypeStruct((pairs_here, zrows, GX, GY), jnp.float32),
        compiler_params=pltpu.CompilerParams(vmem_limit_bytes=VMEM_BYTES),
        name="synthesise",
    )(returned, *(jnp.asarray(t) for t in tables))


def shards(band, pairs, extents):
    tiles, slabs = lax.axis_size("tile"), lax.axis_size("zslab")
    zrows = band.shape[2]
    if tiles * slabs != GX or zrows % ZTILE or pairs.shape[0] % (2 * tiles):
        return general_shards(band, pairs, extents)
    pairs, extents = pairs.T, extents.T
    tile = lax.axis_index("tile").astype(jnp.int32)
    device = lax.axis_index("zslab").astype(jnp.int32) * tiles + tile
    spectra = analyse(band, pairs, extents, tile[None])
    spread = lax.all_to_all(spectra, ("zslab", "tile"), split_axis=0, concat_axis=0, tiled=True)
    w = correlate(spread, pairs, device[None], slabs, band.shape[0])
    returned = lax.all_to_all(w, ("zslab", "tile"), split_axis=0, concat_axis=0, tiled=True)
    return synthesise(returned)


def solution(mesh):
    placed = (P("tile", None, "zslab", None, None), P(), P())
    return jax.shard_map(
        shards,
        mesh=mesh,
        in_specs=placed,
        out_specs=P("tile", "zslab", None, None),
        check_vma=False,
    )
```

```python
import functools
import math


import jax
import jax.numpy as jnp
import numpy as np
from jax import lax
from jax.experimental import pallas as pl
from jax.experimental.pallas import tpu as pltpu
from jax.sharding import PartitionSpec as P

GX = 32
GY = 256
GZ = 128
FACES = 4


def dft_tables(length):
    indices = jnp.arange(length, dtype=jnp.int32)
    modular = indices[:, None] * indices[None, :] % length
    angles = modular.astype(jnp.float32) * (2.0 * math.pi / length)
    factor = 1.0 / math.sqrt(length)
    return (
        (jnp.cos(angles) * factor).astype(jnp.bfloat16),
        (jnp.sin(angles) * factor).astype(jnp.bfloat16),
    )


def product(form, left, right):
    return jnp.einsum(form, left, right, preferred_element_type=jnp.float32)


def reduce_resolution(image_volume, crop_bounds):
    row_mask = (
        jnp.arange(image_volume.shape[2], dtype=jnp.int32)[None, :] < crop_bounds[:, 0:1]
    ).astype(jnp.bfloat16)
    col_mask = (
        jnp.arange(image_volume.shape[3], dtype=jnp.int32)[None, :] < crop_bounds[:, 1:2]
    ).astype(jnp.bfloat16)
    masked = image_volume * row_mask[:, None, :, None] * col_mask[:, None, None, :]
    raw_cols = jnp.arange(image_volume.shape[3], dtype=jnp.int32)
    pooled_cols = jnp.arange(GY, dtype=jnp.int32)
    pooling = jnp.where(raw_cols[:, None] // 2 == pooled_cols[None, :], 0.5, 0.0).astype(
        jnp.bfloat16
    )
    along_pooled = product("szxy,yk->szxk", masked, pooling)
    shaped = along_pooled.reshape(image_volume.shape[0], image_volume.shape[1], GX, 2, GY)
    return (shaped[:, :, :, 0, :] + shaped[:, :, :, 1, :]).astype(jnp.bfloat16)


def cross_phase(owner_re, owner_im, pairs, tiles_here):
    first_dev = pairs[:, 0] // tiles_here
    first_pos = pairs[:, 0] % tiles_here * FACES + pairs[:, 1]
    second_tile_device = pairs[:, 2] // tiles_here
    second_pos = pairs[:, 2] % tiles_here * FACES + pairs[:, 3]
    first_re = owner_re[first_dev, :, first_pos].astype(jnp.float32)
    first_im = owner_im[first_dev, :, first_pos].astype(jnp.float32)
    second_re = owner_re[second_tile_device, :, second_pos].astype(jnp.float32)
    second_im = owner_im[second_tile_device, :, second_pos].astype(jnp.float32)
    cross_re = first_re * second_re + first_im * second_im
    cross_im = first_im * second_re - first_re * second_im
    scaled = jnp.sqrt(cross_re * cross_re + cross_im * cross_im + 1.0)
    return ((cross_re / scaled).astype(jnp.bfloat16), (cross_im / scaled).astype(jnp.bfloat16))


def inverse_z(phase_real_part, phase_im, tables_z):
    w_re = (
        product("pmjk,mz->pzjk", phase_real_part, tables_z[0])
        - product("pmjk,mz->pzjk", phase_im, tables_z[1])
    ).astype(jnp.bfloat16)
    w_im = (
        product("pmjk,mz->pzjk", phase_im, tables_z[0])
        + product("pmjk,mz->pzjk", phase_real_part, tables_z[1])
    ).astype(jnp.bfloat16)
    return (w_re, w_im)


def inverse_x(w_re, w_im, tables_x):
    v_re = (
        product("pzjk,jx->pzxk", w_re, tables_x[0]) - product("pzjk,jx->pzxk", w_im, tables_x[1])
    ).astype(jnp.bfloat16)
    v_im = (
        product("pzjk,jx->pzxk", w_im, tables_x[0]) + product("pzjk,jx->pzxk", w_re, tables_x[1])
    ).astype(jnp.bfloat16)
    return (v_re, v_im)


def general_shards(band, pairs, extents):
    tables_x = dft_tables(GX)
    tables_y = dft_tables(GY)
    tables_z = dft_tables(GZ)
    tiles_here = band.shape[0]
    slots = tiles_here * FACES
    zrows = band.shape[2]
    tile_pos = lax.axis_index("tile")
    global_slot = tile_pos * slots + jnp.arange(slots, dtype=jnp.int32)
    first_slot = pairs[:, 0] * FACES + pairs[:, 1]
    second_slot = pairs[:, 2] * FACES + pairs[:, 3]
    matches = (
        (first_slot[None, :] == global_slot[:, None])
        | (second_slot[None, :] == global_slot[:, None])
    ).astype(jnp.int32)
    crop_bounds = jnp.sum(matches[:, :, None] * extents[None, :, :], axis=1)
    image_volume = band.reshape(slots, zrows, 2 * GX, 2 * GY)
    reduced_volume = reduce_resolution(image_volume, crop_bounds)
    y_re = product("szxy,yk->szxk", reduced_volume, tables_y[0]).astype(jnp.bfloat16)
    y_im = (-product("szxy,yk->szxk", reduced_volume, tables_y[1])).astype(jnp.bfloat16)
    x_re = (
        product("szxk,xj->szjk", y_re, tables_x[0]) + product("szxk,xj->szjk", y_im, tables_x[1])
    ).astype(jnp.bfloat16)
    x_im = (
        product("szxk,xj->szjk", y_im, tables_x[0]) - product("szxk,xj->szjk", y_re, tables_x[1])
    ).astype(jnp.bfloat16)
    kx_part = GX // lax.axis_size("zslab")
    re_in = lax.all_to_all(x_re, "zslab", split_axis=2, concat_axis=1, tiled=True)
    im_in = lax.all_to_all(x_im, "zslab", split_axis=2, concat_axis=1, tiled=True)
    out_re = (
        product("szjk,zm->msjk", re_in, tables_z[0]) + product("szjk,zm->msjk", im_in, tables_z[1])
    ).astype(jnp.bfloat16)
    out_im = (
        product("szjk,zm->msjk", im_in, tables_z[0]) - product("szjk,zm->msjk", re_in, tables_z[1])
    ).astype(jnp.bfloat16)
    tile_count = lax.axis_size("tile")
    kz_part = GZ // tile_count
    spectra = (
        lax.all_to_all(out_re, "tile", split_axis=0, concat_axis=0, tiled=True),
        lax.all_to_all(out_im, "tile", split_axis=0, concat_axis=0, tiled=True),
    )
    owner_re = spectra[0].reshape(tile_count, kz_part, slots, kx_part, GY)
    owner_im = spectra[1].reshape(tile_count, kz_part, slots, kx_part, GY)
    phase_real_part, phase_im = cross_phase(owner_re, owner_im, pairs, tiles_here)
    returned = (
        lax.all_to_all(phase_real_part, "tile", split_axis=0, concat_axis=1, tiled=True),
        lax.all_to_all(phase_im, "tile", split_axis=0, concat_axis=1, tiled=True),
    )
    w_re, w_im = inverse_z(returned[0], returned[1], tables_z)
    v_re, v_im = inverse_x(
        lax.all_to_all(w_re, "zslab", split_axis=1, concat_axis=2, tiled=True),
        lax.all_to_all(w_im, "zslab", split_axis=1, concat_axis=2, tiled=True),
        tables_x,
    )
    return product("pzxk,ky->pzxy", v_re, tables_y[0]) - product("pzxk,ky->pzxy", v_im, tables_y[1])


HALF = GY // 2
ZTILE = 16
ZHALF = ZTILE // 2
VMEM_BYTES = 32 * 1024 * 1024


def host_tables(length):
    indices = np.arange(length, dtype=np.int32)
    modular = indices[:, None] * indices[None, :] % length
    angles = modular.astype(np.float32) * np.float32(2.0 * math.pi / length)
    factor = np.float32(1.0 / math.sqrt(length))
    return (
        (np.cos(angles) * factor).astype(jnp.bfloat16),
        (np.sin(angles) * factor).astype(jnp.bfloat16),
    )


def pooling_table():
    raw = np.arange(2 * GY)[:, None] // 2
    return np.where(raw == np.arange(GY)[None, :], 0.5, 0.0).astype(jnp.bfloat16)


def half_y_table():
    cosine, sine = host_tables(GY)
    imag = -sine[:, :HALF]
    imag[:, 0] = cosine[:, HALF]
    return np.concatenate([cosine[:, :HALF], imag], axis=1)


def half_y_inverse():
    cosine, sine = host_tables(GY)
    two = np.array(2.0, jnp.bfloat16)
    real = cosine[:HALF, :] * two
    real[0] = cosine[0]
    imag = -sine[:HALF, :] * two
    imag[0] = cosine[HALF]
    return np.concatenate([real, imag], axis=0)


def spread_x(table):
    planes = np.eye(ZHALF, dtype=np.float32)
    grid = np.einsum("jx,az->jazx", table.astype(np.float32), planes)
    return grid.reshape(GX * ZHALF, ZHALF * GX).astype(jnp.bfloat16)


def mirror_order():
    order = [0, GX // 2]
    for j in range(1, GX // 2):
        order += [j, GX - j]
    return order


def forward_x_table():
    cosine, sine = (spread_x(table) for table in host_tables(GX))
    real = np.concatenate([cosine, sine], axis=1).reshape(GX, ZHALF, -1)
    imag = np.concatenate([-sine, cosine], axis=1).reshape(GX, ZHALF, -1)
    rows = np.stack([real, imag], axis=1)[mirror_order()]
    return rows.reshape(2 * GX * ZHALF, -1)


def inverse_x_table():
    cosine, sine = (spread_x(table) for table in host_tables(GX))
    return np.ascontiguousarray(np.block([[cosine, sine], [-sine, cosine]]).T)


def forward_z_table():
    cosine, sine = host_tables(GZ)
    return np.block([[cosine, sine], [-sine, cosine]])


def inverse_z_table():
    cosine, sine = host_tables(GZ)
    return np.block([[cosine, -sine], [sine, cosine]])


def dot(left, right):
    return jnp.dot(left, right, preferred_element_type=jnp.float32)


def analyse_kernel(
    slots, pairs_ref, extents_ref, tile_ref, band_ref, pool_ref, wy_ref, wx_ref, out_ref, pooled_ref
):
    slot = tile_ref[0] * slots + pl.program_id(0)
    across, along = jnp.int32(0), jnp.int32(0)
    for p in range(pairs_ref.shape[1]):
        first = pairs_ref[0, p] * FACES + pairs_ref[1, p]
        second = pairs_ref[2, p] * FACES + pairs_ref[3, p]
        named = (first == slot) | (second == slot)
        across = jnp.where(named, extents_ref[0, p], across)
        along = jnp.where(named, extents_ref[1, p], along)
    raw_col = lax.broadcasted_iota(jnp.int32, (2 * GY, GY), 0)
    pool = jnp.where(raw_col < along, pool_ref[...].astype(jnp.float32), 0.0).astype(jnp.bfloat16)
    rows = ZHALF * GX
    cell = lax.broadcasted_iota(jnp.int32, (ZHALF, GX, 128), 1)
    even_live = 2 * cell < across
    odd_live = 2 * cell + 1 < across
    lane0 = lax.broadcasted_iota(jnp.int32, (ZTILE, HALF), 1) == 0

    def along_y(unit):
        raw = band_ref[0, 0, unit * ZHALF : (unit + 1) * ZHALF].reshape(2 * rows, 2 * GY)
        pooled = dot(raw, pool)
        cells = []
        for lane in range(GY // 128):
            part_ref = pooled_ref.at[unit, lane]
            part_ref[...] = pooled[:, lane * 128 : (lane + 1) * 128]
            even = part_ref[pl.ds(0, rows, stride=2), :].reshape(ZHALF, GX, 128)
            odd = part_ref[pl.ds(1, rows, stride=2), :].reshape(ZHALF, GX, 128)
            both = jnp.where(even_live, even, 0.0) + jnp.where(odd_live, odd, 0.0)
            cells.append(both.reshape(rows, 128).astype(jnp.bfloat16))
        return dot(jnp.concatenate(cells, axis=1), wy_ref[...]).astype(jnp.bfloat16)

    for part in range(band_ref.shape[2] // ZTILE):
        units = [along_y(2 * part), along_y(2 * part + 1)]
        stacked = jnp.concatenate(
            [
                jnp.concatenate([y[:, :HALF] for y in units], axis=1),
                jnp.concatenate([y[:, HALF:] for y in units], axis=1),
            ],
            axis=0,
        )
        spectra = dot(wx_ref[...], stacked)
        zs = slice(part * ZTILE, (part + 1) * ZTILE)

        def at(n):
            blocks = [spectra[m * ZHALF : (m + 1) * ZHALF] for m in (2 * n, 2 * n + 1)]
            return [jnp.concatenate([b[:, :HALF], b[:, HALF:]], axis=0) for b in blocks]

        def put(j, re, im):
            out_ref[j, 0, zs, 0:HALF] = re.astype(jnp.bfloat16)
            out_ref[j, 0, zs, HALF:] = im.astype(jnp.bfloat16)

        put(0, *at(0))
        put(GX // 2, *at(1))
        for j in range(1, GX // 2):
            re, im = at(2 * j)
            re_m, im_m = at(2 * j + 1)
            put(j, jnp.where(lane0, 0.5 * (re + re_m), re), jnp.where(lane0, 0.5 * (im - im_m), im))
            put(
                GX - j,
                jnp.where(lane0, 0.5 * (im + im_m), re_m),
                jnp.where(lane0, 0.5 * (re - re_m), im_m),
            )


def analyse(band, pairs, extents, tile):
    slots, zrows = band.shape[0] * FACES, band.shape[2]
    tables = (pooling_table(), half_y_table(), forward_x_table())
    whole = [pl.BlockSpec(t.shape, lambda i, *_: (0, 0)) for t in tables]
    return pl.pallas_call(
        functools.partial(analyse_kernel, slots),
        grid_spec=pltpu.PrefetchScalarGridSpec(
            num_scalar_prefetch=3,
            grid=(slots,),
            in_specs=[
                pl.BlockSpec(
                    (1, 1, zrows, 2 * GX, 2 * GY), lambda i, *_: (i // FACES, i % FACES, 0, 0, 0)
                )
            ]
            + whole,
            out_specs=pl.BlockSpec((GX, 1, zrows, GY), lambda i, *_: (0, i, 0, 0)),
            scratch_shapes=[
                pltpu.VMEM((zrows // ZHALF, GY // 128, 2 * ZHALF * GX, 128), jnp.float32)
            ],
        ),
        out_shape=jax.ShapeDtypeStruct((GX, slots, zrows, GY), jnp.bfloat16),
        compiler_params=pltpu.CompilerParams(vmem_limit_bytes=VMEM_BYTES + VMEM_BYTES * 3 // 4),
        name="analyse",
    )(pairs, extents, tile, band, *(jnp.asarray(t) for t in tables))


def normalised(a_re, a_im, b_re, b_im):
    cross_re = a_re * b_re + a_im * b_im
    cross_im = a_im * b_re - a_re * b_im
    scale = lax.rsqrt(cross_re * cross_re + cross_im * cross_im + 1.0)
    return (cross_re * scale).astype(jnp.bfloat16), (cross_im * scale).astype(jnp.bfloat16)


def correlate_kernel(
    slabs, tiles_here, pairs_ref, place_ref, in_ref, wz_ref, wzi_ref, out_ref
):
    tiles = in_ref.shape[0] // slabs
    total = pairs_ref.shape[1]
    pairs_here = out_ref.shape[1]
    zrows = GZ // slabs
    both_real = (place_ref[0] == 0) | (place_ref[0] == GX // 2)
    lane = lax.broadcasted_iota(jnp.int32, (GZ, HALF), 1)
    lane0 = lane == 0

    def load(p, end, half):
        tile = pairs_ref[2 * end, p]
        row = tile // tiles_here
        pos = tile % tiles_here * FACES + pairs_ref[2 * end + 1, p]
        lanes = slice(half * HALF, (half + 1) * HALF)
        return jnp.concatenate([in_ref[row + s * tiles, pos, :, lanes] for s in range(slabs)], axis=0)

    def forward(re, im):
        spec = dot(wz_ref[...], jnp.concatenate([re, im], axis=0))
        return spec.astype(jnp.bfloat16).astype(jnp.float32)

    def phase_of(spec):
        return normalised(spec[:GZ, :HALF], spec[GZ:, :HALF], spec[:GZ, HALF:], spec[GZ:, HALF:])

    keep = jnp.where(lane0 & both_real, 0.0, 1.0).astype(jnp.bfloat16)
    for p in range(0, total, 2):
        phases = []
        for q in (p, p + 1):
            re = jnp.concatenate([load(q, 0, 0), load(q, 1, 0)], axis=1)
            im = jnp.concatenate([load(q, 0, 1) * keep, load(q, 1, 1) * keep], axis=1)
            phases.append(phase_of(forward(re, im)))
        stacked = jnp.concatenate(
            [
                jnp.concatenate([phases[0][0], phases[1][0]], axis=1),
                jnp.concatenate([phases[0][1], phases[1][1]], axis=1),
            ],
            axis=0,
        )
        w = dot(wzi_ref[...], stacked).astype(jnp.bfloat16)
        for k, q in enumerate((p, p + 1)):
            for half in (0, 1):
                plane = w[half * GZ : (half + 1) * GZ, k * HALF : (k + 1) * HALF]
                for s in range(slabs):
                    out_ref[
                        q // pairs_here + s * tiles,
                        q % pairs_here,
                        :,
                        half * HALF : (half + 1) * HALF,
                    ] = plane[s * zrows : (s + 1) * zrows]

    @pl.when(both_real)
    def _():
        first = jnp.zeros((GZ, HALF), jnp.float32)
        second = jnp.zeros((GZ, HALF), jnp.float32)
        for p in range(total):
            a = load(p, 0, 1).astype(jnp.float32)[:, 0:1]
            b = load(p, 1, 1).astype(jnp.float32)[:, 0:1]
            first = jnp.where(lane == p, a, first)
            second = jnp.where(lane == p, b, second)
        re = jnp.concatenate([first, second], axis=1).astype(jnp.bfloat16)
        phase = phase_of(forward(re, jnp.zeros_like(re)))
        w = dot(wzi_ref[...], jnp.concatenate(phase, axis=0))[:GZ]
        for p in range(total):
            column = w[:, p : p + 1]
            for s in range(slabs):
                at = (p // pairs_here + s * tiles, p % pairs_here, slice(None), slice(HALF, 2 * HALF))
                old = out_ref[at].astype(jnp.float32)
                rows = slice(s * zrows, (s + 1) * zrows)
                out_ref[at] = jnp.where(lane0[rows], column[rows], old).astype(jnp.bfloat16)


def correlate(spread, pairs, place, slabs, tiles_here):
    devices, _, zrows, _ = spread.shape
    pairs_here = pairs.shape[1] * slabs // devices
    tables = (forward_z_table(), inverse_z_table())
    vmem = pl.BlockSpec(memory_space=pltpu.VMEM)
    smem = pl.BlockSpec(memory_space=pltpu.SMEM)
    return pl.pallas_call(
        functools.partial(correlate_kernel, slabs, tiles_here),
        in_specs=[smem, smem, vmem, vmem, vmem],
        out_specs=vmem,
        out_shape=jax.ShapeDtypeStruct((devices, pairs_here, zrows, GY), jnp.bfloat16),
        compiler_params=pltpu.CompilerParams(vmem_limit_bytes=VMEM_BYTES),
        name="correlate",
    )(pairs, place, spread, *(jnp.asarray(t) for t in tables))


def synthesise_kernel(in_ref, wx_ref, wy_ref, out_ref):
    rows = ZHALF * GX
    lane0 = lax.broadcasted_iota(jnp.int32, (ZTILE, HALF), 1) == 0

    def at(j):
        return in_ref[j, 0, :, 0:HALF].astype(jnp.float32), in_ref[j, 0, :, HALF:].astype(jnp.float32)

    blocks = [None] * GX
    for j in (0, GX // 2):
        blocks[j] = at(j)
    for j in range(1, GX // 2):
        re, im = at(j)
        re_m, im_m = at(GX - j)
        blocks[j] = (jnp.where(lane0, re + im_m, re), jnp.where(lane0, im + re_m, im))
        blocks[GX - j] = (jnp.where(lane0, re - im_m, re_m), jnp.where(lane0, re_m - im, im_m))
    stacked = jnp.concatenate(
        [
            jnp.concatenate(
                [
                    jnp.concatenate([b[part][half * ZHALF : (half + 1) * ZHALF] for b in blocks], axis=0)
                    for half in range(2)
                ],
                axis=1,
            )
            for part in range(2)
        ],
        axis=0,
    ).astype(jnp.bfloat16)
    v_re = dot(wx_ref[:rows, :], stacked).astype(jnp.bfloat16)
    v_im = dot(wx_ref[rows:, :], stacked).astype(jnp.bfloat16)
    for half in range(2):
        lanes = slice(half * HALF, (half + 1) * HALF)
        v = jnp.concatenate([v_re[:, lanes], v_im[:, lanes]], axis=1)
        out_ref[0, half * ZHALF : (half + 1) * ZHALF] = dot(v, wy_ref[...]).reshape(ZHALF, GX, GY)


def synthesise(returned):
    _, pairs_here, zrows, _ = returned.shape
    tables = (inverse_x_table(), half_y_inverse())
    return pl.pallas_call(
        synthesise_kernel,
        grid=(pairs_here, zrows // ZTILE),
        in_specs=[pl.BlockSpec((GX, 1, ZTILE, GY), lambda i, z: (0, i, z, 0))]
        + [pl.BlockSpec(t.shape, lambda i, z: (0, 0)) for t in tables],
        out_specs=pl.BlockSpec((1, ZTILE, GX, GY), lambda i, z: (i, z, 0, 0)),
        out_shape=jax.ShapeDtypeStruct((pairs_here, zrows, GX, GY), jnp.float32),
        compiler_params=pltpu.CompilerParams(vmem_limit_bytes=VMEM_BYTES),
        name="synthesise",
    )(returned, *(jnp.asarray(t) for t in tables))


def shards(band, pairs, extents):
    tiles, slabs = lax.axis_size("tile"), lax.axis_size("zslab")
    zrows = band.shape[2]
    if tiles * slabs != GX or zrows % ZTILE or pairs.shape[0] % (2 * tiles):
        return general_shards(band, pairs, extents)
    pairs, extents = pairs.T, extents.T
    tile = lax.axis_index("tile").astype(jnp.int32)
    device = lax.axis_index("zslab").astype(jnp.int32) * tiles + tile
    spectra = analyse(band, pairs, extents, tile[None])
    spread = lax.all_to_all(spectra, ("zslab", "tile"), split_axis=0, concat_axis=0, tiled=True)
    w = correlate(spread, pairs, device[None], slabs, band.shape[0])
    returned = lax.all_to_all(w, ("zslab", "tile"), split_axis=0, concat_axis=0, tiled=True)
    return synthesise(returned)


def solution(mesh):
    placed = (P("tile", None, "zslab", None, None), P(), P())
    return jax.shard_map(
        shards,
        mesh=mesh,
        in_specs=placed,
        out_specs=P("tile", "zslab", None, None),
        check_vma=False,
    )
```

```python
import functools
import math


import jax
import jax.numpy as jnp
import numpy as np
from jax import lax
from jax.experimental import pallas as pl
from jax.experimental.pallas import tpu as pltpu
from jax.sharding import PartitionSpec as P

GX = 32
GY = 256
GZ = 128
FACES = 4


def dft_tables(length):
    indices = jnp.arange(length, dtype=jnp.int32)
    modular = indices[:, None] * indices[None, :] % length
    angles = modular.astype(jnp.float32) * (2.0 * math.pi / length)
    factor = 1.0 / math.sqrt(length)
    return (
        (jnp.cos(angles) * factor).astype(jnp.bfloat16),
        (jnp.sin(angles) * factor).astype(jnp.bfloat16),
    )


def product(form, left, right):
    return jnp.einsum(form, left, right, preferred_element_type=jnp.float32)


def reduce_resolution(image_volume, crop_bounds):
    row_mask = (
        jnp.arange(image_volume.shape[2], dtype=jnp.int32)[None, :] < crop_bounds[:, 0:1]
    ).astype(jnp.bfloat16)
    col_mask = (
        jnp.arange(image_volume.shape[3], dtype=jnp.int32)[None, :] < crop_bounds[:, 1:2]
    ).astype(jnp.bfloat16)
    masked = image_volume * row_mask[:, None, :, None] * col_mask[:, None, None, :]
    raw_cols = jnp.arange(image_volume.shape[3], dtype=jnp.int32)
    pooled_cols = jnp.arange(GY, dtype=jnp.int32)
    pooling = jnp.where(raw_cols[:, None] // 2 == pooled_cols[None, :], 0.5, 0.0).astype(
        jnp.bfloat16
    )
    along_pooled = product("szxy,yk->szxk", masked, pooling)
    shaped = along_pooled.reshape(image_volume.shape[0], image_volume.shape[1], GX, 2, GY)
    return (shaped[:, :, :, 0, :] + shaped[:, :, :, 1, :]).astype(jnp.bfloat16)


def cross_phase(owner_re, owner_im, pairs, tiles_here):
    first_dev = pairs[:, 0] // tiles_here
    first_pos = pairs[:, 0] % tiles_here * FACES + pairs[:, 1]
    second_tile_device = pairs[:, 2] // tiles_here
    second_pos = pairs[:, 2] % tiles_here * FACES + pairs[:, 3]
    first_re = owner_re[first_dev, :, first_pos].astype(jnp.float32)
    first_im = owner_im[first_dev, :, first_pos].astype(jnp.float32)
    second_re = owner_re[second_tile_device, :, second_pos].astype(jnp.float32)
    second_im = owner_im[second_tile_device, :, second_pos].astype(jnp.float32)
    cross_re = first_re * second_re + first_im * second_im
    cross_im = first_im * second_re - first_re * second_im
    scaled = jnp.sqrt(cross_re * cross_re + cross_im * cross_im + 1.0)
    return ((cross_re / scaled).astype(jnp.bfloat16), (cross_im / scaled).astype(jnp.bfloat16))


def inverse_z(phase_real_part, phase_im, tables_z):
    w_re = (
        product("pmjk,mz->pzjk", phase_real_part, tables_z[0])
        - product("pmjk,mz->pzjk", phase_im, tables_z[1])
    ).astype(jnp.bfloat16)
    w_im = (
        product("pmjk,mz->pzjk", phase_im, tables_z[0])
        + product("pmjk,mz->pzjk", phase_real_part, tables_z[1])
    ).astype(jnp.bfloat16)
    return (w_re, w_im)


def inverse_x(w_re, w_im, tables_x):
    v_re = (
        product("pzjk,jx->pzxk", w_re, tables_x[0]) - product("pzjk,jx->pzxk", w_im, tables_x[1])
    ).astype(jnp.bfloat16)
    v_im = (
        product("pzjk,jx->pzxk", w_im, tables_x[0]) + product("pzjk,jx->pzxk", w_re, tables_x[1])
    ).astype(jnp.bfloat16)
    return (v_re, v_im)


def general_shards(band, pairs, extents):
    tables_x = dft_tables(GX)
    tables_y = dft_tables(GY)
    tables_z = dft_tables(GZ)
    tiles_here = band.shape[0]
    slots = tiles_here * FACES
    zrows = band.shape[2]
    tile_pos = lax.axis_index("tile")
    global_slot = tile_pos * slots + jnp.arange(slots, dtype=jnp.int32)
    first_slot = pairs[:, 0] * FACES + pairs[:, 1]
    second_slot = pairs[:, 2] * FACES + pairs[:, 3]
    matches = (
        (first_slot[None, :] == global_slot[:, None])
        | (second_slot[None, :] == global_slot[:, None])
    ).astype(jnp.int32)
    crop_bounds = jnp.sum(matches[:, :, None] * extents[None, :, :], axis=1)
    image_volume = band.reshape(slots, zrows, 2 * GX, 2 * GY)
    reduced_volume = reduce_resolution(image_volume, crop_bounds)
    y_re = product("szxy,yk->szxk", reduced_volume, tables_y[0]).astype(jnp.bfloat16)
    y_im = (-product("szxy,yk->szxk", reduced_volume, tables_y[1])).astype(jnp.bfloat16)
    x_re = (
        product("szxk,xj->szjk", y_re, tables_x[0]) + product("szxk,xj->szjk", y_im, tables_x[1])
    ).astype(jnp.bfloat16)
    x_im = (
        product("szxk,xj->szjk", y_im, tables_x[0]) - product("szxk,xj->szjk", y_re, tables_x[1])
    ).astype(jnp.bfloat16)
    kx_part = GX // lax.axis_size("zslab")
    re_in = lax.all_to_all(x_re, "zslab", split_axis=2, concat_axis=1, tiled=True)
    im_in = lax.all_to_all(x_im, "zslab", split_axis=2, concat_axis=1, tiled=True)
    out_re = (
        product("szjk,zm->msjk", re_in, tables_z[0]) + product("szjk,zm->msjk", im_in, tables_z[1])
    ).astype(jnp.bfloat16)
    out_im = (
        product("szjk,zm->msjk", im_in, tables_z[0]) - product("szjk,zm->msjk", re_in, tables_z[1])
    ).astype(jnp.bfloat16)
    tile_count = lax.axis_size("tile")
    kz_part = GZ // tile_count
    spectra = (
        lax.all_to_all(out_re, "tile", split_axis=0, concat_axis=0, tiled=True),
        lax.all_to_all(out_im, "tile", split_axis=0, concat_axis=0, tiled=True),
    )
    owner_re = spectra[0].reshape(tile_count, kz_part, slots, kx_part, GY)
    owner_im = spectra[1].reshape(tile_count, kz_part, slots, kx_part, GY)
    phase_real_part, phase_im = cross_phase(owner_re, owner_im, pairs, tiles_here)
    returned = (
        lax.all_to_all(phase_real_part, "tile", split_axis=0, concat_axis=1, tiled=True),
        lax.all_to_all(phase_im, "tile", split_axis=0, concat_axis=1, tiled=True),
    )
    w_re, w_im = inverse_z(returned[0], returned[1], tables_z)
    v_re, v_im = inverse_x(
        lax.all_to_all(w_re, "zslab", split_axis=1, concat_axis=2, tiled=True),
        lax.all_to_all(w_im, "zslab", split_axis=1, concat_axis=2, tiled=True),
        tables_x,
    )
    return product("pzxk,ky->pzxy", v_re, tables_y[0]) - product("pzxk,ky->pzxy", v_im, tables_y[1])


HALF = GY // 2
ZTILE = 16
ZHALF = ZTILE // 2
VMEM_BYTES = 32 * 1024 * 1024


def host_tables(length):
    indices = np.arange(length, dtype=np.int32)
    modular = indices[:, None] * indices[None, :] % length
    angles = modular.astype(np.float32) * np.float32(2.0 * math.pi / length)
    factor = np.float32(1.0 / math.sqrt(length))
    return (
        (np.cos(angles) * factor).astype(jnp.bfloat16),
        (np.sin(angles) * factor).astype(jnp.bfloat16),
    )


def pooling_table():
    raw = np.arange(2 * GY)[:, None] // 2
    return np.where(raw == np.arange(GY)[None, :], 0.5, 0.0).astype(jnp.bfloat16)


def half_y_table():
    cosine, sine = host_tables(GY)
    imag = -sine[:, :HALF]
    imag[:, 0] = cosine[:, HALF]
    return np.concatenate([cosine[:, :HALF], imag], axis=1)


def half_y_inverse():
    cosine, sine = host_tables(GY)
    two = np.array(2.0, jnp.bfloat16)
    real = cosine[:HALF, :] * two
    real[0] = cosine[0]
    imag = -sine[:HALF, :] * two
    imag[0] = cosine[HALF]
    return np.concatenate([real, imag], axis=0)


def spread_x(table):
    planes = np.eye(ZHALF, dtype=np.float32)
    grid = np.einsum("jx,az->jazx", table.astype(np.float32), planes)
    return grid.reshape(GX * ZHALF, ZHALF * GX).astype(jnp.bfloat16)


def mirror_order():
    order = [0, GX // 2]
    for j in range(1, GX // 2):
        order += [j, GX - j]
    return order


def forward_x_table():
    cosine, sine = (spread_x(table) for table in host_tables(GX))
    real = np.concatenate([cosine, sine], axis=1).reshape(GX, ZHALF, -1)
    imag = np.concatenate([-sine, cosine], axis=1).reshape(GX, ZHALF, -1)
    rows = np.stack([real, imag], axis=1)[mirror_order()]
    return rows.reshape(2 * GX * ZHALF, -1)


def inverse_x_table():
    cosine, sine = (spread_x(table) for table in host_tables(GX))
    return np.ascontiguousarray(np.block([[cosine, sine], [-sine, cosine]]).T)


def forward_z_table():
    cosine, sine = host_tables(GZ)
    return np.block([[cosine, sine], [-sine, cosine]])


def inverse_z_table():
    cosine, sine = host_tables(GZ)
    return np.block([[cosine, -sine], [sine, cosine]])


def dot(left, right):
    return jnp.dot(left, right, preferred_element_type=jnp.float32)


def analyse_kernel(
    slots, pairs_ref, extents_ref, place_ref, band_ref, pool_ref, wy_ref, wx_ref, *rest
):
    out_refs, pooled_ref = rest[:-1], rest[-1]
    per_part = GX // len(out_refs)
    slot = place_ref[0] * slots + pl.program_id(0)
    across, along = jnp.int32(0), jnp.int32(0)
    for p in range(pairs_ref.shape[1]):
        first = pairs_ref[0, p] * FACES + pairs_ref[1, p]
        second = pairs_ref[2, p] * FACES + pairs_ref[3, p]
        named = (first == slot) | (second == slot)
        across = jnp.where(named, extents_ref[0, p], across)
        along = jnp.where(named, extents_ref[1, p], along)
    raw_col = lax.broadcasted_iota(jnp.int32, (2 * GY, GY), 0)
    pool = jnp.where(raw_col < along, pool_ref[...].astype(jnp.float32), 0.0).astype(jnp.bfloat16)
    rows = ZHALF * GX
    cell = lax.broadcasted_iota(jnp.int32, (ZHALF, GX, 128), 1)
    even_live = 2 * cell < across
    odd_live = 2 * cell + 1 < across
    lane0 = lax.broadcasted_iota(jnp.int32, (ZTILE, HALF), 1) == 0

    def along_y(unit):
        raw = band_ref[0, 0, unit * ZHALF : (unit + 1) * ZHALF].reshape(2 * rows, 2 * GY)
        pooled = dot(raw, pool)
        cells = []
        for lane in range(GY // 128):
            part_ref = pooled_ref.at[unit, lane]
            part_ref[...] = pooled[:, lane * 128 : (lane + 1) * 128]
            even = part_ref[pl.ds(0, rows, stride=2), :].reshape(ZHALF, GX, 128)
            odd = part_ref[pl.ds(1, rows, stride=2), :].reshape(ZHALF, GX, 128)
            both = jnp.where(even_live, even, 0.0) + jnp.where(odd_live, odd, 0.0)
            cells.append(both.reshape(rows, 128).astype(jnp.bfloat16))
        return dot(jnp.concatenate(cells, axis=1), wy_ref[...]).astype(jnp.bfloat16)

    for part in range(band_ref.shape[2] // ZTILE):
        units = [along_y(2 * part), along_y(2 * part + 1)]
        stacked = jnp.concatenate(
            [
                jnp.concatenate([y[:, :HALF] for y in units], axis=1),
                jnp.concatenate([y[:, HALF:] for y in units], axis=1),
            ],
            axis=0,
        )
        spectra = dot(wx_ref[...], stacked)
        zs = slice(part * ZTILE, (part + 1) * ZTILE)

        def at(n):
            blocks = [spectra[m * ZHALF : (m + 1) * ZHALF] for m in (2 * n, 2 * n + 1)]
            return [jnp.concatenate([b[:, :HALF], b[:, HALF:]], axis=0) for b in blocks]

        def put(j, re, im):
            out_ref = out_refs[j // per_part]
            out_ref[j % per_part, 0, zs, 0:HALF] = re.astype(jnp.bfloat16)
            out_ref[j % per_part, 0, zs, HALF:] = im.astype(jnp.bfloat16)

        put(0, *at(0))
        put(GX // 2, *at(1))
        for j in range(1, GX // 2):
            re, im = at(2 * j)
            re_m, im_m = at(2 * j + 1)
            put(j, jnp.where(lane0, 0.5 * (re + re_m), re), jnp.where(lane0, 0.5 * (im - im_m), im))
            put(
                GX - j,
                jnp.where(lane0, 0.5 * (im + im_m), re_m),
                jnp.where(lane0, 0.5 * (re - re_m), im_m),
            )


def analyse(band, pairs, extents, place, chunks):
    slots, zrows = band.shape[0] * FACES, band.shape[2]
    tables = (pooling_table(), half_y_table(), forward_x_table())
    whole = [pl.BlockSpec(t.shape, lambda i, *_: (0, 0)) for t in tables]
    return pl.pallas_call(
        functools.partial(analyse_kernel, slots),
        grid_spec=pltpu.PrefetchScalarGridSpec(
            num_scalar_prefetch=3,
            grid=(slots,),
            in_specs=[
                pl.BlockSpec(
                    (1, 1, zrows, 2 * GX, 2 * GY), lambda i, *_: (i // FACES, i % FACES, 0, 0, 0)
                )
            ]
            + whole,
            out_specs=[pl.BlockSpec((GX // chunks, 1, zrows, GY), lambda i, *_: (0, i, 0, 0))] * chunks,
            scratch_shapes=[
                pltpu.VMEM((zrows // ZHALF, GY // 128, 2 * ZHALF * GX, 128), jnp.float32)
            ],
        ),
        out_shape=[jax.ShapeDtypeStruct((GX // chunks, slots, zrows, GY), jnp.bfloat16)] * chunks,
        compiler_params=pltpu.CompilerParams(vmem_limit_bytes=VMEM_BYTES + VMEM_BYTES * 3 // 4),
        name="analyse",
    )(pairs, extents, place, band, *(jnp.asarray(t) for t in tables))


def normalised(a_re, a_im, b_re, b_im):
    cross_re = a_re * b_re + a_im * b_im
    cross_im = a_im * b_re - a_re * b_im
    scale = lax.rsqrt(cross_re * cross_re + cross_im * cross_im + 1.0)
    return (cross_re * scale).astype(jnp.bfloat16), (cross_im * scale).astype(jnp.bfloat16)


def joined(wz_ref, wzi_ref, keep, ends):
    phases = []
    for first, second in ends:
        re = jnp.concatenate([first[:, :HALF], second[:, :HALF]], axis=1)
        im = jnp.concatenate([first[:, HALF:] * keep, second[:, HALF:] * keep], axis=1)
        phases.append(phase_of(wz_ref, re, im))
    stacked = jnp.concatenate(
        [jnp.concatenate([phase[part] for phase in phases], axis=1) for part in (0, 1)], axis=0
    )
    w = dot(wzi_ref[...], stacked).astype(jnp.bfloat16)
    return [
        jnp.concatenate([w[:GZ, k * HALF : (k + 1) * HALF], w[GZ:, k * HALF : (k + 1) * HALF]], axis=1)
        for k in range(len(ends))
    ]


def phase_of(wz_ref, re, im):
    spec = dot(wz_ref[...], jnp.concatenate([re, im], axis=0))
    spec = spec.astype(jnp.bfloat16).astype(jnp.float32)
    return normalised(spec[:GZ, :HALF], spec[GZ:, :HALF], spec[:GZ, HALF:], spec[GZ:, HALF:])


def last_columns(wz_ref, wzi_ref, ends):
    lane = lax.broadcasted_iota(jnp.int32, (GZ, HALF), 1)
    first = jnp.zeros((GZ, HALF), jnp.float32)
    second = jnp.zeros((GZ, HALF), jnp.float32)
    for k, (a, b) in enumerate(ends):
        first = jnp.where(lane == k, a[:, HALF:].astype(jnp.float32)[:, 0:1], first)
        second = jnp.where(lane == k, b[:, HALF:].astype(jnp.float32)[:, 0:1], second)
    re = jnp.concatenate([first, second], axis=1).astype(jnp.bfloat16)
    phase = phase_of(wz_ref, re, jnp.zeros_like(re))
    return dot(wzi_ref[...], jnp.concatenate(phase, axis=0))[:GZ]


def with_lane0(w, column):
    imag = w[:, HALF:].astype(jnp.float32)
    lane0 = lax.broadcasted_iota(jnp.int32, imag.shape, 1) == 0
    imag = jnp.where(lane0, column, imag).astype(jnp.bfloat16)
    return jnp.concatenate([w[:, :HALF], imag], axis=1)


class Ends:
    def __init__(self, pairs_ref, p, half, quads, tiles_here):
        self.mine, self.row, self.pos = [], [], []
        for end in (0, 1):
            tile = pairs_ref[2 * end, p]
            device = tile // tiles_here
            self.mine.append(device // quads == half)
            self.row.append(device % quads)
            self.pos.append(tile % tiles_here * FACES + pairs_ref[2 * end + 1, p])


def slot_of(in_ref, row, pos, slabs):
    return jnp.concatenate([in_ref[row * slabs + s, pos] for s in range(slabs)], axis=0)


def keep_lanes(place_ref):
    lane0 = lax.broadcasted_iota(jnp.int32, (GZ, HALF), 1) == 0
    return jnp.where(lane0 & (place_ref[2] == 0), 0.0, 1.0).astype(jnp.bfloat16)


def offer_kernel(slabs, tiles_here, pairs_ref, place_ref, in_ref, wz_ref, wzi_ref, out_ref):
    half = place_ref[1]
    quads = in_ref.shape[0] // slabs
    keep = keep_lanes(place_ref)
    count = out_ref.shape[0]
    ends = [
        Ends(pairs_ref, (1 - half) * count + i, half, quads, tiles_here) for i in range(count)
    ]
    for i, at in enumerate(ends):
        row = jnp.where(at.mine[0], at.row[0], at.row[1])
        pos = jnp.where(at.mine[0], at.pos[0], at.pos[1])
        out_ref[i] = slot_of(in_ref, row, pos, slabs)

    def load(at):
        return [slot_of(in_ref, at.row[end], at.pos[end], slabs) for end in (0, 1)]

    for i, at in enumerate(ends):

        @pl.when(at.mine[0] & at.mine[1])
        def _():
            out_ref[i] = joined(wz_ref, wzi_ref, keep, [load(at)])[0]

    @pl.when(place_ref[2] == 0)
    def _():
        columns = last_columns(wz_ref, wzi_ref, [load(at) for at in ends])
        for i, at in enumerate(ends):

            @pl.when(at.mine[0] & at.mine[1])
            def _():
                out_ref[i] = with_lane0(out_ref[i], columns[:, i : i + 1])


def join_kernel(
    slabs, tiles_here, pairs_ref, place_ref, in_ref, item_ref, wz_ref, wzi_ref, out_ref, *ends_refs
):
    half = place_ref[1]
    quads = in_ref.shape[0] // slabs
    pairs_here = out_ref.shape[1]
    zrows = out_ref.shape[2]
    keep = keep_lanes(place_ref)
    count = item_ref.shape[0]
    ends = [Ends(pairs_ref, half * count + i, half, quads, tiles_here) for i in range(count)]
    for i, at in enumerate(ends):
        for end in (0, 1):

            @pl.when(at.mine[end])
            def _():
                ends_refs[end][i] = slot_of(in_ref, at.row[end], at.pos[end], slabs)

            @pl.when(jnp.logical_not(at.mine[end]))
            def _():
                ends_refs[end][i] = item_ref[i]

    def load(i):
        return [ends_refs[end][i] for end in (0, 1)]

    def put(i, w):
        for s in range(slabs):
            out_ref[i // pairs_here * slabs + s, i % pairs_here] = w[s * zrows : (s + 1) * zrows]

    for i in range(0, count, 2):
        for k, w in enumerate(joined(wz_ref, wzi_ref, keep, [load(i), load(i + 1)])):
            put(i + k, w)

    @pl.when(place_ref[2] == 0)
    def _():
        columns = last_columns(wz_ref, wzi_ref, [load(i) for i in range(count)])
        for i in range(count):
            w = slot_of(out_ref, i // pairs_here, i % pairs_here, slabs)
            put(i, with_lane0(w, columns[:, i : i + 1]))

    for i, at in enumerate(ends):

        @pl.when(jnp.logical_not(at.mine[0] | at.mine[1]))
        def _():
            put(i, item_ref[i])


def correlate(kernel, arrays, pairs, place, slabs, tiles_here, shape, scratch):
    tables = (forward_z_table(), inverse_z_table())
    vmem = pl.BlockSpec(memory_space=pltpu.VMEM)
    smem = pl.BlockSpec(memory_space=pltpu.SMEM)
    return pl.pallas_call(
        functools.partial(kernel, slabs, tiles_here),
        in_specs=[smem, smem] + [vmem] * (len(arrays) + len(tables)),
        out_specs=vmem,
        out_shape=jax.ShapeDtypeStruct(shape, jnp.bfloat16),
        scratch_shapes=scratch,
        compiler_params=pltpu.CompilerParams(vmem_limit_bytes=VMEM_BYTES),
        name=kernel.__name__,
    )(pairs, place, *arrays, *(jnp.asarray(t) for t in tables))


def offer(spread, pairs, place, slabs, tiles_here):
    count = pairs.shape[1] // 2
    return correlate(
        offer_kernel, (spread,), pairs, place, slabs, tiles_here, (count, GZ, GY), ()
    )


def join(spread, items, pairs, place, slabs, tiles_here):
    devices, _, zrows, _ = spread.shape
    count = items.shape[0]
    return correlate(
        join_kernel,
        (spread, items),
        pairs,
        place,
        slabs,
        tiles_here,
        (devices, count * slabs // devices, zrows, GY),
        [pltpu.VMEM((count, GZ, GY), jnp.bfloat16)] * 2,
    )


def synthesise_kernel(wx_ref, wy_ref, *rest):
    in_refs, out_ref = rest[:-1], rest[-1]
    per_part = GX // len(in_refs)
    rows = ZHALF * GX
    lane0 = lax.broadcasted_iota(jnp.int32, (ZTILE, HALF), 1) == 0

    def at(j):
        both = in_refs[j // per_part][j % per_part, 0].astype(jnp.float32)
        return both[:, :HALF], both[:, HALF:]

    blocks = [None] * GX
    for j in (0, GX // 2):
        blocks[j] = at(j)
    for j in range(1, GX // 2):
        re, im = at(j)
        re_m, im_m = at(GX - j)
        blocks[j] = (jnp.where(lane0, re + im_m, re), jnp.where(lane0, im + re_m, im))
        blocks[GX - j] = (jnp.where(lane0, re - im_m, re_m), jnp.where(lane0, re_m - im, im_m))
    stacked = jnp.concatenate(
        [
            jnp.concatenate(
                [
                    jnp.concatenate([b[part][half * ZHALF : (half + 1) * ZHALF] for b in blocks], axis=0)
                    for half in range(2)
                ],
                axis=1,
            )
            for part in range(2)
        ],
        axis=0,
    ).astype(jnp.bfloat16)
    v_re = dot(wx_ref[:rows, :], stacked).astype(jnp.bfloat16)
    v_im = dot(wx_ref[rows:, :], stacked).astype(jnp.bfloat16)
    for half in range(2):
        lanes = slice(half * HALF, (half + 1) * HALF)
        v = jnp.concatenate([v_re[:, lanes], v_im[:, lanes]], axis=1)
        out_ref[0, half * ZHALF : (half + 1) * ZHALF] = dot(v, wy_ref[...]).reshape(ZHALF, GX, GY)


def synthesise(returned):
    per_part, pairs_here, zrows, _ = returned[0].shape
    tables = (inverse_x_table(), half_y_inverse())
    return pl.pallas_call(
        synthesise_kernel,
        grid=(pairs_here, zrows // ZTILE),
        in_specs=[pl.BlockSpec(t.shape, lambda i, z: (0, 0)) for t in tables]
        + [pl.BlockSpec((per_part, 1, ZTILE, GY), lambda i, z: (0, i, z, 0))] * len(returned),
        out_specs=pl.BlockSpec((1, ZTILE, GX, GY), lambda i, z: (i, z, 0, 0)),
        out_shape=jax.ShapeDtypeStruct((pairs_here, zrows, GX, GY), jnp.float32),
        compiler_params=pltpu.CompilerParams(vmem_limit_bytes=VMEM_BYTES),
        name="synthesise",
    )(*(jnp.asarray(t) for t in tables), *returned)


def halves_shards(band, pairs, extents):
    quads, slabs = lax.axis_size("quad"), lax.axis_size("zslab")
    tiles_here = band.shape[0]
    pairs, extents = pairs.T, extents.T
    half, quad = lax.axis_index("half"), lax.axis_index("quad")
    place = jnp.stack(
        [half * quads + quad, half, quad * slabs + lax.axis_index("zslab")]
    ).astype(jnp.int32)

    def spread_in_half(blocks):
        return lax.all_to_all(blocks, ("quad", "zslab"), split_axis=0, concat_axis=0, tiled=True)

    returned = []
    for spectra in analyse(band, pairs, extents, place, GX // (quads * slabs)):
        spread = spread_in_half(spectra)
        items = offer(spread, pairs, place, slabs, tiles_here)
        items = lax.ppermute(items, "half", [(0, 1), (1, 0)])
        returned.append(spread_in_half(join(spread, items, pairs, place, slabs, tiles_here)))
    return synthesise(returned)


def solution(mesh):
    tiles, slabs = mesh.devices.shape
    per_half = tiles // 2 * slabs
    if tiles % 2 == 0 and GX % per_half == 0 and GZ // slabs % ZTILE == 0:
        halves = jax.sharding.Mesh(
            mesh.devices.reshape(2, tiles // 2, slabs), ("half", "quad", "zslab")
        )
        tile, body, over = ("half", "quad"), halves_shards, halves
    else:
        tile, body, over = "tile", general_shards, mesh
    return jax.shard_map(
        body,
        mesh=over,
        in_specs=(P(tile, None, "zslab", None, None), P(), P()),
        out_specs=P(tile, "zslab", None, None),
        check_vma=False,
    )
```

```python
import functools
import math


import jax
import jax.numpy as jnp
import numpy as np
from jax import lax
from jax.experimental import pallas as pl
from jax.experimental.pallas import tpu as pltpu
from jax.sharding import PartitionSpec as P

GX = 32
GY = 256
GZ = 128
FACES = 4


def dft_tables(length):
    indices = jnp.arange(length, dtype=jnp.int32)
    modular = indices[:, None] * indices[None, :] % length
    angles = modular.astype(jnp.float32) * (2.0 * math.pi / length)
    factor = 1.0 / math.sqrt(length)
    return (
        (jnp.cos(angles) * factor).astype(jnp.bfloat16),
        (jnp.sin(angles) * factor).astype(jnp.bfloat16),
    )


def product(form, left, right):
    return jnp.einsum(form, left, right, preferred_element_type=jnp.float32)


def reduce_resolution(image_volume, crop_bounds):
    row_mask = (
        jnp.arange(image_volume.shape[2], dtype=jnp.int32)[None, :] < crop_bounds[:, 0:1]
    ).astype(jnp.bfloat16)
    col_mask = (
        jnp.arange(image_volume.shape[3], dtype=jnp.int32)[None, :] < crop_bounds[:, 1:2]
    ).astype(jnp.bfloat16)
    masked = image_volume * row_mask[:, None, :, None] * col_mask[:, None, None, :]
    raw_cols = jnp.arange(image_volume.shape[3], dtype=jnp.int32)
    pooled_cols = jnp.arange(GY, dtype=jnp.int32)
    pooling = jnp.where(raw_cols[:, None] // 2 == pooled_cols[None, :], 0.5, 0.0).astype(
        jnp.bfloat16
    )
    along_pooled = product("szxy,yk->szxk", masked, pooling)
    shaped = along_pooled.reshape(image_volume.shape[0], image_volume.shape[1], GX, 2, GY)
    return (shaped[:, :, :, 0, :] + shaped[:, :, :, 1, :]).astype(jnp.bfloat16)


def cross_phase(owner_re, owner_im, pairs, tiles_here):
    first_dev = pairs[:, 0] // tiles_here
    first_pos = pairs[:, 0] % tiles_here * FACES + pairs[:, 1]
    second_tile_device = pairs[:, 2] // tiles_here
    second_pos = pairs[:, 2] % tiles_here * FACES + pairs[:, 3]
    first_re = owner_re[first_dev, :, first_pos].astype(jnp.float32)
    first_im = owner_im[first_dev, :, first_pos].astype(jnp.float32)
    second_re = owner_re[second_tile_device, :, second_pos].astype(jnp.float32)
    second_im = owner_im[second_tile_device, :, second_pos].astype(jnp.float32)
    cross_re = first_re * second_re + first_im * second_im
    cross_im = first_im * second_re - first_re * second_im
    scaled = jnp.sqrt(cross_re * cross_re + cross_im * cross_im + 1.0)
    return ((cross_re / scaled).astype(jnp.bfloat16), (cross_im / scaled).astype(jnp.bfloat16))


def inverse_z(phase_real_part, phase_im, tables_z):
    w_re = (
        product("pmjk,mz->pzjk", phase_real_part, tables_z[0])
        - product("pmjk,mz->pzjk", phase_im, tables_z[1])
    ).astype(jnp.bfloat16)
    w_im = (
        product("pmjk,mz->pzjk", phase_im, tables_z[0])
        + product("pmjk,mz->pzjk", phase_real_part, tables_z[1])
    ).astype(jnp.bfloat16)
    return (w_re, w_im)


def inverse_x(w_re, w_im, tables_x):
    v_re = (
        product("pzjk,jx->pzxk", w_re, tables_x[0]) - product("pzjk,jx->pzxk", w_im, tables_x[1])
    ).astype(jnp.bfloat16)
    v_im = (
        product("pzjk,jx->pzxk", w_im, tables_x[0]) + product("pzjk,jx->pzxk", w_re, tables_x[1])
    ).astype(jnp.bfloat16)
    return (v_re, v_im)


def general_shards(band, pairs, extents):
    tables_x = dft_tables(GX)
    tables_y = dft_tables(GY)
    tables_z = dft_tables(GZ)
    tiles_here = band.shape[0]
    slots = tiles_here * FACES
    zrows = band.shape[2]
    tile_pos = lax.axis_index("tile")
    global_slot = tile_pos * slots + jnp.arange(slots, dtype=jnp.int32)
    first_slot = pairs[:, 0] * FACES + pairs[:, 1]
    second_slot = pairs[:, 2] * FACES + pairs[:, 3]
    matches = (
        (first_slot[None, :] == global_slot[:, None])
        | (second_slot[None, :] == global_slot[:, None])
    ).astype(jnp.int32)
    crop_bounds = jnp.sum(matches[:, :, None] * extents[None, :, :], axis=1)
    image_volume = band.reshape(slots, zrows, 2 * GX, 2 * GY)
    reduced_volume = reduce_resolution(image_volume, crop_bounds)
    y_re = product("szxy,yk->szxk", reduced_volume, tables_y[0]).astype(jnp.bfloat16)
    y_im = (-product("szxy,yk->szxk", reduced_volume, tables_y[1])).astype(jnp.bfloat16)
    x_re = (
        product("szxk,xj->szjk", y_re, tables_x[0]) + product("szxk,xj->szjk", y_im, tables_x[1])
    ).astype(jnp.bfloat16)
    x_im = (
        product("szxk,xj->szjk", y_im, tables_x[0]) - product("szxk,xj->szjk", y_re, tables_x[1])
    ).astype(jnp.bfloat16)
    kx_part = GX // lax.axis_size("zslab")
    re_in = lax.all_to_all(x_re, "zslab", split_axis=2, concat_axis=1, tiled=True)
    im_in = lax.all_to_all(x_im, "zslab", split_axis=2, concat_axis=1, tiled=True)
    out_re = (
        product("szjk,zm->msjk", re_in, tables_z[0]) + product("szjk,zm->msjk", im_in, tables_z[1])
    ).astype(jnp.bfloat16)
    out_im = (
        product("szjk,zm->msjk", im_in, tables_z[0]) - product("szjk,zm->msjk", re_in, tables_z[1])
    ).astype(jnp.bfloat16)
    tile_count = lax.axis_size("tile")
    kz_part = GZ // tile_count
    spectra = (
        lax.all_to_all(out_re, "tile", split_axis=0, concat_axis=0, tiled=True),
        lax.all_to_all(out_im, "tile", split_axis=0, concat_axis=0, tiled=True),
    )
    owner_re = spectra[0].reshape(tile_count, kz_part, slots, kx_part, GY)
    owner_im = spectra[1].reshape(tile_count, kz_part, slots, kx_part, GY)
    phase_real_part, phase_im = cross_phase(owner_re, owner_im, pairs, tiles_here)
    returned = (
        lax.all_to_all(phase_real_part, "tile", split_axis=0, concat_axis=1, tiled=True),
        lax.all_to_all(phase_im, "tile", split_axis=0, concat_axis=1, tiled=True),
    )
    w_re, w_im = inverse_z(returned[0], returned[1], tables_z)
    v_re, v_im = inverse_x(
        lax.all_to_all(w_re, "zslab", split_axis=1, concat_axis=2, tiled=True),
        lax.all_to_all(w_im, "zslab", split_axis=1, concat_axis=2, tiled=True),
        tables_x,
    )
    return product("pzxk,ky->pzxy", v_re, tables_y[0]) - product("pzxk,ky->pzxy", v_im, tables_y[1])


HALF = GY // 2
ZTILE = 16
ZHALF = ZTILE // 2
VMEM_BYTES = 32 * 1024 * 1024


def host_tables(length):
    indices = np.arange(length, dtype=np.int32)
    modular = indices[:, None] * indices[None, :] % length
    angles = modular.astype(np.float32) * np.float32(2.0 * math.pi / length)
    factor = np.float32(1.0 / math.sqrt(length))
    return (
        (np.cos(angles) * factor).astype(jnp.bfloat16),
        (np.sin(angles) * factor).astype(jnp.bfloat16),
    )


def half_y_table():
    cosine, sine = host_tables(GY)
    imag = -sine[:, :HALF]
    imag[:, 0] = cosine[:, HALF]
    return np.concatenate([cosine[:, :HALF], imag], axis=1)


def pooled_y_table():
    return np.repeat(half_y_table() * np.array(0.5, jnp.bfloat16), 2, axis=0)


def half_y_inverse():
    cosine, sine = host_tables(GY)
    two = np.array(2.0, jnp.bfloat16)
    real = cosine[:HALF, :] * two
    real[0] = cosine[0]
    imag = -sine[:HALF, :] * two
    imag[0] = cosine[HALF]
    return np.concatenate([real, imag], axis=0)


def spread_x(table):
    planes = np.eye(ZHALF, dtype=np.float32)
    grid = np.einsum("jx,az->jazx", table.astype(np.float32), planes)
    return grid.reshape(GX * ZHALF, ZHALF * GX).astype(jnp.bfloat16)


def mirror_order():
    order = [0, GX // 2]
    for j in range(1, GX // 2):
        order += [j, GX - j]
    return order


def forward_x_table():
    cosine, sine = (spread_x(table) for table in host_tables(GX))
    real = np.concatenate([cosine, sine], axis=1).reshape(GX, ZHALF, -1)
    imag = np.concatenate([-sine, cosine], axis=1).reshape(GX, ZHALF, -1)
    rows = np.stack([real, imag], axis=1)[mirror_order()]
    return rows.reshape(2 * GX * ZHALF, -1)


def inverse_x_table():
    cosine, sine = (spread_x(table) for table in host_tables(GX))
    return np.ascontiguousarray(np.block([[cosine, sine], [-sine, cosine]]).T)


def forward_z_table():
    cosine, sine = host_tables(GZ)
    return np.block([[cosine, sine], [-sine, cosine]])


def inverse_z_table():
    cosine, sine = host_tables(GZ)
    return np.block([[cosine, -sine], [sine, cosine]])


def dot(left, right):
    return jnp.dot(left, right, preferred_element_type=jnp.float32)


def analyse_kernel(
    slots, pairs_ref, extents_ref, tile_ref, band_ref, wy_ref, wx_ref, out_ref, pooled_ref, crop_ref
):
    slot = pl.program_id(0)

    @pl.when(slot == 0)
    def _():
        for p in range(pairs_ref.shape[1]):
            for end in (0, 1):
                named = pairs_ref[2 * end, p] * FACES + pairs_ref[2 * end + 1, p] - tile_ref[0] * slots

                @pl.when((named >= 0) & (named < slots))
                def _():
                    crop_ref[named, 0] = extents_ref[0, p]
                    crop_ref[named, 1] = extents_ref[1, p]

    across, along = crop_ref[slot, 0], crop_ref[slot, 1]
    raw_col = lax.broadcasted_iota(jnp.int32, (2 * GY, GY), 0)
    wy = jnp.where(raw_col < along, wy_ref[...].astype(jnp.float32), 0.0).astype(jnp.bfloat16)
    rows = ZHALF * GX
    cell = lax.broadcasted_iota(jnp.int32, (ZHALF, GX, 128), 1)
    even_live = 2 * cell < across
    odd_live = 2 * cell + 1 < across
    lane0 = lax.broadcasted_iota(jnp.int32, (ZTILE, HALF), 1) == 0

    def along_y(unit):
        raw = band_ref[0, 0, unit * ZHALF : (unit + 1) * ZHALF].reshape(2 * rows, 2 * GY)
        y_raw = dot(raw, wy)
        parts = []
        for lane in range(GY // 128):
            part_ref = pooled_ref.at[unit, lane]
            part_ref[...] = y_raw[:, lane * 128 : (lane + 1) * 128]
            even = part_ref[pl.ds(0, rows, stride=2), :].reshape(ZHALF, GX, 128)
            odd = part_ref[pl.ds(1, rows, stride=2), :].reshape(ZHALF, GX, 128)
            both = jnp.where(even_live, even, 0.0) + jnp.where(odd_live, odd, 0.0)
            parts.append(both.reshape(rows, 128).astype(jnp.bfloat16))
        return jnp.concatenate(parts, axis=1)

    for part in range(band_ref.shape[2] // ZTILE):
        units = [along_y(2 * part), along_y(2 * part + 1)]
        stacked = jnp.concatenate(
            [
                jnp.concatenate([y[:, :HALF] for y in units], axis=1),
                jnp.concatenate([y[:, HALF:] for y in units], axis=1),
            ],
            axis=0,
        )
        spectra = dot(wx_ref[...], stacked)
        zs = slice(part * ZTILE, (part + 1) * ZTILE)

        def at(n):
            blocks = [spectra[m * ZHALF : (m + 1) * ZHALF] for m in (2 * n, 2 * n + 1)]
            return [jnp.concatenate([b[:, :HALF], b[:, HALF:]], axis=0) for b in blocks]

        def put(j, re, im):
            out_ref[j, 0, zs, 0:HALF] = re.astype(jnp.bfloat16)
            out_ref[j, 0, zs, HALF:] = im.astype(jnp.bfloat16)

        put(0, *at(0))
        put(GX // 2, *at(1))
        for j in range(1, GX // 2):
            re, im = at(2 * j)
            re_m, im_m = at(2 * j + 1)
            put(j, jnp.where(lane0, 0.5 * (re + re_m), re), jnp.where(lane0, 0.5 * (im - im_m), im))
            put(
                GX - j,
                jnp.where(lane0, 0.5 * (im + im_m), re_m),
                jnp.where(lane0, 0.5 * (re - re_m), im_m),
            )


def analyse(band, pairs, extents, tile):
    slots, zrows = band.shape[0] * FACES, band.shape[2]
    tables = (pooled_y_table(), forward_x_table())
    whole = [pl.BlockSpec(t.shape, lambda i, *_: (0, 0)) for t in tables]
    return pl.pallas_call(
        functools.partial(analyse_kernel, slots),
        grid_spec=pltpu.PrefetchScalarGridSpec(
            num_scalar_prefetch=3,
            grid=(slots,),
            in_specs=[
                pl.BlockSpec(
                    (1, 1, zrows, 2 * GX, 2 * GY), lambda i, *_: (i // FACES, i % FACES, 0, 0, 0)
                )
            ]
            + whole,
            out_specs=pl.BlockSpec((GX, 1, zrows, GY), lambda i, *_: (0, i, 0, 0)),
            scratch_shapes=[
                pltpu.VMEM((zrows // ZHALF, GY // 128, 2 * ZHALF * GX, 128), jnp.float32),
                pltpu.SMEM((slots, 2), jnp.int32),
            ],
        ),
        out_shape=jax.ShapeDtypeStruct((GX, slots, zrows, GY), jnp.bfloat16),
        compiler_params=pltpu.CompilerParams(vmem_limit_bytes=VMEM_BYTES + VMEM_BYTES * 3 // 4),
        name="analyse",
    )(pairs, extents, tile, band, *(jnp.asarray(t) for t in tables))


def normalised(a_re, a_im, b_re, b_im):
    cross_re = a_re * b_re + a_im * b_im
    cross_im = a_im * b_re - a_re * b_im
    scale = lax.rsqrt(cross_re * cross_re + cross_im * cross_im + 1.0)
    return (cross_re * scale).astype(jnp.bfloat16), (cross_im * scale).astype(jnp.bfloat16)


def correlate_kernel(
    slabs, tiles_here, pairs_ref, place_ref, in_ref, wz_ref, wzi_ref, out_ref
):
    tiles = in_ref.shape[0] // slabs
    total = pairs_ref.shape[1]
    pairs_here = out_ref.shape[1]
    zrows = GZ // slabs
    both_real = (place_ref[0] == 0) | (place_ref[0] == GX // 2)
    lane = lax.broadcasted_iota(jnp.int32, (GZ, HALF), 1)
    lane0 = lane == 0

    def load(p, end, half):
        tile = pairs_ref[2 * end, p]
        row = tile // tiles_here
        pos = tile % tiles_here * FACES + pairs_ref[2 * end + 1, p]
        lanes = slice(half * HALF, (half + 1) * HALF)
        return jnp.concatenate([in_ref[row + s * tiles, pos, :, lanes] for s in range(slabs)], axis=0)

    def forward(re, im):
        spec = dot(wz_ref[...], jnp.concatenate([re, im], axis=0))
        return spec.astype(jnp.bfloat16).astype(jnp.float32)

    def phase_of(spec):
        return normalised(spec[:GZ, :HALF], spec[GZ:, :HALF], spec[:GZ, HALF:], spec[GZ:, HALF:])

    keep = jnp.where(lane0 & both_real, 0.0, 1.0).astype(jnp.bfloat16)
    for p in range(0, total, 2):
        phases = []
        for q in (p, p + 1):
            re = jnp.concatenate([load(q, 0, 0), load(q, 1, 0)], axis=1)
            im = jnp.concatenate([load(q, 0, 1) * keep, load(q, 1, 1) * keep], axis=1)
            phases.append(phase_of(forward(re, im)))
        stacked = jnp.concatenate(
            [
                jnp.concatenate([phases[0][0], phases[1][0]], axis=1),
                jnp.concatenate([phases[0][1], phases[1][1]], axis=1),
            ],
            axis=0,
        )
        w = dot(wzi_ref[...], stacked).astype(jnp.bfloat16)
        for k, q in enumerate((p, p + 1)):
            for half in (0, 1):
                plane = w[half * GZ : (half + 1) * GZ, k * HALF : (k + 1) * HALF]
                for s in range(slabs):
                    out_ref[
                        q // pairs_here + s * tiles,
                        q % pairs_here,
                        :,
                        half * HALF : (half + 1) * HALF,
                    ] = plane[s * zrows : (s + 1) * zrows]

    @pl.when(both_real)
    def _():
        first = jnp.zeros((GZ, HALF), jnp.float32)
        second = jnp.zeros((GZ, HALF), jnp.float32)
        for p in range(total):
            a = load(p, 0, 1).astype(jnp.float32)[:, 0:1]
            b = load(p, 1, 1).astype(jnp.float32)[:, 0:1]
            first = jnp.where(lane == p, a, first)
            second = jnp.where(lane == p, b, second)
        re = jnp.concatenate([first, second], axis=1).astype(jnp.bfloat16)
        phase = phase_of(forward(re, jnp.zeros_like(re)))
        w = dot(wzi_ref[...], jnp.concatenate(phase, axis=0))[:GZ]
        for p in range(total):
            column = w[:, p : p + 1]
            for s in range(slabs):
                at = (p // pairs_here + s * tiles, p % pairs_here, slice(None), slice(HALF, 2 * HALF))
                old = out_ref[at].astype(jnp.float32)
                rows = slice(s * zrows, (s + 1) * zrows)
                out_ref[at] = jnp.where(lane0[rows], column[rows], old).astype(jnp.bfloat16)


def correlate(spread, pairs, place, slabs, tiles_here):
    devices, _, zrows, _ = spread.shape
    pairs_here = pairs.shape[1] * slabs // devices
    tables = (forward_z_table(), inverse_z_table())
    vmem = pl.BlockSpec(memory_space=pltpu.VMEM)
    smem = pl.BlockSpec(memory_space=pltpu.SMEM)
    return pl.pallas_call(
        functools.partial(correlate_kernel, slabs, tiles_here),
        in_specs=[smem, smem, vmem, vmem, vmem],
        out_specs=vmem,
        out_shape=jax.ShapeDtypeStruct((devices, pairs_here, zrows, GY), jnp.bfloat16),
        compiler_params=pltpu.CompilerParams(vmem_limit_bytes=VMEM_BYTES),
        name="correlate",
    )(pairs, place, spread, *(jnp.asarray(t) for t in tables))


def synthesise_kernel(in_ref, wx_ref, wy_ref, out_ref):
    rows = ZHALF * GX
    lane0 = lax.broadcasted_iota(jnp.int32, (ZTILE, HALF), 1) == 0

    def at(j):
        return in_ref[j, 0, :, 0:HALF].astype(jnp.float32), in_ref[j, 0, :, HALF:].astype(jnp.float32)

    blocks = [None] * GX
    for j in (0, GX // 2):
        blocks[j] = at(j)
    for j in range(1, GX // 2):
        re, im = at(j)
        re_m, im_m = at(GX - j)
        blocks[j] = (jnp.where(lane0, re + im_m, re), jnp.where(lane0, im + re_m, im))
        blocks[GX - j] = (jnp.where(lane0, re - im_m, re_m), jnp.where(lane0, re_m - im, im_m))
    stacked = jnp.concatenate(
        [
            jnp.concatenate(
                [
                    jnp.concatenate([b[part][half * ZHALF : (half + 1) * ZHALF] for b in blocks], axis=0)
                    for half in range(2)
                ],
                axis=1,
            )
            for part in range(2)
        ],
        axis=0,
    ).astype(jnp.bfloat16)
    v_re = dot(wx_ref[:rows, :], stacked).astype(jnp.bfloat16)
    v_im = dot(wx_ref[rows:, :], stacked).astype(jnp.bfloat16)
    for half in range(2):
        lanes = slice(half * HALF, (half + 1) * HALF)
        v = jnp.concatenate([v_re[:, lanes], v_im[:, lanes]], axis=1)
        out_ref[0, half * ZHALF : (half + 1) * ZHALF] = dot(v, wy_ref[...]).reshape(ZHALF, GX, GY)


def synthesise(returned):
    _, pairs_here, zrows, _ = returned.shape
    tables = (inverse_x_table(), half_y_inverse())
    return pl.pallas_call(
        synthesise_kernel,
        grid=(pairs_here, zrows // ZTILE),
        in_specs=[pl.BlockSpec((GX, 1, ZTILE, GY), lambda i, z: (0, i, z, 0))]
        + [pl.BlockSpec(t.shape, lambda i, z: (0, 0)) for t in tables],
        out_specs=pl.BlockSpec((1, ZTILE, GX, GY), lambda i, z: (i, z, 0, 0)),
        out_shape=jax.ShapeDtypeStruct((pairs_here, zrows, GX, GY), jnp.float32),
        compiler_params=pltpu.CompilerParams(vmem_limit_bytes=VMEM_BYTES),
        name="synthesise",
    )(returned, *(jnp.asarray(t) for t in tables))


def shards(band, pairs, extents):
    tiles, slabs = lax.axis_size("tile"), lax.axis_size("zslab")
    zrows = band.shape[2]
    if tiles * slabs != GX or zrows % ZTILE or pairs.shape[0] % (2 * tiles):
        return general_shards(band, pairs, extents)
    pairs, extents = pairs.T, extents.T
    tile = lax.axis_index("tile").astype(jnp.int32)
    device = lax.axis_index("zslab").astype(jnp.int32) * tiles + tile
    spectra = analyse(band, pairs, extents, tile[None])
    spread = lax.all_to_all(spectra, ("zslab", "tile"), split_axis=0, concat_axis=0, tiled=True)
    w = correlate(spread, pairs, device[None], slabs, band.shape[0])
    returned = lax.all_to_all(w, ("zslab", "tile"), split_axis=0, concat_axis=0, tiled=True)
    return synthesise(returned)


def solution(mesh):
    placed = (P("tile", None, "zslab", None, None), P(), P())
    return jax.shard_map(
        shards,
        mesh=mesh,
        in_specs=placed,
        out_specs=P("tile", "zslab", None, None),
        check_vma=False,
    )
```

```python
import functools
import math


import jax
import jax.numpy as jnp
import numpy as np
from jax import lax
from jax.experimental import pallas as pl
from jax.experimental.pallas import tpu as pltpu
from jax.sharding import PartitionSpec as P

GX = 32
GY = 256
GZ = 128
FACES = 4


def dft_tables(length):
    indices = jnp.arange(length, dtype=jnp.int32)
    modular = indices[:, None] * indices[None, :] % length
    angles = modular.astype(jnp.float32) * (2.0 * math.pi / length)
    factor = 1.0 / math.sqrt(length)
    return (
        (jnp.cos(angles) * factor).astype(jnp.bfloat16),
        (jnp.sin(angles) * factor).astype(jnp.bfloat16),
    )


def product(form, left, right):
    return jnp.einsum(form, left, right, preferred_element_type=jnp.float32)


def reduce_resolution(image_volume, crop_bounds):
    row_mask = (
        jnp.arange(image_volume.shape[2], dtype=jnp.int32)[None, :] < crop_bounds[:, 0:1]
    ).astype(jnp.bfloat16)
    col_mask = (
        jnp.arange(image_volume.shape[3], dtype=jnp.int32)[None, :] < crop_bounds[:, 1:2]
    ).astype(jnp.bfloat16)
    masked = image_volume * row_mask[:, None, :, None] * col_mask[:, None, None, :]
    raw_cols = jnp.arange(image_volume.shape[3], dtype=jnp.int32)
    pooled_cols = jnp.arange(GY, dtype=jnp.int32)
    pooling = jnp.where(raw_cols[:, None] // 2 == pooled_cols[None, :], 0.5, 0.0).astype(
        jnp.bfloat16
    )
    along_pooled = product("szxy,yk->szxk", masked, pooling)
    shaped = along_pooled.reshape(image_volume.shape[0], image_volume.shape[1], GX, 2, GY)
    return (shaped[:, :, :, 0, :] + shaped[:, :, :, 1, :]).astype(jnp.bfloat16)


def cross_phase(owner_re, owner_im, pairs, tiles_here):
    first_dev = pairs[:, 0] // tiles_here
    first_pos = pairs[:, 0] % tiles_here * FACES + pairs[:, 1]
    second_tile_device = pairs[:, 2] // tiles_here
    second_pos = pairs[:, 2] % tiles_here * FACES + pairs[:, 3]
    first_re = owner_re[first_dev, :, first_pos].astype(jnp.float32)
    first_im = owner_im[first_dev, :, first_pos].astype(jnp.float32)
    second_re = owner_re[second_tile_device, :, second_pos].astype(jnp.float32)
    second_im = owner_im[second_tile_device, :, second_pos].astype(jnp.float32)
    cross_re = first_re * second_re + first_im * second_im
    cross_im = first_im * second_re - first_re * second_im
    scaled = jnp.sqrt(cross_re * cross_re + cross_im * cross_im + 1.0)
    return ((cross_re / scaled).astype(jnp.bfloat16), (cross_im / scaled).astype(jnp.bfloat16))


def inverse_z(phase_real_part, phase_im, tables_z):
    w_re = (
        product("pmjk,mz->pzjk", phase_real_part, tables_z[0])
        - product("pmjk,mz->pzjk", phase_im, tables_z[1])
    ).astype(jnp.bfloat16)
    w_im = (
        product("pmjk,mz->pzjk", phase_im, tables_z[0])
        + product("pmjk,mz->pzjk", phase_real_part, tables_z[1])
    ).astype(jnp.bfloat16)
    return (w_re, w_im)


def inverse_x(w_re, w_im, tables_x):
    v_re = (
        product("pzjk,jx->pzxk", w_re, tables_x[0]) - product("pzjk,jx->pzxk", w_im, tables_x[1])
    ).astype(jnp.bfloat16)
    v_im = (
        product("pzjk,jx->pzxk", w_im, tables_x[0]) + product("pzjk,jx->pzxk", w_re, tables_x[1])
    ).astype(jnp.bfloat16)
    return (v_re, v_im)


def general_shards(band, pairs, extents):
    tables_x = dft_tables(GX)
    tables_y = dft_tables(GY)
    tables_z = dft_tables(GZ)
    tiles_here = band.shape[0]
    slots = tiles_here * FACES
    zrows = band.shape[2]
    tile_pos = lax.axis_index("tile")
    global_slot = tile_pos * slots + jnp.arange(slots, dtype=jnp.int32)
    first_slot = pairs[:, 0] * FACES + pairs[:, 1]
    second_slot = pairs[:, 2] * FACES + pairs[:, 3]
    matches = (
        (first_slot[None, :] == global_slot[:, None])
        | (second_slot[None, :] == global_slot[:, None])
    ).astype(jnp.int32)
    crop_bounds = jnp.sum(matches[:, :, None] * extents[None, :, :], axis=1)
    image_volume = band.reshape(slots, zrows, 2 * GX, 2 * GY)
    reduced_volume = reduce_resolution(image_volume, crop_bounds)
    y_re = product("szxy,yk->szxk", reduced_volume, tables_y[0]).astype(jnp.bfloat16)
    y_im = (-product("szxy,yk->szxk", reduced_volume, tables_y[1])).astype(jnp.bfloat16)
    x_re = (
        product("szxk,xj->szjk", y_re, tables_x[0]) + product("szxk,xj->szjk", y_im, tables_x[1])
    ).astype(jnp.bfloat16)
    x_im = (
        product("szxk,xj->szjk", y_im, tables_x[0]) - product("szxk,xj->szjk", y_re, tables_x[1])
    ).astype(jnp.bfloat16)
    kx_part = GX // lax.axis_size("zslab")
    re_in = lax.all_to_all(x_re, "zslab", split_axis=2, concat_axis=1, tiled=True)
    im_in = lax.all_to_all(x_im, "zslab", split_axis=2, concat_axis=1, tiled=True)
    out_re = (
        product("szjk,zm->msjk", re_in, tables_z[0]) + product("szjk,zm->msjk", im_in, tables_z[1])
    ).astype(jnp.bfloat16)
    out_im = (
        product("szjk,zm->msjk", im_in, tables_z[0]) - product("szjk,zm->msjk", re_in, tables_z[1])
    ).astype(jnp.bfloat16)
    tile_count = lax.axis_size("tile")
    kz_part = GZ // tile_count
    spectra = (
        lax.all_to_all(out_re, "tile", split_axis=0, concat_axis=0, tiled=True),
        lax.all_to_all(out_im, "tile", split_axis=0, concat_axis=0, tiled=True),
    )
    owner_re = spectra[0].reshape(tile_count, kz_part, slots, kx_part, GY)
    owner_im = spectra[1].reshape(tile_count, kz_part, slots, kx_part, GY)
    phase_real_part, phase_im = cross_phase(owner_re, owner_im, pairs, tiles_here)
    returned = (
        lax.all_to_all(phase_real_part, "tile", split_axis=0, concat_axis=1, tiled=True),
        lax.all_to_all(phase_im, "tile", split_axis=0, concat_axis=1, tiled=True),
    )
    w_re, w_im = inverse_z(returned[0], returned[1], tables_z)
    v_re, v_im = inverse_x(
        lax.all_to_all(w_re, "zslab", split_axis=1, concat_axis=2, tiled=True),
        lax.all_to_all(w_im, "zslab", split_axis=1, concat_axis=2, tiled=True),
        tables_x,
    )
    return product("pzxk,ky->pzxy", v_re, tables_y[0]) - product("pzxk,ky->pzxy", v_im, tables_y[1])


HALF = GY // 2
ZTILE = 16
ZHALF = ZTILE // 2
VMEM_BYTES = 32 * 1024 * 1024


def host_tables(length):
    indices = np.arange(length, dtype=np.int32)
    modular = indices[:, None] * indices[None, :] % length
    angles = modular.astype(np.float32) * np.float32(2.0 * math.pi / length)
    factor = np.float32(1.0 / math.sqrt(length))
    return (
        (np.cos(angles) * factor).astype(jnp.bfloat16),
        (np.sin(angles) * factor).astype(jnp.bfloat16),
    )


def pooling_table():
    raw = np.arange(2 * GY)[:, None] // 2
    return np.where(raw == np.arange(GY)[None, :], 0.5, 0.0).astype(jnp.bfloat16)


def half_y_table():
    cosine, sine = host_tables(GY)
    imag = -sine[:, :HALF]
    imag[:, 0] = cosine[:, HALF]
    return np.concatenate([cosine[:, :HALF], imag], axis=1)


def half_y_inverse():
    cosine, sine = host_tables(GY)
    two = np.array(2.0, jnp.bfloat16)
    real = cosine[:HALF, :] * two
    real[0] = cosine[0]
    imag = -sine[:HALF, :] * two
    imag[0] = cosine[HALF]
    return np.concatenate([real, imag], axis=0)


def spread_x(table):
    planes = np.eye(ZHALF, dtype=np.float32)
    grid = np.einsum("jx,az->jazx", table.astype(np.float32), planes)
    return grid.reshape(GX * ZHALF, ZHALF * GX).astype(jnp.bfloat16)


def paired_columns(table):
    split = table.reshape(table.shape[0], 2, 2, ZHALF // 2, GX)
    return np.ascontiguousarray(split.transpose(0, 1, 3, 4, 2)).reshape(table.shape)


def mirror_order():
    order = [0, GX // 2]
    for j in range(1, GX // 2):
        order += [j, GX - j]
    return order


def forward_x_table():
    cosine, sine = (spread_x(table) for table in host_tables(GX))
    real = np.concatenate([cosine, sine], axis=1).reshape(GX, ZHALF, -1)
    imag = np.concatenate([-sine, cosine], axis=1).reshape(GX, ZHALF, -1)
    rows = np.stack([real, imag], axis=1)[mirror_order()]
    return paired_columns(rows.reshape(2 * GX * ZHALF, -1))


def inverse_x_table():
    cosine, sine = (spread_x(table) for table in host_tables(GX))
    return np.ascontiguousarray(np.block([[cosine, sine], [-sine, cosine]]).T)


def forward_z_table():
    cosine, sine = host_tables(GZ)
    return np.block([[cosine, sine], [-sine, cosine]])


def inverse_z_table():
    cosine, sine = host_tables(GZ)
    return np.block([[cosine, -sine], [sine, cosine]])


def dot(left, right):
    return jnp.dot(left, right, preferred_element_type=jnp.float32)


def analyse_kernel(
    slots, pairs_ref, extents_ref, tile_ref, band_ref, pool_ref, wy_ref, wx_ref, out_ref, crop_ref
):
    slot = pl.program_id(0)

    @pl.when(slot == 0)
    def _():
        for p in range(pairs_ref.shape[1]):
            for end in (0, 1):
                named = pairs_ref[2 * end, p] * FACES + pairs_ref[2 * end + 1, p] - tile_ref[0] * slots

                @pl.when((named >= 0) & (named < slots))
                def _():
                    crop_ref[named, 0] = extents_ref[0, p]
                    crop_ref[named, 1] = extents_ref[1, p]

    across, along = crop_ref[slot, 0], crop_ref[slot, 1]
    raw_col = lax.broadcasted_iota(jnp.int32, (2 * GY, GY), 0)
    pool = jnp.where(raw_col < along, pool_ref[...].astype(jnp.float32), 0.0).astype(jnp.bfloat16)
    rows = ZHALF * GX
    grouped = (ZHALF // 2, 2 * GX // 8, 8, GY)
    sublane = lax.broadcasted_iota(jnp.int32, grouped, 2)
    live = lax.broadcasted_iota(jnp.int32, grouped, 1) * 8 + sublane < across
    even = sublane % 2 == 0
    lane0 = lax.broadcasted_iota(jnp.int32, (ZTILE, HALF), 1) == 0

    def pair_sums(planes, shift):
        planes = jnp.where(live, planes.reshape(grouped), 0.0)
        flat = planes.reshape(-1, 8, GY)
        return planes + pltpu.roll(flat, shift, 1).reshape(grouped)

    def along_y(unit):
        raw = band_ref[0, 0, unit * ZHALF : (unit + 1) * ZHALF].reshape(2 * rows, 2 * GY)
        pooled = dot(raw, pool)
        down = jnp.where(even, pair_sums(pooled[:rows], 7), pair_sums(pooled[rows:], 1))
        return dot(down.reshape(rows, GY).astype(jnp.bfloat16), wy_ref[...]).astype(jnp.bfloat16)

    for part in range(band_ref.shape[2] // ZTILE):
        units = [along_y(2 * part), along_y(2 * part + 1)]
        stacked = jnp.concatenate(
            [
                jnp.concatenate([y[:, :HALF] for y in units], axis=1),
                jnp.concatenate([y[:, HALF:] for y in units], axis=1),
            ],
            axis=0,
        )
        spectra = dot(wx_ref[...], stacked)
        zs = slice(part * ZTILE, (part + 1) * ZTILE)

        def at(n):
            blocks = [spectra[m * ZHALF : (m + 1) * ZHALF] for m in (2 * n, 2 * n + 1)]
            return [jnp.concatenate([b[:, :HALF], b[:, HALF:]], axis=0) for b in blocks]

        def put(j, re, im):
            out_ref[j, 0, zs, 0:HALF] = re.astype(jnp.bfloat16)
            out_ref[j, 0, zs, HALF:] = im.astype(jnp.bfloat16)

        put(0, *at(0))
        put(GX // 2, *at(1))
        for j in range(1, GX // 2):
            re, im = at(2 * j)
            re_m, im_m = at(2 * j + 1)
            put(j, jnp.where(lane0, 0.5 * (re + re_m), re), jnp.where(lane0, 0.5 * (im - im_m), im))
            put(
                GX - j,
                jnp.where(lane0, 0.5 * (im + im_m), re_m),
                jnp.where(lane0, 0.5 * (re - re_m), im_m),
            )


def analyse(band, pairs, extents, tile):
    slots, zrows = band.shape[0] * FACES, band.shape[2]
    tables = (pooling_table(), half_y_table(), forward_x_table())
    whole = [pl.BlockSpec(t.shape, lambda i, *_: (0, 0)) for t in tables]
    return pl.pallas_call(
        functools.partial(analyse_kernel, slots),
        grid_spec=pltpu.PrefetchScalarGridSpec(
            num_scalar_prefetch=3,
            grid=(slots,),
            in_specs=[
                pl.BlockSpec(
                    (1, 1, zrows, 2 * GX, 2 * GY), lambda i, *_: (i // FACES, i % FACES, 0, 0, 0)
                )
            ]
            + whole,
            out_specs=pl.BlockSpec((GX, 1, zrows, GY), lambda i, *_: (0, i, 0, 0)),
            scratch_shapes=[pltpu.SMEM((slots, 2), jnp.int32)],
        ),
        out_shape=jax.ShapeDtypeStruct((GX, slots, zrows, GY), jnp.bfloat16),
        compiler_params=pltpu.CompilerParams(vmem_limit_bytes=VMEM_BYTES + VMEM_BYTES * 3 // 4),
        name="analyse",
    )(pairs, extents, tile, band, *(jnp.asarray(t) for t in tables))


def normalised(a_re, a_im, b_re, b_im):
    cross_re = a_re * b_re + a_im * b_im
    cross_im = a_im * b_re - a_re * b_im
    scale = lax.rsqrt(cross_re * cross_re + cross_im * cross_im + 1.0)
    return (cross_re * scale).astype(jnp.bfloat16), (cross_im * scale).astype(jnp.bfloat16)


def correlate_kernel(
    slabs, tiles_here, pairs_ref, place_ref, in_ref, wz_ref, wzi_ref, out_ref
):
    tiles = in_ref.shape[0] // slabs
    total = pairs_ref.shape[1]
    pairs_here = out_ref.shape[1]
    zrows = GZ // slabs
    both_real = (place_ref[0] == 0) | (place_ref[0] == GX // 2)
    lane = lax.broadcasted_iota(jnp.int32, (GZ, HALF), 1)
    lane0 = lane == 0

    def load(p, end, half):
        tile = pairs_ref[2 * end, p]
        row = tile // tiles_here
        pos = tile % tiles_here * FACES + pairs_ref[2 * end + 1, p]
        lanes = slice(half * HALF, (half + 1) * HALF)
        return jnp.concatenate([in_ref[row + s * tiles, pos, :, lanes] for s in range(slabs)], axis=0)

    def forward(re, im):
        spec = dot(wz_ref[...], jnp.concatenate([re, im], axis=0))
        return spec.astype(jnp.bfloat16).astype(jnp.float32)

    def phase_of(spec):
        return normalised(spec[:GZ, :HALF], spec[GZ:, :HALF], spec[:GZ, HALF:], spec[GZ:, HALF:])

    keep = jnp.where(lane0 & both_real, 0.0, 1.0).astype(jnp.bfloat16)
    for p in range(0, total, 2):
        phases = []
        for q in (p, p + 1):
            re = jnp.concatenate([load(q, 0, 0), load(q, 1, 0)], axis=1)
            im = jnp.concatenate([load(q, 0, 1) * keep, load(q, 1, 1) * keep], axis=1)
            phases.append(phase_of(forward(re, im)))
        stacked = jnp.concatenate(
            [
                jnp.concatenate([phases[0][0], phases[1][0]], axis=1),
                jnp.concatenate([phases[0][1], phases[1][1]], axis=1),
            ],
            axis=0,
        )
        w = dot(wzi_ref[...], stacked).astype(jnp.bfloat16)
        for k, q in enumerate((p, p + 1)):
            for half in (0, 1):
                plane = w[half * GZ : (half + 1) * GZ, k * HALF : (k + 1) * HALF]
                for s in range(slabs):
                    out_ref[
                        q // pairs_here + s * tiles,
                        q % pairs_here,
                        :,
                        half * HALF : (half + 1) * HALF,
                    ] = plane[s * zrows : (s + 1) * zrows]

    @pl.when(both_real)
    def _():
        first = jnp.zeros((GZ, HALF), jnp.float32)
        second = jnp.zeros((GZ, HALF), jnp.float32)
        for p in range(total):
            a = load(p, 0, 1).astype(jnp.float32)[:, 0:1]
            b = load(p, 1, 1).astype(jnp.float32)[:, 0:1]
            first = jnp.where(lane == p, a, first)
            second = jnp.where(lane == p, b, second)
        re = jnp.concatenate([first, second], axis=1).astype(jnp.bfloat16)
        phase = phase_of(forward(re, jnp.zeros_like(re)))
        w = dot(wzi_ref[...], jnp.concatenate(phase, axis=0))[:GZ]
        for p in range(total):
            column = w[:, p : p + 1]
            for s in range(slabs):
                at = (p // pairs_here + s * tiles, p % pairs_here, slice(None), slice(HALF, 2 * HALF))
                old = out_ref[at].astype(jnp.float32)
                rows = slice(s * zrows, (s + 1) * zrows)
                out_ref[at] = jnp.where(lane0[rows], column[rows], old).astype(jnp.bfloat16)


def correlate(spread, pairs, place, slabs, tiles_here):
    devices, _, zrows, _ = spread.shape
    pairs_here = pairs.shape[1] * slabs // devices
    tables = (forward_z_table(), inverse_z_table())
    vmem = pl.BlockSpec(memory_space=pltpu.VMEM)
    smem = pl.BlockSpec(memory_space=pltpu.SMEM)
    return pl.pallas_call(
        functools.partial(correlate_kernel, slabs, tiles_here),
        in_specs=[smem, smem, vmem, vmem, vmem],
        out_specs=vmem,
        out_shape=jax.ShapeDtypeStruct((devices, pairs_here, zrows, GY), jnp.bfloat16),
        compiler_params=pltpu.CompilerParams(vmem_limit_bytes=VMEM_BYTES),
        name="correlate",
    )(pairs, place, spread, *(jnp.asarray(t) for t in tables))


def synthesise_kernel(in_ref, wx_ref, wy_ref, out_ref):
    rows = ZHALF * GX
    lane0 = lax.broadcasted_iota(jnp.int32, (ZTILE, HALF), 1) == 0

    def at(j):
        return in_ref[j, 0, :, 0:HALF].astype(jnp.float32), in_ref[j, 0, :, HALF:].astype(jnp.float32)

    blocks = [None] * GX
    for j in (0, GX // 2):
        blocks[j] = at(j)
    for j in range(1, GX // 2):
        re, im = at(j)
        re_m, im_m = at(GX - j)
        blocks[j] = (jnp.where(lane0, re + im_m, re), jnp.where(lane0, im + re_m, im))
        blocks[GX - j] = (jnp.where(lane0, re - im_m, re_m), jnp.where(lane0, re_m - im, im_m))
    stacked = jnp.concatenate(
        [
            jnp.concatenate(
                [
                    jnp.concatenate([b[part][half * ZHALF : (half + 1) * ZHALF] for b in blocks], axis=0)
                    for half in range(2)
                ],
                axis=1,
            )
            for part in range(2)
        ],
        axis=0,
    ).astype(jnp.bfloat16)
    v_re = dot(wx_ref[:rows, :], stacked).astype(jnp.bfloat16)
    v_im = dot(wx_ref[rows:, :], stacked).astype(jnp.bfloat16)
    for half in range(2):
        lanes = slice(half * HALF, (half + 1) * HALF)
        v = jnp.concatenate([v_re[:, lanes], v_im[:, lanes]], axis=1)
        out_ref[0, half * ZHALF : (half + 1) * ZHALF] = dot(v, wy_ref[...]).reshape(ZHALF, GX, GY)


def synthesise(returned):
    _, pairs_here, zrows, _ = returned.shape
    tables = (inverse_x_table(), half_y_inverse())
    return pl.pallas_call(
        synthesise_kernel,
        grid=(pairs_here, zrows // ZTILE),
        in_specs=[pl.BlockSpec((GX, 1, ZTILE, GY), lambda i, z: (0, i, z, 0))]
        + [pl.BlockSpec(t.shape, lambda i, z: (0, 0)) for t in tables],
        out_specs=pl.BlockSpec((1, ZTILE, GX, GY), lambda i, z: (i, z, 0, 0)),
        out_shape=jax.ShapeDtypeStruct((pairs_here, zrows, GX, GY), jnp.float32),
        compiler_params=pltpu.CompilerParams(vmem_limit_bytes=VMEM_BYTES),
        name="synthesise",
    )(returned, *(jnp.asarray(t) for t in tables))


def shards(band, pairs, extents):
    tiles, slabs = lax.axis_size("tile"), lax.axis_size("zslab")
    zrows = band.shape[2]
    if tiles * slabs != GX or zrows % ZTILE or pairs.shape[0] % (2 * tiles):
        return general_shards(band, pairs, extents)
    pairs, extents = pairs.T, extents.T
    tile = lax.axis_index("tile").astype(jnp.int32)
    device = lax.axis_index("zslab").astype(jnp.int32) * tiles + tile
    spectra = analyse(band, pairs, extents, tile[None])
    spread = lax.all_to_all(spectra, ("zslab", "tile"), split_axis=0, concat_axis=0, tiled=True)
    w = correlate(spread, pairs, device[None], slabs, band.shape[0])
    returned = lax.all_to_all(w, ("zslab", "tile"), split_axis=0, concat_axis=0, tiled=True)
    return synthesise(returned)


def solution(mesh):
    placed = (P("tile", None, "zslab", None, None), P(), P())
    return jax.shard_map(
        shards,
        mesh=mesh,
        in_specs=placed,
        out_specs=P("tile", "zslab", None, None),
        check_vma=False,
    )
```

```python
import functools
import math


import jax
import jax.numpy as jnp
import numpy as np
from jax import lax
from jax.experimental import pallas as pl
from jax.experimental.pallas import tpu as pltpu
from jax.sharding import PartitionSpec as P

GX = 32
GY = 256
GZ = 128
FACES = 4


def dft_tables(length):
    indices = jnp.arange(length, dtype=jnp.int32)
    modular = indices[:, None] * indices[None, :] % length
    angles = modular.astype(jnp.float32) * (2.0 * math.pi / length)
    factor = 1.0 / math.sqrt(length)
    return (
        (jnp.cos(angles) * factor).astype(jnp.bfloat16),
        (jnp.sin(angles) * factor).astype(jnp.bfloat16),
    )


def product(form, left, right):
    return jnp.einsum(form, left, right, preferred_element_type=jnp.float32)


def reduce_resolution(image_volume, crop_bounds):
    row_mask = (
        jnp.arange(image_volume.shape[2], dtype=jnp.int32)[None, :] < crop_bounds[:, 0:1]
    ).astype(jnp.bfloat16)
    col_mask = (
        jnp.arange(image_volume.shape[3], dtype=jnp.int32)[None, :] < crop_bounds[:, 1:2]
    ).astype(jnp.bfloat16)
    masked = image_volume * row_mask[:, None, :, None] * col_mask[:, None, None, :]
    raw_cols = jnp.arange(image_volume.shape[3], dtype=jnp.int32)
    pooled_cols = jnp.arange(GY, dtype=jnp.int32)
    pooling = jnp.where(raw_cols[:, None] // 2 == pooled_cols[None, :], 0.5, 0.0).astype(
        jnp.bfloat16
    )
    along_pooled = product("szxy,yk->szxk", masked, pooling)
    shaped = along_pooled.reshape(image_volume.shape[0], image_volume.shape[1], GX, 2, GY)
    return (shaped[:, :, :, 0, :] + shaped[:, :, :, 1, :]).astype(jnp.bfloat16)


def cross_phase(owner_re, owner_im, pairs, tiles_here):
    first_dev = pairs[:, 0] // tiles_here
    first_pos = pairs[:, 0] % tiles_here * FACES + pairs[:, 1]
    second_tile_device = pairs[:, 2] // tiles_here
    second_pos = pairs[:, 2] % tiles_here * FACES + pairs[:, 3]
    first_re = owner_re[first_dev, :, first_pos].astype(jnp.float32)
    first_im = owner_im[first_dev, :, first_pos].astype(jnp.float32)
    second_re = owner_re[second_tile_device, :, second_pos].astype(jnp.float32)
    second_im = owner_im[second_tile_device, :, second_pos].astype(jnp.float32)
    cross_re = first_re * second_re + first_im * second_im
    cross_im = first_im * second_re - first_re * second_im
    scaled = jnp.sqrt(cross_re * cross_re + cross_im * cross_im + 1.0)
    return ((cross_re / scaled).astype(jnp.bfloat16), (cross_im / scaled).astype(jnp.bfloat16))


def inverse_z(phase_real_part, phase_im, tables_z):
    w_re = (
        product("pmjk,mz->pzjk", phase_real_part, tables_z[0])
        - product("pmjk,mz->pzjk", phase_im, tables_z[1])
    ).astype(jnp.bfloat16)
    w_im = (
        product("pmjk,mz->pzjk", phase_im, tables_z[0])
        + product("pmjk,mz->pzjk", phase_real_part, tables_z[1])
    ).astype(jnp.bfloat16)
    return (w_re, w_im)


def inverse_x(w_re, w_im, tables_x):
    v_re = (
        product("pzjk,jx->pzxk", w_re, tables_x[0]) - product("pzjk,jx->pzxk", w_im, tables_x[1])
    ).astype(jnp.bfloat16)
    v_im = (
        product("pzjk,jx->pzxk", w_im, tables_x[0]) + product("pzjk,jx->pzxk", w_re, tables_x[1])
    ).astype(jnp.bfloat16)
    return (v_re, v_im)


def general_shards(band, pairs, extents):
    tables_x = dft_tables(GX)
    tables_y = dft_tables(GY)
    tables_z = dft_tables(GZ)
    tiles_here = band.shape[0]
    slots = tiles_here * FACES
    zrows = band.shape[2]
    tile_pos = lax.axis_index("tile")
    global_slot = tile_pos * slots + jnp.arange(slots, dtype=jnp.int32)
    first_slot = pairs[:, 0] * FACES + pairs[:, 1]
    second_slot = pairs[:, 2] * FACES + pairs[:, 3]
    matches = (
        (first_slot[None, :] == global_slot[:, None])
        | (second_slot[None, :] == global_slot[:, None])
    ).astype(jnp.int32)
    crop_bounds = jnp.sum(matches[:, :, None] * extents[None, :, :], axis=1)
    image_volume = band.reshape(slots, zrows, 2 * GX, 2 * GY)
    reduced_volume = reduce_resolution(image_volume, crop_bounds)
    y_re = product("szxy,yk->szxk", reduced_volume, tables_y[0]).astype(jnp.bfloat16)
    y_im = (-product("szxy,yk->szxk", reduced_volume, tables_y[1])).astype(jnp.bfloat16)
    x_re = (
        product("szxk,xj->szjk", y_re, tables_x[0]) + product("szxk,xj->szjk", y_im, tables_x[1])
    ).astype(jnp.bfloat16)
    x_im = (
        product("szxk,xj->szjk", y_im, tables_x[0]) - product("szxk,xj->szjk", y_re, tables_x[1])
    ).astype(jnp.bfloat16)
    kx_part = GX // lax.axis_size("zslab")
    re_in = lax.all_to_all(x_re, "zslab", split_axis=2, concat_axis=1, tiled=True)
    im_in = lax.all_to_all(x_im, "zslab", split_axis=2, concat_axis=1, tiled=True)
    out_re = (
        product("szjk,zm->msjk", re_in, tables_z[0]) + product("szjk,zm->msjk", im_in, tables_z[1])
    ).astype(jnp.bfloat16)
    out_im = (
        product("szjk,zm->msjk", im_in, tables_z[0]) - product("szjk,zm->msjk", re_in, tables_z[1])
    ).astype(jnp.bfloat16)
    tile_count = lax.axis_size("tile")
    kz_part = GZ // tile_count
    spectra = (
        lax.all_to_all(out_re, "tile", split_axis=0, concat_axis=0, tiled=True),
        lax.all_to_all(out_im, "tile", split_axis=0, concat_axis=0, tiled=True),
    )
    owner_re = spectra[0].reshape(tile_count, kz_part, slots, kx_part, GY)
    owner_im = spectra[1].reshape(tile_count, kz_part, slots, kx_part, GY)
    phase_real_part, phase_im = cross_phase(owner_re, owner_im, pairs, tiles_here)
    returned = (
        lax.all_to_all(phase_real_part, "tile", split_axis=0, concat_axis=1, tiled=True),
        lax.all_to_all(phase_im, "tile", split_axis=0, concat_axis=1, tiled=True),
    )
    w_re, w_im = inverse_z(returned[0], returned[1], tables_z)
    v_re, v_im = inverse_x(
        lax.all_to_all(w_re, "zslab", split_axis=1, concat_axis=2, tiled=True),
        lax.all_to_all(w_im, "zslab", split_axis=1, concat_axis=2, tiled=True),
        tables_x,
    )
    return product("pzxk,ky->pzxy", v_re, tables_y[0]) - product("pzxk,ky->pzxy", v_im, tables_y[1])


HALF = GY // 2
ZTILE = 16
ZHALF = ZTILE // 2
VMEM_BYTES = 32 * 1024 * 1024


def host_tables(length):
    indices = np.arange(length, dtype=np.int32)
    modular = indices[:, None] * indices[None, :] % length
    angles = modular.astype(np.float32) * np.float32(2.0 * math.pi / length)
    factor = np.float32(1.0 / math.sqrt(length))
    return (
        (np.cos(angles) * factor).astype(jnp.bfloat16),
        (np.sin(angles) * factor).astype(jnp.bfloat16),
    )


def pooling_table():
    raw = np.arange(2 * GY)[:, None] // 2
    return np.where(raw == np.arange(GY)[None, :], 0.5, 0.0).astype(jnp.bfloat16)


def half_y_table():
    cosine, sine = host_tables(GY)
    imag = -sine[:, :HALF]
    imag[:, 0] = cosine[:, HALF]
    return np.concatenate([cosine[:, :HALF], imag], axis=1)


def half_y_inverse():
    cosine, sine = host_tables(GY)
    two = np.array(2.0, jnp.bfloat16)
    real = cosine[:HALF, :] * two
    real[0] = cosine[0]
    imag = -sine[:HALF, :] * two
    imag[0] = cosine[HALF]
    return np.concatenate([real, imag], axis=0)


def spread_x(table):
    planes = np.eye(ZHALF, dtype=np.float32)
    grid = np.einsum("jx,az->jazx", table.astype(np.float32), planes)
    return grid.reshape(GX * ZHALF, ZHALF * GX).astype(jnp.bfloat16)


def paired_columns(table):
    split = table.reshape(table.shape[0], 2, 2, ZHALF // 2, GX)
    return np.ascontiguousarray(split.transpose(0, 1, 3, 4, 2)).reshape(table.shape)


def mirror_order():
    order = [0, GX // 2]
    for j in range(1, GX // 2):
        order += [j, GX - j]
    return order


def forward_x_table():
    cosine, sine = (spread_x(table) for table in host_tables(GX))
    real = np.concatenate([cosine, sine], axis=1).reshape(GX, ZHALF, -1)
    imag = np.concatenate([-sine, cosine], axis=1).reshape(GX, ZHALF, -1)
    rows = np.stack([real, imag], axis=1)[mirror_order()]
    return paired_columns(rows.reshape(2 * GX * ZHALF, -1))


def inverse_x_table():
    cosine, sine = (spread_x(table) for table in host_tables(GX))
    return np.ascontiguousarray(np.block([[cosine, sine], [-sine, cosine]]).T)


def forward_z_table():
    cosine, sine = host_tables(GZ)
    return np.block([[cosine, sine], [-sine, cosine]])


def inverse_z_table():
    cosine, sine = host_tables(GZ)
    return np.block([[cosine, -sine], [sine, cosine]])


def dot(left, right):
    return jnp.dot(left, right, preferred_element_type=jnp.float32)


def analyse_kernel(
    slots, pairs_ref, extents_ref, tile_ref, band_ref, pool_ref, wy_ref, wx_ref, out_ref, crop_ref
):
    slot = pl.program_id(0)

    @pl.when(slot == 0)
    def _():
        for p in range(pairs_ref.shape[1]):
            for end in (0, 1):
                named = pairs_ref[2 * end, p] * FACES + pairs_ref[2 * end + 1, p] - tile_ref[0] * slots

                @pl.when((named >= 0) & (named < slots))
                def _():
                    crop_ref[named, 0] = extents_ref[0, p]
                    crop_ref[named, 1] = extents_ref[1, p]

    across, along = crop_ref[slot, 0], crop_ref[slot, 1]
    raw_col = lax.broadcasted_iota(jnp.int32, (2 * GY, GY), 0)
    pool = jnp.where(raw_col < along, pool_ref[...].astype(jnp.float32), 0.0).astype(jnp.bfloat16)
    units = band_ref.shape[2] // ZHALF
    grouped = (units, ZHALF // 2, 2 * GX // 8, 8, GY)
    sublane = lax.broadcasted_iota(jnp.int32, grouped[1:], 2)
    live = lax.broadcasted_iota(jnp.int32, grouped[1:], 1) * 8 + sublane < across
    even = sublane % 2 == 0
    lane0 = lax.broadcasted_iota(jnp.int32, (ZTILE, HALF), 1) == 0

    def pair_sums(planes, shift):
        planes = jnp.where(live, planes, 0.0)
        flat = planes.reshape(-1, 8, GY)
        return planes + pltpu.roll(flat, shift, 1).reshape(grouped)

    raw = band_ref[0, 0].reshape(-1, 2 * GY)
    pooled = dot(raw, pool).reshape(units, 2, *grouped[1:])
    down = jnp.where(even, pair_sums(pooled[:, 0], 7), pair_sums(pooled[:, 1], 1))
    y = dot(down.reshape(-1, GY).astype(jnp.bfloat16), wy_ref[...]).astype(jnp.bfloat16)
    y = y.reshape(units, ZHALF * GX, GY)
    stacked = jnp.concatenate(
        [
            jnp.concatenate([y[unit, :, :HALF] for unit in range(units)], axis=1),
            jnp.concatenate([y[unit, :, HALF:] for unit in range(units)], axis=1),
        ],
        axis=0,
    )
    spectra = dot(wx_ref[...], stacked)

    def at(n):
        blocks = [spectra[m * ZHALF : (m + 1) * ZHALF] for m in (2 * n, 2 * n + 1)]
        return [
            [
                jnp.concatenate([b[:, u * HALF : (u + 1) * HALF] for u in (unit, unit + 1)], axis=0)
                for b in blocks
            ]
            for unit in range(0, units, 2)
        ]

    def put(j, part, re, im):
        zs = slice(part * ZTILE, (part + 1) * ZTILE)
        out_ref[j, 0, zs, 0:HALF] = re.astype(jnp.bfloat16)
        out_ref[j, 0, zs, HALF:] = im.astype(jnp.bfloat16)

    for n, j in enumerate((0, GX // 2)):
        for part, both in enumerate(at(n)):
            put(j, part, *both)
    for j in range(1, GX // 2):
        for part, ((re, im), (re_m, im_m)) in enumerate(zip(at(2 * j), at(2 * j + 1))):
            put(
                j,
                part,
                jnp.where(lane0, 0.5 * (re + re_m), re),
                jnp.where(lane0, 0.5 * (im - im_m), im),
            )
            put(
                GX - j,
                part,
                jnp.where(lane0, 0.5 * (im + im_m), re_m),
                jnp.where(lane0, 0.5 * (re - re_m), im_m),
            )


def analyse(band, pairs, extents, tile):
    slots, zrows = band.shape[0] * FACES, band.shape[2]
    tables = (pooling_table(), half_y_table(), forward_x_table())
    whole = [pl.BlockSpec(t.shape, lambda i, *_: (0, 0)) for t in tables]
    return pl.pallas_call(
        functools.partial(analyse_kernel, slots),
        grid_spec=pltpu.PrefetchScalarGridSpec(
            num_scalar_prefetch=3,
            grid=(slots,),
            in_specs=[
                pl.BlockSpec(
                    (1, 1, zrows, 2 * GX, 2 * GY), lambda i, *_: (i // FACES, i % FACES, 0, 0, 0)
                )
            ]
            + whole,
            out_specs=pl.BlockSpec((GX, 1, zrows, GY), lambda i, *_: (0, i, 0, 0)),
            scratch_shapes=[pltpu.SMEM((slots, 2), jnp.int32)],
        ),
        out_shape=jax.ShapeDtypeStruct((GX, slots, zrows, GY), jnp.bfloat16),
        compiler_params=pltpu.CompilerParams(vmem_limit_bytes=VMEM_BYTES + VMEM_BYTES * 3 // 4),
        name="analyse",
    )(pairs, extents, tile, band, *(jnp.asarray(t) for t in tables))


def normalised(a_re, a_im, b_re, b_im):
    cross_re = a_re * b_re + a_im * b_im
    cross_im = a_im * b_re - a_re * b_im
    scale = lax.rsqrt(cross_re * cross_re + cross_im * cross_im + 1.0)
    return (cross_re * scale).astype(jnp.bfloat16), (cross_im * scale).astype(jnp.bfloat16)


def correlate_kernel(
    slabs, tiles_here, pairs_ref, place_ref, in_ref, wz_ref, wzi_ref, out_ref
):
    tiles = in_ref.shape[0] // slabs
    total = pairs_ref.shape[1]
    pairs_here = out_ref.shape[1]
    zrows = GZ // slabs
    both_real = (place_ref[0] == 0) | (place_ref[0] == GX // 2)
    lane = lax.broadcasted_iota(jnp.int32, (GZ, HALF), 1)
    lane0 = lane == 0

    def load(p, end, half):
        tile = pairs_ref[2 * end, p]
        row = tile // tiles_here
        pos = tile % tiles_here * FACES + pairs_ref[2 * end + 1, p]
        lanes = slice(half * HALF, (half + 1) * HALF)
        return jnp.concatenate([in_ref[row + s * tiles, pos, :, lanes] for s in range(slabs)], axis=0)

    def forward(re, im):
        spec = dot(wz_ref[...], jnp.concatenate([re, im], axis=0))
        return spec.astype(jnp.bfloat16).astype(jnp.float32)

    def phase_of(spec):
        return normalised(spec[:GZ, :HALF], spec[GZ:, :HALF], spec[:GZ, HALF:], spec[GZ:, HALF:])

    keep = jnp.where(lane0 & both_real, 0.0, 1.0).astype(jnp.bfloat16)
    for p in range(0, total, 2):
        phases = []
        for q in (p, p + 1):
            re = jnp.concatenate([load(q, 0, 0), load(q, 1, 0)], axis=1)
            im = jnp.concatenate([load(q, 0, 1) * keep, load(q, 1, 1) * keep], axis=1)
            phases.append(phase_of(forward(re, im)))
        stacked = jnp.concatenate(
            [
                jnp.concatenate([phases[0][0], phases[1][0]], axis=1),
                jnp.concatenate([phases[0][1], phases[1][1]], axis=1),
            ],
            axis=0,
        )
        w = dot(wzi_ref[...], stacked).astype(jnp.bfloat16)
        for k, q in enumerate((p, p + 1)):
            for half in (0, 1):
                plane = w[half * GZ : (half + 1) * GZ, k * HALF : (k + 1) * HALF]
                for s in range(slabs):
                    out_ref[
                        q // pairs_here + s * tiles,
                        q % pairs_here,
                        :,
                        half * HALF : (half + 1) * HALF,
                    ] = plane[s * zrows : (s + 1) * zrows]

    @pl.when(both_real)
    def _():
        first = jnp.zeros((GZ, HALF), jnp.float32)
        second = jnp.zeros((GZ, HALF), jnp.float32)
        for p in range(total):
            a = load(p, 0, 1).astype(jnp.float32)[:, 0:1]
            b = load(p, 1, 1).astype(jnp.float32)[:, 0:1]
            first = jnp.where(lane == p, a, first)
            second = jnp.where(lane == p, b, second)
        re = jnp.concatenate([first, second], axis=1).astype(jnp.bfloat16)
        phase = phase_of(forward(re, jnp.zeros_like(re)))
        w = dot(wzi_ref[...], jnp.concatenate(phase, axis=0))[:GZ]
        for p in range(total):
            column = w[:, p : p + 1]
            for s in range(slabs):
                at = (p // pairs_here + s * tiles, p % pairs_here, slice(None), slice(HALF, 2 * HALF))
                old = out_ref[at].astype(jnp.float32)
                rows = slice(s * zrows, (s + 1) * zrows)
                out_ref[at] = jnp.where(lane0[rows], column[rows], old).astype(jnp.bfloat16)


def correlate(spread, pairs, place, slabs, tiles_here):
    devices, _, zrows, _ = spread.shape
    pairs_here = pairs.shape[1] * slabs // devices
    tables = (forward_z_table(), inverse_z_table())
    vmem = pl.BlockSpec(memory_space=pltpu.VMEM)
    smem = pl.BlockSpec(memory_space=pltpu.SMEM)
    return pl.pallas_call(
        functools.partial(correlate_kernel, slabs, tiles_here),
        in_specs=[smem, smem, vmem, vmem, vmem],
        out_specs=vmem,
        out_shape=jax.ShapeDtypeStruct((devices, pairs_here, zrows, GY), jnp.bfloat16),
        compiler_params=pltpu.CompilerParams(vmem_limit_bytes=VMEM_BYTES),
        name="correlate",
    )(pairs, place, spread, *(jnp.asarray(t) for t in tables))


def synthesise_kernel(in_ref, wx_ref, wy_ref, out_ref):
    rows = ZHALF * GX
    lane0 = lax.broadcasted_iota(jnp.int32, (ZTILE, HALF), 1) == 0

    def at(j):
        return in_ref[j, 0, :, 0:HALF].astype(jnp.float32), in_ref[j, 0, :, HALF:].astype(jnp.float32)

    blocks = [None] * GX
    for j in (0, GX // 2):
        blocks[j] = at(j)
    for j in range(1, GX // 2):
        re, im = at(j)
        re_m, im_m = at(GX - j)
        blocks[j] = (jnp.where(lane0, re + im_m, re), jnp.where(lane0, im + re_m, im))
        blocks[GX - j] = (jnp.where(lane0, re - im_m, re_m), jnp.where(lane0, re_m - im, im_m))
    stacked = jnp.concatenate(
        [
            jnp.concatenate(
                [
                    jnp.concatenate([b[part][half * ZHALF : (half + 1) * ZHALF] for b in blocks], axis=0)
                    for half in range(2)
                ],
                axis=1,
            )
            for part in range(2)
        ],
        axis=0,
    ).astype(jnp.bfloat16)
    v_re = dot(wx_ref[:rows, :], stacked).astype(jnp.bfloat16)
    v_im = dot(wx_ref[rows:, :], stacked).astype(jnp.bfloat16)
    for half in range(2):
        lanes = slice(half * HALF, (half + 1) * HALF)
        v = jnp.concatenate([v_re[:, lanes], v_im[:, lanes]], axis=1)
        out_ref[0, half * ZHALF : (half + 1) * ZHALF] = dot(v, wy_ref[...]).reshape(ZHALF, GX, GY)


def synthesise(returned):
    _, pairs_here, zrows, _ = returned.shape
    tables = (inverse_x_table(), half_y_inverse())
    return pl.pallas_call(
        synthesise_kernel,
        grid=(pairs_here, zrows // ZTILE),
        in_specs=[pl.BlockSpec((GX, 1, ZTILE, GY), lambda i, z: (0, i, z, 0))]
        + [pl.BlockSpec(t.shape, lambda i, z: (0, 0)) for t in tables],
        out_specs=pl.BlockSpec((1, ZTILE, GX, GY), lambda i, z: (i, z, 0, 0)),
        out_shape=jax.ShapeDtypeStruct((pairs_here, zrows, GX, GY), jnp.float32),
        compiler_params=pltpu.CompilerParams(vmem_limit_bytes=VMEM_BYTES),
        name="synthesise",
    )(returned, *(jnp.asarray(t) for t in tables))


def shards(band, pairs, extents):
    tiles, slabs = lax.axis_size("tile"), lax.axis_size("zslab")
    zrows = band.shape[2]
    if tiles * slabs != GX or zrows % ZTILE or pairs.shape[0] % (2 * tiles):
        return general_shards(band, pairs, extents)
    pairs, extents = pairs.T, extents.T
    tile = lax.axis_index("tile").astype(jnp.int32)
    device = lax.axis_index("zslab").astype(jnp.int32) * tiles + tile
    spectra = analyse(band, pairs, extents, tile[None])
    spread = lax.all_to_all(spectra, ("zslab", "tile"), split_axis=0, concat_axis=0, tiled=True)
    w = correlate(spread, pairs, device[None], slabs, band.shape[0])
    returned = lax.all_to_all(w, ("zslab", "tile"), split_axis=0, concat_axis=0, tiled=True)
    return synthesise(returned)


def solution(mesh):
    placed = (P("tile", None, "zslab", None, None), P(), P())
    return jax.shard_map(
        shards,
        mesh=mesh,
        in_specs=placed,
        out_specs=P("tile", "zslab", None, None),
        check_vma=False,
    )
```

```python
import functools
import math


import jax
import jax.numpy as jnp
import numpy as np
from jax import lax
from jax.experimental import pallas as pl
from jax.experimental.pallas import tpu as pltpu
from jax.sharding import PartitionSpec as P

GX = 32
GY = 256
GZ = 128
FACES = 4


def dft_tables(length):
    indices = jnp.arange(length, dtype=jnp.int32)
    modular = indices[:, None] * indices[None, :] % length
    angles = modular.astype(jnp.float32) * (2.0 * math.pi / length)
    factor = 1.0 / math.sqrt(length)
    return (
        (jnp.cos(angles) * factor).astype(jnp.bfloat16),
        (jnp.sin(angles) * factor).astype(jnp.bfloat16),
    )


def product(form, left, right):
    return jnp.einsum(form, left, right, preferred_element_type=jnp.float32)


def reduce_resolution(image_volume, crop_bounds):
    row_mask = (
        jnp.arange(image_volume.shape[2], dtype=jnp.int32)[None, :] < crop_bounds[:, 0:1]
    ).astype(jnp.bfloat16)
    col_mask = (
        jnp.arange(image_volume.shape[3], dtype=jnp.int32)[None, :] < crop_bounds[:, 1:2]
    ).astype(jnp.bfloat16)
    masked = image_volume * row_mask[:, None, :, None] * col_mask[:, None, None, :]
    raw_cols = jnp.arange(image_volume.shape[3], dtype=jnp.int32)
    pooled_cols = jnp.arange(GY, dtype=jnp.int32)
    pooling = jnp.where(raw_cols[:, None] // 2 == pooled_cols[None, :], 0.5, 0.0).astype(
        jnp.bfloat16
    )
    along_pooled = product("szxy,yk->szxk", masked, pooling)
    shaped = along_pooled.reshape(image_volume.shape[0], image_volume.shape[1], GX, 2, GY)
    return (shaped[:, :, :, 0, :] + shaped[:, :, :, 1, :]).astype(jnp.bfloat16)


def cross_phase(owner_re, owner_im, pairs, tiles_here):
    first_dev = pairs[:, 0] // tiles_here
    first_pos = pairs[:, 0] % tiles_here * FACES + pairs[:, 1]
    second_tile_device = pairs[:, 2] // tiles_here
    second_pos = pairs[:, 2] % tiles_here * FACES + pairs[:, 3]
    first_re = owner_re[first_dev, :, first_pos].astype(jnp.float32)
    first_im = owner_im[first_dev, :, first_pos].astype(jnp.float32)
    second_re = owner_re[second_tile_device, :, second_pos].astype(jnp.float32)
    second_im = owner_im[second_tile_device, :, second_pos].astype(jnp.float32)
    cross_re = first_re * second_re + first_im * second_im
    cross_im = first_im * second_re - first_re * second_im
    scaled = jnp.sqrt(cross_re * cross_re + cross_im * cross_im + 1.0)
    return ((cross_re / scaled).astype(jnp.bfloat16), (cross_im / scaled).astype(jnp.bfloat16))


def inverse_z(phase_real_part, phase_im, tables_z):
    w_re = (
        product("pmjk,mz->pzjk", phase_real_part, tables_z[0])
        - product("pmjk,mz->pzjk", phase_im, tables_z[1])
    ).astype(jnp.bfloat16)
    w_im = (
        product("pmjk,mz->pzjk", phase_im, tables_z[0])
        + product("pmjk,mz->pzjk", phase_real_part, tables_z[1])
    ).astype(jnp.bfloat16)
    return (w_re, w_im)


def inverse_x(w_re, w_im, tables_x):
    v_re = (
        product("pzjk,jx->pzxk", w_re, tables_x[0]) - product("pzjk,jx->pzxk", w_im, tables_x[1])
    ).astype(jnp.bfloat16)
    v_im = (
        product("pzjk,jx->pzxk", w_im, tables_x[0]) + product("pzjk,jx->pzxk", w_re, tables_x[1])
    ).astype(jnp.bfloat16)
    return (v_re, v_im)


def general_shards(band, pairs, extents):
    tables_x = dft_tables(GX)
    tables_y = dft_tables(GY)
    tables_z = dft_tables(GZ)
    tiles_here = band.shape[0]
    slots = tiles_here * FACES
    zrows = band.shape[2]
    tile_pos = lax.axis_index("tile")
    global_slot = tile_pos * slots + jnp.arange(slots, dtype=jnp.int32)
    first_slot = pairs[:, 0] * FACES + pairs[:, 1]
    second_slot = pairs[:, 2] * FACES + pairs[:, 3]
    matches = (
        (first_slot[None, :] == global_slot[:, None])
        | (second_slot[None, :] == global_slot[:, None])
    ).astype(jnp.int32)
    crop_bounds = jnp.sum(matches[:, :, None] * extents[None, :, :], axis=1)
    image_volume = band.reshape(slots, zrows, 2 * GX, 2 * GY)
    reduced_volume = reduce_resolution(image_volume, crop_bounds)
    y_re = product("szxy,yk->szxk", reduced_volume, tables_y[0]).astype(jnp.bfloat16)
    y_im = (-product("szxy,yk->szxk", reduced_volume, tables_y[1])).astype(jnp.bfloat16)
    x_re = (
        product("szxk,xj->szjk", y_re, tables_x[0]) + product("szxk,xj->szjk", y_im, tables_x[1])
    ).astype(jnp.bfloat16)
    x_im = (
        product("szxk,xj->szjk", y_im, tables_x[0]) - product("szxk,xj->szjk", y_re, tables_x[1])
    ).astype(jnp.bfloat16)
    kx_part = GX // lax.axis_size("zslab")
    re_in = lax.all_to_all(x_re, "zslab", split_axis=2, concat_axis=1, tiled=True)
    im_in = lax.all_to_all(x_im, "zslab", split_axis=2, concat_axis=1, tiled=True)
    out_re = (
        product("szjk,zm->msjk", re_in, tables_z[0]) + product("szjk,zm->msjk", im_in, tables_z[1])
    ).astype(jnp.bfloat16)
    out_im = (
        product("szjk,zm->msjk", im_in, tables_z[0]) - product("szjk,zm->msjk", re_in, tables_z[1])
    ).astype(jnp.bfloat16)
    tile_count = lax.axis_size("tile")
    kz_part = GZ // tile_count
    spectra = (
        lax.all_to_all(out_re, "tile", split_axis=0, concat_axis=0, tiled=True),
        lax.all_to_all(out_im, "tile", split_axis=0, concat_axis=0, tiled=True),
    )
    owner_re = spectra[0].reshape(tile_count, kz_part, slots, kx_part, GY)
    owner_im = spectra[1].reshape(tile_count, kz_part, slots, kx_part, GY)
    phase_real_part, phase_im = cross_phase(owner_re, owner_im, pairs, tiles_here)
    returned = (
        lax.all_to_all(phase_real_part, "tile", split_axis=0, concat_axis=1, tiled=True),
        lax.all_to_all(phase_im, "tile", split_axis=0, concat_axis=1, tiled=True),
    )
    w_re, w_im = inverse_z(returned[0], returned[1], tables_z)
    v_re, v_im = inverse_x(
        lax.all_to_all(w_re, "zslab", split_axis=1, concat_axis=2, tiled=True),
        lax.all_to_all(w_im, "zslab", split_axis=1, concat_axis=2, tiled=True),
        tables_x,
    )
    return product("pzxk,ky->pzxy", v_re, tables_y[0]) - product("pzxk,ky->pzxy", v_im, tables_y[1])


HALF = GY // 2
PLANES = 4
VMEM_BYTES = 32 * 1024 * 1024


def host_tables(length):
    indices = np.arange(length, dtype=np.int32)
    modular = indices[:, None] * indices[None, :] % length
    angles = modular.astype(np.float32) * np.float32(2.0 * math.pi / length)
    factor = np.float32(1.0 / math.sqrt(length))
    return (
        (np.cos(angles) * factor).astype(jnp.bfloat16),
        (np.sin(angles) * factor).astype(jnp.bfloat16),
    )


def half_y_table():
    cosine, sine = host_tables(GY)
    imag = -sine[:, :HALF]
    imag[:, 0] = cosine[:, HALF]
    return np.concatenate([cosine[:, :HALF], imag], axis=1)


def paired_y_table():
    table = np.zeros((2 * GY, GY), jnp.bfloat16)
    table[::2] = half_y_table() * np.array(0.5, jnp.bfloat16)
    return table


def half_y_inverse():
    cosine, sine = host_tables(GY)
    two = np.array(2.0, jnp.bfloat16)
    real = cosine[:HALF, :] * two
    real[0] = cosine[0]
    imag = -sine[:HALF, :] * two
    imag[0] = cosine[HALF]
    return np.concatenate([real, imag], axis=0)


def mirror_order():
    order = [0, GX // 2]
    for j in range(1, GX // 2):
        order += [j, GX - j]
    return order


def complex_blocks(length, sign):
    cosine, sine = (table.astype(np.float32) for table in host_tables(length))
    return np.array([[cosine, -sign * sine], [sign * sine, cosine]])


def forward_x_table():
    table = np.einsum("oijx,az->joaizx", complex_blocks(GX, -1), np.eye(PLANES))[mirror_order()]
    table = table.reshape(2 * GX * PLANES, 2, PLANES // 2, 2, GX).transpose(0, 1, 2, 4, 3)
    return table.reshape(2 * GX * PLANES, -1).astype(jnp.bfloat16)


def inverse_x_table():
    table = np.einsum("oijx,az->oaxjiz", complex_blocks(GX, 1), np.eye(PLANES))
    return table.reshape(2 * PLANES * GX, -1).astype(jnp.bfloat16)


def z_rows():
    return np.arange(2 * GZ).reshape(2, GZ // PLANES, PLANES).transpose(1, 0, 2).reshape(-1)


def z_tables():
    forward, inverse = (
        complex_blocks(GZ, sign).transpose(0, 2, 1, 3).reshape(2 * GZ, 2 * GZ) for sign in (-1, 1)
    )
    none = np.zeros((2 * GZ, GZ), np.float32)
    forward_last = np.concatenate([none, forward[:, :GZ]], axis=1)
    inverse_last = np.concatenate([none.T, inverse[:GZ]], axis=0)
    order = z_rows()
    return [
        np.ascontiguousarray(table).astype(jnp.bfloat16)
        for table in (
            forward[:, order],
            inverse[order],
            forward_last[:, order],
            inverse_last[order],
        )
    ]


def imaginary_rows(shape):
    return lax.broadcasted_iota(jnp.int32, shape, 0) % (2 * PLANES) >= PLANES


def first_lane(shape):
    return lax.broadcasted_iota(jnp.int32, shape, 1) == 0


def dot(left, right):
    return jnp.dot(left, right, preferred_element_type=jnp.float32)


def analyse_kernel(
    slots, pairs_ref, extents_ref, tile_ref, band_ref, wy_ref, wx_ref, out_ref, crop_ref
):
    slot = pl.program_id(0)

    @pl.when(slot == 0)
    def _():
        for p in range(pairs_ref.shape[1]):
            for end in (0, 1):
                named = pairs_ref[2 * end, p] * FACES + pairs_ref[2 * end + 1, p] - tile_ref[0] * slots

                @pl.when((named >= 0) & (named < slots))
                def _():
                    crop_ref[named, 0] = extents_ref[0, p]
                    crop_ref[named, 1] = extents_ref[1, p]

    plane = (2 * GX, 2 * GY)
    row = lax.broadcasted_iota(jnp.int32, plane, 0)
    live = (row < crop_ref[slot, 0]) & (
        lax.broadcasted_iota(jnp.int32, plane, 1) < crop_ref[slot, 1]
    )
    live = jnp.where(live, 1.0, 0.0)
    even = row % 2 == 0
    groups = (2 * GX // 8, 8, 2 * GY)
    block = (2 * PLANES, HALF)
    lane0, imaginary = first_lane(block), imaginary_rows(block)
    sign = jnp.where(imaginary, -0.5, 0.5)

    def row_pairs(z, shift):
        raw = band_ref[0, 0, z].astype(jnp.float32) * live
        return raw + pltpu.roll(raw.reshape(groups), shift, 1).reshape(plane)

    def cells(z):
        both = jnp.where(even, row_pairs(z, 7), row_pairs(z + 1, 1))
        lanes = [both[:, k : k + 128] for k in range(0, 2 * GY, 128)]
        return jnp.concatenate(
            [(part + pltpu.roll(part, 127, 1)).astype(jnp.bfloat16) for part in lanes], axis=1
        )

    zpart = 4 * PLANES
    for start in range(0, band_ref.shape[2], zpart):
        down = jnp.concatenate([cells(z) for z in range(start, start + zpart, 2)], axis=0)
        y = dot(down, wy_ref[...]).astype(jnp.bfloat16).reshape(zpart // PLANES, PLANES * GX, GY)
        units = [
            jnp.concatenate([y[unit, :, :HALF], y[unit, :, HALF:]], axis=0)
            for unit in range(zpart // PLANES)
        ]
        spectra = dot(wx_ref[...], jnp.concatenate(units, axis=1))

        def at(n):
            rows = spectra[2 * PLANES * n : 2 * PLANES * (n + 1)]
            return [rows[:, k : k + HALF] for k in range(0, rows.shape[1], HALF)]

        def put(j, blocks):
            rows = slice(2 * start, 2 * (start + zpart))
            out_ref[j, 0, rows] = jnp.concatenate(blocks, axis=0).astype(jnp.bfloat16)

        put(0, at(0))
        put(GX // 2, at(1))
        for j in range(1, GX // 2):
            here, mirror = at(2 * j), at(2 * j + 1)
            put(j, [jnp.where(lane0, 0.5 * a + sign * b, a) for a, b in zip(here, mirror)])
            put(
                GX - j,
                [
                    jnp.where(lane0, pltpu.roll(0.5 * a - sign * b, PLANES, 0), b)
                    for a, b in zip(here, mirror)
                ],
            )


def analyse(band, pairs, extents, tile):
    slots, zrows = band.shape[0] * FACES, band.shape[2]
    tables = (paired_y_table(), forward_x_table())
    whole = [pl.BlockSpec(t.shape, lambda i, *_: (0, 0)) for t in tables]
    return pl.pallas_call(
        functools.partial(analyse_kernel, slots),
        grid_spec=pltpu.PrefetchScalarGridSpec(
            num_scalar_prefetch=3,
            grid=(slots,),
            in_specs=[
                pl.BlockSpec(
                    (1, 1, zrows, 2 * GX, 2 * GY), lambda i, *_: (i // FACES, i % FACES, 0, 0, 0)
                )
            ]
            + whole,
            out_specs=pl.BlockSpec((GX, 1, 2 * zrows, HALF), lambda i, *_: (0, i, 0, 0)),
            scratch_shapes=[pltpu.SMEM((slots, 2), jnp.int32)],
        ),
        out_shape=jax.ShapeDtypeStruct((GX, slots, 2 * zrows, HALF), jnp.bfloat16),
        compiler_params=pltpu.CompilerParams(vmem_limit_bytes=VMEM_BYTES + VMEM_BYTES * 3 // 4),
        name="analyse",
    )(pairs, extents, tile, band, *(jnp.asarray(t) for t in tables))


def normalised(a_re, a_im, b_re, b_im):
    cross_re = a_re * b_re + a_im * b_im
    cross_im = a_im * b_re - a_re * b_im
    scale = lax.rsqrt(cross_re * cross_re + cross_im * cross_im + 1.0)
    return (cross_re * scale).astype(jnp.bfloat16), (cross_im * scale).astype(jnp.bfloat16)


def correlate_kernel(
    slabs, tiles_here, pairs_ref, place_ref, in_ref, wz_ref, wzi_ref, wz_last_ref, wzi_last_ref, out_ref
):
    tiles = in_ref.shape[0] // slabs
    total = pairs_ref.shape[1]
    pairs_here = out_ref.shape[1]
    slab_rows = out_ref.shape[2]
    both_real = (place_ref[0] == 0) | (place_ref[0] == GX // 2)
    block = (2 * GZ, HALF)
    shared = first_lane(block) & imaginary_rows(block)

    def load(p, end):
        tile = pairs_ref[2 * end, p]
        row = tile // tiles_here
        pos = tile % tiles_here * FACES + pairs_ref[2 * end + 1, p]
        return jnp.concatenate([in_ref[row + s * tiles, pos] for s in range(slabs)], axis=0)

    def phase_of(table_ref, first, second):
        spec = dot(table_ref[...], jnp.concatenate([first, second], axis=1))
        spec = spec.astype(jnp.bfloat16).astype(jnp.float32)
        phase = normalised(spec[:GZ, :HALF], spec[GZ:, :HALF], spec[:GZ, HALF:], spec[GZ:, HALF:])
        return jnp.concatenate(phase, axis=0)

    keep = jnp.where(shared & both_real, 0.0, 1.0).astype(jnp.bfloat16)
    for p in range(0, total, 2):
        phases = [phase_of(wz_ref, load(q, 0) * keep, load(q, 1) * keep) for q in (p, p + 1)]
        w = dot(wzi_ref[...], jnp.concatenate(phases, axis=1)).astype(jnp.bfloat16)
        for k, q in enumerate((p, p + 1)):
            for s in range(slabs):
                out_ref[q // pairs_here + s * tiles, q % pairs_here] = w[
                    s * slab_rows : (s + 1) * slab_rows, k * HALF : (k + 1) * HALF
                ]

    @pl.when(both_real)
    def _():
        lane = lax.broadcasted_iota(jnp.int32, block, 1)
        ends = [jnp.zeros(block, jnp.float32)] * 2
        for p in range(total):
            for end in (0, 1):
                column = load(p, end).astype(jnp.float32)[:, 0:1]
                ends[end] = jnp.where(lane == p, column, ends[end])
        phase = phase_of(wz_last_ref, *(end.astype(jnp.bfloat16) for end in ends))
        w = dot(wzi_last_ref[...], phase)
        for p in range(total):
            column = w[:, p : p + 1]
            for s in range(slabs):
                rows = slice(s * slab_rows, (s + 1) * slab_rows)
                at = (p // pairs_here + s * tiles, p % pairs_here)
                old = out_ref[at].astype(jnp.float32)
                out_ref[at] = jnp.where(shared[rows], column[rows], old).astype(jnp.bfloat16)


def correlate(spread, pairs, place, slabs, tiles_here):
    devices, _, slab_rows, _ = spread.shape
    pairs_here = pairs.shape[1] * slabs // devices
    tables = z_tables()
    vmem = pl.BlockSpec(memory_space=pltpu.VMEM)
    smem = pl.BlockSpec(memory_space=pltpu.SMEM)
    return pl.pallas_call(
        functools.partial(correlate_kernel, slabs, tiles_here),
        in_specs=[smem, smem] + [vmem] * (1 + len(tables)),
        out_specs=vmem,
        out_shape=jax.ShapeDtypeStruct((devices, pairs_here, slab_rows, HALF), jnp.bfloat16),
        compiler_params=pltpu.CompilerParams(vmem_limit_bytes=VMEM_BYTES),
        name="correlate",
    )(pairs, place, spread, *(jnp.asarray(t) for t in tables))


def synthesise_kernel(in_ref, wx_ref, wy_ref, out_ref):
    zpart = out_ref.shape[1]
    units = zpart // PLANES
    block = (2 * zpart, HALF)
    lane0, imaginary = first_lane(block), imaginary_rows(block)
    sign = jnp.where(imaginary, -1.0, 1.0)
    groups = (units, 2 * PLANES, HALF)

    def at(j):
        return in_ref[j, 0].astype(jnp.float32)

    blocks = [None] * GX
    for j in (0, GX // 2):
        blocks[j] = at(j)
    for j in range(1, GX // 2):
        here, mirror = at(j), at(GX - j)
        swapped = pltpu.roll(mirror.reshape(groups), PLANES, 1).reshape(block)
        blocks[j] = jnp.where(lane0, here + swapped, here)
        blocks[GX - j] = jnp.where(lane0, sign * (here - swapped), mirror)
    stacked = jnp.concatenate(
        [
            jnp.concatenate([b[u * 2 * PLANES : (u + 1) * 2 * PLANES] for b in blocks], axis=0)
            for u in range(units)
        ],
        axis=1,
    ).astype(jnp.bfloat16)
    v = dot(wx_ref[...], stacked).astype(jnp.bfloat16)
    rows = PLANES * GX
    cells = [
        jnp.concatenate([v[:rows, k : k + HALF], v[rows:, k : k + HALF]], axis=1)
        for k in range(0, units * HALF, HALF)
    ]
    maps = dot(jnp.concatenate(cells, axis=0), wy_ref[...])
    out_ref[0] = maps.reshape(zpart, GX, GY)


def synthesise(returned):
    _, pairs_here, slab_rows, _ = returned.shape
    zpart = 4 * PLANES
    tables = (inverse_x_table(), half_y_inverse())
    return pl.pallas_call(
        synthesise_kernel,
        grid=(pairs_here, slab_rows // (2 * zpart)),
        in_specs=[pl.BlockSpec((GX, 1, 2 * zpart, HALF), lambda i, z: (0, i, z, 0))]
        + [pl.BlockSpec(t.shape, lambda i, z: (0, 0)) for t in tables],
        out_specs=pl.BlockSpec((1, zpart, GX, GY), lambda i, z: (i, z, 0, 0)),
        out_shape=jax.ShapeDtypeStruct((pairs_here, slab_rows // 2, GX, GY), jnp.float32),
        compiler_params=pltpu.CompilerParams(vmem_limit_bytes=VMEM_BYTES),
        name="synthesise",
    )(returned, *(jnp.asarray(t) for t in tables))


def shards(band, pairs, extents):
    tiles, slabs = lax.axis_size("tile"), lax.axis_size("zslab")
    zrows = band.shape[2]
    if tiles * slabs != GX or zrows % (4 * PLANES) or pairs.shape[0] % (2 * tiles):
        return general_shards(band, pairs, extents)
    pairs, extents = pairs.T, extents.T
    tile = lax.axis_index("tile").astype(jnp.int32)
    device = lax.axis_index("zslab").astype(jnp.int32) * tiles + tile
    spectra = analyse(band, pairs, extents, tile[None])
    spread = lax.all_to_all(spectra, ("zslab", "tile"), split_axis=0, concat_axis=0, tiled=True)
    w = correlate(spread, pairs, device[None], slabs, band.shape[0])
    returned = lax.all_to_all(w, ("zslab", "tile"), split_axis=0, concat_axis=0, tiled=True)
    return synthesise(returned)


def solution(mesh):
    placed = (P("tile", None, "zslab", None, None), P(), P())
    return jax.shard_map(
        shards,
        mesh=mesh,
        in_specs=placed,
        out_specs=P("tile", "zslab", None, None),
        check_vma=False,
    )
```

```python
import functools
import math


import jax
import jax.numpy as jnp
import numpy as np
from jax import lax
from jax.experimental import pallas as pl
from jax.experimental.pallas import tpu as pltpu
from jax.sharding import PartitionSpec as P

GX = 32
GY = 256
GZ = 128
FACES = 4


def dft_tables(length):
    indices = jnp.arange(length, dtype=jnp.int32)
    modular = indices[:, None] * indices[None, :] % length
    angles = modular.astype(jnp.float32) * (2.0 * math.pi / length)
    factor = 1.0 / math.sqrt(length)
    return (
        (jnp.cos(angles) * factor).astype(jnp.bfloat16),
        (jnp.sin(angles) * factor).astype(jnp.bfloat16),
    )


def product(form, left, right):
    return jnp.einsum(form, left, right, preferred_element_type=jnp.float32)


def reduce_resolution(image_volume, crop_bounds):
    row_mask = (
        jnp.arange(image_volume.shape[2], dtype=jnp.int32)[None, :] < crop_bounds[:, 0:1]
    ).astype(jnp.bfloat16)
    col_mask = (
        jnp.arange(image_volume.shape[3], dtype=jnp.int32)[None, :] < crop_bounds[:, 1:2]
    ).astype(jnp.bfloat16)
    masked = image_volume * row_mask[:, None, :, None] * col_mask[:, None, None, :]
    raw_cols = jnp.arange(image_volume.shape[3], dtype=jnp.int32)
    pooled_cols = jnp.arange(GY, dtype=jnp.int32)
    pooling = jnp.where(raw_cols[:, None] // 2 == pooled_cols[None, :], 0.5, 0.0).astype(
        jnp.bfloat16
    )
    along_pooled = product("szxy,yk->szxk", masked, pooling)
    shaped = along_pooled.reshape(image_volume.shape[0], image_volume.shape[1], GX, 2, GY)
    return (shaped[:, :, :, 0, :] + shaped[:, :, :, 1, :]).astype(jnp.bfloat16)


def cross_phase(owner_re, owner_im, pairs, tiles_here):
    first_dev = pairs[:, 0] // tiles_here
    first_pos = pairs[:, 0] % tiles_here * FACES + pairs[:, 1]
    second_tile_device = pairs[:, 2] // tiles_here
    second_pos = pairs[:, 2] % tiles_here * FACES + pairs[:, 3]
    first_re = owner_re[first_dev, :, first_pos].astype(jnp.float32)
    first_im = owner_im[first_dev, :, first_pos].astype(jnp.float32)
    second_re = owner_re[second_tile_device, :, second_pos].astype(jnp.float32)
    second_im = owner_im[second_tile_device, :, second_pos].astype(jnp.float32)
    cross_re = first_re * second_re + first_im * second_im
    cross_im = first_im * second_re - first_re * second_im
    scaled = jnp.sqrt(cross_re * cross_re + cross_im * cross_im + 1.0)
    return ((cross_re / scaled).astype(jnp.bfloat16), (cross_im / scaled).astype(jnp.bfloat16))


def inverse_z(phase_real_part, phase_im, tables_z):
    w_re = (
        product("pmjk,mz->pzjk", phase_real_part, tables_z[0])
        - product("pmjk,mz->pzjk", phase_im, tables_z[1])
    ).astype(jnp.bfloat16)
    w_im = (
        product("pmjk,mz->pzjk", phase_im, tables_z[0])
        + product("pmjk,mz->pzjk", phase_real_part, tables_z[1])
    ).astype(jnp.bfloat16)
    return (w_re, w_im)


def inverse_x(w_re, w_im, tables_x):
    v_re = (
        product("pzjk,jx->pzxk", w_re, tables_x[0]) - product("pzjk,jx->pzxk", w_im, tables_x[1])
    ).astype(jnp.bfloat16)
    v_im = (
        product("pzjk,jx->pzxk", w_im, tables_x[0]) + product("pzjk,jx->pzxk", w_re, tables_x[1])
    ).astype(jnp.bfloat16)
    return (v_re, v_im)


def general_shards(band, pairs, extents):
    tables_x = dft_tables(GX)
    tables_y = dft_tables(GY)
    tables_z = dft_tables(GZ)
    tiles_here = band.shape[0]
    slots = tiles_here * FACES
    zrows = band.shape[2]
    tile_pos = lax.axis_index("tile")
    global_slot = tile_pos * slots + jnp.arange(slots, dtype=jnp.int32)
    first_slot = pairs[:, 0] * FACES + pairs[:, 1]
    second_slot = pairs[:, 2] * FACES + pairs[:, 3]
    matches = (
        (first_slot[None, :] == global_slot[:, None])
        | (second_slot[None, :] == global_slot[:, None])
    ).astype(jnp.int32)
    crop_bounds = jnp.sum(matches[:, :, None] * extents[None, :, :], axis=1)
    image_volume = band.reshape(slots, zrows, 2 * GX, 2 * GY)
    reduced_volume = reduce_resolution(image_volume, crop_bounds)
    y_re = product("szxy,yk->szxk", reduced_volume, tables_y[0]).astype(jnp.bfloat16)
    y_im = (-product("szxy,yk->szxk", reduced_volume, tables_y[1])).astype(jnp.bfloat16)
    x_re = (
        product("szxk,xj->szjk", y_re, tables_x[0]) + product("szxk,xj->szjk", y_im, tables_x[1])
    ).astype(jnp.bfloat16)
    x_im = (
        product("szxk,xj->szjk", y_im, tables_x[0]) - product("szxk,xj->szjk", y_re, tables_x[1])
    ).astype(jnp.bfloat16)
    kx_part = GX // lax.axis_size("zslab")
    re_in = lax.all_to_all(x_re, "zslab", split_axis=2, concat_axis=1, tiled=True)
    im_in = lax.all_to_all(x_im, "zslab", split_axis=2, concat_axis=1, tiled=True)
    out_re = (
        product("szjk,zm->msjk", re_in, tables_z[0]) + product("szjk,zm->msjk", im_in, tables_z[1])
    ).astype(jnp.bfloat16)
    out_im = (
        product("szjk,zm->msjk", im_in, tables_z[0]) - product("szjk,zm->msjk", re_in, tables_z[1])
    ).astype(jnp.bfloat16)
    tile_count = lax.axis_size("tile")
    kz_part = GZ // tile_count
    spectra = (
        lax.all_to_all(out_re, "tile", split_axis=0, concat_axis=0, tiled=True),
        lax.all_to_all(out_im, "tile", split_axis=0, concat_axis=0, tiled=True),
    )
    owner_re = spectra[0].reshape(tile_count, kz_part, slots, kx_part, GY)
    owner_im = spectra[1].reshape(tile_count, kz_part, slots, kx_part, GY)
    phase_real_part, phase_im = cross_phase(owner_re, owner_im, pairs, tiles_here)
    returned = (
        lax.all_to_all(phase_real_part, "tile", split_axis=0, concat_axis=1, tiled=True),
        lax.all_to_all(phase_im, "tile", split_axis=0, concat_axis=1, tiled=True),
    )
    w_re, w_im = inverse_z(returned[0], returned[1], tables_z)
    v_re, v_im = inverse_x(
        lax.all_to_all(w_re, "zslab", split_axis=1, concat_axis=2, tiled=True),
        lax.all_to_all(w_im, "zslab", split_axis=1, concat_axis=2, tiled=True),
        tables_x,
    )
    return product("pzxk,ky->pzxy", v_re, tables_y[0]) - product("pzxk,ky->pzxy", v_im, tables_y[1])


HALF = GY // 2
PLANES = 4
VMEM_BYTES = 32 * 1024 * 1024


def host_tables(length):
    indices = np.arange(length, dtype=np.int32)
    modular = indices[:, None] * indices[None, :] % length
    angles = modular.astype(np.float32) * np.float32(2.0 * math.pi / length)
    factor = np.float32(1.0 / math.sqrt(length))
    return (
        (np.cos(angles) * factor).astype(jnp.bfloat16),
        (np.sin(angles) * factor).astype(jnp.bfloat16),
    )


def half_y_table():
    cosine, sine = host_tables(GY)
    imag = -sine[:, :HALF]
    imag[:, 0] = cosine[:, HALF]
    return np.concatenate([cosine[:, :HALF], imag], axis=1)


def paired_y_table():
    table = np.zeros((2 * GY, GY), jnp.bfloat16)
    table[::2] = half_y_table() * np.array(0.5, jnp.bfloat16)
    return table


def half_y_inverse():
    cosine, sine = host_tables(GY)
    two = np.array(2.0, jnp.bfloat16)
    real = cosine[:HALF, :] * two
    real[0] = cosine[0]
    imag = -sine[:HALF, :] * two
    imag[0] = cosine[HALF]
    return np.concatenate([real, imag], axis=0)


def mirror_order():
    order = [0, GX // 2]
    for j in range(1, GX // 2):
        order += [j, GX - j]
    return order


def complex_blocks(length, sign):
    cosine, sine = (table.astype(np.float32) for table in host_tables(length))
    return np.array([[cosine, -sign * sine], [sign * sine, cosine]])


def forward_x_table():
    table = np.einsum("oijx,az->joaizx", complex_blocks(GX, -1), np.eye(PLANES))[mirror_order()]
    return table.reshape(2 * GX * PLANES, -1).astype(jnp.bfloat16)


def inverse_x_table():
    table = np.einsum("oijx,az->oaxjiz", complex_blocks(GX, 1), np.eye(PLANES))
    return table.reshape(2 * PLANES * GX, -1).astype(jnp.bfloat16)


def z_rows():
    return np.arange(2 * GZ).reshape(2, GZ // PLANES, PLANES).transpose(1, 0, 2).reshape(-1)


def z_tables():
    forward, inverse = (
        complex_blocks(GZ, sign).transpose(0, 2, 1, 3).reshape(2 * GZ, 2 * GZ) for sign in (-1, 1)
    )
    none = np.zeros((2 * GZ, GZ), np.float32)
    forward_last = np.concatenate([none, forward[:, :GZ]], axis=1)
    inverse_last = np.concatenate([none.T, inverse[:GZ]], axis=0)
    order = z_rows()
    return [
        np.ascontiguousarray(table).astype(jnp.bfloat16)
        for table in (
            forward[:, order],
            inverse[order],
            forward_last[:, order],
            inverse_last[order],
        )
    ]


def imaginary_rows(shape):
    return lax.broadcasted_iota(jnp.int32, shape, 0) % (2 * PLANES) >= PLANES


def first_lane(shape):
    return lax.broadcasted_iota(jnp.int32, shape, 1) == 0


def dot(left, right):
    return jnp.dot(left, right, preferred_element_type=jnp.float32)


def analyse_kernel(
    slots, pairs_ref, extents_ref, tile_ref, *rest
):
    band_refs, (wy_ref, wx_ref, out_ref, crop_ref) = rest[:-4], rest[-4:]
    slot = pl.program_id(0)

    @pl.when(slot == 0)
    def _():
        for p in range(pairs_ref.shape[1]):
            for end in (0, 1):
                named = pairs_ref[2 * end, p] * FACES + pairs_ref[2 * end + 1, p] - tile_ref[0] * slots

                @pl.when((named >= 0) & (named < slots))
                def _():
                    crop_ref[named, 0] = extents_ref[0, p]
                    crop_ref[named, 1] = extents_ref[1, p]

    cells_shape = (GX, 128)
    x = lax.broadcasted_iota(jnp.int32, cells_shape, 0)
    lane = lax.broadcasted_iota(jnp.int32, cells_shape, 1)
    live = [
        [
            jnp.where((2 * x + a < crop_ref[slot, 0]) & (k * 128 + lane < crop_ref[slot, 1]), 1.0, 0.0)
            for a in (0, 1)
        ]
        for k in range(len(band_refs))
    ]
    block = (2 * PLANES, HALF)
    lane0, imaginary = first_lane(block), imaginary_rows(block)
    sign = jnp.where(imaginary, -0.5, 0.5)

    def cells(z):
        parts = []
        for ref, masks in zip(band_refs, live):
            even, odd = (
                ref[0, 0, z, pl.ds(a, GX, stride=2), :].astype(jnp.float32) * masks[a] for a in (0, 1)
            )
            rows = even + odd
            parts.append((rows + pltpu.roll(rows, 127, 1)).astype(jnp.bfloat16))
        return jnp.concatenate(parts, axis=1)

    zpart = 4 * PLANES
    for start in range(0, band_refs[0].shape[2], zpart):
        down = jnp.concatenate([cells(z) for z in range(start, start + zpart)], axis=0)
        y = dot(down, wy_ref[...]).astype(jnp.bfloat16).reshape(zpart // PLANES, PLANES * GX, GY)
        units = [
            jnp.concatenate([y[unit, :, :HALF], y[unit, :, HALF:]], axis=0)
            for unit in range(zpart // PLANES)
        ]
        spectra = dot(wx_ref[...], jnp.concatenate(units, axis=1))

        def at(n):
            rows = spectra[2 * PLANES * n : 2 * PLANES * (n + 1)]
            return [rows[:, k : k + HALF] for k in range(0, rows.shape[1], HALF)]

        def put(j, blocks):
            rows = slice(2 * start, 2 * (start + zpart))
            out_ref[j, 0, rows] = jnp.concatenate(blocks, axis=0).astype(jnp.bfloat16)

        put(0, at(0))
        put(GX // 2, at(1))
        for j in range(1, GX // 2):
            here, mirror = at(2 * j), at(2 * j + 1)
            put(j, [jnp.where(lane0, 0.5 * a + sign * b, a) for a, b in zip(here, mirror)])
            put(
                GX - j,
                [
                    jnp.where(lane0, pltpu.roll(0.5 * a - sign * b, PLANES, 0), b)
                    for a, b in zip(here, mirror)
                ],
            )


def analyse(band, pairs, extents, tile):
    slots, zrows = band.shape[0] * FACES, band.shape[2]
    tables = (paired_y_table(), forward_x_table())
    whole = [pl.BlockSpec(t.shape, lambda i, *_: (0, 0)) for t in tables]
    lane_blocks = 2 * GY // 128
    return pl.pallas_call(
        functools.partial(analyse_kernel, slots),
        grid_spec=pltpu.PrefetchScalarGridSpec(
            num_scalar_prefetch=3,
            grid=(slots,),
            in_specs=[
                pl.BlockSpec(
                    (1, 1, zrows, 2 * GX, 128),
                    lambda i, *_, k=k: (i // FACES, i % FACES, 0, 0, k),
                )
                for k in range(lane_blocks)
            ]
            + whole,
            out_specs=pl.BlockSpec((GX, 1, 2 * zrows, HALF), lambda i, *_: (0, i, 0, 0)),
            scratch_shapes=[pltpu.SMEM((slots, 2), jnp.int32)],
        ),
        out_shape=jax.ShapeDtypeStruct((GX, slots, 2 * zrows, HALF), jnp.bfloat16),
        compiler_params=pltpu.CompilerParams(vmem_limit_bytes=VMEM_BYTES + VMEM_BYTES * 3 // 4),
        name="analyse",
    )(pairs, extents, tile, *[band] * lane_blocks, *(jnp.asarray(t) for t in tables))


def normalised(a_re, a_im, b_re, b_im):
    cross_re = a_re * b_re + a_im * b_im
    cross_im = a_im * b_re - a_re * b_im
    scale = lax.rsqrt(cross_re * cross_re + cross_im * cross_im + 1.0)
    return (cross_re * scale).astype(jnp.bfloat16), (cross_im * scale).astype(jnp.bfloat16)


def correlate_kernel(
    slabs, tiles_here, pairs_ref, place_ref, in_ref, wz_ref, wzi_ref, wz_last_ref, wzi_last_ref, out_ref
):
    tiles = in_ref.shape[0] // slabs
    total = pairs_ref.shape[1]
    pairs_here = out_ref.shape[1]
    slab_rows = out_ref.shape[2]
    both_real = (place_ref[0] == 0) | (place_ref[0] == GX // 2)
    block = (2 * GZ, HALF)
    shared = first_lane(block) & imaginary_rows(block)

    def load(p, end):
        tile = pairs_ref[2 * end, p]
        row = tile // tiles_here
        pos = tile % tiles_here * FACES + pairs_ref[2 * end + 1, p]
        return jnp.concatenate([in_ref[row + s * tiles, pos] for s in range(slabs)], axis=0)

    def phase_of(table_ref, first, second):
        spec = dot(table_ref[...], jnp.concatenate([first, second], axis=1))
        spec = spec.astype(jnp.bfloat16).astype(jnp.float32)
        phase = normalised(spec[:GZ, :HALF], spec[GZ:, :HALF], spec[:GZ, HALF:], spec[GZ:, HALF:])
        return jnp.concatenate(phase, axis=0)

    keep = jnp.where(shared & both_real, 0.0, 1.0).astype(jnp.bfloat16)
    for p in range(0, total, 2):
        phases = [phase_of(wz_ref, load(q, 0) * keep, load(q, 1) * keep) for q in (p, p + 1)]
        w = dot(wzi_ref[...], jnp.concatenate(phases, axis=1)).astype(jnp.bfloat16)
        for k, q in enumerate((p, p + 1)):
            for s in range(slabs):
                out_ref[q // pairs_here + s * tiles, q % pairs_here] = w[
                    s * slab_rows : (s + 1) * slab_rows, k * HALF : (k + 1) * HALF
                ]

    @pl.when(both_real)
    def _():
        lane = lax.broadcasted_iota(jnp.int32, block, 1)
        ends = [jnp.zeros(block, jnp.bfloat16)] * 2
        for p in range(total):
            for end in (0, 1):
                ends[end] = jnp.where(lane == p, load(p, end)[:, 0:1], ends[end])
        w = dot(wzi_last_ref[...], phase_of(wz_last_ref, *ends)).astype(jnp.bfloat16)
        for p in range(total):
            column = w[:, p : p + 1]
            for s in range(slabs):
                rows = slice(s * slab_rows, (s + 1) * slab_rows)
                at = (p // pairs_here + s * tiles, p % pairs_here)
                out_ref[at] = jnp.where(shared[rows], column[rows], out_ref[at])


def correlate(spread, pairs, place, slabs, tiles_here):
    devices, _, slab_rows, _ = spread.shape
    pairs_here = pairs.shape[1] * slabs // devices
    tables = z_tables()
    vmem = pl.BlockSpec(memory_space=pltpu.VMEM)
    smem = pl.BlockSpec(memory_space=pltpu.SMEM)
    return pl.pallas_call(
        functools.partial(correlate_kernel, slabs, tiles_here),
        in_specs=[smem, smem] + [vmem] * (1 + len(tables)),
        out_specs=vmem,
        out_shape=jax.ShapeDtypeStruct((devices, pairs_here, slab_rows, HALF), jnp.bfloat16),
        compiler_params=pltpu.CompilerParams(vmem_limit_bytes=VMEM_BYTES),
        name="correlate",
    )(pairs, place, spread, *(jnp.asarray(t) for t in tables))


def synthesise_kernel(in_ref, wx_ref, wy_ref, out_ref):
    zpart = out_ref.shape[1]
    units = zpart // PLANES
    block = (2 * zpart, HALF)
    lane0, imaginary = first_lane(block), imaginary_rows(block)
    sign = jnp.where(imaginary, -1.0, 1.0)
    groups = (units, 2 * PLANES, HALF)

    def at(j):
        return in_ref[j, 0].astype(jnp.float32)

    blocks = [None] * GX
    for j in (0, GX // 2):
        blocks[j] = at(j)
    for j in range(1, GX // 2):
        here, mirror = at(j), at(GX - j)
        swapped = pltpu.roll(mirror.reshape(groups), PLANES, 1).reshape(block)
        blocks[j] = jnp.where(lane0, here + swapped, here)
        blocks[GX - j] = jnp.where(lane0, sign * (here - swapped), mirror)
    stacked = jnp.concatenate(
        [
            jnp.concatenate([b[u * 2 * PLANES : (u + 1) * 2 * PLANES] for b in blocks], axis=0)
            for u in range(units)
        ],
        axis=1,
    ).astype(jnp.bfloat16)
    v = dot(wx_ref[...], stacked).astype(jnp.bfloat16)
    rows = PLANES * GX
    cells = [
        jnp.concatenate([v[:rows, k : k + HALF], v[rows:, k : k + HALF]], axis=1)
        for k in range(0, units * HALF, HALF)
    ]
    maps = dot(jnp.concatenate(cells, axis=0), wy_ref[...])
    out_ref[0] = maps.reshape(zpart, GX, GY)


def synthesise(returned):
    _, pairs_here, slab_rows, _ = returned.shape
    zpart = 4 * PLANES
    tables = (inverse_x_table(), half_y_inverse())
    return pl.pallas_call(
        synthesise_kernel,
        grid=(pairs_here, slab_rows // (2 * zpart)),
        in_specs=[pl.BlockSpec((GX, 1, 2 * zpart, HALF), lambda i, z: (0, i, z, 0))]
        + [pl.BlockSpec(t.shape, lambda i, z: (0, 0)) for t in tables],
        out_specs=pl.BlockSpec((1, zpart, GX, GY), lambda i, z: (i, z, 0, 0)),
        out_shape=jax.ShapeDtypeStruct((pairs_here, slab_rows // 2, GX, GY), jnp.float32),
        compiler_params=pltpu.CompilerParams(vmem_limit_bytes=VMEM_BYTES),
        name="synthesise",
    )(returned, *(jnp.asarray(t) for t in tables))


def shards(band, pairs, extents):
    tiles, slabs = lax.axis_size("tile"), lax.axis_size("zslab")
    zrows = band.shape[2]
    if tiles * slabs != GX or zrows % (4 * PLANES) or pairs.shape[0] % (2 * tiles):
        return general_shards(band, pairs, extents)
    pairs, extents = pairs.T, extents.T
    tile = lax.axis_index("tile").astype(jnp.int32)
    device = lax.axis_index("zslab").astype(jnp.int32) * tiles + tile
    spectra = analyse(band, pairs, extents, tile[None])
    spread = lax.all_to_all(spectra, ("zslab", "tile"), split_axis=0, concat_axis=0, tiled=True)
    w = correlate(spread, pairs, device[None], slabs, band.shape[0])
    returned = lax.all_to_all(w, ("zslab", "tile"), split_axis=0, concat_axis=0, tiled=True)
    return synthesise(returned)


def solution(mesh):
    placed = (P("tile", None, "zslab", None, None), P(), P())
    return jax.shard_map(
        shards,
        mesh=mesh,
        in_specs=placed,
        out_specs=P("tile", "zslab", None, None),
        check_vma=False,
    )
```

```python
import functools
import math


import jax
import jax.numpy as jnp
import numpy as np
from jax import lax
from jax.experimental import pallas as pl
from jax.experimental.pallas import tpu as pltpu
from jax.sharding import PartitionSpec as P

GX = 32
GY = 256
GZ = 128
FACES = 4


def dft_tables(length):
    indices = jnp.arange(length, dtype=jnp.int32)
    modular = indices[:, None] * indices[None, :] % length
    angles = modular.astype(jnp.float32) * (2.0 * math.pi / length)
    factor = 1.0 / math.sqrt(length)
    return (
        (jnp.cos(angles) * factor).astype(jnp.bfloat16),
        (jnp.sin(angles) * factor).astype(jnp.bfloat16),
    )


def product(form, left, right):
    return jnp.einsum(form, left, right, preferred_element_type=jnp.float32)


def reduce_resolution(image_volume, crop_bounds):
    row_mask = (
        jnp.arange(image_volume.shape[2], dtype=jnp.int32)[None, :] < crop_bounds[:, 0:1]
    ).astype(jnp.bfloat16)
    col_mask = (
        jnp.arange(image_volume.shape[3], dtype=jnp.int32)[None, :] < crop_bounds[:, 1:2]
    ).astype(jnp.bfloat16)
    masked = image_volume * row_mask[:, None, :, None] * col_mask[:, None, None, :]
    raw_cols = jnp.arange(image_volume.shape[3], dtype=jnp.int32)
    pooled_cols = jnp.arange(GY, dtype=jnp.int32)
    pooling = jnp.where(raw_cols[:, None] // 2 == pooled_cols[None, :], 0.5, 0.0).astype(
        jnp.bfloat16
    )
    along_pooled = product("szxy,yk->szxk", masked, pooling)
    shaped = along_pooled.reshape(image_volume.shape[0], image_volume.shape[1], GX, 2, GY)
    return (shaped[:, :, :, 0, :] + shaped[:, :, :, 1, :]).astype(jnp.bfloat16)


def cross_phase(owner_re, owner_im, pairs, tiles_here):
    first_dev = pairs[:, 0] // tiles_here
    first_pos = pairs[:, 0] % tiles_here * FACES + pairs[:, 1]
    second_tile_device = pairs[:, 2] // tiles_here
    second_pos = pairs[:, 2] % tiles_here * FACES + pairs[:, 3]
    first_re = owner_re[first_dev, :, first_pos].astype(jnp.float32)
    first_im = owner_im[first_dev, :, first_pos].astype(jnp.float32)
    second_re = owner_re[second_tile_device, :, second_pos].astype(jnp.float32)
    second_im = owner_im[second_tile_device, :, second_pos].astype(jnp.float32)
    cross_re = first_re * second_re + first_im * second_im
    cross_im = first_im * second_re - first_re * second_im
    scaled = jnp.sqrt(cross_re * cross_re + cross_im * cross_im + 1.0)
    return ((cross_re / scaled).astype(jnp.bfloat16), (cross_im / scaled).astype(jnp.bfloat16))


def inverse_z(phase_real_part, phase_im, tables_z):
    w_re = (
        product("pmjk,mz->pzjk", phase_real_part, tables_z[0])
        - product("pmjk,mz->pzjk", phase_im, tables_z[1])
    ).astype(jnp.bfloat16)
    w_im = (
        product("pmjk,mz->pzjk", phase_im, tables_z[0])
        + product("pmjk,mz->pzjk", phase_real_part, tables_z[1])
    ).astype(jnp.bfloat16)
    return (w_re, w_im)


def inverse_x(w_re, w_im, tables_x):
    v_re = (
        product("pzjk,jx->pzxk", w_re, tables_x[0]) - product("pzjk,jx->pzxk", w_im, tables_x[1])
    ).astype(jnp.bfloat16)
    v_im = (
        product("pzjk,jx->pzxk", w_im, tables_x[0]) + product("pzjk,jx->pzxk", w_re, tables_x[1])
    ).astype(jnp.bfloat16)
    return (v_re, v_im)


def general_shards(band, pairs, extents):
    tables_x = dft_tables(GX)
    tables_y = dft_tables(GY)
    tables_z = dft_tables(GZ)
    tiles_here = band.shape[0]
    slots = tiles_here * FACES
    zrows = band.shape[2]
    tile_pos = lax.axis_index("tile")
    global_slot = tile_pos * slots + jnp.arange(slots, dtype=jnp.int32)
    first_slot = pairs[:, 0] * FACES + pairs[:, 1]
    second_slot = pairs[:, 2] * FACES + pairs[:, 3]
    matches = (
        (first_slot[None, :] == global_slot[:, None])
        | (second_slot[None, :] == global_slot[:, None])
    ).astype(jnp.int32)
    crop_bounds = jnp.sum(matches[:, :, None] * extents[None, :, :], axis=1)
    image_volume = band.reshape(slots, zrows, 2 * GX, 2 * GY)
    reduced_volume = reduce_resolution(image_volume, crop_bounds)
    y_re = product("szxy,yk->szxk", reduced_volume, tables_y[0]).astype(jnp.bfloat16)
    y_im = (-product("szxy,yk->szxk", reduced_volume, tables_y[1])).astype(jnp.bfloat16)
    x_re = (
        product("szxk,xj->szjk", y_re, tables_x[0]) + product("szxk,xj->szjk", y_im, tables_x[1])
    ).astype(jnp.bfloat16)
    x_im = (
        product("szxk,xj->szjk", y_im, tables_x[0]) - product("szxk,xj->szjk", y_re, tables_x[1])
    ).astype(jnp.bfloat16)
    kx_part = GX // lax.axis_size("zslab")
    re_in = lax.all_to_all(x_re, "zslab", split_axis=2, concat_axis=1, tiled=True)
    im_in = lax.all_to_all(x_im, "zslab", split_axis=2, concat_axis=1, tiled=True)
    out_re = (
        product("szjk,zm->msjk", re_in, tables_z[0]) + product("szjk,zm->msjk", im_in, tables_z[1])
    ).astype(jnp.bfloat16)
    out_im = (
        product("szjk,zm->msjk", im_in, tables_z[0]) - product("szjk,zm->msjk", re_in, tables_z[1])
    ).astype(jnp.bfloat16)
    tile_count = lax.axis_size("tile")
    kz_part = GZ // tile_count
    spectra = (
        lax.all_to_all(out_re, "tile", split_axis=0, concat_axis=0, tiled=True),
        lax.all_to_all(out_im, "tile", split_axis=0, concat_axis=0, tiled=True),
    )
    owner_re = spectra[0].reshape(tile_count, kz_part, slots, kx_part, GY)
    owner_im = spectra[1].reshape(tile_count, kz_part, slots, kx_part, GY)
    phase_real_part, phase_im = cross_phase(owner_re, owner_im, pairs, tiles_here)
    returned = (
        lax.all_to_all(phase_real_part, "tile", split_axis=0, concat_axis=1, tiled=True),
        lax.all_to_all(phase_im, "tile", split_axis=0, concat_axis=1, tiled=True),
    )
    w_re, w_im = inverse_z(returned[0], returned[1], tables_z)
    v_re, v_im = inverse_x(
        lax.all_to_all(w_re, "zslab", split_axis=1, concat_axis=2, tiled=True),
        lax.all_to_all(w_im, "zslab", split_axis=1, concat_axis=2, tiled=True),
        tables_x,
    )
    return product("pzxk,ky->pzxy", v_re, tables_y[0]) - product("pzxk,ky->pzxy", v_im, tables_y[1])


HALF = GY // 2
PLANES = 4
VMEM_BYTES = 32 * 1024 * 1024


def host_tables(length):
    indices = np.arange(length, dtype=np.int32)
    modular = indices[:, None] * indices[None, :] % length
    angles = modular.astype(np.float32) * np.float32(2.0 * math.pi / length)
    factor = np.float32(1.0 / math.sqrt(length))
    return (
        (np.cos(angles) * factor).astype(jnp.bfloat16),
        (np.sin(angles) * factor).astype(jnp.bfloat16),
    )


def half_y_table():
    cosine, sine = host_tables(GY)
    imag = -sine[:, :HALF]
    imag[:, 0] = cosine[:, HALF]
    return np.concatenate([cosine[:, :HALF], imag], axis=1)


def paired_y_table():
    table = np.zeros((2 * GY, GY), jnp.bfloat16)
    table[::2] = half_y_table() * np.array(0.5, jnp.bfloat16)
    return table


def half_y_inverse():
    cosine, sine = host_tables(GY)
    two = np.array(2.0, jnp.bfloat16)
    real = cosine[:HALF, :] * two
    real[0] = cosine[0]
    imag = -sine[:HALF, :] * two
    imag[0] = cosine[HALF]
    return np.concatenate([real, imag], axis=0)


def mirror_order():
    order = [0, GX // 2]
    for j in range(1, GX // 2):
        order += [j, GX - j]
    return order


def complex_blocks(length, sign):
    cosine, sine = (table.astype(np.float32) for table in host_tables(length))
    return np.array([[cosine, -sign * sine], [sign * sine, cosine]])


def forward_x_table():
    table = np.einsum("oijx,az->joaizx", complex_blocks(GX, -1), np.eye(PLANES))[mirror_order()]
    return table.reshape(2 * GX * PLANES, -1).astype(jnp.bfloat16)


def inverse_x_table():
    table = np.einsum("oijx,az->oaxjiz", complex_blocks(GX, 1), np.eye(PLANES))
    return table.reshape(2 * PLANES * GX, -1).astype(jnp.bfloat16)


def z_rows():
    return np.arange(2 * GZ).reshape(2, GZ // PLANES, PLANES).transpose(1, 0, 2).reshape(-1)


def z_tables():
    forward, inverse = (
        complex_blocks(GZ, sign).transpose(0, 2, 1, 3).reshape(2 * GZ, 2 * GZ) for sign in (-1, 1)
    )
    none = np.zeros((2 * GZ, GZ), np.float32)
    forward_last = np.concatenate([none, forward[:, :GZ]], axis=1)
    inverse_last = np.concatenate([none.T, inverse[:GZ]], axis=0)
    order = z_rows()
    return [
        np.ascontiguousarray(table).astype(jnp.bfloat16)
        for table in (
            forward[:, order],
            inverse[order],
            forward_last[:, order],
            inverse_last[order],
        )
    ]


def imaginary_rows(shape):
    return lax.broadcasted_iota(jnp.int32, shape, 0) % (2 * PLANES) >= PLANES


def first_lane(shape):
    return lax.broadcasted_iota(jnp.int32, shape, 1) == 0


def dot(left, right):
    return jnp.dot(left, right, preferred_element_type=jnp.float32)


def analyse_kernel(
    pairs_ref,
    extents_ref,
    tile_ref,
    band_ref,
    wy_in_ref,
    wx_in_ref,
    out_ref,
    crop_ref,
    raw_ref,
    wy_ref,
    wx_ref,
    down_ref,
    spec_ref,
    table_sems,
    raw_sems,
    spec_sems,
):
    parts, lane_blocks, zpart = raw_ref.shape[:3]
    slots = crop_ref.shape[0]
    per_slot = parts // slots

    def fetch(p, k):
        slot, z = p // per_slot, p % per_slot * zpart
        source = band_ref.at[
            slot // FACES, slot % FACES, pl.ds(z, zpart), :, pl.ds(k * 128, 128)
        ]
        return pltpu.make_async_copy(source, raw_ref.at[p, k], raw_sems.at[p, k])

    def leave(p):
        rows = pl.ds(p % per_slot * 2 * zpart, 2 * zpart)
        return pltpu.make_async_copy(
            spec_ref.at[p], out_ref.at[:, p // per_slot, rows], spec_sems.at[p]
        )

    tables = [
        pltpu.make_async_copy(wy_in_ref, wy_ref, table_sems.at[0]),
        pltpu.make_async_copy(wx_in_ref, wx_ref, table_sems.at[1]),
    ]
    fetches = [[fetch(p, k) for k in range(lane_blocks)] for p in range(parts)]
    leaves = [leave(p) for p in range(parts)]
    for copy in fetches[0] + tables:
        copy.start()
    for copies in fetches[1:]:
        for copy in copies:
            copy.start()

    for p in range(pairs_ref.shape[1]):
        for end in (0, 1):
            named = pairs_ref[2 * end, p] * FACES + pairs_ref[2 * end + 1, p] - tile_ref[0] * slots

            @pl.when((named >= 0) & (named < slots))
            def _():
                crop_ref[named, 0] = extents_ref[0, p]
                crop_ref[named, 1] = extents_ref[1, p]

    cells_shape = (GX, 128)
    x = lax.broadcasted_iota(jnp.int32, cells_shape, 0)
    lane = lax.broadcasted_iota(jnp.int32, cells_shape, 1)
    block = (2 * PLANES, HALF)
    lane0, imaginary = first_lane(block), imaginary_rows(block)
    sign = jnp.where(imaginary, -0.5, 0.5)

    def pool(p):
        across, along = crop_ref[p // per_slot, 0], crop_ref[p // per_slot, 1]
        for k in range(lane_blocks):
            masks = [
                jnp.where((2 * x + a < across) & (k * 128 + lane < along), 1.0, 0.0) for a in (0, 1)
            ]
            for z in range(zpart):
                even, odd = (
                    raw_ref[p, k, z, pl.ds(a, GX, stride=2), :].astype(jnp.float32) * masks[a]
                    for a in (0, 1)
                )
                rows = even + odd
                down_ref[p % 2, z * GX : (z + 1) * GX, k * 128 : (k + 1) * 128] = (
                    rows + pltpu.roll(rows, 127, 1)
                ).astype(jnp.bfloat16)

    def transform(p):
        y = dot(down_ref[p % 2], wy_ref[...]).astype(jnp.bfloat16)
        y = y.reshape(zpart // PLANES, PLANES * GX, GY)
        units = [
            jnp.concatenate([y[unit, :, :HALF], y[unit, :, HALF:]], axis=0)
            for unit in range(zpart // PLANES)
        ]
        spectra = dot(wx_ref[...], jnp.concatenate(units, axis=1))

        def at(n):
            rows = spectra[2 * PLANES * n : 2 * PLANES * (n + 1)]
            return [rows[:, k : k + HALF] for k in range(0, rows.shape[1], HALF)]

        def put(j, blocks):
            spec_ref[p, j] = jnp.concatenate(blocks, axis=0).astype(jnp.bfloat16)

        put(0, at(0))
        put(GX // 2, at(1))
        for j in range(1, GX // 2):
            here, mirror = at(2 * j), at(2 * j + 1)
            put(j, [jnp.where(lane0, 0.5 * a + sign * b, a) for a, b in zip(here, mirror)])
            put(
                GX - j,
                [
                    jnp.where(lane0, pltpu.roll(0.5 * a - sign * b, PLANES, 0), b)
                    for a, b in zip(here, mirror)
                ],
            )

    for p in range(parts + 1):
        if p < parts:
            for copy in fetches[p]:
                copy.wait()
        if p == 1:
            for copy in tables:
                copy.wait()
        if p < parts:
            pool(p)
        if p > 0:
            transform(p - 1)
            leaves[p - 1].start()
    for copy in leaves:
        copy.wait()


def analyse(band, pairs, extents, tile):
    slots, zrows = band.shape[0] * FACES, band.shape[2]
    zpart = 4 * PLANES
    parts = slots * zrows // zpart
    lane_blocks = 2 * GY // 128
    tables = (paired_y_table(), forward_x_table())
    smem = pl.BlockSpec(memory_space=pltpu.SMEM)
    anywhere = pl.BlockSpec(memory_space=pl.ANY)
    return pl.pallas_call(
        analyse_kernel,
        in_specs=[smem] * 3 + [anywhere] * (1 + len(tables)),
        out_specs=anywhere,
        out_shape=jax.ShapeDtypeStruct((GX, slots, 2 * zrows, HALF), jnp.bfloat16),
        scratch_shapes=[
            pltpu.SMEM((slots, 2), jnp.int32),
            pltpu.VMEM((parts, lane_blocks, zpart, 2 * GX, 128), jnp.bfloat16),
            *[pltpu.VMEM(t.shape, jnp.bfloat16) for t in tables],
            pltpu.VMEM((2, zpart * GX, 2 * GY), jnp.bfloat16),
            pltpu.VMEM((parts, GX, 2 * zpart, HALF), jnp.bfloat16),
            pltpu.SemaphoreType.DMA((len(tables),)),
            pltpu.SemaphoreType.DMA((parts, lane_blocks)),
            pltpu.SemaphoreType.DMA((parts,)),
        ],
        compiler_params=pltpu.CompilerParams(vmem_limit_bytes=VMEM_BYTES + VMEM_BYTES * 3 // 4),
        name="analyse",
    )(pairs, extents, tile, band, *(jnp.asarray(t) for t in tables))


def normalised(a_re, a_im, b_re, b_im):
    cross_re = a_re * b_re + a_im * b_im
    cross_im = a_im * b_re - a_re * b_im
    scale = lax.rsqrt(cross_re * cross_re + cross_im * cross_im + 1.0)
    return (cross_re * scale).astype(jnp.bfloat16), (cross_im * scale).astype(jnp.bfloat16)


def correlate_kernel(
    slabs, tiles_here, pairs_ref, place_ref, in_ref, wz_ref, wzi_ref, wz_last_ref, wzi_last_ref, out_ref
):
    tiles = in_ref.shape[0] // slabs
    total = pairs_ref.shape[1]
    pairs_here = out_ref.shape[1]
    slab_rows = out_ref.shape[2]
    both_real = (place_ref[0] == 0) | (place_ref[0] == GX // 2)
    block = (2 * GZ, HALF)
    shared = first_lane(block) & imaginary_rows(block)

    def load(p, end):
        tile = pairs_ref[2 * end, p]
        row = tile // tiles_here
        pos = tile % tiles_here * FACES + pairs_ref[2 * end + 1, p]
        return jnp.concatenate([in_ref[row + s * tiles, pos] for s in range(slabs)], axis=0)

    def phase_of(table_ref, first, second):
        spec = dot(table_ref[...], jnp.concatenate([first, second], axis=1))
        spec = spec.astype(jnp.bfloat16).astype(jnp.float32)
        phase = normalised(spec[:GZ, :HALF], spec[GZ:, :HALF], spec[:GZ, HALF:], spec[GZ:, HALF:])
        return jnp.concatenate(phase, axis=0)

    keep = jnp.where(shared & both_real, 0.0, 1.0).astype(jnp.bfloat16)
    for p in range(0, total, 2):
        phases = [phase_of(wz_ref, load(q, 0) * keep, load(q, 1) * keep) for q in (p, p + 1)]
        w = dot(wzi_ref[...], jnp.concatenate(phases, axis=1)).astype(jnp.bfloat16)
        for k, q in enumerate((p, p + 1)):
            for s in range(slabs):
                out_ref[q // pairs_here + s * tiles, q % pairs_here] = w[
                    s * slab_rows : (s + 1) * slab_rows, k * HALF : (k + 1) * HALF
                ]

    @pl.when(both_real)
    def _():
        lane = lax.broadcasted_iota(jnp.int32, block, 1)
        ends = [jnp.zeros(block, jnp.bfloat16)] * 2
        for p in range(total):
            for end in (0, 1):
                ends[end] = jnp.where(lane == p, load(p, end)[:, 0:1], ends[end])
        w = dot(wzi_last_ref[...], phase_of(wz_last_ref, *ends)).astype(jnp.bfloat16)
        for p in range(total):
            column = w[:, p : p + 1]
            for s in range(slabs):
                rows = slice(s * slab_rows, (s + 1) * slab_rows)
                at = (p // pairs_here + s * tiles, p % pairs_here)
                out_ref[at] = jnp.where(shared[rows], column[rows], out_ref[at])


def correlate(spread, pairs, place, slabs, tiles_here):
    devices, _, slab_rows, _ = spread.shape
    pairs_here = pairs.shape[1] * slabs // devices
    tables = z_tables()
    vmem = pl.BlockSpec(memory_space=pltpu.VMEM)
    smem = pl.BlockSpec(memory_space=pltpu.SMEM)
    return pl.pallas_call(
        functools.partial(correlate_kernel, slabs, tiles_here),
        in_specs=[smem, smem] + [vmem] * (1 + len(tables)),
        out_specs=vmem,
        out_shape=jax.ShapeDtypeStruct((devices, pairs_here, slab_rows, HALF), jnp.bfloat16),
        compiler_params=pltpu.CompilerParams(vmem_limit_bytes=VMEM_BYTES),
        name="correlate",
    )(pairs, place, spread, *(jnp.asarray(t) for t in tables))


def synthesise_kernel(in_ref, wx_ref, wy_ref, out_ref):
    zpart = out_ref.shape[1]
    units = zpart // PLANES
    block = (2 * zpart, HALF)
    lane0, imaginary = first_lane(block), imaginary_rows(block)
    sign = jnp.where(imaginary, -1.0, 1.0)
    groups = (units, 2 * PLANES, HALF)

    def at(j):
        return in_ref[j, 0].astype(jnp.float32)

    blocks = [None] * GX
    for j in (0, GX // 2):
        blocks[j] = at(j)
    for j in range(1, GX // 2):
        here, mirror = at(j), at(GX - j)
        swapped = pltpu.roll(mirror.reshape(groups), PLANES, 1).reshape(block)
        blocks[j] = jnp.where(lane0, here + swapped, here)
        blocks[GX - j] = jnp.where(lane0, sign * (here - swapped), mirror)
    stacked = jnp.concatenate(
        [
            jnp.concatenate([b[u * 2 * PLANES : (u + 1) * 2 * PLANES] for b in blocks], axis=0)
            for u in range(units)
        ],
        axis=1,
    ).astype(jnp.bfloat16)
    v = dot(wx_ref[...], stacked).astype(jnp.bfloat16)
    rows = PLANES * GX
    cells = [
        jnp.concatenate([v[:rows, k : k + HALF], v[rows:, k : k + HALF]], axis=1)
        for k in range(0, units * HALF, HALF)
    ]
    maps = dot(jnp.concatenate(cells, axis=0), wy_ref[...])
    out_ref[0] = maps.reshape(zpart, GX, GY)


def synthesise(returned):
    _, pairs_here, slab_rows, _ = returned.shape
    zpart = 4 * PLANES
    tables = (inverse_x_table(), half_y_inverse())
    return pl.pallas_call(
        synthesise_kernel,
        grid=(pairs_here, slab_rows // (2 * zpart)),
        in_specs=[pl.BlockSpec((GX, 1, 2 * zpart, HALF), lambda i, z: (0, i, z, 0))]
        + [pl.BlockSpec(t.shape, lambda i, z: (0, 0)) for t in tables],
        out_specs=pl.BlockSpec((1, zpart, GX, GY), lambda i, z: (i, z, 0, 0)),
        out_shape=jax.ShapeDtypeStruct((pairs_here, slab_rows // 2, GX, GY), jnp.float32),
        compiler_params=pltpu.CompilerParams(vmem_limit_bytes=VMEM_BYTES),
        name="synthesise",
    )(returned, *(jnp.asarray(t) for t in tables))


def shards(band, pairs, extents):
    tiles, slabs = lax.axis_size("tile"), lax.axis_size("zslab")
    zrows = band.shape[2]
    if tiles * slabs != GX or zrows % (4 * PLANES) or pairs.shape[0] % (2 * tiles):
        return general_shards(band, pairs, extents)
    pairs, extents = pairs.T, extents.T
    tile = lax.axis_index("tile").astype(jnp.int32)
    device = lax.axis_index("zslab").astype(jnp.int32) * tiles + tile
    spectra = analyse(band, pairs, extents, tile[None])
    spread = lax.all_to_all(spectra, ("zslab", "tile"), split_axis=0, concat_axis=0, tiled=True)
    w = correlate(spread, pairs, device[None], slabs, band.shape[0])
    returned = lax.all_to_all(w, ("zslab", "tile"), split_axis=0, concat_axis=0, tiled=True)
    return synthesise(returned)


def solution(mesh):
    placed = (P("tile", None, "zslab", None, None), P(), P())
    return jax.shard_map(
        shards,
        mesh=mesh,
        in_specs=placed,
        out_specs=P("tile", "zslab", None, None),
        check_vma=False,
    )
```

```python
import functools
import math


import jax
import jax.numpy as jnp
import numpy as np
from jax import lax
from jax.experimental import pallas as pl
from jax.experimental.pallas import tpu as pltpu
from jax.sharding import PartitionSpec as P

GX = 32
GY = 256
GZ = 128
FACES = 4


def dft_tables(length):
    indices = jnp.arange(length, dtype=jnp.int32)
    modular = indices[:, None] * indices[None, :] % length
    angles = modular.astype(jnp.float32) * (2.0 * math.pi / length)
    factor = 1.0 / math.sqrt(length)
    return (
        (jnp.cos(angles) * factor).astype(jnp.bfloat16),
        (jnp.sin(angles) * factor).astype(jnp.bfloat16),
    )


def product(form, left, right):
    return jnp.einsum(form, left, right, preferred_element_type=jnp.float32)


def reduce_resolution(image_volume, crop_bounds):
    row_mask = (
        jnp.arange(image_volume.shape[2], dtype=jnp.int32)[None, :] < crop_bounds[:, 0:1]
    ).astype(jnp.bfloat16)
    col_mask = (
        jnp.arange(image_volume.shape[3], dtype=jnp.int32)[None, :] < crop_bounds[:, 1:2]
    ).astype(jnp.bfloat16)
    masked = image_volume * row_mask[:, None, :, None] * col_mask[:, None, None, :]
    raw_cols = jnp.arange(image_volume.shape[3], dtype=jnp.int32)
    pooled_cols = jnp.arange(GY, dtype=jnp.int32)
    pooling = jnp.where(raw_cols[:, None] // 2 == pooled_cols[None, :], 0.5, 0.0).astype(
        jnp.bfloat16
    )
    along_pooled = product("szxy,yk->szxk", masked, pooling)
    shaped = along_pooled.reshape(image_volume.shape[0], image_volume.shape[1], GX, 2, GY)
    return (shaped[:, :, :, 0, :] + shaped[:, :, :, 1, :]).astype(jnp.bfloat16)


def cross_phase(owner_re, owner_im, pairs, tiles_here):
    first_dev = pairs[:, 0] // tiles_here
    first_pos = pairs[:, 0] % tiles_here * FACES + pairs[:, 1]
    second_tile_device = pairs[:, 2] // tiles_here
    second_pos = pairs[:, 2] % tiles_here * FACES + pairs[:, 3]
    first_re = owner_re[first_dev, :, first_pos].astype(jnp.float32)
    first_im = owner_im[first_dev, :, first_pos].astype(jnp.float32)
    second_re = owner_re[second_tile_device, :, second_pos].astype(jnp.float32)
    second_im = owner_im[second_tile_device, :, second_pos].astype(jnp.float32)
    cross_re = first_re * second_re + first_im * second_im
    cross_im = first_im * second_re - first_re * second_im
    scaled = jnp.sqrt(cross_re * cross_re + cross_im * cross_im + 1.0)
    return ((cross_re / scaled).astype(jnp.bfloat16), (cross_im / scaled).astype(jnp.bfloat16))


def inverse_z(phase_real_part, phase_im, tables_z):
    w_re = (
        product("pmjk,mz->pzjk", phase_real_part, tables_z[0])
        - product("pmjk,mz->pzjk", phase_im, tables_z[1])
    ).astype(jnp.bfloat16)
    w_im = (
        product("pmjk,mz->pzjk", phase_im, tables_z[0])
        + product("pmjk,mz->pzjk", phase_real_part, tables_z[1])
    ).astype(jnp.bfloat16)
    return (w_re, w_im)


def inverse_x(w_re, w_im, tables_x):
    v_re = (
        product("pzjk,jx->pzxk", w_re, tables_x[0]) - product("pzjk,jx->pzxk", w_im, tables_x[1])
    ).astype(jnp.bfloat16)
    v_im = (
        product("pzjk,jx->pzxk", w_im, tables_x[0]) + product("pzjk,jx->pzxk", w_re, tables_x[1])
    ).astype(jnp.bfloat16)
    return (v_re, v_im)


def general_shards(band, pairs, extents):
    tables_x = dft_tables(GX)
    tables_y = dft_tables(GY)
    tables_z = dft_tables(GZ)
    tiles_here = band.shape[0]
    slots = tiles_here * FACES
    zrows = band.shape[2]
    tile_pos = lax.axis_index("tile")
    global_slot = tile_pos * slots + jnp.arange(slots, dtype=jnp.int32)
    first_slot = pairs[:, 0] * FACES + pairs[:, 1]
    second_slot = pairs[:, 2] * FACES + pairs[:, 3]
    matches = (
        (first_slot[None, :] == global_slot[:, None])
        | (second_slot[None, :] == global_slot[:, None])
    ).astype(jnp.int32)
    crop_bounds = jnp.sum(matches[:, :, None] * extents[None, :, :], axis=1)
    image_volume = band.reshape(slots, zrows, 2 * GX, 2 * GY)
    reduced_volume = reduce_resolution(image_volume, crop_bounds)
    y_re = product("szxy,yk->szxk", reduced_volume, tables_y[0]).astype(jnp.bfloat16)
    y_im = (-product("szxy,yk->szxk", reduced_volume, tables_y[1])).astype(jnp.bfloat16)
    x_re = (
        product("szxk,xj->szjk", y_re, tables_x[0]) + product("szxk,xj->szjk", y_im, tables_x[1])
    ).astype(jnp.bfloat16)
    x_im = (
        product("szxk,xj->szjk", y_im, tables_x[0]) - product("szxk,xj->szjk", y_re, tables_x[1])
    ).astype(jnp.bfloat16)
    kx_part = GX // lax.axis_size("zslab")
    re_in = lax.all_to_all(x_re, "zslab", split_axis=2, concat_axis=1, tiled=True)
    im_in = lax.all_to_all(x_im, "zslab", split_axis=2, concat_axis=1, tiled=True)
    out_re = (
        product("szjk,zm->msjk", re_in, tables_z[0]) + product("szjk,zm->msjk", im_in, tables_z[1])
    ).astype(jnp.bfloat16)
    out_im = (
        product("szjk,zm->msjk", im_in, tables_z[0]) - product("szjk,zm->msjk", re_in, tables_z[1])
    ).astype(jnp.bfloat16)
    tile_count = lax.axis_size("tile")
    kz_part = GZ // tile_count
    spectra = (
        lax.all_to_all(out_re, "tile", split_axis=0, concat_axis=0, tiled=True),
        lax.all_to_all(out_im, "tile", split_axis=0, concat_axis=0, tiled=True),
    )
    owner_re = spectra[0].reshape(tile_count, kz_part, slots, kx_part, GY)
    owner_im = spectra[1].reshape(tile_count, kz_part, slots, kx_part, GY)
    phase_real_part, phase_im = cross_phase(owner_re, owner_im, pairs, tiles_here)
    returned = (
        lax.all_to_all(phase_real_part, "tile", split_axis=0, concat_axis=1, tiled=True),
        lax.all_to_all(phase_im, "tile", split_axis=0, concat_axis=1, tiled=True),
    )
    w_re, w_im = inverse_z(returned[0], returned[1], tables_z)
    v_re, v_im = inverse_x(
        lax.all_to_all(w_re, "zslab", split_axis=1, concat_axis=2, tiled=True),
        lax.all_to_all(w_im, "zslab", split_axis=1, concat_axis=2, tiled=True),
        tables_x,
    )
    return product("pzxk,ky->pzxy", v_re, tables_y[0]) - product("pzxk,ky->pzxy", v_im, tables_y[1])


HALF = GY // 2
PLANES = 4
VMEM_BYTES = 32 * 1024 * 1024


def host_tables(length):
    indices = np.arange(length, dtype=np.int32)
    modular = indices[:, None] * indices[None, :] % length
    angles = modular.astype(np.float32) * np.float32(2.0 * math.pi / length)
    factor = np.float32(1.0 / math.sqrt(length))
    return (
        (np.cos(angles) * factor).astype(jnp.bfloat16),
        (np.sin(angles) * factor).astype(jnp.bfloat16),
    )


def half_y_table():
    cosine, sine = host_tables(GY)
    imag = -sine[:, :HALF]
    imag[:, 0] = cosine[:, HALF]
    return np.concatenate([cosine[:, :HALF], imag], axis=1)


def paired_y_table():
    table = np.zeros((2 * GY, GY), jnp.bfloat16)
    table[::2] = half_y_table() * np.array(0.5, jnp.bfloat16)
    return table


def half_y_inverse():
    cosine, sine = host_tables(GY)
    two = np.array(2.0, jnp.bfloat16)
    real = cosine[:HALF, :] * two
    real[0] = cosine[0]
    imag = -sine[:HALF, :] * two
    imag[0] = cosine[HALF]
    return np.concatenate([real, imag], axis=0)


def mirror_order():
    order = [0, GX // 2]
    for j in range(1, GX // 2):
        order += [j, GX - j]
    return order


def complex_blocks(length, sign):
    cosine, sine = (table.astype(np.float32) for table in host_tables(length))
    return np.array([[cosine, -sign * sine], [sign * sine, cosine]])


def forward_x_table():
    table = np.einsum("oijx,az->joaizx", complex_blocks(GX, -1), np.eye(PLANES))[mirror_order()]
    return table.reshape(2 * GX * PLANES, -1).astype(jnp.bfloat16)


def inverse_x_table():
    table = np.einsum("oijx,az->oaxjiz", complex_blocks(GX, 1), np.eye(PLANES))
    return table.reshape(2 * PLANES * GX, -1).astype(jnp.bfloat16)


def z_rows():
    return np.arange(2 * GZ).reshape(2, GZ // PLANES, PLANES).transpose(1, 0, 2).reshape(-1)


def z_tables():
    forward, inverse = (
        complex_blocks(GZ, sign).transpose(0, 2, 1, 3).reshape(2 * GZ, 2 * GZ) for sign in (-1, 1)
    )
    none = np.zeros((2 * GZ, GZ), np.float32)
    forward_last = np.concatenate([none, forward[:, :GZ]], axis=1)
    inverse_last = np.concatenate([none.T, inverse[:GZ]], axis=0)
    order = z_rows()
    return [
        np.ascontiguousarray(table).astype(jnp.bfloat16)
        for table in (
            forward[:, order],
            inverse[order],
            forward_last[:, order],
            inverse_last[order],
        )
    ]


def imaginary_rows(shape):
    return lax.broadcasted_iota(jnp.int32, shape, 0) % (2 * PLANES) >= PLANES


def first_lane(shape):
    return lax.broadcasted_iota(jnp.int32, shape, 1) == 0


def dot(left, right):
    return jnp.dot(left, right, preferred_element_type=jnp.float32)


def analyse_kernel(
    slots, pairs_ref, extents_ref, tile_ref, *rest
):
    band_refs, (wy_ref, wx_ref, out_ref, crop_ref) = rest[:-4], rest[-4:]
    slot = pl.program_id(0)

    @pl.when((slot == 0) & (pl.program_id(1) == 0))
    def _():
        for p in range(pairs_ref.shape[1]):
            for end in (0, 1):
                named = pairs_ref[2 * end, p] * FACES + pairs_ref[2 * end + 1, p] - tile_ref[0] * slots

                @pl.when((named >= 0) & (named < slots))
                def _():
                    crop_ref[named, 0] = extents_ref[0, p]
                    crop_ref[named, 1] = extents_ref[1, p]

    cells_shape = (GX, 128)
    x = lax.broadcasted_iota(jnp.int32, cells_shape, 0)
    lane = lax.broadcasted_iota(jnp.int32, cells_shape, 1)
    live = [
        [
            jnp.where((2 * x + a < crop_ref[slot, 0]) & (k * 128 + lane < crop_ref[slot, 1]), 1.0, 0.0)
            for a in (0, 1)
        ]
        for k in range(len(band_refs))
    ]
    block = (2 * PLANES, HALF)
    lane0, imaginary = first_lane(block), imaginary_rows(block)
    sign = jnp.where(imaginary, -0.5, 0.5)

    def cells(z):
        parts = []
        for ref, masks in zip(band_refs, live):
            even, odd = (
                ref[0, 0, z, pl.ds(a, GX, stride=2), :].astype(jnp.float32) * masks[a] for a in (0, 1)
            )
            rows = even + odd
            parts.append((rows + pltpu.roll(rows, 127, 1)).astype(jnp.bfloat16))
        return jnp.concatenate(parts, axis=1)

    zpart = 4 * PLANES
    for start in range(0, band_refs[0].shape[2], zpart):
        down = jnp.concatenate([cells(z) for z in range(start, start + zpart)], axis=0)
        y = dot(down, wy_ref[...]).astype(jnp.bfloat16).reshape(zpart // PLANES, PLANES * GX, GY)
        units = [
            jnp.concatenate([y[unit, :, :HALF], y[unit, :, HALF:]], axis=0)
            for unit in range(zpart // PLANES)
        ]
        spectra = dot(wx_ref[...], jnp.concatenate(units, axis=1))

        def at(n):
            rows = spectra[2 * PLANES * n : 2 * PLANES * (n + 1)]
            return [rows[:, k : k + HALF] for k in range(0, rows.shape[1], HALF)]

        def put(j, blocks):
            rows = slice(2 * start, 2 * (start + zpart))
            out_ref[j, 0, rows] = jnp.concatenate(blocks, axis=0).astype(jnp.bfloat16)

        put(0, at(0))
        put(GX // 2, at(1))
        for j in range(1, GX // 2):
            here, mirror = at(2 * j), at(2 * j + 1)
            put(j, [jnp.where(lane0, 0.5 * a + sign * b, a) for a, b in zip(here, mirror)])
            put(
                GX - j,
                [
                    jnp.where(lane0, pltpu.roll(0.5 * a - sign * b, PLANES, 0), b)
                    for a, b in zip(here, mirror)
                ],
            )


def analyse(band, pairs, extents, tile):
    slots, zrows = band.shape[0] * FACES, band.shape[2]
    tables = (paired_y_table(), forward_x_table())
    whole = [pl.BlockSpec(t.shape, lambda i, *_: (0, 0)) for t in tables]
    lane_blocks = 2 * GY // 128
    zpart = 4 * PLANES
    return pl.pallas_call(
        functools.partial(analyse_kernel, slots),
        grid_spec=pltpu.PrefetchScalarGridSpec(
            num_scalar_prefetch=3,
            grid=(slots, zrows // zpart),
            in_specs=[
                pl.BlockSpec(
                    (1, 1, zpart, 2 * GX, 128),
                    lambda i, z, *_, k=k: (i // FACES, i % FACES, z, 0, k),
                )
                for k in range(lane_blocks)
            ]
            + whole,
            out_specs=pl.BlockSpec((GX, 1, 2 * zpart, HALF), lambda i, z, *_: (0, i, z, 0)),
            scratch_shapes=[pltpu.SMEM((slots, 2), jnp.int32)],
        ),
        out_shape=jax.ShapeDtypeStruct((GX, slots, 2 * zrows, HALF), jnp.bfloat16),
        compiler_params=pltpu.CompilerParams(vmem_limit_bytes=VMEM_BYTES + VMEM_BYTES * 3 // 4),
        name="analyse",
    )(pairs, extents, tile, *[band] * lane_blocks, *(jnp.asarray(t) for t in tables))


def normalised(a_re, a_im, b_re, b_im):
    cross_re = a_re * b_re + a_im * b_im
    cross_im = a_im * b_re - a_re * b_im
    scale = lax.rsqrt(cross_re * cross_re + cross_im * cross_im + 1.0)
    return (cross_re * scale).astype(jnp.bfloat16), (cross_im * scale).astype(jnp.bfloat16)


def correlate_kernel(
    slabs, tiles_here, pairs_ref, place_ref, in_ref, wz_ref, wzi_ref, wz_last_ref, wzi_last_ref, out_ref
):
    tiles = in_ref.shape[0] // slabs
    total = pairs_ref.shape[1]
    pairs_here = out_ref.shape[1]
    slab_rows = out_ref.shape[2]
    both_real = (place_ref[0] == 0) | (place_ref[0] == GX // 2)
    block = (2 * GZ, HALF)
    shared = first_lane(block) & imaginary_rows(block)

    def load(p, end):
        tile = pairs_ref[2 * end, p]
        row = tile // tiles_here
        pos = tile % tiles_here * FACES + pairs_ref[2 * end + 1, p]
        return jnp.concatenate([in_ref[row + s * tiles, pos] for s in range(slabs)], axis=0)

    def phase_of(table_ref, first, second):
        spec = dot(table_ref[...], jnp.concatenate([first, second], axis=1))
        spec = spec.astype(jnp.bfloat16).astype(jnp.float32)
        phase = normalised(spec[:GZ, :HALF], spec[GZ:, :HALF], spec[:GZ, HALF:], spec[GZ:, HALF:])
        return jnp.concatenate(phase, axis=0)

    keep = jnp.where(shared & both_real, 0.0, 1.0).astype(jnp.bfloat16)
    lane = lax.broadcasted_iota(jnp.int32, block, 1)
    ends = [jnp.zeros(block, jnp.bfloat16)] * 2
    for p in range(total):
        for end in (0, 1):
            ends[end] = jnp.where(lane == p, load(p, end)[:, 0:1], ends[end])
    last = dot(wzi_last_ref[...], phase_of(wz_last_ref, *ends)).astype(jnp.bfloat16)
    fix = shared & both_real
    for p in range(0, total, 2):
        phases = [phase_of(wz_ref, load(q, 0) * keep, load(q, 1) * keep) for q in (p, p + 1)]
        w = dot(wzi_ref[...], jnp.concatenate(phases, axis=1)).astype(jnp.bfloat16)
        for k, q in enumerate((p, p + 1)):
            whole = jnp.where(fix, last[:, q : q + 1], w[:, k * HALF : (k + 1) * HALF])
            for s in range(slabs):
                out_ref[q // pairs_here + s * tiles, q % pairs_here] = whole[
                    s * slab_rows : (s + 1) * slab_rows
                ]


def correlate(spread, pairs, place, slabs, tiles_here):
    devices, _, slab_rows, _ = spread.shape
    pairs_here = pairs.shape[1] * slabs // devices
    tables = z_tables()
    vmem = pl.BlockSpec(memory_space=pltpu.VMEM)
    smem = pl.BlockSpec(memory_space=pltpu.SMEM)
    return pl.pallas_call(
        functools.partial(correlate_kernel, slabs, tiles_here),
        in_specs=[smem, smem] + [vmem] * (1 + len(tables)),
        out_specs=vmem,
        out_shape=jax.ShapeDtypeStruct((devices, pairs_here, slab_rows, HALF), jnp.bfloat16),
        compiler_params=pltpu.CompilerParams(vmem_limit_bytes=VMEM_BYTES),
        name="correlate",
    )(pairs, place, spread, *(jnp.asarray(t) for t in tables))


def synthesise_kernel(in_ref, wx_ref, wy_ref, out_ref):
    zpart = out_ref.shape[1]
    units = zpart // PLANES
    block = (2 * zpart, HALF)
    lane0, imaginary = first_lane(block), imaginary_rows(block)
    sign = jnp.where(imaginary, -1.0, 1.0)
    groups = (units, 2 * PLANES, HALF)

    def at(j):
        return in_ref[j, 0].astype(jnp.float32)

    blocks = [None] * GX
    for j in (0, GX // 2):
        blocks[j] = at(j)
    for j in range(1, GX // 2):
        here, mirror = at(j), at(GX - j)
        swapped = pltpu.roll(mirror.reshape(groups), PLANES, 1).reshape(block)
        blocks[j] = jnp.where(lane0, here + swapped, here)
        blocks[GX - j] = jnp.where(lane0, sign * (here - swapped), mirror)
    stacked = jnp.concatenate(
        [
            jnp.concatenate([b[u * 2 * PLANES : (u + 1) * 2 * PLANES] for b in blocks], axis=0)
            for u in range(units)
        ],
        axis=1,
    ).astype(jnp.bfloat16)
    v = dot(wx_ref[...], stacked).astype(jnp.bfloat16)
    rows = PLANES * GX
    cells = [
        jnp.concatenate([v[:rows, k : k + HALF], v[rows:, k : k + HALF]], axis=1)
        for k in range(0, units * HALF, HALF)
    ]
    maps = dot(jnp.concatenate(cells, axis=0), wy_ref[...])
    out_ref[0] = maps.reshape(zpart, GX, GY)


def synthesise(returned):
    _, pairs_here, slab_rows, _ = returned.shape
    zpart = slab_rows // 2
    tables = (inverse_x_table(), half_y_inverse())
    return pl.pallas_call(
        synthesise_kernel,
        grid=(pairs_here, slab_rows // (2 * zpart)),
        in_specs=[pl.BlockSpec((GX, 1, 2 * zpart, HALF), lambda i, z: (0, i, z, 0))]
        + [pl.BlockSpec(t.shape, lambda i, z: (0, 0)) for t in tables],
        out_specs=pl.BlockSpec((1, zpart, GX, GY), lambda i, z: (i, z, 0, 0)),
        out_shape=jax.ShapeDtypeStruct((pairs_here, slab_rows // 2, GX, GY), jnp.float32),
        compiler_params=pltpu.CompilerParams(vmem_limit_bytes=VMEM_BYTES),
        name="synthesise",
    )(returned, *(jnp.asarray(t) for t in tables))


def shards(band, pairs, extents):
    tiles, slabs = lax.axis_size("tile"), lax.axis_size("zslab")
    zrows = band.shape[2]
    if tiles * slabs != GX or zrows % (4 * PLANES) or pairs.shape[0] % (2 * tiles):
        return general_shards(band, pairs, extents)
    pairs, extents = pairs.T, extents.T
    tile = lax.axis_index("tile").astype(jnp.int32)
    device = lax.axis_index("zslab").astype(jnp.int32) * tiles + tile
    spectra = analyse(band, pairs, extents, tile[None])
    spread = lax.all_to_all(spectra, ("zslab", "tile"), split_axis=0, concat_axis=0, tiled=True)
    w = correlate(spread, pairs, device[None], slabs, band.shape[0])
    returned = lax.all_to_all(w, ("zslab", "tile"), split_axis=0, concat_axis=0, tiled=True)
    return synthesise(returned)


def solution(mesh):
    placed = (P("tile", None, "zslab", None, None), P(), P())
    return jax.shard_map(
        shards,
        mesh=mesh,
        in_specs=placed,
        out_specs=P("tile", "zslab", None, None),
        check_vma=False,
    )
```

```python
import functools
import math


import jax
import jax.numpy as jnp
import numpy as np
from jax import lax
from jax.experimental import pallas as pl
from jax.experimental.pallas import tpu as pltpu
from jax.sharding import PartitionSpec as P

GX = 32
GY = 256
GZ = 128
FACES = 4


def dft_tables(length):
    indices = jnp.arange(length, dtype=jnp.int32)
    modular = indices[:, None] * indices[None, :] % length
    angles = modular.astype(jnp.float32) * (2.0 * math.pi / length)
    factor = 1.0 / math.sqrt(length)
    return (
        (jnp.cos(angles) * factor).astype(jnp.bfloat16),
        (jnp.sin(angles) * factor).astype(jnp.bfloat16),
    )


def product(form, left, right):
    return jnp.einsum(form, left, right, preferred_element_type=jnp.float32)


def reduce_resolution(image_volume, crop_bounds):
    row_mask = (
        jnp.arange(image_volume.shape[2], dtype=jnp.int32)[None, :] < crop_bounds[:, 0:1]
    ).astype(jnp.bfloat16)
    col_mask = (
        jnp.arange(image_volume.shape[3], dtype=jnp.int32)[None, :] < crop_bounds[:, 1:2]
    ).astype(jnp.bfloat16)
    masked = image_volume * row_mask[:, None, :, None] * col_mask[:, None, None, :]
    raw_cols = jnp.arange(image_volume.shape[3], dtype=jnp.int32)
    pooled_cols = jnp.arange(GY, dtype=jnp.int32)
    pooling = jnp.where(raw_cols[:, None] // 2 == pooled_cols[None, :], 0.5, 0.0).astype(
        jnp.bfloat16
    )
    along_pooled = product("szxy,yk->szxk", masked, pooling)
    shaped = along_pooled.reshape(image_volume.shape[0], image_volume.shape[1], GX, 2, GY)
    return (shaped[:, :, :, 0, :] + shaped[:, :, :, 1, :]).astype(jnp.bfloat16)


def cross_phase(owner_re, owner_im, pairs, tiles_here):
    first_dev = pairs[:, 0] // tiles_here
    first_pos = pairs[:, 0] % tiles_here * FACES + pairs[:, 1]
    second_tile_device = pairs[:, 2] // tiles_here
    second_pos = pairs[:, 2] % tiles_here * FACES + pairs[:, 3]
    first_re = owner_re[first_dev, :, first_pos].astype(jnp.float32)
    first_im = owner_im[first_dev, :, first_pos].astype(jnp.float32)
    second_re = owner_re[second_tile_device, :, second_pos].astype(jnp.float32)
    second_im = owner_im[second_tile_device, :, second_pos].astype(jnp.float32)
    cross_re = first_re * second_re + first_im * second_im
    cross_im = first_im * second_re - first_re * second_im
    scaled = jnp.sqrt(cross_re * cross_re + cross_im * cross_im + 1.0)
    return ((cross_re / scaled).astype(jnp.bfloat16), (cross_im / scaled).astype(jnp.bfloat16))


def inverse_z(phase_real_part, phase_im, tables_z):
    w_re = (
        product("pmjk,mz->pzjk", phase_real_part, tables_z[0])
        - product("pmjk,mz->pzjk", phase_im, tables_z[1])
    ).astype(jnp.bfloat16)
    w_im = (
        product("pmjk,mz->pzjk", phase_im, tables_z[0])
        + product("pmjk,mz->pzjk", phase_real_part, tables_z[1])
    ).astype(jnp.bfloat16)
    return (w_re, w_im)


def inverse_x(w_re, w_im, tables_x):
    v_re = (
        product("pzjk,jx->pzxk", w_re, tables_x[0]) - product("pzjk,jx->pzxk", w_im, tables_x[1])
    ).astype(jnp.bfloat16)
    v_im = (
        product("pzjk,jx->pzxk", w_im, tables_x[0]) + product("pzjk,jx->pzxk", w_re, tables_x[1])
    ).astype(jnp.bfloat16)
    return (v_re, v_im)


def general_shards(band, pairs, extents):
    tables_x = dft_tables(GX)
    tables_y = dft_tables(GY)
    tables_z = dft_tables(GZ)
    tiles_here = band.shape[0]
    slots = tiles_here * FACES
    zrows = band.shape[2]
    tile_pos = lax.axis_index("tile")
    global_slot = tile_pos * slots + jnp.arange(slots, dtype=jnp.int32)
    first_slot = pairs[:, 0] * FACES + pairs[:, 1]
    second_slot = pairs[:, 2] * FACES + pairs[:, 3]
    matches = (
        (first_slot[None, :] == global_slot[:, None])
        | (second_slot[None, :] == global_slot[:, None])
    ).astype(jnp.int32)
    crop_bounds = jnp.sum(matches[:, :, None] * extents[None, :, :], axis=1)
    image_volume = band.reshape(slots, zrows, 2 * GX, 2 * GY)
    reduced_volume = reduce_resolution(image_volume, crop_bounds)
    y_re = product("szxy,yk->szxk", reduced_volume, tables_y[0]).astype(jnp.bfloat16)
    y_im = (-product("szxy,yk->szxk", reduced_volume, tables_y[1])).astype(jnp.bfloat16)
    x_re = (
        product("szxk,xj->szjk", y_re, tables_x[0]) + product("szxk,xj->szjk", y_im, tables_x[1])
    ).astype(jnp.bfloat16)
    x_im = (
        product("szxk,xj->szjk", y_im, tables_x[0]) - product("szxk,xj->szjk", y_re, tables_x[1])
    ).astype(jnp.bfloat16)
    kx_part = GX // lax.axis_size("zslab")
    re_in = lax.all_to_all(x_re, "zslab", split_axis=2, concat_axis=1, tiled=True)
    im_in = lax.all_to_all(x_im, "zslab", split_axis=2, concat_axis=1, tiled=True)
    out_re = (
        product("szjk,zm->msjk", re_in, tables_z[0]) + product("szjk,zm->msjk", im_in, tables_z[1])
    ).astype(jnp.bfloat16)
    out_im = (
        product("szjk,zm->msjk", im_in, tables_z[0]) - product("szjk,zm->msjk", re_in, tables_z[1])
    ).astype(jnp.bfloat16)
    tile_count = lax.axis_size("tile")
    kz_part = GZ // tile_count
    spectra = (
        lax.all_to_all(out_re, "tile", split_axis=0, concat_axis=0, tiled=True),
        lax.all_to_all(out_im, "tile", split_axis=0, concat_axis=0, tiled=True),
    )
    owner_re = spectra[0].reshape(tile_count, kz_part, slots, kx_part, GY)
    owner_im = spectra[1].reshape(tile_count, kz_part, slots, kx_part, GY)
    phase_real_part, phase_im = cross_phase(owner_re, owner_im, pairs, tiles_here)
    returned = (
        lax.all_to_all(phase_real_part, "tile", split_axis=0, concat_axis=1, tiled=True),
        lax.all_to_all(phase_im, "tile", split_axis=0, concat_axis=1, tiled=True),
    )
    w_re, w_im = inverse_z(returned[0], returned[1], tables_z)
    v_re, v_im = inverse_x(
        lax.all_to_all(w_re, "zslab", split_axis=1, concat_axis=2, tiled=True),
        lax.all_to_all(w_im, "zslab", split_axis=1, concat_axis=2, tiled=True),
        tables_x,
    )
    return product("pzxk,ky->pzxy", v_re, tables_y[0]) - product("pzxk,ky->pzxy", v_im, tables_y[1])


HALF = GY // 2
PLANES = 4
VMEM_BYTES = 32 * 1024 * 1024


def host_tables(length):
    indices = np.arange(length, dtype=np.int32)
    modular = indices[:, None] * indices[None, :] % length
    angles = modular.astype(np.float32) * np.float32(2.0 * math.pi / length)
    factor = np.float32(1.0 / math.sqrt(length))
    return (
        (np.cos(angles) * factor).astype(jnp.bfloat16),
        (np.sin(angles) * factor).astype(jnp.bfloat16),
    )


def half_y_table():
    cosine, sine = host_tables(GY)
    imag = -sine[:, :HALF]
    imag[:, 0] = cosine[:, HALF]
    return np.concatenate([cosine[:, :HALF], imag], axis=1)


def paired_y_table():
    table = np.zeros((2 * GY, GY), jnp.bfloat16)
    table[::2] = half_y_table() * np.array(0.5, jnp.bfloat16)
    return table


def half_y_inverse():
    cosine, sine = host_tables(GY)
    two = np.array(2.0, jnp.bfloat16)
    real = cosine[:HALF, :] * two
    real[0] = cosine[0]
    imag = -sine[:HALF, :] * two
    imag[0] = cosine[HALF]
    return np.concatenate([real, imag], axis=0)


def mirror_order():
    order = [0, GX // 2]
    for j in range(1, GX // 2):
        order += [j, GX - j]
    return order


def complex_blocks(length, sign):
    cosine, sine = (table.astype(np.float32) for table in host_tables(length))
    return np.array([[cosine, -sign * sine], [sign * sine, cosine]])


def forward_x_table():
    table = np.einsum("oijx,az->joaizx", complex_blocks(GX, -1), np.eye(PLANES))[mirror_order()]
    table = table.reshape(2 * GX * PLANES, 2, PLANES // 2, 2, GX).transpose(0, 1, 2, 4, 3)
    return table.reshape(2 * GX * PLANES, -1).astype(jnp.bfloat16)


def inverse_x_table():
    table = np.einsum("oijx,az->oaxjiz", complex_blocks(GX, 1), np.eye(PLANES))
    return table.reshape(2 * PLANES * GX, -1).astype(jnp.bfloat16)


def z_rows():
    return np.arange(2 * GZ).reshape(2, GZ // PLANES, PLANES).transpose(1, 0, 2).reshape(-1)


def z_tables():
    forward, inverse = (
        complex_blocks(GZ, sign).transpose(0, 2, 1, 3).reshape(2 * GZ, 2 * GZ) for sign in (-1, 1)
    )
    none = np.zeros((2 * GZ, GZ), np.float32)
    forward_last = np.concatenate([none, forward[:, :GZ]], axis=1)
    inverse_last = np.concatenate([none.T, inverse[:GZ]], axis=0)
    order = z_rows()
    return [
        np.ascontiguousarray(table).astype(jnp.bfloat16)
        for table in (
            forward[:, order],
            inverse[order],
            forward_last[:, order],
            inverse_last[order],
        )
    ]


def imaginary_rows(shape):
    return lax.broadcasted_iota(jnp.int32, shape, 0) % (2 * PLANES) >= PLANES


def first_lane(shape):
    return lax.broadcasted_iota(jnp.int32, shape, 1) == 0


def dot(left, right):
    return jnp.dot(left, right, preferred_element_type=jnp.float32)


def analyse_kernel(
    pairs_ref,
    extents_ref,
    tile_ref,
    band_ref,
    wy_in_ref,
    wx_in_ref,
    out_ref,
    crop_ref,
    raw_ref,
    wy_ref,
    wx_ref,
    spec_ref,
    table_sems,
    raw_sems,
    spec_sems,
):
    slots, zrows = raw_ref.shape[:2]
    zpart = 4 * PLANES

    def fetch(slot, part):
        zs = pl.ds(part * zpart, zpart)
        return pltpu.make_async_copy(
            band_ref.at[slot // FACES, slot % FACES, zs], raw_ref.at[slot, zs], raw_sems.at[slot, part]
        )

    def leave(slot):
        return pltpu.make_async_copy(spec_ref.at[slot], out_ref.at[:, slot], spec_sems.at[slot])

    tables = [
        pltpu.make_async_copy(wy_in_ref, wy_ref, table_sems.at[0]),
        pltpu.make_async_copy(wx_in_ref, wx_ref, table_sems.at[1]),
    ]
    parts = range(zrows // zpart)
    fetch(0, 0).start()
    for copy in tables:
        copy.start()
    for slot in range(slots):
        for part in parts:
            if slot or part:
                fetch(slot, part).start()

    for p in range(pairs_ref.shape[1]):
        for end in (0, 1):
            named = pairs_ref[2 * end, p] * FACES + pairs_ref[2 * end + 1, p] - tile_ref[0] * slots

            @pl.when((named >= 0) & (named < slots))
            def _():
                crop_ref[named, 0] = extents_ref[0, p]
                crop_ref[named, 1] = extents_ref[1, p]

    plane = (2 * GX, 2 * GY)
    row = lax.broadcasted_iota(jnp.int32, plane, 0)
    col = lax.broadcasted_iota(jnp.int32, plane, 1)
    even = row % 2 == 0
    groups = (2 * GX // 8, 8, 2 * GY)
    block = (2 * PLANES, HALF)
    lane0, imaginary = first_lane(block), imaginary_rows(block)
    sign = jnp.where(imaginary, -0.5, 0.5)
    for copy in tables:
        copy.wait()

    def transform(slot, part, live):
        def row_pairs(z, shift):
            raw = (raw_ref[slot, z] * live).astype(jnp.float32)
            return raw + pltpu.roll(raw.reshape(groups), shift, 1).reshape(plane)

        def cells(z):
            both = jnp.where(even, row_pairs(z, 7), row_pairs(z + 1, 1))
            lanes = [both[:, k : k + 128] for k in range(0, 2 * GY, 128)]
            return jnp.concatenate(
                [(one + pltpu.roll(one, 127, 1)).astype(jnp.bfloat16) for one in lanes], axis=1
            )

        start = part * zpart
        down = jnp.concatenate([cells(z) for z in range(start, start + zpart, 2)], axis=0)
        y = dot(down, wy_ref[...]).astype(jnp.bfloat16).reshape(zpart // PLANES, PLANES * GX, GY)
        units = [
            jnp.concatenate([y[unit, :, :HALF], y[unit, :, HALF:]], axis=0)
            for unit in range(zpart // PLANES)
        ]
        spectra = dot(wx_ref[...], jnp.concatenate(units, axis=1))

        def at(n):
            rows = spectra[2 * PLANES * n : 2 * PLANES * (n + 1)]
            return [rows[:, k : k + HALF] for k in range(0, rows.shape[1], HALF)]

        def put(j, blocks):
            rows = slice(2 * start, 2 * (start + zpart))
            spec_ref[slot, j, rows] = jnp.concatenate(blocks, axis=0).astype(jnp.bfloat16)

        put(0, at(0))
        put(GX // 2, at(1))
        for j in range(1, GX // 2):
            here, mirror = at(2 * j), at(2 * j + 1)
            put(j, [jnp.where(lane0, 0.5 * a + sign * b, a) for a, b in zip(here, mirror)])
            put(
                GX - j,
                [
                    jnp.where(lane0, pltpu.roll(0.5 * a - sign * b, PLANES, 0), b)
                    for a, b in zip(here, mirror)
                ],
            )

    @pl.loop(0, slots)
    def _(slot):
        live = (row < crop_ref[slot, 0]) & (col < crop_ref[slot, 1])
        live = jnp.where(live, 1.0, 0.0).astype(jnp.bfloat16)
        for part in parts:
            fetch(slot, part).wait()
        for part in parts:
            transform(slot, part, live)
        leave(slot).start()

    for slot in range(slots):
        leave(slot).wait()


def analyse(band, pairs, extents, tile):
    slots, zrows = band.shape[0] * FACES, band.shape[2]
    tables = (paired_y_table(), forward_x_table())
    smem = pl.BlockSpec(memory_space=pltpu.SMEM)
    anywhere = pl.BlockSpec(memory_space=pl.ANY)
    return pl.pallas_call(
        analyse_kernel,
        in_specs=[smem] * 3 + [anywhere] * (1 + len(tables)),
        out_specs=anywhere,
        out_shape=jax.ShapeDtypeStruct((GX, slots, 2 * zrows, HALF), jnp.bfloat16),
        scratch_shapes=[
            pltpu.SMEM((slots, 2), jnp.int32),
            pltpu.VMEM((slots, zrows, 2 * GX, 2 * GY), jnp.bfloat16),
            *[pltpu.VMEM(t.shape, jnp.bfloat16) for t in tables],
            pltpu.VMEM((slots, GX, 2 * zrows, HALF), jnp.bfloat16),
            pltpu.SemaphoreType.DMA((len(tables),)),
            pltpu.SemaphoreType.DMA((slots, zrows // (4 * PLANES))),
            pltpu.SemaphoreType.DMA((slots,)),
        ],
        compiler_params=pltpu.CompilerParams(vmem_limit_bytes=VMEM_BYTES + VMEM_BYTES * 3 // 4),
        name="analyse",
    )(pairs, extents, tile, band, *(jnp.asarray(t) for t in tables))


def normalised(a_re, a_im, b_re, b_im):
    cross_re = a_re * b_re + a_im * b_im
    cross_im = a_im * b_re - a_re * b_im
    scale = lax.rsqrt(cross_re * cross_re + cross_im * cross_im + 1.0)
    return (cross_re * scale).astype(jnp.bfloat16), (cross_im * scale).astype(jnp.bfloat16)


def correlate_kernel(
    slabs, tiles_here, pairs_ref, place_ref, in_ref, wz_ref, wzi_ref, wz_last_ref, wzi_last_ref, out_ref
):
    tiles = in_ref.shape[0] // slabs
    total = pairs_ref.shape[1]
    pairs_here = out_ref.shape[1]
    slab_rows = out_ref.shape[2]
    both_real = (place_ref[0] == 0) | (place_ref[0] == GX // 2)
    block = (2 * GZ, HALF)
    shared = first_lane(block) & imaginary_rows(block)

    def load(p, end):
        tile = pairs_ref[2 * end, p]
        row = tile // tiles_here
        pos = tile % tiles_here * FACES + pairs_ref[2 * end + 1, p]
        return jnp.concatenate([in_ref[row + s * tiles, pos] for s in range(slabs)], axis=0)

    def phase_of(table_ref, first, second):
        spec = dot(table_ref[...], jnp.concatenate([first, second], axis=1))
        spec = spec.astype(jnp.bfloat16).astype(jnp.float32)
        phase = normalised(spec[:GZ, :HALF], spec[GZ:, :HALF], spec[:GZ, HALF:], spec[GZ:, HALF:])
        return jnp.concatenate(phase, axis=0)

    keep = jnp.where(shared & both_real, 0.0, 1.0).astype(jnp.bfloat16)
    lane = lax.broadcasted_iota(jnp.int32, block, 1)
    ends = [jnp.zeros(block, jnp.bfloat16)] * 2
    for p in range(total):
        for end in (0, 1):
            ends[end] = jnp.where(lane == p, load(p, end)[:, 0:1], ends[end])
    last = dot(wzi_last_ref[...], phase_of(wz_last_ref, *ends)).astype(jnp.bfloat16)
    fix = shared & both_real
    for p in range(0, total, 2):
        phases = [phase_of(wz_ref, load(q, 0) * keep, load(q, 1) * keep) for q in (p, p + 1)]
        w = dot(wzi_ref[...], jnp.concatenate(phases, axis=1)).astype(jnp.bfloat16)
        for k, q in enumerate((p, p + 1)):
            whole = jnp.where(fix, last[:, q : q + 1], w[:, k * HALF : (k + 1) * HALF])
            for s in range(slabs):
                out_ref[q // pairs_here + s * tiles, q % pairs_here] = whole[
                    s * slab_rows : (s + 1) * slab_rows
                ]


def correlate(spread, pairs, place, slabs, tiles_here):
    devices, _, slab_rows, _ = spread.shape
    pairs_here = pairs.shape[1] * slabs // devices
    tables = z_tables()
    vmem = pl.BlockSpec(memory_space=pltpu.VMEM)
    smem = pl.BlockSpec(memory_space=pltpu.SMEM)
    return pl.pallas_call(
        functools.partial(correlate_kernel, slabs, tiles_here),
        in_specs=[smem, smem] + [vmem] * (1 + len(tables)),
        out_specs=vmem,
        out_shape=jax.ShapeDtypeStruct((devices, pairs_here, slab_rows, HALF), jnp.bfloat16),
        compiler_params=pltpu.CompilerParams(vmem_limit_bytes=VMEM_BYTES),
        name="correlate",
    )(pairs, place, spread, *(jnp.asarray(t) for t in tables))


def synthesise_kernel(in_ref, wx_ref, wy_ref, out_ref):
    zpart = out_ref.shape[1]
    units = zpart // PLANES
    block = (2 * zpart, HALF)
    lane0, imaginary = first_lane(block), imaginary_rows(block)
    sign = jnp.where(imaginary, -1.0, 1.0)
    groups = (units, 2 * PLANES, HALF)

    def at(j):
        return in_ref[j, 0].astype(jnp.float32)

    blocks = [None] * GX
    for j in (0, GX // 2):
        blocks[j] = at(j)
    for j in range(1, GX // 2):
        here, mirror = at(j), at(GX - j)
        swapped = pltpu.roll(mirror.reshape(groups), PLANES, 1).reshape(block)
        blocks[j] = jnp.where(lane0, here + swapped, here)
        blocks[GX - j] = jnp.where(lane0, sign * (here - swapped), mirror)
    stacked = jnp.concatenate(
        [
            jnp.concatenate([b[u * 2 * PLANES : (u + 1) * 2 * PLANES] for b in blocks], axis=0)
            for u in range(units)
        ],
        axis=1,
    ).astype(jnp.bfloat16)
    v = dot(wx_ref[...], stacked).astype(jnp.bfloat16)
    rows = PLANES * GX
    cells = [
        jnp.concatenate([v[:rows, k : k + HALF], v[rows:, k : k + HALF]], axis=1)
        for k in range(0, units * HALF, HALF)
    ]
    maps = dot(jnp.concatenate(cells, axis=0), wy_ref[...])
    out_ref[0] = maps.reshape(zpart, GX, GY)


def synthesise(returned):
    _, pairs_here, slab_rows, _ = returned.shape
    zpart = slab_rows // 2
    tables = (inverse_x_table(), half_y_inverse())
    return pl.pallas_call(
        synthesise_kernel,
        grid=(pairs_here, slab_rows // (2 * zpart)),
        in_specs=[pl.BlockSpec((GX, 1, 2 * zpart, HALF), lambda i, z: (0, i, z, 0))]
        + [pl.BlockSpec(t.shape, lambda i, z: (0, 0)) for t in tables],
        out_specs=pl.BlockSpec((1, zpart, GX, GY), lambda i, z: (i, z, 0, 0)),
        out_shape=jax.ShapeDtypeStruct((pairs_here, slab_rows // 2, GX, GY), jnp.float32),
        compiler_params=pltpu.CompilerParams(vmem_limit_bytes=VMEM_BYTES),
        name="synthesise",
    )(returned, *(jnp.asarray(t) for t in tables))


def shards(band, pairs, extents):
    tiles, slabs = lax.axis_size("tile"), lax.axis_size("zslab")
    zrows = band.shape[2]
    if tiles * slabs != GX or zrows % (4 * PLANES) or pairs.shape[0] % (2 * tiles):
        return general_shards(band, pairs, extents)
    pairs, extents = pairs.T, extents.T
    tile = lax.axis_index("tile").astype(jnp.int32)
    device = lax.axis_index("zslab").astype(jnp.int32) * tiles + tile
    spectra = analyse(band, pairs, extents, tile[None])
    spread = lax.all_to_all(spectra, ("zslab", "tile"), split_axis=0, concat_axis=0, tiled=True)
    w = correlate(spread, pairs, device[None], slabs, band.shape[0])
    returned = lax.all_to_all(w, ("zslab", "tile"), split_axis=0, concat_axis=0, tiled=True)
    return synthesise(returned)


def solution(mesh):
    placed = (P("tile", None, "zslab", None, None), P(), P())
    return jax.shard_map(
        shards,
        mesh=mesh,
        in_specs=placed,
        out_specs=P("tile", "zslab", None, None),
        check_vma=False,
    )
```

```python
import functools
import math


import jax
import jax.numpy as jnp
import numpy as np
from jax import lax
from jax.experimental import pallas as pl
from jax.experimental.pallas import tpu as pltpu
from jax.sharding import PartitionSpec as P

GX = 32
GY = 256
GZ = 128
FACES = 4


def dft_tables(length):
    indices = jnp.arange(length, dtype=jnp.int32)
    modular = indices[:, None] * indices[None, :] % length
    angles = modular.astype(jnp.float32) * (2.0 * math.pi / length)
    factor = 1.0 / math.sqrt(length)
    return (
        (jnp.cos(angles) * factor).astype(jnp.bfloat16),
        (jnp.sin(angles) * factor).astype(jnp.bfloat16),
    )


def product(form, left, right):
    return jnp.einsum(form, left, right, preferred_element_type=jnp.float32)


def reduce_resolution(image_volume, crop_bounds):
    row_mask = (
        jnp.arange(image_volume.shape[2], dtype=jnp.int32)[None, :] < crop_bounds[:, 0:1]
    ).astype(jnp.bfloat16)
    col_mask = (
        jnp.arange(image_volume.shape[3], dtype=jnp.int32)[None, :] < crop_bounds[:, 1:2]
    ).astype(jnp.bfloat16)
    masked = image_volume * row_mask[:, None, :, None] * col_mask[:, None, None, :]
    raw_cols = jnp.arange(image_volume.shape[3], dtype=jnp.int32)
    pooled_cols = jnp.arange(GY, dtype=jnp.int32)
    pooling = jnp.where(raw_cols[:, None] // 2 == pooled_cols[None, :], 0.5, 0.0).astype(
        jnp.bfloat16
    )
    along_pooled = product("szxy,yk->szxk", masked, pooling)
    shaped = along_pooled.reshape(image_volume.shape[0], image_volume.shape[1], GX, 2, GY)
    return (shaped[:, :, :, 0, :] + shaped[:, :, :, 1, :]).astype(jnp.bfloat16)


def cross_phase(owner_re, owner_im, pairs, tiles_here):
    first_dev = pairs[:, 0] // tiles_here
    first_pos = pairs[:, 0] % tiles_here * FACES + pairs[:, 1]
    second_tile_device = pairs[:, 2] // tiles_here
    second_pos = pairs[:, 2] % tiles_here * FACES + pairs[:, 3]
    first_re = owner_re[first_dev, :, first_pos].astype(jnp.float32)
    first_im = owner_im[first_dev, :, first_pos].astype(jnp.float32)
    second_re = owner_re[second_tile_device, :, second_pos].astype(jnp.float32)
    second_im = owner_im[second_tile_device, :, second_pos].astype(jnp.float32)
    cross_re = first_re * second_re + first_im * second_im
    cross_im = first_im * second_re - first_re * second_im
    scaled = jnp.sqrt(cross_re * cross_re + cross_im * cross_im + 1.0)
    return ((cross_re / scaled).astype(jnp.bfloat16), (cross_im / scaled).astype(jnp.bfloat16))


def inverse_z(phase_real_part, phase_im, tables_z):
    w_re = (
        product("pmjk,mz->pzjk", phase_real_part, tables_z[0])
        - product("pmjk,mz->pzjk", phase_im, tables_z[1])
    ).astype(jnp.bfloat16)
    w_im = (
        product("pmjk,mz->pzjk", phase_im, tables_z[0])
        + product("pmjk,mz->pzjk", phase_real_part, tables_z[1])
    ).astype(jnp.bfloat16)
    return (w_re, w_im)


def inverse_x(w_re, w_im, tables_x):
    v_re = (
        product("pzjk,jx->pzxk", w_re, tables_x[0]) - product("pzjk,jx->pzxk", w_im, tables_x[1])
    ).astype(jnp.bfloat16)
    v_im = (
        product("pzjk,jx->pzxk", w_im, tables_x[0]) + product("pzjk,jx->pzxk", w_re, tables_x[1])
    ).astype(jnp.bfloat16)
    return (v_re, v_im)


def general_shards(band, pairs, extents):
    tables_x = dft_tables(GX)
    tables_y = dft_tables(GY)
    tables_z = dft_tables(GZ)
    tiles_here = band.shape[0]
    slots = tiles_here * FACES
    zrows = band.shape[2]
    tile_pos = lax.axis_index("tile")
    global_slot = tile_pos * slots + jnp.arange(slots, dtype=jnp.int32)
    first_slot = pairs[:, 0] * FACES + pairs[:, 1]
    second_slot = pairs[:, 2] * FACES + pairs[:, 3]
    matches = (
        (first_slot[None, :] == global_slot[:, None])
        | (second_slot[None, :] == global_slot[:, None])
    ).astype(jnp.int32)
    crop_bounds = jnp.sum(matches[:, :, None] * extents[None, :, :], axis=1)
    image_volume = band.reshape(slots, zrows, 2 * GX, 2 * GY)
    reduced_volume = reduce_resolution(image_volume, crop_bounds)
    y_re = product("szxy,yk->szxk", reduced_volume, tables_y[0]).astype(jnp.bfloat16)
    y_im = (-product("szxy,yk->szxk", reduced_volume, tables_y[1])).astype(jnp.bfloat16)
    x_re = (
        product("szxk,xj->szjk", y_re, tables_x[0]) + product("szxk,xj->szjk", y_im, tables_x[1])
    ).astype(jnp.bfloat16)
    x_im = (
        product("szxk,xj->szjk", y_im, tables_x[0]) - product("szxk,xj->szjk", y_re, tables_x[1])
    ).astype(jnp.bfloat16)
    kx_part = GX // lax.axis_size("zslab")
    re_in = lax.all_to_all(x_re, "zslab", split_axis=2, concat_axis=1, tiled=True)
    im_in = lax.all_to_all(x_im, "zslab", split_axis=2, concat_axis=1, tiled=True)
    out_re = (
        product("szjk,zm->msjk", re_in, tables_z[0]) + product("szjk,zm->msjk", im_in, tables_z[1])
    ).astype(jnp.bfloat16)
    out_im = (
        product("szjk,zm->msjk", im_in, tables_z[0]) - product("szjk,zm->msjk", re_in, tables_z[1])
    ).astype(jnp.bfloat16)
    tile_count = lax.axis_size("tile")
    kz_part = GZ // tile_count
    spectra = (
        lax.all_to_all(out_re, "tile", split_axis=0, concat_axis=0, tiled=True),
        lax.all_to_all(out_im, "tile", split_axis=0, concat_axis=0, tiled=True),
    )
    owner_re = spectra[0].reshape(tile_count, kz_part, slots, kx_part, GY)
    owner_im = spectra[1].reshape(tile_count, kz_part, slots, kx_part, GY)
    phase_real_part, phase_im = cross_phase(owner_re, owner_im, pairs, tiles_here)
    returned = (
        lax.all_to_all(phase_real_part, "tile", split_axis=0, concat_axis=1, tiled=True),
        lax.all_to_all(phase_im, "tile", split_axis=0, concat_axis=1, tiled=True),
    )
    w_re, w_im = inverse_z(returned[0], returned[1], tables_z)
    v_re, v_im = inverse_x(
        lax.all_to_all(w_re, "zslab", split_axis=1, concat_axis=2, tiled=True),
        lax.all_to_all(w_im, "zslab", split_axis=1, concat_axis=2, tiled=True),
        tables_x,
    )
    return product("pzxk,ky->pzxy", v_re, tables_y[0]) - product("pzxk,ky->pzxy", v_im, tables_y[1])


HALF = GY // 2
PLANES = 4
VMEM_BYTES = 32 * 1024 * 1024


def host_tables(length):
    indices = np.arange(length, dtype=np.int32)
    modular = indices[:, None] * indices[None, :] % length
    angles = modular.astype(np.float32) * np.float32(2.0 * math.pi / length)
    factor = np.float32(1.0 / math.sqrt(length))
    return (
        (np.cos(angles) * factor).astype(jnp.bfloat16),
        (np.sin(angles) * factor).astype(jnp.bfloat16),
    )


def half_y_table():
    cosine, sine = host_tables(GY)
    imag = -sine[:, :HALF]
    imag[:, 0] = cosine[:, HALF]
    return np.concatenate([cosine[:, :HALF], imag], axis=1)


def paired_y_table():
    table = np.zeros((2 * GY, GY), jnp.bfloat16)
    table[::2] = half_y_table() * np.array(0.5, jnp.bfloat16)
    return table


def half_y_inverse():
    cosine, sine = host_tables(GY)
    two = np.array(2.0, jnp.bfloat16)
    real = cosine[:HALF, :] * two
    real[0] = cosine[0]
    imag = -sine[:HALF, :] * two
    imag[0] = cosine[HALF]
    return np.concatenate([real, imag], axis=0)


def mirror_order():
    order = [0, GX // 2]
    for j in range(1, GX // 2):
        order += [j, GX - j]
    return order


def complex_blocks(length, sign):
    cosine, sine = (table.astype(np.float32) for table in host_tables(length))
    return np.array([[cosine, -sign * sine], [sign * sine, cosine]])


def forward_x_table():
    table = np.einsum("oijx,az->joaizx", complex_blocks(GX, -1), np.eye(PLANES))[mirror_order()]
    return table.reshape(2 * GX * PLANES, -1).astype(jnp.bfloat16)


def inverse_x_table():
    table = np.einsum("oijx,az->oaxjiz", complex_blocks(GX, 1), np.eye(PLANES))
    return table.reshape(2 * PLANES * GX, -1).astype(jnp.bfloat16)


def z_rows():
    return np.arange(2 * GZ).reshape(2, GZ // PLANES, PLANES).transpose(1, 0, 2).reshape(-1)


def z_tables():
    forward, inverse = (
        complex_blocks(GZ, sign).transpose(0, 2, 1, 3).reshape(2 * GZ, 2 * GZ) for sign in (-1, 1)
    )
    none = np.zeros((2 * GZ, GZ), np.float32)
    forward_last = np.concatenate([none, forward[:, :GZ]], axis=1)
    inverse_last = np.concatenate([none.T, inverse[:GZ]], axis=0)
    order = z_rows()
    return [
        np.ascontiguousarray(table).astype(jnp.bfloat16)
        for table in (
            forward[:, order],
            inverse[order],
            forward_last[:, order],
            inverse_last[order],
        )
    ]


def imaginary_rows(shape):
    return lax.broadcasted_iota(jnp.int32, shape, 0) % (2 * PLANES) >= PLANES


def first_lane(shape):
    return lax.broadcasted_iota(jnp.int32, shape, 1) == 0


def dot(left, right):
    return jnp.dot(left, right, preferred_element_type=jnp.float32)


def analyse_kernel(
    slots, pairs_ref, extents_ref, tile_ref, *rest
):
    band_refs, (wy_ref, wx_ref, out_ref, crop_ref) = rest[:-4], rest[-4:]
    slot = pl.program_id(0)

    @pl.when(slot == 0)
    def _():
        for p in range(pairs_ref.shape[1]):
            for end in (0, 1):
                named = pairs_ref[2 * end, p] * FACES + pairs_ref[2 * end + 1, p] - tile_ref[0] * slots

                @pl.when((named >= 0) & (named < slots))
                def _():
                    crop_ref[named, 0] = extents_ref[0, p]
                    crop_ref[named, 1] = extents_ref[1, p]

    cells_shape = (GX, 128)
    x = lax.broadcasted_iota(jnp.int32, cells_shape, 0)
    lane = lax.broadcasted_iota(jnp.int32, cells_shape, 1)
    live = [
        [
            jnp.where((2 * x + a < crop_ref[slot, 0]) & (k * 128 + lane < crop_ref[slot, 1]), 1.0, 0.0)
            for a in (0, 1)
        ]
        for k in range(len(band_refs))
    ]
    block = (2 * PLANES, HALF)
    lane0, imaginary = first_lane(block), imaginary_rows(block)
    sign = jnp.where(imaginary, -0.5, 0.5)

    def cells(z):
        parts = []
        for ref, masks in zip(band_refs, live):
            even, odd = (
                ref[0, 0, z, pl.ds(a, GX, stride=2), :].astype(jnp.float32) * masks[a] for a in (0, 1)
            )
            rows = even + odd
            parts.append((rows + pltpu.roll(rows, 127, 1)).astype(jnp.bfloat16))
        return jnp.concatenate(parts, axis=1)

    zpart = 4 * PLANES
    for start in range(0, band_refs[0].shape[2], zpart):
        down = jnp.concatenate([cells(z) for z in range(start, start + zpart)], axis=0)
        y = dot(down, wy_ref[...]).astype(jnp.bfloat16).reshape(zpart // PLANES, PLANES * GX, GY)
        units = [
            jnp.concatenate([y[unit, :, :HALF], y[unit, :, HALF:]], axis=0)
            for unit in range(zpart // PLANES)
        ]
        spectra = dot(wx_ref[...], jnp.concatenate(units, axis=1))

        def at(n):
            rows = spectra[2 * PLANES * n : 2 * PLANES * (n + 1)]
            return [rows[:, k : k + HALF] for k in range(0, rows.shape[1], HALF)]

        def put(j, blocks):
            rows = slice(2 * start, 2 * (start + zpart))
            out_ref[j, 0, rows] = jnp.concatenate(blocks, axis=0).astype(jnp.bfloat16)

        put(0, at(0))
        put(GX // 2, at(1))
        for j in range(1, GX // 2):
            here, mirror = at(2 * j), at(2 * j + 1)
            put(j, [jnp.where(lane0, 0.5 * a + sign * b, a) for a, b in zip(here, mirror)])
            put(
                GX - j,
                [
                    jnp.where(lane0, pltpu.roll(0.5 * a - sign * b, PLANES, 0), b)
                    for a, b in zip(here, mirror)
                ],
            )


def analyse(band, pairs, extents, tile):
    slots, zrows = band.shape[0] * FACES, band.shape[2]
    tables = (paired_y_table(), forward_x_table())
    whole = [pl.BlockSpec(t.shape, lambda i, *_: (0, 0)) for t in tables]
    lane_blocks = 2 * GY // 128
    return pl.pallas_call(
        functools.partial(analyse_kernel, slots),
        grid_spec=pltpu.PrefetchScalarGridSpec(
            num_scalar_prefetch=3,
            grid=(slots,),
            in_specs=[
                pl.BlockSpec(
                    (1, 1, zrows, 2 * GX, 128),
                    lambda i, *_, k=k: (i // FACES, i % FACES, 0, 0, k),
                )
                for k in range(lane_blocks)
            ]
            + whole,
            out_specs=pl.BlockSpec((GX, 1, 2 * zrows, HALF), lambda i, *_: (0, i, 0, 0)),
            scratch_shapes=[pltpu.SMEM((slots, 2), jnp.int32)],
        ),
        out_shape=jax.ShapeDtypeStruct((GX, slots, 2 * zrows, HALF), jnp.bfloat16),
        compiler_params=pltpu.CompilerParams(vmem_limit_bytes=VMEM_BYTES + VMEM_BYTES * 3 // 4),
        name="analyse",
    )(pairs, extents, tile, *[band] * lane_blocks, *(jnp.asarray(t) for t in tables))


def normalised(a_re, a_im, b_re, b_im):
    cross_re = a_re * b_re + a_im * b_im
    cross_im = a_im * b_re - a_re * b_im
    scale = lax.rsqrt(cross_re * cross_re + cross_im * cross_im + 1.0)
    return (cross_re * scale).astype(jnp.bfloat16), (cross_im * scale).astype(jnp.bfloat16)


def correlate_kernel(
    slabs, tiles_here, pairs_ref, place_ref, in_ref, wz_ref, wzi_ref, wz_last_ref, wzi_last_ref, out_ref
):
    tiles = in_ref.shape[0] // slabs
    total = pairs_ref.shape[1]
    pairs_here = out_ref.shape[1]
    slab_rows = out_ref.shape[2]
    both_real = (place_ref[0] == 0) | (place_ref[0] == GX // 2)
    block = (2 * GZ, HALF)
    shared = first_lane(block) & imaginary_rows(block)

    def load(p, end):
        tile = pairs_ref[2 * end, p]
        row = tile // tiles_here
        pos = tile % tiles_here * FACES + pairs_ref[2 * end + 1, p]
        return jnp.concatenate([in_ref[row + s * tiles, pos] for s in range(slabs)], axis=0)

    def phase_of(table_ref, first, second):
        spec = dot(table_ref[...], jnp.concatenate([first, second], axis=1))
        spec = spec.astype(jnp.bfloat16).astype(jnp.float32)
        phase = normalised(spec[:GZ, :HALF], spec[GZ:, :HALF], spec[:GZ, HALF:], spec[GZ:, HALF:])
        return jnp.concatenate(phase, axis=0)

    keep = jnp.where(shared & both_real, 0.0, 1.0).astype(jnp.bfloat16)
    lane = lax.broadcasted_iota(jnp.int32, block, 1)
    ends = [jnp.zeros(block, jnp.bfloat16)] * 2
    for p in range(total):
        for end in (0, 1):
            ends[end] = jnp.where(lane == p, load(p, end)[:, 0:1], ends[end])
    last = dot(wzi_last_ref[...], phase_of(wz_last_ref, *ends)).astype(jnp.bfloat16)
    fix = shared & both_real
    for p in range(0, total, 2):
        phases = [phase_of(wz_ref, load(q, 0) * keep, load(q, 1) * keep) for q in (p, p + 1)]
        w = dot(wzi_ref[...], jnp.concatenate(phases, axis=1)).astype(jnp.bfloat16)
        for k, q in enumerate((p, p + 1)):
            whole = jnp.where(fix, last[:, q : q + 1], w[:, k * HALF : (k + 1) * HALF])
            for s in range(slabs):
                out_ref[q // pairs_here + s * tiles, q % pairs_here] = whole[
                    s * slab_rows : (s + 1) * slab_rows
                ]


def correlate(spread, pairs, place, slabs, tiles_here):
    devices, _, slab_rows, _ = spread.shape
    pairs_here = pairs.shape[1] * slabs // devices
    tables = z_tables()
    vmem = pl.BlockSpec(memory_space=pltpu.VMEM)
    smem = pl.BlockSpec(memory_space=pltpu.SMEM)
    return pl.pallas_call(
        functools.partial(correlate_kernel, slabs, tiles_here),
        in_specs=[smem, smem] + [vmem] * (1 + len(tables)),
        out_specs=vmem,
        out_shape=jax.ShapeDtypeStruct((devices, pairs_here, slab_rows, HALF), jnp.bfloat16),
        compiler_params=pltpu.CompilerParams(vmem_limit_bytes=VMEM_BYTES),
        name="correlate",
    )(pairs, place, spread, *(jnp.asarray(t) for t in tables))


def synthesise_kernel(in_ref, wx_ref, wy_ref, out_ref):
    zpart = out_ref.shape[1]
    units = zpart // PLANES
    block = (2 * zpart, HALF)
    lane0, imaginary = first_lane(block), imaginary_rows(block)
    sign = jnp.where(imaginary, -1.0, 1.0)
    groups = (units, 2 * PLANES, HALF)

    def at(j):
        return in_ref[j, 0].astype(jnp.float32)

    blocks = [None] * GX
    for j in (0, GX // 2):
        blocks[j] = at(j)
    for j in range(1, GX // 2):
        here, mirror = at(j), at(GX - j)
        swapped = pltpu.roll(mirror.reshape(groups), PLANES, 1).reshape(block)
        blocks[j] = jnp.where(lane0, here + swapped, here)
        blocks[GX - j] = jnp.where(lane0, sign * (here - swapped), mirror)
    stacked = jnp.concatenate(
        [
            jnp.concatenate([b[u * 2 * PLANES : (u + 1) * 2 * PLANES] for b in blocks], axis=0)
            for u in range(units)
        ],
        axis=1,
    ).astype(jnp.bfloat16)
    v = dot(wx_ref[...], stacked).astype(jnp.bfloat16)
    rows = PLANES * GX
    cells = [
        jnp.concatenate([v[:rows, k : k + HALF], v[rows:, k : k + HALF]], axis=1)
        for k in range(0, units * HALF, HALF)
    ]
    maps = dot(jnp.concatenate(cells, axis=0), wy_ref[...])
    out_ref[0] = maps.reshape(zpart, GX, GY)


def synthesise(returned):
    _, pairs_here, slab_rows, _ = returned.shape
    zpart = slab_rows // 2
    tables = (inverse_x_table(), half_y_inverse())
    return pl.pallas_call(
        synthesise_kernel,
        grid=(pairs_here, slab_rows // (2 * zpart)),
        in_specs=[pl.BlockSpec((GX, 1, 2 * zpart, HALF), lambda i, z: (0, i, z, 0))]
        + [pl.BlockSpec(t.shape, lambda i, z: (0, 0)) for t in tables],
        out_specs=pl.BlockSpec((1, zpart, GX, GY), lambda i, z: (i, z, 0, 0)),
        out_shape=jax.ShapeDtypeStruct((pairs_here, slab_rows // 2, GX, GY), jnp.float32),
        compiler_params=pltpu.CompilerParams(vmem_limit_bytes=VMEM_BYTES),
        name="synthesise",
    )(returned, *(jnp.asarray(t) for t in tables))


def shards(band, pairs, extents):
    tiles, slabs = lax.axis_size("tile"), lax.axis_size("zslab")
    zrows = band.shape[2]
    if tiles * slabs != GX or zrows % (4 * PLANES) or pairs.shape[0] % (2 * tiles):
        return general_shards(band, pairs, extents)
    pairs, extents = pairs.T, extents.T
    tile = lax.axis_index("tile").astype(jnp.int32)
    device = lax.axis_index("zslab").astype(jnp.int32) * tiles + tile
    spectra = analyse(band, pairs, extents, tile[None])
    spread = lax.all_to_all(spectra, ("zslab", "tile"), split_axis=0, concat_axis=0, tiled=True)
    w = correlate(spread, pairs, device[None], slabs, band.shape[0])
    returned = lax.all_to_all(w, ("zslab", "tile"), split_axis=0, concat_axis=0, tiled=True)
    return synthesise(returned)


def solution(mesh):
    placed = (P("tile", None, "zslab", None, None), P(), P())
    return jax.shard_map(
        shards,
        mesh=mesh,
        in_specs=placed,
        out_specs=P("tile", "zslab", None, None),
        check_vma=False,
    )
```

```python
import functools
import math


import jax
import jax.numpy as jnp
import numpy as np
from jax import lax
from jax.experimental import pallas as pl
from jax.experimental.pallas import tpu as pltpu
from jax.sharding import PartitionSpec as P

GX = 32
GY = 256
GZ = 128
FACES = 4


def dft_tables(length):
    indices = jnp.arange(length, dtype=jnp.int32)
    modular = indices[:, None] * indices[None, :] % length
    angles = modular.astype(jnp.float32) * (2.0 * math.pi / length)
    factor = 1.0 / math.sqrt(length)
    return (
        (jnp.cos(angles) * factor).astype(jnp.bfloat16),
        (jnp.sin(angles) * factor).astype(jnp.bfloat16),
    )


def product(form, left, right):
    return jnp.einsum(form, left, right, preferred_element_type=jnp.float32)


def reduce_resolution(image_volume, crop_bounds):
    row_mask = (
        jnp.arange(image_volume.shape[2], dtype=jnp.int32)[None, :] < crop_bounds[:, 0:1]
    ).astype(jnp.bfloat16)
    col_mask = (
        jnp.arange(image_volume.shape[3], dtype=jnp.int32)[None, :] < crop_bounds[:, 1:2]
    ).astype(jnp.bfloat16)
    masked = image_volume * row_mask[:, None, :, None] * col_mask[:, None, None, :]
    raw_cols = jnp.arange(image_volume.shape[3], dtype=jnp.int32)
    pooled_cols = jnp.arange(GY, dtype=jnp.int32)
    pooling = jnp.where(raw_cols[:, None] // 2 == pooled_cols[None, :], 0.5, 0.0).astype(
        jnp.bfloat16
    )
    along_pooled = product("szxy,yk->szxk", masked, pooling)
    shaped = along_pooled.reshape(image_volume.shape[0], image_volume.shape[1], GX, 2, GY)
    return (shaped[:, :, :, 0, :] + shaped[:, :, :, 1, :]).astype(jnp.bfloat16)


def cross_phase(owner_re, owner_im, pairs, tiles_here):
    first_dev = pairs[:, 0] // tiles_here
    first_pos = pairs[:, 0] % tiles_here * FACES + pairs[:, 1]
    second_tile_device = pairs[:, 2] // tiles_here
    second_pos = pairs[:, 2] % tiles_here * FACES + pairs[:, 3]
    first_re = owner_re[first_dev, :, first_pos].astype(jnp.float32)
    first_im = owner_im[first_dev, :, first_pos].astype(jnp.float32)
    second_re = owner_re[second_tile_device, :, second_pos].astype(jnp.float32)
    second_im = owner_im[second_tile_device, :, second_pos].astype(jnp.float32)
    cross_re = first_re * second_re + first_im * second_im
    cross_im = first_im * second_re - first_re * second_im
    scaled = jnp.sqrt(cross_re * cross_re + cross_im * cross_im + 1.0)
    return ((cross_re / scaled).astype(jnp.bfloat16), (cross_im / scaled).astype(jnp.bfloat16))


def inverse_z(phase_real_part, phase_im, tables_z):
    w_re = (
        product("pmjk,mz->pzjk", phase_real_part, tables_z[0])
        - product("pmjk,mz->pzjk", phase_im, tables_z[1])
    ).astype(jnp.bfloat16)
    w_im = (
        product("pmjk,mz->pzjk", phase_im, tables_z[0])
        + product("pmjk,mz->pzjk", phase_real_part, tables_z[1])
    ).astype(jnp.bfloat16)
    return (w_re, w_im)


def inverse_x(w_re, w_im, tables_x):
    v_re = (
        product("pzjk,jx->pzxk", w_re, tables_x[0]) - product("pzjk,jx->pzxk", w_im, tables_x[1])
    ).astype(jnp.bfloat16)
    v_im = (
        product("pzjk,jx->pzxk", w_im, tables_x[0]) + product("pzjk,jx->pzxk", w_re, tables_x[1])
    ).astype(jnp.bfloat16)
    return (v_re, v_im)


def general_shards(band, pairs, extents):
    tables_x = dft_tables(GX)
    tables_y = dft_tables(GY)
    tables_z = dft_tables(GZ)
    tiles_here = band.shape[0]
    slots = tiles_here * FACES
    zrows = band.shape[2]
    tile_pos = lax.axis_index("tile")
    global_slot = tile_pos * slots + jnp.arange(slots, dtype=jnp.int32)
    first_slot = pairs[:, 0] * FACES + pairs[:, 1]
    second_slot = pairs[:, 2] * FACES + pairs[:, 3]
    matches = (
        (first_slot[None, :] == global_slot[:, None])
        | (second_slot[None, :] == global_slot[:, None])
    ).astype(jnp.int32)
    crop_bounds = jnp.sum(matches[:, :, None] * extents[None, :, :], axis=1)
    image_volume = band.reshape(slots, zrows, 2 * GX, 2 * GY)
    reduced_volume = reduce_resolution(image_volume, crop_bounds)
    y_re = product("szxy,yk->szxk", reduced_volume, tables_y[0]).astype(jnp.bfloat16)
    y_im = (-product("szxy,yk->szxk", reduced_volume, tables_y[1])).astype(jnp.bfloat16)
    x_re = (
        product("szxk,xj->szjk", y_re, tables_x[0]) + product("szxk,xj->szjk", y_im, tables_x[1])
    ).astype(jnp.bfloat16)
    x_im = (
        product("szxk,xj->szjk", y_im, tables_x[0]) - product("szxk,xj->szjk", y_re, tables_x[1])
    ).astype(jnp.bfloat16)
    kx_part = GX // lax.axis_size("zslab")
    re_in = lax.all_to_all(x_re, "zslab", split_axis=2, concat_axis=1, tiled=True)
    im_in = lax.all_to_all(x_im, "zslab", split_axis=2, concat_axis=1, tiled=True)
    out_re = (
        product("szjk,zm->msjk", re_in, tables_z[0]) + product("szjk,zm->msjk", im_in, tables_z[1])
    ).astype(jnp.bfloat16)
    out_im = (
        product("szjk,zm->msjk", im_in, tables_z[0]) - product("szjk,zm->msjk", re_in, tables_z[1])
    ).astype(jnp.bfloat16)
    tile_count = lax.axis_size("tile")
    kz_part = GZ // tile_count
    spectra = (
        lax.all_to_all(out_re, "tile", split_axis=0, concat_axis=0, tiled=True),
        lax.all_to_all(out_im, "tile", split_axis=0, concat_axis=0, tiled=True),
    )
    owner_re = spectra[0].reshape(tile_count, kz_part, slots, kx_part, GY)
    owner_im = spectra[1].reshape(tile_count, kz_part, slots, kx_part, GY)
    phase_real_part, phase_im = cross_phase(owner_re, owner_im, pairs, tiles_here)
    returned = (
        lax.all_to_all(phase_real_part, "tile", split_axis=0, concat_axis=1, tiled=True),
        lax.all_to_all(phase_im, "tile", split_axis=0, concat_axis=1, tiled=True),
    )
    w_re, w_im = inverse_z(returned[0], returned[1], tables_z)
    v_re, v_im = inverse_x(
        lax.all_to_all(w_re, "zslab", split_axis=1, concat_axis=2, tiled=True),
        lax.all_to_all(w_im, "zslab", split_axis=1, concat_axis=2, tiled=True),
        tables_x,
    )
    return product("pzxk,ky->pzxy", v_re, tables_y[0]) - product("pzxk,ky->pzxy", v_im, tables_y[1])


HALF = GY // 2
PLANES = 4
VMEM_BYTES = 32 * 1024 * 1024


def host_tables(length):
    indices = np.arange(length, dtype=np.int32)
    modular = indices[:, None] * indices[None, :] % length
    angles = modular.astype(np.float32) * np.float32(2.0 * math.pi / length)
    factor = np.float32(1.0 / math.sqrt(length))
    return (
        (np.cos(angles) * factor).astype(jnp.bfloat16),
        (np.sin(angles) * factor).astype(jnp.bfloat16),
    )


def half_y_table():
    cosine, sine = host_tables(GY)
    imag = -sine[:, :HALF]
    imag[:, 0] = cosine[:, HALF]
    return np.concatenate([cosine[:, :HALF], imag], axis=1)


def paired_y_table():
    table = np.zeros((2 * GY, GY), jnp.bfloat16)
    table[::2] = half_y_table() * np.array(0.5, jnp.bfloat16)
    return table


def half_y_inverse():
    cosine, sine = host_tables(GY)
    two = np.array(2.0, jnp.bfloat16)
    real = cosine[:HALF, :] * two
    real[0] = cosine[0]
    imag = -sine[:HALF, :] * two
    imag[0] = cosine[HALF]
    return np.concatenate([real, imag], axis=0)


def mirror_order():
    order = [0, GX // 2]
    for j in range(1, GX // 2):
        order += [j, GX - j]
    return order


def complex_blocks(length, sign):
    cosine, sine = (table.astype(np.float32) for table in host_tables(length))
    return np.array([[cosine, -sign * sine], [sign * sine, cosine]])


def forward_x_table():
    table = np.einsum("oijx,az->joaizx", complex_blocks(GX, -1), np.eye(PLANES))[mirror_order()]
    return table.reshape(2 * GX * PLANES, -1).astype(jnp.bfloat16)


def inverse_x_table():
    table = np.einsum("oijx,az->oaxjiz", complex_blocks(GX, 1), np.eye(PLANES))
    return table.reshape(2 * PLANES * GX, -1).astype(jnp.bfloat16)


def z_rows():
    return np.arange(2 * GZ).reshape(2, GZ // PLANES, PLANES).transpose(1, 0, 2).reshape(-1)


def z_tables():
    forward, inverse = (
        complex_blocks(GZ, sign).transpose(0, 2, 1, 3).reshape(2 * GZ, 2 * GZ) for sign in (-1, 1)
    )
    none = np.zeros((2 * GZ, GZ), np.float32)
    forward_last = np.concatenate([none, forward[:, :GZ]], axis=1)
    inverse_last = np.concatenate([none.T, inverse[:GZ]], axis=0)
    order = z_rows()
    return [
        np.ascontiguousarray(table).astype(jnp.bfloat16)
        for table in (
            forward[:, order],
            inverse[order],
            forward_last[:, order],
            inverse_last[order],
        )
    ]


def imaginary_rows(shape):
    return lax.broadcasted_iota(jnp.int32, shape, 0) % (2 * PLANES) >= PLANES


def first_lane(shape):
    return lax.broadcasted_iota(jnp.int32, shape, 1) == 0


def dot(left, right):
    return jnp.dot(left, right, preferred_element_type=jnp.float32)


def analyse_kernel(
    slots, pairs_ref, extents_ref, tile_ref, *rest
):
    band_refs, (wy_ref, wx_ref, out_ref, crop_ref) = rest[:-4], rest[-4:]
    slot = pl.program_id(0)

    @pl.when(slot == 0)
    def _():
        for p in range(pairs_ref.shape[1]):
            for end in (0, 1):
                named = pairs_ref[2 * end, p] * FACES + pairs_ref[2 * end + 1, p] - tile_ref[0] * slots

                @pl.when((named >= 0) & (named < slots))
                def _():
                    crop_ref[named, 0] = extents_ref[0, p]
                    crop_ref[named, 1] = extents_ref[1, p]

    cells_shape = (GX, 128)
    x = lax.broadcasted_iota(jnp.int32, cells_shape, 0)
    lane = lax.broadcasted_iota(jnp.int32, cells_shape, 1)
    live = [
        [
            jnp.where((2 * x + a < crop_ref[slot, 0]) & (k * 128 + lane < crop_ref[slot, 1]), 1.0, 0.0)
            for a in (0, 1)
        ]
        for k in range(len(band_refs))
    ]
    block = (2 * PLANES, HALF)
    lane0, imaginary = first_lane(block), imaginary_rows(block)
    sign = jnp.where(imaginary, -0.5, 0.5)

    def cells(z):
        parts = []
        for ref, masks in zip(band_refs, live):
            even, odd = (
                ref[0, 0, z, pl.ds(a, GX, stride=2), :].astype(jnp.float32) * masks[a] for a in (0, 1)
            )
            rows = even + odd
            parts.append((rows + pltpu.roll(rows, 127, 1)).astype(jnp.bfloat16))
        return jnp.concatenate(parts, axis=1)

    zpart = 4 * PLANES
    starts = range(0, band_refs[0].shape[2], zpart)

    def pool(start, count):
        return [cells(z) for z in range(start, start + count)]

    def along_y(planes):
        y = dot(jnp.concatenate(planes, axis=0), wy_ref[...]).astype(jnp.bfloat16)
        y = y.reshape(zpart // PLANES, PLANES * GX, GY)
        units = [
            jnp.concatenate([y[unit, :, :HALF], y[unit, :, HALF:]], axis=0)
            for unit in range(zpart // PLANES)
        ]
        return jnp.concatenate(units, axis=1)

    def store(start, spectra):
        def at(n):
            rows = spectra[2 * PLANES * n : 2 * PLANES * (n + 1)]
            return [rows[:, k : k + HALF] for k in range(0, rows.shape[1], HALF)]

        def put(j, blocks):
            rows = slice(2 * start, 2 * (start + zpart))
            out_ref[j, 0, rows] = jnp.concatenate(blocks, axis=0).astype(jnp.bfloat16)

        put(0, at(0))
        put(GX // 2, at(1))
        for j in range(1, GX // 2):
            here, mirror = at(2 * j), at(2 * j + 1)
            put(j, [jnp.where(lane0, 0.5 * a + sign * b, a) for a, b in zip(here, mirror)])
            put(
                GX - j,
                [
                    jnp.where(lane0, pltpu.roll(0.5 * a - sign * b, PLANES, 0), b)
                    for a, b in zip(here, mirror)
                ],
            )

    planes = pool(0, zpart)
    for start in starts:
        y, after = along_y(planes), start + zpart
        planes = pool(after, zpart // 2) if after in starts else []
        spectra = dot(wx_ref[...], y)
        planes += pool(after + zpart // 2, zpart // 2) if after in starts else []
        store(start, spectra)


def analyse(band, pairs, extents, tile):
    slots, zrows = band.shape[0] * FACES, band.shape[2]
    tables = (paired_y_table(), forward_x_table())
    whole = [pl.BlockSpec(t.shape, lambda i, *_: (0, 0)) for t in tables]
    lane_blocks = 2 * GY // 128
    return pl.pallas_call(
        functools.partial(analyse_kernel, slots),
        grid_spec=pltpu.PrefetchScalarGridSpec(
            num_scalar_prefetch=3,
            grid=(slots,),
            in_specs=[
                pl.BlockSpec(
                    (1, 1, zrows, 2 * GX, 128),
                    lambda i, *_, k=k: (i // FACES, i % FACES, 0, 0, k),
                )
                for k in range(lane_blocks)
            ]
            + whole,
            out_specs=pl.BlockSpec((GX, 1, 2 * zrows, HALF), lambda i, *_: (0, i, 0, 0)),
            scratch_shapes=[pltpu.SMEM((slots, 2), jnp.int32)],
        ),
        out_shape=jax.ShapeDtypeStruct((GX, slots, 2 * zrows, HALF), jnp.bfloat16),
        compiler_params=pltpu.CompilerParams(vmem_limit_bytes=VMEM_BYTES + VMEM_BYTES * 3 // 4),
        name="analyse",
    )(pairs, extents, tile, *[band] * lane_blocks, *(jnp.asarray(t) for t in tables))


def normalised(a_re, a_im, b_re, b_im):
    cross_re = a_re * b_re + a_im * b_im
    cross_im = a_im * b_re - a_re * b_im
    scale = lax.rsqrt(cross_re * cross_re + cross_im * cross_im + 1.0)
    return (cross_re * scale).astype(jnp.bfloat16), (cross_im * scale).astype(jnp.bfloat16)


def correlate_kernel(
    slabs, tiles_here, pairs_ref, place_ref, in_ref, wz_ref, wzi_ref, wz_last_ref, wzi_last_ref, out_ref
):
    tiles = in_ref.shape[0] // slabs
    total = pairs_ref.shape[1]
    pairs_here = out_ref.shape[1]
    slab_rows = out_ref.shape[2]
    both_real = (place_ref[0] == 0) | (place_ref[0] == GX // 2)
    block = (2 * GZ, HALF)
    shared = first_lane(block) & imaginary_rows(block)

    def load(p, end):
        tile = pairs_ref[2 * end, p]
        row = tile // tiles_here
        pos = tile % tiles_here * FACES + pairs_ref[2 * end + 1, p]
        return jnp.concatenate([in_ref[row + s * tiles, pos] for s in range(slabs)], axis=0)

    def phase_of(table_ref, first, second):
        spec = dot(table_ref[...], jnp.concatenate([first, second], axis=1))
        spec = spec.astype(jnp.bfloat16).astype(jnp.float32)
        phase = normalised(spec[:GZ, :HALF], spec[GZ:, :HALF], spec[:GZ, HALF:], spec[GZ:, HALF:])
        return jnp.concatenate(phase, axis=0)

    keep = jnp.where(shared & both_real, 0.0, 1.0).astype(jnp.bfloat16)
    for p in range(0, total, 2):
        phases = [phase_of(wz_ref, load(q, 0) * keep, load(q, 1) * keep) for q in (p, p + 1)]
        w = dot(wzi_ref[...], jnp.concatenate(phases, axis=1)).astype(jnp.bfloat16)
        for k, q in enumerate((p, p + 1)):
            for s in range(slabs):
                out_ref[q // pairs_here + s * tiles, q % pairs_here] = w[
                    s * slab_rows : (s + 1) * slab_rows, k * HALF : (k + 1) * HALF
                ]

    @pl.when(both_real)
    def _():
        lane = lax.broadcasted_iota(jnp.int32, block, 1)
        ends = [jnp.zeros(block, jnp.bfloat16)] * 2
        for p in range(total):
            for end in (0, 1):
                ends[end] = jnp.where(lane == p, load(p, end)[:, 0:1], ends[end])
        w = dot(wzi_last_ref[...], phase_of(wz_last_ref, *ends)).astype(jnp.bfloat16)
        for p in range(total):
            column = w[:, p : p + 1]
            for s in range(slabs):
                rows = slice(s * slab_rows, (s + 1) * slab_rows)
                at = (p // pairs_here + s * tiles, p % pairs_here)
                out_ref[at] = jnp.where(shared[rows], column[rows], out_ref[at])


def correlate(spread, pairs, place, slabs, tiles_here):
    devices, _, slab_rows, _ = spread.shape
    pairs_here = pairs.shape[1] * slabs // devices
    tables = z_tables()
    vmem = pl.BlockSpec(memory_space=pltpu.VMEM)
    smem = pl.BlockSpec(memory_space=pltpu.SMEM)
    return pl.pallas_call(
        functools.partial(correlate_kernel, slabs, tiles_here),
        in_specs=[smem, smem] + [vmem] * (1 + len(tables)),
        out_specs=vmem,
        out_shape=jax.ShapeDtypeStruct((devices, pairs_here, slab_rows, HALF), jnp.bfloat16),
        compiler_params=pltpu.CompilerParams(vmem_limit_bytes=VMEM_BYTES),
        name="correlate",
    )(pairs, place, spread, *(jnp.asarray(t) for t in tables))


def synthesise_kernel(in_ref, wx_ref, wy_ref, out_ref):
    zpart = out_ref.shape[1]
    units = zpart // PLANES
    block = (2 * zpart, HALF)
    lane0, imaginary = first_lane(block), imaginary_rows(block)
    sign = jnp.where(imaginary, -1.0, 1.0)
    groups = (units, 2 * PLANES, HALF)

    def at(j):
        return in_ref[j, 0].astype(jnp.float32)

    blocks = [None] * GX
    for j in (0, GX // 2):
        blocks[j] = at(j)
    for j in range(1, GX // 2):
        here, mirror = at(j), at(GX - j)
        swapped = pltpu.roll(mirror.reshape(groups), PLANES, 1).reshape(block)
        blocks[j] = jnp.where(lane0, here + swapped, here)
        blocks[GX - j] = jnp.where(lane0, sign * (here - swapped), mirror)
    stacked = jnp.concatenate(
        [
            jnp.concatenate([b[u * 2 * PLANES : (u + 1) * 2 * PLANES] for b in blocks], axis=0)
            for u in range(units)
        ],
        axis=1,
    ).astype(jnp.bfloat16)
    v = dot(wx_ref[...], stacked).astype(jnp.bfloat16)
    rows = PLANES * GX
    cells = [
        jnp.concatenate([v[:rows, k : k + HALF], v[rows:, k : k + HALF]], axis=1)
        for k in range(0, units * HALF, HALF)
    ]
    maps = dot(jnp.concatenate(cells, axis=0), wy_ref[...])
    out_ref[0] = maps.reshape(zpart, GX, GY)


def synthesise(returned):
    _, pairs_here, slab_rows, _ = returned.shape
    zpart = slab_rows // 2
    tables = (inverse_x_table(), half_y_inverse())
    return pl.pallas_call(
        synthesise_kernel,
        grid=(pairs_here, slab_rows // (2 * zpart)),
        in_specs=[pl.BlockSpec((GX, 1, 2 * zpart, HALF), lambda i, z: (0, i, z, 0))]
        + [pl.BlockSpec(t.shape, lambda i, z: (0, 0)) for t in tables],
        out_specs=pl.BlockSpec((1, zpart, GX, GY), lambda i, z: (i, z, 0, 0)),
        out_shape=jax.ShapeDtypeStruct((pairs_here, slab_rows // 2, GX, GY), jnp.float32),
        compiler_params=pltpu.CompilerParams(vmem_limit_bytes=VMEM_BYTES),
        name="synthesise",
    )(returned, *(jnp.asarray(t) for t in tables))


def shards(band, pairs, extents):
    tiles, slabs = lax.axis_size("tile"), lax.axis_size("zslab")
    zrows = band.shape[2]
    if tiles * slabs != GX or zrows % (4 * PLANES) or pairs.shape[0] % (2 * tiles):
        return general_shards(band, pairs, extents)
    pairs, extents = pairs.T, extents.T
    tile = lax.axis_index("tile").astype(jnp.int32)
    device = lax.axis_index("zslab").astype(jnp.int32) * tiles + tile
    spectra = analyse(band, pairs, extents, tile[None])
    spread = lax.all_to_all(spectra, ("zslab", "tile"), split_axis=0, concat_axis=0, tiled=True)
    w = correlate(spread, pairs, device[None], slabs, band.shape[0])
    returned = lax.all_to_all(w, ("zslab", "tile"), split_axis=0, concat_axis=0, tiled=True)
    return synthesise(returned)


def solution(mesh):
    placed = (P("tile", None, "zslab", None, None), P(), P())
    return jax.shard_map(
        shards,
        mesh=mesh,
        in_specs=placed,
        out_specs=P("tile", "zslab", None, None),
        check_vma=False,
    )
```

```python
import functools
import math


import jax
import jax.numpy as jnp
import numpy as np
from jax import lax
from jax.experimental import pallas as pl
from jax.experimental.pallas import tpu as pltpu
from jax.sharding import PartitionSpec as P

GX = 32
GY = 256
GZ = 128
FACES = 4


def dft_tables(length):
    indices = jnp.arange(length, dtype=jnp.int32)
    modular = indices[:, None] * indices[None, :] % length
    angles = modular.astype(jnp.float32) * (2.0 * math.pi / length)
    factor = 1.0 / math.sqrt(length)
    return (
        (jnp.cos(angles) * factor).astype(jnp.bfloat16),
        (jnp.sin(angles) * factor).astype(jnp.bfloat16),
    )


def product(form, left, right):
    return jnp.einsum(form, left, right, preferred_element_type=jnp.float32)


def reduce_resolution(image_volume, crop_bounds):
    row_mask = (
        jnp.arange(image_volume.shape[2], dtype=jnp.int32)[None, :] < crop_bounds[:, 0:1]
    ).astype(jnp.bfloat16)
    col_mask = (
        jnp.arange(image_volume.shape[3], dtype=jnp.int32)[None, :] < crop_bounds[:, 1:2]
    ).astype(jnp.bfloat16)
    masked = image_volume * row_mask[:, None, :, None] * col_mask[:, None, None, :]
    raw_cols = jnp.arange(image_volume.shape[3], dtype=jnp.int32)
    pooled_cols = jnp.arange(GY, dtype=jnp.int32)
    pooling = jnp.where(raw_cols[:, None] // 2 == pooled_cols[None, :], 0.5, 0.0).astype(
        jnp.bfloat16
    )
    along_pooled = product("szxy,yk->szxk", masked, pooling)
    shaped = along_pooled.reshape(image_volume.shape[0], image_volume.shape[1], GX, 2, GY)
    return (shaped[:, :, :, 0, :] + shaped[:, :, :, 1, :]).astype(jnp.bfloat16)


def cross_phase(owner_re, owner_im, pairs, tiles_here):
    first_dev = pairs[:, 0] // tiles_here
    first_pos = pairs[:, 0] % tiles_here * FACES + pairs[:, 1]
    second_tile_device = pairs[:, 2] // tiles_here
    second_pos = pairs[:, 2] % tiles_here * FACES + pairs[:, 3]
    first_re = owner_re[first_dev, :, first_pos].astype(jnp.float32)
    first_im = owner_im[first_dev, :, first_pos].astype(jnp.float32)
    second_re = owner_re[second_tile_device, :, second_pos].astype(jnp.float32)
    second_im = owner_im[second_tile_device, :, second_pos].astype(jnp.float32)
    cross_re = first_re * second_re + first_im * second_im
    cross_im = first_im * second_re - first_re * second_im
    scaled = jnp.sqrt(cross_re * cross_re + cross_im * cross_im + 1.0)
    return ((cross_re / scaled).astype(jnp.bfloat16), (cross_im / scaled).astype(jnp.bfloat16))


def inverse_z(phase_real_part, phase_im, tables_z):
    w_re = (
        product("pmjk,mz->pzjk", phase_real_part, tables_z[0])
        - product("pmjk,mz->pzjk", phase_im, tables_z[1])
    ).astype(jnp.bfloat16)
    w_im = (
        product("pmjk,mz->pzjk", phase_im, tables_z[0])
        + product("pmjk,mz->pzjk", phase_real_part, tables_z[1])
    ).astype(jnp.bfloat16)
    return (w_re, w_im)


def inverse_x(w_re, w_im, tables_x):
    v_re = (
        product("pzjk,jx->pzxk", w_re, tables_x[0]) - product("pzjk,jx->pzxk", w_im, tables_x[1])
    ).astype(jnp.bfloat16)
    v_im = (
        product("pzjk,jx->pzxk", w_im, tables_x[0]) + product("pzjk,jx->pzxk", w_re, tables_x[1])
    ).astype(jnp.bfloat16)
    return (v_re, v_im)


def general_shards(band, pairs, extents):
    tables_x = dft_tables(GX)
    tables_y = dft_tables(GY)
    tables_z = dft_tables(GZ)
    tiles_here = band.shape[0]
    slots = tiles_here * FACES
    zrows = band.shape[2]
    tile_pos = lax.axis_index("tile")
    global_slot = tile_pos * slots + jnp.arange(slots, dtype=jnp.int32)
    first_slot = pairs[:, 0] * FACES + pairs[:, 1]
    second_slot = pairs[:, 2] * FACES + pairs[:, 3]
    matches = (
        (first_slot[None, :] == global_slot[:, None])
        | (second_slot[None, :] == global_slot[:, None])
    ).astype(jnp.int32)
    crop_bounds = jnp.sum(matches[:, :, None] * extents[None, :, :], axis=1)
    image_volume = band.reshape(slots, zrows, 2 * GX, 2 * GY)
    reduced_volume = reduce_resolution(image_volume, crop_bounds)
    y_re = product("szxy,yk->szxk", reduced_volume, tables_y[0]).astype(jnp.bfloat16)
    y_im = (-product("szxy,yk->szxk", reduced_volume, tables_y[1])).astype(jnp.bfloat16)
    x_re = (
        product("szxk,xj->szjk", y_re, tables_x[0]) + product("szxk,xj->szjk", y_im, tables_x[1])
    ).astype(jnp.bfloat16)
    x_im = (
        product("szxk,xj->szjk", y_im, tables_x[0]) - product("szxk,xj->szjk", y_re, tables_x[1])
    ).astype(jnp.bfloat16)
    kx_part = GX // lax.axis_size("zslab")
    re_in = lax.all_to_all(x_re, "zslab", split_axis=2, concat_axis=1, tiled=True)
    im_in = lax.all_to_all(x_im, "zslab", split_axis=2, concat_axis=1, tiled=True)
    out_re = (
        product("szjk,zm->msjk", re_in, tables_z[0]) + product("szjk,zm->msjk", im_in, tables_z[1])
    ).astype(jnp.bfloat16)
    out_im = (
        product("szjk,zm->msjk", im_in, tables_z[0]) - product("szjk,zm->msjk", re_in, tables_z[1])
    ).astype(jnp.bfloat16)
    tile_count = lax.axis_size("tile")
    kz_part = GZ // tile_count
    spectra = (
        lax.all_to_all(out_re, "tile", split_axis=0, concat_axis=0, tiled=True),
        lax.all_to_all(out_im, "tile", split_axis=0, concat_axis=0, tiled=True),
    )
    owner_re = spectra[0].reshape(tile_count, kz_part, slots, kx_part, GY)
    owner_im = spectra[1].reshape(tile_count, kz_part, slots, kx_part, GY)
    phase_real_part, phase_im = cross_phase(owner_re, owner_im, pairs, tiles_here)
    returned = (
        lax.all_to_all(phase_real_part, "tile", split_axis=0, concat_axis=1, tiled=True),
        lax.all_to_all(phase_im, "tile", split_axis=0, concat_axis=1, tiled=True),
    )
    w_re, w_im = inverse_z(returned[0], returned[1], tables_z)
    v_re, v_im = inverse_x(
        lax.all_to_all(w_re, "zslab", split_axis=1, concat_axis=2, tiled=True),
        lax.all_to_all(w_im, "zslab", split_axis=1, concat_axis=2, tiled=True),
        tables_x,
    )
    return product("pzxk,ky->pzxy", v_re, tables_y[0]) - product("pzxk,ky->pzxy", v_im, tables_y[1])


HALF = GY // 2
PLANES = 4
VMEM_BYTES = 32 * 1024 * 1024


def host_tables(length):
    indices = np.arange(length, dtype=np.int32)
    modular = indices[:, None] * indices[None, :] % length
    angles = modular.astype(np.float32) * np.float32(2.0 * math.pi / length)
    factor = np.float32(1.0 / math.sqrt(length))
    return (
        (np.cos(angles) * factor).astype(jnp.bfloat16),
        (np.sin(angles) * factor).astype(jnp.bfloat16),
    )


def half_y_table():
    cosine, sine = host_tables(GY)
    imag = -sine[:, :HALF]
    imag[:, 0] = cosine[:, HALF]
    return np.concatenate([cosine[:, :HALF], imag], axis=1)


def paired_y_table():
    table = np.zeros((2 * GY, GY), jnp.bfloat16)
    table[::2] = half_y_table() * np.array(0.5, jnp.bfloat16)
    return table


def half_y_inverse():
    cosine, sine = host_tables(GY)
    two = np.array(2.0, jnp.bfloat16)
    real = cosine[:HALF, :] * two
    real[0] = cosine[0]
    imag = -sine[:HALF, :] * two
    imag[0] = cosine[HALF]
    return np.concatenate([real, imag], axis=0)


def mirror_order():
    order = [0, GX // 2]
    for j in range(1, GX // 2):
        order += [j, GX - j]
    return order


def complex_blocks(length, sign):
    cosine, sine = (table.astype(np.float32) for table in host_tables(length))
    return np.array([[cosine, -sign * sine], [sign * sine, cosine]])


def forward_x_table():
    table = np.einsum("oijx,az->joaizx", complex_blocks(GX, -1), np.eye(PLANES))[mirror_order()]
    table = table.reshape(2 * GX * PLANES, 2, PLANES, GX)
    woven = table[:, :, :2].transpose(0, 1, 3, 2).reshape(-1, 2, 2 * GX)
    plain = table[:, :, 2:].reshape(-1, 2, (PLANES - 2) * GX)
    table = np.concatenate([woven, plain], axis=2)
    return table.reshape(2 * GX * PLANES, -1).astype(jnp.bfloat16)


def inverse_x_table():
    table = np.einsum("oijx,az->oaxjiz", complex_blocks(GX, 1), np.eye(PLANES))
    return table.reshape(2 * PLANES * GX, -1).astype(jnp.bfloat16)


def z_rows():
    return np.arange(2 * GZ).reshape(2, GZ // PLANES, PLANES).transpose(1, 0, 2).reshape(-1)


def z_tables():
    forward, inverse = (
        complex_blocks(GZ, sign).transpose(0, 2, 1, 3).reshape(2 * GZ, 2 * GZ) for sign in (-1, 1)
    )
    none = np.zeros((2 * GZ, GZ), np.float32)
    forward_last = np.concatenate([none, forward[:, :GZ]], axis=1)
    inverse_last = np.concatenate([none.T, inverse[:GZ]], axis=0)
    order = z_rows()
    return [
        np.ascontiguousarray(table).astype(jnp.bfloat16)
        for table in (
            forward[:, order],
            inverse[order],
            forward_last[:, order],
            inverse_last[order],
        )
    ]


def imaginary_rows(shape):
    return lax.broadcasted_iota(jnp.int32, shape, 0) % (2 * PLANES) >= PLANES


def first_lane(shape):
    return lax.broadcasted_iota(jnp.int32, shape, 1) == 0


def dot(left, right):
    return jnp.dot(left, right, preferred_element_type=jnp.float32)


def analyse_kernel(
    slots, pairs_ref, extents_ref, tile_ref, *rest
):
    band_refs, (wy_ref, wx_ref, out_ref, crop_ref) = rest[:-4], rest[-4:]
    slot = pl.program_id(0)

    @pl.when(slot == 0)
    def _():
        for p in range(pairs_ref.shape[1]):
            for end in (0, 1):
                named = pairs_ref[2 * end, p] * FACES + pairs_ref[2 * end + 1, p] - tile_ref[0] * slots

                @pl.when((named >= 0) & (named < slots))
                def _():
                    crop_ref[named, 0] = extents_ref[0, p]
                    crop_ref[named, 1] = extents_ref[1, p]

    across, along = crop_ref[slot, 0], crop_ref[slot, 1]

    def live(k, rows):
        lane = lax.broadcasted_iota(jnp.int32, rows.shape, 1)
        return jnp.where((rows < across) & (k * 128 + lane < along), 1.0, 0.0)

    def halves(rows):
        return (rows + pltpu.roll(rows, 127, 1)).astype(jnp.bfloat16)

    raw_row = lax.broadcasted_iota(jnp.int32, (2 * GX, 128), 0)
    pooled_row = lax.broadcasted_iota(jnp.int32, (GX, 128), 0)
    even = raw_row % 2 == 0
    groups = (2 * GX // 8, 8, 128)
    lives = [
        (live(k, raw_row), live(k, 2 * pooled_row), live(k, 2 * pooled_row + 1))
        for k in range(len(band_refs))
    ]
    block = (2 * PLANES, HALF)
    lane0, imaginary = first_lane(block), imaginary_rows(block)
    sign = jnp.where(imaginary, -0.5, 0.5)

    def row_pairs(ref, z, mask, shift):
        raw = ref[0, 0, z].astype(jnp.float32) * mask
        return raw + pltpu.roll(raw.reshape(groups), shift, 1).reshape(raw.shape)

    def woven(z):
        return [
            halves(jnp.where(even, row_pairs(ref, z, mask, 7), row_pairs(ref, z + 1, mask, 1)))
            for ref, (mask, _, _) in zip(band_refs, lives)
        ]

    def plain(z):
        parts = []
        for ref, (_, *masks) in zip(band_refs, lives):
            rows = [ref[0, 0, z, pl.ds(a, GX, stride=2), :].astype(jnp.float32) for a in (0, 1)]
            parts.append(halves(rows[0] * masks[0] + rows[1] * masks[1]))
        return parts

    def pool(z):
        return [
            jnp.concatenate(parts, axis=1)
            for parts in (woven(z), *(plain(z + k) for k in range(2, PLANES)))
        ]

    zpart = 4 * PLANES
    zrows = band_refs[0].shape[2]
    planes = sum((pool(z) for z in range(0, zrows, PLANES)), [])
    y = dot(jnp.concatenate(planes, axis=0), wy_ref[...]).astype(jnp.bfloat16)
    y = y.reshape(zrows // PLANES, PLANES * GX, GY)

    def store(start, spectra):
        def at(n):
            rows = spectra[2 * PLANES * n : 2 * PLANES * (n + 1)]
            return [rows[:, k : k + HALF] for k in range(0, rows.shape[1], HALF)]

        def put(j, blocks):
            rows = slice(2 * start, 2 * (start + zpart))
            out_ref[j, 0, rows] = jnp.concatenate(blocks, axis=0).astype(jnp.bfloat16)

        put(0, at(0))
        put(GX // 2, at(1))
        for j in range(1, GX // 2):
            here, mirror = at(2 * j), at(2 * j + 1)
            put(j, [jnp.where(lane0, 0.5 * a + sign * b, a) for a, b in zip(here, mirror)])
            put(
                GX - j,
                [
                    jnp.where(lane0, pltpu.roll(0.5 * a - sign * b, PLANES, 0), b)
                    for a, b in zip(here, mirror)
                ],
            )

    for start in range(0, zrows, zpart):
        units = [
            jnp.concatenate([y[unit, :, :HALF], y[unit, :, HALF:]], axis=0)
            for unit in range(start // PLANES, (start + zpart) // PLANES)
        ]
        store(start, dot(wx_ref[...], jnp.concatenate(units, axis=1)))


def analyse(band, pairs, extents, tile):
    slots, zrows = band.shape[0] * FACES, band.shape[2]
    tables = (paired_y_table(), forward_x_table())
    whole = [pl.BlockSpec(t.shape, lambda i, *_: (0, 0)) for t in tables]
    lane_blocks = 2 * GY // 128
    return pl.pallas_call(
        functools.partial(analyse_kernel, slots),
        grid_spec=pltpu.PrefetchScalarGridSpec(
            num_scalar_prefetch=3,
            grid=(slots,),
            in_specs=[
                pl.BlockSpec(
                    (1, 1, zrows, 2 * GX, 128),
                    lambda i, *_, k=k: (i // FACES, i % FACES, 0, 0, k),
                )
                for k in range(lane_blocks)
            ]
            + whole,
            out_specs=pl.BlockSpec((GX, 1, 2 * zrows, HALF), lambda i, *_: (0, i, 0, 0)),
            scratch_shapes=[pltpu.SMEM((slots, 2), jnp.int32)],
        ),
        out_shape=jax.ShapeDtypeStruct((GX, slots, 2 * zrows, HALF), jnp.bfloat16),
        compiler_params=pltpu.CompilerParams(vmem_limit_bytes=VMEM_BYTES + VMEM_BYTES * 3 // 4),
        name="analyse",
    )(pairs, extents, tile, *[band] * lane_blocks, *(jnp.asarray(t) for t in tables))


def normalised(a_re, a_im, b_re, b_im):
    cross_re = a_re * b_re + a_im * b_im
    cross_im = a_im * b_re - a_re * b_im
    scale = lax.rsqrt(cross_re * cross_re + cross_im * cross_im + 1.0)
    return (cross_re * scale).astype(jnp.bfloat16), (cross_im * scale).astype(jnp.bfloat16)


def correlate_kernel(
    slabs, tiles_here, pairs_ref, place_ref, in_ref, wz_ref, wzi_ref, wz_last_ref, wzi_last_ref, out_ref
):
    tiles = in_ref.shape[0] // slabs
    total = pairs_ref.shape[1]
    pairs_here = out_ref.shape[1]
    slab_rows = out_ref.shape[2]
    both_real = (place_ref[0] == 0) | (place_ref[0] == GX // 2)
    block = (2 * GZ, HALF)
    shared = first_lane(block) & imaginary_rows(block)

    def load(p, end):
        tile = pairs_ref[2 * end, p]
        row = tile // tiles_here
        pos = tile % tiles_here * FACES + pairs_ref[2 * end + 1, p]
        return jnp.concatenate([in_ref[row + s * tiles, pos] for s in range(slabs)], axis=0)

    def phase_of(table_ref, first, second):
        spec = dot(table_ref[...], jnp.concatenate([first, second], axis=1))
        spec = spec.astype(jnp.bfloat16).astype(jnp.float32)
        phase = normalised(spec[:GZ, :HALF], spec[GZ:, :HALF], spec[:GZ, HALF:], spec[GZ:, HALF:])
        return jnp.concatenate(phase, axis=0)

    keep = jnp.where(shared & both_real, 0.0, 1.0).astype(jnp.bfloat16)
    for p in range(0, total, 2):
        phases = [phase_of(wz_ref, load(q, 0) * keep, load(q, 1) * keep) for q in (p, p + 1)]
        w = dot(wzi_ref[...], jnp.concatenate(phases, axis=1)).astype(jnp.bfloat16)
        for k, q in enumerate((p, p + 1)):
            for s in range(slabs):
                out_ref[q // pairs_here + s * tiles, q % pairs_here] = w[
                    s * slab_rows : (s + 1) * slab_rows, k * HALF : (k + 1) * HALF
                ]

    @pl.when(both_real)
    def _():
        lane = lax.broadcasted_iota(jnp.int32, block, 1)
        ends = [jnp.zeros(block, jnp.bfloat16)] * 2
        for p in range(total):
            for end in (0, 1):
                ends[end] = jnp.where(lane == p, load(p, end)[:, 0:1], ends[end])
        w = dot(wzi_last_ref[...], phase_of(wz_last_ref, *ends)).astype(jnp.bfloat16)
        for p in range(total):
            column = w[:, p : p + 1]
            for s in range(slabs):
                rows = slice(s * slab_rows, (s + 1) * slab_rows)
                at = (p // pairs_here + s * tiles, p % pairs_here)
                out_ref[at] = jnp.where(shared[rows], column[rows], out_ref[at])


def correlate(spread, pairs, place, slabs, tiles_here):
    devices, _, slab_rows, _ = spread.shape
    pairs_here = pairs.shape[1] * slabs // devices
    tables = z_tables()
    vmem = pl.BlockSpec(memory_space=pltpu.VMEM)
    smem = pl.BlockSpec(memory_space=pltpu.SMEM)
    return pl.pallas_call(
        functools.partial(correlate_kernel, slabs, tiles_here),
        in_specs=[smem, smem] + [vmem] * (1 + len(tables)),
        out_specs=vmem,
        out_shape=jax.ShapeDtypeStruct((devices, pairs_here, slab_rows, HALF), jnp.bfloat16),
        compiler_params=pltpu.CompilerParams(vmem_limit_bytes=VMEM_BYTES),
        name="correlate",
    )(pairs, place, spread, *(jnp.asarray(t) for t in tables))


def synthesise_kernel(in_ref, wx_ref, wy_ref, out_ref):
    zpart = out_ref.shape[1]
    units = zpart // PLANES
    block = (2 * zpart, HALF)
    lane0, imaginary = first_lane(block), imaginary_rows(block)
    sign = jnp.where(imaginary, -1.0, 1.0)
    groups = (units, 2 * PLANES, HALF)

    def at(j):
        return in_ref[j, 0].astype(jnp.float32)

    blocks = [None] * GX
    for j in (0, GX // 2):
        blocks[j] = at(j)
    for j in range(1, GX // 2):
        here, mirror = at(j), at(GX - j)
        swapped = pltpu.roll(mirror.reshape(groups), PLANES, 1).reshape(block)
        blocks[j] = jnp.where(lane0, here + swapped, here)
        blocks[GX - j] = jnp.where(lane0, sign * (here - swapped), mirror)
    stacked = jnp.concatenate(
        [
            jnp.concatenate([b[u * 2 * PLANES : (u + 1) * 2 * PLANES] for b in blocks], axis=0)
            for u in range(units)
        ],
        axis=1,
    ).astype(jnp.bfloat16)
    v = dot(wx_ref[...], stacked).astype(jnp.bfloat16)
    rows = PLANES * GX
    cells = [
        jnp.concatenate([v[:rows, k : k + HALF], v[rows:, k : k + HALF]], axis=1)
        for k in range(0, units * HALF, HALF)
    ]
    maps = dot(jnp.concatenate(cells, axis=0), wy_ref[...])
    out_ref[0] = maps.reshape(zpart, GX, GY)


def synthesise(returned):
    _, pairs_here, slab_rows, _ = returned.shape
    zpart = slab_rows // 2
    tables = (inverse_x_table(), half_y_inverse())
    return pl.pallas_call(
        synthesise_kernel,
        grid=(pairs_here, slab_rows // (2 * zpart)),
        in_specs=[pl.BlockSpec((GX, 1, 2 * zpart, HALF), lambda i, z: (0, i, z, 0))]
        + [pl.BlockSpec(t.shape, lambda i, z: (0, 0)) for t in tables],
        out_specs=pl.BlockSpec((1, zpart, GX, GY), lambda i, z: (i, z, 0, 0)),
        out_shape=jax.ShapeDtypeStruct((pairs_here, slab_rows // 2, GX, GY), jnp.float32),
        compiler_params=pltpu.CompilerParams(vmem_limit_bytes=VMEM_BYTES),
        name="synthesise",
    )(returned, *(jnp.asarray(t) for t in tables))


def shards(band, pairs, extents):
    tiles, slabs = lax.axis_size("tile"), lax.axis_size("zslab")
    zrows = band.shape[2]
    if tiles * slabs != GX or zrows % (4 * PLANES) or pairs.shape[0] % (2 * tiles):
        return general_shards(band, pairs, extents)
    pairs, extents = pairs.T, extents.T
    tile = lax.axis_index("tile").astype(jnp.int32)
    device = lax.axis_index("zslab").astype(jnp.int32) * tiles + tile
    spectra = analyse(band, pairs, extents, tile[None])
    spread = lax.all_to_all(spectra, ("zslab", "tile"), split_axis=0, concat_axis=0, tiled=True)
    w = correlate(spread, pairs, device[None], slabs, band.shape[0])
    returned = lax.all_to_all(w, ("zslab", "tile"), split_axis=0, concat_axis=0, tiled=True)
    return synthesise(returned)


def solution(mesh):
    placed = (P("tile", None, "zslab", None, None), P(), P())
    return jax.shard_map(
        shards,
        mesh=mesh,
        in_specs=placed,
        out_specs=P("tile", "zslab", None, None),
        check_vma=False,
    )
```

```python
import functools
import math


import jax
import jax.numpy as jnp
import numpy as np
from jax import lax
from jax.experimental import pallas as pl
from jax.experimental.pallas import tpu as pltpu
from jax.sharding import PartitionSpec as P

GX = 32
GY = 256
GZ = 128
FACES = 4


def dft_tables(length):
    indices = jnp.arange(length, dtype=jnp.int32)
    modular = indices[:, None] * indices[None, :] % length
    angles = modular.astype(jnp.float32) * (2.0 * math.pi / length)
    factor = 1.0 / math.sqrt(length)
    return (
        (jnp.cos(angles) * factor).astype(jnp.bfloat16),
        (jnp.sin(angles) * factor).astype(jnp.bfloat16),
    )


def product(form, left, right):
    return jnp.einsum(form, left, right, preferred_element_type=jnp.float32)


def reduce_resolution(image_volume, crop_bounds):
    row_mask = (
        jnp.arange(image_volume.shape[2], dtype=jnp.int32)[None, :] < crop_bounds[:, 0:1]
    ).astype(jnp.bfloat16)
    col_mask = (
        jnp.arange(image_volume.shape[3], dtype=jnp.int32)[None, :] < crop_bounds[:, 1:2]
    ).astype(jnp.bfloat16)
    masked = image_volume * row_mask[:, None, :, None] * col_mask[:, None, None, :]
    raw_cols = jnp.arange(image_volume.shape[3], dtype=jnp.int32)
    pooled_cols = jnp.arange(GY, dtype=jnp.int32)
    pooling = jnp.where(raw_cols[:, None] // 2 == pooled_cols[None, :], 0.5, 0.0).astype(
        jnp.bfloat16
    )
    along_pooled = product("szxy,yk->szxk", masked, pooling)
    shaped = along_pooled.reshape(image_volume.shape[0], image_volume.shape[1], GX, 2, GY)
    return (shaped[:, :, :, 0, :] + shaped[:, :, :, 1, :]).astype(jnp.bfloat16)


def cross_phase(owner_re, owner_im, pairs, tiles_here):
    first_dev = pairs[:, 0] // tiles_here
    first_pos = pairs[:, 0] % tiles_here * FACES + pairs[:, 1]
    second_tile_device = pairs[:, 2] // tiles_here
    second_pos = pairs[:, 2] % tiles_here * FACES + pairs[:, 3]
    first_re = owner_re[first_dev, :, first_pos].astype(jnp.float32)
    first_im = owner_im[first_dev, :, first_pos].astype(jnp.float32)
    second_re = owner_re[second_tile_device, :, second_pos].astype(jnp.float32)
    second_im = owner_im[second_tile_device, :, second_pos].astype(jnp.float32)
    cross_re = first_re * second_re + first_im * second_im
    cross_im = first_im * second_re - first_re * second_im
    scaled = jnp.sqrt(cross_re * cross_re + cross_im * cross_im + 1.0)
    return ((cross_re / scaled).astype(jnp.bfloat16), (cross_im / scaled).astype(jnp.bfloat16))


def inverse_z(phase_real_part, phase_im, tables_z):
    w_re = (
        product("pmjk,mz->pzjk", phase_real_part, tables_z[0])
        - product("pmjk,mz->pzjk", phase_im, tables_z[1])
    ).astype(jnp.bfloat16)
    w_im = (
        product("pmjk,mz->pzjk", phase_im, tables_z[0])
        + product("pmjk,mz->pzjk", phase_real_part, tables_z[1])
    ).astype(jnp.bfloat16)
    return (w_re, w_im)


def inverse_x(w_re, w_im, tables_x):
    v_re = (
        product("pzjk,jx->pzxk", w_re, tables_x[0]) - product("pzjk,jx->pzxk", w_im, tables_x[1])
    ).astype(jnp.bfloat16)
    v_im = (
        product("pzjk,jx->pzxk", w_im, tables_x[0]) + product("pzjk,jx->pzxk", w_re, tables_x[1])
    ).astype(jnp.bfloat16)
    return (v_re, v_im)


def general_shards(band, pairs, extents):
    tables_x = dft_tables(GX)
    tables_y = dft_tables(GY)
    tables_z = dft_tables(GZ)
    tiles_here = band.shape[0]
    slots = tiles_here * FACES
    zrows = band.shape[2]
    tile_pos = lax.axis_index("tile")
    global_slot = tile_pos * slots + jnp.arange(slots, dtype=jnp.int32)
    first_slot = pairs[:, 0] * FACES + pairs[:, 1]
    second_slot = pairs[:, 2] * FACES + pairs[:, 3]
    matches = (
        (first_slot[None, :] == global_slot[:, None])
        | (second_slot[None, :] == global_slot[:, None])
    ).astype(jnp.int32)
    crop_bounds = jnp.sum(matches[:, :, None] * extents[None, :, :], axis=1)
    image_volume = band.reshape(slots, zrows, 2 * GX, 2 * GY)
    reduced_volume = reduce_resolution(image_volume, crop_bounds)
    y_re = product("szxy,yk->szxk", reduced_volume, tables_y[0]).astype(jnp.bfloat16)
    y_im = (-product("szxy,yk->szxk", reduced_volume, tables_y[1])).astype(jnp.bfloat16)
    x_re = (
        product("szxk,xj->szjk", y_re, tables_x[0]) + product("szxk,xj->szjk", y_im, tables_x[1])
    ).astype(jnp.bfloat16)
    x_im = (
        product("szxk,xj->szjk", y_im, tables_x[0]) - product("szxk,xj->szjk", y_re, tables_x[1])
    ).astype(jnp.bfloat16)
    kx_part = GX // lax.axis_size("zslab")
    re_in = lax.all_to_all(x_re, "zslab", split_axis=2, concat_axis=1, tiled=True)
    im_in = lax.all_to_all(x_im, "zslab", split_axis=2, concat_axis=1, tiled=True)
    out_re = (
        product("szjk,zm->msjk", re_in, tables_z[0]) + product("szjk,zm->msjk", im_in, tables_z[1])
    ).astype(jnp.bfloat16)
    out_im = (
        product("szjk,zm->msjk", im_in, tables_z[0]) - product("szjk,zm->msjk", re_in, tables_z[1])
    ).astype(jnp.bfloat16)
    tile_count = lax.axis_size("tile")
    kz_part = GZ // tile_count
    spectra = (
        lax.all_to_all(out_re, "tile", split_axis=0, concat_axis=0, tiled=True),
        lax.all_to_all(out_im, "tile", split_axis=0, concat_axis=0, tiled=True),
    )
    owner_re = spectra[0].reshape(tile_count, kz_part, slots, kx_part, GY)
    owner_im = spectra[1].reshape(tile_count, kz_part, slots, kx_part, GY)
    phase_real_part, phase_im = cross_phase(owner_re, owner_im, pairs, tiles_here)
    returned = (
        lax.all_to_all(phase_real_part, "tile", split_axis=0, concat_axis=1, tiled=True),
        lax.all_to_all(phase_im, "tile", split_axis=0, concat_axis=1, tiled=True),
    )
    w_re, w_im = inverse_z(returned[0], returned[1], tables_z)
    v_re, v_im = inverse_x(
        lax.all_to_all(w_re, "zslab", split_axis=1, concat_axis=2, tiled=True),
        lax.all_to_all(w_im, "zslab", split_axis=1, concat_axis=2, tiled=True),
        tables_x,
    )
    return product("pzxk,ky->pzxy", v_re, tables_y[0]) - product("pzxk,ky->pzxy", v_im, tables_y[1])


HALF = GY // 2
PLANES = 4
VMEM_BYTES = 32 * 1024 * 1024


def host_tables(length):
    indices = np.arange(length, dtype=np.int32)
    modular = indices[:, None] * indices[None, :] % length
    angles = modular.astype(np.float32) * np.float32(2.0 * math.pi / length)
    factor = np.float32(1.0 / math.sqrt(length))
    return (
        (np.cos(angles) * factor).astype(jnp.bfloat16),
        (np.sin(angles) * factor).astype(jnp.bfloat16),
    )


def half_y_table():
    cosine, sine = host_tables(GY)
    imag = -sine[:, :HALF]
    imag[:, 0] = cosine[:, HALF]
    return np.concatenate([cosine[:, :HALF], imag], axis=1)


def paired_y_table():
    table = np.zeros((2 * GY, GY), jnp.bfloat16)
    table[::2] = half_y_table() * np.array(0.5, jnp.bfloat16)
    return table


def half_y_inverse():
    cosine, sine = host_tables(GY)
    two = np.array(2.0, jnp.bfloat16)
    real = cosine[:HALF, :] * two
    real[0] = cosine[0]
    imag = -sine[:HALF, :] * two
    imag[0] = cosine[HALF]
    return np.concatenate([real, imag], axis=0)


def mirror_order():
    order = [0, GX // 2]
    for j in range(1, GX // 2):
        order += [j, GX - j]
    return order


def complex_blocks(length, sign):
    cosine, sine = (table.astype(np.float32) for table in host_tables(length))
    return np.array([[cosine, -sign * sine], [sign * sine, cosine]])


def forward_x_table():
    table = np.einsum("oijx,az->joaizx", complex_blocks(GX, -1), np.eye(PLANES))[mirror_order()]
    table = table.reshape(2 * GX * PLANES, 2, PLANES // 2, 2, GX).transpose(0, 1, 2, 4, 3)
    return table.reshape(2 * GX * PLANES, -1).astype(jnp.bfloat16)


def inverse_x_table():
    table = np.einsum("oijx,az->oaxjiz", complex_blocks(GX, 1), np.eye(PLANES))
    return table.reshape(2 * PLANES * GX, -1).astype(jnp.bfloat16)


def z_rows():
    return np.arange(2 * GZ).reshape(2, GZ // PLANES, PLANES).transpose(1, 0, 2).reshape(-1)


def z_tables():
    forward, inverse = (
        complex_blocks(GZ, sign).transpose(0, 2, 1, 3).reshape(2 * GZ, 2 * GZ) for sign in (-1, 1)
    )
    none = np.zeros((2 * GZ, GZ), np.float32)
    forward_last = np.concatenate([none, forward[:, :GZ]], axis=1)
    inverse_last = np.concatenate([none.T, inverse[:GZ]], axis=0)
    order = z_rows()
    return [
        np.ascontiguousarray(table).astype(jnp.bfloat16)
        for table in (
            forward[:, order],
            inverse[order],
            forward_last[:, order],
            inverse_last[order],
        )
    ]


def imaginary_rows(shape):
    return lax.broadcasted_iota(jnp.int32, shape, 0) % (2 * PLANES) >= PLANES


def first_lane(shape):
    return lax.broadcasted_iota(jnp.int32, shape, 1) == 0


def dot(left, right):
    return jnp.dot(left, right, preferred_element_type=jnp.float32)


def analyse_kernel(
    slots,
    pairs_ref,
    extents_ref,
    tile_ref,
    band_ref,
    wy_ref,
    wx_ref,
    out_ref,
    crop_ref,
    down_ref,
    spectra_ref,
):
    slot = pl.program_id(0)

    @pl.when(slot == 0)
    def _():
        for p in range(pairs_ref.shape[1]):
            for end in (0, 1):
                named = pairs_ref[2 * end, p] * FACES + pairs_ref[2 * end + 1, p] - tile_ref[0] * slots

                @pl.when((named >= 0) & (named < slots))
                def _():
                    crop_ref[named, 0] = extents_ref[0, p]
                    crop_ref[named, 1] = extents_ref[1, p]

    across, along = crop_ref[slot, 0], crop_ref[slot, 1]
    zrows = band_ref.shape[2]
    row = lax.broadcasted_iota(jnp.int32, (2 * GX, 128), 0)
    lane = lax.broadcasted_iota(jnp.int32, (2 * GX, 128), 1)
    even = row % 2 == 0
    groups = (2 * GX // 8, 8, 128)

    @pl.loop(0, zrows // PLANES)
    def _(unit):
        for k in range(0, 2 * GY, 128):
            mask = jnp.where((row < across) & (k + lane < along), 1.0, 0.0)

            def row_pairs(plane, shift):
                raw = band_ref[0, 0, unit * PLANES + plane, :, k : k + 128].astype(jnp.float32) * mask
                return raw + pltpu.roll(raw.reshape(groups), shift, 1).reshape(raw.shape)

            cells = []
            for plane in range(0, PLANES, 2):
                both = jnp.where(even, row_pairs(plane, 7), row_pairs(plane + 1, 1))
                cells.append((both + pltpu.roll(both, 127, 1)).astype(jnp.bfloat16))
            at = pl.ds(pl.multiple_of(unit * PLANES * GX, PLANES * GX), PLANES * GX)
            down_ref[at, k : k + 128] = jnp.concatenate(cells, axis=0)

    y = dot(down_ref[...], wy_ref[...]).astype(jnp.bfloat16)
    y = y.reshape(zrows // PLANES, PLANES * GX, GY)
    units = [
        jnp.concatenate([y[unit, :, :HALF], y[unit, :, HALF:]], axis=0)
        for unit in range(zrows // PLANES)
    ]
    spectra = dot(wx_ref[...], jnp.concatenate(units, axis=1))
    spectra_ref[...] = spectra.reshape(spectra_ref.shape)

    block = (2 * PLANES, HALF)
    lane0, imaginary = first_lane(block), imaginary_rows(block)
    sign = jnp.where(imaginary, -0.5, 0.5)

    def at(n):
        return [spectra_ref[n, :, k : k + HALF] for k in range(0, spectra_ref.shape[2], HALF)]

    def put(j, blocks):
        out_ref[j, 0] = jnp.concatenate(blocks, axis=0).astype(jnp.bfloat16)

    put(0, at(0))
    put(GX // 2, at(1))

    @pl.loop(1, GX // 2)
    def _(j):
        here, mirror = at(2 * j), at(2 * j + 1)
        put(j, [jnp.where(lane0, 0.5 * a + sign * b, a) for a, b in zip(here, mirror)])
        put(
            GX - j,
            [
                jnp.where(lane0, pltpu.roll(0.5 * a - sign * b, PLANES, 0), b)
                for a, b in zip(here, mirror)
            ],
        )


def analyse(band, pairs, extents, tile):
    slots, zrows = band.shape[0] * FACES, band.shape[2]
    tables = (paired_y_table(), forward_x_table())
    whole = [pl.BlockSpec(t.shape, lambda i, *_: (0, 0)) for t in tables]
    return pl.pallas_call(
        functools.partial(analyse_kernel, slots),
        grid_spec=pltpu.PrefetchScalarGridSpec(
            num_scalar_prefetch=3,
            grid=(slots,),
            in_specs=[
                pl.BlockSpec(
                    (1, 1, zrows, 2 * GX, 2 * GY), lambda i, *_: (i // FACES, i % FACES, 0, 0, 0)
                )
            ]
            + whole,
            out_specs=pl.BlockSpec((GX, 1, 2 * zrows, HALF), lambda i, *_: (0, i, 0, 0)),
            scratch_shapes=[
                pltpu.SMEM((slots, 2), jnp.int32),
                pltpu.VMEM((zrows * GX, 2 * GY), jnp.bfloat16),
                pltpu.VMEM((GX, 2 * PLANES, zrows // PLANES * HALF), jnp.float32),
            ],
        ),
        out_shape=jax.ShapeDtypeStruct((GX, slots, 2 * zrows, HALF), jnp.bfloat16),
        compiler_params=pltpu.CompilerParams(vmem_limit_bytes=VMEM_BYTES + VMEM_BYTES * 3 // 4),
        name="analyse",
    )(pairs, extents, tile, band, *(jnp.asarray(t) for t in tables))


def normalised(a_re, a_im, b_re, b_im):
    cross_re = a_re * b_re + a_im * b_im
    cross_im = a_im * b_re - a_re * b_im
    scale = lax.rsqrt(cross_re * cross_re + cross_im * cross_im + 1.0)
    return (cross_re * scale).astype(jnp.bfloat16), (cross_im * scale).astype(jnp.bfloat16)


def correlate_kernel(
    slabs, tiles_here, pairs_ref, place_ref, in_ref, wz_ref, wzi_ref, wz_last_ref, wzi_last_ref, out_ref
):
    tiles = in_ref.shape[0] // slabs
    total = pairs_ref.shape[1]
    pairs_here = out_ref.shape[1]
    slab_rows = out_ref.shape[2]
    both_real = (place_ref[0] == 0) | (place_ref[0] == GX // 2)
    block = (2 * GZ, HALF)
    shared = first_lane(block) & imaginary_rows(block)

    def load(p, end):
        tile = pairs_ref[2 * end, p]
        row = tile // tiles_here
        pos = tile % tiles_here * FACES + pairs_ref[2 * end + 1, p]
        return jnp.concatenate([in_ref[row + s * tiles, pos] for s in range(slabs)], axis=0)

    def phase_of(table_ref, first, second):
        spec = dot(table_ref[...], jnp.concatenate([first, second], axis=1))
        spec = spec.astype(jnp.bfloat16).astype(jnp.float32)
        phase = normalised(spec[:GZ, :HALF], spec[GZ:, :HALF], spec[:GZ, HALF:], spec[GZ:, HALF:])
        return jnp.concatenate(phase, axis=0)

    keep = jnp.where(shared & both_real, 0.0, 1.0).astype(jnp.bfloat16)
    for p in range(0, total, 2):
        phases = [phase_of(wz_ref, load(q, 0) * keep, load(q, 1) * keep) for q in (p, p + 1)]
        w = dot(wzi_ref[...], jnp.concatenate(phases, axis=1)).astype(jnp.bfloat16)
        for k, q in enumerate((p, p + 1)):
            for s in range(slabs):
                out_ref[q // pairs_here + s * tiles, q % pairs_here] = w[
                    s * slab_rows : (s + 1) * slab_rows, k * HALF : (k + 1) * HALF
                ]

    @pl.when(both_real)
    def _():
        lane = lax.broadcasted_iota(jnp.int32, block, 1)
        ends = [jnp.zeros(block, jnp.bfloat16)] * 2
        for p in range(total):
            for end in (0, 1):
                ends[end] = jnp.where(lane == p, load(p, end)[:, 0:1], ends[end])
        w = dot(wzi_last_ref[...], phase_of(wz_last_ref, *ends)).astype(jnp.bfloat16)
        for p in range(total):
            column = w[:, p : p + 1]
            for s in range(slabs):
                rows = slice(s * slab_rows, (s + 1) * slab_rows)
                at = (p // pairs_here + s * tiles, p % pairs_here)
                out_ref[at] = jnp.where(shared[rows], column[rows], out_ref[at])


def correlate(spread, pairs, place, slabs, tiles_here):
    devices, _, slab_rows, _ = spread.shape
    pairs_here = pairs.shape[1] * slabs // devices
    tables = z_tables()
    vmem = pl.BlockSpec(memory_space=pltpu.VMEM)
    smem = pl.BlockSpec(memory_space=pltpu.SMEM)
    return pl.pallas_call(
        functools.partial(correlate_kernel, slabs, tiles_here),
        in_specs=[smem, smem] + [vmem] * (1 + len(tables)),
        out_specs=vmem,
        out_shape=jax.ShapeDtypeStruct((devices, pairs_here, slab_rows, HALF), jnp.bfloat16),
        compiler_params=pltpu.CompilerParams(vmem_limit_bytes=VMEM_BYTES),
        name="correlate",
    )(pairs, place, spread, *(jnp.asarray(t) for t in tables))


def synthesise_kernel(in_ref, wx_ref, wy_ref, out_ref):
    zpart = out_ref.shape[1]
    units = zpart // PLANES
    block = (2 * zpart, HALF)
    lane0, imaginary = first_lane(block), imaginary_rows(block)
    sign = jnp.where(imaginary, -1.0, 1.0)
    groups = (units, 2 * PLANES, HALF)

    def at(j):
        return in_ref[j, 0].astype(jnp.float32)

    blocks = [None] * GX
    for j in (0, GX // 2):
        blocks[j] = at(j)
    for j in range(1, GX // 2):
        here, mirror = at(j), at(GX - j)
        swapped = pltpu.roll(mirror.reshape(groups), PLANES, 1).reshape(block)
        blocks[j] = jnp.where(lane0, here + swapped, here)
        blocks[GX - j] = jnp.where(lane0, sign * (here - swapped), mirror)
    stacked = jnp.concatenate(
        [
            jnp.concatenate([b[u * 2 * PLANES : (u + 1) * 2 * PLANES] for b in blocks], axis=0)
            for u in range(units)
        ],
        axis=1,
    ).astype(jnp.bfloat16)
    v = dot(wx_ref[...], stacked).astype(jnp.bfloat16)
    rows = PLANES * GX
    cells = [
        jnp.concatenate([v[:rows, k : k + HALF], v[rows:, k : k + HALF]], axis=1)
        for k in range(0, units * HALF, HALF)
    ]
    maps = dot(jnp.concatenate(cells, axis=0), wy_ref[...])
    out_ref[0] = maps.reshape(zpart, GX, GY)


def synthesise(returned):
    _, pairs_here, slab_rows, _ = returned.shape
    zpart = slab_rows // 2
    tables = (inverse_x_table(), half_y_inverse())
    return pl.pallas_call(
        synthesise_kernel,
        grid=(pairs_here, slab_rows // (2 * zpart)),
        in_specs=[pl.BlockSpec((GX, 1, 2 * zpart, HALF), lambda i, z: (0, i, z, 0))]
        + [pl.BlockSpec(t.shape, lambda i, z: (0, 0)) for t in tables],
        out_specs=pl.BlockSpec((1, zpart, GX, GY), lambda i, z: (i, z, 0, 0)),
        out_shape=jax.ShapeDtypeStruct((pairs_here, slab_rows // 2, GX, GY), jnp.float32),
        compiler_params=pltpu.CompilerParams(vmem_limit_bytes=VMEM_BYTES),
        name="synthesise",
    )(returned, *(jnp.asarray(t) for t in tables))


def shards(band, pairs, extents):
    tiles, slabs = lax.axis_size("tile"), lax.axis_size("zslab")
    zrows = band.shape[2]
    if tiles * slabs != GX or zrows % (4 * PLANES) or pairs.shape[0] % (2 * tiles):
        return general_shards(band, pairs, extents)
    pairs, extents = pairs.T, extents.T
    tile = lax.axis_index("tile").astype(jnp.int32)
    device = lax.axis_index("zslab").astype(jnp.int32) * tiles + tile
    spectra = analyse(band, pairs, extents, tile[None])
    spread = lax.all_to_all(spectra, ("zslab", "tile"), split_axis=0, concat_axis=0, tiled=True)
    w = correlate(spread, pairs, device[None], slabs, band.shape[0])
    returned = lax.all_to_all(w, ("zslab", "tile"), split_axis=0, concat_axis=0, tiled=True)
    return synthesise(returned)


def solution(mesh):
    placed = (P("tile", None, "zslab", None, None), P(), P())
    return jax.shard_map(
        shards,
        mesh=mesh,
        in_specs=placed,
        out_specs=P("tile", "zslab", None, None),
        check_vma=False,
    )
```

```python
import functools
import math


import jax
import jax.numpy as jnp
import numpy as np
from jax import lax
from jax.experimental import pallas as pl
from jax.experimental.pallas import tpu as pltpu
from jax.sharding import PartitionSpec as P

GX = 32
GY = 256
GZ = 128
FACES = 4


def dft_tables(length):
    indices = jnp.arange(length, dtype=jnp.int32)
    modular = indices[:, None] * indices[None, :] % length
    angles = modular.astype(jnp.float32) * (2.0 * math.pi / length)
    factor = 1.0 / math.sqrt(length)
    return (
        (jnp.cos(angles) * factor).astype(jnp.bfloat16),
        (jnp.sin(angles) * factor).astype(jnp.bfloat16),
    )


def product(form, left, right):
    return jnp.einsum(form, left, right, preferred_element_type=jnp.float32)


def reduce_resolution(image_volume, crop_bounds):
    row_mask = (
        jnp.arange(image_volume.shape[2], dtype=jnp.int32)[None, :] < crop_bounds[:, 0:1]
    ).astype(jnp.bfloat16)
    col_mask = (
        jnp.arange(image_volume.shape[3], dtype=jnp.int32)[None, :] < crop_bounds[:, 1:2]
    ).astype(jnp.bfloat16)
    masked = image_volume * row_mask[:, None, :, None] * col_mask[:, None, None, :]
    raw_cols = jnp.arange(image_volume.shape[3], dtype=jnp.int32)
    pooled_cols = jnp.arange(GY, dtype=jnp.int32)
    pooling = jnp.where(raw_cols[:, None] // 2 == pooled_cols[None, :], 0.5, 0.0).astype(
        jnp.bfloat16
    )
    along_pooled = product("szxy,yk->szxk", masked, pooling)
    shaped = along_pooled.reshape(image_volume.shape[0], image_volume.shape[1], GX, 2, GY)
    return (shaped[:, :, :, 0, :] + shaped[:, :, :, 1, :]).astype(jnp.bfloat16)


def cross_phase(owner_re, owner_im, pairs, tiles_here):
    first_dev = pairs[:, 0] // tiles_here
    first_pos = pairs[:, 0] % tiles_here * FACES + pairs[:, 1]
    second_tile_device = pairs[:, 2] // tiles_here
    second_pos = pairs[:, 2] % tiles_here * FACES + pairs[:, 3]
    first_re = owner_re[first_dev, :, first_pos].astype(jnp.float32)
    first_im = owner_im[first_dev, :, first_pos].astype(jnp.float32)
    second_re = owner_re[second_tile_device, :, second_pos].astype(jnp.float32)
    second_im = owner_im[second_tile_device, :, second_pos].astype(jnp.float32)
    cross_re = first_re * second_re + first_im * second_im
    cross_im = first_im * second_re - first_re * second_im
    scaled = jnp.sqrt(cross_re * cross_re + cross_im * cross_im + 1.0)
    return ((cross_re / scaled).astype(jnp.bfloat16), (cross_im / scaled).astype(jnp.bfloat16))


def inverse_z(phase_real_part, phase_im, tables_z):
    w_re = (
        product("pmjk,mz->pzjk", phase_real_part, tables_z[0])
        - product("pmjk,mz->pzjk", phase_im, tables_z[1])
    ).astype(jnp.bfloat16)
    w_im = (
        product("pmjk,mz->pzjk", phase_im, tables_z[0])
        + product("pmjk,mz->pzjk", phase_real_part, tables_z[1])
    ).astype(jnp.bfloat16)
    return (w_re, w_im)


def inverse_x(w_re, w_im, tables_x):
    v_re = (
        product("pzjk,jx->pzxk", w_re, tables_x[0]) - product("pzjk,jx->pzxk", w_im, tables_x[1])
    ).astype(jnp.bfloat16)
    v_im = (
        product("pzjk,jx->pzxk", w_im, tables_x[0]) + product("pzjk,jx->pzxk", w_re, tables_x[1])
    ).astype(jnp.bfloat16)
    return (v_re, v_im)


def general_shards(band, pairs, extents):
    tables_x = dft_tables(GX)
    tables_y = dft_tables(GY)
    tables_z = dft_tables(GZ)
    tiles_here = band.shape[0]
    slots = tiles_here * FACES
    zrows = band.shape[2]
    tile_pos = lax.axis_index("tile")
    global_slot = tile_pos * slots + jnp.arange(slots, dtype=jnp.int32)
    first_slot = pairs[:, 0] * FACES + pairs[:, 1]
    second_slot = pairs[:, 2] * FACES + pairs[:, 3]
    matches = (
        (first_slot[None, :] == global_slot[:, None])
        | (second_slot[None, :] == global_slot[:, None])
    ).astype(jnp.int32)
    crop_bounds = jnp.sum(matches[:, :, None] * extents[None, :, :], axis=1)
    image_volume = band.reshape(slots, zrows, 2 * GX, 2 * GY)
    reduced_volume = reduce_resolution(image_volume, crop_bounds)
    y_re = product("szxy,yk->szxk", reduced_volume, tables_y[0]).astype(jnp.bfloat16)
    y_im = (-product("szxy,yk->szxk", reduced_volume, tables_y[1])).astype(jnp.bfloat16)
    x_re = (
        product("szxk,xj->szjk", y_re, tables_x[0]) + product("szxk,xj->szjk", y_im, tables_x[1])
    ).astype(jnp.bfloat16)
    x_im = (
        product("szxk,xj->szjk", y_im, tables_x[0]) - product("szxk,xj->szjk", y_re, tables_x[1])
    ).astype(jnp.bfloat16)
    kx_part = GX // lax.axis_size("zslab")
    re_in = lax.all_to_all(x_re, "zslab", split_axis=2, concat_axis=1, tiled=True)
    im_in = lax.all_to_all(x_im, "zslab", split_axis=2, concat_axis=1, tiled=True)
    out_re = (
        product("szjk,zm->msjk", re_in, tables_z[0]) + product("szjk,zm->msjk", im_in, tables_z[1])
    ).astype(jnp.bfloat16)
    out_im = (
        product("szjk,zm->msjk", im_in, tables_z[0]) - product("szjk,zm->msjk", re_in, tables_z[1])
    ).astype(jnp.bfloat16)
    tile_count = lax.axis_size("tile")
    kz_part = GZ // tile_count
    spectra = (
        lax.all_to_all(out_re, "tile", split_axis=0, concat_axis=0, tiled=True),
        lax.all_to_all(out_im, "tile", split_axis=0, concat_axis=0, tiled=True),
    )
    owner_re = spectra[0].reshape(tile_count, kz_part, slots, kx_part, GY)
    owner_im = spectra[1].reshape(tile_count, kz_part, slots, kx_part, GY)
    phase_real_part, phase_im = cross_phase(owner_re, owner_im, pairs, tiles_here)
    returned = (
        lax.all_to_all(phase_real_part, "tile", split_axis=0, concat_axis=1, tiled=True),
        lax.all_to_all(phase_im, "tile", split_axis=0, concat_axis=1, tiled=True),
    )
    w_re, w_im = inverse_z(returned[0], returned[1], tables_z)
    v_re, v_im = inverse_x(
        lax.all_to_all(w_re, "zslab", split_axis=1, concat_axis=2, tiled=True),
        lax.all_to_all(w_im, "zslab", split_axis=1, concat_axis=2, tiled=True),
        tables_x,
    )
    return product("pzxk,ky->pzxy", v_re, tables_y[0]) - product("pzxk,ky->pzxy", v_im, tables_y[1])


HALF = GY // 2
PLANES = 4
VMEM_BYTES = 32 * 1024 * 1024


def host_tables(length):
    indices = np.arange(length, dtype=np.int32)
    modular = indices[:, None] * indices[None, :] % length
    angles = modular.astype(np.float32) * np.float32(2.0 * math.pi / length)
    factor = np.float32(1.0 / math.sqrt(length))
    return (
        (np.cos(angles) * factor).astype(jnp.bfloat16),
        (np.sin(angles) * factor).astype(jnp.bfloat16),
    )


def half_y_table():
    cosine, sine = host_tables(GY)
    imag = -sine[:, :HALF]
    imag[:, 0] = cosine[:, HALF]
    return np.concatenate([cosine[:, :HALF], imag], axis=1)


def paired_y_table():
    table = np.zeros((2 * GY, GY), jnp.bfloat16)
    table[::2] = half_y_table() * np.array(0.5, jnp.bfloat16)
    return table


def half_y_inverse():
    cosine, sine = host_tables(GY)
    two = np.array(2.0, jnp.bfloat16)
    real = cosine[:HALF, :] * two
    real[0] = cosine[0]
    imag = -sine[:HALF, :] * two
    imag[0] = cosine[HALF]
    return np.concatenate([real, imag], axis=0)


def mirror_order():
    order = [0, GX // 2]
    for j in range(1, GX // 2):
        order += [j, GX - j]
    return order


def complex_blocks(length, sign):
    cosine, sine = (table.astype(np.float32) for table in host_tables(length))
    return np.array([[cosine, -sign * sine], [sign * sine, cosine]])


def forward_x_table():
    table = np.einsum("oijx,az->joaizx", complex_blocks(GX, -1), np.eye(PLANES))[mirror_order()]
    table = table.reshape(2 * GX * PLANES, 2, PLANES, GX)
    woven = table[:, :, :2].transpose(0, 1, 3, 2).reshape(-1, 2, 2 * GX)
    plain = table[:, :, 2:].reshape(-1, 2, (PLANES - 2) * GX)
    table = np.concatenate([woven, plain], axis=2)
    return table.reshape(2 * GX * PLANES, -1).astype(jnp.bfloat16)


def inverse_x_table():
    table = np.einsum("oijx,az->oaxjiz", complex_blocks(GX, 1), np.eye(PLANES))
    return table.reshape(2 * PLANES * GX, -1).astype(jnp.bfloat16)


def z_rows():
    return np.arange(2 * GZ).reshape(2, GZ // PLANES, PLANES).transpose(1, 0, 2).reshape(-1)


def z_tables():
    forward, inverse = (
        complex_blocks(GZ, sign).transpose(0, 2, 1, 3).reshape(2 * GZ, 2 * GZ) for sign in (-1, 1)
    )
    none = np.zeros((2 * GZ, GZ), np.float32)
    forward_last = np.concatenate([none, forward[:, :GZ]], axis=1)
    inverse_last = np.concatenate([none.T, inverse[:GZ]], axis=0)
    order = z_rows()
    return [
        np.ascontiguousarray(table).astype(jnp.bfloat16)
        for table in (
            forward[:, order],
            inverse[order],
            forward_last[:, order],
            inverse_last[order],
        )
    ]


def imaginary_rows(shape):
    return lax.broadcasted_iota(jnp.int32, shape, 0) % (2 * PLANES) >= PLANES


def first_lane(shape):
    return lax.broadcasted_iota(jnp.int32, shape, 1) == 0


def dot(left, right):
    return jnp.dot(left, right, preferred_element_type=jnp.float32)


def analyse_kernel(
    slots, pairs_ref, extents_ref, tile_ref, *rest
):
    band_refs, (wy_ref, wx_ref, out_ref, crop_ref) = rest[:-4], rest[-4:]
    slot = pl.program_id(0)

    @pl.when(slot == 0)
    def _():
        for p in range(pairs_ref.shape[1]):
            for end in (0, 1):
                named = pairs_ref[2 * end, p] * FACES + pairs_ref[2 * end + 1, p] - tile_ref[0] * slots

                @pl.when((named >= 0) & (named < slots))
                def _():
                    crop_ref[named, 0] = extents_ref[0, p]
                    crop_ref[named, 1] = extents_ref[1, p]

    across, along = crop_ref[slot, 0], crop_ref[slot, 1]

    def live(k, rows):
        lane = lax.broadcasted_iota(jnp.int32, rows.shape, 1)
        return jnp.where((rows < across) & (k * 128 + lane < along), 1.0, 0.0)

    def halves(rows):
        return (rows + pltpu.roll(rows, 127, 1)).astype(jnp.bfloat16)

    raw_row = lax.broadcasted_iota(jnp.int32, (2 * GX, 128), 0)
    pooled_row = lax.broadcasted_iota(jnp.int32, (GX, 128), 0)
    even = raw_row % 2 == 0
    groups = (2 * GX // 8, 8, 128)
    lives = [
        (live(k, raw_row), live(k, 2 * pooled_row), live(k, 2 * pooled_row + 1))
        for k in range(len(band_refs))
    ]
    block = (2 * PLANES, HALF)
    lane0, imaginary = first_lane(block), imaginary_rows(block)
    sign = jnp.where(imaginary, -0.5, 0.5)

    def row_pairs(ref, z, mask, shift):
        raw = ref[0, 0, z].astype(jnp.float32) * mask
        return raw + pltpu.roll(raw.reshape(groups), shift, 1).reshape(raw.shape)

    def woven(z):
        return [
            halves(jnp.where(even, row_pairs(ref, z, mask, 7), row_pairs(ref, z + 1, mask, 1)))
            for ref, (mask, _, _) in zip(band_refs, lives)
        ]

    def plain(z):
        parts = []
        for ref, (_, *masks) in zip(band_refs, lives):
            rows = [ref[0, 0, z, pl.ds(a, GX, stride=2), :].astype(jnp.float32) for a in (0, 1)]
            parts.append(halves(rows[0] * masks[0] + rows[1] * masks[1]))
        return parts

    def pool(z):
        return [
            jnp.concatenate(parts, axis=1)
            for parts in (woven(z), *(plain(z + k) for k in range(2, PLANES)))
        ]

    zpart = 4 * PLANES
    zrows = band_refs[0].shape[2]
    planes = sum((pool(z) for z in range(0, zrows, PLANES)), [])
    y = dot(jnp.concatenate(planes, axis=0), wy_ref[...]).astype(jnp.bfloat16)
    y = y.reshape(zrows // PLANES, PLANES * GX, GY)

    def store(start, spectra):
        def at(n):
            rows = spectra[2 * PLANES * n : 2 * PLANES * (n + 1)]
            return [rows[:, k : k + HALF] for k in range(0, rows.shape[1], HALF)]

        def put(j, blocks):
            rows = slice(2 * start, 2 * (start + zpart))
            out_ref[j, 0, rows] = jnp.concatenate(blocks, axis=0).astype(jnp.bfloat16)

        put(0, at(0))
        put(GX // 2, at(1))
        for j in range(1, GX // 2):
            here, mirror = at(2 * j), at(2 * j + 1)
            put(j, [jnp.where(lane0, 0.5 * a + sign * b, a) for a, b in zip(here, mirror)])
            put(
                GX - j,
                [
                    jnp.where(lane0, pltpu.roll(0.5 * a - sign * b, PLANES, 0), b)
                    for a, b in zip(here, mirror)
                ],
            )

    for start in range(0, zrows, zpart):
        units = [
            jnp.concatenate([y[unit, :, :HALF], y[unit, :, HALF:]], axis=0)
            for unit in range(start // PLANES, (start + zpart) // PLANES)
        ]
        store(start, dot(wx_ref[...], jnp.concatenate(units, axis=1)))


def analyse(band, pairs, extents, tile):
    slots, zrows = band.shape[0] * FACES, band.shape[2]
    tables = (paired_y_table(), forward_x_table())
    whole = [pl.BlockSpec(t.shape, lambda i, *_: (0, 0)) for t in tables]
    lane_blocks = 2 * GY // 128
    return pl.pallas_call(
        functools.partial(analyse_kernel, slots),
        grid_spec=pltpu.PrefetchScalarGridSpec(
            num_scalar_prefetch=3,
            grid=(slots,),
            in_specs=[
                pl.BlockSpec(
                    (1, 1, zrows, 2 * GX, 128),
                    lambda i, *_, k=k: (i // FACES, i % FACES, 0, 0, k),
                )
                for k in range(lane_blocks)
            ]
            + whole,
            out_specs=pl.BlockSpec((GX, 1, 2 * zrows, HALF), lambda i, *_: (0, i, 0, 0)),
            scratch_shapes=[pltpu.SMEM((slots, 2), jnp.int32)],
        ),
        out_shape=jax.ShapeDtypeStruct((GX, slots, 2 * zrows, HALF), jnp.bfloat16),
        compiler_params=pltpu.CompilerParams(vmem_limit_bytes=VMEM_BYTES + VMEM_BYTES * 3 // 4),
        name="analyse",
    )(pairs, extents, tile, *[band] * lane_blocks, *(jnp.asarray(t) for t in tables))


def normalised(a_re, a_im, b_re, b_im):
    cross_re = a_re * b_re + a_im * b_im
    cross_im = a_im * b_re - a_re * b_im
    scale = lax.rsqrt(cross_re * cross_re + cross_im * cross_im + 1.0)
    return (cross_re * scale).astype(jnp.bfloat16), (cross_im * scale).astype(jnp.bfloat16)


def correlate_kernel(
    slabs, tiles_here, pairs_ref, place_ref, in_ref, wz_ref, wzi_ref, wz_last_ref, wzi_last_ref, out_ref
):
    tiles = in_ref.shape[0] // slabs
    total = pairs_ref.shape[1]
    pairs_here = out_ref.shape[1]
    slab_rows = out_ref.shape[2]
    both_real = (place_ref[0] == 0) | (place_ref[0] == GX // 2)
    block = (2 * GZ, HALF)
    shared = first_lane(block) & imaginary_rows(block)

    def load(p, end):
        tile = pairs_ref[2 * end, p]
        row = tile // tiles_here
        pos = tile % tiles_here * FACES + pairs_ref[2 * end + 1, p]
        return jnp.concatenate([in_ref[row + s * tiles, pos] for s in range(slabs)], axis=0)

    def phase_of(table_ref, ends):
        spec = dot(table_ref[...], jnp.concatenate(ends, axis=1))
        spec = spec.astype(jnp.bfloat16).astype(jnp.float32)
        parts = [spec[:GZ], spec[GZ:]]
        phases = []
        for k in range(0, spec.shape[1], 2 * HALF):
            a, b = slice(k, k + HALF), slice(k + HALF, k + 2 * HALF)
            phase = normalised(parts[0][:, a], parts[1][:, a], parts[0][:, b], parts[1][:, b])
            phases.append(jnp.concatenate(phase, axis=0))
        return jnp.concatenate(phases, axis=1)

    keep = jnp.where(shared & both_real, 0.0, 1.0).astype(jnp.bfloat16)
    group = 4
    for p in range(0, total, group):
        ends = [load(q, end) * keep for q in range(p, p + group) for end in (0, 1)]
        w = dot(wzi_ref[...], phase_of(wz_ref, ends)).astype(jnp.bfloat16)
        for k, q in enumerate(range(p, p + group)):
            for s in range(slabs):
                out_ref[q // pairs_here + s * tiles, q % pairs_here] = w[
                    s * slab_rows : (s + 1) * slab_rows, k * HALF : (k + 1) * HALF
                ]

    @pl.when(both_real)
    def _():
        lane = lax.broadcasted_iota(jnp.int32, block, 1)
        ends = [jnp.zeros(block, jnp.bfloat16)] * 2
        for p in range(total):
            for end in (0, 1):
                ends[end] = jnp.where(lane == p, load(p, end)[:, 0:1], ends[end])
        w = dot(wzi_last_ref[...], phase_of(wz_last_ref, ends)).astype(jnp.bfloat16)
        for p in range(total):
            column = w[:, p : p + 1]
            for s in range(slabs):
                rows = slice(s * slab_rows, (s + 1) * slab_rows)
                at = (p // pairs_here + s * tiles, p % pairs_here)
                out_ref[at] = jnp.where(shared[rows], column[rows], out_ref[at])


def correlate(spread, pairs, place, slabs, tiles_here):
    devices, _, slab_rows, _ = spread.shape
    pairs_here = pairs.shape[1] * slabs // devices
    tables = z_tables()
    vmem = pl.BlockSpec(memory_space=pltpu.VMEM)
    smem = pl.BlockSpec(memory_space=pltpu.SMEM)
    return pl.pallas_call(
        functools.partial(correlate_kernel, slabs, tiles_here),
        in_specs=[smem, smem] + [vmem] * (1 + len(tables)),
        out_specs=vmem,
        out_shape=jax.ShapeDtypeStruct((devices, pairs_here, slab_rows, HALF), jnp.bfloat16),
        compiler_params=pltpu.CompilerParams(vmem_limit_bytes=VMEM_BYTES),
        name="correlate",
    )(pairs, place, spread, *(jnp.asarray(t) for t in tables))


def synthesise_kernel(in_ref, wx_ref, wy_ref, out_ref):
    zpart = out_ref.shape[1]
    units = zpart // PLANES
    block = (2 * zpart, HALF)
    lane0, imaginary = first_lane(block), imaginary_rows(block)
    sign = jnp.where(imaginary, -1.0, 1.0)
    groups = (units, 2 * PLANES, HALF)

    def at(j):
        return in_ref[j, 0].astype(jnp.float32)

    blocks = [None] * GX
    for j in (0, GX // 2):
        blocks[j] = at(j)
    for j in range(1, GX // 2):
        here, mirror = at(j), at(GX - j)
        swapped = pltpu.roll(mirror.reshape(groups), PLANES, 1).reshape(block)
        blocks[j] = jnp.where(lane0, here + swapped, here)
        blocks[GX - j] = jnp.where(lane0, sign * (here - swapped), mirror)
    stacked = jnp.concatenate(
        [
            jnp.concatenate([b[u * 2 * PLANES : (u + 1) * 2 * PLANES] for b in blocks], axis=0)
            for u in range(units)
        ],
        axis=1,
    ).astype(jnp.bfloat16)
    v = dot(wx_ref[...], stacked).astype(jnp.bfloat16)
    rows = PLANES * GX
    cells = [
        jnp.concatenate([v[:rows, k : k + HALF], v[rows:, k : k + HALF]], axis=1)
        for k in range(0, units * HALF, HALF)
    ]
    maps = dot(jnp.concatenate(cells, axis=0), wy_ref[...])
    out_ref[0] = maps.reshape(zpart, GX, GY)


def synthesise(returned):
    _, pairs_here, slab_rows, _ = returned.shape
    zpart = slab_rows // 2
    tables = (inverse_x_table(), half_y_inverse())
    return pl.pallas_call(
        synthesise_kernel,
        grid=(pairs_here, slab_rows // (2 * zpart)),
        in_specs=[pl.BlockSpec((GX, 1, 2 * zpart, HALF), lambda i, z: (0, i, z, 0))]
        + [pl.BlockSpec(t.shape, lambda i, z: (0, 0)) for t in tables],
        out_specs=pl.BlockSpec((1, zpart, GX, GY), lambda i, z: (i, z, 0, 0)),
        out_shape=jax.ShapeDtypeStruct((pairs_here, slab_rows // 2, GX, GY), jnp.float32),
        compiler_params=pltpu.CompilerParams(vmem_limit_bytes=VMEM_BYTES),
        name="synthesise",
    )(returned, *(jnp.asarray(t) for t in tables))


def shards(band, pairs, extents):
    tiles, slabs = lax.axis_size("tile"), lax.axis_size("zslab")
    zrows = band.shape[2]
    if tiles * slabs != GX or zrows % (4 * PLANES) or pairs.shape[0] % 4 or pairs.shape[0] % tiles:
        return general_shards(band, pairs, extents)
    pairs, extents = pairs.T, extents.T
    tile = lax.axis_index("tile").astype(jnp.int32)
    device = lax.axis_index("zslab").astype(jnp.int32) * tiles + tile
    spectra = analyse(band, pairs, extents, tile[None])
    spread = lax.all_to_all(spectra, ("zslab", "tile"), split_axis=0, concat_axis=0, tiled=True)
    w = correlate(spread, pairs, device[None], slabs, band.shape[0])
    returned = lax.all_to_all(w, ("zslab", "tile"), split_axis=0, concat_axis=0, tiled=True)
    return synthesise(returned)


def solution(mesh):
    placed = (P("tile", None, "zslab", None, None), P(), P())
    return jax.shard_map(
        shards,
        mesh=mesh,
        in_specs=placed,
        out_specs=P("tile", "zslab", None, None),
        check_vma=False,
    )
```

```python
import functools
import math


import jax
import jax.numpy as jnp
import numpy as np
from jax import lax
from jax.experimental import pallas as pl
from jax.experimental.pallas import tpu as pltpu
from jax.sharding import PartitionSpec as P

GX = 32
GY = 256
GZ = 128
FACES = 4


def dft_tables(length):
    indices = jnp.arange(length, dtype=jnp.int32)
    modular = indices[:, None] * indices[None, :] % length
    angles = modular.astype(jnp.float32) * (2.0 * math.pi / length)
    factor = 1.0 / math.sqrt(length)
    return (
        (jnp.cos(angles) * factor).astype(jnp.bfloat16),
        (jnp.sin(angles) * factor).astype(jnp.bfloat16),
    )


def product(form, left, right):
    return jnp.einsum(form, left, right, preferred_element_type=jnp.float32)


def reduce_resolution(image_volume, crop_bounds):
    row_mask = (
        jnp.arange(image_volume.shape[2], dtype=jnp.int32)[None, :] < crop_bounds[:, 0:1]
    ).astype(jnp.bfloat16)
    col_mask = (
        jnp.arange(image_volume.shape[3], dtype=jnp.int32)[None, :] < crop_bounds[:, 1:2]
    ).astype(jnp.bfloat16)
    masked = image_volume * row_mask[:, None, :, None] * col_mask[:, None, None, :]
    raw_cols = jnp.arange(image_volume.shape[3], dtype=jnp.int32)
    pooled_cols = jnp.arange(GY, dtype=jnp.int32)
    pooling = jnp.where(raw_cols[:, None] // 2 == pooled_cols[None, :], 0.5, 0.0).astype(
        jnp.bfloat16
    )
    along_pooled = product("szxy,yk->szxk", masked, pooling)
    shaped = along_pooled.reshape(image_volume.shape[0], image_volume.shape[1], GX, 2, GY)
    return (shaped[:, :, :, 0, :] + shaped[:, :, :, 1, :]).astype(jnp.bfloat16)


def cross_phase(owner_re, owner_im, pairs, tiles_here):
    first_dev = pairs[:, 0] // tiles_here
    first_pos = pairs[:, 0] % tiles_here * FACES + pairs[:, 1]
    second_tile_device = pairs[:, 2] // tiles_here
    second_pos = pairs[:, 2] % tiles_here * FACES + pairs[:, 3]
    first_re = owner_re[first_dev, :, first_pos].astype(jnp.float32)
    first_im = owner_im[first_dev, :, first_pos].astype(jnp.float32)
    second_re = owner_re[second_tile_device, :, second_pos].astype(jnp.float32)
    second_im = owner_im[second_tile_device, :, second_pos].astype(jnp.float32)
    cross_re = first_re * second_re + first_im * second_im
    cross_im = first_im * second_re - first_re * second_im
    scaled = jnp.sqrt(cross_re * cross_re + cross_im * cross_im + 1.0)
    return ((cross_re / scaled).astype(jnp.bfloat16), (cross_im / scaled).astype(jnp.bfloat16))


def inverse_z(phase_real_part, phase_im, tables_z):
    w_re = (
        product("pmjk,mz->pzjk", phase_real_part, tables_z[0])
        - product("pmjk,mz->pzjk", phase_im, tables_z[1])
    ).astype(jnp.bfloat16)
    w_im = (
        product("pmjk,mz->pzjk", phase_im, tables_z[0])
        + product("pmjk,mz->pzjk", phase_real_part, tables_z[1])
    ).astype(jnp.bfloat16)
    return (w_re, w_im)


def inverse_x(w_re, w_im, tables_x):
    v_re = (
        product("pzjk,jx->pzxk", w_re, tables_x[0]) - product("pzjk,jx->pzxk", w_im, tables_x[1])
    ).astype(jnp.bfloat16)
    v_im = (
        product("pzjk,jx->pzxk", w_im, tables_x[0]) + product("pzjk,jx->pzxk", w_re, tables_x[1])
    ).astype(jnp.bfloat16)
    return (v_re, v_im)


def general_shards(band, pairs, extents):
    tables_x = dft_tables(GX)
    tables_y = dft_tables(GY)
    tables_z = dft_tables(GZ)
    tiles_here = band.shape[0]
    slots = tiles_here * FACES
    zrows = band.shape[2]
    tile_pos = lax.axis_index("tile")
    global_slot = tile_pos * slots + jnp.arange(slots, dtype=jnp.int32)
    first_slot = pairs[:, 0] * FACES + pairs[:, 1]
    second_slot = pairs[:, 2] * FACES + pairs[:, 3]
    matches = (
        (first_slot[None, :] == global_slot[:, None])
        | (second_slot[None, :] == global_slot[:, None])
    ).astype(jnp.int32)
    crop_bounds = jnp.sum(matches[:, :, None] * extents[None, :, :], axis=1)
    image_volume = band.reshape(slots, zrows, 2 * GX, 2 * GY)
    reduced_volume = reduce_resolution(image_volume, crop_bounds)
    y_re = product("szxy,yk->szxk", reduced_volume, tables_y[0]).astype(jnp.bfloat16)
    y_im = (-product("szxy,yk->szxk", reduced_volume, tables_y[1])).astype(jnp.bfloat16)
    x_re = (
        product("szxk,xj->szjk", y_re, tables_x[0]) + product("szxk,xj->szjk", y_im, tables_x[1])
    ).astype(jnp.bfloat16)
    x_im = (
        product("szxk,xj->szjk", y_im, tables_x[0]) - product("szxk,xj->szjk", y_re, tables_x[1])
    ).astype(jnp.bfloat16)
    kx_part = GX // lax.axis_size("zslab")
    re_in = lax.all_to_all(x_re, "zslab", split_axis=2, concat_axis=1, tiled=True)
    im_in = lax.all_to_all(x_im, "zslab", split_axis=2, concat_axis=1, tiled=True)
    out_re = (
        product("szjk,zm->msjk", re_in, tables_z[0]) + product("szjk,zm->msjk", im_in, tables_z[1])
    ).astype(jnp.bfloat16)
    out_im = (
        product("szjk,zm->msjk", im_in, tables_z[0]) - product("szjk,zm->msjk", re_in, tables_z[1])
    ).astype(jnp.bfloat16)
    tile_count = lax.axis_size("tile")
    kz_part = GZ // tile_count
    spectra = (
        lax.all_to_all(out_re, "tile", split_axis=0, concat_axis=0, tiled=True),
        lax.all_to_all(out_im, "tile", split_axis=0, concat_axis=0, tiled=True),
    )
    owner_re = spectra[0].reshape(tile_count, kz_part, slots, kx_part, GY)
    owner_im = spectra[1].reshape(tile_count, kz_part, slots, kx_part, GY)
    phase_real_part, phase_im = cross_phase(owner_re, owner_im, pairs, tiles_here)
    returned = (
        lax.all_to_all(phase_real_part, "tile", split_axis=0, concat_axis=1, tiled=True),
        lax.all_to_all(phase_im, "tile", split_axis=0, concat_axis=1, tiled=True),
    )
    w_re, w_im = inverse_z(returned[0], returned[1], tables_z)
    v_re, v_im = inverse_x(
        lax.all_to_all(w_re, "zslab", split_axis=1, concat_axis=2, tiled=True),
        lax.all_to_all(w_im, "zslab", split_axis=1, concat_axis=2, tiled=True),
        tables_x,
    )
    return product("pzxk,ky->pzxy", v_re, tables_y[0]) - product("pzxk,ky->pzxy", v_im, tables_y[1])


HALF = GY // 2
PLANES = 4
VMEM_BYTES = 32 * 1024 * 1024


def host_tables(length):
    indices = np.arange(length, dtype=np.int32)
    modular = indices[:, None] * indices[None, :] % length
    angles = modular.astype(np.float32) * np.float32(2.0 * math.pi / length)
    factor = np.float32(1.0 / math.sqrt(length))
    return (
        (np.cos(angles) * factor).astype(jnp.bfloat16),
        (np.sin(angles) * factor).astype(jnp.bfloat16),
    )


def half_y_table():
    cosine, sine = host_tables(GY)
    imag = -sine[:, :HALF]
    imag[:, 0] = cosine[:, HALF]
    return np.concatenate([cosine[:, :HALF], imag], axis=1)


def paired_y_table():
    half = half_y_table() * np.array(0.5, jnp.bfloat16)
    table = np.zeros((2 * GY, 2 * GY), jnp.bfloat16)
    table[::2, :GY] = half
    table[1::2, GY:] = half
    return table


def half_y_inverse():
    cosine, sine = host_tables(GY)
    two = np.array(2.0, jnp.bfloat16)
    real = cosine[:HALF, :] * two
    real[0] = cosine[0]
    imag = -sine[:HALF, :] * two
    imag[0] = cosine[HALF]
    return np.concatenate([real, imag], axis=0)


def mirror_order():
    order = [0, GX // 2]
    for j in range(1, GX // 2):
        order += [j, GX - j]
    return order


def complex_blocks(length, sign):
    cosine, sine = (table.astype(np.float32) for table in host_tables(length))
    return np.array([[cosine, -sign * sine], [sign * sine, cosine]])


def forward_x_table():
    table = np.einsum("oijx,az->joaizx", complex_blocks(GX, -1), np.eye(PLANES))[mirror_order()]
    table = table.reshape(2 * GX * PLANES, 2, PLANES, GX)
    woven = table[:, :, :2].transpose(0, 1, 3, 2).reshape(-1, 2, 2 * GX)
    plain = table[:, :, 2:].reshape(-1, 2, (PLANES - 2) * GX)
    table = np.concatenate([woven, plain], axis=2)
    return table.reshape(2 * GX * PLANES, -1).astype(jnp.bfloat16)


def inverse_x_table():
    table = np.einsum("oijx,az->oaxjiz", complex_blocks(GX, 1), np.eye(PLANES))
    return table.reshape(2 * PLANES * GX, -1).astype(jnp.bfloat16)


def z_rows():
    return np.arange(2 * GZ).reshape(2, GZ // PLANES, PLANES).transpose(1, 0, 2).reshape(-1)


def z_tables():
    forward, inverse = (
        complex_blocks(GZ, sign).transpose(0, 2, 1, 3).reshape(2 * GZ, 2 * GZ) for sign in (-1, 1)
    )
    none = np.zeros((2 * GZ, GZ), np.float32)
    forward_last = np.concatenate([none, forward[:, :GZ]], axis=1)
    inverse_last = np.concatenate([none.T, inverse[:GZ]], axis=0)
    order = z_rows()
    return [
        np.ascontiguousarray(table).astype(jnp.bfloat16)
        for table in (
            forward[:, order],
            inverse[order],
            forward_last[:, order],
            inverse_last[order],
        )
    ]


def imaginary_rows(shape):
    return lax.broadcasted_iota(jnp.int32, shape, 0) % (2 * PLANES) >= PLANES


def first_lane(shape):
    return lax.broadcasted_iota(jnp.int32, shape, 1) == 0


def dot(left, right):
    return jnp.dot(left, right, preferred_element_type=jnp.float32)


def analyse_kernel(
    slots, pairs_ref, extents_ref, tile_ref, *rest
):
    band_refs, (wy_ref, wx_ref, out_ref, crop_ref) = rest[:-4], rest[-4:]
    slot = pl.program_id(0)

    @pl.when(slot == 0)
    def _():
        for p in range(pairs_ref.shape[1]):
            for end in (0, 1):
                named = pairs_ref[2 * end, p] * FACES + pairs_ref[2 * end + 1, p] - tile_ref[0] * slots

                @pl.when((named >= 0) & (named < slots))
                def _():
                    crop_ref[named, 0] = extents_ref[0, p]
                    crop_ref[named, 1] = extents_ref[1, p]

    across, along = crop_ref[slot, 0], crop_ref[slot, 1]

    def live(k, rows):
        lane = lax.broadcasted_iota(jnp.int32, rows.shape, 1)
        return jnp.where((rows < across) & (k * 128 + lane < along), 1.0, 0.0)

    def alternate(first, second):
        first = first + pltpu.roll(first, 127, 1)
        second = second + pltpu.roll(second, 1, 1)
        return jnp.where(even_lane, first, second).astype(jnp.bfloat16)

    raw_row = lax.broadcasted_iota(jnp.int32, (2 * GX, 128), 0)
    pooled_row = lax.broadcasted_iota(jnp.int32, (GX, 128), 0)
    even = raw_row % 2 == 0
    even_lane = lax.broadcasted_iota(jnp.int32, (2 * GX, 128), 1) % 2 == 0
    groups = (2 * GX // 8, 8, 128)
    lives = [
        (live(k, raw_row), live(k, 2 * pooled_row), live(k, 2 * pooled_row + 1))
        for k in range(len(band_refs))
    ]
    block = (2 * PLANES, HALF)
    lane0, imaginary = first_lane(block), imaginary_rows(block)
    sign = jnp.where(imaginary, -0.5, 0.5)

    def row_pairs(ref, z, mask, shift):
        raw = ref[0, 0, z].astype(jnp.float32) * mask
        return raw + pltpu.roll(raw.reshape(groups), shift, 1).reshape(raw.shape)

    def cells(z):
        blocks = []
        for ref, (mask, *masks) in zip(band_refs, lives):
            woven = jnp.where(even, row_pairs(ref, z, mask, 7), row_pairs(ref, z + 1, mask, 1))
            plain = []
            for plane in (z + 2, z + 3):
                rows = [
                    ref[0, 0, plane, pl.ds(a, GX, stride=2), :].astype(jnp.float32) for a in (0, 1)
                ]
                plain.append(rows[0] * masks[0] + rows[1] * masks[1])
            blocks.append(alternate(woven, jnp.concatenate(plain, axis=0)))
        return jnp.concatenate(blocks, axis=1)

    zrows = band_refs[0].shape[2]
    down = jnp.concatenate([cells(z) for z in range(0, zrows, PLANES)], axis=0)
    y = dot(down, wy_ref[...]).astype(jnp.bfloat16).reshape(zrows // PLANES, 2 * GX, 2 * GY)
    units = [
        jnp.concatenate([y[unit, :, k : k + HALF] for k in (0, GY, HALF, GY + HALF)], axis=0)
        for unit in range(zrows // PLANES)
    ]
    spectra = dot(wx_ref[...], jnp.concatenate(units, axis=1))

    def at(n):
        rows = spectra[2 * PLANES * n : 2 * PLANES * (n + 1)]
        return [rows[:, k : k + HALF] for k in range(0, rows.shape[1], HALF)]

    def put(j, blocks):
        out_ref[j, 0] = jnp.concatenate(blocks, axis=0).astype(jnp.bfloat16)

    put(0, at(0))
    put(GX // 2, at(1))
    for j in range(1, GX // 2):
        here, mirror = at(2 * j), at(2 * j + 1)
        put(j, [jnp.where(lane0, 0.5 * a + sign * b, a) for a, b in zip(here, mirror)])
        put(
            GX - j,
            [
                jnp.where(lane0, pltpu.roll(0.5 * a - sign * b, PLANES, 0), b)
                for a, b in zip(here, mirror)
            ],
        )


def analyse(band, pairs, extents, tile):
    slots, zrows = band.shape[0] * FACES, band.shape[2]
    tables = (paired_y_table(), forward_x_table())
    whole = [pl.BlockSpec(t.shape, lambda i, *_: (0, 0)) for t in tables]
    lane_blocks = 2 * GY // 128
    return pl.pallas_call(
        functools.partial(analyse_kernel, slots),
        grid_spec=pltpu.PrefetchScalarGridSpec(
            num_scalar_prefetch=3,
            grid=(slots,),
            in_specs=[
                pl.BlockSpec(
                    (1, 1, zrows, 2 * GX, 128),
                    lambda i, *_, k=k: (i // FACES, i % FACES, 0, 0, k),
                )
                for k in range(lane_blocks)
            ]
            + whole,
            out_specs=pl.BlockSpec((GX, 1, 2 * zrows, HALF), lambda i, *_: (0, i, 0, 0)),
            scratch_shapes=[pltpu.SMEM((slots, 2), jnp.int32)],
        ),
        out_shape=jax.ShapeDtypeStruct((GX, slots, 2 * zrows, HALF), jnp.bfloat16),
        compiler_params=pltpu.CompilerParams(vmem_limit_bytes=VMEM_BYTES + VMEM_BYTES * 3 // 4),
        name="analyse",
    )(pairs, extents, tile, *[band] * lane_blocks, *(jnp.asarray(t) for t in tables))


def normalised(a_re, a_im, b_re, b_im):
    cross_re = a_re * b_re + a_im * b_im
    cross_im = a_im * b_re - a_re * b_im
    scale = lax.rsqrt(cross_re * cross_re + cross_im * cross_im + 1.0)
    return (cross_re * scale).astype(jnp.bfloat16), (cross_im * scale).astype(jnp.bfloat16)


def correlate_kernel(
    slabs, tiles_here, pairs_ref, place_ref, in_ref, wz_ref, wzi_ref, wz_last_ref, wzi_last_ref, out_ref
):
    tiles = in_ref.shape[0] // slabs
    total = pairs_ref.shape[1]
    pairs_here = out_ref.shape[1]
    slab_rows = out_ref.shape[2]
    both_real = (place_ref[0] == 0) | (place_ref[0] == GX // 2)
    block = (2 * GZ, HALF)
    shared = first_lane(block) & imaginary_rows(block)

    def load(p, end):
        tile = pairs_ref[2 * end, p]
        row = tile // tiles_here
        pos = tile % tiles_here * FACES + pairs_ref[2 * end + 1, p]
        return jnp.concatenate([in_ref[row + s * tiles, pos] for s in range(slabs)], axis=0)

    def phase_of(table_ref, ends):
        spec = dot(table_ref[...], jnp.concatenate(ends, axis=1))
        spec = spec.astype(jnp.bfloat16).astype(jnp.float32)
        parts = [spec[:GZ], spec[GZ:]]
        phases = []
        for k in range(0, spec.shape[1], 2 * HALF):
            a, b = slice(k, k + HALF), slice(k + HALF, k + 2 * HALF)
            phase = normalised(parts[0][:, a], parts[1][:, a], parts[0][:, b], parts[1][:, b])
            phases.append(jnp.concatenate(phase, axis=0))
        return jnp.concatenate(phases, axis=1)

    keep = jnp.where(shared & both_real, 0.0, 1.0).astype(jnp.bfloat16)
    group = 8
    for p in range(0, total, group):
        ends = [load(q, end) * keep for q in range(p, p + group) for end in (0, 1)]
        w = dot(wzi_ref[...], phase_of(wz_ref, ends)).astype(jnp.bfloat16)
        for k, q in enumerate(range(p, p + group)):
            for s in range(slabs):
                out_ref[q // pairs_here + s * tiles, q % pairs_here] = w[
                    s * slab_rows : (s + 1) * slab_rows, k * HALF : (k + 1) * HALF
                ]

    @pl.when(both_real)
    def _():
        lane = lax.broadcasted_iota(jnp.int32, block, 1)
        ends = [jnp.zeros(block, jnp.bfloat16)] * 2
        for p in range(total):
            for end in (0, 1):
                ends[end] = jnp.where(lane == p, load(p, end)[:, 0:1], ends[end])
        w = dot(wzi_last_ref[...], phase_of(wz_last_ref, ends)).astype(jnp.bfloat16)
        for p in range(total):
            column = w[:, p : p + 1]
            for s in range(slabs):
                rows = slice(s * slab_rows, (s + 1) * slab_rows)
                at = (p // pairs_here + s * tiles, p % pairs_here)
                out_ref[at] = jnp.where(shared[rows], column[rows], out_ref[at])


def correlate(spread, pairs, place, slabs, tiles_here):
    devices, _, slab_rows, _ = spread.shape
    pairs_here = pairs.shape[1] * slabs // devices
    tables = z_tables()
    vmem = pl.BlockSpec(memory_space=pltpu.VMEM)
    smem = pl.BlockSpec(memory_space=pltpu.SMEM)
    return pl.pallas_call(
        functools.partial(correlate_kernel, slabs, tiles_here),
        in_specs=[smem, smem] + [vmem] * (1 + len(tables)),
        out_specs=vmem,
        out_shape=jax.ShapeDtypeStruct((devices, pairs_here, slab_rows, HALF), jnp.bfloat16),
        compiler_params=pltpu.CompilerParams(vmem_limit_bytes=VMEM_BYTES),
        name="correlate",
    )(pairs, place, spread, *(jnp.asarray(t) for t in tables))


def synthesise_kernel(in_ref, wx_ref, wy_ref, out_ref):
    zpart = out_ref.shape[1]
    units = zpart // PLANES
    block = (2 * zpart, HALF)
    lane0, imaginary = first_lane(block), imaginary_rows(block)
    sign = jnp.where(imaginary, -1.0, 1.0)
    groups = (units, 2 * PLANES, HALF)

    def at(j):
        return in_ref[j, 0].astype(jnp.float32)

    blocks = [None] * GX
    for j in (0, GX // 2):
        blocks[j] = at(j)
    for j in range(1, GX // 2):
        here, mirror = at(j), at(GX - j)
        swapped = pltpu.roll(mirror.reshape(groups), PLANES, 1).reshape(block)
        blocks[j] = jnp.where(lane0, here + swapped, here)
        blocks[GX - j] = jnp.where(lane0, sign * (here - swapped), mirror)
    stacked = jnp.concatenate(
        [
            jnp.concatenate([b[u * 2 * PLANES : (u + 1) * 2 * PLANES] for b in blocks], axis=0)
            for u in range(units)
        ],
        axis=1,
    ).astype(jnp.bfloat16)
    v = dot(wx_ref[...], stacked).astype(jnp.bfloat16)
    rows = PLANES * GX
    cells = [
        jnp.concatenate([v[:rows, k : k + HALF], v[rows:, k : k + HALF]], axis=1)
        for k in range(0, units * HALF, HALF)
    ]
    maps = dot(jnp.concatenate(cells, axis=0), wy_ref[...])
    out_ref[0] = maps.reshape(zpart, GX, GY)


def synthesise(returned):
    _, pairs_here, slab_rows, _ = returned.shape
    zpart = slab_rows // 2
    tables = (inverse_x_table(), half_y_inverse())
    return pl.pallas_call(
        synthesise_kernel,
        grid=(pairs_here, slab_rows // (2 * zpart)),
        in_specs=[pl.BlockSpec((GX, 1, 2 * zpart, HALF), lambda i, z: (0, i, z, 0))]
        + [pl.BlockSpec(t.shape, lambda i, z: (0, 0)) for t in tables],
        out_specs=pl.BlockSpec((1, zpart, GX, GY), lambda i, z: (i, z, 0, 0)),
        out_shape=jax.ShapeDtypeStruct((pairs_here, slab_rows // 2, GX, GY), jnp.float32),
        compiler_params=pltpu.CompilerParams(vmem_limit_bytes=VMEM_BYTES),
        name="synthesise",
    )(returned, *(jnp.asarray(t) for t in tables))


def shards(band, pairs, extents):
    tiles, slabs = lax.axis_size("tile"), lax.axis_size("zslab")
    zrows = band.shape[2]
    if tiles * slabs != GX or zrows % (4 * PLANES) or pairs.shape[0] % 8 or pairs.shape[0] % tiles:
        return general_shards(band, pairs, extents)
    pairs, extents = pairs.T, extents.T
    tile = lax.axis_index("tile").astype(jnp.int32)
    device = lax.axis_index("zslab").astype(jnp.int32) * tiles + tile
    spectra = analyse(band, pairs, extents, tile[None])
    spread = lax.all_to_all(spectra, ("zslab", "tile"), split_axis=0, concat_axis=0, tiled=True)
    w = correlate(spread, pairs, device[None], slabs, band.shape[0])
    returned = lax.all_to_all(w, ("zslab", "tile"), split_axis=0, concat_axis=0, tiled=True)
    return synthesise(returned)


def solution(mesh):
    placed = (P("tile", None, "zslab", None, None), P(), P())
    return jax.shard_map(
        shards,
        mesh=mesh,
        in_specs=placed,
        out_specs=P("tile", "zslab", None, None),
        check_vma=False,
    )
```

```python
import functools
import math


import jax
import jax.numpy as jnp
import numpy as np
from jax import lax
from jax.experimental import pallas as pl
from jax.experimental.pallas import tpu as pltpu
from jax.sharding import PartitionSpec as P

GX = 32
GY = 256
GZ = 128
FACES = 4


def dft_tables(length):
    indices = jnp.arange(length, dtype=jnp.int32)
    modular = indices[:, None] * indices[None, :] % length
    angles = modular.astype(jnp.float32) * (2.0 * math.pi / length)
    factor = 1.0 / math.sqrt(length)
    return (
        (jnp.cos(angles) * factor).astype(jnp.bfloat16),
        (jnp.sin(angles) * factor).astype(jnp.bfloat16),
    )


def product(form, left, right):
    return jnp.einsum(form, left, right, preferred_element_type=jnp.float32)


def reduce_resolution(image_volume, crop_bounds):
    row_mask = (
        jnp.arange(image_volume.shape[2], dtype=jnp.int32)[None, :] < crop_bounds[:, 0:1]
    ).astype(jnp.bfloat16)
    col_mask = (
        jnp.arange(image_volume.shape[3], dtype=jnp.int32)[None, :] < crop_bounds[:, 1:2]
    ).astype(jnp.bfloat16)
    masked = image_volume * row_mask[:, None, :, None] * col_mask[:, None, None, :]
    raw_cols = jnp.arange(image_volume.shape[3], dtype=jnp.int32)
    pooled_cols = jnp.arange(GY, dtype=jnp.int32)
    pooling = jnp.where(raw_cols[:, None] // 2 == pooled_cols[None, :], 0.5, 0.0).astype(
        jnp.bfloat16
    )
    along_pooled = product("szxy,yk->szxk", masked, pooling)
    shaped = along_pooled.reshape(image_volume.shape[0], image_volume.shape[1], GX, 2, GY)
    return (shaped[:, :, :, 0, :] + shaped[:, :, :, 1, :]).astype(jnp.bfloat16)


def cross_phase(owner_re, owner_im, pairs, tiles_here):
    first_dev = pairs[:, 0] // tiles_here
    first_pos = pairs[:, 0] % tiles_here * FACES + pairs[:, 1]
    second_tile_device = pairs[:, 2] // tiles_here
    second_pos = pairs[:, 2] % tiles_here * FACES + pairs[:, 3]
    first_re = owner_re[first_dev, :, first_pos].astype(jnp.float32)
    first_im = owner_im[first_dev, :, first_pos].astype(jnp.float32)
    second_re = owner_re[second_tile_device, :, second_pos].astype(jnp.float32)
    second_im = owner_im[second_tile_device, :, second_pos].astype(jnp.float32)
    cross_re = first_re * second_re + first_im * second_im
    cross_im = first_im * second_re - first_re * second_im
    scaled = jnp.sqrt(cross_re * cross_re + cross_im * cross_im + 1.0)
    return ((cross_re / scaled).astype(jnp.bfloat16), (cross_im / scaled).astype(jnp.bfloat16))


def inverse_z(phase_real_part, phase_im, tables_z):
    w_re = (
        product("pmjk,mz->pzjk", phase_real_part, tables_z[0])
        - product("pmjk,mz->pzjk", phase_im, tables_z[1])
    ).astype(jnp.bfloat16)
    w_im = (
        product("pmjk,mz->pzjk", phase_im, tables_z[0])
        + product("pmjk,mz->pzjk", phase_real_part, tables_z[1])
    ).astype(jnp.bfloat16)
    return (w_re, w_im)


def inverse_x(w_re, w_im, tables_x):
    v_re = (
        product("pzjk,jx->pzxk", w_re, tables_x[0]) - product("pzjk,jx->pzxk", w_im, tables_x[1])
    ).astype(jnp.bfloat16)
    v_im = (
        product("pzjk,jx->pzxk", w_im, tables_x[0]) + product("pzjk,jx->pzxk", w_re, tables_x[1])
    ).astype(jnp.bfloat16)
    return (v_re, v_im)


def general_shards(band, pairs, extents):
    tables_x = dft_tables(GX)
    tables_y = dft_tables(GY)
    tables_z = dft_tables(GZ)
    tiles_here = band.shape[0]
    slots = tiles_here * FACES
    zrows = band.shape[2]
    tile_pos = lax.axis_index("tile")
    global_slot = tile_pos * slots + jnp.arange(slots, dtype=jnp.int32)
    first_slot = pairs[:, 0] * FACES + pairs[:, 1]
    second_slot = pairs[:, 2] * FACES + pairs[:, 3]
    matches = (
        (first_slot[None, :] == global_slot[:, None])
        | (second_slot[None, :] == global_slot[:, None])
    ).astype(jnp.int32)
    crop_bounds = jnp.sum(matches[:, :, None] * extents[None, :, :], axis=1)
    image_volume = band.reshape(slots, zrows, 2 * GX, 2 * GY)
    reduced_volume = reduce_resolution(image_volume, crop_bounds)
    y_re = product("szxy,yk->szxk", reduced_volume, tables_y[0]).astype(jnp.bfloat16)
    y_im = (-product("szxy,yk->szxk", reduced_volume, tables_y[1])).astype(jnp.bfloat16)
    x_re = (
        product("szxk,xj->szjk", y_re, tables_x[0]) + product("szxk,xj->szjk", y_im, tables_x[1])
    ).astype(jnp.bfloat16)
    x_im = (
        product("szxk,xj->szjk", y_im, tables_x[0]) - product("szxk,xj->szjk", y_re, tables_x[1])
    ).astype(jnp.bfloat16)
    kx_part = GX // lax.axis_size("zslab")
    re_in = lax.all_to_all(x_re, "zslab", split_axis=2, concat_axis=1, tiled=True)
    im_in = lax.all_to_all(x_im, "zslab", split_axis=2, concat_axis=1, tiled=True)
    out_re = (
        product("szjk,zm->msjk", re_in, tables_z[0]) + product("szjk,zm->msjk", im_in, tables_z[1])
    ).astype(jnp.bfloat16)
    out_im = (
        product("szjk,zm->msjk", im_in, tables_z[0]) - product("szjk,zm->msjk", re_in, tables_z[1])
    ).astype(jnp.bfloat16)
    tile_count = lax.axis_size("tile")
    kz_part = GZ // tile_count
    spectra = (
        lax.all_to_all(out_re, "tile", split_axis=0, concat_axis=0, tiled=True),
        lax.all_to_all(out_im, "tile", split_axis=0, concat_axis=0, tiled=True),
    )
    owner_re = spectra[0].reshape(tile_count, kz_part, slots, kx_part, GY)
    owner_im = spectra[1].reshape(tile_count, kz_part, slots, kx_part, GY)
    phase_real_part, phase_im = cross_phase(owner_re, owner_im, pairs, tiles_here)
    returned = (
        lax.all_to_all(phase_real_part, "tile", split_axis=0, concat_axis=1, tiled=True),
        lax.all_to_all(phase_im, "tile", split_axis=0, concat_axis=1, tiled=True),
    )
    w_re, w_im = inverse_z(returned[0], returned[1], tables_z)
    v_re, v_im = inverse_x(
        lax.all_to_all(w_re, "zslab", split_axis=1, concat_axis=2, tiled=True),
        lax.all_to_all(w_im, "zslab", split_axis=1, concat_axis=2, tiled=True),
        tables_x,
    )
    return product("pzxk,ky->pzxy", v_re, tables_y[0]) - product("pzxk,ky->pzxy", v_im, tables_y[1])


HALF = GY // 2
PLANES = 4
VMEM_BYTES = 32 * 1024 * 1024


def host_tables(length):
    indices = np.arange(length, dtype=np.int32)
    modular = indices[:, None] * indices[None, :] % length
    angles = modular.astype(np.float32) * np.float32(2.0 * math.pi / length)
    factor = np.float32(1.0 / math.sqrt(length))
    return (
        (np.cos(angles) * factor).astype(jnp.bfloat16),
        (np.sin(angles) * factor).astype(jnp.bfloat16),
    )


def half_y_table():
    cosine, sine = host_tables(GY)
    imag = -sine[:, :HALF]
    imag[:, 0] = cosine[:, HALF]
    return np.concatenate([cosine[:, :HALF], imag], axis=1)


def paired_y_table():
    half = half_y_table() * np.array(0.5, jnp.bfloat16)
    table = np.zeros((2 * GY, 2 * GY), jnp.bfloat16)
    table[::2, :GY] = half
    table[1::2, GY:] = half
    return table


def half_y_inverse():
    cosine, sine = host_tables(GY)
    two = np.array(2.0, jnp.bfloat16)
    real = cosine[:HALF, :] * two
    real[0] = cosine[0]
    imag = -sine[:HALF, :] * two
    imag[0] = cosine[HALF]
    return np.concatenate([real, imag], axis=0)


def mirror_order():
    order = [0, GX // 2]
    for j in range(1, GX // 2):
        order += [j, GX - j]
    return order


def complex_blocks(length, sign):
    cosine, sine = (table.astype(np.float32) for table in host_tables(length))
    return np.array([[cosine, -sign * sine], [sign * sine, cosine]])


def forward_x_table():
    table = np.einsum("oijx,az->joaizx", complex_blocks(GX, -1), np.eye(PLANES))[mirror_order()]
    table = table.reshape(2 * GX * PLANES, 2, PLANES // 2, 2, GX).transpose(0, 1, 2, 4, 3)
    return table.reshape(2 * GX * PLANES, -1).astype(jnp.bfloat16)


def inverse_x_table():
    table = np.einsum("oijx,az->oaxjiz", complex_blocks(GX, 1), np.eye(PLANES))
    return table.reshape(2 * PLANES * GX, -1).astype(jnp.bfloat16)


def z_rows():
    return np.arange(2 * GZ).reshape(2, GZ // PLANES, PLANES).transpose(1, 0, 2).reshape(-1)


def z_tables():
    forward, inverse = (
        complex_blocks(GZ, sign).transpose(0, 2, 1, 3).reshape(2 * GZ, 2 * GZ) for sign in (-1, 1)
    )
    none = np.zeros((2 * GZ, GZ), np.float32)
    forward_last = np.concatenate([none, forward[:, :GZ]], axis=1)
    inverse_last = np.concatenate([none.T, inverse[:GZ]], axis=0)
    order = z_rows()
    return [
        np.ascontiguousarray(table).astype(jnp.bfloat16)
        for table in (
            forward[:, order],
            inverse[order],
            forward_last[:, order],
            inverse_last[order],
        )
    ]


def imaginary_rows(shape):
    return lax.broadcasted_iota(jnp.int32, shape, 0) % (2 * PLANES) >= PLANES


def first_lane(shape):
    return lax.broadcasted_iota(jnp.int32, shape, 1) == 0


def dot(left, right):
    return jnp.dot(left, right, preferred_element_type=jnp.float32)


def analyse_kernel(
    slots, pairs_ref, extents_ref, tile_ref, band_ref, wy_ref, wx_ref, out_ref, crop_ref
):
    slot = pl.program_id(0)

    @pl.when(slot == 0)
    def _():
        for p in range(pairs_ref.shape[1]):
            for end in (0, 1):
                named = pairs_ref[2 * end, p] * FACES + pairs_ref[2 * end + 1, p] - tile_ref[0] * slots

                @pl.when((named >= 0) & (named < slots))
                def _():
                    crop_ref[named, 0] = extents_ref[0, p]
                    crop_ref[named, 1] = extents_ref[1, p]

    across, along = crop_ref[slot, 0], crop_ref[slot, 1]

    def alternate(first, second):
        first = first + pltpu.roll(first, 127, 1)
        second = second + pltpu.roll(second, 1, 1)
        return jnp.where(even_lane, first, second).astype(jnp.bfloat16)

    row = lax.broadcasted_iota(jnp.int32, (2 * GX, 128), 0)
    lane = lax.broadcasted_iota(jnp.int32, (2 * GX, 128), 1)
    even, even_lane = row % 2 == 0, lane % 2 == 0
    groups = (2 * GX // 8, 8, 128)
    lanes = range(0, 2 * GY, 128)
    lives = [jnp.where((row < across) & (k + lane < along), 1.0, 0.0) for k in lanes]
    block = (2 * PLANES, HALF)
    lane0, imaginary = first_lane(block), imaginary_rows(block)
    sign = jnp.where(imaginary, -0.5, 0.5)

    def row_pairs(z, k, shift):
        raw = band_ref[0, 0, z, :, k : k + 128].astype(jnp.float32) * lives[k // 128]
        return raw + pltpu.roll(raw.reshape(groups), shift, 1).reshape(raw.shape)

    def woven(z, k):
        return jnp.where(even, row_pairs(z, k, 7), row_pairs(z + 1, k, 1))

    def cells(z):
        return jnp.concatenate([alternate(woven(z, k), woven(z + 2, k)) for k in lanes], axis=1)

    zrows = band_ref.shape[2]
    down = jnp.concatenate([cells(z) for z in range(0, zrows, PLANES)], axis=0)
    y = dot(down, wy_ref[...]).astype(jnp.bfloat16).reshape(zrows // PLANES, 2 * GX, 2 * GY)
    units = [
        jnp.concatenate([y[unit, :, k : k + HALF] for k in (0, GY, HALF, GY + HALF)], axis=0)
        for unit in range(zrows // PLANES)
    ]
    spectra = dot(wx_ref[...], jnp.concatenate(units, axis=1))

    def at(n):
        rows = spectra[2 * PLANES * n : 2 * PLANES * (n + 1)]
        return [rows[:, k : k + HALF] for k in range(0, rows.shape[1], HALF)]

    def put(j, blocks):
        out_ref[j, 0] = jnp.concatenate(blocks, axis=0).astype(jnp.bfloat16)

    put(0, at(0))
    put(GX // 2, at(1))
    for j in range(1, GX // 2):
        here, mirror = at(2 * j), at(2 * j + 1)
        put(j, [jnp.where(lane0, 0.5 * a + sign * b, a) for a, b in zip(here, mirror)])
        put(
            GX - j,
            [
                jnp.where(lane0, pltpu.roll(0.5 * a - sign * b, PLANES, 0), b)
                for a, b in zip(here, mirror)
            ],
        )


def analyse(band, pairs, extents, tile):
    slots, zrows = band.shape[0] * FACES, band.shape[2]
    tables = (paired_y_table(), forward_x_table())
    whole = [pl.BlockSpec(t.shape, lambda i, *_: (0, 0)) for t in tables]
    return pl.pallas_call(
        functools.partial(analyse_kernel, slots),
        grid_spec=pltpu.PrefetchScalarGridSpec(
            num_scalar_prefetch=3,
            grid=(slots,),
            in_specs=[
                pl.BlockSpec(
                    (1, 1, zrows, 2 * GX, 2 * GY), lambda i, *_: (i // FACES, i % FACES, 0, 0, 0)
                )
            ]
            + whole,
            out_specs=pl.BlockSpec((GX, 1, 2 * zrows, HALF), lambda i, *_: (0, i, 0, 0)),
            scratch_shapes=[pltpu.SMEM((slots, 2), jnp.int32)],
        ),
        out_shape=jax.ShapeDtypeStruct((GX, slots, 2 * zrows, HALF), jnp.bfloat16),
        compiler_params=pltpu.CompilerParams(vmem_limit_bytes=VMEM_BYTES + VMEM_BYTES * 3 // 4),
        name="analyse",
    )(pairs, extents, tile, band, *(jnp.asarray(t) for t in tables))


def normalised(a_re, a_im, b_re, b_im):
    cross_re = a_re * b_re + a_im * b_im
    cross_im = a_im * b_re - a_re * b_im
    scale = lax.rsqrt(cross_re * cross_re + cross_im * cross_im + 1.0)
    return (cross_re * scale).astype(jnp.bfloat16), (cross_im * scale).astype(jnp.bfloat16)


def correlate_kernel(
    slabs, tiles_here, pairs_ref, place_ref, in_ref, wz_ref, wzi_ref, wz_last_ref, wzi_last_ref, out_ref
):
    tiles = in_ref.shape[0] // slabs
    total = pairs_ref.shape[1]
    pairs_here = out_ref.shape[1]
    slab_rows = out_ref.shape[2]
    both_real = (place_ref[0] == 0) | (place_ref[0] == GX // 2)
    block = (2 * GZ, HALF)
    shared = first_lane(block) & imaginary_rows(block)

    def load(p, end):
        tile = pairs_ref[2 * end, p]
        row = tile // tiles_here
        pos = tile % tiles_here * FACES + pairs_ref[2 * end + 1, p]
        return jnp.concatenate([in_ref[row + s * tiles, pos] for s in range(slabs)], axis=0)

    def phase_of(table_ref, ends):
        spec = dot(table_ref[...], jnp.concatenate(ends, axis=1))
        spec = spec.astype(jnp.bfloat16).astype(jnp.float32)
        parts = [spec[:GZ], spec[GZ:]]
        phases = []
        for k in range(0, spec.shape[1], 2 * HALF):
            a, b = slice(k, k + HALF), slice(k + HALF, k + 2 * HALF)
            phase = normalised(parts[0][:, a], parts[1][:, a], parts[0][:, b], parts[1][:, b])
            phases.append(jnp.concatenate(phase, axis=0))
        return jnp.concatenate(phases, axis=1)

    keep = jnp.where(shared & both_real, 0.0, 1.0).astype(jnp.bfloat16)
    group = 8
    for p in range(0, total, group):
        ends = [load(q, end) * keep for q in range(p, p + group) for end in (0, 1)]
        w = dot(wzi_ref[...], phase_of(wz_ref, ends)).astype(jnp.bfloat16)
        for k, q in enumerate(range(p, p + group)):
            for s in range(slabs):
                out_ref[q // pairs_here + s * tiles, q % pairs_here] = w[
                    s * slab_rows : (s + 1) * slab_rows, k * HALF : (k + 1) * HALF
                ]

    @pl.when(both_real)
    def _():
        lane = lax.broadcasted_iota(jnp.int32, block, 1)
        ends = [jnp.zeros(block, jnp.bfloat16)] * 2
        for p in range(total):
            for end in (0, 1):
                ends[end] = jnp.where(lane == p, load(p, end)[:, 0:1], ends[end])
        w = dot(wzi_last_ref[...], phase_of(wz_last_ref, ends)).astype(jnp.bfloat16)
        for p in range(total):
            column = w[:, p : p + 1]
            for s in range(slabs):
                rows = slice(s * slab_rows, (s + 1) * slab_rows)
                at = (p // pairs_here + s * tiles, p % pairs_here)
                out_ref[at] = jnp.where(shared[rows], column[rows], out_ref[at])


def correlate(spread, pairs, place, slabs, tiles_here):
    devices, _, slab_rows, _ = spread.shape
    pairs_here = pairs.shape[1] * slabs // devices
    tables = z_tables()
    vmem = pl.BlockSpec(memory_space=pltpu.VMEM)
    smem = pl.BlockSpec(memory_space=pltpu.SMEM)
    return pl.pallas_call(
        functools.partial(correlate_kernel, slabs, tiles_here),
        in_specs=[smem, smem] + [vmem] * (1 + len(tables)),
        out_specs=vmem,
        out_shape=jax.ShapeDtypeStruct((devices, pairs_here, slab_rows, HALF), jnp.bfloat16),
        compiler_params=pltpu.CompilerParams(vmem_limit_bytes=VMEM_BYTES),
        name="correlate",
    )(pairs, place, spread, *(jnp.asarray(t) for t in tables))


def synthesise_kernel(in_ref, wx_ref, wy_ref, out_ref):
    zpart = out_ref.shape[1]
    units = zpart // PLANES
    block = (2 * zpart, HALF)
    lane0, imaginary = first_lane(block), imaginary_rows(block)
    sign = jnp.where(imaginary, -1.0, 1.0)
    groups = (units, 2 * PLANES, HALF)

    def at(j):
        return in_ref[j, 0].astype(jnp.float32)

    blocks = [None] * GX
    for j in (0, GX // 2):
        blocks[j] = at(j)
    for j in range(1, GX // 2):
        here, mirror = at(j), at(GX - j)
        swapped = pltpu.roll(mirror.reshape(groups), PLANES, 1).reshape(block)
        blocks[j] = jnp.where(lane0, here + swapped, here)
        blocks[GX - j] = jnp.where(lane0, sign * (here - swapped), mirror)
    stacked = jnp.concatenate(
        [
            jnp.concatenate([b[u * 2 * PLANES : (u + 1) * 2 * PLANES] for b in blocks], axis=0)
            for u in range(units)
        ],
        axis=1,
    ).astype(jnp.bfloat16)
    v = dot(wx_ref[...], stacked).astype(jnp.bfloat16)
    rows = PLANES * GX
    cells = [
        jnp.concatenate([v[:rows, k : k + HALF], v[rows:, k : k + HALF]], axis=1)
        for k in range(0, units * HALF, HALF)
    ]
    maps = dot(jnp.concatenate(cells, axis=0), wy_ref[...])
    out_ref[0] = maps.reshape(zpart, GX, GY)


def synthesise(returned):
    _, pairs_here, slab_rows, _ = returned.shape
    zpart = slab_rows // 2
    tables = (inverse_x_table(), half_y_inverse())
    return pl.pallas_call(
        synthesise_kernel,
        grid=(pairs_here, slab_rows // (2 * zpart)),
        in_specs=[pl.BlockSpec((GX, 1, 2 * zpart, HALF), lambda i, z: (0, i, z, 0))]
        + [pl.BlockSpec(t.shape, lambda i, z: (0, 0)) for t in tables],
        out_specs=pl.BlockSpec((1, zpart, GX, GY), lambda i, z: (i, z, 0, 0)),
        out_shape=jax.ShapeDtypeStruct((pairs_here, slab_rows // 2, GX, GY), jnp.float32),
        compiler_params=pltpu.CompilerParams(vmem_limit_bytes=VMEM_BYTES),
        name="synthesise",
    )(returned, *(jnp.asarray(t) for t in tables))


def shards(band, pairs, extents):
    tiles, slabs = lax.axis_size("tile"), lax.axis_size("zslab")
    zrows = band.shape[2]
    if tiles * slabs != GX or zrows % (4 * PLANES) or pairs.shape[0] % 8 or pairs.shape[0] % tiles:
        return general_shards(band, pairs, extents)
    pairs, extents = pairs.T, extents.T
    tile = lax.axis_index("tile").astype(jnp.int32)
    device = lax.axis_index("zslab").astype(jnp.int32) * tiles + tile
    spectra = analyse(band, pairs, extents, tile[None])
    spread = lax.all_to_all(spectra, ("zslab", "tile"), split_axis=0, concat_axis=0, tiled=True)
    w = correlate(spread, pairs, device[None], slabs, band.shape[0])
    returned = lax.all_to_all(w, ("zslab", "tile"), split_axis=0, concat_axis=0, tiled=True)
    return synthesise(returned)


def solution(mesh):
    placed = (P("tile", None, "zslab", None, None), P(), P())
    return jax.shard_map(
        shards,
        mesh=mesh,
        in_specs=placed,
        out_specs=P("tile", "zslab", None, None),
        check_vma=False,
    )
```

```python
import functools
import math


import jax
import jax.numpy as jnp
import numpy as np
from jax import lax
from jax.experimental import pallas as pl
from jax.experimental.pallas import tpu as pltpu
from jax.sharding import PartitionSpec as P

GX = 32
GY = 256
GZ = 128
FACES = 4


def dft_tables(length):
    indices = jnp.arange(length, dtype=jnp.int32)
    modular = indices[:, None] * indices[None, :] % length
    angles = modular.astype(jnp.float32) * (2.0 * math.pi / length)
    factor = 1.0 / math.sqrt(length)
    return (
        (jnp.cos(angles) * factor).astype(jnp.bfloat16),
        (jnp.sin(angles) * factor).astype(jnp.bfloat16),
    )


def product(form, left, right):
    return jnp.einsum(form, left, right, preferred_element_type=jnp.float32)


def reduce_resolution(image_volume, crop_bounds):
    row_mask = (
        jnp.arange(image_volume.shape[2], dtype=jnp.int32)[None, :] < crop_bounds[:, 0:1]
    ).astype(jnp.bfloat16)
    col_mask = (
        jnp.arange(image_volume.shape[3], dtype=jnp.int32)[None, :] < crop_bounds[:, 1:2]
    ).astype(jnp.bfloat16)
    masked = image_volume * row_mask[:, None, :, None] * col_mask[:, None, None, :]
    raw_cols = jnp.arange(image_volume.shape[3], dtype=jnp.int32)
    pooled_cols = jnp.arange(GY, dtype=jnp.int32)
    pooling = jnp.where(raw_cols[:, None] // 2 == pooled_cols[None, :], 0.5, 0.0).astype(
        jnp.bfloat16
    )
    along_pooled = product("szxy,yk->szxk", masked, pooling)
    shaped = along_pooled.reshape(image_volume.shape[0], image_volume.shape[1], GX, 2, GY)
    return (shaped[:, :, :, 0, :] + shaped[:, :, :, 1, :]).astype(jnp.bfloat16)


def cross_phase(owner_re, owner_im, pairs, tiles_here):
    first_dev = pairs[:, 0] // tiles_here
    first_pos = pairs[:, 0] % tiles_here * FACES + pairs[:, 1]
    second_tile_device = pairs[:, 2] // tiles_here
    second_pos = pairs[:, 2] % tiles_here * FACES + pairs[:, 3]
    first_re = owner_re[first_dev, :, first_pos].astype(jnp.float32)
    first_im = owner_im[first_dev, :, first_pos].astype(jnp.float32)
    second_re = owner_re[second_tile_device, :, second_pos].astype(jnp.float32)
    second_im = owner_im[second_tile_device, :, second_pos].astype(jnp.float32)
    cross_re = first_re * second_re + first_im * second_im
    cross_im = first_im * second_re - first_re * second_im
    scaled = jnp.sqrt(cross_re * cross_re + cross_im * cross_im + 1.0)
    return ((cross_re / scaled).astype(jnp.bfloat16), (cross_im / scaled).astype(jnp.bfloat16))


def inverse_z(phase_real_part, phase_im, tables_z):
    w_re = (
        product("pmjk,mz->pzjk", phase_real_part, tables_z[0])
        - product("pmjk,mz->pzjk", phase_im, tables_z[1])
    ).astype(jnp.bfloat16)
    w_im = (
        product("pmjk,mz->pzjk", phase_im, tables_z[0])
        + product("pmjk,mz->pzjk", phase_real_part, tables_z[1])
    ).astype(jnp.bfloat16)
    return (w_re, w_im)


def inverse_x(w_re, w_im, tables_x):
    v_re = (
        product("pzjk,jx->pzxk", w_re, tables_x[0]) - product("pzjk,jx->pzxk", w_im, tables_x[1])
    ).astype(jnp.bfloat16)
    v_im = (
        product("pzjk,jx->pzxk", w_im, tables_x[0]) + product("pzjk,jx->pzxk", w_re, tables_x[1])
    ).astype(jnp.bfloat16)
    return (v_re, v_im)


def general_shards(band, pairs, extents):
    tables_x = dft_tables(GX)
    tables_y = dft_tables(GY)
    tables_z = dft_tables(GZ)
    tiles_here = band.shape[0]
    slots = tiles_here * FACES
    zrows = band.shape[2]
    tile_pos = lax.axis_index("tile")
    global_slot = tile_pos * slots + jnp.arange(slots, dtype=jnp.int32)
    first_slot = pairs[:, 0] * FACES + pairs[:, 1]
    second_slot = pairs[:, 2] * FACES + pairs[:, 3]
    matches = (
        (first_slot[None, :] == global_slot[:, None])
        | (second_slot[None, :] == global_slot[:, None])
    ).astype(jnp.int32)
    crop_bounds = jnp.sum(matches[:, :, None] * extents[None, :, :], axis=1)
    image_volume = band.reshape(slots, zrows, 2 * GX, 2 * GY)
    reduced_volume = reduce_resolution(image_volume, crop_bounds)
    y_re = product("szxy,yk->szxk", reduced_volume, tables_y[0]).astype(jnp.bfloat16)
    y_im = (-product("szxy,yk->szxk", reduced_volume, tables_y[1])).astype(jnp.bfloat16)
    x_re = (
        product("szxk,xj->szjk", y_re, tables_x[0]) + product("szxk,xj->szjk", y_im, tables_x[1])
    ).astype(jnp.bfloat16)
    x_im = (
        product("szxk,xj->szjk", y_im, tables_x[0]) - product("szxk,xj->szjk", y_re, tables_x[1])
    ).astype(jnp.bfloat16)
    kx_part = GX // lax.axis_size("zslab")
    re_in = lax.all_to_all(x_re, "zslab", split_axis=2, concat_axis=1, tiled=True)
    im_in = lax.all_to_all(x_im, "zslab", split_axis=2, concat_axis=1, tiled=True)
    out_re = (
        product("szjk,zm->msjk", re_in, tables_z[0]) + product("szjk,zm->msjk", im_in, tables_z[1])
    ).astype(jnp.bfloat16)
    out_im = (
        product("szjk,zm->msjk", im_in, tables_z[0]) - product("szjk,zm->msjk", re_in, tables_z[1])
    ).astype(jnp.bfloat16)
    tile_count = lax.axis_size("tile")
    kz_part = GZ // tile_count
    spectra = (
        lax.all_to_all(out_re, "tile", split_axis=0, concat_axis=0, tiled=True),
        lax.all_to_all(out_im, "tile", split_axis=0, concat_axis=0, tiled=True),
    )
    owner_re = spectra[0].reshape(tile_count, kz_part, slots, kx_part, GY)
    owner_im = spectra[1].reshape(tile_count, kz_part, slots, kx_part, GY)
    phase_real_part, phase_im = cross_phase(owner_re, owner_im, pairs, tiles_here)
    returned = (
        lax.all_to_all(phase_real_part, "tile", split_axis=0, concat_axis=1, tiled=True),
        lax.all_to_all(phase_im, "tile", split_axis=0, concat_axis=1, tiled=True),
    )
    w_re, w_im = inverse_z(returned[0], returned[1], tables_z)
    v_re, v_im = inverse_x(
        lax.all_to_all(w_re, "zslab", split_axis=1, concat_axis=2, tiled=True),
        lax.all_to_all(w_im, "zslab", split_axis=1, concat_axis=2, tiled=True),
        tables_x,
    )
    return product("pzxk,ky->pzxy", v_re, tables_y[0]) - product("pzxk,ky->pzxy", v_im, tables_y[1])


HALF = GY // 2
PLANES = 4
VMEM_BYTES = 32 * 1024 * 1024


def host_tables(length):
    indices = np.arange(length, dtype=np.int32)
    modular = indices[:, None] * indices[None, :] % length
    angles = modular.astype(np.float32) * np.float32(2.0 * math.pi / length)
    factor = np.float32(1.0 / math.sqrt(length))
    return (
        (np.cos(angles) * factor).astype(jnp.bfloat16),
        (np.sin(angles) * factor).astype(jnp.bfloat16),
    )


def half_y_table():
    cosine, sine = host_tables(GY)
    imag = -sine[:, :HALF]
    imag[:, 0] = cosine[:, HALF]
    return np.concatenate([cosine[:, :HALF], imag], axis=1)


def paired_y_table():
    half = half_y_table() * np.array(0.5, jnp.bfloat16)
    table = np.zeros((2 * GY, 2 * GY), jnp.bfloat16)
    table[::2, :GY] = half
    table[1::2, GY:] = half
    return table


def half_y_inverse():
    cosine, sine = host_tables(GY)
    two = np.array(2.0, jnp.bfloat16)
    real = cosine[:HALF, :] * two
    real[0] = cosine[0]
    imag = -sine[:HALF, :] * two
    imag[0] = cosine[HALF]
    return np.concatenate([real, imag], axis=0)


def mirror_order():
    order = [0, GX // 2]
    for j in range(1, GX // 2):
        order += [j, GX - j]
    return order


def complex_blocks(length, sign):
    cosine, sine = (table.astype(np.float32) for table in host_tables(length))
    return np.array([[cosine, -sign * sine], [sign * sine, cosine]])


def forward_x_table():
    table = np.einsum("oijx,az->joaizx", complex_blocks(GX, -1), np.eye(PLANES))[mirror_order()]
    table = table.reshape(2 * GX * PLANES, 2, PLANES // 2, 2, GX).transpose(0, 1, 2, 4, 3)
    return table.reshape(2 * GX * PLANES, -1).astype(jnp.bfloat16)


def inverse_x_table():
    table = np.einsum("oijx,az->oaxjiz", complex_blocks(GX, 1), np.eye(PLANES))
    return table.reshape(2 * PLANES * GX, -1).astype(jnp.bfloat16)


def z_rows():
    return np.arange(2 * GZ).reshape(2, GZ // PLANES, PLANES).transpose(1, 0, 2).reshape(-1)


def z_tables():
    forward, inverse = (
        complex_blocks(GZ, sign).transpose(0, 2, 1, 3).reshape(2 * GZ, 2 * GZ) for sign in (-1, 1)
    )
    none = np.zeros((2 * GZ, GZ), np.float32)
    forward_last = np.concatenate([none, forward[:, :GZ]], axis=1)
    inverse_last = np.concatenate([none.T, inverse[:GZ]], axis=0)
    order = z_rows()
    return [
        np.ascontiguousarray(table).astype(jnp.bfloat16)
        for table in (
            forward[:, order],
            inverse[order],
            forward_last[:, order],
            inverse_last[order],
        )
    ]


def imaginary_rows(shape):
    return lax.broadcasted_iota(jnp.int32, shape, 0) % (2 * PLANES) >= PLANES


def first_lane(shape):
    return lax.broadcasted_iota(jnp.int32, shape, 1) == 0


def dot(left, right):
    return jnp.dot(left, right, preferred_element_type=jnp.float32)


def analyse_kernel(
    slots, pairs_ref, extents_ref, tile_ref, *rest
):
    band_refs, (wy_ref, wx_ref, out_ref, crop_ref) = rest[:-4], rest[-4:]
    per_ref = band_refs[0].shape[2]
    slot = pl.program_id(0)

    @pl.when(slot == 0)
    def _():
        for p in range(pairs_ref.shape[1]):
            for end in (0, 1):
                named = pairs_ref[2 * end, p] * FACES + pairs_ref[2 * end + 1, p] - tile_ref[0] * slots

                @pl.when((named >= 0) & (named < slots))
                def _():
                    crop_ref[named, 0] = extents_ref[0, p]
                    crop_ref[named, 1] = extents_ref[1, p]

    across, along = crop_ref[slot, 0], crop_ref[slot, 1]

    def alternate(first, second):
        first = first + pltpu.roll(first, 127, 1)
        second = second + pltpu.roll(second, 1, 1)
        return jnp.where(even_lane, first, second).astype(jnp.bfloat16)

    row = lax.broadcasted_iota(jnp.int32, (2 * GX, 128), 0)
    lane = lax.broadcasted_iota(jnp.int32, (2 * GX, 128), 1)
    even, even_lane = row % 2 == 0, lane % 2 == 0
    groups = (2 * GX // 8, 8, 128)
    lanes = range(0, 2 * GY, 128)
    lives = [jnp.where((row < across) & (k + lane < along), 1.0, 0.0) for k in lanes]
    block = (2 * PLANES, HALF)
    lane0, imaginary = first_lane(block), imaginary_rows(block)
    sign = jnp.where(imaginary, -0.5, 0.5)

    def row_pairs(z, k, shift):
        raw = band_refs[z // per_ref][0, 0, z % per_ref, :, k : k + 128].astype(jnp.float32) * lives[k // 128]
        return raw + pltpu.roll(raw.reshape(groups), shift, 1).reshape(raw.shape)

    def woven(z, k):
        return jnp.where(even, row_pairs(z, k, 7), row_pairs(z + 1, k, 1))

    def cells(z):
        return jnp.concatenate([alternate(woven(z, k), woven(z + 2, k)) for k in lanes], axis=1)

    zrows = per_ref * len(band_refs)
    down = jnp.concatenate([cells(z) for z in range(0, zrows, PLANES)], axis=0)
    y = dot(down, wy_ref[...]).astype(jnp.bfloat16).reshape(zrows // PLANES, 2 * GX, 2 * GY)
    units = [
        jnp.concatenate([y[unit, :, k : k + HALF] for k in (0, GY, HALF, GY + HALF)], axis=0)
        for unit in range(zrows // PLANES)
    ]
    spectra = dot(wx_ref[...], jnp.concatenate(units, axis=1))

    def at(n):
        rows = spectra[2 * PLANES * n : 2 * PLANES * (n + 1)]
        return [rows[:, k : k + HALF] for k in range(0, rows.shape[1], HALF)]

    def put(j, blocks):
        out_ref[j, 0] = jnp.concatenate(blocks, axis=0).astype(jnp.bfloat16)

    put(0, at(0))
    put(GX // 2, at(1))
    for j in range(1, GX // 2):
        here, mirror = at(2 * j), at(2 * j + 1)
        put(j, [jnp.where(lane0, 0.5 * a + sign * b, a) for a, b in zip(here, mirror)])
        put(
            GX - j,
            [
                jnp.where(lane0, pltpu.roll(0.5 * a - sign * b, PLANES, 0), b)
                for a, b in zip(here, mirror)
            ],
        )


def analyse(band, pairs, extents, tile):
    slots, zrows = band.shape[0] * FACES, band.shape[2]
    tables = (paired_y_table(), forward_x_table())
    windows = 4
    whole = [pl.BlockSpec(t.shape, lambda i, *_: (0, 0)) for t in tables]
    return pl.pallas_call(
        functools.partial(analyse_kernel, slots),
        grid_spec=pltpu.PrefetchScalarGridSpec(
            num_scalar_prefetch=3,
            grid=(slots,),
            in_specs=[
                pl.BlockSpec(
                    (1, 1, zrows // windows, 2 * GX, 2 * GY),
                    lambda i, *_, k=k: (i // FACES, i % FACES, k, 0, 0),
                )
                for k in range(windows)
            ]
            + whole,
            out_specs=pl.BlockSpec((GX, 1, 2 * zrows, HALF), lambda i, *_: (0, i, 0, 0)),
            scratch_shapes=[pltpu.SMEM((slots, 2), jnp.int32)],
        ),
        out_shape=jax.ShapeDtypeStruct((GX, slots, 2 * zrows, HALF), jnp.bfloat16),
        compiler_params=pltpu.CompilerParams(vmem_limit_bytes=VMEM_BYTES + VMEM_BYTES * 3 // 4),
        name="analyse",
    )(pairs, extents, tile, *[band] * windows, *(jnp.asarray(t) for t in tables))


def normalised(a_re, a_im, b_re, b_im):
    cross_re = a_re * b_re + a_im * b_im
    cross_im = a_im * b_re - a_re * b_im
    scale = lax.rsqrt(cross_re * cross_re + cross_im * cross_im + 1.0)
    return (cross_re * scale).astype(jnp.bfloat16), (cross_im * scale).astype(jnp.bfloat16)


def correlate_kernel(
    slabs, tiles_here, pairs_ref, place_ref, in_ref, wz_ref, wzi_ref, wz_last_ref, wzi_last_ref, out_ref
):
    tiles = in_ref.shape[0] // slabs
    total = pairs_ref.shape[1]
    pairs_here = out_ref.shape[1]
    slab_rows = out_ref.shape[2]
    both_real = (place_ref[0] == 0) | (place_ref[0] == GX // 2)
    block = (2 * GZ, HALF)
    shared = first_lane(block) & imaginary_rows(block)

    def load(p, end):
        tile = pairs_ref[2 * end, p]
        row = tile // tiles_here
        pos = tile % tiles_here * FACES + pairs_ref[2 * end + 1, p]
        return jnp.concatenate([in_ref[row + s * tiles, pos] for s in range(slabs)], axis=0)

    def phase_of(table_ref, ends):
        spec = dot(table_ref[...], jnp.concatenate(ends, axis=1))
        spec = spec.astype(jnp.bfloat16).astype(jnp.float32)
        parts = [spec[:GZ], spec[GZ:]]
        phases = []
        for k in range(0, spec.shape[1], 2 * HALF):
            a, b = slice(k, k + HALF), slice(k + HALF, k + 2 * HALF)
            phase = normalised(parts[0][:, a], parts[1][:, a], parts[0][:, b], parts[1][:, b])
            phases.append(jnp.concatenate(phase, axis=0))
        return jnp.concatenate(phases, axis=1)

    keep = jnp.where(shared & both_real, 0.0, 1.0).astype(jnp.bfloat16)
    group = 8
    for p in range(0, total, group):
        ends = [load(q, end) * keep for q in range(p, p + group) for end in (0, 1)]
        w = dot(wzi_ref[...], phase_of(wz_ref, ends)).astype(jnp.bfloat16)
        for k, q in enumerate(range(p, p + group)):
            for s in range(slabs):
                out_ref[q // pairs_here + s * tiles, q % pairs_here] = w[
                    s * slab_rows : (s + 1) * slab_rows, k * HALF : (k + 1) * HALF
                ]

    @pl.when(both_real)
    def _():
        lane = lax.broadcasted_iota(jnp.int32, block, 1)
        ends = [jnp.zeros(block, jnp.bfloat16)] * 2
        for p in range(total):
            for end in (0, 1):
                ends[end] = jnp.where(lane == p, load(p, end)[:, 0:1], ends[end])
        w = dot(wzi_last_ref[...], phase_of(wz_last_ref, ends)).astype(jnp.bfloat16)
        for p in range(total):
            column = w[:, p : p + 1]
            for s in range(slabs):
                rows = slice(s * slab_rows, (s + 1) * slab_rows)
                at = (p // pairs_here + s * tiles, p % pairs_here)
                out_ref[at] = jnp.where(shared[rows], column[rows], out_ref[at])


def correlate(spread, pairs, place, slabs, tiles_here):
    devices, _, slab_rows, _ = spread.shape
    pairs_here = pairs.shape[1] * slabs // devices
    tables = z_tables()
    vmem = pl.BlockSpec(memory_space=pltpu.VMEM)
    smem = pl.BlockSpec(memory_space=pltpu.SMEM)
    return pl.pallas_call(
        functools.partial(correlate_kernel, slabs, tiles_here),
        in_specs=[smem, smem] + [vmem] * (1 + len(tables)),
        out_specs=vmem,
        out_shape=jax.ShapeDtypeStruct((devices, pairs_here, slab_rows, HALF), jnp.bfloat16),
        compiler_params=pltpu.CompilerParams(vmem_limit_bytes=VMEM_BYTES),
        name="correlate",
    )(pairs, place, spread, *(jnp.asarray(t) for t in tables))


def synthesise_kernel(in_ref, wx_ref, wy_ref, out_ref):
    zpart = out_ref.shape[1]
    units = zpart // PLANES
    block = (2 * zpart, HALF)
    lane0, imaginary = first_lane(block), imaginary_rows(block)
    sign = jnp.where(imaginary, -1.0, 1.0)
    groups = (units, 2 * PLANES, HALF)

    def at(j):
        return in_ref[j, 0].astype(jnp.float32)

    blocks = [None] * GX
    for j in (0, GX // 2):
        blocks[j] = at(j)
    for j in range(1, GX // 2):
        here, mirror = at(j), at(GX - j)
        swapped = pltpu.roll(mirror.reshape(groups), PLANES, 1).reshape(block)
        blocks[j] = jnp.where(lane0, here + swapped, here)
        blocks[GX - j] = jnp.where(lane0, sign * (here - swapped), mirror)
    stacked = jnp.concatenate(
        [
            jnp.concatenate([b[u * 2 * PLANES : (u + 1) * 2 * PLANES] for b in blocks], axis=0)
            for u in range(units)
        ],
        axis=1,
    ).astype(jnp.bfloat16)
    v = dot(wx_ref[...], stacked).astype(jnp.bfloat16)
    rows = PLANES * GX
    cells = [
        jnp.concatenate([v[:rows, k : k + HALF], v[rows:, k : k + HALF]], axis=1)
        for k in range(0, units * HALF, HALF)
    ]
    maps = dot(jnp.concatenate(cells, axis=0), wy_ref[...])
    out_ref[0] = maps.reshape(zpart, GX, GY)


def synthesise(returned):
    _, pairs_here, slab_rows, _ = returned.shape
    zpart = slab_rows // 2
    tables = (inverse_x_table(), half_y_inverse())
    return pl.pallas_call(
        synthesise_kernel,
        grid=(pairs_here, slab_rows // (2 * zpart)),
        in_specs=[pl.BlockSpec((GX, 1, 2 * zpart, HALF), lambda i, z: (0, i, z, 0))]
        + [pl.BlockSpec(t.shape, lambda i, z: (0, 0)) for t in tables],
        out_specs=pl.BlockSpec((1, zpart, GX, GY), lambda i, z: (i, z, 0, 0)),
        out_shape=jax.ShapeDtypeStruct((pairs_here, slab_rows // 2, GX, GY), jnp.float32),
        compiler_params=pltpu.CompilerParams(vmem_limit_bytes=VMEM_BYTES),
        name="synthesise",
    )(returned, *(jnp.asarray(t) for t in tables))


def shards(band, pairs, extents):
    tiles, slabs = lax.axis_size("tile"), lax.axis_size("zslab")
    zrows = band.shape[2]
    if tiles * slabs != GX or zrows % (4 * PLANES) or pairs.shape[0] % 8 or pairs.shape[0] % tiles:
        return general_shards(band, pairs, extents)
    pairs, extents = pairs.T, extents.T
    tile = lax.axis_index("tile").astype(jnp.int32)
    device = lax.axis_index("zslab").astype(jnp.int32) * tiles + tile
    spectra = analyse(band, pairs, extents, tile[None])
    spread = lax.all_to_all(spectra, ("zslab", "tile"), split_axis=0, concat_axis=0, tiled=True)
    w = correlate(spread, pairs, device[None], slabs, band.shape[0])
    returned = lax.all_to_all(w, ("zslab", "tile"), split_axis=0, concat_axis=0, tiled=True)
    return synthesise(returned)


def solution(mesh):
    placed = (P("tile", None, "zslab", None, None), P(), P())
    return jax.shard_map(
        shards,
        mesh=mesh,
        in_specs=placed,
        out_specs=P("tile", "zslab", None, None),
        check_vma=False,
    )
```

```python
import functools
import math


import jax
import jax.numpy as jnp
import numpy as np
from jax import lax
from jax.experimental import pallas as pl
from jax.experimental.pallas import tpu as pltpu
from jax.sharding import PartitionSpec as P

GX = 32
GY = 256
GZ = 128
FACES = 4


def dft_tables(length):
    indices = jnp.arange(length, dtype=jnp.int32)
    modular = indices[:, None] * indices[None, :] % length
    angles = modular.astype(jnp.float32) * (2.0 * math.pi / length)
    factor = 1.0 / math.sqrt(length)
    return (
        (jnp.cos(angles) * factor).astype(jnp.bfloat16),
        (jnp.sin(angles) * factor).astype(jnp.bfloat16),
    )


def product(form, left, right):
    return jnp.einsum(form, left, right, preferred_element_type=jnp.float32)


def reduce_resolution(image_volume, crop_bounds):
    row_mask = (
        jnp.arange(image_volume.shape[2], dtype=jnp.int32)[None, :] < crop_bounds[:, 0:1]
    ).astype(jnp.bfloat16)
    col_mask = (
        jnp.arange(image_volume.shape[3], dtype=jnp.int32)[None, :] < crop_bounds[:, 1:2]
    ).astype(jnp.bfloat16)
    masked = image_volume * row_mask[:, None, :, None] * col_mask[:, None, None, :]
    raw_cols = jnp.arange(image_volume.shape[3], dtype=jnp.int32)
    pooled_cols = jnp.arange(GY, dtype=jnp.int32)
    pooling = jnp.where(raw_cols[:, None] // 2 == pooled_cols[None, :], 0.5, 0.0).astype(
        jnp.bfloat16
    )
    along_pooled = product("szxy,yk->szxk", masked, pooling)
    shaped = along_pooled.reshape(image_volume.shape[0], image_volume.shape[1], GX, 2, GY)
    return (shaped[:, :, :, 0, :] + shaped[:, :, :, 1, :]).astype(jnp.bfloat16)


def cross_phase(owner_re, owner_im, pairs, tiles_here):
    first_dev = pairs[:, 0] // tiles_here
    first_pos = pairs[:, 0] % tiles_here * FACES + pairs[:, 1]
    second_tile_device = pairs[:, 2] // tiles_here
    second_pos = pairs[:, 2] % tiles_here * FACES + pairs[:, 3]
    first_re = owner_re[first_dev, :, first_pos].astype(jnp.float32)
    first_im = owner_im[first_dev, :, first_pos].astype(jnp.float32)
    second_re = owner_re[second_tile_device, :, second_pos].astype(jnp.float32)
    second_im = owner_im[second_tile_device, :, second_pos].astype(jnp.float32)
    cross_re = first_re * second_re + first_im * second_im
    cross_im = first_im * second_re - first_re * second_im
    scaled = jnp.sqrt(cross_re * cross_re + cross_im * cross_im + 1.0)
    return ((cross_re / scaled).astype(jnp.bfloat16), (cross_im / scaled).astype(jnp.bfloat16))


def inverse_z(phase_real_part, phase_im, tables_z):
    w_re = (
        product("pmjk,mz->pzjk", phase_real_part, tables_z[0])
        - product("pmjk,mz->pzjk", phase_im, tables_z[1])
    ).astype(jnp.bfloat16)
    w_im = (
        product("pmjk,mz->pzjk", phase_im, tables_z[0])
        + product("pmjk,mz->pzjk", phase_real_part, tables_z[1])
    ).astype(jnp.bfloat16)
    return (w_re, w_im)


def inverse_x(w_re, w_im, tables_x):
    v_re = (
        product("pzjk,jx->pzxk", w_re, tables_x[0]) - product("pzjk,jx->pzxk", w_im, tables_x[1])
    ).astype(jnp.bfloat16)
    v_im = (
        product("pzjk,jx->pzxk", w_im, tables_x[0]) + product("pzjk,jx->pzxk", w_re, tables_x[1])
    ).astype(jnp.bfloat16)
    return (v_re, v_im)


def general_shards(band, pairs, extents):
    tables_x = dft_tables(GX)
    tables_y = dft_tables(GY)
    tables_z = dft_tables(GZ)
    tiles_here = band.shape[0]
    slots = tiles_here * FACES
    zrows = band.shape[2]
    tile_pos = lax.axis_index("tile")
    global_slot = tile_pos * slots + jnp.arange(slots, dtype=jnp.int32)
    first_slot = pairs[:, 0] * FACES + pairs[:, 1]
    second_slot = pairs[:, 2] * FACES + pairs[:, 3]
    matches = (
        (first_slot[None, :] == global_slot[:, None])
        | (second_slot[None, :] == global_slot[:, None])
    ).astype(jnp.int32)
    crop_bounds = jnp.sum(matches[:, :, None] * extents[None, :, :], axis=1)
    image_volume = band.reshape(slots, zrows, 2 * GX, 2 * GY)
    reduced_volume = reduce_resolution(image_volume, crop_bounds)
    y_re = product("szxy,yk->szxk", reduced_volume, tables_y[0]).astype(jnp.bfloat16)
    y_im = (-product("szxy,yk->szxk", reduced_volume, tables_y[1])).astype(jnp.bfloat16)
    x_re = (
        product("szxk,xj->szjk", y_re, tables_x[0]) + product("szxk,xj->szjk", y_im, tables_x[1])
    ).astype(jnp.bfloat16)
    x_im = (
        product("szxk,xj->szjk", y_im, tables_x[0]) - product("szxk,xj->szjk", y_re, tables_x[1])
    ).astype(jnp.bfloat16)
    kx_part = GX // lax.axis_size("zslab")
    re_in = lax.all_to_all(x_re, "zslab", split_axis=2, concat_axis=1, tiled=True)
    im_in = lax.all_to_all(x_im, "zslab", split_axis=2, concat_axis=1, tiled=True)
    out_re = (
        product("szjk,zm->msjk", re_in, tables_z[0]) + product("szjk,zm->msjk", im_in, tables_z[1])
    ).astype(jnp.bfloat16)
    out_im = (
        product("szjk,zm->msjk", im_in, tables_z[0]) - product("szjk,zm->msjk", re_in, tables_z[1])
    ).astype(jnp.bfloat16)
    tile_count = lax.axis_size("tile")
    kz_part = GZ // tile_count
    spectra = (
        lax.all_to_all(out_re, "tile", split_axis=0, concat_axis=0, tiled=True),
        lax.all_to_all(out_im, "tile", split_axis=0, concat_axis=0, tiled=True),
    )
    owner_re = spectra[0].reshape(tile_count, kz_part, slots, kx_part, GY)
    owner_im = spectra[1].reshape(tile_count, kz_part, slots, kx_part, GY)
    phase_real_part, phase_im = cross_phase(owner_re, owner_im, pairs, tiles_here)
    returned = (
        lax.all_to_all(phase_real_part, "tile", split_axis=0, concat_axis=1, tiled=True),
        lax.all_to_all(phase_im, "tile", split_axis=0, concat_axis=1, tiled=True),
    )
    w_re, w_im = inverse_z(returned[0], returned[1], tables_z)
    v_re, v_im = inverse_x(
        lax.all_to_all(w_re, "zslab", split_axis=1, concat_axis=2, tiled=True),
        lax.all_to_all(w_im, "zslab", split_axis=1, concat_axis=2, tiled=True),
        tables_x,
    )
    return product("pzxk,ky->pzxy", v_re, tables_y[0]) - product("pzxk,ky->pzxy", v_im, tables_y[1])


HALF = GY // 2
PLANES = 4
VMEM_BYTES = 32 * 1024 * 1024


def host_tables(length):
    indices = np.arange(length, dtype=np.int32)
    modular = indices[:, None] * indices[None, :] % length
    angles = modular.astype(np.float32) * np.float32(2.0 * math.pi / length)
    factor = np.float32(1.0 / math.sqrt(length))
    return (
        (np.cos(angles) * factor).astype(jnp.bfloat16),
        (np.sin(angles) * factor).astype(jnp.bfloat16),
    )


def half_y_table():
    cosine, sine = host_tables(GY)
    imag = -sine[:, :HALF]
    imag[:, 0] = cosine[:, HALF]
    return np.concatenate([cosine[:, :HALF], imag], axis=1)


def paired_y_table():
    half = half_y_table() * np.array(0.5, jnp.bfloat16)
    table = np.zeros((2 * GY, 2 * GY), jnp.bfloat16)
    table[::2, :GY] = half
    table[1::2, GY:] = half
    return table


def half_y_inverse():
    cosine, sine = host_tables(GY)
    two = np.array(2.0, jnp.bfloat16)
    real = cosine[:HALF, :] * two
    real[0] = cosine[0]
    imag = -sine[:HALF, :] * two
    imag[0] = cosine[HALF]
    return np.concatenate([real, imag], axis=0)


def mirror_order():
    order = [0, GX // 2]
    for j in range(1, GX // 2):
        order += [j, GX - j]
    return order


def complex_blocks(length, sign):
    cosine, sine = (table.astype(np.float32) for table in host_tables(length))
    return np.array([[cosine, -sign * sine], [sign * sine, cosine]])


def forward_x_table():
    table = np.einsum("oijx,az->joaizx", complex_blocks(GX, -1), np.eye(PLANES))[mirror_order()]
    return table.reshape(2 * GX * PLANES, -1).astype(jnp.bfloat16)


def row_pair_table():
    raw = np.arange(2 * PLANES * GX)[None, :] // 2
    return (raw == np.arange(PLANES * GX)[:, None]).astype(jnp.bfloat16)


def inverse_x_table():
    table = np.einsum("oijx,az->oaxjiz", complex_blocks(GX, 1), np.eye(PLANES))
    return table.reshape(2 * PLANES * GX, -1).astype(jnp.bfloat16)


def z_rows():
    return np.arange(2 * GZ).reshape(2, GZ // PLANES, PLANES).transpose(1, 0, 2).reshape(-1)


def z_tables():
    forward, inverse = (
        complex_blocks(GZ, sign).transpose(0, 2, 1, 3).reshape(2 * GZ, 2 * GZ) for sign in (-1, 1)
    )
    none = np.zeros((2 * GZ, GZ), np.float32)
    forward_last = np.concatenate([none, forward[:, :GZ]], axis=1)
    inverse_last = np.concatenate([none.T, inverse[:GZ]], axis=0)
    order = z_rows()
    return [
        np.ascontiguousarray(table).astype(jnp.bfloat16)
        for table in (
            forward[:, order],
            inverse[order],
            forward_last[:, order],
            inverse_last[order],
        )
    ]


def imaginary_rows(shape):
    return lax.broadcasted_iota(jnp.int32, shape, 0) % (2 * PLANES) >= PLANES


def first_lane(shape):
    return lax.broadcasted_iota(jnp.int32, shape, 1) == 0


def dot(left, right):
    return jnp.dot(left, right, preferred_element_type=jnp.float32)


def analyse_kernel(
    slots, pairs_ref, extents_ref, tile_ref, band_ref, wp_ref, wy_ref, wx_ref, out_ref, crop_ref
):
    slot = pl.program_id(0)

    @pl.when(slot == 0)
    def _():
        for p in range(pairs_ref.shape[1]):
            for end in (0, 1):
                named = pairs_ref[2 * end, p] * FACES + pairs_ref[2 * end + 1, p] - tile_ref[0] * slots

                @pl.when((named >= 0) & (named < slots))
                def _():
                    crop_ref[named, 0] = extents_ref[0, p]
                    crop_ref[named, 1] = extents_ref[1, p]

    across, along = crop_ref[slot, 0], crop_ref[slot, 1]

    raw_row = lax.broadcasted_iota(jnp.int32, wp_ref.shape, 1) % (2 * GX)
    wp = jnp.where(raw_row < across, wp_ref[...].astype(jnp.float32), 0.0).astype(jnp.bfloat16)
    half_rows = PLANES // 2 * GX
    lane = lax.broadcasted_iota(jnp.int32, (half_rows, 128), 1)
    even_lane = lane % 2 == 0
    lanes = range(0, 2 * GY, 128)
    lives = [jnp.where(k + lane < along, 1.0, 0.0) for k in lanes]
    block = (2 * PLANES, HALF)
    lane0, imaginary = first_lane(block), imaginary_rows(block)
    sign = jnp.where(imaginary, -0.5, 0.5)

    def cells(z):
        rows = dot(wp, band_ref[0, 0, z : z + PLANES].reshape(-1, 2 * GY))
        blocks = []
        for k, live in zip(lanes, lives):
            first = rows[:half_rows, k : k + 128] * live
            second = rows[half_rows:, k : k + 128] * live
            first = first + pltpu.roll(first, 127, 1)
            second = second + pltpu.roll(second, 1, 1)
            blocks.append(jnp.where(even_lane, first, second).astype(jnp.bfloat16))
        return jnp.concatenate(blocks, axis=1)

    zrows = band_ref.shape[2]
    down = jnp.concatenate([cells(z) for z in range(0, zrows, PLANES)], axis=0)
    y = dot(down, wy_ref[...]).astype(jnp.bfloat16).reshape(zrows // PLANES, 2 * GX, 2 * GY)
    units = [
        jnp.concatenate([y[unit, :, k : k + HALF] for k in (0, GY, HALF, GY + HALF)], axis=0)
        for unit in range(zrows // PLANES)
    ]
    spectra = dot(wx_ref[...], jnp.concatenate(units, axis=1))

    def at(n):
        rows = spectra[2 * PLANES * n : 2 * PLANES * (n + 1)]
        return [rows[:, k : k + HALF] for k in range(0, rows.shape[1], HALF)]

    def put(j, blocks):
        out_ref[j, 0] = jnp.concatenate(blocks, axis=0).astype(jnp.bfloat16)

    put(0, at(0))
    put(GX // 2, at(1))
    for j in range(1, GX // 2):
        here, mirror = at(2 * j), at(2 * j + 1)
        put(j, [jnp.where(lane0, 0.5 * a + sign * b, a) for a, b in zip(here, mirror)])
        put(
            GX - j,
            [
                jnp.where(lane0, pltpu.roll(0.5 * a - sign * b, PLANES, 0), b)
                for a, b in zip(here, mirror)
            ],
        )


def analyse(band, pairs, extents, tile):
    slots, zrows = band.shape[0] * FACES, band.shape[2]
    tables = (row_pair_table(), paired_y_table(), forward_x_table())
    whole = [pl.BlockSpec(t.shape, lambda i, *_: (0, 0)) for t in tables]
    return pl.pallas_call(
        functools.partial(analyse_kernel, slots),
        grid_spec=pltpu.PrefetchScalarGridSpec(
            num_scalar_prefetch=3,
            grid=(slots,),
            in_specs=[
                pl.BlockSpec(
                    (1, 1, zrows, 2 * GX, 2 * GY), lambda i, *_: (i // FACES, i % FACES, 0, 0, 0)
                )
            ]
            + whole,
            out_specs=pl.BlockSpec((GX, 1, 2 * zrows, HALF), lambda i, *_: (0, i, 0, 0)),
            scratch_shapes=[pltpu.SMEM((slots, 2), jnp.int32)],
        ),
        out_shape=jax.ShapeDtypeStruct((GX, slots, 2 * zrows, HALF), jnp.bfloat16),
        compiler_params=pltpu.CompilerParams(vmem_limit_bytes=VMEM_BYTES + VMEM_BYTES * 3 // 4),
        name="analyse",
    )(pairs, extents, tile, band, *(jnp.asarray(t) for t in tables))


def normalised(a_re, a_im, b_re, b_im):
    cross_re = a_re * b_re + a_im * b_im
    cross_im = a_im * b_re - a_re * b_im
    scale = lax.rsqrt(cross_re * cross_re + cross_im * cross_im + 1.0)
    return (cross_re * scale).astype(jnp.bfloat16), (cross_im * scale).astype(jnp.bfloat16)


def correlate_kernel(
    slabs, tiles_here, pairs_ref, place_ref, in_ref, wz_ref, wzi_ref, wz_last_ref, wzi_last_ref, out_ref
):
    tiles = in_ref.shape[0] // slabs
    total = pairs_ref.shape[1]
    pairs_here = out_ref.shape[1]
    slab_rows = out_ref.shape[2]
    both_real = (place_ref[0] == 0) | (place_ref[0] == GX // 2)
    block = (2 * GZ, HALF)
    shared = first_lane(block) & imaginary_rows(block)

    def load(p, end):
        tile = pairs_ref[2 * end, p]
        row = tile // tiles_here
        pos = tile % tiles_here * FACES + pairs_ref[2 * end + 1, p]
        return jnp.concatenate([in_ref[row + s * tiles, pos] for s in range(slabs)], axis=0)

    def phase_of(table_ref, ends):
        spec = dot(table_ref[...], jnp.concatenate(ends, axis=1))
        spec = spec.astype(jnp.bfloat16).astype(jnp.float32)
        parts = [spec[:GZ], spec[GZ:]]
        phases = []
        for k in range(0, spec.shape[1], 2 * HALF):
            a, b = slice(k, k + HALF), slice(k + HALF, k + 2 * HALF)
            phase = normalised(parts[0][:, a], parts[1][:, a], parts[0][:, b], parts[1][:, b])
            phases.append(jnp.concatenate(phase, axis=0))
        return jnp.concatenate(phases, axis=1)

    keep = jnp.where(shared & both_real, 0.0, 1.0).astype(jnp.bfloat16)
    group = 8
    for p in range(0, total, group):
        ends = [load(q, end) * keep for q in range(p, p + group) for end in (0, 1)]
        w = dot(wzi_ref[...], phase_of(wz_ref, ends)).astype(jnp.bfloat16)
        for k, q in enumerate(range(p, p + group)):
            for s in range(slabs):
                out_ref[q // pairs_here + s * tiles, q % pairs_here] = w[
                    s * slab_rows : (s + 1) * slab_rows, k * HALF : (k + 1) * HALF
                ]

    @pl.when(both_real)
    def _():
        lane = lax.broadcasted_iota(jnp.int32, block, 1)
        ends = [jnp.zeros(block, jnp.bfloat16)] * 2
        for p in range(total):
            for end in (0, 1):
                ends[end] = jnp.where(lane == p, load(p, end)[:, 0:1], ends[end])
        w = dot(wzi_last_ref[...], phase_of(wz_last_ref, ends)).astype(jnp.bfloat16)
        for p in range(total):
            column = w[:, p : p + 1]
            for s in range(slabs):
                rows = slice(s * slab_rows, (s + 1) * slab_rows)
                at = (p // pairs_here + s * tiles, p % pairs_here)
                out_ref[at] = jnp.where(shared[rows], column[rows], out_ref[at])


def correlate(spread, pairs, place, slabs, tiles_here):
    devices, _, slab_rows, _ = spread.shape
    pairs_here = pairs.shape[1] * slabs // devices
    tables = z_tables()
    vmem = pl.BlockSpec(memory_space=pltpu.VMEM)
    smem = pl.BlockSpec(memory_space=pltpu.SMEM)
    return pl.pallas_call(
        functools.partial(correlate_kernel, slabs, tiles_here),
        in_specs=[smem, smem] + [vmem] * (1 + len(tables)),
        out_specs=vmem,
        out_shape=jax.ShapeDtypeStruct((devices, pairs_here, slab_rows, HALF), jnp.bfloat16),
        compiler_params=pltpu.CompilerParams(vmem_limit_bytes=VMEM_BYTES),
        name="correlate",
    )(pairs, place, spread, *(jnp.asarray(t) for t in tables))


def synthesise_kernel(in_ref, wx_ref, wy_ref, out_ref):
    zpart = out_ref.shape[1]
    units = zpart // PLANES
    block = (2 * zpart, HALF)
    lane0, imaginary = first_lane(block), imaginary_rows(block)
    sign = jnp.where(imaginary, -1.0, 1.0)
    groups = (units, 2 * PLANES, HALF)

    def at(j):
        return in_ref[j, 0].astype(jnp.float32)

    blocks = [None] * GX
    for j in (0, GX // 2):
        blocks[j] = at(j)
    for j in range(1, GX // 2):
        here, mirror = at(j), at(GX - j)
        swapped = pltpu.roll(mirror.reshape(groups), PLANES, 1).reshape(block)
        blocks[j] = jnp.where(lane0, here + swapped, here)
        blocks[GX - j] = jnp.where(lane0, sign * (here - swapped), mirror)
    stacked = jnp.concatenate(
        [
            jnp.concatenate([b[u * 2 * PLANES : (u + 1) * 2 * PLANES] for b in blocks], axis=0)
            for u in range(units)
        ],
        axis=1,
    ).astype(jnp.bfloat16)
    v = dot(wx_ref[...], stacked).astype(jnp.bfloat16)
    rows = PLANES * GX
    cells = [
        jnp.concatenate([v[:rows, k : k + HALF], v[rows:, k : k + HALF]], axis=1)
        for k in range(0, units * HALF, HALF)
    ]
    maps = dot(jnp.concatenate(cells, axis=0), wy_ref[...])
    out_ref[0] = maps.reshape(zpart, GX, GY)


def synthesise(returned):
    _, pairs_here, slab_rows, _ = returned.shape
    zpart = slab_rows // 2
    tables = (inverse_x_table(), half_y_inverse())
    return pl.pallas_call(
        synthesise_kernel,
        grid=(pairs_here, slab_rows // (2 * zpart)),
        in_specs=[pl.BlockSpec((GX, 1, 2 * zpart, HALF), lambda i, z: (0, i, z, 0))]
        + [pl.BlockSpec(t.shape, lambda i, z: (0, 0)) for t in tables],
        out_specs=pl.BlockSpec((1, zpart, GX, GY), lambda i, z: (i, z, 0, 0)),
        out_shape=jax.ShapeDtypeStruct((pairs_here, slab_rows // 2, GX, GY), jnp.float32),
        compiler_params=pltpu.CompilerParams(vmem_limit_bytes=VMEM_BYTES),
        name="synthesise",
    )(returned, *(jnp.asarray(t) for t in tables))


def shards(band, pairs, extents):
    tiles, slabs = lax.axis_size("tile"), lax.axis_size("zslab")
    zrows = band.shape[2]
    if tiles * slabs != GX or zrows % (4 * PLANES) or pairs.shape[0] % 8 or pairs.shape[0] % tiles:
        return general_shards(band, pairs, extents)
    pairs, extents = pairs.T, extents.T
    tile = lax.axis_index("tile").astype(jnp.int32)
    device = lax.axis_index("zslab").astype(jnp.int32) * tiles + tile
    spectra = analyse(band, pairs, extents, tile[None])
    spread = lax.all_to_all(spectra, ("zslab", "tile"), split_axis=0, concat_axis=0, tiled=True)
    w = correlate(spread, pairs, device[None], slabs, band.shape[0])
    returned = lax.all_to_all(w, ("zslab", "tile"), split_axis=0, concat_axis=0, tiled=True)
    return synthesise(returned)


def solution(mesh):
    placed = (P("tile", None, "zslab", None, None), P(), P())
    return jax.shard_map(
        shards,
        mesh=mesh,
        in_specs=placed,
        out_specs=P("tile", "zslab", None, None),
        check_vma=False,
    )
```

```python
import functools
import math


import jax
import jax.numpy as jnp
import numpy as np
from jax import lax
from jax.experimental import pallas as pl
from jax.experimental.pallas import tpu as pltpu
from jax.sharding import PartitionSpec as P

GX = 32
GY = 256
GZ = 128
FACES = 4


def dft_tables(length):
    indices = jnp.arange(length, dtype=jnp.int32)
    modular = indices[:, None] * indices[None, :] % length
    angles = modular.astype(jnp.float32) * (2.0 * math.pi / length)
    factor = 1.0 / math.sqrt(length)
    return (
        (jnp.cos(angles) * factor).astype(jnp.bfloat16),
        (jnp.sin(angles) * factor).astype(jnp.bfloat16),
    )


def product(form, left, right):
    return jnp.einsum(form, left, right, preferred_element_type=jnp.float32)


def reduce_resolution(image_volume, crop_bounds):
    row_mask = (
        jnp.arange(image_volume.shape[2], dtype=jnp.int32)[None, :] < crop_bounds[:, 0:1]
    ).astype(jnp.bfloat16)
    col_mask = (
        jnp.arange(image_volume.shape[3], dtype=jnp.int32)[None, :] < crop_bounds[:, 1:2]
    ).astype(jnp.bfloat16)
    masked = image_volume * row_mask[:, None, :, None] * col_mask[:, None, None, :]
    raw_cols = jnp.arange(image_volume.shape[3], dtype=jnp.int32)
    pooled_cols = jnp.arange(GY, dtype=jnp.int32)
    pooling = jnp.where(raw_cols[:, None] // 2 == pooled_cols[None, :], 0.5, 0.0).astype(
        jnp.bfloat16
    )
    along_pooled = product("szxy,yk->szxk", masked, pooling)
    shaped = along_pooled.reshape(image_volume.shape[0], image_volume.shape[1], GX, 2, GY)
    return (shaped[:, :, :, 0, :] + shaped[:, :, :, 1, :]).astype(jnp.bfloat16)


def cross_phase(owner_re, owner_im, pairs, tiles_here):
    first_dev = pairs[:, 0] // tiles_here
    first_pos = pairs[:, 0] % tiles_here * FACES + pairs[:, 1]
    second_tile_device = pairs[:, 2] // tiles_here
    second_pos = pairs[:, 2] % tiles_here * FACES + pairs[:, 3]
    first_re = owner_re[first_dev, :, first_pos].astype(jnp.float32)
    first_im = owner_im[first_dev, :, first_pos].astype(jnp.float32)
    second_re = owner_re[second_tile_device, :, second_pos].astype(jnp.float32)
    second_im = owner_im[second_tile_device, :, second_pos].astype(jnp.float32)
    cross_re = first_re * second_re + first_im * second_im
    cross_im = first_im * second_re - first_re * second_im
    scaled = jnp.sqrt(cross_re * cross_re + cross_im * cross_im + 1.0)
    return ((cross_re / scaled).astype(jnp.bfloat16), (cross_im / scaled).astype(jnp.bfloat16))


def inverse_z(phase_real_part, phase_im, tables_z):
    w_re = (
        product("pmjk,mz->pzjk", phase_real_part, tables_z[0])
        - product("pmjk,mz->pzjk", phase_im, tables_z[1])
    ).astype(jnp.bfloat16)
    w_im = (
        product("pmjk,mz->pzjk", phase_im, tables_z[0])
        + product("pmjk,mz->pzjk", phase_real_part, tables_z[1])
    ).astype(jnp.bfloat16)
    return (w_re, w_im)


def inverse_x(w_re, w_im, tables_x):
    v_re = (
        product("pzjk,jx->pzxk", w_re, tables_x[0]) - product("pzjk,jx->pzxk", w_im, tables_x[1])
    ).astype(jnp.bfloat16)
    v_im = (
        product("pzjk,jx->pzxk", w_im, tables_x[0]) + product("pzjk,jx->pzxk", w_re, tables_x[1])
    ).astype(jnp.bfloat16)
    return (v_re, v_im)


def general_shards(band, pairs, extents):
    tables_x = dft_tables(GX)
    tables_y = dft_tables(GY)
    tables_z = dft_tables(GZ)
    tiles_here = band.shape[0]
    slots = tiles_here * FACES
    zrows = band.shape[2]
    tile_pos = lax.axis_index("tile")
    global_slot = tile_pos * slots + jnp.arange(slots, dtype=jnp.int32)
    first_slot = pairs[:, 0] * FACES + pairs[:, 1]
    second_slot = pairs[:, 2] * FACES + pairs[:, 3]
    matches = (
        (first_slot[None, :] == global_slot[:, None])
        | (second_slot[None, :] == global_slot[:, None])
    ).astype(jnp.int32)
    crop_bounds = jnp.sum(matches[:, :, None] * extents[None, :, :], axis=1)
    image_volume = band.reshape(slots, zrows, 2 * GX, 2 * GY)
    reduced_volume = reduce_resolution(image_volume, crop_bounds)
    y_re = product("szxy,yk->szxk", reduced_volume, tables_y[0]).astype(jnp.bfloat16)
    y_im = (-product("szxy,yk->szxk", reduced_volume, tables_y[1])).astype(jnp.bfloat16)
    x_re = (
        product("szxk,xj->szjk", y_re, tables_x[0]) + product("szxk,xj->szjk", y_im, tables_x[1])
    ).astype(jnp.bfloat16)
    x_im = (
        product("szxk,xj->szjk", y_im, tables_x[0]) - product("szxk,xj->szjk", y_re, tables_x[1])
    ).astype(jnp.bfloat16)
    kx_part = GX // lax.axis_size("zslab")
    re_in = lax.all_to_all(x_re, "zslab", split_axis=2, concat_axis=1, tiled=True)
    im_in = lax.all_to_all(x_im, "zslab", split_axis=2, concat_axis=1, tiled=True)
    out_re = (
        product("szjk,zm->msjk", re_in, tables_z[0]) + product("szjk,zm->msjk", im_in, tables_z[1])
    ).astype(jnp.bfloat16)
    out_im = (
        product("szjk,zm->msjk", im_in, tables_z[0]) - product("szjk,zm->msjk", re_in, tables_z[1])
    ).astype(jnp.bfloat16)
    tile_count = lax.axis_size("tile")
    kz_part = GZ // tile_count
    spectra = (
        lax.all_to_all(out_re, "tile", split_axis=0, concat_axis=0, tiled=True),
        lax.all_to_all(out_im, "tile", split_axis=0, concat_axis=0, tiled=True),
    )
    owner_re = spectra[0].reshape(tile_count, kz_part, slots, kx_part, GY)
    owner_im = spectra[1].reshape(tile_count, kz_part, slots, kx_part, GY)
    phase_real_part, phase_im = cross_phase(owner_re, owner_im, pairs, tiles_here)
    returned = (
        lax.all_to_all(phase_real_part, "tile", split_axis=0, concat_axis=1, tiled=True),
        lax.all_to_all(phase_im, "tile", split_axis=0, concat_axis=1, tiled=True),
    )
    w_re, w_im = inverse_z(returned[0], returned[1], tables_z)
    v_re, v_im = inverse_x(
        lax.all_to_all(w_re, "zslab", split_axis=1, concat_axis=2, tiled=True),
        lax.all_to_all(w_im, "zslab", split_axis=1, concat_axis=2, tiled=True),
        tables_x,
    )
    return product("pzxk,ky->pzxy", v_re, tables_y[0]) - product("pzxk,ky->pzxy", v_im, tables_y[1])


HALF = GY // 2
PLANES = 4
VMEM_BYTES = 32 * 1024 * 1024


def host_tables(length):
    indices = np.arange(length, dtype=np.int32)
    modular = indices[:, None] * indices[None, :] % length
    angles = modular.astype(np.float32) * np.float32(2.0 * math.pi / length)
    factor = np.float32(1.0 / math.sqrt(length))
    return (
        (np.cos(angles) * factor).astype(jnp.bfloat16),
        (np.sin(angles) * factor).astype(jnp.bfloat16),
    )


def half_y_table():
    cosine, sine = host_tables(GY)
    imag = -sine[:, :HALF]
    imag[:, 0] = cosine[:, HALF]
    return np.concatenate([cosine[:, :HALF], imag], axis=1)


def paired_y_table():
    half = half_y_table() * np.array(0.5, jnp.bfloat16)
    table = np.zeros((2 * GY, 2 * GY), jnp.bfloat16)
    table[::2, :GY] = half
    table[1::2, GY:] = half
    return table


def half_y_inverse():
    cosine, sine = host_tables(GY)
    two = np.array(2.0, jnp.bfloat16)
    real = cosine[:HALF, :] * two
    real[0] = cosine[0]
    imag = -sine[:HALF, :] * two
    imag[0] = cosine[HALF]
    return np.concatenate([real, imag], axis=0)


def mirror_order():
    order = [0, GX // 2]
    for j in range(1, GX // 2):
        order += [j, GX - j]
    return order


def complex_blocks(length, sign):
    cosine, sine = (table.astype(np.float32) for table in host_tables(length))
    return np.array([[cosine, -sign * sine], [sign * sine, cosine]])


def forward_x_table():
    table = np.einsum("oijx,az->joaizx", complex_blocks(GX, -1), np.eye(PLANES))[mirror_order()]
    return table.reshape(2 * GX * PLANES, -1).astype(jnp.bfloat16)


def row_pair_table():
    raw = np.arange(2 * PLANES * GX)[None, :] // 2
    return (raw == np.arange(PLANES * GX)[:, None]).astype(jnp.bfloat16)


def inverse_x_table():
    table = np.einsum("oijx,az->oaxjiz", complex_blocks(GX, 1), np.eye(PLANES))
    return table.reshape(2 * PLANES * GX, -1).astype(jnp.bfloat16)


def z_rows():
    return np.arange(2 * GZ).reshape(2, GZ // PLANES, PLANES).transpose(1, 0, 2).reshape(-1)


def z_tables():
    forward, inverse = (
        complex_blocks(GZ, sign).transpose(0, 2, 1, 3).reshape(2 * GZ, 2 * GZ) for sign in (-1, 1)
    )
    none = np.zeros((2 * GZ, GZ), np.float32)
    forward_last = np.concatenate([none, forward[:, :GZ]], axis=1)
    inverse_last = np.concatenate([none.T, inverse[:GZ]], axis=0)
    order = z_rows()
    return [
        np.ascontiguousarray(table).astype(jnp.bfloat16)
        for table in (
            forward[:, order],
            inverse[order],
            forward_last[:, order],
            inverse_last[order],
        )
    ]


def imaginary_rows(shape):
    return lax.broadcasted_iota(jnp.int32, shape, 0) % (2 * PLANES) >= PLANES


def first_lane(shape):
    return lax.broadcasted_iota(jnp.int32, shape, 1) == 0


def dot(left, right):
    return jnp.dot(left, right, preferred_element_type=jnp.float32)


def analyse_kernel(
    pairs_ref,
    extents_ref,
    tile_ref,
    band_ref,
    wp_in_ref,
    wy_in_ref,
    wx_in_ref,
    out_ref,
    crop_ref,
    raw_ref,
    wp_ref,
    wy_ref,
    wx_ref,
    spec_ref,
    table_sems,
    raw_sems,
    spec_sems,
):
    slots, pieces = raw_sems.shape
    halves = spec_sems.shape[1]
    zpiece = raw_ref.shape[1] // pieces
    zhalf = raw_ref.shape[1] // halves

    def fetch(slot, piece):
        zs = pl.ds(piece * zpiece, zpiece)
        source = band_ref.at[slot // FACES, slot % FACES, zs]
        return pltpu.make_async_copy(source, raw_ref.at[slot, zs], raw_sems.at[slot, piece])

    def leave(slot, half):
        rows = pl.ds(half * 2 * zhalf, 2 * zhalf)
        return pltpu.make_async_copy(
            spec_ref.at[slot, half], out_ref.at[:, slot, rows], spec_sems.at[slot, half]
        )

    tables = [
        pltpu.make_async_copy(source, table, table_sems.at[k])
        for k, (source, table) in enumerate(
            ((wp_in_ref, wp_ref), (wy_in_ref, wy_ref), (wx_in_ref, wx_ref))
        )
    ]
    tables[0].start()
    for slot in range(slots):
        for piece in range(pieces):
            fetch(slot, piece).start()
            if slot == 0 and piece == 0:
                for copy in tables[1:]:
                    copy.start()

    for p in range(pairs_ref.shape[1]):
        for end in (0, 1):
            named = pairs_ref[2 * end, p] * FACES + pairs_ref[2 * end + 1, p] - tile_ref[0] * slots

            @pl.when((named >= 0) & (named < slots))
            def _():
                crop_ref[named, 0] = extents_ref[0, p]
                crop_ref[named, 1] = extents_ref[1, p]

    half_rows = PLANES // 2 * GX
    lane = lax.broadcasted_iota(jnp.int32, (half_rows, 128), 1)
    even_lane = lane % 2 == 0
    lanes = range(0, 2 * GY, 128)
    raw_row = lax.broadcasted_iota(jnp.int32, wp_ref.shape, 1) % (2 * GX)
    block = (2 * PLANES, HALF)
    lane0, imaginary = first_lane(block), imaginary_rows(block)
    sign = jnp.where(imaginary, -0.5, 0.5)
    for copy in tables:
        copy.wait()

    def transform(slot, half, down):
        y = dot(down, wy_ref[...]).astype(jnp.bfloat16).reshape(zhalf // PLANES, 2 * GX, 2 * GY)
        units = [
            jnp.concatenate([y[unit, :, k : k + HALF] for k in (0, GY, HALF, GY + HALF)], axis=0)
            for unit in range(zhalf // PLANES)
        ]
        spectra = dot(wx_ref[...], jnp.concatenate(units, axis=1))

        def at(n):
            rows = spectra[2 * PLANES * n : 2 * PLANES * (n + 1)]
            return [rows[:, k : k + HALF] for k in range(0, rows.shape[1], HALF)]

        def put(j, blocks):
            spec_ref[slot, half, j] = jnp.concatenate(blocks, axis=0).astype(jnp.bfloat16)

        put(0, at(0))
        put(GX // 2, at(1))
        for j in range(1, GX // 2):
            here, mirror = at(2 * j), at(2 * j + 1)
            put(j, [jnp.where(lane0, 0.5 * a + sign * b, a) for a, b in zip(here, mirror)])
            put(
                GX - j,
                [
                    jnp.where(lane0, pltpu.roll(0.5 * a - sign * b, PLANES, 0), b)
                    for a, b in zip(here, mirror)
                ],
            )

    @pl.loop(0, slots)
    def _(slot):
        across, along = crop_ref[slot, 0], crop_ref[slot, 1]
        wp = jnp.where(raw_row < across, wp_ref[...].astype(jnp.float32), 0.0).astype(jnp.bfloat16)
        lives = [jnp.where(k + lane < along, 1.0, 0.0) for k in lanes]

        def cells(z):
            rows = dot(wp, raw_ref[slot, z : z + PLANES].reshape(-1, 2 * GY))
            blocks = []
            for k, live in zip(lanes, lives):
                first = rows[:half_rows, k : k + 128] * live
                second = rows[half_rows:, k : k + 128] * live
                first = first + pltpu.roll(first, 127, 1)
                second = second + pltpu.roll(second, 1, 1)
                blocks.append(jnp.where(even_lane, first, second).astype(jnp.bfloat16))
            return jnp.concatenate(blocks, axis=1)

        for half in range(halves):
            down = []
            for piece in range(half * pieces // halves, (half + 1) * pieces // halves):
                fetch(slot, piece).wait()
                down += [cells(z) for z in range(piece * zpiece, (piece + 1) * zpiece, PLANES)]
            transform(slot, half, jnp.concatenate(down, axis=0))
            leave(slot, half).start()

    for slot in range(slots):
        for half in range(halves):
            leave(slot, half).wait()


def analyse(band, pairs, extents, tile):
    slots, zrows = band.shape[0] * FACES, band.shape[2]
    tables = (row_pair_table(), paired_y_table(), forward_x_table())
    halves = zrows // (4 * PLANES)
    smem = pl.BlockSpec(memory_space=pltpu.SMEM)
    anywhere = pl.BlockSpec(memory_space=pl.ANY)
    return pl.pallas_call(
        analyse_kernel,
        in_specs=[smem] * 3 + [anywhere] * (1 + len(tables)),
        out_specs=anywhere,
        out_shape=jax.ShapeDtypeStruct((GX, slots, 2 * zrows, HALF), jnp.bfloat16),
        scratch_shapes=[
            pltpu.SMEM((slots, 2), jnp.int32),
            pltpu.VMEM((slots, zrows, 2 * GX, 2 * GY), jnp.bfloat16),
            *[pltpu.VMEM(t.shape, jnp.bfloat16) for t in tables],
            pltpu.VMEM((slots, halves, GX, 8 * PLANES, HALF), jnp.bfloat16),
            pltpu.SemaphoreType.DMA((len(tables),)),
            pltpu.SemaphoreType.DMA((slots, 2 * halves)),
            pltpu.SemaphoreType.DMA((slots, halves)),
        ],
        compiler_params=pltpu.CompilerParams(vmem_limit_bytes=VMEM_BYTES + VMEM_BYTES * 3 // 4),
        name="analyse",
    )(pairs, extents, tile, band, *(jnp.asarray(t) for t in tables))


def normalised(a_re, a_im, b_re, b_im):
    cross_re = a_re * b_re + a_im * b_im
    cross_im = a_im * b_re - a_re * b_im
    scale = lax.rsqrt(cross_re * cross_re + cross_im * cross_im + 1.0)
    return (cross_re * scale).astype(jnp.bfloat16), (cross_im * scale).astype(jnp.bfloat16)


def correlate_kernel(
    slabs, tiles_here, pairs_ref, place_ref, in_ref, wz_ref, wzi_ref, wz_last_ref, wzi_last_ref, out_ref
):
    tiles = in_ref.shape[0] // slabs
    total = pairs_ref.shape[1]
    pairs_here = out_ref.shape[1]
    slab_rows = out_ref.shape[2]
    both_real = (place_ref[0] == 0) | (place_ref[0] == GX // 2)
    block = (2 * GZ, HALF)
    shared = first_lane(block) & imaginary_rows(block)

    def load(p, end):
        tile = pairs_ref[2 * end, p]
        row = tile // tiles_here
        pos = tile % tiles_here * FACES + pairs_ref[2 * end + 1, p]
        return jnp.concatenate([in_ref[row + s * tiles, pos] for s in range(slabs)], axis=0)

    def phase_of(table_ref, ends):
        spec = dot(table_ref[...], jnp.concatenate(ends, axis=1))
        spec = spec.astype(jnp.bfloat16).astype(jnp.float32)
        parts = [spec[:GZ], spec[GZ:]]
        phases = []
        for k in range(0, spec.shape[1], 2 * HALF):
            a, b = slice(k, k + HALF), slice(k + HALF, k + 2 * HALF)
            phase = normalised(parts[0][:, a], parts[1][:, a], parts[0][:, b], parts[1][:, b])
            phases.append(jnp.concatenate(phase, axis=0))
        return jnp.concatenate(phases, axis=1)

    keep = jnp.where(shared & both_real, 0.0, 1.0).astype(jnp.bfloat16)
    group = 8
    for p in range(0, total, group):
        ends = [load(q, end) * keep for q in range(p, p + group) for end in (0, 1)]
        w = dot(wzi_ref[...], phase_of(wz_ref, ends)).astype(jnp.bfloat16)
        for k, q in enumerate(range(p, p + group)):
            for s in range(slabs):
                out_ref[q // pairs_here + s * tiles, q % pairs_here] = w[
                    s * slab_rows : (s + 1) * slab_rows, k * HALF : (k + 1) * HALF
                ]

    @pl.when(both_real)
    def _():
        lane = lax.broadcasted_iota(jnp.int32, block, 1)
        ends = [jnp.zeros(block, jnp.bfloat16)] * 2
        for p in range(total):
            for end in (0, 1):
                ends[end] = jnp.where(lane == p, load(p, end)[:, 0:1], ends[end])
        w = dot(wzi_last_ref[...], phase_of(wz_last_ref, ends)).astype(jnp.bfloat16)
        for p in range(total):
            column = w[:, p : p + 1]
            for s in range(slabs):
                rows = slice(s * slab_rows, (s + 1) * slab_rows)
                at = (p // pairs_here + s * tiles, p % pairs_here)
                out_ref[at] = jnp.where(shared[rows], column[rows], out_ref[at])


def correlate(spread, pairs, place, slabs, tiles_here):
    devices, _, slab_rows, _ = spread.shape
    pairs_here = pairs.shape[1] * slabs // devices
    tables = z_tables()
    vmem = pl.BlockSpec(memory_space=pltpu.VMEM)
    smem = pl.BlockSpec(memory_space=pltpu.SMEM)
    return pl.pallas_call(
        functools.partial(correlate_kernel, slabs, tiles_here),
        in_specs=[smem, smem] + [vmem] * (1 + len(tables)),
        out_specs=vmem,
        out_shape=jax.ShapeDtypeStruct((devices, pairs_here, slab_rows, HALF), jnp.bfloat16),
        compiler_params=pltpu.CompilerParams(vmem_limit_bytes=VMEM_BYTES),
        name="correlate",
    )(pairs, place, spread, *(jnp.asarray(t) for t in tables))


def synthesise_kernel(in_ref, wx_ref, wy_ref, out_ref):
    zpart = out_ref.shape[1]
    units = zpart // PLANES
    block = (2 * zpart, HALF)
    lane0, imaginary = first_lane(block), imaginary_rows(block)
    sign = jnp.where(imaginary, -1.0, 1.0)
    groups = (units, 2 * PLANES, HALF)

    def at(j):
        return in_ref[j, 0].astype(jnp.float32)

    blocks = [None] * GX
    for j in (0, GX // 2):
        blocks[j] = at(j)
    for j in range(1, GX // 2):
        here, mirror = at(j), at(GX - j)
        swapped = pltpu.roll(mirror.reshape(groups), PLANES, 1).reshape(block)
        blocks[j] = jnp.where(lane0, here + swapped, here)
        blocks[GX - j] = jnp.where(lane0, sign * (here - swapped), mirror)
    stacked = jnp.concatenate(
        [
            jnp.concatenate([b[u * 2 * PLANES : (u + 1) * 2 * PLANES] for b in blocks], axis=0)
            for u in range(units)
        ],
        axis=1,
    ).astype(jnp.bfloat16)
    v = dot(wx_ref[...], stacked).astype(jnp.bfloat16)
    rows = PLANES * GX
    cells = [
        jnp.concatenate([v[:rows, k : k + HALF], v[rows:, k : k + HALF]], axis=1)
        for k in range(0, units * HALF, HALF)
    ]
    maps = dot(jnp.concatenate(cells, axis=0), wy_ref[...])
    out_ref[0] = maps.reshape(zpart, GX, GY)


def synthesise(returned):
    _, pairs_here, slab_rows, _ = returned.shape
    zpart = slab_rows // 2
    tables = (inverse_x_table(), half_y_inverse())
    return pl.pallas_call(
        synthesise_kernel,
        grid=(pairs_here, slab_rows // (2 * zpart)),
        in_specs=[pl.BlockSpec((GX, 1, 2 * zpart, HALF), lambda i, z: (0, i, z, 0))]
        + [pl.BlockSpec(t.shape, lambda i, z: (0, 0)) for t in tables],
        out_specs=pl.BlockSpec((1, zpart, GX, GY), lambda i, z: (i, z, 0, 0)),
        out_shape=jax.ShapeDtypeStruct((pairs_here, slab_rows // 2, GX, GY), jnp.float32),
        compiler_params=pltpu.CompilerParams(vmem_limit_bytes=VMEM_BYTES),
        name="synthesise",
    )(returned, *(jnp.asarray(t) for t in tables))


def shards(band, pairs, extents):
    tiles, slabs = lax.axis_size("tile"), lax.axis_size("zslab")
    zrows = band.shape[2]
    if tiles * slabs != GX or zrows % (4 * PLANES) or pairs.shape[0] % 8 or pairs.shape[0] % tiles:
        return general_shards(band, pairs, extents)
    pairs, extents = pairs.T, extents.T
    tile = lax.axis_index("tile").astype(jnp.int32)
    device = lax.axis_index("zslab").astype(jnp.int32) * tiles + tile
    spectra = analyse(band, pairs, extents, tile[None])
    spread = lax.all_to_all(spectra, ("zslab", "tile"), split_axis=0, concat_axis=0, tiled=True)
    w = correlate(spread, pairs, device[None], slabs, band.shape[0])
    returned = lax.all_to_all(w, ("zslab", "tile"), split_axis=0, concat_axis=0, tiled=True)
    return synthesise(returned)


def solution(mesh):
    placed = (P("tile", None, "zslab", None, None), P(), P())
    return jax.shard_map(
        shards,
        mesh=mesh,
        in_specs=placed,
        out_specs=P("tile", "zslab", None, None),
        check_vma=False,
    )
```

```python
import functools
import math


import jax
import jax.numpy as jnp
import numpy as np
from jax import lax
from jax.experimental import pallas as pl
from jax.experimental.pallas import tpu as pltpu
from jax.sharding import PartitionSpec as P

GX = 32
GY = 256
GZ = 128
FACES = 4


def dft_tables(length):
    indices = jnp.arange(length, dtype=jnp.int32)
    modular = indices[:, None] * indices[None, :] % length
    angles = modular.astype(jnp.float32) * (2.0 * math.pi / length)
    factor = 1.0 / math.sqrt(length)
    return (
        (jnp.cos(angles) * factor).astype(jnp.bfloat16),
        (jnp.sin(angles) * factor).astype(jnp.bfloat16),
    )


def product(form, left, right):
    return jnp.einsum(form, left, right, preferred_element_type=jnp.float32)


def reduce_resolution(image_volume, crop_bounds):
    row_mask = (
        jnp.arange(image_volume.shape[2], dtype=jnp.int32)[None, :] < crop_bounds[:, 0:1]
    ).astype(jnp.bfloat16)
    col_mask = (
        jnp.arange(image_volume.shape[3], dtype=jnp.int32)[None, :] < crop_bounds[:, 1:2]
    ).astype(jnp.bfloat16)
    masked = image_volume * row_mask[:, None, :, None] * col_mask[:, None, None, :]
    raw_cols = jnp.arange(image_volume.shape[3], dtype=jnp.int32)
    pooled_cols = jnp.arange(GY, dtype=jnp.int32)
    pooling = jnp.where(raw_cols[:, None] // 2 == pooled_cols[None, :], 0.5, 0.0).astype(
        jnp.bfloat16
    )
    along_pooled = product("szxy,yk->szxk", masked, pooling)
    shaped = along_pooled.reshape(image_volume.shape[0], image_volume.shape[1], GX, 2, GY)
    return (shaped[:, :, :, 0, :] + shaped[:, :, :, 1, :]).astype(jnp.bfloat16)


def cross_phase(owner_re, owner_im, pairs, tiles_here):
    first_dev = pairs[:, 0] // tiles_here
    first_pos = pairs[:, 0] % tiles_here * FACES + pairs[:, 1]
    second_tile_device = pairs[:, 2] // tiles_here
    second_pos = pairs[:, 2] % tiles_here * FACES + pairs[:, 3]
    first_re = owner_re[first_dev, :, first_pos].astype(jnp.float32)
    first_im = owner_im[first_dev, :, first_pos].astype(jnp.float32)
    second_re = owner_re[second_tile_device, :, second_pos].astype(jnp.float32)
    second_im = owner_im[second_tile_device, :, second_pos].astype(jnp.float32)
    cross_re = first_re * second_re + first_im * second_im
    cross_im = first_im * second_re - first_re * second_im
    scaled = jnp.sqrt(cross_re * cross_re + cross_im * cross_im + 1.0)
    return ((cross_re / scaled).astype(jnp.bfloat16), (cross_im / scaled).astype(jnp.bfloat16))


def inverse_z(phase_real_part, phase_im, tables_z):
    w_re = (
        product("pmjk,mz->pzjk", phase_real_part, tables_z[0])
        - product("pmjk,mz->pzjk", phase_im, tables_z[1])
    ).astype(jnp.bfloat16)
    w_im = (
        product("pmjk,mz->pzjk", phase_im, tables_z[0])
        + product("pmjk,mz->pzjk", phase_real_part, tables_z[1])
    ).astype(jnp.bfloat16)
    return (w_re, w_im)


def inverse_x(w_re, w_im, tables_x):
    v_re = (
        product("pzjk,jx->pzxk", w_re, tables_x[0]) - product("pzjk,jx->pzxk", w_im, tables_x[1])
    ).astype(jnp.bfloat16)
    v_im = (
        product("pzjk,jx->pzxk", w_im, tables_x[0]) + product("pzjk,jx->pzxk", w_re, tables_x[1])
    ).astype(jnp.bfloat16)
    return (v_re, v_im)


def general_shards(band, pairs, extents):
    tables_x = dft_tables(GX)
    tables_y = dft_tables(GY)
    tables_z = dft_tables(GZ)
    tiles_here = band.shape[0]
    slots = tiles_here * FACES
    zrows = band.shape[2]
    tile_pos = lax.axis_index("tile")
    global_slot = tile_pos * slots + jnp.arange(slots, dtype=jnp.int32)
    first_slot = pairs[:, 0] * FACES + pairs[:, 1]
    second_slot = pairs[:, 2] * FACES + pairs[:, 3]
    matches = (
        (first_slot[None, :] == global_slot[:, None])
        | (second_slot[None, :] == global_slot[:, None])
    ).astype(jnp.int32)
    crop_bounds = jnp.sum(matches[:, :, None] * extents[None, :, :], axis=1)
    image_volume = band.reshape(slots, zrows, 2 * GX, 2 * GY)
    reduced_volume = reduce_resolution(image_volume, crop_bounds)
    y_re = product("szxy,yk->szxk", reduced_volume, tables_y[0]).astype(jnp.bfloat16)
    y_im = (-product("szxy,yk->szxk", reduced_volume, tables_y[1])).astype(jnp.bfloat16)
    x_re = (
        product("szxk,xj->szjk", y_re, tables_x[0]) + product("szxk,xj->szjk", y_im, tables_x[1])
    ).astype(jnp.bfloat16)
    x_im = (
        product("szxk,xj->szjk", y_im, tables_x[0]) - product("szxk,xj->szjk", y_re, tables_x[1])
    ).astype(jnp.bfloat16)
    kx_part = GX // lax.axis_size("zslab")
    re_in = lax.all_to_all(x_re, "zslab", split_axis=2, concat_axis=1, tiled=True)
    im_in = lax.all_to_all(x_im, "zslab", split_axis=2, concat_axis=1, tiled=True)
    out_re = (
        product("szjk,zm->msjk", re_in, tables_z[0]) + product("szjk,zm->msjk", im_in, tables_z[1])
    ).astype(jnp.bfloat16)
    out_im = (
        product("szjk,zm->msjk", im_in, tables_z[0]) - product("szjk,zm->msjk", re_in, tables_z[1])
    ).astype(jnp.bfloat16)
    tile_count = lax.axis_size("tile")
    kz_part = GZ // tile_count
    spectra = (
        lax.all_to_all(out_re, "tile", split_axis=0, concat_axis=0, tiled=True),
        lax.all_to_all(out_im, "tile", split_axis=0, concat_axis=0, tiled=True),
    )
    owner_re = spectra[0].reshape(tile_count, kz_part, slots, kx_part, GY)
    owner_im = spectra[1].reshape(tile_count, kz_part, slots, kx_part, GY)
    phase_real_part, phase_im = cross_phase(owner_re, owner_im, pairs, tiles_here)
    returned = (
        lax.all_to_all(phase_real_part, "tile", split_axis=0, concat_axis=1, tiled=True),
        lax.all_to_all(phase_im, "tile", split_axis=0, concat_axis=1, tiled=True),
    )
    w_re, w_im = inverse_z(returned[0], returned[1], tables_z)
    v_re, v_im = inverse_x(
        lax.all_to_all(w_re, "zslab", split_axis=1, concat_axis=2, tiled=True),
        lax.all_to_all(w_im, "zslab", split_axis=1, concat_axis=2, tiled=True),
        tables_x,
    )
    return product("pzxk,ky->pzxy", v_re, tables_y[0]) - product("pzxk,ky->pzxy", v_im, tables_y[1])


HALF = GY // 2
PLANES = 4
VMEM_BYTES = 32 * 1024 * 1024


def host_tables(length):
    indices = np.arange(length, dtype=np.int32)
    modular = indices[:, None] * indices[None, :] % length
    angles = modular.astype(np.float32) * np.float32(2.0 * math.pi / length)
    factor = np.float32(1.0 / math.sqrt(length))
    return (
        (np.cos(angles) * factor).astype(jnp.bfloat16),
        (np.sin(angles) * factor).astype(jnp.bfloat16),
    )


def half_y_table():
    cosine, sine = host_tables(GY)
    imag = -sine[:, :HALF]
    imag[:, 0] = cosine[:, HALF]
    return np.concatenate([cosine[:, :HALF], imag], axis=1)


def paired_y_table():
    half = half_y_table() * np.array(0.5, jnp.bfloat16)
    table = np.zeros((2 * GY, 2 * GY), jnp.bfloat16)
    table[::2, :GY] = half
    table[1::2, GY:] = half
    return table


def half_y_inverse():
    cosine, sine = host_tables(GY)
    two = np.array(2.0, jnp.bfloat16)
    real = cosine[:HALF, :] * two
    real[0] = cosine[0]
    imag = -sine[:HALF, :] * two
    imag[0] = cosine[HALF]
    return np.concatenate([real, imag], axis=0)


def mirror_order():
    order = [0, GX // 2]
    for j in range(1, GX // 2):
        order += [j, GX - j]
    return order


def complex_blocks(length, sign):
    cosine, sine = (table.astype(np.float32) for table in host_tables(length))
    return np.array([[cosine, -sign * sine], [sign * sine, cosine]])


def forward_x_table():
    table = np.einsum("oijx,az->joaizx", complex_blocks(GX, -1), np.eye(PLANES))[mirror_order()]
    table = table.reshape(2 * GX * PLANES, 2, PLANES // 2, 2, GX).transpose(0, 1, 2, 4, 3)
    return table.reshape(2 * GX * PLANES, -1).astype(jnp.bfloat16)


def inverse_x_table():
    table = np.einsum("oijx,az->oaxjiz", complex_blocks(GX, 1), np.eye(PLANES))
    return table.reshape(2 * PLANES * GX, -1).astype(jnp.bfloat16)


def z_rows():
    return np.arange(2 * GZ).reshape(2, GZ // PLANES, PLANES).transpose(1, 0, 2).reshape(-1)


def z_tables():
    forward, inverse = (
        complex_blocks(GZ, sign).transpose(0, 2, 1, 3).reshape(2 * GZ, 2 * GZ) for sign in (-1, 1)
    )
    none = np.zeros((2 * GZ, GZ), np.float32)
    forward_last = np.concatenate([none, forward[:, :GZ]], axis=1)
    inverse_last = np.concatenate([none.T, inverse[:GZ]], axis=0)
    order = z_rows()
    return [
        np.ascontiguousarray(table).astype(jnp.bfloat16)
        for table in (
            forward[:, order],
            inverse[order],
            forward_last[:, order],
            inverse_last[order],
        )
    ]


def imaginary_rows(shape):
    return lax.broadcasted_iota(jnp.int32, shape, 0) % (2 * PLANES) >= PLANES


def first_lane(shape):
    return lax.broadcasted_iota(jnp.int32, shape, 1) == 0


def dot(left, right):
    return jnp.dot(left, right, preferred_element_type=jnp.float32)


def analyse_kernel(
    slots,
    pairs_ref,
    extents_ref,
    tile_ref,
    band_ref,
    wy_ref,
    wx_ref,
    out_ref,
    crop_ref,
    down_ref,
):
    step = pl.program_id(0)
    slot = jnp.minimum(step, slots - 1)

    @pl.when(slot == 0)
    def _():
        for p in range(pairs_ref.shape[1]):
            for end in (0, 1):
                named = pairs_ref[2 * end, p] * FACES + pairs_ref[2 * end + 1, p] - tile_ref[0] * slots

                @pl.when((named >= 0) & (named < slots))
                def _():
                    crop_ref[named, 0] = extents_ref[0, p]
                    crop_ref[named, 1] = extents_ref[1, p]

    across, along = crop_ref[slot, 0], crop_ref[slot, 1]

    def alternate(first, second):
        first = first + pltpu.roll(first, 127, 1)
        second = second + pltpu.roll(second, 1, 1)
        return jnp.where(even_lane, first, second).astype(jnp.bfloat16)

    row = lax.broadcasted_iota(jnp.int32, (2 * GX, 128), 0)
    lane = lax.broadcasted_iota(jnp.int32, (2 * GX, 128), 1)
    even, even_lane = row % 2 == 0, lane % 2 == 0
    groups = (2 * GX // 8, 8, 128)
    lanes = range(0, 2 * GY, 128)
    lives = [jnp.where((row < across) & (k + lane < along), 1.0, 0.0) for k in lanes]
    block = (2 * PLANES, HALF)
    lane0, imaginary = first_lane(block), imaginary_rows(block)
    sign = jnp.where(imaginary, -0.5, 0.5)

    def row_pairs(z, k, shift):
        raw = band_ref[0, 0, z, :, k : k + 128].astype(jnp.float32) * lives[k // 128]
        return raw + pltpu.roll(raw.reshape(groups), shift, 1).reshape(raw.shape)

    def woven(z, k):
        return jnp.where(even, row_pairs(z, k, 7), row_pairs(z + 1, k, 1))

    def cells(z):
        return jnp.concatenate([alternate(woven(z, k), woven(z + 2, k)) for k in lanes], axis=1)

    zrows = band_ref.shape[2]

    def pool():
        for z in range(0, zrows, PLANES):
            unit = z // PLANES * 2 * GX
            down_ref[unit : unit + 2 * GX] = cells(z)

    def along_y():
        return dot(down_ref[...], wy_ref[...]).astype(jnp.bfloat16)

    def along_x(y):
        y = y.reshape(zrows // PLANES, 2 * GX, 2 * GY)
        units = [
            jnp.concatenate([y[unit, :, k : k + HALF] for k in (0, GY, HALF, GY + HALF)], axis=0)
            for unit in range(zrows // PLANES)
        ]
        spectra = dot(wx_ref[...], jnp.concatenate(units, axis=1))

        def at(n):
            rows = spectra[2 * PLANES * n : 2 * PLANES * (n + 1)]
            return [rows[:, k : k + HALF] for k in range(0, rows.shape[1], HALF)]

        def put(j, blocks):
            out_ref[j, 0] = jnp.concatenate(blocks, axis=0).astype(jnp.bfloat16)

        put(0, at(0))
        put(GX // 2, at(1))
        for j in range(1, GX // 2):
            here, mirror = at(2 * j), at(2 * j + 1)
            put(j, [jnp.where(lane0, 0.5 * a + sign * b, a) for a, b in zip(here, mirror)])
            put(
                GX - j,
                [
                    jnp.where(lane0, pltpu.roll(0.5 * a - sign * b, PLANES, 0), b)
                    for a, b in zip(here, mirror)
                ],
            )

    @pl.when(step == 0)
    def _():
        pool()

    @pl.when((step > 0) & (step < slots))
    def _():
        y = along_y()
        pool()
        along_x(y)

    @pl.when(step == slots)
    def _():
        along_x(along_y())


def analyse(band, pairs, extents, tile):
    slots, zrows = band.shape[0] * FACES, band.shape[2]
    tables = (paired_y_table(), forward_x_table())
    whole = [pl.BlockSpec(t.shape, lambda i, *_: (0, 0)) for t in tables]
    return pl.pallas_call(
        functools.partial(analyse_kernel, slots),
        grid_spec=pltpu.PrefetchScalarGridSpec(
            num_scalar_prefetch=3,
            grid=(slots + 1,),
            in_specs=[
                pl.BlockSpec(
                    (1, 1, zrows, 2 * GX, 2 * GY),
                    lambda i, *_: (
                        jnp.minimum(i, slots - 1) // FACES,
                        jnp.minimum(i, slots - 1) % FACES,
                        0,
                        0,
                        0,
                    ),
                )
            ]
            + whole,
            out_specs=pl.BlockSpec(
                (GX, 1, 2 * zrows, HALF), lambda i, *_: (0, jnp.maximum(i - 1, 0), 0, 0)
            ),
            scratch_shapes=[
                pltpu.SMEM((slots, 2), jnp.int32),
                pltpu.VMEM((zrows // PLANES * 2 * GX, 2 * GY), jnp.bfloat16),
            ],
        ),
        out_shape=jax.ShapeDtypeStruct((GX, slots, 2 * zrows, HALF), jnp.bfloat16),
        compiler_params=pltpu.CompilerParams(vmem_limit_bytes=VMEM_BYTES + VMEM_BYTES * 3 // 4),
        name="analyse",
    )(pairs, extents, tile, band, *(jnp.asarray(t) for t in tables))


def normalised(a_re, a_im, b_re, b_im):
    cross_re = a_re * b_re + a_im * b_im
    cross_im = a_im * b_re - a_re * b_im
    scale = lax.rsqrt(cross_re * cross_re + cross_im * cross_im + 1.0)
    return (cross_re * scale).astype(jnp.bfloat16), (cross_im * scale).astype(jnp.bfloat16)


def correlate_kernel(
    slabs, tiles_here, pairs_ref, place_ref, in_ref, wz_ref, wzi_ref, wz_last_ref, wzi_last_ref, out_ref
):
    tiles = in_ref.shape[0] // slabs
    total = pairs_ref.shape[1]
    pairs_here = out_ref.shape[1]
    slab_rows = out_ref.shape[2]
    both_real = (place_ref[0] == 0) | (place_ref[0] == GX // 2)
    block = (2 * GZ, HALF)
    shared = first_lane(block) & imaginary_rows(block)

    def load(p, end):
        tile = pairs_ref[2 * end, p]
        row = tile // tiles_here
        pos = tile % tiles_here * FACES + pairs_ref[2 * end + 1, p]
        return jnp.concatenate([in_ref[row + s * tiles, pos] for s in range(slabs)], axis=0)

    def phase_of(table_ref, ends):
        spec = dot(table_ref[...], jnp.concatenate(ends, axis=1))
        spec = spec.astype(jnp.bfloat16).astype(jnp.float32)
        parts = [spec[:GZ], spec[GZ:]]
        phases = []
        for k in range(0, spec.shape[1], 2 * HALF):
            a, b = slice(k, k + HALF), slice(k + HALF, k + 2 * HALF)
            phase = normalised(parts[0][:, a], parts[1][:, a], parts[0][:, b], parts[1][:, b])
            phases.append(jnp.concatenate(phase, axis=0))
        return jnp.concatenate(phases, axis=1)

    keep = jnp.where(shared & both_real, 0.0, 1.0).astype(jnp.bfloat16)
    group = 8
    for p in range(0, total, group):
        ends = [load(q, end) * keep for q in range(p, p + group) for end in (0, 1)]
        w = dot(wzi_ref[...], phase_of(wz_ref, ends)).astype(jnp.bfloat16)
        for k, q in enumerate(range(p, p + group)):
            for s in range(slabs):
                out_ref[q // pairs_here + s * tiles, q % pairs_here] = w[
                    s * slab_rows : (s + 1) * slab_rows, k * HALF : (k + 1) * HALF
                ]

    @pl.when(both_real)
    def _():
        lane = lax.broadcasted_iota(jnp.int32, block, 1)
        ends = [jnp.zeros(block, jnp.bfloat16)] * 2
        for p in range(total):
            for end in (0, 1):
                ends[end] = jnp.where(lane == p, load(p, end)[:, 0:1], ends[end])
        w = dot(wzi_last_ref[...], phase_of(wz_last_ref, ends)).astype(jnp.bfloat16)
        for p in range(total):
            column = w[:, p : p + 1]
            for s in range(slabs):
                rows = slice(s * slab_rows, (s + 1) * slab_rows)
                at = (p // pairs_here + s * tiles, p % pairs_here)
                out_ref[at] = jnp.where(shared[rows], column[rows], out_ref[at])


def correlate(spread, pairs, place, slabs, tiles_here):
    devices, _, slab_rows, _ = spread.shape
    pairs_here = pairs.shape[1] * slabs // devices
    tables = z_tables()
    vmem = pl.BlockSpec(memory_space=pltpu.VMEM)
    smem = pl.BlockSpec(memory_space=pltpu.SMEM)
    return pl.pallas_call(
        functools.partial(correlate_kernel, slabs, tiles_here),
        in_specs=[smem, smem] + [vmem] * (1 + len(tables)),
        out_specs=vmem,
        out_shape=jax.ShapeDtypeStruct((devices, pairs_here, slab_rows, HALF), jnp.bfloat16),
        compiler_params=pltpu.CompilerParams(vmem_limit_bytes=VMEM_BYTES),
        name="correlate",
    )(pairs, place, spread, *(jnp.asarray(t) for t in tables))


def synthesise_kernel(in_ref, wx_ref, wy_ref, out_ref):
    zpart = out_ref.shape[1]
    units = zpart // PLANES
    block = (2 * zpart, HALF)
    lane0, imaginary = first_lane(block), imaginary_rows(block)
    sign = jnp.where(imaginary, -1.0, 1.0)
    groups = (units, 2 * PLANES, HALF)

    def at(j):
        return in_ref[j, 0].astype(jnp.float32)

    blocks = [None] * GX
    for j in (0, GX // 2):
        blocks[j] = at(j)
    for j in range(1, GX // 2):
        here, mirror = at(j), at(GX - j)
        swapped = pltpu.roll(mirror.reshape(groups), PLANES, 1).reshape(block)
        blocks[j] = jnp.where(lane0, here + swapped, here)
        blocks[GX - j] = jnp.where(lane0, sign * (here - swapped), mirror)
    stacked = jnp.concatenate(
        [
            jnp.concatenate([b[u * 2 * PLANES : (u + 1) * 2 * PLANES] for b in blocks], axis=0)
            for u in range(units)
        ],
        axis=1,
    ).astype(jnp.bfloat16)
    v = dot(wx_ref[...], stacked).astype(jnp.bfloat16)
    rows = PLANES * GX
    cells = [
        jnp.concatenate([v[:rows, k : k + HALF], v[rows:, k : k + HALF]], axis=1)
        for k in range(0, units * HALF, HALF)
    ]
    maps = dot(jnp.concatenate(cells, axis=0), wy_ref[...])
    out_ref[0] = maps.reshape(zpart, GX, GY)


def synthesise(returned):
    _, pairs_here, slab_rows, _ = returned.shape
    zpart = slab_rows // 2
    tables = (inverse_x_table(), half_y_inverse())
    return pl.pallas_call(
        synthesise_kernel,
        grid=(pairs_here, slab_rows // (2 * zpart)),
        in_specs=[pl.BlockSpec((GX, 1, 2 * zpart, HALF), lambda i, z: (0, i, z, 0))]
        + [pl.BlockSpec(t.shape, lambda i, z: (0, 0)) for t in tables],
        out_specs=pl.BlockSpec((1, zpart, GX, GY), lambda i, z: (i, z, 0, 0)),
        out_shape=jax.ShapeDtypeStruct((pairs_here, slab_rows // 2, GX, GY), jnp.float32),
        compiler_params=pltpu.CompilerParams(vmem_limit_bytes=VMEM_BYTES),
        name="synthesise",
    )(returned, *(jnp.asarray(t) for t in tables))


def shards(band, pairs, extents):
    tiles, slabs = lax.axis_size("tile"), lax.axis_size("zslab")
    zrows = band.shape[2]
    if tiles * slabs != GX or zrows % (4 * PLANES) or pairs.shape[0] % 8 or pairs.shape[0] % tiles:
        return general_shards(band, pairs, extents)
    pairs, extents = pairs.T, extents.T
    tile = lax.axis_index("tile").astype(jnp.int32)
    device = lax.axis_index("zslab").astype(jnp.int32) * tiles + tile
    spectra = analyse(band, pairs, extents, tile[None])
    spread = lax.all_to_all(spectra, ("zslab", "tile"), split_axis=0, concat_axis=0, tiled=True)
    w = correlate(spread, pairs, device[None], slabs, band.shape[0])
    returned = lax.all_to_all(w, ("zslab", "tile"), split_axis=0, concat_axis=0, tiled=True)
    return synthesise(returned)


def solution(mesh):
    placed = (P("tile", None, "zslab", None, None), P(), P())
    return jax.shard_map(
        shards,
        mesh=mesh,
        in_specs=placed,
        out_specs=P("tile", "zslab", None, None),
        check_vma=False,
    )
```

```python
import functools
import math


import jax
import jax.numpy as jnp
import numpy as np
from jax import lax
from jax.experimental import pallas as pl
from jax.experimental.pallas import tpu as pltpu
from jax.sharding import PartitionSpec as P

GX = 32
GY = 256
GZ = 128
FACES = 4


def dft_tables(length):
    indices = jnp.arange(length, dtype=jnp.int32)
    modular = indices[:, None] * indices[None, :] % length
    angles = modular.astype(jnp.float32) * (2.0 * math.pi / length)
    factor = 1.0 / math.sqrt(length)
    return (
        (jnp.cos(angles) * factor).astype(jnp.bfloat16),
        (jnp.sin(angles) * factor).astype(jnp.bfloat16),
    )


def product(form, left, right):
    return jnp.einsum(form, left, right, preferred_element_type=jnp.float32)


def reduce_resolution(image_volume, crop_bounds):
    row_mask = (
        jnp.arange(image_volume.shape[2], dtype=jnp.int32)[None, :] < crop_bounds[:, 0:1]
    ).astype(jnp.bfloat16)
    col_mask = (
        jnp.arange(image_volume.shape[3], dtype=jnp.int32)[None, :] < crop_bounds[:, 1:2]
    ).astype(jnp.bfloat16)
    masked = image_volume * row_mask[:, None, :, None] * col_mask[:, None, None, :]
    raw_cols = jnp.arange(image_volume.shape[3], dtype=jnp.int32)
    pooled_cols = jnp.arange(GY, dtype=jnp.int32)
    pooling = jnp.where(raw_cols[:, None] // 2 == pooled_cols[None, :], 0.5, 0.0).astype(
        jnp.bfloat16
    )
    along_pooled = product("szxy,yk->szxk", masked, pooling)
    shaped = along_pooled.reshape(image_volume.shape[0], image_volume.shape[1], GX, 2, GY)
    return (shaped[:, :, :, 0, :] + shaped[:, :, :, 1, :]).astype(jnp.bfloat16)


def cross_phase(owner_re, owner_im, pairs, tiles_here):
    first_dev = pairs[:, 0] // tiles_here
    first_pos = pairs[:, 0] % tiles_here * FACES + pairs[:, 1]
    second_tile_device = pairs[:, 2] // tiles_here
    second_pos = pairs[:, 2] % tiles_here * FACES + pairs[:, 3]
    first_re = owner_re[first_dev, :, first_pos].astype(jnp.float32)
    first_im = owner_im[first_dev, :, first_pos].astype(jnp.float32)
    second_re = owner_re[second_tile_device, :, second_pos].astype(jnp.float32)
    second_im = owner_im[second_tile_device, :, second_pos].astype(jnp.float32)
    cross_re = first_re * second_re + first_im * second_im
    cross_im = first_im * second_re - first_re * second_im
    scaled = jnp.sqrt(cross_re * cross_re + cross_im * cross_im + 1.0)
    return ((cross_re / scaled).astype(jnp.bfloat16), (cross_im / scaled).astype(jnp.bfloat16))


def inverse_z(phase_real_part, phase_im, tables_z):
    w_re = (
        product("pmjk,mz->pzjk", phase_real_part, tables_z[0])
        - product("pmjk,mz->pzjk", phase_im, tables_z[1])
    ).astype(jnp.bfloat16)
    w_im = (
        product("pmjk,mz->pzjk", phase_im, tables_z[0])
        + product("pmjk,mz->pzjk", phase_real_part, tables_z[1])
    ).astype(jnp.bfloat16)
    return (w_re, w_im)


def inverse_x(w_re, w_im, tables_x):
    v_re = (
        product("pzjk,jx->pzxk", w_re, tables_x[0]) - product("pzjk,jx->pzxk", w_im, tables_x[1])
    ).astype(jnp.bfloat16)
    v_im = (
        product("pzjk,jx->pzxk", w_im, tables_x[0]) + product("pzjk,jx->pzxk", w_re, tables_x[1])
    ).astype(jnp.bfloat16)
    return (v_re, v_im)


def general_shards(band, pairs, extents):
    tables_x = dft_tables(GX)
    tables_y = dft_tables(GY)
    tables_z = dft_tables(GZ)
    tiles_here = band.shape[0]
    slots = tiles_here * FACES
    zrows = band.shape[2]
    tile_pos = lax.axis_index("tile")
    global_slot = tile_pos * slots + jnp.arange(slots, dtype=jnp.int32)
    first_slot = pairs[:, 0] * FACES + pairs[:, 1]
    second_slot = pairs[:, 2] * FACES + pairs[:, 3]
    matches = (
        (first_slot[None, :] == global_slot[:, None])
        | (second_slot[None, :] == global_slot[:, None])
    ).astype(jnp.int32)
    crop_bounds = jnp.sum(matches[:, :, None] * extents[None, :, :], axis=1)
    image_volume = band.reshape(slots, zrows, 2 * GX, 2 * GY)
    reduced_volume = reduce_resolution(image_volume, crop_bounds)
    y_re = product("szxy,yk->szxk", reduced_volume, tables_y[0]).astype(jnp.bfloat16)
    y_im = (-product("szxy,yk->szxk", reduced_volume, tables_y[1])).astype(jnp.bfloat16)
    x_re = (
        product("szxk,xj->szjk", y_re, tables_x[0]) + product("szxk,xj->szjk", y_im, tables_x[1])
    ).astype(jnp.bfloat16)
    x_im = (
        product("szxk,xj->szjk", y_im, tables_x[0]) - product("szxk,xj->szjk", y_re, tables_x[1])
    ).astype(jnp.bfloat16)
    kx_part = GX // lax.axis_size("zslab")
    re_in = lax.all_to_all(x_re, "zslab", split_axis=2, concat_axis=1, tiled=True)
    im_in = lax.all_to_all(x_im, "zslab", split_axis=2, concat_axis=1, tiled=True)
    out_re = (
        product("szjk,zm->msjk", re_in, tables_z[0]) + product("szjk,zm->msjk", im_in, tables_z[1])
    ).astype(jnp.bfloat16)
    out_im = (
        product("szjk,zm->msjk", im_in, tables_z[0]) - product("szjk,zm->msjk", re_in, tables_z[1])
    ).astype(jnp.bfloat16)
    tile_count = lax.axis_size("tile")
    kz_part = GZ // tile_count
    spectra = (
        lax.all_to_all(out_re, "tile", split_axis=0, concat_axis=0, tiled=True),
        lax.all_to_all(out_im, "tile", split_axis=0, concat_axis=0, tiled=True),
    )
    owner_re = spectra[0].reshape(tile_count, kz_part, slots, kx_part, GY)
    owner_im = spectra[1].reshape(tile_count, kz_part, slots, kx_part, GY)
    phase_real_part, phase_im = cross_phase(owner_re, owner_im, pairs, tiles_here)
    returned = (
        lax.all_to_all(phase_real_part, "tile", split_axis=0, concat_axis=1, tiled=True),
        lax.all_to_all(phase_im, "tile", split_axis=0, concat_axis=1, tiled=True),
    )
    w_re, w_im = inverse_z(returned[0], returned[1], tables_z)
    v_re, v_im = inverse_x(
        lax.all_to_all(w_re, "zslab", split_axis=1, concat_axis=2, tiled=True),
        lax.all_to_all(w_im, "zslab", split_axis=1, concat_axis=2, tiled=True),
        tables_x,
    )
    return product("pzxk,ky->pzxy", v_re, tables_y[0]) - product("pzxk,ky->pzxy", v_im, tables_y[1])


HALF = GY // 2
PLANES = 4
VMEM_BYTES = 32 * 1024 * 1024


def host_tables(length):
    indices = np.arange(length, dtype=np.int32)
    modular = indices[:, None] * indices[None, :] % length
    angles = modular.astype(np.float32) * np.float32(2.0 * math.pi / length)
    factor = np.float32(1.0 / math.sqrt(length))
    return (
        (np.cos(angles) * factor).astype(jnp.bfloat16),
        (np.sin(angles) * factor).astype(jnp.bfloat16),
    )


def half_y_table():
    cosine, sine = host_tables(GY)
    imag = -sine[:, :HALF]
    imag[:, 0] = cosine[:, HALF]
    return np.concatenate([cosine[:, :HALF], imag], axis=1)


def paired_y_table():
    half = half_y_table() * np.array(0.5, jnp.bfloat16)
    table = np.zeros((2 * GY, 2 * GY), jnp.bfloat16)
    table[::2, :GY] = half
    table[1::2, GY:] = half
    return table


def half_y_inverse():
    cosine, sine = host_tables(GY)
    two = np.array(2.0, jnp.bfloat16)
    real = cosine[:HALF, :] * two
    real[0] = cosine[0]
    imag = -sine[:HALF, :] * two
    imag[0] = cosine[HALF]
    return np.concatenate([real, imag], axis=0)


def mirror_order():
    order = [0, GX // 2]
    for j in range(1, GX // 2):
        order += [j, GX - j]
    return order


def complex_blocks(length, sign):
    cosine, sine = (table.astype(np.float32) for table in host_tables(length))
    return np.array([[cosine, -sign * sine], [sign * sine, cosine]])


def forward_x_table():
    table = np.einsum("oijx,az->joaizx", complex_blocks(GX, -1), np.eye(PLANES))[mirror_order()]
    table = table.reshape(2 * GX * PLANES, 2, PLANES // 2, 2, GX).transpose(0, 1, 2, 4, 3)
    return table.reshape(2 * GX * PLANES, -1).astype(jnp.bfloat16)


def inverse_x_table():
    table = np.einsum("oijx,az->oaxjiz", complex_blocks(GX, 1), np.eye(PLANES))
    return table.reshape(2 * PLANES * GX, -1).astype(jnp.bfloat16)


def z_rows():
    return np.arange(2 * GZ).reshape(2, GZ // PLANES, PLANES).transpose(1, 0, 2).reshape(-1)


def z_tables():
    forward, inverse = (
        complex_blocks(GZ, sign).transpose(0, 2, 1, 3).reshape(2 * GZ, 2 * GZ) for sign in (-1, 1)
    )
    none = np.zeros((2 * GZ, GZ), np.float32)
    forward_last = np.concatenate([none, forward[:, :GZ]], axis=1)
    inverse_last = np.concatenate([none.T, inverse[:GZ]], axis=0)
    order = z_rows()
    return [
        np.ascontiguousarray(table).astype(jnp.bfloat16)
        for table in (
            forward[:, order],
            inverse[order],
            forward_last[:, order],
            inverse_last[order],
        )
    ]


def imaginary_rows(shape):
    return lax.broadcasted_iota(jnp.int32, shape, 0) % (2 * PLANES) >= PLANES


def first_lane(shape):
    return lax.broadcasted_iota(jnp.int32, shape, 1) == 0


def dot(left, right):
    return jnp.dot(left, right, preferred_element_type=jnp.float32)


def cuts(least, parts):
    size = least // parts
    return [(0, least)] + [(least + k * size, size) for k in range(parts)]


def analyse_kernel(
    slots,
    pairs_ref,
    extents_ref,
    tile_ref,
    band_ref,
    wy_ref,
    wx_ref,
    out_ref,
    crop_ref,
    down_ref,
    raw_ref,
    raw_sems,
):
    step = pl.program_id(0)
    slot = jnp.minimum(step, slots - 1)
    zrows = raw_ref.shape[1]
    pieces = [(rows, columns) for rows in cuts(GX, 2) for columns in cuts(GY, 2)]

    @pl.when(slot == 0)
    def _():
        for p in range(pairs_ref.shape[1]):
            for end in (0, 1):
                named = pairs_ref[2 * end, p] * FACES + pairs_ref[2 * end + 1, p] - tile_ref[0] * slots

                @pl.when((named >= 0) & (named < slots))
                def _():
                    crop_ref[named, 0] = extents_ref[0, p]
                    crop_ref[named, 1] = extents_ref[1, p]

    def reached(of, piece):
        (row0, _), (col0, _) = pieces[piece]
        return (crop_ref[of, 0] > row0) & (crop_ref[of, 1] > col0)

    def fetch(of, piece):
        (row0, rows), (col0, cols) = pieces[piece]
        part = (slice(None), pl.ds(row0, rows), pl.ds(col0, cols))
        return pltpu.make_async_copy(
            band_ref.at[(of // FACES, of % FACES, *part)],
            raw_ref.at[(of, *part)],
            raw_sems.at[of, piece],
        )

    def start(of):
        for piece in range(len(pieces)):

            @pl.when(reached(of, piece))
            def _():
                fetch(of, piece).start()

    @pl.when(step == 0)
    def _():
        start(0)
        for of in range(slots):
            for piece, ((row0, rows), (col0, cols)) in enumerate(pieces):

                @pl.when(jnp.logical_not(reached(of, piece)))
                def _():
                    raw_ref[of, :, row0 : row0 + rows, col0 : col0 + cols] = jnp.zeros(
                        (zrows, rows, cols), raw_ref.dtype
                    )

    @pl.when(step < slots)
    def _():
        for piece in range(len(pieces)):

            @pl.when(reached(slot, piece))
            def _():
                fetch(slot, piece).wait()

    @pl.when(step + 1 < slots)
    def _():
        start(step + 1)

    across, along = crop_ref[slot, 0], crop_ref[slot, 1]

    def alternate(first, second):
        first = first + pltpu.roll(first, 127, 1)
        second = second + pltpu.roll(second, 1, 1)
        return jnp.where(even_lane, first, second).astype(jnp.bfloat16)

    row = lax.broadcasted_iota(jnp.int32, (2 * GX, 128), 0)
    lane = lax.broadcasted_iota(jnp.int32, (2 * GX, 128), 1)
    even, even_lane = row % 2 == 0, lane % 2 == 0
    groups = (2 * GX // 8, 8, 128)
    lanes = range(0, 2 * GY, 128)
    lives = [jnp.where((row < across) & (k + lane < along), 1.0, 0.0) for k in lanes]
    block = (2 * PLANES, HALF)
    lane0, imaginary = first_lane(block), imaginary_rows(block)
    sign = jnp.where(imaginary, -0.5, 0.5)

    def row_pairs(z, k, shift):
        raw = raw_ref[slot, z, :, k : k + 128].astype(jnp.float32) * lives[k // 128]
        return raw + pltpu.roll(raw.reshape(groups), shift, 1).reshape(raw.shape)

    def woven(z, k):
        return jnp.where(even, row_pairs(z, k, 7), row_pairs(z + 1, k, 1))

    def cells(z):
        return jnp.concatenate([alternate(woven(z, k), woven(z + 2, k)) for k in lanes], axis=1)


    def pool():
        for z in range(0, zrows, PLANES):
            unit = z // PLANES * 2 * GX
            down_ref[unit : unit + 2 * GX] = cells(z)

    def along_y():
        return dot(down_ref[...], wy_ref[...]).astype(jnp.bfloat16)

    def along_x(y):
        y = y.reshape(zrows // PLANES, 2 * GX, 2 * GY)
        units = [
            jnp.concatenate([y[unit, :, k : k + HALF] for k in (0, GY, HALF, GY + HALF)], axis=0)
            for unit in range(zrows // PLANES)
        ]
        spectra = dot(wx_ref[...], jnp.concatenate(units, axis=1))

        def at(n):
            rows = spectra[2 * PLANES * n : 2 * PLANES * (n + 1)]
            return [rows[:, k : k + HALF] for k in range(0, rows.shape[1], HALF)]

        def put(j, blocks):
            out_ref[j, 0] = jnp.concatenate(blocks, axis=0).astype(jnp.bfloat16)

        put(0, at(0))
        put(GX // 2, at(1))
        for j in range(1, GX // 2):
            here, mirror = at(2 * j), at(2 * j + 1)
            put(j, [jnp.where(lane0, 0.5 * a + sign * b, a) for a, b in zip(here, mirror)])
            put(
                GX - j,
                [
                    jnp.where(lane0, pltpu.roll(0.5 * a - sign * b, PLANES, 0), b)
                    for a, b in zip(here, mirror)
                ],
            )

    @pl.when(step == 0)
    def _():
        pool()

    @pl.when((step > 0) & (step < slots))
    def _():
        y = along_y()
        pool()
        along_x(y)

    @pl.when(step == slots)
    def _():
        along_x(along_y())


def analyse(band, pairs, extents, tile):
    slots, zrows = band.shape[0] * FACES, band.shape[2]
    tables = (paired_y_table(), forward_x_table())
    whole = [pl.BlockSpec(t.shape, lambda i, *_: (0, 0)) for t in tables]
    return pl.pallas_call(
        functools.partial(analyse_kernel, slots),
        grid_spec=pltpu.PrefetchScalarGridSpec(
            num_scalar_prefetch=3,
            grid=(slots + 1,),
            in_specs= [pl.BlockSpec(memory_space=pl.ANY)]
            + whole,
            out_specs=pl.BlockSpec(
                (GX, 1, 2 * zrows, HALF), lambda i, *_: (0, jnp.maximum(i - 1, 0), 0, 0)
            ),
            scratch_shapes=[
                pltpu.SMEM((slots, 2), jnp.int32),
                pltpu.VMEM((zrows // PLANES * 2 * GX, 2 * GY), jnp.bfloat16),
                pltpu.VMEM((slots, zrows, 2 * GX, 2 * GY), jnp.bfloat16),
                pltpu.SemaphoreType.DMA((slots, 9)),
            ],
        ),
        out_shape=jax.ShapeDtypeStruct((GX, slots, 2 * zrows, HALF), jnp.bfloat16),
        compiler_params=pltpu.CompilerParams(vmem_limit_bytes=VMEM_BYTES + VMEM_BYTES * 3 // 4),
        name="analyse",
    )(pairs, extents, tile, band, *(jnp.asarray(t) for t in tables))


def normalised(a_re, a_im, b_re, b_im):
    cross_re = a_re * b_re + a_im * b_im
    cross_im = a_im * b_re - a_re * b_im
    scale = lax.rsqrt(cross_re * cross_re + cross_im * cross_im + 1.0)
    return (cross_re * scale).astype(jnp.bfloat16), (cross_im * scale).astype(jnp.bfloat16)


def correlate_kernel(
    slabs, tiles_here, pairs_ref, place_ref, in_ref, wz_ref, wzi_ref, wz_last_ref, wzi_last_ref, out_ref
):
    tiles = in_ref.shape[0] // slabs
    total = pairs_ref.shape[1]
    pairs_here = out_ref.shape[1]
    slab_rows = out_ref.shape[2]
    both_real = (place_ref[0] == 0) | (place_ref[0] == GX // 2)
    block = (2 * GZ, HALF)
    shared = first_lane(block) & imaginary_rows(block)

    def load(p, end):
        tile = pairs_ref[2 * end, p]
        row = tile // tiles_here
        pos = tile % tiles_here * FACES + pairs_ref[2 * end + 1, p]
        return jnp.concatenate([in_ref[row + s * tiles, pos] for s in range(slabs)], axis=0)

    def phase_of(table_ref, ends):
        spec = dot(table_ref[...], jnp.concatenate(ends, axis=1))
        spec = spec.astype(jnp.bfloat16).astype(jnp.float32)
        parts = [spec[:GZ], spec[GZ:]]
        phases = []
        for k in range(0, spec.shape[1], 2 * HALF):
            a, b = slice(k, k + HALF), slice(k + HALF, k + 2 * HALF)
            phase = normalised(parts[0][:, a], parts[1][:, a], parts[0][:, b], parts[1][:, b])
            phases.append(jnp.concatenate(phase, axis=0))
        return jnp.concatenate(phases, axis=1)

    keep = jnp.where(shared & both_real, 0.0, 1.0).astype(jnp.bfloat16)
    group = 8
    for p in range(0, total, group):
        ends = [load(q, end) * keep for q in range(p, p + group) for end in (0, 1)]
        w = dot(wzi_ref[...], phase_of(wz_ref, ends)).astype(jnp.bfloat16)
        for k, q in enumerate(range(p, p + group)):
            for s in range(slabs):
                out_ref[q // pairs_here + s * tiles, q % pairs_here] = w[
                    s * slab_rows : (s + 1) * slab_rows, k * HALF : (k + 1) * HALF
                ]

    @pl.when(both_real)
    def _():
        lane = lax.broadcasted_iota(jnp.int32, block, 1)
        ends = [jnp.zeros(block, jnp.bfloat16)] * 2
        for p in range(total):
            for end in (0, 1):
                ends[end] = jnp.where(lane == p, load(p, end)[:, 0:1], ends[end])
        w = dot(wzi_last_ref[...], phase_of(wz_last_ref, ends)).astype(jnp.bfloat16)
        for p in range(total):
            column = w[:, p : p + 1]
            for s in range(slabs):
                rows = slice(s * slab_rows, (s + 1) * slab_rows)
                at = (p // pairs_here + s * tiles, p % pairs_here)
                out_ref[at] = jnp.where(shared[rows], column[rows], out_ref[at])


def correlate(spread, pairs, place, slabs, tiles_here):
    devices, _, slab_rows, _ = spread.shape
    pairs_here = pairs.shape[1] * slabs // devices
    tables = z_tables()
    vmem = pl.BlockSpec(memory_space=pltpu.VMEM)
    smem = pl.BlockSpec(memory_space=pltpu.SMEM)
    return pl.pallas_call(
        functools.partial(correlate_kernel, slabs, tiles_here),
        in_specs=[smem, smem] + [vmem] * (1 + len(tables)),
        out_specs=vmem,
        out_shape=jax.ShapeDtypeStruct((devices, pairs_here, slab_rows, HALF), jnp.bfloat16),
        compiler_params=pltpu.CompilerParams(vmem_limit_bytes=VMEM_BYTES),
        name="correlate",
    )(pairs, place, spread, *(jnp.asarray(t) for t in tables))


def synthesise_kernel(in_ref, wx_ref, wy_ref, out_ref):
    zpart = out_ref.shape[1]
    units = zpart // PLANES
    block = (2 * zpart, HALF)
    lane0, imaginary = first_lane(block), imaginary_rows(block)
    sign = jnp.where(imaginary, -1.0, 1.0)
    groups = (units, 2 * PLANES, HALF)

    def at(j):
        return in_ref[j, 0].astype(jnp.float32)

    blocks = [None] * GX
    for j in (0, GX // 2):
        blocks[j] = at(j)
    for j in range(1, GX // 2):
        here, mirror = at(j), at(GX - j)
        swapped = pltpu.roll(mirror.reshape(groups), PLANES, 1).reshape(block)
        blocks[j] = jnp.where(lane0, here + swapped, here)
        blocks[GX - j] = jnp.where(lane0, sign * (here - swapped), mirror)
    stacked = jnp.concatenate(
        [
            jnp.concatenate([b[u * 2 * PLANES : (u + 1) * 2 * PLANES] for b in blocks], axis=0)
            for u in range(units)
        ],
        axis=1,
    ).astype(jnp.bfloat16)
    v = dot(wx_ref[...], stacked).astype(jnp.bfloat16)
    rows = PLANES * GX
    cells = [
        jnp.concatenate([v[:rows, k : k + HALF], v[rows:, k : k + HALF]], axis=1)
        for k in range(0, units * HALF, HALF)
    ]
    maps = dot(jnp.concatenate(cells, axis=0), wy_ref[...])
    out_ref[0] = maps.reshape(zpart, GX, GY)


def synthesise(returned):
    _, pairs_here, slab_rows, _ = returned.shape
    zpart = slab_rows // 2
    tables = (inverse_x_table(), half_y_inverse())
    return pl.pallas_call(
        synthesise_kernel,
        grid=(pairs_here, slab_rows // (2 * zpart)),
        in_specs=[pl.BlockSpec((GX, 1, 2 * zpart, HALF), lambda i, z: (0, i, z, 0))]
        + [pl.BlockSpec(t.shape, lambda i, z: (0, 0)) for t in tables],
        out_specs=pl.BlockSpec((1, zpart, GX, GY), lambda i, z: (i, z, 0, 0)),
        out_shape=jax.ShapeDtypeStruct((pairs_here, slab_rows // 2, GX, GY), jnp.float32),
        compiler_params=pltpu.CompilerParams(vmem_limit_bytes=VMEM_BYTES),
        name="synthesise",
    )(returned, *(jnp.asarray(t) for t in tables))


def shards(band, pairs, extents):
    tiles, slabs = lax.axis_size("tile"), lax.axis_size("zslab")
    zrows = band.shape[2]
    if tiles * slabs != GX or zrows % (4 * PLANES) or pairs.shape[0] % 8 or pairs.shape[0] % tiles:
        return general_shards(band, pairs, extents)
    pairs, extents = pairs.T, extents.T
    tile = lax.axis_index("tile").astype(jnp.int32)
    device = lax.axis_index("zslab").astype(jnp.int32) * tiles + tile
    spectra = analyse(band, pairs, extents, tile[None])
    spread = lax.all_to_all(spectra, ("zslab", "tile"), split_axis=0, concat_axis=0, tiled=True)
    w = correlate(spread, pairs, device[None], slabs, band.shape[0])
    returned = lax.all_to_all(w, ("zslab", "tile"), split_axis=0, concat_axis=0, tiled=True)
    return synthesise(returned)


def solution(mesh):
    placed = (P("tile", None, "zslab", None, None), P(), P())
    return jax.shard_map(
        shards,
        mesh=mesh,
        in_specs=placed,
        out_specs=P("tile", "zslab", None, None),
        check_vma=False,
    )
```

```python
import functools
import math


import jax
import jax.numpy as jnp
import numpy as np
from jax import lax
from jax.experimental import pallas as pl
from jax.experimental.pallas import tpu as pltpu
from jax.sharding import PartitionSpec as P

GX = 32
GY = 256
GZ = 128
FACES = 4


def dft_tables(length):
    indices = jnp.arange(length, dtype=jnp.int32)
    modular = indices[:, None] * indices[None, :] % length
    angles = modular.astype(jnp.float32) * (2.0 * math.pi / length)
    factor = 1.0 / math.sqrt(length)
    return (
        (jnp.cos(angles) * factor).astype(jnp.bfloat16),
        (jnp.sin(angles) * factor).astype(jnp.bfloat16),
    )


def product(form, left, right):
    return jnp.einsum(form, left, right, preferred_element_type=jnp.float32)


def reduce_resolution(image_volume, crop_bounds):
    row_mask = (
        jnp.arange(image_volume.shape[2], dtype=jnp.int32)[None, :] < crop_bounds[:, 0:1]
    ).astype(jnp.bfloat16)
    col_mask = (
        jnp.arange(image_volume.shape[3], dtype=jnp.int32)[None, :] < crop_bounds[:, 1:2]
    ).astype(jnp.bfloat16)
    masked = image_volume * row_mask[:, None, :, None] * col_mask[:, None, None, :]
    raw_cols = jnp.arange(image_volume.shape[3], dtype=jnp.int32)
    pooled_cols = jnp.arange(GY, dtype=jnp.int32)
    pooling = jnp.where(raw_cols[:, None] // 2 == pooled_cols[None, :], 0.5, 0.0).astype(
        jnp.bfloat16
    )
    along_pooled = product("szxy,yk->szxk", masked, pooling)
    shaped = along_pooled.reshape(image_volume.shape[0], image_volume.shape[1], GX, 2, GY)
    return (shaped[:, :, :, 0, :] + shaped[:, :, :, 1, :]).astype(jnp.bfloat16)


def cross_phase(owner_re, owner_im, pairs, tiles_here):
    first_dev = pairs[:, 0] // tiles_here
    first_pos = pairs[:, 0] % tiles_here * FACES + pairs[:, 1]
    second_tile_device = pairs[:, 2] // tiles_here
    second_pos = pairs[:, 2] % tiles_here * FACES + pairs[:, 3]
    first_re = owner_re[first_dev, :, first_pos].astype(jnp.float32)
    first_im = owner_im[first_dev, :, first_pos].astype(jnp.float32)
    second_re = owner_re[second_tile_device, :, second_pos].astype(jnp.float32)
    second_im = owner_im[second_tile_device, :, second_pos].astype(jnp.float32)
    cross_re = first_re * second_re + first_im * second_im
    cross_im = first_im * second_re - first_re * second_im
    scaled = jnp.sqrt(cross_re * cross_re + cross_im * cross_im + 1.0)
    return ((cross_re / scaled).astype(jnp.bfloat16), (cross_im / scaled).astype(jnp.bfloat16))


def inverse_z(phase_real_part, phase_im, tables_z):
    w_re = (
        product("pmjk,mz->pzjk", phase_real_part, tables_z[0])
        - product("pmjk,mz->pzjk", phase_im, tables_z[1])
    ).astype(jnp.bfloat16)
    w_im = (
        product("pmjk,mz->pzjk", phase_im, tables_z[0])
        + product("pmjk,mz->pzjk", phase_real_part, tables_z[1])
    ).astype(jnp.bfloat16)
    return (w_re, w_im)


def inverse_x(w_re, w_im, tables_x):
    v_re = (
        product("pzjk,jx->pzxk", w_re, tables_x[0]) - product("pzjk,jx->pzxk", w_im, tables_x[1])
    ).astype(jnp.bfloat16)
    v_im = (
        product("pzjk,jx->pzxk", w_im, tables_x[0]) + product("pzjk,jx->pzxk", w_re, tables_x[1])
    ).astype(jnp.bfloat16)
    return (v_re, v_im)


def general_shards(band, pairs, extents):
    tables_x = dft_tables(GX)
    tables_y = dft_tables(GY)
    tables_z = dft_tables(GZ)
    tiles_here = band.shape[0]
    slots = tiles_here * FACES
    zrows = band.shape[2]
    tile_pos = lax.axis_index("tile")
    global_slot = tile_pos * slots + jnp.arange(slots, dtype=jnp.int32)
    first_slot = pairs[:, 0] * FACES + pairs[:, 1]
    second_slot = pairs[:, 2] * FACES + pairs[:, 3]
    matches = (
        (first_slot[None, :] == global_slot[:, None])
        | (second_slot[None, :] == global_slot[:, None])
    ).astype(jnp.int32)
    crop_bounds = jnp.sum(matches[:, :, None] * extents[None, :, :], axis=1)
    image_volume = band.reshape(slots, zrows, 2 * GX, 2 * GY)
    reduced_volume = reduce_resolution(image_volume, crop_bounds)
    y_re = product("szxy,yk->szxk", reduced_volume, tables_y[0]).astype(jnp.bfloat16)
    y_im = (-product("szxy,yk->szxk", reduced_volume, tables_y[1])).astype(jnp.bfloat16)
    x_re = (
        product("szxk,xj->szjk", y_re, tables_x[0]) + product("szxk,xj->szjk", y_im, tables_x[1])
    ).astype(jnp.bfloat16)
    x_im = (
        product("szxk,xj->szjk", y_im, tables_x[0]) - product("szxk,xj->szjk", y_re, tables_x[1])
    ).astype(jnp.bfloat16)
    kx_part = GX // lax.axis_size("zslab")
    re_in = lax.all_to_all(x_re, "zslab", split_axis=2, concat_axis=1, tiled=True)
    im_in = lax.all_to_all(x_im, "zslab", split_axis=2, concat_axis=1, tiled=True)
    out_re = (
        product("szjk,zm->msjk", re_in, tables_z[0]) + product("szjk,zm->msjk", im_in, tables_z[1])
    ).astype(jnp.bfloat16)
    out_im = (
        product("szjk,zm->msjk", im_in, tables_z[0]) - product("szjk,zm->msjk", re_in, tables_z[1])
    ).astype(jnp.bfloat16)
    tile_count = lax.axis_size("tile")
    kz_part = GZ // tile_count
    spectra = (
        lax.all_to_all(out_re, "tile", split_axis=0, concat_axis=0, tiled=True),
        lax.all_to_all(out_im, "tile", split_axis=0, concat_axis=0, tiled=True),
    )
    owner_re = spectra[0].reshape(tile_count, kz_part, slots, kx_part, GY)
    owner_im = spectra[1].reshape(tile_count, kz_part, slots, kx_part, GY)
    phase_real_part, phase_im = cross_phase(owner_re, owner_im, pairs, tiles_here)
    returned = (
        lax.all_to_all(phase_real_part, "tile", split_axis=0, concat_axis=1, tiled=True),
        lax.all_to_all(phase_im, "tile", split_axis=0, concat_axis=1, tiled=True),
    )
    w_re, w_im = inverse_z(returned[0], returned[1], tables_z)
    v_re, v_im = inverse_x(
        lax.all_to_all(w_re, "zslab", split_axis=1, concat_axis=2, tiled=True),
        lax.all_to_all(w_im, "zslab", split_axis=1, concat_axis=2, tiled=True),
        tables_x,
    )
    return product("pzxk,ky->pzxy", v_re, tables_y[0]) - product("pzxk,ky->pzxy", v_im, tables_y[1])


HALF = GY // 2
PLANES = 4
VMEM_BYTES = 32 * 1024 * 1024


def host_tables(length):
    indices = np.arange(length, dtype=np.int32)
    modular = indices[:, None] * indices[None, :] % length
    angles = modular.astype(np.float32) * np.float32(2.0 * math.pi / length)
    factor = np.float32(1.0 / math.sqrt(length))
    return (
        (np.cos(angles) * factor).astype(jnp.bfloat16),
        (np.sin(angles) * factor).astype(jnp.bfloat16),
    )


def half_y_table():
    cosine, sine = host_tables(GY)
    imag = -sine[:, :HALF]
    imag[:, 0] = cosine[:, HALF]
    return np.concatenate([cosine[:, :HALF], imag], axis=1)


def paired_y_table():
    half = half_y_table() * np.array(0.5, jnp.bfloat16)
    table = np.zeros((2 * GY, 2 * GY), jnp.bfloat16)
    table[::2, :GY] = half
    table[1::2, GY:] = half
    return table


def half_y_inverse():
    cosine, sine = host_tables(GY)
    two = np.array(2.0, jnp.bfloat16)
    real = cosine[:HALF, :] * two
    real[0] = cosine[0]
    imag = -sine[:HALF, :] * two
    imag[0] = cosine[HALF]
    return np.concatenate([real, imag], axis=0)


def mirror_order():
    order = [0, GX // 2]
    for j in range(1, GX // 2):
        order += [j, GX - j]
    return order


def complex_blocks(length, sign):
    cosine, sine = (table.astype(np.float32) for table in host_tables(length))
    return np.array([[cosine, -sign * sine], [sign * sine, cosine]])


def forward_x_table():
    table = np.einsum("oijx,az->joaizx", complex_blocks(GX, -1), np.eye(PLANES))[mirror_order()]
    table = table.reshape(2 * GX * PLANES, 2, PLANES // 2, 2, GX).transpose(0, 1, 2, 4, 3)
    return table.reshape(2 * GX * PLANES, -1).astype(jnp.bfloat16)


def inverse_x_table():
    table = np.einsum("oijx,az->oaxjiz", complex_blocks(GX, 1), np.eye(PLANES))
    return table.reshape(2 * PLANES * GX, -1).astype(jnp.bfloat16)


def z_rows():
    return np.arange(2 * GZ).reshape(2, GZ // PLANES, PLANES).transpose(1, 0, 2).reshape(-1)


def z_tables():
    forward, inverse = (
        complex_blocks(GZ, sign).transpose(0, 2, 1, 3).reshape(2 * GZ, 2 * GZ) for sign in (-1, 1)
    )
    none = np.zeros((2 * GZ, GZ), np.float32)
    forward_last = np.concatenate([none, forward[:, :GZ]], axis=1)
    inverse_last = np.concatenate([none.T, inverse[:GZ]], axis=0)
    order = z_rows()
    return [
        np.ascontiguousarray(table).astype(jnp.bfloat16)
        for table in (
            forward[:, order],
            inverse[order],
            forward_last[:, order],
            inverse_last[order],
        )
    ]


def imaginary_rows(shape):
    return lax.broadcasted_iota(jnp.int32, shape, 0) % (2 * PLANES) >= PLANES


def first_lane(shape):
    return lax.broadcasted_iota(jnp.int32, shape, 1) == 0


def dot(left, right):
    return jnp.dot(left, right, preferred_element_type=jnp.float32)


def analyse_kernel(
    pairs_ref,
    extents_ref,
    tile_ref,
    band_ref,
    wy_in_ref,
    wx_in_ref,
    out_ref,
    crop_ref,
    raw_ref,
    wy_ref,
    wx_ref,
    spec_ref,
    table_sems,
    raw_sems,
    spec_sems,
):
    slots, zrows = raw_ref.shape[:2]

    def fetch(slot):
        source = band_ref.at[slot // FACES, slot % FACES]
        return pltpu.make_async_copy(source, raw_ref.at[slot], raw_sems.at[slot])

    def leave(slot):
        return pltpu.make_async_copy(spec_ref.at[slot], out_ref.at[:, slot], spec_sems.at[slot])

    tables = [
        pltpu.make_async_copy(wy_in_ref, wy_ref, table_sems.at[0]),
        pltpu.make_async_copy(wx_in_ref, wx_ref, table_sems.at[1]),
    ]
    fetch(0).start()
    for copy in tables:
        copy.start()
    for slot in range(1, slots):
        fetch(slot).start()

    for p in range(pairs_ref.shape[1]):
        for end in (0, 1):
            named = pairs_ref[2 * end, p] * FACES + pairs_ref[2 * end + 1, p] - tile_ref[0] * slots

            @pl.when((named >= 0) & (named < slots))
            def _():
                crop_ref[named, 0] = extents_ref[0, p]
                crop_ref[named, 1] = extents_ref[1, p]

    row = lax.broadcasted_iota(jnp.int32, (2 * GX, 128), 0)
    lane = lax.broadcasted_iota(jnp.int32, (2 * GX, 128), 1)
    even, even_lane = row % 2 == 0, lane % 2 == 0
    groups = (2 * GX // 8, 8, 128)
    lanes = range(0, 2 * GY, 128)
    block = (2 * PLANES, HALF)
    lane0, imaginary = first_lane(block), imaginary_rows(block)
    sign = jnp.where(imaginary, -0.5, 0.5)

    def alternate(first, second):
        first = first + pltpu.roll(first, 127, 1)
        second = second + pltpu.roll(second, 1, 1)
        return jnp.where(even_lane, first, second).astype(jnp.bfloat16)

    for copy in tables:
        copy.wait()

    @pl.loop(0, slots)
    def _(slot):
        across, along = crop_ref[slot, 0], crop_ref[slot, 1]
        lives = [jnp.where((row < across) & (k + lane < along), 1.0, 0.0) for k in lanes]
        fetch(slot).wait()

        def row_pairs(z, k, shift):
            raw = raw_ref[slot, z, :, k : k + 128].astype(jnp.float32) * lives[k // 128]
            return raw + pltpu.roll(raw.reshape(groups), shift, 1).reshape(raw.shape)

        def woven(z, k):
            return jnp.where(even, row_pairs(z, k, 7), row_pairs(z + 1, k, 1))

        def cells(z):
            return jnp.concatenate([alternate(woven(z, k), woven(z + 2, k)) for k in lanes], axis=1)

        down = jnp.concatenate([cells(z) for z in range(0, zrows, PLANES)], axis=0)
        y = dot(down, wy_ref[...]).astype(jnp.bfloat16).reshape(zrows // PLANES, 2 * GX, 2 * GY)
        units = [
            jnp.concatenate([y[unit, :, k : k + HALF] for k in (0, GY, HALF, GY + HALF)], axis=0)
            for unit in range(zrows // PLANES)
        ]
        spectra = dot(wx_ref[...], jnp.concatenate(units, axis=1))

        def at(n):
            rows = spectra[2 * PLANES * n : 2 * PLANES * (n + 1)]
            return [rows[:, k : k + HALF] for k in range(0, rows.shape[1], HALF)]

        def put(j, blocks):
            spec_ref[slot, j] = jnp.concatenate(blocks, axis=0).astype(jnp.bfloat16)

        put(0, at(0))
        put(GX // 2, at(1))
        for j in range(1, GX // 2):
            here, mirror = at(2 * j), at(2 * j + 1)
            put(j, [jnp.where(lane0, 0.5 * a + sign * b, a) for a, b in zip(here, mirror)])
            put(
                GX - j,
                [
                    jnp.where(lane0, pltpu.roll(0.5 * a - sign * b, PLANES, 0), b)
                    for a, b in zip(here, mirror)
                ],
            )
        leave(slot).start()

    for slot in range(slots):
        leave(slot).wait()


def analyse(band, pairs, extents, tile):
    slots, zrows = band.shape[0] * FACES, band.shape[2]
    tables = (paired_y_table(), forward_x_table())
    smem = pl.BlockSpec(memory_space=pltpu.SMEM)
    anywhere = pl.BlockSpec(memory_space=pl.ANY)
    return pl.pallas_call(
        analyse_kernel,
        in_specs=[smem] * 3 + [anywhere] * (1 + len(tables)),
        out_specs=anywhere,
        out_shape=jax.ShapeDtypeStruct((GX, slots, 2 * zrows, HALF), jnp.bfloat16),
        scratch_shapes=[
            pltpu.SMEM((slots, 2), jnp.int32),
            pltpu.VMEM((slots, zrows, 2 * GX, 2 * GY), jnp.bfloat16),
            *[pltpu.VMEM(t.shape, jnp.bfloat16) for t in tables],
            pltpu.VMEM((slots, GX, 2 * zrows, HALF), jnp.bfloat16),
            pltpu.SemaphoreType.DMA((len(tables),)),
            pltpu.SemaphoreType.DMA((slots,)),
            pltpu.SemaphoreType.DMA((slots,)),
        ],
        compiler_params=pltpu.CompilerParams(vmem_limit_bytes=VMEM_BYTES + VMEM_BYTES * 3 // 4),
        name="analyse",
    )(pairs, extents, tile, band, *(jnp.asarray(t) for t in tables))


def normalised(a_re, a_im, b_re, b_im):
    cross_re = a_re * b_re + a_im * b_im
    cross_im = a_im * b_re - a_re * b_im
    scale = lax.rsqrt(cross_re * cross_re + cross_im * cross_im + 1.0)
    return (cross_re * scale).astype(jnp.bfloat16), (cross_im * scale).astype(jnp.bfloat16)


def correlate_kernel(
    slabs, tiles_here, pairs_ref, place_ref, in_ref, wz_ref, wzi_ref, wz_last_ref, wzi_last_ref, out_ref
):
    tiles = in_ref.shape[0] // slabs
    total = pairs_ref.shape[1]
    pairs_here = out_ref.shape[1]
    slab_rows = out_ref.shape[2]
    both_real = (place_ref[0] == 0) | (place_ref[0] == GX // 2)
    block = (2 * GZ, HALF)
    shared = first_lane(block) & imaginary_rows(block)

    def load(p, end):
        tile = pairs_ref[2 * end, p]
        row = tile // tiles_here
        pos = tile % tiles_here * FACES + pairs_ref[2 * end + 1, p]
        return jnp.concatenate([in_ref[row + s * tiles, pos] for s in range(slabs)], axis=0)

    def phase_of(table_ref, ends):
        spec = dot(table_ref[...], jnp.concatenate(ends, axis=1))
        spec = spec.astype(jnp.bfloat16).astype(jnp.float32)
        parts = [spec[:GZ], spec[GZ:]]
        phases = []
        for k in range(0, spec.shape[1], 2 * HALF):
            a, b = slice(k, k + HALF), slice(k + HALF, k + 2 * HALF)
            phase = normalised(parts[0][:, a], parts[1][:, a], parts[0][:, b], parts[1][:, b])
            phases.append(jnp.concatenate(phase, axis=0))
        return jnp.concatenate(phases, axis=1)

    keep = jnp.where(shared & both_real, 0.0, 1.0).astype(jnp.bfloat16)
    group = 16 if total % 16 == 0 else 8
    for p in range(0, total, group):
        ends = [load(q, end) * keep for q in range(p, p + group) for end in (0, 1)]
        w = dot(wzi_ref[...], phase_of(wz_ref, ends)).astype(jnp.bfloat16)
        for k, q in enumerate(range(p, p + group)):
            for s in range(slabs):
                out_ref[q // pairs_here + s * tiles, q % pairs_here] = w[
                    s * slab_rows : (s + 1) * slab_rows, k * HALF : (k + 1) * HALF
                ]

    @pl.when(both_real)
    def _():
        lane = lax.broadcasted_iota(jnp.int32, block, 1)
        ends = [jnp.zeros(block, jnp.bfloat16)] * 2
        for p in range(total):
            for end in (0, 1):
                ends[end] = jnp.where(lane == p, load(p, end)[:, 0:1], ends[end])
        w = dot(wzi_last_ref[...], phase_of(wz_last_ref, ends)).astype(jnp.bfloat16)
        for p in range(total):
            column = w[:, p : p + 1]
            for s in range(slabs):
                rows = slice(s * slab_rows, (s + 1) * slab_rows)
                at = (p // pairs_here + s * tiles, p % pairs_here)
                out_ref[at] = jnp.where(shared[rows], column[rows], out_ref[at])


def correlate(spread, pairs, place, slabs, tiles_here):
    devices, _, slab_rows, _ = spread.shape
    pairs_here = pairs.shape[1] * slabs // devices
    tables = z_tables()
    vmem = pl.BlockSpec(memory_space=pltpu.VMEM)
    smem = pl.BlockSpec(memory_space=pltpu.SMEM)
    return pl.pallas_call(
        functools.partial(correlate_kernel, slabs, tiles_here),
        in_specs=[smem, smem] + [vmem] * (1 + len(tables)),
        out_specs=vmem,
        out_shape=jax.ShapeDtypeStruct((devices, pairs_here, slab_rows, HALF), jnp.bfloat16),
        compiler_params=pltpu.CompilerParams(vmem_limit_bytes=VMEM_BYTES),
        name="correlate",
    )(pairs, place, spread, *(jnp.asarray(t) for t in tables))


def synthesise_kernel(in_ref, wx_ref, wy_ref, out_ref):
    zpart = out_ref.shape[1]
    units = zpart // PLANES
    block = (2 * zpart, HALF)
    lane0, imaginary = first_lane(block), imaginary_rows(block)
    sign = jnp.where(imaginary, -1.0, 1.0)
    groups = (units, 2 * PLANES, HALF)

    def at(j):
        return in_ref[j, 0].astype(jnp.float32)

    blocks = [None] * GX
    for j in (0, GX // 2):
        blocks[j] = at(j)
    for j in range(1, GX // 2):
        here, mirror = at(j), at(GX - j)
        swapped = pltpu.roll(mirror.reshape(groups), PLANES, 1).reshape(block)
        blocks[j] = jnp.where(lane0, here + swapped, here)
        blocks[GX - j] = jnp.where(lane0, sign * (here - swapped), mirror)
    stacked = jnp.concatenate(
        [
            jnp.concatenate([b[u * 2 * PLANES : (u + 1) * 2 * PLANES] for b in blocks], axis=0)
            for u in range(units)
        ],
        axis=1,
    ).astype(jnp.bfloat16)
    v = dot(wx_ref[...], stacked).astype(jnp.bfloat16)
    rows = PLANES * GX
    cells = [
        jnp.concatenate([v[:rows, k : k + HALF], v[rows:, k : k + HALF]], axis=1)
        for k in range(0, units * HALF, HALF)
    ]
    maps = dot(jnp.concatenate(cells, axis=0), wy_ref[...])
    out_ref[0] = maps.reshape(zpart, GX, GY)


def synthesise(returned):
    _, pairs_here, slab_rows, _ = returned.shape
    zpart = slab_rows // 2
    tables = (inverse_x_table(), half_y_inverse())
    return pl.pallas_call(
        synthesise_kernel,
        grid=(pairs_here, slab_rows // (2 * zpart)),
        in_specs=[pl.BlockSpec((GX, 1, 2 * zpart, HALF), lambda i, z: (0, i, z, 0))]
        + [pl.BlockSpec(t.shape, lambda i, z: (0, 0)) for t in tables],
        out_specs=pl.BlockSpec((1, zpart, GX, GY), lambda i, z: (i, z, 0, 0)),
        out_shape=jax.ShapeDtypeStruct((pairs_here, slab_rows // 2, GX, GY), jnp.float32),
        compiler_params=pltpu.CompilerParams(vmem_limit_bytes=VMEM_BYTES),
        name="synthesise",
    )(returned, *(jnp.asarray(t) for t in tables))


def shards(band, pairs, extents):
    tiles, slabs = lax.axis_size("tile"), lax.axis_size("zslab")
    zrows = band.shape[2]
    if tiles * slabs != GX or zrows % (4 * PLANES) or pairs.shape[0] % 8 or pairs.shape[0] % tiles:
        return general_shards(band, pairs, extents)
    pairs, extents = pairs.T, extents.T
    tile = lax.axis_index("tile").astype(jnp.int32)
    device = lax.axis_index("zslab").astype(jnp.int32) * tiles + tile
    spectra = analyse(band, pairs, extents, tile[None])
    spread = lax.all_to_all(spectra, ("zslab", "tile"), split_axis=0, concat_axis=0, tiled=True)
    w = correlate(spread, pairs, device[None], slabs, band.shape[0])
    returned = lax.all_to_all(w, ("zslab", "tile"), split_axis=0, concat_axis=0, tiled=True)
    return synthesise(returned)


def solution(mesh):
    placed = (P("tile", None, "zslab", None, None), P(), P())
    return jax.shard_map(
        shards,
        mesh=mesh,
        in_specs=placed,
        out_specs=P("tile", "zslab", None, None),
        check_vma=False,
    )
```

```python
import functools
import math


import jax
import jax.numpy as jnp
import numpy as np
from jax import lax
from jax.experimental import pallas as pl
from jax.experimental.pallas import tpu as pltpu
from jax.sharding import PartitionSpec as P

GX = 32
GY = 256
GZ = 128
FACES = 4


def dft_tables(length):
    indices = jnp.arange(length, dtype=jnp.int32)
    modular = indices[:, None] * indices[None, :] % length
    angles = modular.astype(jnp.float32) * (2.0 * math.pi / length)
    factor = 1.0 / math.sqrt(length)
    return (
        (jnp.cos(angles) * factor).astype(jnp.bfloat16),
        (jnp.sin(angles) * factor).astype(jnp.bfloat16),
    )


def product(form, left, right):
    return jnp.einsum(form, left, right, preferred_element_type=jnp.float32)


def reduce_resolution(image_volume, crop_bounds):
    row_mask = (
        jnp.arange(image_volume.shape[2], dtype=jnp.int32)[None, :] < crop_bounds[:, 0:1]
    ).astype(jnp.bfloat16)
    col_mask = (
        jnp.arange(image_volume.shape[3], dtype=jnp.int32)[None, :] < crop_bounds[:, 1:2]
    ).astype(jnp.bfloat16)
    masked = image_volume * row_mask[:, None, :, None] * col_mask[:, None, None, :]
    raw_cols = jnp.arange(image_volume.shape[3], dtype=jnp.int32)
    pooled_cols = jnp.arange(GY, dtype=jnp.int32)
    pooling = jnp.where(raw_cols[:, None] // 2 == pooled_cols[None, :], 0.5, 0.0).astype(
        jnp.bfloat16
    )
    along_pooled = product("szxy,yk->szxk", masked, pooling)
    shaped = along_pooled.reshape(image_volume.shape[0], image_volume.shape[1], GX, 2, GY)
    return (shaped[:, :, :, 0, :] + shaped[:, :, :, 1, :]).astype(jnp.bfloat16)


def cross_phase(owner_re, owner_im, pairs, tiles_here):
    first_dev = pairs[:, 0] // tiles_here
    first_pos = pairs[:, 0] % tiles_here * FACES + pairs[:, 1]
    second_tile_device = pairs[:, 2] // tiles_here
    second_pos = pairs[:, 2] % tiles_here * FACES + pairs[:, 3]
    first_re = owner_re[first_dev, :, first_pos].astype(jnp.float32)
    first_im = owner_im[first_dev, :, first_pos].astype(jnp.float32)
    second_re = owner_re[second_tile_device, :, second_pos].astype(jnp.float32)
    second_im = owner_im[second_tile_device, :, second_pos].astype(jnp.float32)
    cross_re = first_re * second_re + first_im * second_im
    cross_im = first_im * second_re - first_re * second_im
    scaled = jnp.sqrt(cross_re * cross_re + cross_im * cross_im + 1.0)
    return ((cross_re / scaled).astype(jnp.bfloat16), (cross_im / scaled).astype(jnp.bfloat16))


def inverse_z(phase_real_part, phase_im, tables_z):
    w_re = (
        product("pmjk,mz->pzjk", phase_real_part, tables_z[0])
        - product("pmjk,mz->pzjk", phase_im, tables_z[1])
    ).astype(jnp.bfloat16)
    w_im = (
        product("pmjk,mz->pzjk", phase_im, tables_z[0])
        + product("pmjk,mz->pzjk", phase_real_part, tables_z[1])
    ).astype(jnp.bfloat16)
    return (w_re, w_im)


def inverse_x(w_re, w_im, tables_x):
    v_re = (
        product("pzjk,jx->pzxk", w_re, tables_x[0]) - product("pzjk,jx->pzxk", w_im, tables_x[1])
    ).astype(jnp.bfloat16)
    v_im = (
        product("pzjk,jx->pzxk", w_im, tables_x[0]) + product("pzjk,jx->pzxk", w_re, tables_x[1])
    ).astype(jnp.bfloat16)
    return (v_re, v_im)


def general_shards(band, pairs, extents):
    tables_x = dft_tables(GX)
    tables_y = dft_tables(GY)
    tables_z = dft_tables(GZ)
    tiles_here = band.shape[0]
    slots = tiles_here * FACES
    zrows = band.shape[2]
    tile_pos = lax.axis_index("tile")
    global_slot = tile_pos * slots + jnp.arange(slots, dtype=jnp.int32)
    first_slot = pairs[:, 0] * FACES + pairs[:, 1]
    second_slot = pairs[:, 2] * FACES + pairs[:, 3]
    matches = (
        (first_slot[None, :] == global_slot[:, None])
        | (second_slot[None, :] == global_slot[:, None])
    ).astype(jnp.int32)
    crop_bounds = jnp.sum(matches[:, :, None] * extents[None, :, :], axis=1)
    image_volume = band.reshape(slots, zrows, 2 * GX, 2 * GY)
    reduced_volume = reduce_resolution(image_volume, crop_bounds)
    y_re = product("szxy,yk->szxk", reduced_volume, tables_y[0]).astype(jnp.bfloat16)
    y_im = (-product("szxy,yk->szxk", reduced_volume, tables_y[1])).astype(jnp.bfloat16)
    x_re = (
        product("szxk,xj->szjk", y_re, tables_x[0]) + product("szxk,xj->szjk", y_im, tables_x[1])
    ).astype(jnp.bfloat16)
    x_im = (
        product("szxk,xj->szjk", y_im, tables_x[0]) - product("szxk,xj->szjk", y_re, tables_x[1])
    ).astype(jnp.bfloat16)
    kx_part = GX // lax.axis_size("zslab")
    re_in = lax.all_to_all(x_re, "zslab", split_axis=2, concat_axis=1, tiled=True)
    im_in = lax.all_to_all(x_im, "zslab", split_axis=2, concat_axis=1, tiled=True)
    out_re = (
        product("szjk,zm->msjk", re_in, tables_z[0]) + product("szjk,zm->msjk", im_in, tables_z[1])
    ).astype(jnp.bfloat16)
    out_im = (
        product("szjk,zm->msjk", im_in, tables_z[0]) - product("szjk,zm->msjk", re_in, tables_z[1])
    ).astype(jnp.bfloat16)
    tile_count = lax.axis_size("tile")
    kz_part = GZ // tile_count
    spectra = (
        lax.all_to_all(out_re, "tile", split_axis=0, concat_axis=0, tiled=True),
        lax.all_to_all(out_im, "tile", split_axis=0, concat_axis=0, tiled=True),
    )
    owner_re = spectra[0].reshape(tile_count, kz_part, slots, kx_part, GY)
    owner_im = spectra[1].reshape(tile_count, kz_part, slots, kx_part, GY)
    phase_real_part, phase_im = cross_phase(owner_re, owner_im, pairs, tiles_here)
    returned = (
        lax.all_to_all(phase_real_part, "tile", split_axis=0, concat_axis=1, tiled=True),
        lax.all_to_all(phase_im, "tile", split_axis=0, concat_axis=1, tiled=True),
    )
    w_re, w_im = inverse_z(returned[0], returned[1], tables_z)
    v_re, v_im = inverse_x(
        lax.all_to_all(w_re, "zslab", split_axis=1, concat_axis=2, tiled=True),
        lax.all_to_all(w_im, "zslab", split_axis=1, concat_axis=2, tiled=True),
        tables_x,
    )
    return product("pzxk,ky->pzxy", v_re, tables_y[0]) - product("pzxk,ky->pzxy", v_im, tables_y[1])


HALF = GY // 2
PLANES = 4
VMEM_BYTES = 32 * 1024 * 1024


def host_tables(length):
    indices = np.arange(length, dtype=np.int32)
    modular = indices[:, None] * indices[None, :] % length
    angles = modular.astype(np.float32) * np.float32(2.0 * math.pi / length)
    factor = np.float32(1.0 / math.sqrt(length))
    return (
        (np.cos(angles) * factor).astype(jnp.bfloat16),
        (np.sin(angles) * factor).astype(jnp.bfloat16),
    )


def half_y_table():
    cosine, sine = host_tables(GY)
    imag = -sine[:, :HALF]
    imag[:, 0] = cosine[:, HALF]
    return np.concatenate([cosine[:, :HALF], imag], axis=1)


def paired_y_table():
    table = np.zeros((2 * GY, GY), jnp.bfloat16)
    table[::2] = half_y_table() * np.array(0.5, jnp.bfloat16)
    return table


def half_y_inverse():
    cosine, sine = host_tables(GY)
    two = np.array(2.0, jnp.bfloat16)
    real = cosine[:HALF, :] * two
    real[0] = cosine[0]
    imag = -sine[:HALF, :] * two
    imag[0] = cosine[HALF]
    return np.concatenate([real, imag], axis=0)


def mirror_order():
    order = [0, GX // 2]
    for j in range(1, GX // 2):
        order += [j, GX - j]
    return order


def complex_blocks(length, sign):
    cosine, sine = (table.astype(np.float32) for table in host_tables(length))
    return np.array([[cosine, -sign * sine], [sign * sine, cosine]])


def forward_x_table():
    table = np.einsum("oijx,az->joaizx", complex_blocks(GX, -1), np.eye(PLANES))[mirror_order()]
    table = table.reshape(2 * GX * PLANES, 2, PLANES, GX)
    woven = table[:, :, :2].transpose(0, 1, 3, 2).reshape(-1, 2, 2 * GX)
    plain = table[:, :, 2:].reshape(-1, 2, (PLANES - 2) * GX)
    table = np.concatenate([woven, plain], axis=2)
    return table.reshape(2 * GX * PLANES, -1).astype(jnp.bfloat16)


def inverse_x_table():
    table = np.einsum("oijx,az->oaxjiz", complex_blocks(GX, 1), np.eye(PLANES))
    return table.reshape(2 * PLANES * GX, -1).astype(jnp.bfloat16)


def z_rows():
    return np.arange(2 * GZ).reshape(2, GZ // PLANES, PLANES).transpose(1, 0, 2).reshape(-1)


def z_tables():
    forward, inverse = (
        complex_blocks(GZ, sign).transpose(0, 2, 1, 3).reshape(2 * GZ, 2 * GZ) for sign in (-1, 1)
    )
    none = np.zeros((2 * GZ, GZ), np.float32)
    forward_last = np.concatenate([none, forward[:, :GZ]], axis=1)
    inverse_last = np.concatenate([none.T, inverse[:GZ]], axis=0)
    order = z_rows()
    return [
        np.ascontiguousarray(table).astype(jnp.bfloat16)
        for table in (
            forward[:, order],
            inverse[order],
            forward_last[:, order],
            inverse_last[order],
        )
    ]


def imaginary_rows(shape):
    return lax.broadcasted_iota(jnp.int32, shape, 0) % (2 * PLANES) >= PLANES


def first_lane(shape):
    return lax.broadcasted_iota(jnp.int32, shape, 1) == 0


def dot(left, right):
    return jnp.dot(left, right, preferred_element_type=jnp.float32)


def analyse_kernel(
    slots, pairs_ref, extents_ref, tile_ref, *rest
):
    band_refs, (wy_ref, wx_ref, out_ref, crop_ref) = rest[:-4], rest[-4:]
    slot = pl.program_id(0)

    @pl.when(slot == 0)
    def _():
        for p in range(pairs_ref.shape[1]):
            for end in (0, 1):
                named = pairs_ref[2 * end, p] * FACES + pairs_ref[2 * end + 1, p] - tile_ref[0] * slots

                @pl.when((named >= 0) & (named < slots))
                def _():
                    crop_ref[named, 0] = extents_ref[0, p]
                    crop_ref[named, 1] = extents_ref[1, p]

    across, along = crop_ref[slot, 0], crop_ref[slot, 1]

    def live(k, rows):
        lane = lax.broadcasted_iota(jnp.int32, rows.shape, 1)
        return jnp.where((rows < across) & (k * 128 + lane < along), 1.0, 0.0)

    def halves(rows):
        return (rows + pltpu.roll(rows, 127, 1)).astype(jnp.bfloat16)

    raw_row = lax.broadcasted_iota(jnp.int32, (2 * GX, 128), 0)
    pooled_row = lax.broadcasted_iota(jnp.int32, (GX, 128), 0)
    even = raw_row % 2 == 0
    groups = (2 * GX // 8, 8, 128)
    lives = [
        (live(k, raw_row), live(k, 2 * pooled_row), live(k, 2 * pooled_row + 1))
        for k in range(len(band_refs))
    ]
    block = (2 * PLANES, HALF)
    lane0, imaginary = first_lane(block), imaginary_rows(block)
    sign = jnp.where(imaginary, -0.5, 0.5)

    def row_pairs(ref, z, mask, shift):
        raw = ref[0, 0, z].astype(jnp.float32) * mask
        return raw + pltpu.roll(raw.reshape(groups), shift, 1).reshape(raw.shape)

    def woven(z):
        return [
            halves(jnp.where(even, row_pairs(ref, z, mask, 7), row_pairs(ref, z + 1, mask, 1)))
            for ref, (mask, _, _) in zip(band_refs, lives)
        ]

    def plain(z):
        parts = []
        for ref, (_, *masks) in zip(band_refs, lives):
            rows = [ref[0, 0, z, pl.ds(a, GX, stride=2), :].astype(jnp.float32) for a in (0, 1)]
            parts.append(halves(rows[0] * masks[0] + rows[1] * masks[1]))
        return parts

    def pool(z):
        return [
            jnp.concatenate(parts, axis=1)
            for parts in (woven(z), *(plain(z + k) for k in range(2, PLANES)))
        ]

    zpart = 4 * PLANES
    zrows = band_refs[0].shape[2]
    planes = sum((pool(z) for z in range(0, zrows, PLANES)), [])
    y = dot(jnp.concatenate(planes, axis=0), wy_ref[...]).astype(jnp.bfloat16)
    y = y.reshape(zrows // PLANES, PLANES * GX, GY)

    def store(start, spectra):
        def at(n):
            rows = spectra[2 * PLANES * n : 2 * PLANES * (n + 1)]
            return [rows[:, k : k + HALF] for k in range(0, rows.shape[1], HALF)]

        def put(j, blocks):
            rows = slice(2 * start, 2 * (start + zpart))
            out_ref[j, 0, rows] = jnp.concatenate(blocks, axis=0).astype(jnp.bfloat16)

        put(0, at(0))
        put(GX // 2, at(1))
        for j in range(1, GX // 2):
            here, mirror = at(2 * j), at(2 * j + 1)
            put(j, [jnp.where(lane0, 0.5 * a + sign * b, a) for a, b in zip(here, mirror)])
            put(
                GX - j,
                [
                    jnp.where(lane0, pltpu.roll(0.5 * a - sign * b, PLANES, 0), b)
                    for a, b in zip(here, mirror)
                ],
            )

    for start in range(0, zrows, zpart):
        units = [
            jnp.concatenate([y[unit, :, :HALF], y[unit, :, HALF:]], axis=0)
            for unit in range(start // PLANES, (start + zpart) // PLANES)
        ]
        store(start, dot(wx_ref[...], jnp.concatenate(units, axis=1)))


def analyse(band, pairs, extents, tile):
    slots, zrows = band.shape[0] * FACES, band.shape[2]
    tables = (paired_y_table(), forward_x_table())
    whole = [pl.BlockSpec(t.shape, lambda i, *_: (0, 0)) for t in tables]
    lane_blocks = 2 * GY // 128
    return pl.pallas_call(
        functools.partial(analyse_kernel, slots),
        grid_spec=pltpu.PrefetchScalarGridSpec(
            num_scalar_prefetch=3,
            grid=(slots,),
            in_specs=[
                pl.BlockSpec(
                    (1, 1, zrows, 2 * GX, 128),
                    lambda i, *_, k=k: (i // FACES, i % FACES, 0, 0, k),
                )
                for k in range(lane_blocks)
            ]
            + whole,
            out_specs=pl.BlockSpec((GX, 1, 2 * zrows, HALF), lambda i, *_: (0, i, 0, 0)),
            scratch_shapes=[pltpu.SMEM((slots, 2), jnp.int32)],
        ),
        out_shape=jax.ShapeDtypeStruct((GX, slots, 2 * zrows, HALF), jnp.bfloat16),
        compiler_params=pltpu.CompilerParams(vmem_limit_bytes=VMEM_BYTES + VMEM_BYTES * 3 // 4),
        name="analyse",
    )(pairs, extents, tile, *[band] * lane_blocks, *(jnp.asarray(t) for t in tables))


def normalised(a_re, a_im, b_re, b_im):
    cross_re = a_re * b_re + a_im * b_im
    cross_im = a_im * b_re - a_re * b_im
    scale = lax.rsqrt(cross_re * cross_re + cross_im * cross_im + 1.0)
    return (cross_re * scale).astype(jnp.bfloat16), (cross_im * scale).astype(jnp.bfloat16)


def correlate_kernel(
    slabs, tiles_here, pairs_ref, place_ref, in_ref, wz_ref, wzi_ref, wz_last_ref, wzi_last_ref, out_ref
):
    tiles = in_ref.shape[0] // slabs
    total = pairs_ref.shape[1]
    pairs_here = out_ref.shape[1]
    slab_rows = out_ref.shape[2]
    both_real = (place_ref[0] == 0) | (place_ref[0] == GX // 2)
    block = (2 * GZ, HALF)
    shared = first_lane(block) & imaginary_rows(block)

    def load(p, end):
        tile = pairs_ref[2 * end, p]
        row = tile // tiles_here
        pos = tile % tiles_here * FACES + pairs_ref[2 * end + 1, p]
        return jnp.concatenate([in_ref[row + s * tiles, pos] for s in range(slabs)], axis=0)

    def phase_of(table_ref, ends):
        spec = dot(table_ref[...], jnp.concatenate(ends, axis=1))
        spec = spec.astype(jnp.bfloat16).astype(jnp.float32)
        parts = [spec[:GZ], spec[GZ:]]
        phases = []
        for k in range(0, spec.shape[1], 2 * HALF):
            a, b = slice(k, k + HALF), slice(k + HALF, k + 2 * HALF)
            phase = normalised(parts[0][:, a], parts[1][:, a], parts[0][:, b], parts[1][:, b])
            phases.append(jnp.concatenate(phase, axis=0))
        return jnp.concatenate(phases, axis=1)

    def join(special):
        if special:
            keep = jnp.where(shared, 0.0, 1.0).astype(jnp.bfloat16)
            lane = lax.broadcasted_iota(jnp.int32, block, 1)
            lasts = [jnp.zeros(block, jnp.bfloat16)] * 2
            for p in range(total):
                for end in (0, 1):
                    lasts[end] = jnp.where(lane == p, load(p, end)[:, 0:1], lasts[end])
            last = dot(wzi_last_ref[...], phase_of(wz_last_ref, lasts)).astype(jnp.bfloat16)
        group = 16 if total % 16 == 0 else 8
        for p in range(0, total, group):
            ends = [load(q, end) for q in range(p, p + group) for end in (0, 1)]
            if special:
                ends = [end * keep for end in ends]
            w = dot(wzi_ref[...], phase_of(wz_ref, ends)).astype(jnp.bfloat16)
            for k, q in enumerate(range(p, p + group)):
                whole = w[:, k * HALF : (k + 1) * HALF]
                if special:
                    whole = jnp.where(shared, last[:, q : q + 1], whole)
                for s in range(slabs):
                    out_ref[q // pairs_here + s * tiles, q % pairs_here] = whole[
                        s * slab_rows : (s + 1) * slab_rows
                    ]

    @pl.when(both_real)
    def _():
        join(True)

    @pl.when(jnp.logical_not(both_real))
    def _():
        join(False)


def correlate(spread, pairs, place, slabs, tiles_here):
    devices, _, slab_rows, _ = spread.shape
    pairs_here = pairs.shape[1] * slabs // devices
    tables = z_tables()
    vmem = pl.BlockSpec(memory_space=pltpu.VMEM)
    smem = pl.BlockSpec(memory_space=pltpu.SMEM)
    return pl.pallas_call(
        functools.partial(correlate_kernel, slabs, tiles_here),
        in_specs=[smem, smem] + [vmem] * (1 + len(tables)),
        out_specs=vmem,
        out_shape=jax.ShapeDtypeStruct((devices, pairs_here, slab_rows, HALF), jnp.bfloat16),
        compiler_params=pltpu.CompilerParams(vmem_limit_bytes=VMEM_BYTES),
        name="correlate",
    )(pairs, place, spread, *(jnp.asarray(t) for t in tables))


def synthesise_kernel(in_ref, wx_ref, wy_ref, out_ref):
    zpart = out_ref.shape[1]
    units = zpart // PLANES
    block = (2 * zpart, HALF)
    lane0, imaginary = first_lane(block), imaginary_rows(block)
    sign = jnp.where(imaginary, -1.0, 1.0)
    groups = (units, 2 * PLANES, HALF)

    def at(j):
        return in_ref[j, 0].astype(jnp.float32)

    blocks = [None] * GX
    for j in (0, GX // 2):
        blocks[j] = at(j)
    for j in range(1, GX // 2):
        here, mirror = at(j), at(GX - j)
        swapped = pltpu.roll(mirror.reshape(groups), PLANES, 1).reshape(block)
        blocks[j] = jnp.where(lane0, here + swapped, here)
        blocks[GX - j] = jnp.where(lane0, sign * (here - swapped), mirror)
    stacked = jnp.concatenate(
        [
            jnp.concatenate([b[u * 2 * PLANES : (u + 1) * 2 * PLANES] for b in blocks], axis=0)
            for u in range(units)
        ],
        axis=1,
    ).astype(jnp.bfloat16)
    v = dot(wx_ref[...], stacked).astype(jnp.bfloat16)
    rows = PLANES * GX
    cells = [
        jnp.concatenate([v[:rows, k : k + HALF], v[rows:, k : k + HALF]], axis=1)
        for k in range(0, units * HALF, HALF)
    ]
    maps = dot(jnp.concatenate(cells, axis=0), wy_ref[...])
    out_ref[0] = maps.reshape(zpart, GX, GY)


def synthesise(returned):
    _, pairs_here, slab_rows, _ = returned.shape
    zpart = slab_rows // 2
    tables = (inverse_x_table(), half_y_inverse())
    return pl.pallas_call(
        synthesise_kernel,
        grid=(pairs_here, slab_rows // (2 * zpart)),
        in_specs=[pl.BlockSpec((GX, 1, 2 * zpart, HALF), lambda i, z: (0, i, z, 0))]
        + [pl.BlockSpec(t.shape, lambda i, z: (0, 0)) for t in tables],
        out_specs=pl.BlockSpec((1, zpart, GX, GY), lambda i, z: (i, z, 0, 0)),
        out_shape=jax.ShapeDtypeStruct((pairs_here, slab_rows // 2, GX, GY), jnp.float32),
        compiler_params=pltpu.CompilerParams(vmem_limit_bytes=VMEM_BYTES),
        name="synthesise",
    )(returned, *(jnp.asarray(t) for t in tables))


def shards(band, pairs, extents):
    tiles, slabs = lax.axis_size("tile"), lax.axis_size("zslab")
    zrows = band.shape[2]
    if tiles * slabs != GX or zrows % (4 * PLANES) or pairs.shape[0] % 8 or pairs.shape[0] % tiles:
        return general_shards(band, pairs, extents)
    pairs, extents = pairs.T, extents.T
    tile = lax.axis_index("tile").astype(jnp.int32)
    device = lax.axis_index("zslab").astype(jnp.int32) * tiles + tile
    spectra = analyse(band, pairs, extents, tile[None])
    spread = lax.all_to_all(spectra, ("zslab", "tile"), split_axis=0, concat_axis=0, tiled=True)
    w = correlate(spread, pairs, device[None], slabs, band.shape[0])
    returned = lax.all_to_all(w, ("zslab", "tile"), split_axis=0, concat_axis=0, tiled=True)
    return synthesise(returned)


def solution(mesh):
    placed = (P("tile", None, "zslab", None, None), P(), P())
    return jax.shard_map(
        shards,
        mesh=mesh,
        in_specs=placed,
        out_specs=P("tile", "zslab", None, None),
        check_vma=False,
    )
```

```python
import functools
import math


import jax
import jax.numpy as jnp
import numpy as np
from jax import lax
from jax.experimental import pallas as pl
from jax.experimental.pallas import tpu as pltpu
from jax.sharding import PartitionSpec as P

GX = 32
GY = 256
GZ = 128
FACES = 4


def dft_tables(length):
    indices = jnp.arange(length, dtype=jnp.int32)
    modular = indices[:, None] * indices[None, :] % length
    angles = modular.astype(jnp.float32) * (2.0 * math.pi / length)
    factor = 1.0 / math.sqrt(length)
    return (
        (jnp.cos(angles) * factor).astype(jnp.bfloat16),
        (jnp.sin(angles) * factor).astype(jnp.bfloat16),
    )


def product(form, left, right):
    return jnp.einsum(form, left, right, preferred_element_type=jnp.float32)


def reduce_resolution(image_volume, crop_bounds):
    row_mask = (
        jnp.arange(image_volume.shape[2], dtype=jnp.int32)[None, :] < crop_bounds[:, 0:1]
    ).astype(jnp.bfloat16)
    col_mask = (
        jnp.arange(image_volume.shape[3], dtype=jnp.int32)[None, :] < crop_bounds[:, 1:2]
    ).astype(jnp.bfloat16)
    masked = image_volume * row_mask[:, None, :, None] * col_mask[:, None, None, :]
    raw_cols = jnp.arange(image_volume.shape[3], dtype=jnp.int32)
    pooled_cols = jnp.arange(GY, dtype=jnp.int32)
    pooling = jnp.where(raw_cols[:, None] // 2 == pooled_cols[None, :], 0.5, 0.0).astype(
        jnp.bfloat16
    )
    along_pooled = product("szxy,yk->szxk", masked, pooling)
    shaped = along_pooled.reshape(image_volume.shape[0], image_volume.shape[1], GX, 2, GY)
    return (shaped[:, :, :, 0, :] + shaped[:, :, :, 1, :]).astype(jnp.bfloat16)


def cross_phase(owner_re, owner_im, pairs, tiles_here):
    first_dev = pairs[:, 0] // tiles_here
    first_pos = pairs[:, 0] % tiles_here * FACES + pairs[:, 1]
    second_tile_device = pairs[:, 2] // tiles_here
    second_pos = pairs[:, 2] % tiles_here * FACES + pairs[:, 3]
    first_re = owner_re[first_dev, :, first_pos].astype(jnp.float32)
    first_im = owner_im[first_dev, :, first_pos].astype(jnp.float32)
    second_re = owner_re[second_tile_device, :, second_pos].astype(jnp.float32)
    second_im = owner_im[second_tile_device, :, second_pos].astype(jnp.float32)
    cross_re = first_re * second_re + first_im * second_im
    cross_im = first_im * second_re - first_re * second_im
    scaled = jnp.sqrt(cross_re * cross_re + cross_im * cross_im + 1.0)
    return ((cross_re / scaled).astype(jnp.bfloat16), (cross_im / scaled).astype(jnp.bfloat16))


def inverse_z(phase_real_part, phase_im, tables_z):
    w_re = (
        product("pmjk,mz->pzjk", phase_real_part, tables_z[0])
        - product("pmjk,mz->pzjk", phase_im, tables_z[1])
    ).astype(jnp.bfloat16)
    w_im = (
        product("pmjk,mz->pzjk", phase_im, tables_z[0])
        + product("pmjk,mz->pzjk", phase_real_part, tables_z[1])
    ).astype(jnp.bfloat16)
    return (w_re, w_im)


def inverse_x(w_re, w_im, tables_x):
    v_re = (
        product("pzjk,jx->pzxk", w_re, tables_x[0]) - product("pzjk,jx->pzxk", w_im, tables_x[1])
    ).astype(jnp.bfloat16)
    v_im = (
        product("pzjk,jx->pzxk", w_im, tables_x[0]) + product("pzjk,jx->pzxk", w_re, tables_x[1])
    ).astype(jnp.bfloat16)
    return (v_re, v_im)


def general_shards(band, pairs, extents):
    tables_x = dft_tables(GX)
    tables_y = dft_tables(GY)
    tables_z = dft_tables(GZ)
    tiles_here = band.shape[0]
    slots = tiles_here * FACES
    zrows = band.shape[2]
    tile_pos = lax.axis_index("tile")
    global_slot = tile_pos * slots + jnp.arange(slots, dtype=jnp.int32)
    first_slot = pairs[:, 0] * FACES + pairs[:, 1]
    second_slot = pairs[:, 2] * FACES + pairs[:, 3]
    matches = (
        (first_slot[None, :] == global_slot[:, None])
        | (second_slot[None, :] == global_slot[:, None])
    ).astype(jnp.int32)
    crop_bounds = jnp.sum(matches[:, :, None] * extents[None, :, :], axis=1)
    image_volume = band.reshape(slots, zrows, 2 * GX, 2 * GY)
    reduced_volume = reduce_resolution(image_volume, crop_bounds)
    y_re = product("szxy,yk->szxk", reduced_volume, tables_y[0]).astype(jnp.bfloat16)
    y_im = (-product("szxy,yk->szxk", reduced_volume, tables_y[1])).astype(jnp.bfloat16)
    x_re = (
        product("szxk,xj->szjk", y_re, tables_x[0]) + product("szxk,xj->szjk", y_im, tables_x[1])
    ).astype(jnp.bfloat16)
    x_im = (
        product("szxk,xj->szjk", y_im, tables_x[0]) - product("szxk,xj->szjk", y_re, tables_x[1])
    ).astype(jnp.bfloat16)
    kx_part = GX // lax.axis_size("zslab")
    re_in = lax.all_to_all(x_re, "zslab", split_axis=2, concat_axis=1, tiled=True)
    im_in = lax.all_to_all(x_im, "zslab", split_axis=2, concat_axis=1, tiled=True)
    out_re = (
        product("szjk,zm->msjk", re_in, tables_z[0]) + product("szjk,zm->msjk", im_in, tables_z[1])
    ).astype(jnp.bfloat16)
    out_im = (
        product("szjk,zm->msjk", im_in, tables_z[0]) - product("szjk,zm->msjk", re_in, tables_z[1])
    ).astype(jnp.bfloat16)
    tile_count = lax.axis_size("tile")
    kz_part = GZ // tile_count
    spectra = (
        lax.all_to_all(out_re, "tile", split_axis=0, concat_axis=0, tiled=True),
        lax.all_to_all(out_im, "tile", split_axis=0, concat_axis=0, tiled=True),
    )
    owner_re = spectra[0].reshape(tile_count, kz_part, slots, kx_part, GY)
    owner_im = spectra[1].reshape(tile_count, kz_part, slots, kx_part, GY)
    phase_real_part, phase_im = cross_phase(owner_re, owner_im, pairs, tiles_here)
    returned = (
        lax.all_to_all(phase_real_part, "tile", split_axis=0, concat_axis=1, tiled=True),
        lax.all_to_all(phase_im, "tile", split_axis=0, concat_axis=1, tiled=True),
    )
    w_re, w_im = inverse_z(returned[0], returned[1], tables_z)
    v_re, v_im = inverse_x(
        lax.all_to_all(w_re, "zslab", split_axis=1, concat_axis=2, tiled=True),
        lax.all_to_all(w_im, "zslab", split_axis=1, concat_axis=2, tiled=True),
        tables_x,
    )
    return product("pzxk,ky->pzxy", v_re, tables_y[0]) - product("pzxk,ky->pzxy", v_im, tables_y[1])


HALF = GY // 2
PLANES = 4
VMEM_BYTES = 32 * 1024 * 1024


def host_tables(length):
    indices = np.arange(length, dtype=np.int32)
    modular = indices[:, None] * indices[None, :] % length
    angles = modular.astype(np.float32) * np.float32(2.0 * math.pi / length)
    factor = np.float32(1.0 / math.sqrt(length))
    return (
        (np.cos(angles) * factor).astype(jnp.bfloat16),
        (np.sin(angles) * factor).astype(jnp.bfloat16),
    )


def half_y_table():
    cosine, sine = host_tables(GY)
    imag = -sine[:, :HALF]
    imag[:, 0] = cosine[:, HALF]
    return np.concatenate([cosine[:, :HALF], imag], axis=1)


def paired_y_table():
    table = np.zeros((2 * GY, GY), jnp.bfloat16)
    table[::2] = half_y_table() * np.array(0.5, jnp.bfloat16)
    return table


def half_y_inverse():
    cosine, sine = host_tables(GY)
    two = np.array(2.0, jnp.bfloat16)
    real = cosine[:HALF, :] * two
    real[0] = cosine[0]
    imag = -sine[:HALF, :] * two
    imag[0] = cosine[HALF]
    return np.concatenate([real, imag], axis=0)


def mirror_order():
    order = [0, GX // 2]
    for j in range(1, GX // 2):
        order += [j, GX - j]
    return order


def complex_blocks(length, sign):
    cosine, sine = (table.astype(np.float32) for table in host_tables(length))
    return np.array([[cosine, -sign * sine], [sign * sine, cosine]])


def forward_x_table():
    table = np.einsum("oijx,az->joaizx", complex_blocks(GX, -1), np.eye(PLANES))[mirror_order()]
    table = table.reshape(2 * GX * PLANES, 2, PLANES, GX)
    woven = table[:, :, :2].transpose(0, 1, 3, 2).reshape(-1, 2, 2 * GX)
    plain = table[:, :, 2:].reshape(-1, 2, (PLANES - 2) * GX)
    table = np.concatenate([woven, plain], axis=2)
    return table.reshape(2 * GX * PLANES, -1).astype(jnp.bfloat16)


def inverse_x_table():
    table = np.einsum("oijx,az->oaxjiz", complex_blocks(GX, 1), np.eye(PLANES))
    return table.reshape(2 * PLANES * GX, -1).astype(jnp.bfloat16)


def z_rows():
    return np.arange(2 * GZ).reshape(2, GZ // PLANES, PLANES).transpose(1, 0, 2).reshape(-1)


def z_tables():
    forward, inverse = (
        complex_blocks(GZ, sign).transpose(0, 2, 1, 3).reshape(2 * GZ, 2 * GZ) for sign in (-1, 1)
    )
    none = np.zeros((2 * GZ, GZ), np.float32)
    forward_last = np.concatenate([none, forward[:, :GZ]], axis=1)
    inverse_last = np.concatenate([none.T, inverse[:GZ]], axis=0)
    order = z_rows()
    return [
        np.ascontiguousarray(table).astype(jnp.bfloat16)
        for table in (
            forward[:, order],
            inverse[order],
            forward_last[:, order],
            inverse_last[order],
        )
    ]


def imaginary_rows(shape):
    return lax.broadcasted_iota(jnp.int32, shape, 0) % (2 * PLANES) >= PLANES


def first_lane(shape):
    return lax.broadcasted_iota(jnp.int32, shape, 1) == 0


def dot(left, right):
    return jnp.dot(left, right, preferred_element_type=jnp.float32)


def analyse_kernel(
    slots, pairs_ref, extents_ref, tile_ref, *rest
):
    band_refs, (wy_ref, wx_ref, out_ref, crop_ref) = rest[:-4], rest[-4:]
    slot = pl.program_id(0)

    @pl.when(slot == 0)
    def _():
        for p in range(pairs_ref.shape[1]):
            for end in (0, 1):
                named = pairs_ref[2 * end, p] * FACES + pairs_ref[2 * end + 1, p] - tile_ref[0] * slots

                @pl.when((named >= 0) & (named < slots))
                def _():
                    crop_ref[named, 0] = extents_ref[0, p]
                    crop_ref[named, 1] = extents_ref[1, p]

    across, along = crop_ref[slot, 0], crop_ref[slot, 1]

    def live(k, rows):
        lane = lax.broadcasted_iota(jnp.int32, rows.shape, 1)
        return jnp.where((rows < across) & (k * 128 + lane < along), 1.0, 0.0)

    def halves(rows):
        return (rows + pltpu.roll(rows, 127, 1)).astype(jnp.bfloat16)

    raw_row = lax.broadcasted_iota(jnp.int32, (2 * GX, 128), 0)
    pooled_row = lax.broadcasted_iota(jnp.int32, (GX, 128), 0)
    even = raw_row % 2 == 0
    groups = (2 * GX // 8, 8, 128)
    lives = [
        (live(k, raw_row), live(k, 2 * pooled_row), live(k, 2 * pooled_row + 1))
        for k in range(len(band_refs))
    ]
    block = (2 * PLANES, HALF)
    lane0, imaginary = first_lane(block), imaginary_rows(block)
    sign = jnp.where(imaginary, -0.5, 0.5)

    def row_pairs(ref, z, mask, shift):
        raw = ref[0, 0, z].astype(jnp.float32) * mask
        return raw + pltpu.roll(raw.reshape(groups), shift, 1).reshape(raw.shape)

    def woven(z):
        return [
            halves(jnp.where(even, row_pairs(ref, z, mask, 7), row_pairs(ref, z + 1, mask, 1)))
            for ref, (mask, _, _) in zip(band_refs, lives)
        ]

    def plain(z):
        parts = []
        for ref, (_, *masks) in zip(band_refs, lives):
            rows = [ref[0, 0, z, pl.ds(a, GX, stride=2), :].astype(jnp.float32) for a in (0, 1)]
            parts.append(halves(rows[0] * masks[0] + rows[1] * masks[1]))
        return parts

    def pool(z):
        return [
            jnp.concatenate(parts, axis=1)
            for parts in (woven(z), *(plain(z + k) for k in range(2, PLANES)))
        ]

    zpart = 4 * PLANES
    zrows = band_refs[0].shape[2]
    planes = sum((pool(z) for z in range(0, zrows, PLANES)), [])
    y = dot(jnp.concatenate(planes, axis=0), wy_ref[...]).astype(jnp.bfloat16)
    y = y.reshape(zrows // PLANES, PLANES * GX, GY)

    def store(start, spectra):
        def at(n):
            rows = spectra[2 * PLANES * n : 2 * PLANES * (n + 1)]
            return [rows[:, k : k + HALF] for k in range(0, rows.shape[1], HALF)]

        def put(j, blocks):
            rows = slice(2 * start, 2 * (start + zpart))
            out_ref[j, 0, rows] = jnp.concatenate(blocks, axis=0).astype(jnp.bfloat16)

        put(0, at(0))
        put(GX // 2, at(1))
        for j in range(1, GX // 2):
            here, mirror = at(2 * j), at(2 * j + 1)
            put(j, [jnp.where(lane0, 0.5 * a + sign * b, a) for a, b in zip(here, mirror)])
            put(
                GX - j,
                [
                    jnp.where(lane0, pltpu.roll(0.5 * a - sign * b, PLANES, 0), b)
                    for a, b in zip(here, mirror)
                ],
            )

    for start in range(0, zrows, zpart):
        units = [
            jnp.concatenate([y[unit, :, :HALF], y[unit, :, HALF:]], axis=0)
            for unit in range(start // PLANES, (start + zpart) // PLANES)
        ]
        store(start, dot(wx_ref[...], jnp.concatenate(units, axis=1)))


def analyse(band, pairs, extents, tile):
    slots, zrows = band.shape[0] * FACES, band.shape[2]
    tables = (paired_y_table(), forward_x_table())
    whole = [pl.BlockSpec(t.shape, lambda i, *_: (0, 0)) for t in tables]
    lane_blocks = 2 * GY // 128
    return pl.pallas_call(
        functools.partial(analyse_kernel, slots),
        grid_spec=pltpu.PrefetchScalarGridSpec(
            num_scalar_prefetch=3,
            grid=(slots,),
            in_specs=[
                pl.BlockSpec(
                    (1, 1, zrows, 2 * GX, 128),
                    lambda i, *_, k=k: (i // FACES, i % FACES, 0, 0, k),
                )
                for k in range(lane_blocks)
            ]
            + whole,
            out_specs=pl.BlockSpec((GX, 1, 2 * zrows, HALF), lambda i, *_: (0, i, 0, 0)),
            scratch_shapes=[pltpu.SMEM((slots, 2), jnp.int32)],
        ),
        out_shape=jax.ShapeDtypeStruct((GX, slots, 2 * zrows, HALF), jnp.bfloat16),
        compiler_params=pltpu.CompilerParams(vmem_limit_bytes=VMEM_BYTES + VMEM_BYTES * 3 // 4),
        name="analyse",
    )(pairs, extents, tile, *[band] * lane_blocks, *(jnp.asarray(t) for t in tables))


def normalised(a_re, a_im, b_re, b_im):
    cross_re = a_re * b_re + a_im * b_im
    cross_im = a_im * b_re - a_re * b_im
    scale = lax.rsqrt(cross_re * cross_re + cross_im * cross_im + 1.0)
    return (cross_re * scale).astype(jnp.bfloat16), (cross_im * scale).astype(jnp.bfloat16)


def correlate_kernel(
    slabs, tiles_here, pairs_ref, place_ref, in_ref, wz_ref, wzi_ref, wz_last_ref, wzi_last_ref, out_ref
):
    tiles = in_ref.shape[0] // slabs
    total = pairs_ref.shape[1]
    pairs_here = out_ref.shape[1]
    slab_rows = out_ref.shape[2]
    both_real = (place_ref[0] == 0) | (place_ref[0] == GX // 2)
    block = (2 * GZ, HALF)
    shared = first_lane(block) & imaginary_rows(block)

    def load(p, end):
        tile = pairs_ref[2 * end, p]
        row = tile // tiles_here
        pos = tile % tiles_here * FACES + pairs_ref[2 * end + 1, p]
        return jnp.concatenate([in_ref[row + s * tiles, pos] for s in range(slabs)], axis=0)

    def phase_of(table_ref, ends):
        spec = dot(table_ref[...], jnp.concatenate(ends, axis=1))
        spec = spec.astype(jnp.bfloat16).astype(jnp.float32)
        parts = [spec[:GZ], spec[GZ:]]
        phases = []
        for k in range(0, spec.shape[1], 2 * HALF):
            a, b = slice(k, k + HALF), slice(k + HALF, k + 2 * HALF)
            phase = normalised(parts[0][:, a], parts[1][:, a], parts[0][:, b], parts[1][:, b])
            phases.append(jnp.concatenate(phase, axis=0))
        return jnp.concatenate(phases, axis=1)

    def join(special):
        if special:
            keep = jnp.where(shared, 0.0, 1.0).astype(jnp.bfloat16)
            lane = lax.broadcasted_iota(jnp.int32, block, 1)
            lasts = [jnp.zeros(block, jnp.bfloat16)] * 2
            for p in range(total):
                for end in (0, 1):
                    lasts[end] = jnp.where(lane == p, load(p, end)[:, 0:1], lasts[end])
            last = dot(wzi_last_ref[...], phase_of(wz_last_ref, lasts)).astype(jnp.bfloat16)
        group = 16 if total % 16 == 0 else 8
        for p in range(0, total, group):
            ends = [load(q, end) for q in range(p, p + group) for end in (0, 1)]
            if special:
                ends = [end * keep for end in ends]
            w = dot(wzi_ref[...], phase_of(wz_ref, ends)).astype(jnp.bfloat16)
            for k, q in enumerate(range(p, p + group)):
                whole = w[:, k * HALF : (k + 1) * HALF]
                if special:
                    whole = jnp.where(shared, last[:, q : q + 1], whole)
                for s in range(slabs):
                    out_ref[q // pairs_here + s * tiles, q % pairs_here] = whole[
                        s * slab_rows : (s + 1) * slab_rows
                    ]

    @pl.when(both_real)
    def _():
        join(True)

    @pl.when(jnp.logical_not(both_real))
    def _():
        join(False)


def correlate(spread, pairs, place, slabs, tiles_here):
    devices, _, slab_rows, _ = spread.shape
    pairs_here = pairs.shape[1] * slabs // devices
    tables = z_tables()
    vmem = pl.BlockSpec(memory_space=pltpu.VMEM)
    smem = pl.BlockSpec(memory_space=pltpu.SMEM)
    return pl.pallas_call(
        functools.partial(correlate_kernel, slabs, tiles_here),
        in_specs=[smem, smem] + [vmem] * (1 + len(tables)),
        out_specs=vmem,
        out_shape=jax.ShapeDtypeStruct((devices, pairs_here, slab_rows, HALF), jnp.bfloat16),
        compiler_params=pltpu.CompilerParams(vmem_limit_bytes=VMEM_BYTES),
        name="correlate",
    )(pairs, place, spread, *(jnp.asarray(t) for t in tables))


def synthesise_kernel(in_ref, wx_ref, wy_ref, out_ref, maps_ref, sems):
    pairs_here, slab_rows = in_ref.shape[1:3]
    zrows = slab_rows // 2
    units = zrows // PLANES
    block = (slab_rows, HALF)
    lane0, imaginary = first_lane(block), imaginary_rows(block)
    sign = jnp.where(imaginary, -1.0, 1.0)
    groups = (units, 2 * PLANES, HALF)
    zpart = zrows // sems.shape[1]
    rows = PLANES * GX

    def leave(p, part):
        zs = pl.ds(part * zpart, zpart)
        return pltpu.make_async_copy(maps_ref.at[p, zs], out_ref.at[p, zs], sems.at[p, part])

    for p in range(pairs_here):
        blocks = [None] * GX
        for j in (0, GX // 2):
            blocks[j] = in_ref[j, p].astype(jnp.float32)
        for j in range(1, GX // 2):
            here, mirror = in_ref[j, p].astype(jnp.float32), in_ref[GX - j, p].astype(jnp.float32)
            swapped = pltpu.roll(mirror.reshape(groups), PLANES, 1).reshape(block)
            blocks[j] = jnp.where(lane0, here + swapped, here)
            blocks[GX - j] = jnp.where(lane0, sign * (here - swapped), mirror)
        stacked = jnp.concatenate(
            [
                jnp.concatenate([b[u * 2 * PLANES : (u + 1) * 2 * PLANES] for b in blocks], axis=0)
                for u in range(units)
            ],
            axis=1,
        ).astype(jnp.bfloat16)
        v = dot(wx_ref[...], stacked).astype(jnp.bfloat16)
        cells = [
            jnp.concatenate([v[:rows, k : k + HALF], v[rows:, k : k + HALF]], axis=1)
            for k in range(0, units * HALF, HALF)
        ]
        for part in range(sems.shape[1]):
            of = cells[part * zpart // PLANES : (part + 1) * zpart // PLANES]
            maps = dot(jnp.concatenate(of, axis=0), wy_ref[...])
            maps_ref[p, part * zpart : (part + 1) * zpart] = maps.reshape(zpart, GX, GY)
            leave(p, part).start()
    for p in range(pairs_here):
        for part in range(sems.shape[1]):
            leave(p, part).wait()


def synthesise(returned):
    _, pairs_here, slab_rows, _ = returned.shape
    tables = (inverse_x_table(), half_y_inverse())
    shape = (pairs_here, slab_rows // 2, GX, GY)
    vmem = pl.BlockSpec(memory_space=pltpu.VMEM)
    return pl.pallas_call(
        synthesise_kernel,
        in_specs=[vmem] * (1 + len(tables)),
        out_specs=pl.BlockSpec(memory_space=pl.ANY),
        out_shape=jax.ShapeDtypeStruct(shape, jnp.float32),
        scratch_shapes=[
            pltpu.VMEM(shape, jnp.float32),
            pltpu.SemaphoreType.DMA((pairs_here, slab_rows // (8 * PLANES))),
        ],
        compiler_params=pltpu.CompilerParams(vmem_limit_bytes=VMEM_BYTES),
        name="synthesise",
    )(returned, *(jnp.asarray(t) for t in tables))


def shards(band, pairs, extents):
    tiles, slabs = lax.axis_size("tile"), lax.axis_size("zslab")
    zrows = band.shape[2]
    if tiles * slabs != GX or zrows % (4 * PLANES) or pairs.shape[0] % 8 or pairs.shape[0] % tiles:
        return general_shards(band, pairs, extents)
    pairs, extents = pairs.T, extents.T
    tile = lax.axis_index("tile").astype(jnp.int32)
    device = lax.axis_index("zslab").astype(jnp.int32) * tiles + tile
    spectra = analyse(band, pairs, extents, tile[None])
    spread = lax.all_to_all(spectra, ("zslab", "tile"), split_axis=0, concat_axis=0, tiled=True)
    w = correlate(spread, pairs, device[None], slabs, band.shape[0])
    returned = lax.all_to_all(w, ("zslab", "tile"), split_axis=0, concat_axis=0, tiled=True)
    return synthesise(returned)


def solution(mesh):
    placed = (P("tile", None, "zslab", None, None), P(), P())
    return jax.shard_map(
        shards,
        mesh=mesh,
        in_specs=placed,
        out_specs=P("tile", "zslab", None, None),
        check_vma=False,
    )
```

```python
import functools
import math


import jax
import jax.numpy as jnp
import numpy as np
from jax import lax
from jax.experimental import pallas as pl
from jax.experimental.pallas import tpu as pltpu
from jax.sharding import PartitionSpec as P

GX = 32
GY = 256
GZ = 128
FACES = 4


def dft_tables(length):
    indices = jnp.arange(length, dtype=jnp.int32)
    modular = indices[:, None] * indices[None, :] % length
    angles = modular.astype(jnp.float32) * (2.0 * math.pi / length)
    factor = 1.0 / math.sqrt(length)
    return (
        (jnp.cos(angles) * factor).astype(jnp.bfloat16),
        (jnp.sin(angles) * factor).astype(jnp.bfloat16),
    )


def product(form, left, right):
    return jnp.einsum(form, left, right, preferred_element_type=jnp.float32)


def reduce_resolution(image_volume, crop_bounds):
    row_mask = (
        jnp.arange(image_volume.shape[2], dtype=jnp.int32)[None, :] < crop_bounds[:, 0:1]
    ).astype(jnp.bfloat16)
    col_mask = (
        jnp.arange(image_volume.shape[3], dtype=jnp.int32)[None, :] < crop_bounds[:, 1:2]
    ).astype(jnp.bfloat16)
    masked = image_volume * row_mask[:, None, :, None] * col_mask[:, None, None, :]
    raw_cols = jnp.arange(image_volume.shape[3], dtype=jnp.int32)
    pooled_cols = jnp.arange(GY, dtype=jnp.int32)
    pooling = jnp.where(raw_cols[:, None] // 2 == pooled_cols[None, :], 0.5, 0.0).astype(
        jnp.bfloat16
    )
    along_pooled = product("szxy,yk->szxk", masked, pooling)
    shaped = along_pooled.reshape(image_volume.shape[0], image_volume.shape[1], GX, 2, GY)
    return (shaped[:, :, :, 0, :] + shaped[:, :, :, 1, :]).astype(jnp.bfloat16)


def cross_phase(owner_re, owner_im, pairs, tiles_here):
    first_dev = pairs[:, 0] // tiles_here
    first_pos = pairs[:, 0] % tiles_here * FACES + pairs[:, 1]
    second_tile_device = pairs[:, 2] // tiles_here
    second_pos = pairs[:, 2] % tiles_here * FACES + pairs[:, 3]
    first_re = owner_re[first_dev, :, first_pos].astype(jnp.float32)
    first_im = owner_im[first_dev, :, first_pos].astype(jnp.float32)
    second_re = owner_re[second_tile_device, :, second_pos].astype(jnp.float32)
    second_im = owner_im[second_tile_device, :, second_pos].astype(jnp.float32)
    cross_re = first_re * second_re + first_im * second_im
    cross_im = first_im * second_re - first_re * second_im
    scaled = jnp.sqrt(cross_re * cross_re + cross_im * cross_im + 1.0)
    return ((cross_re / scaled).astype(jnp.bfloat16), (cross_im / scaled).astype(jnp.bfloat16))


def inverse_z(phase_real_part, phase_im, tables_z):
    w_re = (
        product("pmjk,mz->pzjk", phase_real_part, tables_z[0])
        - product("pmjk,mz->pzjk", phase_im, tables_z[1])
    ).astype(jnp.bfloat16)
    w_im = (
        product("pmjk,mz->pzjk", phase_im, tables_z[0])
        + product("pmjk,mz->pzjk", phase_real_part, tables_z[1])
    ).astype(jnp.bfloat16)
    return (w_re, w_im)


def inverse_x(w_re, w_im, tables_x):
    v_re = (
        product("pzjk,jx->pzxk", w_re, tables_x[0]) - product("pzjk,jx->pzxk", w_im, tables_x[1])
    ).astype(jnp.bfloat16)
    v_im = (
        product("pzjk,jx->pzxk", w_im, tables_x[0]) + product("pzjk,jx->pzxk", w_re, tables_x[1])
    ).astype(jnp.bfloat16)
    return (v_re, v_im)


def general_shards(band, pairs, extents):
    tables_x = dft_tables(GX)
    tables_y = dft_tables(GY)
    tables_z = dft_tables(GZ)
    tiles_here = band.shape[0]
    slots = tiles_here * FACES
    zrows = band.shape[2]
    tile_pos = lax.axis_index("tile")
    global_slot = tile_pos * slots + jnp.arange(slots, dtype=jnp.int32)
    first_slot = pairs[:, 0] * FACES + pairs[:, 1]
    second_slot = pairs[:, 2] * FACES + pairs[:, 3]
    matches = (
        (first_slot[None, :] == global_slot[:, None])
        | (second_slot[None, :] == global_slot[:, None])
    ).astype(jnp.int32)
    crop_bounds = jnp.sum(matches[:, :, None] * extents[None, :, :], axis=1)
    image_volume = band.reshape(slots, zrows, 2 * GX, 2 * GY)
    reduced_volume = reduce_resolution(image_volume, crop_bounds)
    y_re = product("szxy,yk->szxk", reduced_volume, tables_y[0]).astype(jnp.bfloat16)
    y_im = (-product("szxy,yk->szxk", reduced_volume, tables_y[1])).astype(jnp.bfloat16)
    x_re = (
        product("szxk,xj->szjk", y_re, tables_x[0]) + product("szxk,xj->szjk", y_im, tables_x[1])
    ).astype(jnp.bfloat16)
    x_im = (
        product("szxk,xj->szjk", y_im, tables_x[0]) - product("szxk,xj->szjk", y_re, tables_x[1])
    ).astype(jnp.bfloat16)
    kx_part = GX // lax.axis_size("zslab")
    re_in = lax.all_to_all(x_re, "zslab", split_axis=2, concat_axis=1, tiled=True)
    im_in = lax.all_to_all(x_im, "zslab", split_axis=2, concat_axis=1, tiled=True)
    out_re = (
        product("szjk,zm->msjk", re_in, tables_z[0]) + product("szjk,zm->msjk", im_in, tables_z[1])
    ).astype(jnp.bfloat16)
    out_im = (
        product("szjk,zm->msjk", im_in, tables_z[0]) - product("szjk,zm->msjk", re_in, tables_z[1])
    ).astype(jnp.bfloat16)
    tile_count = lax.axis_size("tile")
    kz_part = GZ // tile_count
    spectra = (
        lax.all_to_all(out_re, "tile", split_axis=0, concat_axis=0, tiled=True),
        lax.all_to_all(out_im, "tile", split_axis=0, concat_axis=0, tiled=True),
    )
    owner_re = spectra[0].reshape(tile_count, kz_part, slots, kx_part, GY)
    owner_im = spectra[1].reshape(tile_count, kz_part, slots, kx_part, GY)
    phase_real_part, phase_im = cross_phase(owner_re, owner_im, pairs, tiles_here)
    returned = (
        lax.all_to_all(phase_real_part, "tile", split_axis=0, concat_axis=1, tiled=True),
        lax.all_to_all(phase_im, "tile", split_axis=0, concat_axis=1, tiled=True),
    )
    w_re, w_im = inverse_z(returned[0], returned[1], tables_z)
    v_re, v_im = inverse_x(
        lax.all_to_all(w_re, "zslab", split_axis=1, concat_axis=2, tiled=True),
        lax.all_to_all(w_im, "zslab", split_axis=1, concat_axis=2, tiled=True),
        tables_x,
    )
    return product("pzxk,ky->pzxy", v_re, tables_y[0]) - product("pzxk,ky->pzxy", v_im, tables_y[1])


HALF = GY // 2
PLANES = 4
VMEM_BYTES = 32 * 1024 * 1024


def host_tables(length):
    indices = np.arange(length, dtype=np.int32)
    modular = indices[:, None] * indices[None, :] % length
    angles = modular.astype(np.float32) * np.float32(2.0 * math.pi / length)
    factor = np.float32(1.0 / math.sqrt(length))
    return (
        (np.cos(angles) * factor).astype(jnp.bfloat16),
        (np.sin(angles) * factor).astype(jnp.bfloat16),
    )


def half_y_table():
    cosine, sine = host_tables(GY)
    imag = -sine[:, :HALF]
    imag[:, 0] = cosine[:, HALF]
    return np.concatenate([cosine[:, :HALF], imag], axis=1)


def paired_y_table():
    table = np.zeros((2 * GY, GY), jnp.bfloat16)
    table[::2] = half_y_table() * np.array(0.5, jnp.bfloat16)
    table[:, [0, HALF]] *= np.array(0.5, jnp.bfloat16)
    return table


def half_y_inverse():
    cosine, sine = host_tables(GY)
    two = np.array(2.0, jnp.bfloat16)
    real = cosine[:HALF, :] * two
    real[0] = cosine[0]
    imag = -sine[:HALF, :] * two
    imag[0] = cosine[HALF]
    return np.concatenate([real, imag], axis=0)


def mirror_order():
    order = [0, GX // 2]
    for j in range(1, GX // 2):
        order += [j, GX - j]
    return order


def complex_blocks(length, sign):
    cosine, sine = (table.astype(np.float32) for table in host_tables(length))
    return np.array([[cosine, -sign * sine], [sign * sine, cosine]])


def forward_x_table():
    table = np.einsum("oijx,az->joaizx", complex_blocks(GX, -1), np.eye(PLANES))[mirror_order()]
    table = table.reshape(2 * GX * PLANES, 2, PLANES, GX)
    woven = table[:, :, :2].transpose(0, 1, 3, 2).reshape(-1, 2, 2 * GX)
    plain = table[:, :, 2:].reshape(-1, 2, (PLANES - 2) * GX)
    table = np.concatenate([woven, plain], axis=2)
    return table.reshape(2 * GX * PLANES, -1).astype(jnp.bfloat16)


def inverse_x_table():
    table = np.einsum("oijx,az->oaxjiz", complex_blocks(GX, 1), np.eye(PLANES))
    return table.reshape(2 * PLANES * GX, -1).astype(jnp.bfloat16)


def z_rows():
    return np.arange(2 * GZ).reshape(2, GZ // PLANES, PLANES).transpose(1, 0, 2).reshape(-1)


def z_tables():
    forward, inverse = (
        complex_blocks(GZ, sign).transpose(0, 2, 1, 3).reshape(2 * GZ, 2 * GZ) for sign in (-1, 1)
    )
    none = np.zeros((2 * GZ, GZ), np.float32)
    forward_last = np.concatenate([none, forward[:, :GZ]], axis=1)
    inverse_last = np.concatenate([none.T, inverse[:GZ]], axis=0)
    order = z_rows()
    return [
        np.ascontiguousarray(table).astype(jnp.bfloat16)
        for table in (
            forward[:, order],
            inverse[order],
            forward_last[:, order],
            inverse_last[order],
        )
    ]


def imaginary_rows(shape):
    return lax.broadcasted_iota(jnp.int32, shape, 0) % (2 * PLANES) >= PLANES


def first_lane(shape):
    return lax.broadcasted_iota(jnp.int32, shape, 1) == 0


def dot(left, right):
    return jnp.dot(left, right, preferred_element_type=jnp.float32)


def analyse_kernel(
    slots, pairs_ref, extents_ref, tile_ref, *rest
):
    band_refs, (wy_ref, wx_ref, out_ref, crop_ref) = rest[:-4], rest[-4:]
    slot = pl.program_id(0)

    @pl.when(slot == 0)
    def _():
        for p in range(pairs_ref.shape[1]):
            for end in (0, 1):
                named = pairs_ref[2 * end, p] * FACES + pairs_ref[2 * end + 1, p] - tile_ref[0] * slots

                @pl.when((named >= 0) & (named < slots))
                def _():
                    crop_ref[named, 0] = extents_ref[0, p]
                    crop_ref[named, 1] = extents_ref[1, p]

    across, along = crop_ref[slot, 0], crop_ref[slot, 1]

    def live(k, rows):
        lane = lax.broadcasted_iota(jnp.int32, rows.shape, 1)
        return jnp.where((rows < across) & (k * 128 + lane < along), 1.0, 0.0).astype(jnp.bfloat16)

    def halves(rows):
        return (rows + pltpu.roll(rows, 127, 1)).astype(jnp.bfloat16)

    raw_row = lax.broadcasted_iota(jnp.int32, (2 * GX, 128), 0)
    pooled_row = lax.broadcasted_iota(jnp.int32, (GX, 128), 0)
    even = raw_row % 2 == 0
    groups = (2 * GX // 8, 8, 128)
    lives = [
        (live(k, raw_row), live(k, 2 * pooled_row), live(k, 2 * pooled_row + 1))
        for k in range(len(band_refs))
    ]
    block = (2 * PLANES, HALF)
    lane0, imaginary = first_lane(block), imaginary_rows(block)
    sign = jnp.where(imaginary, -1.0, 1.0)
    twice = jnp.where(lane0, 2.0, 1.0)

    def row_pairs(ref, z, mask, shift):
        raw = (ref[0, 0, z] * mask).astype(jnp.float32)
        return raw + pltpu.roll(raw.reshape(groups), shift, 1).reshape(raw.shape)

    def woven(z):
        return [
            halves(jnp.where(even, row_pairs(ref, z, mask, 7), row_pairs(ref, z + 1, mask, 1)))
            for ref, (mask, _, _) in zip(band_refs, lives)
        ]

    def plain(z):
        parts = []
        for ref, (_, *masks) in zip(band_refs, lives):
            rows = [
                (ref[0, 0, z, pl.ds(a, GX, stride=2), :] * masks[a]).astype(jnp.float32) for a in (0, 1)
            ]
            parts.append(halves(rows[0] + rows[1]))
        return parts

    def pool(z):
        return [
            jnp.concatenate(parts, axis=1)
            for parts in (woven(z), *(plain(z + k) for k in range(2, PLANES)))
        ]

    zpart = 4 * PLANES
    zrows = band_refs[0].shape[2]
    planes = sum((pool(z) for z in range(0, zrows, PLANES)), [])
    y = dot(jnp.concatenate(planes, axis=0), wy_ref[...]).astype(jnp.bfloat16)
    y = y.reshape(zrows // PLANES, PLANES * GX, GY)

    def store(start, spectra):
        def at(n):
            rows = spectra[2 * PLANES * n : 2 * PLANES * (n + 1)]
            return [rows[:, k : k + HALF] for k in range(0, rows.shape[1], HALF)]

        def put(j, blocks):
            rows = slice(2 * start, 2 * (start + zpart))
            out_ref[j, 0, rows] = jnp.concatenate(blocks, axis=0).astype(jnp.bfloat16)

        put(0, [a * twice for a in at(0)])
        put(GX // 2, [a * twice for a in at(1)])
        for j in range(1, GX // 2):
            here, mirror = at(2 * j), at(2 * j + 1)
            put(j, [jnp.where(lane0, a + sign * b, a) for a, b in zip(here, mirror)])
            put(
                GX - j,
                [
                    jnp.where(lane0, pltpu.roll(a - sign * b, PLANES, 0), b)
                    for a, b in zip(here, mirror)
                ],
            )

    for start in range(0, zrows, zpart):
        units = [
            jnp.concatenate([y[unit, :, :HALF], y[unit, :, HALF:]], axis=0)
            for unit in range(start // PLANES, (start + zpart) // PLANES)
        ]
        store(start, dot(wx_ref[...], jnp.concatenate(units, axis=1)))


def analyse(band, pairs, extents, tile):
    slots, zrows = band.shape[0] * FACES, band.shape[2]
    tables = (paired_y_table(), forward_x_table())
    whole = [pl.BlockSpec(t.shape, lambda i, *_: (0, 0)) for t in tables]
    lane_blocks = 2 * GY // 128
    return pl.pallas_call(
        functools.partial(analyse_kernel, slots),
        grid_spec=pltpu.PrefetchScalarGridSpec(
            num_scalar_prefetch=3,
            grid=(slots,),
            in_specs=[
                pl.BlockSpec(
                    (1, 1, zrows, 2 * GX, 128),
                    lambda i, *_, k=k: (i // FACES, i % FACES, 0, 0, k),
                )
                for k in range(lane_blocks)
            ]
            + whole,
            out_specs=pl.BlockSpec((GX, 1, 2 * zrows, HALF), lambda i, *_: (0, i, 0, 0)),
            scratch_shapes=[pltpu.SMEM((slots, 2), jnp.int32)],
        ),
        out_shape=jax.ShapeDtypeStruct((GX, slots, 2 * zrows, HALF), jnp.bfloat16),
        compiler_params=pltpu.CompilerParams(vmem_limit_bytes=VMEM_BYTES + VMEM_BYTES * 3 // 4),
        name="analyse",
    )(pairs, extents, tile, *[band] * lane_blocks, *(jnp.asarray(t) for t in tables))


def normalised(a_re, a_im, b_re, b_im):
    cross_re = a_re * b_re + a_im * b_im
    cross_im = a_im * b_re - a_re * b_im
    scale = lax.rsqrt(cross_re * cross_re + cross_im * cross_im + 1.0)
    return (cross_re * scale).astype(jnp.bfloat16), (cross_im * scale).astype(jnp.bfloat16)


def correlate_kernel(
    slabs, tiles_here, pairs_ref, place_ref, in_ref, wz_ref, wzi_ref, wz_last_ref, wzi_last_ref, out_ref
):
    tiles = in_ref.shape[0] // slabs
    total = pairs_ref.shape[1]
    pairs_here = out_ref.shape[1]
    slab_rows = out_ref.shape[2]
    both_real = (place_ref[0] == 0) | (place_ref[0] == GX // 2)
    block = (2 * GZ, HALF)
    shared = first_lane(block) & imaginary_rows(block)

    def load(p, end):
        tile = pairs_ref[2 * end, p]
        row = tile // tiles_here
        pos = tile % tiles_here * FACES + pairs_ref[2 * end + 1, p]
        return jnp.concatenate([in_ref[row + s * tiles, pos] for s in range(slabs)], axis=0)

    def phase_of(table_ref, ends):
        spec = dot(table_ref[...], jnp.concatenate(ends, axis=1))
        spec = spec.astype(jnp.bfloat16).astype(jnp.float32)
        parts = [spec[:GZ], spec[GZ:]]
        phases = []
        for k in range(0, spec.shape[1], 2 * HALF):
            a, b = slice(k, k + HALF), slice(k + HALF, k + 2 * HALF)
            phase = normalised(parts[0][:, a], parts[1][:, a], parts[0][:, b], parts[1][:, b])
            phases.append(jnp.concatenate(phase, axis=0))
        return jnp.concatenate(phases, axis=1)

    def join(special):
        if special:
            keep = jnp.where(shared, 0.0, 1.0).astype(jnp.bfloat16)
            lane = lax.broadcasted_iota(jnp.int32, block, 1)
            lasts = [jnp.zeros(block, jnp.bfloat16)] * 2
            for p in range(total):
                for end in (0, 1):
                    lasts[end] = jnp.where(lane == p, load(p, end)[:, 0:1], lasts[end])
            last = dot(wzi_last_ref[...], phase_of(wz_last_ref, lasts)).astype(jnp.bfloat16)
        group = 16 if total % 16 == 0 else 8
        for p in range(0, total, group):
            ends = [load(q, end) for q in range(p, p + group) for end in (0, 1)]
            if special:
                ends = [end * keep for end in ends]
            w = dot(wzi_ref[...], phase_of(wz_ref, ends)).astype(jnp.bfloat16)
            for k, q in enumerate(range(p, p + group)):
                whole = w[:, k * HALF : (k + 1) * HALF]
                if special:
                    whole = jnp.where(shared, last[:, q : q + 1], whole)
                for s in range(slabs):
                    out_ref[q // pairs_here + s * tiles, q % pairs_here] = whole[
                        s * slab_rows : (s + 1) * slab_rows
                    ]

    @pl.when(both_real)
    def _():
        join(True)

    @pl.when(jnp.logical_not(both_real))
    def _():
        join(False)


def correlate(spread, pairs, place, slabs, tiles_here):
    devices, _, slab_rows, _ = spread.shape
    pairs_here = pairs.shape[1] * slabs // devices
    tables = z_tables()
    vmem = pl.BlockSpec(memory_space=pltpu.VMEM)
    smem = pl.BlockSpec(memory_space=pltpu.SMEM)
    return pl.pallas_call(
        functools.partial(correlate_kernel, slabs, tiles_here),
        in_specs=[smem, smem] + [vmem] * (1 + len(tables)),
        out_specs=vmem,
        out_shape=jax.ShapeDtypeStruct((devices, pairs_here, slab_rows, HALF), jnp.bfloat16),
        compiler_params=pltpu.CompilerParams(vmem_limit_bytes=VMEM_BYTES),
        name="correlate",
    )(pairs, place, spread, *(jnp.asarray(t) for t in tables))


def synthesise_kernel(in_ref, wx_ref, wy_ref, out_ref, maps_ref, sems):
    pairs_here, slab_rows = in_ref.shape[1:3]
    zrows = slab_rows // 2
    units = zrows // PLANES
    block = (slab_rows, HALF)
    lane0, imaginary = first_lane(block), imaginary_rows(block)
    sign = jnp.where(imaginary, -1.0, 1.0)
    groups = (units, 2 * PLANES, HALF)
    zpart = zrows // sems.shape[1]
    rows = PLANES * GX

    def leave(p, part):
        zs = pl.ds(part * zpart, zpart)
        return pltpu.make_async_copy(maps_ref.at[p, zs], out_ref.at[p, zs], sems.at[p, part])

    for p in range(pairs_here):
        blocks = [None] * GX
        for j in (0, GX // 2):
            blocks[j] = in_ref[j, p].astype(jnp.float32)
        for j in range(1, GX // 2):
            here, mirror = in_ref[j, p].astype(jnp.float32), in_ref[GX - j, p].astype(jnp.float32)
            swapped = pltpu.roll(mirror.reshape(groups), PLANES, 1).reshape(block)
            blocks[j] = jnp.where(lane0, here + swapped, here)
            blocks[GX - j] = jnp.where(lane0, sign * (here - swapped), mirror)
        stacked = jnp.concatenate(
            [
                jnp.concatenate([b[u * 2 * PLANES : (u + 1) * 2 * PLANES] for b in blocks], axis=0)
                for u in range(units)
            ],
            axis=1,
        ).astype(jnp.bfloat16)
        v = dot(wx_ref[...], stacked).astype(jnp.bfloat16)
        cells = [
            jnp.concatenate([v[:rows, k : k + HALF], v[rows:, k : k + HALF]], axis=1)
            for k in range(0, units * HALF, HALF)
        ]
        for part in range(sems.shape[1]):
            of = cells[part * zpart // PLANES : (part + 1) * zpart // PLANES]
            maps = dot(jnp.concatenate(of, axis=0), wy_ref[...])
            maps_ref[p, part * zpart : (part + 1) * zpart] = maps.reshape(zpart, GX, GY)
            leave(p, part).start()
    for p in range(pairs_here):
        for part in range(sems.shape[1]):
            leave(p, part).wait()


def synthesise(returned):
    _, pairs_here, slab_rows, _ = returned.shape
    tables = (inverse_x_table(), half_y_inverse())
    shape = (pairs_here, slab_rows // 2, GX, GY)
    vmem = pl.BlockSpec(memory_space=pltpu.VMEM)
    return pl.pallas_call(
        synthesise_kernel,
        in_specs=[vmem] * (1 + len(tables)),
        out_specs=pl.BlockSpec(memory_space=pl.ANY),
        out_shape=jax.ShapeDtypeStruct(shape, jnp.float32),
        scratch_shapes=[
            pltpu.VMEM(shape, jnp.float32),
            pltpu.SemaphoreType.DMA((pairs_here, slab_rows // (8 * PLANES))),
        ],
        compiler_params=pltpu.CompilerParams(vmem_limit_bytes=VMEM_BYTES),
        name="synthesise",
    )(returned, *(jnp.asarray(t) for t in tables))


def shards(band, pairs, extents):
    tiles, slabs = lax.axis_size("tile"), lax.axis_size("zslab")
    zrows = band.shape[2]
    if tiles * slabs != GX or zrows % (4 * PLANES) or pairs.shape[0] % 8 or pairs.shape[0] % tiles:
        return general_shards(band, pairs, extents)
    pairs, extents = pairs.T, extents.T
    tile = lax.axis_index("tile").astype(jnp.int32)
    device = lax.axis_index("zslab").astype(jnp.int32) * tiles + tile
    spectra = analyse(band, pairs, extents, tile[None])
    spread = lax.all_to_all(spectra, ("zslab", "tile"), split_axis=0, concat_axis=0, tiled=True)
    w = correlate(spread, pairs, device[None], slabs, band.shape[0])
    returned = lax.all_to_all(w, ("zslab", "tile"), split_axis=0, concat_axis=0, tiled=True)
    return synthesise(returned)


def solution(mesh):
    placed = (P("tile", None, "zslab", None, None), P(), P())
    return jax.shard_map(
        shards,
        mesh=mesh,
        in_specs=placed,
        out_specs=P("tile", "zslab", None, None),
        check_vma=False,
    )
```

```python
import functools
import math


import jax
import jax.numpy as jnp
import numpy as np
from jax import lax
from jax.experimental import pallas as pl
from jax.experimental.pallas import tpu as pltpu
from jax.sharding import PartitionSpec as P

GX = 32
GY = 256
GZ = 128
FACES = 4


def dft_tables(length):
    indices = jnp.arange(length, dtype=jnp.int32)
    modular = indices[:, None] * indices[None, :] % length
    angles = modular.astype(jnp.float32) * (2.0 * math.pi / length)
    factor = 1.0 / math.sqrt(length)
    return (
        (jnp.cos(angles) * factor).astype(jnp.bfloat16),
        (jnp.sin(angles) * factor).astype(jnp.bfloat16),
    )


def product(form, left, right):
    return jnp.einsum(form, left, right, preferred_element_type=jnp.float32)


def reduce_resolution(image_volume, crop_bounds):
    row_mask = (
        jnp.arange(image_volume.shape[2], dtype=jnp.int32)[None, :] < crop_bounds[:, 0:1]
    ).astype(jnp.bfloat16)
    col_mask = (
        jnp.arange(image_volume.shape[3], dtype=jnp.int32)[None, :] < crop_bounds[:, 1:2]
    ).astype(jnp.bfloat16)
    masked = image_volume * row_mask[:, None, :, None] * col_mask[:, None, None, :]
    raw_cols = jnp.arange(image_volume.shape[3], dtype=jnp.int32)
    pooled_cols = jnp.arange(GY, dtype=jnp.int32)
    pooling = jnp.where(raw_cols[:, None] // 2 == pooled_cols[None, :], 0.5, 0.0).astype(
        jnp.bfloat16
    )
    along_pooled = product("szxy,yk->szxk", masked, pooling)
    shaped = along_pooled.reshape(image_volume.shape[0], image_volume.shape[1], GX, 2, GY)
    return (shaped[:, :, :, 0, :] + shaped[:, :, :, 1, :]).astype(jnp.bfloat16)


def cross_phase(owner_re, owner_im, pairs, tiles_here):
    first_dev = pairs[:, 0] // tiles_here
    first_pos = pairs[:, 0] % tiles_here * FACES + pairs[:, 1]
    second_tile_device = pairs[:, 2] // tiles_here
    second_pos = pairs[:, 2] % tiles_here * FACES + pairs[:, 3]
    first_re = owner_re[first_dev, :, first_pos].astype(jnp.float32)
    first_im = owner_im[first_dev, :, first_pos].astype(jnp.float32)
    second_re = owner_re[second_tile_device, :, second_pos].astype(jnp.float32)
    second_im = owner_im[second_tile_device, :, second_pos].astype(jnp.float32)
    cross_re = first_re * second_re + first_im * second_im
    cross_im = first_im * second_re - first_re * second_im
    scaled = jnp.sqrt(cross_re * cross_re + cross_im * cross_im + 1.0)
    return ((cross_re / scaled).astype(jnp.bfloat16), (cross_im / scaled).astype(jnp.bfloat16))


def inverse_z(phase_real_part, phase_im, tables_z):
    w_re = (
        product("pmjk,mz->pzjk", phase_real_part, tables_z[0])
        - product("pmjk,mz->pzjk", phase_im, tables_z[1])
    ).astype(jnp.bfloat16)
    w_im = (
        product("pmjk,mz->pzjk", phase_im, tables_z[0])
        + product("pmjk,mz->pzjk", phase_real_part, tables_z[1])
    ).astype(jnp.bfloat16)
    return (w_re, w_im)


def inverse_x(w_re, w_im, tables_x):
    v_re = (
        product("pzjk,jx->pzxk", w_re, tables_x[0]) - product("pzjk,jx->pzxk", w_im, tables_x[1])
    ).astype(jnp.bfloat16)
    v_im = (
        product("pzjk,jx->pzxk", w_im, tables_x[0]) + product("pzjk,jx->pzxk", w_re, tables_x[1])
    ).astype(jnp.bfloat16)
    return (v_re, v_im)


def general_shards(band, pairs, extents):
    tables_x = dft_tables(GX)
    tables_y = dft_tables(GY)
    tables_z = dft_tables(GZ)
    tiles_here = band.shape[0]
    slots = tiles_here * FACES
    zrows = band.shape[2]
    tile_pos = lax.axis_index("tile")
    global_slot = tile_pos * slots + jnp.arange(slots, dtype=jnp.int32)
    first_slot = pairs[:, 0] * FACES + pairs[:, 1]
    second_slot = pairs[:, 2] * FACES + pairs[:, 3]
    matches = (
        (first_slot[None, :] == global_slot[:, None])
        | (second_slot[None, :] == global_slot[:, None])
    ).astype(jnp.int32)
    crop_bounds = jnp.sum(matches[:, :, None] * extents[None, :, :], axis=1)
    image_volume = band.reshape(slots, zrows, 2 * GX, 2 * GY)
    reduced_volume = reduce_resolution(image_volume, crop_bounds)
    y_re = product("szxy,yk->szxk", reduced_volume, tables_y[0]).astype(jnp.bfloat16)
    y_im = (-product("szxy,yk->szxk", reduced_volume, tables_y[1])).astype(jnp.bfloat16)
    x_re = (
        product("szxk,xj->szjk", y_re, tables_x[0]) + product("szxk,xj->szjk", y_im, tables_x[1])
    ).astype(jnp.bfloat16)
    x_im = (
        product("szxk,xj->szjk", y_im, tables_x[0]) - product("szxk,xj->szjk", y_re, tables_x[1])
    ).astype(jnp.bfloat16)
    kx_part = GX // lax.axis_size("zslab")
    re_in = lax.all_to_all(x_re, "zslab", split_axis=2, concat_axis=1, tiled=True)
    im_in = lax.all_to_all(x_im, "zslab", split_axis=2, concat_axis=1, tiled=True)
    out_re = (
        product("szjk,zm->msjk", re_in, tables_z[0]) + product("szjk,zm->msjk", im_in, tables_z[1])
    ).astype(jnp.bfloat16)
    out_im = (
        product("szjk,zm->msjk", im_in, tables_z[0]) - product("szjk,zm->msjk", re_in, tables_z[1])
    ).astype(jnp.bfloat16)
    tile_count = lax.axis_size("tile")
    kz_part = GZ // tile_count
    spectra = (
        lax.all_to_all(out_re, "tile", split_axis=0, concat_axis=0, tiled=True),
        lax.all_to_all(out_im, "tile", split_axis=0, concat_axis=0, tiled=True),
    )
    owner_re = spectra[0].reshape(tile_count, kz_part, slots, kx_part, GY)
    owner_im = spectra[1].reshape(tile_count, kz_part, slots, kx_part, GY)
    phase_real_part, phase_im = cross_phase(owner_re, owner_im, pairs, tiles_here)
    returned = (
        lax.all_to_all(phase_real_part, "tile", split_axis=0, concat_axis=1, tiled=True),
        lax.all_to_all(phase_im, "tile", split_axis=0, concat_axis=1, tiled=True),
    )
    w_re, w_im = inverse_z(returned[0], returned[1], tables_z)
    v_re, v_im = inverse_x(
        lax.all_to_all(w_re, "zslab", split_axis=1, concat_axis=2, tiled=True),
        lax.all_to_all(w_im, "zslab", split_axis=1, concat_axis=2, tiled=True),
        tables_x,
    )
    return product("pzxk,ky->pzxy", v_re, tables_y[0]) - product("pzxk,ky->pzxy", v_im, tables_y[1])


HALF = GY // 2
PLANES = 4
VMEM_BYTES = 32 * 1024 * 1024


def host_tables(length):
    indices = np.arange(length, dtype=np.int32)
    modular = indices[:, None] * indices[None, :] % length
    angles = modular.astype(np.float32) * np.float32(2.0 * math.pi / length)
    factor = np.float32(1.0 / math.sqrt(length))
    return (
        (np.cos(angles) * factor).astype(jnp.bfloat16),
        (np.sin(angles) * factor).astype(jnp.bfloat16),
    )


def half_y_table():
    cosine, sine = host_tables(GY)
    imag = -sine[:, :HALF]
    imag[:, 0] = cosine[:, HALF]
    return np.concatenate([cosine[:, :HALF], imag], axis=1)


def paired_y_table():
    table = np.zeros((2 * GY, GY), jnp.bfloat16)
    table[::2] = half_y_table() * np.array(0.5, jnp.bfloat16)
    table[:, [0, HALF]] *= np.array(0.5, jnp.bfloat16)
    return table


def half_y_inverse():
    cosine, sine = host_tables(GY)
    two = np.array(2.0, jnp.bfloat16)
    real = cosine[:HALF, :] * two
    real[0] = cosine[0]
    imag = -sine[:HALF, :] * two
    imag[0] = cosine[HALF]
    return np.concatenate([real, imag], axis=0)


def mirror_order():
    order = [0, GX // 2]
    for j in range(1, GX // 2):
        order += [j, GX - j]
    return order


def complex_blocks(length, sign):
    cosine, sine = (table.astype(np.float32) for table in host_tables(length))
    return np.array([[cosine, -sign * sine], [sign * sine, cosine]])


def forward_x_table():
    table = np.einsum("oijx,az->joaizx", complex_blocks(GX, -1), np.eye(PLANES))[mirror_order()]
    table = table.reshape(2 * GX * PLANES, 2, PLANES, GX)
    woven = table[:, :, :2].transpose(0, 1, 3, 2).reshape(-1, 2, 2 * GX)
    plain = table[:, :, 2:].reshape(-1, 2, (PLANES - 2) * GX)
    table = np.concatenate([woven, plain], axis=2)
    return table.reshape(2 * GX * PLANES, -1).astype(jnp.bfloat16)


def inverse_x_table():
    table = np.einsum("oijx,az->oaxjiz", complex_blocks(GX, 1), np.eye(PLANES))
    return table.reshape(2 * PLANES * GX, -1).astype(jnp.bfloat16)


def z_rows():
    return np.arange(2 * GZ).reshape(2, GZ // PLANES, PLANES).transpose(1, 0, 2).reshape(-1)


def z_tables():
    forward, inverse = (
        complex_blocks(GZ, sign).transpose(0, 2, 1, 3).reshape(2 * GZ, 2 * GZ) for sign in (-1, 1)
    )
    none = np.zeros((2 * GZ, GZ), np.float32)
    forward_last = np.concatenate([none, forward[:, :GZ]], axis=1)
    inverse_last = np.concatenate([none.T, inverse[:GZ]], axis=0)
    order = z_rows()
    return [
        np.ascontiguousarray(table).astype(jnp.bfloat16)
        for table in (
            forward[:, order],
            inverse[order],
            forward_last[:, order],
            inverse_last[order],
        )
    ]


def imaginary_rows(shape):
    return lax.broadcasted_iota(jnp.int32, shape, 0) % (2 * PLANES) >= PLANES


def first_lane(shape):
    return lax.broadcasted_iota(jnp.int32, shape, 1) == 0


def dot(left, right):
    return jnp.dot(left, right, preferred_element_type=jnp.float32)


def analyse_kernel(
    slots, pairs_ref, extents_ref, tile_ref, *rest
):
    band_refs, (wy_ref, wx_ref, out_ref, crop_ref) = rest[:-4], rest[-4:]
    slot = pl.program_id(0)

    @pl.when(slot == 0)
    def _():
        for p in range(pairs_ref.shape[1]):
            for end in (0, 1):
                named = pairs_ref[2 * end, p] * FACES + pairs_ref[2 * end + 1, p] - tile_ref[0] * slots

                @pl.when((named >= 0) & (named < slots))
                def _():
                    crop_ref[named, 0] = extents_ref[0, p]
                    crop_ref[named, 1] = extents_ref[1, p]

    across, along = crop_ref[slot, 0], crop_ref[slot, 1]

    def live(k, rows):
        lane = lax.broadcasted_iota(jnp.int32, rows.shape, 1)
        return jnp.where((rows < across) & (k * 128 + lane < along), 1.0, 0.0).astype(jnp.bfloat16)

    def halves(rows):
        return (rows + pltpu.roll(rows, 127, 1)).astype(jnp.bfloat16)

    raw_row = lax.broadcasted_iota(jnp.int32, (2 * GX, 128), 0)
    pooled_row = lax.broadcasted_iota(jnp.int32, (GX, 128), 0)
    even = raw_row % 2 == 0
    groups = (2 * GX // 8, 8, 128)
    lives = [
        (live(k, raw_row), live(k, 2 * pooled_row), live(k, 2 * pooled_row + 1))
        for k in range(len(band_refs))
    ]
    block = (2 * PLANES, HALF)
    lane0, imaginary = first_lane(block), imaginary_rows(block)
    sign = jnp.where(imaginary, -1.0, 1.0)
    twice = jnp.where(lane0, 2.0, 1.0)

    def row_pairs(ref, z, mask, shift):
        raw = (ref[0, 0, z] * mask).astype(jnp.float32)
        return raw + pltpu.roll(raw.reshape(groups), shift, 1).reshape(raw.shape)

    def woven(z):
        return [
            halves(jnp.where(even, row_pairs(ref, z, mask, 7), row_pairs(ref, z + 1, mask, 1)))
            for ref, (mask, _, _) in zip(band_refs, lives)
        ]

    def plain(z):
        parts = []
        for ref, (_, *masks) in zip(band_refs, lives):
            rows = [
                (ref[0, 0, z, pl.ds(a, GX, stride=2), :] * masks[a]).astype(jnp.float32) for a in (0, 1)
            ]
            parts.append(halves(rows[0] + rows[1]))
        return parts

    def pool(z):
        return [
            jnp.concatenate(parts, axis=1)
            for parts in (woven(z), *(plain(z + k) for k in range(2, PLANES)))
        ]

    zpart = 4 * PLANES
    zrows = band_refs[0].shape[2]
    planes = sum((pool(z) for z in range(0, zrows, PLANES)), [])
    y = dot(jnp.concatenate(planes, axis=0), wy_ref[...]).astype(jnp.bfloat16)
    y = y.reshape(zrows // PLANES, PLANES * GX, GY)

    def store(start, spectra):
        def at(n):
            rows = spectra[2 * PLANES * n : 2 * PLANES * (n + 1)]
            return [rows[:, k : k + HALF] for k in range(0, rows.shape[1], HALF)]

        def put(j, blocks):
            rows = slice(2 * start, 2 * (start + zpart))
            out_ref[j, 0, rows] = jnp.concatenate(blocks, axis=0).astype(jnp.bfloat16)

        put(0, [a * twice for a in at(0)])
        put(GX // 2, [a * twice for a in at(1)])
        for j in range(1, GX // 2):
            here, mirror = at(2 * j), at(2 * j + 1)
            put(j, [jnp.where(lane0, a + sign * b, a) for a, b in zip(here, mirror)])
            put(
                GX - j,
                [
                    jnp.where(lane0, pltpu.roll(a - sign * b, PLANES, 0), b)
                    for a, b in zip(here, mirror)
                ],
            )

    for start in range(0, zrows, zpart):
        units = [
            jnp.concatenate([y[unit, :, :HALF], y[unit, :, HALF:]], axis=0)
            for unit in range(start // PLANES, (start + zpart) // PLANES)
        ]
        store(start, dot(wx_ref[...], jnp.concatenate(units, axis=1)))


def analyse(band, pairs, extents, tile):
    slots, zrows = band.shape[0] * FACES, band.shape[2]
    tables = (paired_y_table(), forward_x_table())
    whole = [pl.BlockSpec(t.shape, lambda i, *_: (0, 0)) for t in tables]
    lane_blocks = 2 * GY // 128
    return pl.pallas_call(
        functools.partial(analyse_kernel, slots),
        grid_spec=pltpu.PrefetchScalarGridSpec(
            num_scalar_prefetch=3,
            grid=(slots,),
            in_specs=[
                pl.BlockSpec(
                    (1, 1, zrows, 2 * GX, 128),
                    lambda i, *_, k=k: (i // FACES, i % FACES, 0, 0, k),
                )
                for k in range(lane_blocks)
            ]
            + whole,
            out_specs=pl.BlockSpec((GX, 1, 2 * zrows, HALF), lambda i, *_: (0, i, 0, 0)),
            scratch_shapes=[pltpu.SMEM((slots, 2), jnp.int32)],
        ),
        out_shape=jax.ShapeDtypeStruct((GX, slots, 2 * zrows, HALF), jnp.bfloat16),
        compiler_params=pltpu.CompilerParams(vmem_limit_bytes=VMEM_BYTES + VMEM_BYTES * 3 // 4),
        name="analyse",
    )(pairs, extents, tile, *[band] * lane_blocks, *(jnp.asarray(t) for t in tables))


def normalised(a_re, a_im, b_re, b_im):
    cross_re = a_re * b_re + a_im * b_im
    cross_im = a_im * b_re - a_re * b_im
    scale = lax.rsqrt(cross_re * cross_re + cross_im * cross_im + 1.0)
    return (cross_re * scale).astype(jnp.bfloat16), (cross_im * scale).astype(jnp.bfloat16)


def correlate_kernel(
    slabs, tiles_here, pairs_ref, place_ref, in_ref, wz_ref, wzi_ref, wz_last_ref, wzi_last_ref, out_ref
):
    total = pairs_ref.shape[1]
    pairs_here = out_ref.shape[1]
    slab_rows = out_ref.shape[2]
    both_real = (place_ref[0] == 0) | (place_ref[0] == GX // 2)
    block = (2 * GZ, HALF)
    shared = first_lane(block) & imaginary_rows(block)

    def load(p, end):
        tile = pairs_ref[2 * end, p]
        row = tile // tiles_here
        pos = tile % tiles_here * FACES + pairs_ref[2 * end + 1, p]
        return jnp.concatenate([in_ref[row * slabs + s, pos] for s in range(slabs)], axis=0)

    def phase_of(table_ref, ends):
        spec = dot(table_ref[...], jnp.concatenate(ends, axis=1))
        spec = spec.astype(jnp.bfloat16).astype(jnp.float32)
        parts = [spec[:GZ], spec[GZ:]]
        phases = []
        for k in range(0, spec.shape[1], 2 * HALF):
            a, b = slice(k, k + HALF), slice(k + HALF, k + 2 * HALF)
            phase = normalised(parts[0][:, a], parts[1][:, a], parts[0][:, b], parts[1][:, b])
            phases.append(jnp.concatenate(phase, axis=0))
        return jnp.concatenate(phases, axis=1)

    def join(special):
        if special:
            keep = jnp.where(shared, 0.0, 1.0).astype(jnp.bfloat16)
            lane = lax.broadcasted_iota(jnp.int32, block, 1)
            lasts = [jnp.zeros(block, jnp.bfloat16)] * 2
            for p in range(total):
                for end in (0, 1):
                    lasts[end] = jnp.where(lane == p, load(p, end)[:, 0:1], lasts[end])
            last = dot(wzi_last_ref[...], phase_of(wz_last_ref, lasts)).astype(jnp.bfloat16)
        group = 16 if total % 16 == 0 else 8
        for p in range(0, total, group):
            ends = [load(q, end) for q in range(p, p + group) for end in (0, 1)]
            if special:
                ends = [end * keep for end in ends]
            w = dot(wzi_ref[...], phase_of(wz_ref, ends)).astype(jnp.bfloat16)
            for k, q in enumerate(range(p, p + group)):
                whole = w[:, k * HALF : (k + 1) * HALF]
                if special:
                    whole = jnp.where(shared, last[:, q : q + 1], whole)
                for s in range(slabs):
                    out_ref[q // pairs_here * slabs + s, q % pairs_here] = whole[
                        s * slab_rows : (s + 1) * slab_rows
                    ]

    @pl.when(both_real)
    def _():
        join(True)

    @pl.when(jnp.logical_not(both_real))
    def _():
        join(False)


def correlate(spread, pairs, place, slabs, tiles_here):
    devices, _, slab_rows, _ = spread.shape
    pairs_here = pairs.shape[1] * slabs // devices
    tables = z_tables()
    vmem = pl.BlockSpec(memory_space=pltpu.VMEM)
    smem = pl.BlockSpec(memory_space=pltpu.SMEM)
    return pl.pallas_call(
        functools.partial(correlate_kernel, slabs, tiles_here),
        in_specs=[smem, smem] + [vmem] * (1 + len(tables)),
        out_specs=vmem,
        out_shape=jax.ShapeDtypeStruct((devices, pairs_here, slab_rows, HALF), jnp.bfloat16),
        compiler_params=pltpu.CompilerParams(vmem_limit_bytes=VMEM_BYTES),
        name="correlate",
    )(pairs, place, spread, *(jnp.asarray(t) for t in tables))


def synthesise_kernel(in_ref, wx_ref, wy_ref, out_ref, maps_ref, sems):
    pairs_here, slab_rows = in_ref.shape[1:3]
    zrows = slab_rows // 2
    units = zrows // PLANES
    block = (slab_rows, HALF)
    lane0, imaginary = first_lane(block), imaginary_rows(block)
    sign = jnp.where(imaginary, -1.0, 1.0)
    groups = (units, 2 * PLANES, HALF)
    zpart = zrows // sems.shape[1]
    rows = PLANES * GX

    def leave(p, part):
        zs = pl.ds(part * zpart, zpart)
        return pltpu.make_async_copy(maps_ref.at[p, zs], out_ref.at[p, zs], sems.at[p, part])

    for p in range(pairs_here):
        blocks = [None] * GX
        for j in (0, GX // 2):
            blocks[j] = in_ref[j, p].astype(jnp.float32)
        for j in range(1, GX // 2):
            here, mirror = in_ref[j, p].astype(jnp.float32), in_ref[GX - j, p].astype(jnp.float32)
            swapped = pltpu.roll(mirror.reshape(groups), PLANES, 1).reshape(block)
            blocks[j] = jnp.where(lane0, here + swapped, here)
            blocks[GX - j] = jnp.where(lane0, sign * (here - swapped), mirror)
        stacked = jnp.concatenate(
            [
                jnp.concatenate([b[u * 2 * PLANES : (u + 1) * 2 * PLANES] for b in blocks], axis=0)
                for u in range(units)
            ],
            axis=1,
        ).astype(jnp.bfloat16)
        v = dot(wx_ref[...], stacked).astype(jnp.bfloat16)
        cells = [
            jnp.concatenate([v[:rows, k : k + HALF], v[rows:, k : k + HALF]], axis=1)
            for k in range(0, units * HALF, HALF)
        ]
        for part in range(sems.shape[1]):
            of = cells[part * zpart // PLANES : (part + 1) * zpart // PLANES]
            maps = dot(jnp.concatenate(of, axis=0), wy_ref[...])
            maps_ref[p, part * zpart : (part + 1) * zpart] = maps.reshape(zpart, GX, GY)
            leave(p, part).start()
    for p in range(pairs_here):
        for part in range(sems.shape[1]):
            leave(p, part).wait()


def synthesise(returned):
    _, pairs_here, slab_rows, _ = returned.shape
    tables = (inverse_x_table(), half_y_inverse())
    shape = (pairs_here, slab_rows // 2, GX, GY)
    vmem = pl.BlockSpec(memory_space=pltpu.VMEM)
    return pl.pallas_call(
        synthesise_kernel,
        in_specs=[vmem] * (1 + len(tables)),
        out_specs=pl.BlockSpec(memory_space=pl.ANY),
        out_shape=jax.ShapeDtypeStruct(shape, jnp.float32),
        scratch_shapes=[
            pltpu.VMEM(shape, jnp.float32),
            pltpu.SemaphoreType.DMA((pairs_here, slab_rows // (8 * PLANES))),
        ],
        compiler_params=pltpu.CompilerParams(vmem_limit_bytes=VMEM_BYTES),
        name="synthesise",
    )(returned, *(jnp.asarray(t) for t in tables))


def shards(band, pairs, extents):
    tiles, slabs = lax.axis_size("tile"), lax.axis_size("zslab")
    zrows = band.shape[2]
    if tiles * slabs != GX or zrows % (4 * PLANES) or pairs.shape[0] % 8 or pairs.shape[0] % tiles:
        return general_shards(band, pairs, extents)
    pairs, extents = pairs.T, extents.T
    tile = lax.axis_index("tile").astype(jnp.int32)
    device = tile * slabs + lax.axis_index("zslab").astype(jnp.int32)
    spectra = analyse(band, pairs, extents, tile[None])
    spread = lax.all_to_all(spectra, ("tile", "zslab"), split_axis=0, concat_axis=0, tiled=True)
    w = correlate(spread, pairs, device[None], slabs, band.shape[0])
    returned = lax.all_to_all(w, ("tile", "zslab"), split_axis=0, concat_axis=0, tiled=True)
    return synthesise(returned)


def solution(mesh):
    placed = (P("tile", None, "zslab", None, None), P(), P())
    return jax.shard_map(
        shards,
        mesh=mesh,
        in_specs=placed,
        out_specs=P("tile", "zslab", None, None),
        check_vma=False,
    )
```

```python
import functools
import math


import jax
import jax.numpy as jnp
import numpy as np
from jax import lax
from jax.experimental import pallas as pl
from jax.experimental.pallas import tpu as pltpu
from jax.sharding import PartitionSpec as P

GX = 32
GY = 256
GZ = 128
FACES = 4


def dft_tables(length):
    indices = jnp.arange(length, dtype=jnp.int32)
    modular = indices[:, None] * indices[None, :] % length
    angles = modular.astype(jnp.float32) * (2.0 * math.pi / length)
    factor = 1.0 / math.sqrt(length)
    return (
        (jnp.cos(angles) * factor).astype(jnp.bfloat16),
        (jnp.sin(angles) * factor).astype(jnp.bfloat16),
    )


def product(form, left, right):
    return jnp.einsum(form, left, right, preferred_element_type=jnp.float32)


def reduce_resolution(image_volume, crop_bounds):
    row_mask = (
        jnp.arange(image_volume.shape[2], dtype=jnp.int32)[None, :] < crop_bounds[:, 0:1]
    ).astype(jnp.bfloat16)
    col_mask = (
        jnp.arange(image_volume.shape[3], dtype=jnp.int32)[None, :] < crop_bounds[:, 1:2]
    ).astype(jnp.bfloat16)
    masked = image_volume * row_mask[:, None, :, None] * col_mask[:, None, None, :]
    raw_cols = jnp.arange(image_volume.shape[3], dtype=jnp.int32)
    pooled_cols = jnp.arange(GY, dtype=jnp.int32)
    pooling = jnp.where(raw_cols[:, None] // 2 == pooled_cols[None, :], 0.5, 0.0).astype(
        jnp.bfloat16
    )
    along_pooled = product("szxy,yk->szxk", masked, pooling)
    shaped = along_pooled.reshape(image_volume.shape[0], image_volume.shape[1], GX, 2, GY)
    return (shaped[:, :, :, 0, :] + shaped[:, :, :, 1, :]).astype(jnp.bfloat16)


def cross_phase(owner_re, owner_im, pairs, tiles_here):
    first_dev = pairs[:, 0] // tiles_here
    first_pos = pairs[:, 0] % tiles_here * FACES + pairs[:, 1]
    second_tile_device = pairs[:, 2] // tiles_here
    second_pos = pairs[:, 2] % tiles_here * FACES + pairs[:, 3]
    first_re = owner_re[first_dev, :, first_pos].astype(jnp.float32)
    first_im = owner_im[first_dev, :, first_pos].astype(jnp.float32)
    second_re = owner_re[second_tile_device, :, second_pos].astype(jnp.float32)
    second_im = owner_im[second_tile_device, :, second_pos].astype(jnp.float32)
    cross_re = first_re * second_re + first_im * second_im
    cross_im = first_im * second_re - first_re * second_im
    scaled = jnp.sqrt(cross_re * cross_re + cross_im * cross_im + 1.0)
    return ((cross_re / scaled).astype(jnp.bfloat16), (cross_im / scaled).astype(jnp.bfloat16))


def inverse_z(phase_real_part, phase_im, tables_z):
    w_re = (
        product("pmjk,mz->pzjk", phase_real_part, tables_z[0])
        - product("pmjk,mz->pzjk", phase_im, tables_z[1])
    ).astype(jnp.bfloat16)
    w_im = (
        product("pmjk,mz->pzjk", phase_im, tables_z[0])
        + product("pmjk,mz->pzjk", phase_real_part, tables_z[1])
    ).astype(jnp.bfloat16)
    return (w_re, w_im)


def inverse_x(w_re, w_im, tables_x):
    v_re = (
        product("pzjk,jx->pzxk", w_re, tables_x[0]) - product("pzjk,jx->pzxk", w_im, tables_x[1])
    ).astype(jnp.bfloat16)
    v_im = (
        product("pzjk,jx->pzxk", w_im, tables_x[0]) + product("pzjk,jx->pzxk", w_re, tables_x[1])
    ).astype(jnp.bfloat16)
    return (v_re, v_im)


def general_shards(band, pairs, extents):
    tables_x = dft_tables(GX)
    tables_y = dft_tables(GY)
    tables_z = dft_tables(GZ)
    tiles_here = band.shape[0]
    slots = tiles_here * FACES
    zrows = band.shape[2]
    tile_pos = lax.axis_index("tile")
    global_slot = tile_pos * slots + jnp.arange(slots, dtype=jnp.int32)
    first_slot = pairs[:, 0] * FACES + pairs[:, 1]
    second_slot = pairs[:, 2] * FACES + pairs[:, 3]
    matches = (
        (first_slot[None, :] == global_slot[:, None])
        | (second_slot[None, :] == global_slot[:, None])
    ).astype(jnp.int32)
    crop_bounds = jnp.sum(matches[:, :, None] * extents[None, :, :], axis=1)
    image_volume = band.reshape(slots, zrows, 2 * GX, 2 * GY)
    reduced_volume = reduce_resolution(image_volume, crop_bounds)
    y_re = product("szxy,yk->szxk", reduced_volume, tables_y[0]).astype(jnp.bfloat16)
    y_im = (-product("szxy,yk->szxk", reduced_volume, tables_y[1])).astype(jnp.bfloat16)
    x_re = (
        product("szxk,xj->szjk", y_re, tables_x[0]) + product("szxk,xj->szjk", y_im, tables_x[1])
    ).astype(jnp.bfloat16)
    x_im = (
        product("szxk,xj->szjk", y_im, tables_x[0]) - product("szxk,xj->szjk", y_re, tables_x[1])
    ).astype(jnp.bfloat16)
    kx_part = GX // lax.axis_size("zslab")
    re_in = lax.all_to_all(x_re, "zslab", split_axis=2, concat_axis=1, tiled=True)
    im_in = lax.all_to_all(x_im, "zslab", split_axis=2, concat_axis=1, tiled=True)
    out_re = (
        product("szjk,zm->msjk", re_in, tables_z[0]) + product("szjk,zm->msjk", im_in, tables_z[1])
    ).astype(jnp.bfloat16)
    out_im = (
        product("szjk,zm->msjk", im_in, tables_z[0]) - product("szjk,zm->msjk", re_in, tables_z[1])
    ).astype(jnp.bfloat16)
    tile_count = lax.axis_size("tile")
    kz_part = GZ // tile_count
    spectra = (
        lax.all_to_all(out_re, "tile", split_axis=0, concat_axis=0, tiled=True),
        lax.all_to_all(out_im, "tile", split_axis=0, concat_axis=0, tiled=True),
    )
    owner_re = spectra[0].reshape(tile_count, kz_part, slots, kx_part, GY)
    owner_im = spectra[1].reshape(tile_count, kz_part, slots, kx_part, GY)
    phase_real_part, phase_im = cross_phase(owner_re, owner_im, pairs, tiles_here)
    returned = (
        lax.all_to_all(phase_real_part, "tile", split_axis=0, concat_axis=1, tiled=True),
        lax.all_to_all(phase_im, "tile", split_axis=0, concat_axis=1, tiled=True),
    )
    w_re, w_im = inverse_z(returned[0], returned[1], tables_z)
    v_re, v_im = inverse_x(
        lax.all_to_all(w_re, "zslab", split_axis=1, concat_axis=2, tiled=True),
        lax.all_to_all(w_im, "zslab", split_axis=1, concat_axis=2, tiled=True),
        tables_x,
    )
    return product("pzxk,ky->pzxy", v_re, tables_y[0]) - product("pzxk,ky->pzxy", v_im, tables_y[1])


HALF = GY // 2
PLANES = 4
VMEM_BYTES = 32 * 1024 * 1024


def host_tables(length):
    indices = np.arange(length, dtype=np.int32)
    modular = indices[:, None] * indices[None, :] % length
    angles = modular.astype(np.float32) * np.float32(2.0 * math.pi / length)
    factor = np.float32(1.0 / math.sqrt(length))
    return (
        (np.cos(angles) * factor).astype(jnp.bfloat16),
        (np.sin(angles) * factor).astype(jnp.bfloat16),
    )


def half_y_table():
    cosine, sine = host_tables(GY)
    imag = -sine[:, :HALF]
    imag[:, 0] = cosine[:, HALF]
    return np.concatenate([cosine[:, :HALF], imag], axis=1)


def paired_y_table():
    table = np.zeros((2 * GY, GY), jnp.bfloat16)
    table[::2] = half_y_table() * np.array(0.5, jnp.bfloat16)
    table[:, [0, HALF]] *= np.array(0.5, jnp.bfloat16)
    return table


def half_y_inverse():
    cosine, sine = host_tables(GY)
    two = np.array(2.0, jnp.bfloat16)
    real = cosine[:HALF, :] * two
    real[0] = cosine[0]
    imag = -sine[:HALF, :] * two
    imag[0] = cosine[HALF]
    return np.concatenate([real, imag], axis=0)


def mirror_order():
    order = [0, GX // 2]
    for j in range(1, GX // 2):
        order += [j, GX - j]
    return order


def complex_blocks(length, sign):
    cosine, sine = (table.astype(np.float32) for table in host_tables(length))
    return np.array([[cosine, -sign * sine], [sign * sine, cosine]])


def forward_x_table():
    table = np.einsum("oijx,az->joaizx", complex_blocks(GX, -1), np.eye(PLANES))[mirror_order()]
    table = table.reshape(2 * GX * PLANES, 2, PLANES, GX)
    woven = table[:, :, :2].transpose(0, 1, 3, 2).reshape(-1, 2, 2 * GX)
    plain = table[:, :, 2:].reshape(-1, 2, (PLANES - 2) * GX)
    table = np.concatenate([woven, plain], axis=2)
    return table.reshape(2 * GX * PLANES, -1).astype(jnp.bfloat16)


def inverse_x_table():
    table = np.einsum("oijx,az->oaxjiz", complex_blocks(GX, 1), np.eye(PLANES))
    return table.reshape(2 * PLANES * GX, -1).astype(jnp.bfloat16)


def z_rows():
    return np.arange(2 * GZ).reshape(2, GZ // PLANES, PLANES).transpose(1, 0, 2).reshape(-1)


def z_tables():
    forward, inverse = (
        complex_blocks(GZ, sign).transpose(0, 2, 1, 3).reshape(2 * GZ, 2 * GZ) for sign in (-1, 1)
    )
    none = np.zeros((2 * GZ, GZ), np.float32)
    forward_last = np.concatenate([none, forward[:, :GZ]], axis=1)
    inverse_last = np.concatenate([none.T, inverse[:GZ]], axis=0)
    order = z_rows()
    return [
        np.ascontiguousarray(table).astype(jnp.bfloat16)
        for table in (
            forward[:, order],
            inverse[order],
            forward_last[:, order],
            inverse_last[order],
        )
    ]


def imaginary_rows(shape):
    return lax.broadcasted_iota(jnp.int32, shape, 0) % (2 * PLANES) >= PLANES


def first_lane(shape):
    return lax.broadcasted_iota(jnp.int32, shape, 1) == 0


def dot(left, right):
    return jnp.dot(left, right, preferred_element_type=jnp.float32)


def analyse_kernel(
    slots, pairs_ref, extents_ref, tile_ref, *rest
):
    band_refs, (wy_ref, wx_ref, out_ref, crop_ref) = rest[:-4], rest[-4:]
    slot = pl.program_id(0)

    @pl.when(slot == 0)
    def _():
        for p in range(pairs_ref.shape[1]):
            for end in (0, 1):
                named = pairs_ref[2 * end, p] * FACES + pairs_ref[2 * end + 1, p] - tile_ref[0] * slots

                @pl.when((named >= 0) & (named < slots))
                def _():
                    crop_ref[named, 0] = extents_ref[0, p]
                    crop_ref[named, 1] = extents_ref[1, p]

    across, along = crop_ref[slot, 0], crop_ref[slot, 1]

    def live(k, rows):
        lane = lax.broadcasted_iota(jnp.int32, rows.shape, 1)
        return jnp.where((rows < across) & (k * 128 + lane < along), 1.0, 0.0).astype(jnp.bfloat16)

    def halves(rows):
        return (rows + pltpu.roll(rows, 127, 1)).astype(jnp.bfloat16)

    raw_row = lax.broadcasted_iota(jnp.int32, (2 * GX, 128), 0)
    pooled_row = lax.broadcasted_iota(jnp.int32, (GX, 128), 0)
    even = raw_row % 2 == 0
    groups = (2 * GX // 8, 8, 128)
    lives = [
        (live(k, raw_row), live(k, 2 * pooled_row), live(k, 2 * pooled_row + 1))
        for k in range(len(band_refs))
    ]
    block = (2 * PLANES, HALF)
    lane0, imaginary = first_lane(block), imaginary_rows(block)
    sign = jnp.where(imaginary, -1.0, 1.0)
    twice = jnp.where(lane0, 2.0, 1.0)

    def row_pairs(ref, z, mask, shift):
        raw = (ref[0, 0, z] * mask).astype(jnp.float32)
        return raw + pltpu.roll(raw.reshape(groups), shift, 1).reshape(raw.shape)

    def woven(z):
        return [
            halves(jnp.where(even, row_pairs(ref, z, mask, 7), row_pairs(ref, z + 1, mask, 1)))
            for ref, (mask, _, _) in zip(band_refs, lives)
        ]

    def plain(z):
        parts = []
        for ref, (_, *masks) in zip(band_refs, lives):
            rows = [
                (ref[0, 0, z, pl.ds(a, GX, stride=2), :] * masks[a]).astype(jnp.float32) for a in (0, 1)
            ]
            parts.append(halves(rows[0] + rows[1]))
        return parts

    def pool(z):
        return [
            jnp.concatenate(parts, axis=1)
            for parts in (woven(z), *(plain(z + k) for k in range(2, PLANES)))
        ]

    zpart = 4 * PLANES
    zrows = band_refs[0].shape[2]
    planes = sum((pool(z) for z in range(0, zrows, PLANES)), [])
    y = dot(jnp.concatenate(planes, axis=0), wy_ref[...]).astype(jnp.bfloat16)
    y = y.reshape(zrows // PLANES, PLANES * GX, GY)

    def store(start, spectra):
        def at(n):
            rows = spectra[2 * PLANES * n : 2 * PLANES * (n + 1)]
            return [rows[:, k : k + HALF] for k in range(0, rows.shape[1], HALF)]

        def put(j, blocks):
            rows = slice(2 * start, 2 * (start + zpart))
            out_ref[j, 0, rows] = jnp.concatenate(blocks, axis=0).astype(jnp.bfloat16)

        put(0, [a * twice for a in at(0)])
        put(GX // 2, [a * twice for a in at(1)])
        for j in range(1, GX // 2):
            here, mirror = at(2 * j), at(2 * j + 1)
            put(j, [jnp.where(lane0, a + sign * b, a) for a, b in zip(here, mirror)])
            put(
                GX - j,
                [
                    jnp.where(lane0, pltpu.roll(a - sign * b, PLANES, 0), b)
                    for a, b in zip(here, mirror)
                ],
            )

    for start in range(0, zrows, zpart):
        units = [
            jnp.concatenate([y[unit, :, :HALF], y[unit, :, HALF:]], axis=0)
            for unit in range(start // PLANES, (start + zpart) // PLANES)
        ]
        store(start, dot(wx_ref[...], jnp.concatenate(units, axis=1)))


def analyse(band, pairs, extents, tile):
    slots, zrows = band.shape[0] * FACES, band.shape[2]
    tables = (paired_y_table(), forward_x_table())
    whole = [pl.BlockSpec(t.shape, lambda i, *_: (0, 0)) for t in tables]
    lane_blocks = 2 * GY // 128
    return pl.pallas_call(
        functools.partial(analyse_kernel, slots),
        grid_spec=pltpu.PrefetchScalarGridSpec(
            num_scalar_prefetch=3,
            grid=(slots,),
            in_specs=[
                pl.BlockSpec(
                    (1, 1, zrows, 2 * GX, 128),
                    lambda i, *_, k=k: (i // FACES, i % FACES, 0, 0, k),
                )
                for k in range(lane_blocks)
            ]
            + whole,
            out_specs=pl.BlockSpec((GX, 1, 2 * zrows, HALF), lambda i, *_: (0, i, 0, 0)),
            scratch_shapes=[pltpu.SMEM((slots, 2), jnp.int32)],
        ),
        out_shape=jax.ShapeDtypeStruct((GX, slots, 2 * zrows, HALF), jnp.bfloat16),
        compiler_params=pltpu.CompilerParams(vmem_limit_bytes=VMEM_BYTES + VMEM_BYTES * 3 // 4),
        name="analyse",
    )(pairs, extents, tile, *[band] * lane_blocks, *(jnp.asarray(t) for t in tables))


def normalised(a_re, a_im, b_re, b_im):
    cross_re = a_re * b_re + a_im * b_im
    cross_im = a_im * b_re - a_re * b_im
    scale = lax.rsqrt(cross_re * cross_re + cross_im * cross_im + 1.0)
    return (cross_re * scale).astype(jnp.bfloat16), (cross_im * scale).astype(jnp.bfloat16)


def correlate_kernel(
    sizes, tiles_here, pairs_ref, place_ref, in_ref, wz_ref, wzi_ref, wz_last_ref, wzi_last_ref, out_ref
):
    x, y, cores = sizes
    slabs = y * cores

    def place_of(owner, s):
        return owner // x * (y * x * cores) + owner % x * cores + s // cores * (x * cores) + s % cores

    total = pairs_ref.shape[1]
    pairs_here = out_ref.shape[1]
    slab_rows = out_ref.shape[2]
    both_real = (place_ref[0] == 0) | (place_ref[0] == GX // 2)
    block = (2 * GZ, HALF)
    shared = first_lane(block) & imaginary_rows(block)

    def load(p, end):
        tile = pairs_ref[2 * end, p]
        row = tile // tiles_here
        pos = tile % tiles_here * FACES + pairs_ref[2 * end + 1, p]
        return jnp.concatenate([in_ref[place_of(row, s), pos] for s in range(slabs)], axis=0)

    def phase_of(table_ref, ends):
        spec = dot(table_ref[...], jnp.concatenate(ends, axis=1))
        spec = spec.astype(jnp.bfloat16).astype(jnp.float32)
        parts = [spec[:GZ], spec[GZ:]]
        phases = []
        for k in range(0, spec.shape[1], 2 * HALF):
            a, b = slice(k, k + HALF), slice(k + HALF, k + 2 * HALF)
            phase = normalised(parts[0][:, a], parts[1][:, a], parts[0][:, b], parts[1][:, b])
            phases.append(jnp.concatenate(phase, axis=0))
        return jnp.concatenate(phases, axis=1)

    def join(special):
        if special:
            keep = jnp.where(shared, 0.0, 1.0).astype(jnp.bfloat16)
            lane = lax.broadcasted_iota(jnp.int32, block, 1)
            lasts = [jnp.zeros(block, jnp.bfloat16)] * 2
            for p in range(total):
                for end in (0, 1):
                    lasts[end] = jnp.where(lane == p, load(p, end)[:, 0:1], lasts[end])
            last = dot(wzi_last_ref[...], phase_of(wz_last_ref, lasts)).astype(jnp.bfloat16)
        group = 16 if total % 16 == 0 else 8
        for p in range(0, total, group):
            ends = [load(q, end) for q in range(p, p + group) for end in (0, 1)]
            if special:
                ends = [end * keep for end in ends]
            w = dot(wzi_ref[...], phase_of(wz_ref, ends)).astype(jnp.bfloat16)
            for k, q in enumerate(range(p, p + group)):
                whole = w[:, k * HALF : (k + 1) * HALF]
                if special:
                    whole = jnp.where(shared, last[:, q : q + 1], whole)
                for s in range(slabs):
                    out_ref[place_of(q // pairs_here, s), q % pairs_here] = whole[
                        s * slab_rows : (s + 1) * slab_rows
                    ]

    @pl.when(both_real)
    def _():
        join(True)

    @pl.when(jnp.logical_not(both_real))
    def _():
        join(False)


def correlate(spread, pairs, place, sizes, tiles_here):
    devices, _, slab_rows, _ = spread.shape
    pairs_here = pairs.shape[1] * sizes[1] * sizes[2] // devices
    tables = z_tables()
    vmem = pl.BlockSpec(memory_space=pltpu.VMEM)
    smem = pl.BlockSpec(memory_space=pltpu.SMEM)
    return pl.pallas_call(
        functools.partial(correlate_kernel, sizes, tiles_here),
        in_specs=[smem, smem] + [vmem] * (1 + len(tables)),
        out_specs=vmem,
        out_shape=jax.ShapeDtypeStruct((devices, pairs_here, slab_rows, HALF), jnp.bfloat16),
        compiler_params=pltpu.CompilerParams(vmem_limit_bytes=VMEM_BYTES),
        name="correlate",
    )(pairs, place, spread, *(jnp.asarray(t) for t in tables))


def synthesise_kernel(in_ref, wx_ref, wy_ref, out_ref, maps_ref, sems):
    pairs_here, slab_rows = in_ref.shape[1:3]
    zrows = slab_rows // 2
    units = zrows // PLANES
    block = (slab_rows, HALF)
    lane0, imaginary = first_lane(block), imaginary_rows(block)
    sign = jnp.where(imaginary, -1.0, 1.0)
    groups = (units, 2 * PLANES, HALF)
    zpart = zrows // sems.shape[1]
    rows = PLANES * GX

    def leave(p, part):
        zs = pl.ds(part * zpart, zpart)
        return pltpu.make_async_copy(maps_ref.at[p, zs], out_ref.at[p, zs], sems.at[p, part])

    for p in range(pairs_here):
        blocks = [None] * GX
        for j in (0, GX // 2):
            blocks[j] = in_ref[j, p].astype(jnp.float32)
        for j in range(1, GX // 2):
            here, mirror = in_ref[j, p].astype(jnp.float32), in_ref[GX - j, p].astype(jnp.float32)
            swapped = pltpu.roll(mirror.reshape(groups), PLANES, 1).reshape(block)
            blocks[j] = jnp.where(lane0, here + swapped, here)
            blocks[GX - j] = jnp.where(lane0, sign * (here - swapped), mirror)
        stacked = jnp.concatenate(
            [
                jnp.concatenate([b[u * 2 * PLANES : (u + 1) * 2 * PLANES] for b in blocks], axis=0)
                for u in range(units)
            ],
            axis=1,
        ).astype(jnp.bfloat16)
        v = dot(wx_ref[...], stacked).astype(jnp.bfloat16)
        cells = [
            jnp.concatenate([v[:rows, k : k + HALF], v[rows:, k : k + HALF]], axis=1)
            for k in range(0, units * HALF, HALF)
        ]
        for part in range(sems.shape[1]):
            of = cells[part * zpart // PLANES : (part + 1) * zpart // PLANES]
            maps = dot(jnp.concatenate(of, axis=0), wy_ref[...])
            maps_ref[p, part * zpart : (part + 1) * zpart] = maps.reshape(zpart, GX, GY)
            leave(p, part).start()
    for p in range(pairs_here):
        for part in range(sems.shape[1]):
            leave(p, part).wait()


def synthesise(returned):
    _, pairs_here, slab_rows, _ = returned.shape
    tables = (inverse_x_table(), half_y_inverse())
    shape = (pairs_here, slab_rows // 2, GX, GY)
    vmem = pl.BlockSpec(memory_space=pltpu.VMEM)
    return pl.pallas_call(
        synthesise_kernel,
        in_specs=[vmem] * (1 + len(tables)),
        out_specs=pl.BlockSpec(memory_space=pl.ANY),
        out_shape=jax.ShapeDtypeStruct(shape, jnp.float32),
        scratch_shapes=[
            pltpu.VMEM(shape, jnp.float32),
            pltpu.SemaphoreType.DMA((pairs_here, slab_rows // (8 * PLANES))),
        ],
        compiler_params=pltpu.CompilerParams(vmem_limit_bytes=VMEM_BYTES),
        name="synthesise",
    )(returned, *(jnp.asarray(t) for t in tables))


ORDER = ("z", "y", "x", "core")


def placed_shards(band, pairs, extents):
    x, y, cores = (lax.axis_size(axis) for axis in ("x", "y", "core"))
    pairs, extents = pairs.T, extents.T
    tile = (lax.axis_index("z") * x + lax.axis_index("x")).astype(jnp.int32)
    device = lax.axis_index(ORDER).astype(jnp.int32)
    spectra = analyse(band, pairs, extents, tile[None])
    spread = lax.all_to_all(spectra, ORDER, split_axis=0, concat_axis=0, tiled=True)
    w = correlate(spread, pairs, device[None], (x, y, cores), band.shape[0])
    returned = lax.all_to_all(w, ORDER, split_axis=0, concat_axis=0, tiled=True)
    return synthesise(returned)


def solution(mesh):
    tiles, slabs = mesh.devices.shape
    cores = 2
    side = max(slabs // cores, 1)
    if tiles * slabs == GX and slabs % cores == 0 and tiles % side == 0:
        over = jax.sharding.Mesh(
            mesh.devices.reshape(tiles // side, side, slabs // cores, cores), ("z", "x", "y", "core")
        )
        tile, slab, body = ("z", "x"), ("y", "core"), placed_shards
    else:
        over, tile, slab, body = mesh, "tile", "zslab", general_shards
    return jax.shard_map(
        body,
        mesh=over,
        in_specs=(P(tile, None, slab, None, None), P(), P()),
        out_specs=P(tile, slab, None, None),
        check_vma=False,
    )
```

```python
import functools
import math


import jax
import jax.numpy as jnp
import numpy as np
from jax import lax
from jax.experimental import pallas as pl
from jax.experimental.pallas import tpu as pltpu
from jax.sharding import PartitionSpec as P

GX = 32
GY = 256
GZ = 128
FACES = 4


def dft_tables(length):
    indices = jnp.arange(length, dtype=jnp.int32)
    modular = indices[:, None] * indices[None, :] % length
    angles = modular.astype(jnp.float32) * (2.0 * math.pi / length)
    factor = 1.0 / math.sqrt(length)
    return (
        (jnp.cos(angles) * factor).astype(jnp.bfloat16),
        (jnp.sin(angles) * factor).astype(jnp.bfloat16),
    )


def product(form, left, right):
    return jnp.einsum(form, left, right, preferred_element_type=jnp.float32)


def reduce_resolution(image_volume, crop_bounds):
    row_mask = (
        jnp.arange(image_volume.shape[2], dtype=jnp.int32)[None, :] < crop_bounds[:, 0:1]
    ).astype(jnp.bfloat16)
    col_mask = (
        jnp.arange(image_volume.shape[3], dtype=jnp.int32)[None, :] < crop_bounds[:, 1:2]
    ).astype(jnp.bfloat16)
    masked = image_volume * row_mask[:, None, :, None] * col_mask[:, None, None, :]
    raw_cols = jnp.arange(image_volume.shape[3], dtype=jnp.int32)
    pooled_cols = jnp.arange(GY, dtype=jnp.int32)
    pooling = jnp.where(raw_cols[:, None] // 2 == pooled_cols[None, :], 0.5, 0.0).astype(
        jnp.bfloat16
    )
    along_pooled = product("szxy,yk->szxk", masked, pooling)
    shaped = along_pooled.reshape(image_volume.shape[0], image_volume.shape[1], GX, 2, GY)
    return (shaped[:, :, :, 0, :] + shaped[:, :, :, 1, :]).astype(jnp.bfloat16)


def cross_phase(owner_re, owner_im, pairs, tiles_here):
    first_dev = pairs[:, 0] // tiles_here
    first_pos = pairs[:, 0] % tiles_here * FACES + pairs[:, 1]
    second_tile_device = pairs[:, 2] // tiles_here
    second_pos = pairs[:, 2] % tiles_here * FACES + pairs[:, 3]
    first_re = owner_re[first_dev, :, first_pos].astype(jnp.float32)
    first_im = owner_im[first_dev, :, first_pos].astype(jnp.float32)
    second_re = owner_re[second_tile_device, :, second_pos].astype(jnp.float32)
    second_im = owner_im[second_tile_device, :, second_pos].astype(jnp.float32)
    cross_re = first_re * second_re + first_im * second_im
    cross_im = first_im * second_re - first_re * second_im
    scaled = jnp.sqrt(cross_re * cross_re + cross_im * cross_im + 1.0)
    return ((cross_re / scaled).astype(jnp.bfloat16), (cross_im / scaled).astype(jnp.bfloat16))


def inverse_z(phase_real_part, phase_im, tables_z):
    w_re = (
        product("pmjk,mz->pzjk", phase_real_part, tables_z[0])
        - product("pmjk,mz->pzjk", phase_im, tables_z[1])
    ).astype(jnp.bfloat16)
    w_im = (
        product("pmjk,mz->pzjk", phase_im, tables_z[0])
        + product("pmjk,mz->pzjk", phase_real_part, tables_z[1])
    ).astype(jnp.bfloat16)
    return (w_re, w_im)


def inverse_x(w_re, w_im, tables_x):
    v_re = (
        product("pzjk,jx->pzxk", w_re, tables_x[0]) - product("pzjk,jx->pzxk", w_im, tables_x[1])
    ).astype(jnp.bfloat16)
    v_im = (
        product("pzjk,jx->pzxk", w_im, tables_x[0]) + product("pzjk,jx->pzxk", w_re, tables_x[1])
    ).astype(jnp.bfloat16)
    return (v_re, v_im)


def general_shards(band, pairs, extents):
    tables_x = dft_tables(GX)
    tables_y = dft_tables(GY)
    tables_z = dft_tables(GZ)
    tiles_here = band.shape[0]
    slots = tiles_here * FACES
    zrows = band.shape[2]
    tile_pos = lax.axis_index("tile")
    global_slot = tile_pos * slots + jnp.arange(slots, dtype=jnp.int32)
    first_slot = pairs[:, 0] * FACES + pairs[:, 1]
    second_slot = pairs[:, 2] * FACES + pairs[:, 3]
    matches = (
        (first_slot[None, :] == global_slot[:, None])
        | (second_slot[None, :] == global_slot[:, None])
    ).astype(jnp.int32)
    crop_bounds = jnp.sum(matches[:, :, None] * extents[None, :, :], axis=1)
    image_volume = band.reshape(slots, zrows, 2 * GX, 2 * GY)
    reduced_volume = reduce_resolution(image_volume, crop_bounds)
    y_re = product("szxy,yk->szxk", reduced_volume, tables_y[0]).astype(jnp.bfloat16)
    y_im = (-product("szxy,yk->szxk", reduced_volume, tables_y[1])).astype(jnp.bfloat16)
    x_re = (
        product("szxk,xj->szjk", y_re, tables_x[0]) + product("szxk,xj->szjk", y_im, tables_x[1])
    ).astype(jnp.bfloat16)
    x_im = (
        product("szxk,xj->szjk", y_im, tables_x[0]) - product("szxk,xj->szjk", y_re, tables_x[1])
    ).astype(jnp.bfloat16)
    kx_part = GX // lax.axis_size("zslab")
    re_in = lax.all_to_all(x_re, "zslab", split_axis=2, concat_axis=1, tiled=True)
    im_in = lax.all_to_all(x_im, "zslab", split_axis=2, concat_axis=1, tiled=True)
    out_re = (
        product("szjk,zm->msjk", re_in, tables_z[0]) + product("szjk,zm->msjk", im_in, tables_z[1])
    ).astype(jnp.bfloat16)
    out_im = (
        product("szjk,zm->msjk", im_in, tables_z[0]) - product("szjk,zm->msjk", re_in, tables_z[1])
    ).astype(jnp.bfloat16)
    tile_count = lax.axis_size("tile")
    kz_part = GZ // tile_count
    spectra = (
        lax.all_to_all(out_re, "tile", split_axis=0, concat_axis=0, tiled=True),
        lax.all_to_all(out_im, "tile", split_axis=0, concat_axis=0, tiled=True),
    )
    owner_re = spectra[0].reshape(tile_count, kz_part, slots, kx_part, GY)
    owner_im = spectra[1].reshape(tile_count, kz_part, slots, kx_part, GY)
    phase_real_part, phase_im = cross_phase(owner_re, owner_im, pairs, tiles_here)
    returned = (
        lax.all_to_all(phase_real_part, "tile", split_axis=0, concat_axis=1, tiled=True),
        lax.all_to_all(phase_im, "tile", split_axis=0, concat_axis=1, tiled=True),
    )
    w_re, w_im = inverse_z(returned[0], returned[1], tables_z)
    v_re, v_im = inverse_x(
        lax.all_to_all(w_re, "zslab", split_axis=1, concat_axis=2, tiled=True),
        lax.all_to_all(w_im, "zslab", split_axis=1, concat_axis=2, tiled=True),
        tables_x,
    )
    return product("pzxk,ky->pzxy", v_re, tables_y[0]) - product("pzxk,ky->pzxy", v_im, tables_y[1])


HALF = GY // 2
PLANES = 4
VMEM_BYTES = 32 * 1024 * 1024


def host_tables(length):
    indices = np.arange(length, dtype=np.int32)
    modular = indices[:, None] * indices[None, :] % length
    angles = modular.astype(np.float32) * np.float32(2.0 * math.pi / length)
    factor = np.float32(1.0 / math.sqrt(length))
    return (
        (np.cos(angles) * factor).astype(jnp.bfloat16),
        (np.sin(angles) * factor).astype(jnp.bfloat16),
    )


def half_y_table():
    cosine, sine = host_tables(GY)
    imag = -sine[:, :HALF]
    imag[:, 0] = cosine[:, HALF]
    return np.concatenate([cosine[:, :HALF], imag], axis=1)


def paired_y_table():
    table = np.zeros((2 * GY, GY), jnp.bfloat16)
    table[::2] = half_y_table() * np.array(0.5, jnp.bfloat16)
    table[:, [0, HALF]] *= np.array(0.5, jnp.bfloat16)
    return table


def half_y_inverse():
    cosine, sine = host_tables(GY)
    two = np.array(2.0, jnp.bfloat16)
    real = cosine[:HALF, :] * two
    real[0] = cosine[0]
    imag = -sine[:HALF, :] * two
    imag[0] = cosine[HALF]
    return np.concatenate([real, imag], axis=0)


def mirror_order():
    order = [0, GX // 2]
    for j in range(1, GX // 2):
        order += [j, GX - j]
    return order


def complex_blocks(length, sign):
    cosine, sine = (table.astype(np.float32) for table in host_tables(length))
    return np.array([[cosine, -sign * sine], [sign * sine, cosine]])


def forward_x_table():
    table = np.einsum("oijx,az->joaizx", complex_blocks(GX, -1), np.eye(PLANES))[mirror_order()]
    table = table.reshape(2 * GX * PLANES, 2, PLANES, GX)
    woven = table[:, :, :2].transpose(0, 1, 3, 2).reshape(-1, 2, 2 * GX)
    plain = table[:, :, 2:].reshape(-1, 2, (PLANES - 2) * GX)
    table = np.concatenate([woven, plain], axis=2)
    return table.reshape(2 * GX * PLANES, -1).astype(jnp.bfloat16)


def inverse_x_table():
    table = np.einsum("oijx,az->oaxjiz", complex_blocks(GX, 1), np.eye(PLANES))
    return table.reshape(2 * PLANES * GX, -1).astype(jnp.bfloat16)


def z_rows():
    return np.arange(2 * GZ).reshape(2, GZ // PLANES, PLANES).transpose(1, 0, 2).reshape(-1)


def z_tables():
    forward, inverse = (
        complex_blocks(GZ, sign).transpose(0, 2, 1, 3).reshape(2 * GZ, 2 * GZ) for sign in (-1, 1)
    )
    none = np.zeros((2 * GZ, GZ), np.float32)
    forward_last = np.concatenate([none, forward[:, :GZ]], axis=1)
    inverse_last = np.concatenate([none.T, inverse[:GZ]], axis=0)
    order = z_rows()
    return [
        np.ascontiguousarray(table).astype(jnp.bfloat16)
        for table in (
            forward[:, order],
            inverse[order],
            forward_last[:, order],
            inverse_last[order],
        )
    ]


def imaginary_rows(shape):
    return lax.broadcasted_iota(jnp.int32, shape, 0) % (2 * PLANES) >= PLANES


def first_lane(shape):
    return lax.broadcasted_iota(jnp.int32, shape, 1) == 0


def dot(left, right):
    return jnp.dot(left, right, preferred_element_type=jnp.float32)


def analyse_kernel(
    slots, pairs_ref, extents_ref, tile_ref, *rest
):
    band_refs, (wy_ref, wx_ref, out_ref, crop_ref) = rest[:-4], rest[-4:]
    slot = pl.program_id(0)

    @pl.when(slot == 0)
    def _():
        for p in range(pairs_ref.shape[1]):
            for end in (0, 1):
                named = pairs_ref[2 * end, p] * FACES + pairs_ref[2 * end + 1, p] - tile_ref[0] * slots

                @pl.when((named >= 0) & (named < slots))
                def _():
                    crop_ref[named, 0] = extents_ref[0, p]
                    crop_ref[named, 1] = extents_ref[1, p]

    across, along = crop_ref[slot, 0], crop_ref[slot, 1]

    def live(k, rows):
        lane = lax.broadcasted_iota(jnp.int32, rows.shape, 1)
        return jnp.where((rows < across) & (k * 128 + lane < along), 1.0, 0.0).astype(jnp.bfloat16)

    def halves(rows):
        return (rows + pltpu.roll(rows, 127, 1)).astype(jnp.bfloat16)

    raw_row = lax.broadcasted_iota(jnp.int32, (2 * GX, 128), 0)
    pooled_row = lax.broadcasted_iota(jnp.int32, (GX, 128), 0)
    even = raw_row % 2 == 0
    groups = (2 * GX // 8, 8, 128)
    lives = [
        (live(k, raw_row), live(k, 2 * pooled_row), live(k, 2 * pooled_row + 1))
        for k in range(len(band_refs))
    ]
    block = (2 * PLANES, HALF)
    lane0, imaginary = first_lane(block), imaginary_rows(block)
    sign = jnp.where(imaginary, -1.0, 1.0)
    twice = jnp.where(lane0, 2.0, 1.0)

    def row_pairs(ref, z, mask, shift):
        raw = (ref[0, 0, z] * mask).astype(jnp.float32)
        return raw + pltpu.roll(raw.reshape(groups), shift, 1).reshape(raw.shape)

    def woven(z):
        return [
            halves(jnp.where(even, row_pairs(ref, z, mask, 7), row_pairs(ref, z + 1, mask, 1)))
            for ref, (mask, _, _) in zip(band_refs, lives)
        ]

    def plain(z):
        parts = []
        for ref, (_, *masks) in zip(band_refs, lives):
            rows = [
                (ref[0, 0, z, pl.ds(a, GX, stride=2), :] * masks[a]).astype(jnp.float32) for a in (0, 1)
            ]
            parts.append(halves(rows[0] + rows[1]))
        return parts

    def pool(z):
        return [
            jnp.concatenate(parts, axis=1)
            for parts in (woven(z), *(plain(z + k) for k in range(2, PLANES)))
        ]

    zpart = 4 * PLANES
    zrows = band_refs[0].shape[2]
    planes = sum((pool(z) for z in range(0, zrows, PLANES)), [])
    y = dot(jnp.concatenate(planes, axis=0), wy_ref[...]).astype(jnp.bfloat16)
    y = y.reshape(zrows // PLANES, PLANES * GX, GY)

    def store(start, spectra):
        def at(n):
            rows = spectra[2 * PLANES * n : 2 * PLANES * (n + 1)]
            return [rows[:, k : k + HALF] for k in range(0, rows.shape[1], HALF)]

        def put(j, blocks):
            rows = slice(2 * start, 2 * (start + zpart))
            out_ref[j, 0, rows] = jnp.concatenate(blocks, axis=0).astype(jnp.bfloat16)

        put(0, [a * twice for a in at(0)])
        put(GX // 2, [a * twice for a in at(1)])
        for j in range(1, GX // 2):
            here, mirror = at(2 * j), at(2 * j + 1)
            put(j, [jnp.where(lane0, a + sign * b, a) for a, b in zip(here, mirror)])
            put(
                GX - j,
                [
                    jnp.where(lane0, pltpu.roll(a - sign * b, PLANES, 0), b)
                    for a, b in zip(here, mirror)
                ],
            )

    for start in range(0, zrows, zpart):
        units = [
            jnp.concatenate([y[unit, :, :HALF], y[unit, :, HALF:]], axis=0)
            for unit in range(start // PLANES, (start + zpart) // PLANES)
        ]
        store(start, dot(wx_ref[...], jnp.concatenate(units, axis=1)))


def analyse(band, pairs, extents, tile):
    slots, zrows = band.shape[0] * FACES, band.shape[2]
    tables = (paired_y_table(), forward_x_table())
    whole = [pl.BlockSpec(t.shape, lambda i, *_: (0, 0)) for t in tables]
    lane_blocks = 2 * GY // 128
    return pl.pallas_call(
        functools.partial(analyse_kernel, slots),
        grid_spec=pltpu.PrefetchScalarGridSpec(
            num_scalar_prefetch=3,
            grid=(slots,),
            in_specs=[
                pl.BlockSpec(
                    (1, 1, zrows, 2 * GX, 128),
                    lambda i, *_, k=k: (i // FACES, i % FACES, 0, 0, k),
                )
                for k in range(lane_blocks)
            ]
            + whole,
            out_specs=pl.BlockSpec((GX, 1, 2 * zrows, HALF), lambda i, *_: (0, i, 0, 0)),
            scratch_shapes=[pltpu.SMEM((slots, 2), jnp.int32)],
        ),
        out_shape=jax.ShapeDtypeStruct((GX, slots, 2 * zrows, HALF), jnp.bfloat16),
        compiler_params=pltpu.CompilerParams(vmem_limit_bytes=VMEM_BYTES + VMEM_BYTES * 3 // 4),
        name="analyse",
    )(pairs, extents, tile, *[band] * lane_blocks, *(jnp.asarray(t) for t in tables))


def normalised(a_re, a_im, b_re, b_im):
    cross_re = a_re * b_re + a_im * b_im
    cross_im = a_im * b_re - a_re * b_im
    scale = lax.rsqrt(cross_re * cross_re + cross_im * cross_im + 1.0)
    return (cross_re * scale).astype(jnp.bfloat16), (cross_im * scale).astype(jnp.bfloat16)


def correlate_kernel(
    sizes, tiles_here, pairs_ref, place_ref, in_ref, wz_ref, wzi_ref, wz_last_ref, wzi_last_ref, out_ref
):
    _, y, cores = sizes
    slabs = y * cores

    def place_of(owner, s):
        return s % cores * (in_ref.shape[0] // cores) + owner * y + s // cores

    total = pairs_ref.shape[1]
    pairs_here = out_ref.shape[1]
    slab_rows = out_ref.shape[2]
    both_real = (place_ref[0] == 0) | (place_ref[0] == GX // 2)
    block = (2 * GZ, HALF)
    shared = first_lane(block) & imaginary_rows(block)

    def load(p, end):
        tile = pairs_ref[2 * end, p]
        row = tile // tiles_here
        pos = tile % tiles_here * FACES + pairs_ref[2 * end + 1, p]
        return jnp.concatenate([in_ref[place_of(row, s), pos] for s in range(slabs)], axis=0)

    def phase_of(table_ref, ends):
        spec = dot(table_ref[...], jnp.concatenate(ends, axis=1))
        spec = spec.astype(jnp.bfloat16).astype(jnp.float32)
        parts = [spec[:GZ], spec[GZ:]]
        phases = []
        for k in range(0, spec.shape[1], 2 * HALF):
            a, b = slice(k, k + HALF), slice(k + HALF, k + 2 * HALF)
            phase = normalised(parts[0][:, a], parts[1][:, a], parts[0][:, b], parts[1][:, b])
            phases.append(jnp.concatenate(phase, axis=0))
        return jnp.concatenate(phases, axis=1)

    def join(special):
        if special:
            keep = jnp.where(shared, 0.0, 1.0).astype(jnp.bfloat16)
            lane = lax.broadcasted_iota(jnp.int32, block, 1)
            lasts = [jnp.zeros(block, jnp.bfloat16)] * 2
            for p in range(total):
                for end in (0, 1):
                    lasts[end] = jnp.where(lane == p, load(p, end)[:, 0:1], lasts[end])
            last = dot(wzi_last_ref[...], phase_of(wz_last_ref, lasts)).astype(jnp.bfloat16)
        group = 16 if total % 16 == 0 else 8
        for p in range(0, total, group):
            ends = [load(q, end) for q in range(p, p + group) for end in (0, 1)]
            if special:
                ends = [end * keep for end in ends]
            w = dot(wzi_ref[...], phase_of(wz_ref, ends)).astype(jnp.bfloat16)
            for k, q in enumerate(range(p, p + group)):
                whole = w[:, k * HALF : (k + 1) * HALF]
                if special:
                    whole = jnp.where(shared, last[:, q : q + 1], whole)
                for s in range(slabs):
                    out_ref[place_of(q // pairs_here, s), q % pairs_here] = whole[
                        s * slab_rows : (s + 1) * slab_rows
                    ]

    @pl.when(both_real)
    def _():
        join(True)

    @pl.when(jnp.logical_not(both_real))
    def _():
        join(False)


def correlate(spread, pairs, place, sizes, tiles_here):
    devices, _, slab_rows, _ = spread.shape
    pairs_here = pairs.shape[1] * sizes[1] * sizes[2] // devices
    tables = z_tables()
    vmem = pl.BlockSpec(memory_space=pltpu.VMEM)
    smem = pl.BlockSpec(memory_space=pltpu.SMEM)
    return pl.pallas_call(
        functools.partial(correlate_kernel, sizes, tiles_here),
        in_specs=[smem, smem] + [vmem] * (1 + len(tables)),
        out_specs=vmem,
        out_shape=jax.ShapeDtypeStruct((devices, pairs_here, slab_rows, HALF), jnp.bfloat16),
        compiler_params=pltpu.CompilerParams(vmem_limit_bytes=VMEM_BYTES),
        name="correlate",
    )(pairs, place, spread, *(jnp.asarray(t) for t in tables))


def synthesise_kernel(in_ref, wx_ref, wy_ref, out_ref, maps_ref, sems):
    pairs_here, slab_rows = in_ref.shape[1:3]
    zrows = slab_rows // 2
    units = zrows // PLANES
    block = (slab_rows, HALF)
    lane0, imaginary = first_lane(block), imaginary_rows(block)
    sign = jnp.where(imaginary, -1.0, 1.0)
    groups = (units, 2 * PLANES, HALF)
    zpart = zrows // sems.shape[1]
    rows = PLANES * GX

    def leave(p, part):
        zs = pl.ds(part * zpart, zpart)
        return pltpu.make_async_copy(maps_ref.at[p, zs], out_ref.at[p, zs], sems.at[p, part])

    for p in range(pairs_here):
        blocks = [None] * GX
        for j in (0, GX // 2):
            blocks[j] = in_ref[j, p].astype(jnp.float32)
        for j in range(1, GX // 2):
            here, mirror = in_ref[j, p].astype(jnp.float32), in_ref[GX - j, p].astype(jnp.float32)
            swapped = pltpu.roll(mirror.reshape(groups), PLANES, 1).reshape(block)
            blocks[j] = jnp.where(lane0, here + swapped, here)
            blocks[GX - j] = jnp.where(lane0, sign * (here - swapped), mirror)
        stacked = jnp.concatenate(
            [
                jnp.concatenate([b[u * 2 * PLANES : (u + 1) * 2 * PLANES] for b in blocks], axis=0)
                for u in range(units)
            ],
            axis=1,
        ).astype(jnp.bfloat16)
        v = dot(wx_ref[...], stacked).astype(jnp.bfloat16)
        cells = [
            jnp.concatenate([v[:rows, k : k + HALF], v[rows:, k : k + HALF]], axis=1)
            for k in range(0, units * HALF, HALF)
        ]
        for part in range(sems.shape[1]):
            of = cells[part * zpart // PLANES : (part + 1) * zpart // PLANES]
            maps = dot(jnp.concatenate(of, axis=0), wy_ref[...])
            maps_ref[p, part * zpart : (part + 1) * zpart] = maps.reshape(zpart, GX, GY)
            leave(p, part).start()
    for p in range(pairs_here):
        for part in range(sems.shape[1]):
            leave(p, part).wait()


def synthesise(returned):
    _, pairs_here, slab_rows, _ = returned.shape
    tables = (inverse_x_table(), half_y_inverse())
    shape = (pairs_here, slab_rows // 2, GX, GY)
    vmem = pl.BlockSpec(memory_space=pltpu.VMEM)
    return pl.pallas_call(
        synthesise_kernel,
        in_specs=[vmem] * (1 + len(tables)),
        out_specs=pl.BlockSpec(memory_space=pl.ANY),
        out_shape=jax.ShapeDtypeStruct(shape, jnp.float32),
        scratch_shapes=[
            pltpu.VMEM(shape, jnp.float32),
            pltpu.SemaphoreType.DMA((pairs_here, slab_rows // (8 * PLANES))),
        ],
        compiler_params=pltpu.CompilerParams(vmem_limit_bytes=VMEM_BYTES),
        name="synthesise",
    )(returned, *(jnp.asarray(t) for t in tables))


ORDER = ("core", "z", "x", "y")


def placed_shards(band, pairs, extents):
    x, y, cores = (lax.axis_size(axis) for axis in ("x", "y", "core"))
    pairs, extents = pairs.T, extents.T
    tile = (lax.axis_index("z") * x + lax.axis_index("x")).astype(jnp.int32)
    device = lax.axis_index(ORDER).astype(jnp.int32)
    spectra = analyse(band, pairs, extents, tile[None])
    spread = lax.all_to_all(spectra, ORDER, split_axis=0, concat_axis=0, tiled=True)
    w = correlate(spread, pairs, device[None], (x, y, cores), band.shape[0])
    returned = lax.all_to_all(w, ORDER, split_axis=0, concat_axis=0, tiled=True)
    return synthesise(returned)


def solution(mesh):
    tiles, slabs = mesh.devices.shape
    cores = 2
    side = max(slabs // cores, 1)
    if tiles * slabs == GX and slabs % cores == 0 and tiles % side == 0:
        over = jax.sharding.Mesh(
            mesh.devices.reshape(tiles // side, side, slabs // cores, cores), ("z", "x", "y", "core")
        )
        tile, slab, body = ("z", "x"), ("y", "core"), placed_shards
    else:
        over, tile, slab, body = mesh, "tile", "zslab", general_shards
    return jax.shard_map(
        body,
        mesh=over,
        in_specs=(P(tile, None, slab, None, None), P(), P()),
        out_specs=P(tile, slab, None, None),
        check_vma=False,
    )
```

```python
import functools
import math


import jax
import jax.numpy as jnp
import numpy as np
from jax import lax
from jax.experimental import pallas as pl
from jax.experimental.pallas import tpu as pltpu
from jax.sharding import PartitionSpec as P

GX = 32
GY = 256
GZ = 128
FACES = 4


def dft_tables(length):
    indices = jnp.arange(length, dtype=jnp.int32)
    modular = indices[:, None] * indices[None, :] % length
    angles = modular.astype(jnp.float32) * (2.0 * math.pi / length)
    factor = 1.0 / math.sqrt(length)
    return (
        (jnp.cos(angles) * factor).astype(jnp.bfloat16),
        (jnp.sin(angles) * factor).astype(jnp.bfloat16),
    )


def product(form, left, right):
    return jnp.einsum(form, left, right, preferred_element_type=jnp.float32)


def reduce_resolution(image_volume, crop_bounds):
    row_mask = (
        jnp.arange(image_volume.shape[2], dtype=jnp.int32)[None, :] < crop_bounds[:, 0:1]
    ).astype(jnp.bfloat16)
    col_mask = (
        jnp.arange(image_volume.shape[3], dtype=jnp.int32)[None, :] < crop_bounds[:, 1:2]
    ).astype(jnp.bfloat16)
    masked = image_volume * row_mask[:, None, :, None] * col_mask[:, None, None, :]
    raw_cols = jnp.arange(image_volume.shape[3], dtype=jnp.int32)
    pooled_cols = jnp.arange(GY, dtype=jnp.int32)
    pooling = jnp.where(raw_cols[:, None] // 2 == pooled_cols[None, :], 0.5, 0.0).astype(
        jnp.bfloat16
    )
    along_pooled = product("szxy,yk->szxk", masked, pooling)
    shaped = along_pooled.reshape(image_volume.shape[0], image_volume.shape[1], GX, 2, GY)
    return (shaped[:, :, :, 0, :] + shaped[:, :, :, 1, :]).astype(jnp.bfloat16)


def cross_phase(owner_re, owner_im, pairs, tiles_here):
    first_dev = pairs[:, 0] // tiles_here
    first_pos = pairs[:, 0] % tiles_here * FACES + pairs[:, 1]
    second_tile_device = pairs[:, 2] // tiles_here
    second_pos = pairs[:, 2] % tiles_here * FACES + pairs[:, 3]
    first_re = owner_re[first_dev, :, first_pos].astype(jnp.float32)
    first_im = owner_im[first_dev, :, first_pos].astype(jnp.float32)
    second_re = owner_re[second_tile_device, :, second_pos].astype(jnp.float32)
    second_im = owner_im[second_tile_device, :, second_pos].astype(jnp.float32)
    cross_re = first_re * second_re + first_im * second_im
    cross_im = first_im * second_re - first_re * second_im
    scaled = jnp.sqrt(cross_re * cross_re + cross_im * cross_im + 1.0)
    return ((cross_re / scaled).astype(jnp.bfloat16), (cross_im / scaled).astype(jnp.bfloat16))


def inverse_z(phase_real_part, phase_im, tables_z):
    w_re = (
        product("pmjk,mz->pzjk", phase_real_part, tables_z[0])
        - product("pmjk,mz->pzjk", phase_im, tables_z[1])
    ).astype(jnp.bfloat16)
    w_im = (
        product("pmjk,mz->pzjk", phase_im, tables_z[0])
        + product("pmjk,mz->pzjk", phase_real_part, tables_z[1])
    ).astype(jnp.bfloat16)
    return (w_re, w_im)


def inverse_x(w_re, w_im, tables_x):
    v_re = (
        product("pzjk,jx->pzxk", w_re, tables_x[0]) - product("pzjk,jx->pzxk", w_im, tables_x[1])
    ).astype(jnp.bfloat16)
    v_im = (
        product("pzjk,jx->pzxk", w_im, tables_x[0]) + product("pzjk,jx->pzxk", w_re, tables_x[1])
    ).astype(jnp.bfloat16)
    return (v_re, v_im)


def general_shards(band, pairs, extents):
    tables_x = dft_tables(GX)
    tables_y = dft_tables(GY)
    tables_z = dft_tables(GZ)
    tiles_here = band.shape[0]
    slots = tiles_here * FACES
    zrows = band.shape[2]
    tile_pos = lax.axis_index("tile")
    global_slot = tile_pos * slots + jnp.arange(slots, dtype=jnp.int32)
    first_slot = pairs[:, 0] * FACES + pairs[:, 1]
    second_slot = pairs[:, 2] * FACES + pairs[:, 3]
    matches = (
        (first_slot[None, :] == global_slot[:, None])
        | (second_slot[None, :] == global_slot[:, None])
    ).astype(jnp.int32)
    crop_bounds = jnp.sum(matches[:, :, None] * extents[None, :, :], axis=1)
    image_volume = band.reshape(slots, zrows, 2 * GX, 2 * GY)
    reduced_volume = reduce_resolution(image_volume, crop_bounds)
    y_re = product("szxy,yk->szxk", reduced_volume, tables_y[0]).astype(jnp.bfloat16)
    y_im = (-product("szxy,yk->szxk", reduced_volume, tables_y[1])).astype(jnp.bfloat16)
    x_re = (
        product("szxk,xj->szjk", y_re, tables_x[0]) + product("szxk,xj->szjk", y_im, tables_x[1])
    ).astype(jnp.bfloat16)
    x_im = (
        product("szxk,xj->szjk", y_im, tables_x[0]) - product("szxk,xj->szjk", y_re, tables_x[1])
    ).astype(jnp.bfloat16)
    kx_part = GX // lax.axis_size("zslab")
    re_in = lax.all_to_all(x_re, "zslab", split_axis=2, concat_axis=1, tiled=True)
    im_in = lax.all_to_all(x_im, "zslab", split_axis=2, concat_axis=1, tiled=True)
    out_re = (
        product("szjk,zm->msjk", re_in, tables_z[0]) + product("szjk,zm->msjk", im_in, tables_z[1])
    ).astype(jnp.bfloat16)
    out_im = (
        product("szjk,zm->msjk", im_in, tables_z[0]) - product("szjk,zm->msjk", re_in, tables_z[1])
    ).astype(jnp.bfloat16)
    tile_count = lax.axis_size("tile")
    kz_part = GZ // tile_count
    spectra = (
        lax.all_to_all(out_re, "tile", split_axis=0, concat_axis=0, tiled=True),
        lax.all_to_all(out_im, "tile", split_axis=0, concat_axis=0, tiled=True),
    )
    owner_re = spectra[0].reshape(tile_count, kz_part, slots, kx_part, GY)
    owner_im = spectra[1].reshape(tile_count, kz_part, slots, kx_part, GY)
    phase_real_part, phase_im = cross_phase(owner_re, owner_im, pairs, tiles_here)
    returned = (
        lax.all_to_all(phase_real_part, "tile", split_axis=0, concat_axis=1, tiled=True),
        lax.all_to_all(phase_im, "tile", split_axis=0, concat_axis=1, tiled=True),
    )
    w_re, w_im = inverse_z(returned[0], returned[1], tables_z)
    v_re, v_im = inverse_x(
        lax.all_to_all(w_re, "zslab", split_axis=1, concat_axis=2, tiled=True),
        lax.all_to_all(w_im, "zslab", split_axis=1, concat_axis=2, tiled=True),
        tables_x,
    )
    return product("pzxk,ky->pzxy", v_re, tables_y[0]) - product("pzxk,ky->pzxy", v_im, tables_y[1])


HALF = GY // 2
PLANES = 4
VMEM_BYTES = 32 * 1024 * 1024


def host_tables(length):
    indices = np.arange(length, dtype=np.int32)
    modular = indices[:, None] * indices[None, :] % length
    angles = modular.astype(np.float32) * np.float32(2.0 * math.pi / length)
    factor = np.float32(1.0 / math.sqrt(length))
    return (
        (np.cos(angles) * factor).astype(jnp.bfloat16),
        (np.sin(angles) * factor).astype(jnp.bfloat16),
    )


def half_y_table():
    cosine, sine = host_tables(GY)
    imag = -sine[:, :HALF]
    imag[:, 0] = cosine[:, HALF]
    return np.concatenate([cosine[:, :HALF], imag], axis=1)


def paired_y_table():
    table = np.zeros((2 * GY, GY), jnp.bfloat16)
    table[::2] = half_y_table() * np.array(0.5, jnp.bfloat16)
    table[:, [0, HALF]] *= np.array(0.5, jnp.bfloat16)
    return table


def half_y_inverse():
    cosine, sine = host_tables(GY)
    two = np.array(2.0, jnp.bfloat16)
    real = cosine[:HALF, :] * two
    real[0] = cosine[0]
    imag = -sine[:HALF, :] * two
    imag[0] = cosine[HALF]
    return np.concatenate([real, imag], axis=0)


def mirror_order():
    order = [0, GX // 2]
    for j in range(1, GX // 2):
        order += [j, GX - j]
    return order


def complex_blocks(length, sign):
    cosine, sine = (table.astype(np.float32) for table in host_tables(length))
    return np.array([[cosine, -sign * sine], [sign * sine, cosine]])


def forward_x_table():
    table = np.einsum("oijx,az->joaizx", complex_blocks(GX, -1), np.eye(PLANES))[mirror_order()]
    table = table.reshape(2 * GX * PLANES, 2, PLANES, GX)
    woven = table[:, :, :2].transpose(0, 1, 3, 2).reshape(-1, 2, 2 * GX)
    plain = table[:, :, 2:].reshape(-1, 2, (PLANES - 2) * GX)
    table = np.concatenate([woven, plain], axis=2)
    return table.reshape(2 * GX * PLANES, -1).astype(jnp.bfloat16)


def inverse_x_table():
    table = np.einsum("oijx,az->oaxjiz", complex_blocks(GX, 1), np.eye(PLANES))
    return table.reshape(2 * PLANES * GX, -1).astype(jnp.bfloat16)


def z_rows():
    return np.arange(2 * GZ).reshape(2, GZ // PLANES, PLANES).transpose(1, 0, 2).reshape(-1)


def z_tables():
    forward, inverse = (
        complex_blocks(GZ, sign).transpose(0, 2, 1, 3).reshape(2 * GZ, 2 * GZ) for sign in (-1, 1)
    )
    none = np.zeros((2 * GZ, GZ), np.float32)
    forward_last = np.concatenate([none, forward[:, :GZ]], axis=1)
    inverse_last = np.concatenate([none.T, inverse[:GZ]], axis=0)
    order = z_rows()
    return [
        np.ascontiguousarray(table).astype(jnp.bfloat16)
        for table in (
            forward[:, order],
            inverse[order],
            forward_last[:, order],
            inverse_last[order],
        )
    ]


def imaginary_rows(shape):
    return lax.broadcasted_iota(jnp.int32, shape, 0) % (2 * PLANES) >= PLANES


def first_lane(shape):
    return lax.broadcasted_iota(jnp.int32, shape, 1) == 0


def dot(left, right):
    return jnp.dot(left, right, preferred_element_type=jnp.float32)


def analyse_kernel(
    slots, pairs_ref, extents_ref, tile_ref, *rest
):
    band_refs, (wy_ref, wx_ref, out_ref, crop_ref) = rest[:-4], rest[-4:]
    slot = pl.program_id(0)

    @pl.when(slot == 0)
    def _():
        for p in range(pairs_ref.shape[1]):
            for end in (0, 1):
                named = pairs_ref[2 * end, p] * FACES + pairs_ref[2 * end + 1, p] - tile_ref[0] * slots

                @pl.when((named >= 0) & (named < slots))
                def _():
                    crop_ref[named, 0] = extents_ref[0, p]
                    crop_ref[named, 1] = extents_ref[1, p]

    across, along = crop_ref[slot, 0], crop_ref[slot, 1]

    def live(k, rows):
        lane = lax.broadcasted_iota(jnp.int32, rows.shape, 1)
        return jnp.where((rows < across) & (k * 128 + lane < along), 1.0, 0.0).astype(jnp.bfloat16)

    def halves(rows):
        return (rows + pltpu.roll(rows, 127, 1)).astype(jnp.bfloat16)

    raw_row = lax.broadcasted_iota(jnp.int32, (2 * GX, 128), 0)
    pooled_row = lax.broadcasted_iota(jnp.int32, (GX, 128), 0)
    even = raw_row % 2 == 0
    groups = (2 * GX // 8, 8, 128)
    lives = [
        (live(k, raw_row), live(k, 2 * pooled_row), live(k, 2 * pooled_row + 1))
        for k in range(len(band_refs))
    ]
    block = (2 * PLANES, HALF)
    lane0, imaginary = first_lane(block), imaginary_rows(block)
    sign = jnp.where(imaginary, -1.0, 1.0)
    twice = jnp.where(lane0, 2.0, 1.0)

    def row_pairs(ref, z, mask, shift):
        raw = (ref[0, 0, z] * mask).astype(jnp.float32)
        return raw + pltpu.roll(raw.reshape(groups), shift, 1).reshape(raw.shape)

    def woven(z):
        return [
            halves(jnp.where(even, row_pairs(ref, z, mask, 7), row_pairs(ref, z + 1, mask, 1)))
            for ref, (mask, _, _) in zip(band_refs, lives)
        ]

    def plain(z):
        parts = []
        for ref, (_, *masks) in zip(band_refs, lives):
            rows = [
                (ref[0, 0, z, pl.ds(a, GX, stride=2), :] * masks[a]).astype(jnp.float32) for a in (0, 1)
            ]
            parts.append(halves(rows[0] + rows[1]))
        return parts

    def pool(z):
        return [
            jnp.concatenate(parts, axis=1)
            for parts in (woven(z), *(plain(z + k) for k in range(2, PLANES)))
        ]

    zpart = 4 * PLANES
    zrows = band_refs[0].shape[2]
    planes = sum((pool(z) for z in range(0, zrows, PLANES)), [])
    y = dot(jnp.concatenate(planes, axis=0), wy_ref[...]).astype(jnp.bfloat16)
    y = y.reshape(zrows // PLANES, PLANES * GX, GY)

    def store(start, spectra):
        def at(n):
            rows = spectra[2 * PLANES * n : 2 * PLANES * (n + 1)]
            return [rows[:, k : k + HALF] for k in range(0, rows.shape[1], HALF)]

        def put(j, blocks):
            rows = slice(2 * start, 2 * (start + zpart))
            out_ref[j, 0, rows] = jnp.concatenate(blocks, axis=0).astype(jnp.bfloat16)

        put(0, [a * twice for a in at(0)])
        put(GX // 2, [a * twice for a in at(1)])
        for j in range(1, GX // 2):
            here, mirror = at(2 * j), at(2 * j + 1)
            put(j, [jnp.where(lane0, a + sign * b, a) for a, b in zip(here, mirror)])
            put(
                GX - j,
                [
                    jnp.where(lane0, pltpu.roll(a - sign * b, PLANES, 0), b)
                    for a, b in zip(here, mirror)
                ],
            )

    for start in range(0, zrows, zpart):
        units = [
            jnp.concatenate([y[unit, :, :HALF], y[unit, :, HALF:]], axis=0)
            for unit in range(start // PLANES, (start + zpart) // PLANES)
        ]
        store(start, dot(wx_ref[...], jnp.concatenate(units, axis=1)))


def analyse(band, pairs, extents, tile):
    slots, zrows = band.shape[0] * FACES, band.shape[2]
    tables = (paired_y_table(), forward_x_table())
    whole = [pl.BlockSpec(t.shape, lambda i, *_: (0, 0)) for t in tables]
    lane_blocks = 2 * GY // 128
    return pl.pallas_call(
        functools.partial(analyse_kernel, slots),
        grid_spec=pltpu.PrefetchScalarGridSpec(
            num_scalar_prefetch=3,
            grid=(slots,),
            in_specs=[
                pl.BlockSpec(
                    (1, 1, zrows, 2 * GX, 128),
                    lambda i, *_, k=k: (i // FACES, i % FACES, 0, 0, k),
                )
                for k in range(lane_blocks)
            ]
            + whole,
            out_specs=pl.BlockSpec((GX, 1, 2 * zrows, HALF), lambda i, *_: (0, i, 0, 0)),
            scratch_shapes=[pltpu.SMEM((slots, 2), jnp.int32)],
        ),
        out_shape=jax.ShapeDtypeStruct((GX, slots, 2 * zrows, HALF), jnp.bfloat16),
        compiler_params=pltpu.CompilerParams(vmem_limit_bytes=VMEM_BYTES + VMEM_BYTES * 3 // 4),
        name="analyse",
    )(pairs, extents, tile, *[band] * lane_blocks, *(jnp.asarray(t) for t in tables))


def normalised(a_re, a_im, b_re, b_im):
    cross_re = a_re * b_re + a_im * b_im
    cross_im = a_im * b_re - a_re * b_im
    scale = lax.rsqrt(cross_re * cross_re + cross_im * cross_im + 1.0)
    return (cross_re * scale).astype(jnp.bfloat16), (cross_im * scale).astype(jnp.bfloat16)


def correlate_kernel(
    sizes, tiles_here, pairs_ref, place_ref, in_ref, wz_ref, wzi_ref, wz_last_ref, wzi_last_ref, out_ref
):
    x, y, cores = sizes
    slabs = y * cores

    def place_of(owner, s):
        return owner // x * (cores * x * y) + s % cores * (x * y) + owner % x * y + s // cores

    total = pairs_ref.shape[1]
    pairs_here = out_ref.shape[1]
    slab_rows = out_ref.shape[2]
    both_real = (place_ref[0] == 0) | (place_ref[0] == GX // 2)
    block = (2 * GZ, HALF)
    shared = first_lane(block) & imaginary_rows(block)

    def load(p, end):
        tile = pairs_ref[2 * end, p]
        row = tile // tiles_here
        pos = tile % tiles_here * FACES + pairs_ref[2 * end + 1, p]
        return jnp.concatenate([in_ref[place_of(row, s), pos] for s in range(slabs)], axis=0)

    def phase_of(table_ref, ends):
        spec = dot(table_ref[...], jnp.concatenate(ends, axis=1))
        spec = spec.astype(jnp.bfloat16).astype(jnp.float32)
        parts = [spec[:GZ], spec[GZ:]]
        phases = []
        for k in range(0, spec.shape[1], 2 * HALF):
            a, b = slice(k, k + HALF), slice(k + HALF, k + 2 * HALF)
            phase = normalised(parts[0][:, a], parts[1][:, a], parts[0][:, b], parts[1][:, b])
            phases.append(jnp.concatenate(phase, axis=0))
        return jnp.concatenate(phases, axis=1)

    def join(special):
        if special:
            keep = jnp.where(shared, 0.0, 1.0).astype(jnp.bfloat16)
            lane = lax.broadcasted_iota(jnp.int32, block, 1)
            lasts = [jnp.zeros(block, jnp.bfloat16)] * 2
            for p in range(total):
                for end in (0, 1):
                    lasts[end] = jnp.where(lane == p, load(p, end)[:, 0:1], lasts[end])
            last = dot(wzi_last_ref[...], phase_of(wz_last_ref, lasts)).astype(jnp.bfloat16)
        group = 16 if total % 16 == 0 else 8
        for p in range(0, total, group):
            ends = [load(q, end) for q in range(p, p + group) for end in (0, 1)]
            if special:
                ends = [end * keep for end in ends]
            w = dot(wzi_ref[...], phase_of(wz_ref, ends)).astype(jnp.bfloat16)
            for k, q in enumerate(range(p, p + group)):
                whole = w[:, k * HALF : (k + 1) * HALF]
                if special:
                    whole = jnp.where(shared, last[:, q : q + 1], whole)
                for s in range(slabs):
                    out_ref[place_of(q // pairs_here, s), q % pairs_here] = whole[
                        s * slab_rows : (s + 1) * slab_rows
                    ]

    @pl.when(both_real)
    def _():
        join(True)

    @pl.when(jnp.logical_not(both_real))
    def _():
        join(False)


def correlate(spread, pairs, place, sizes, tiles_here):
    devices, _, slab_rows, _ = spread.shape
    pairs_here = pairs.shape[1] * sizes[1] * sizes[2] // devices
    tables = z_tables()
    vmem = pl.BlockSpec(memory_space=pltpu.VMEM)
    smem = pl.BlockSpec(memory_space=pltpu.SMEM)
    return pl.pallas_call(
        functools.partial(correlate_kernel, sizes, tiles_here),
        in_specs=[smem, smem] + [vmem] * (1 + len(tables)),
        out_specs=vmem,
        out_shape=jax.ShapeDtypeStruct((devices, pairs_here, slab_rows, HALF), jnp.bfloat16),
        compiler_params=pltpu.CompilerParams(vmem_limit_bytes=VMEM_BYTES),
        name="correlate",
    )(pairs, place, spread, *(jnp.asarray(t) for t in tables))


def synthesise_kernel(in_ref, wx_ref, wy_ref, out_ref, maps_ref, sems):
    pairs_here, slab_rows = in_ref.shape[1:3]
    zrows = slab_rows // 2
    units = zrows // PLANES
    block = (slab_rows, HALF)
    lane0, imaginary = first_lane(block), imaginary_rows(block)
    sign = jnp.where(imaginary, -1.0, 1.0)
    groups = (units, 2 * PLANES, HALF)
    zpart = zrows // sems.shape[1]
    rows = PLANES * GX

    def leave(p, part):
        zs = pl.ds(part * zpart, zpart)
        return pltpu.make_async_copy(maps_ref.at[p, zs], out_ref.at[p, zs], sems.at[p, part])

    for p in range(pairs_here):
        blocks = [None] * GX
        for j in (0, GX // 2):
            blocks[j] = in_ref[j, p].astype(jnp.float32)
        for j in range(1, GX // 2):
            here, mirror = in_ref[j, p].astype(jnp.float32), in_ref[GX - j, p].astype(jnp.float32)
            swapped = pltpu.roll(mirror.reshape(groups), PLANES, 1).reshape(block)
            blocks[j] = jnp.where(lane0, here + swapped, here)
            blocks[GX - j] = jnp.where(lane0, sign * (here - swapped), mirror)
        stacked = jnp.concatenate(
            [
                jnp.concatenate([b[u * 2 * PLANES : (u + 1) * 2 * PLANES] for b in blocks], axis=0)
                for u in range(units)
            ],
            axis=1,
        ).astype(jnp.bfloat16)
        v = dot(wx_ref[...], stacked).astype(jnp.bfloat16)
        cells = [
            jnp.concatenate([v[:rows, k : k + HALF], v[rows:, k : k + HALF]], axis=1)
            for k in range(0, units * HALF, HALF)
        ]
        for part in range(sems.shape[1]):
            of = cells[part * zpart // PLANES : (part + 1) * zpart // PLANES]
            maps = dot(jnp.concatenate(of, axis=0), wy_ref[...])
            maps_ref[p, part * zpart : (part + 1) * zpart] = maps.reshape(zpart, GX, GY)
            leave(p, part).start()
    for p in range(pairs_here):
        for part in range(sems.shape[1]):
            leave(p, part).wait()


def synthesise(returned):
    _, pairs_here, slab_rows, _ = returned.shape
    tables = (inverse_x_table(), half_y_inverse())
    shape = (pairs_here, slab_rows // 2, GX, GY)
    vmem = pl.BlockSpec(memory_space=pltpu.VMEM)
    return pl.pallas_call(
        synthesise_kernel,
        in_specs=[vmem] * (1 + len(tables)),
        out_specs=pl.BlockSpec(memory_space=pl.ANY),
        out_shape=jax.ShapeDtypeStruct(shape, jnp.float32),
        scratch_shapes=[
            pltpu.VMEM(shape, jnp.float32),
            pltpu.SemaphoreType.DMA((pairs_here, slab_rows // (8 * PLANES))),
        ],
        compiler_params=pltpu.CompilerParams(vmem_limit_bytes=VMEM_BYTES),
        name="synthesise",
    )(returned, *(jnp.asarray(t) for t in tables))


ORDER = ("z", "core", "x", "y")


def placed_shards(band, pairs, extents):
    x, y, cores = (lax.axis_size(axis) for axis in ("x", "y", "core"))
    pairs, extents = pairs.T, extents.T
    tile = (lax.axis_index("z") * x + lax.axis_index("x")).astype(jnp.int32)
    device = lax.axis_index(ORDER).astype(jnp.int32)
    spectra = analyse(band, pairs, extents, tile[None])
    spread = lax.all_to_all(spectra, ORDER, split_axis=0, concat_axis=0, tiled=True)
    w = correlate(spread, pairs, device[None], (x, y, cores), band.shape[0])
    returned = lax.all_to_all(w, ORDER, split_axis=0, concat_axis=0, tiled=True)
    return synthesise(returned)


def solution(mesh):
    tiles, slabs = mesh.devices.shape
    cores = 2
    side = max(slabs // cores, 1)
    if tiles * slabs == GX and slabs % cores == 0 and tiles % side == 0:
        over = jax.sharding.Mesh(
            mesh.devices.reshape(tiles // side, side, slabs // cores, cores), ("z", "x", "y", "core")
        )
        tile, slab, body = ("z", "x"), ("y", "core"), placed_shards
    else:
        over, tile, slab, body = mesh, "tile", "zslab", general_shards
    return jax.shard_map(
        body,
        mesh=over,
        in_specs=(P(tile, None, slab, None, None), P(), P()),
        out_specs=P(tile, slab, None, None),
        check_vma=False,
    )
```

```python
import functools
import math


import jax
import jax.numpy as jnp
import numpy as np
from jax import lax
from jax.experimental import pallas as pl
from jax.experimental.pallas import tpu as pltpu
from jax.sharding import PartitionSpec as P

GX = 32
GY = 256
GZ = 128
FACES = 4


def dft_tables(length):
    indices = jnp.arange(length, dtype=jnp.int32)
    modular = indices[:, None] * indices[None, :] % length
    angles = modular.astype(jnp.float32) * (2.0 * math.pi / length)
    factor = 1.0 / math.sqrt(length)
    return (
        (jnp.cos(angles) * factor).astype(jnp.bfloat16),
        (jnp.sin(angles) * factor).astype(jnp.bfloat16),
    )


def product(form, left, right):
    return jnp.einsum(form, left, right, preferred_element_type=jnp.float32)


def reduce_resolution(image_volume, crop_bounds):
    row_mask = (
        jnp.arange(image_volume.shape[2], dtype=jnp.int32)[None, :] < crop_bounds[:, 0:1]
    ).astype(jnp.bfloat16)
    col_mask = (
        jnp.arange(image_volume.shape[3], dtype=jnp.int32)[None, :] < crop_bounds[:, 1:2]
    ).astype(jnp.bfloat16)
    masked = image_volume * row_mask[:, None, :, None] * col_mask[:, None, None, :]
    raw_cols = jnp.arange(image_volume.shape[3], dtype=jnp.int32)
    pooled_cols = jnp.arange(GY, dtype=jnp.int32)
    pooling = jnp.where(raw_cols[:, None] // 2 == pooled_cols[None, :], 0.5, 0.0).astype(
        jnp.bfloat16
    )
    along_pooled = product("szxy,yk->szxk", masked, pooling)
    shaped = along_pooled.reshape(image_volume.shape[0], image_volume.shape[1], GX, 2, GY)
    return (shaped[:, :, :, 0, :] + shaped[:, :, :, 1, :]).astype(jnp.bfloat16)


def cross_phase(owner_re, owner_im, pairs, tiles_here):
    first_dev = pairs[:, 0] // tiles_here
    first_pos = pairs[:, 0] % tiles_here * FACES + pairs[:, 1]
    second_tile_device = pairs[:, 2] // tiles_here
    second_pos = pairs[:, 2] % tiles_here * FACES + pairs[:, 3]
    first_re = owner_re[first_dev, :, first_pos].astype(jnp.float32)
    first_im = owner_im[first_dev, :, first_pos].astype(jnp.float32)
    second_re = owner_re[second_tile_device, :, second_pos].astype(jnp.float32)
    second_im = owner_im[second_tile_device, :, second_pos].astype(jnp.float32)
    cross_re = first_re * second_re + first_im * second_im
    cross_im = first_im * second_re - first_re * second_im
    scaled = jnp.sqrt(cross_re * cross_re + cross_im * cross_im + 1.0)
    return ((cross_re / scaled).astype(jnp.bfloat16), (cross_im / scaled).astype(jnp.bfloat16))


def inverse_z(phase_real_part, phase_im, tables_z):
    w_re = (
        product("pmjk,mz->pzjk", phase_real_part, tables_z[0])
        - product("pmjk,mz->pzjk", phase_im, tables_z[1])
    ).astype(jnp.bfloat16)
    w_im = (
        product("pmjk,mz->pzjk", phase_im, tables_z[0])
        + product("pmjk,mz->pzjk", phase_real_part, tables_z[1])
    ).astype(jnp.bfloat16)
    return (w_re, w_im)


def inverse_x(w_re, w_im, tables_x):
    v_re = (
        product("pzjk,jx->pzxk", w_re, tables_x[0]) - product("pzjk,jx->pzxk", w_im, tables_x[1])
    ).astype(jnp.bfloat16)
    v_im = (
        product("pzjk,jx->pzxk", w_im, tables_x[0]) + product("pzjk,jx->pzxk", w_re, tables_x[1])
    ).astype(jnp.bfloat16)
    return (v_re, v_im)


def general_shards(band, pairs, extents):
    tables_x = dft_tables(GX)
    tables_y = dft_tables(GY)
    tables_z = dft_tables(GZ)
    tiles_here = band.shape[0]
    slots = tiles_here * FACES
    zrows = band.shape[2]
    tile_pos = lax.axis_index("tile")
    global_slot = tile_pos * slots + jnp.arange(slots, dtype=jnp.int32)
    first_slot = pairs[:, 0] * FACES + pairs[:, 1]
    second_slot = pairs[:, 2] * FACES + pairs[:, 3]
    matches = (
        (first_slot[None, :] == global_slot[:, None])
        | (second_slot[None, :] == global_slot[:, None])
    ).astype(jnp.int32)
    crop_bounds = jnp.sum(matches[:, :, None] * extents[None, :, :], axis=1)
    image_volume = band.reshape(slots, zrows, 2 * GX, 2 * GY)
    reduced_volume = reduce_resolution(image_volume, crop_bounds)
    y_re = product("szxy,yk->szxk", reduced_volume, tables_y[0]).astype(jnp.bfloat16)
    y_im = (-product("szxy,yk->szxk", reduced_volume, tables_y[1])).astype(jnp.bfloat16)
    x_re = (
        product("szxk,xj->szjk", y_re, tables_x[0]) + product("szxk,xj->szjk", y_im, tables_x[1])
    ).astype(jnp.bfloat16)
    x_im = (
        product("szxk,xj->szjk", y_im, tables_x[0]) - product("szxk,xj->szjk", y_re, tables_x[1])
    ).astype(jnp.bfloat16)
    kx_part = GX // lax.axis_size("zslab")
    re_in = lax.all_to_all(x_re, "zslab", split_axis=2, concat_axis=1, tiled=True)
    im_in = lax.all_to_all(x_im, "zslab", split_axis=2, concat_axis=1, tiled=True)
    out_re = (
        product("szjk,zm->msjk", re_in, tables_z[0]) + product("szjk,zm->msjk", im_in, tables_z[1])
    ).astype(jnp.bfloat16)
    out_im = (
        product("szjk,zm->msjk", im_in, tables_z[0]) - product("szjk,zm->msjk", re_in, tables_z[1])
    ).astype(jnp.bfloat16)
    tile_count = lax.axis_size("tile")
    kz_part = GZ // tile_count
    spectra = (
        lax.all_to_all(out_re, "tile", split_axis=0, concat_axis=0, tiled=True),
        lax.all_to_all(out_im, "tile", split_axis=0, concat_axis=0, tiled=True),
    )
    owner_re = spectra[0].reshape(tile_count, kz_part, slots, kx_part, GY)
    owner_im = spectra[1].reshape(tile_count, kz_part, slots, kx_part, GY)
    phase_real_part, phase_im = cross_phase(owner_re, owner_im, pairs, tiles_here)
    returned = (
        lax.all_to_all(phase_real_part, "tile", split_axis=0, concat_axis=1, tiled=True),
        lax.all_to_all(phase_im, "tile", split_axis=0, concat_axis=1, tiled=True),
    )
    w_re, w_im = inverse_z(returned[0], returned[1], tables_z)
    v_re, v_im = inverse_x(
        lax.all_to_all(w_re, "zslab", split_axis=1, concat_axis=2, tiled=True),
        lax.all_to_all(w_im, "zslab", split_axis=1, concat_axis=2, tiled=True),
        tables_x,
    )
    return product("pzxk,ky->pzxy", v_re, tables_y[0]) - product("pzxk,ky->pzxy", v_im, tables_y[1])


HALF = GY // 2
PLANES = 4
VMEM_BYTES = 32 * 1024 * 1024


def host_tables(length):
    indices = np.arange(length, dtype=np.int32)
    modular = indices[:, None] * indices[None, :] % length
    angles = modular.astype(np.float32) * np.float32(2.0 * math.pi / length)
    factor = np.float32(1.0 / math.sqrt(length))
    return (
        (np.cos(angles) * factor).astype(jnp.bfloat16),
        (np.sin(angles) * factor).astype(jnp.bfloat16),
    )


def half_y_table():
    cosine, sine = host_tables(GY)
    imag = -sine[:, :HALF]
    imag[:, 0] = cosine[:, HALF]
    return np.concatenate([cosine[:, :HALF], imag], axis=1)


def paired_y_table():
    table = np.zeros((2 * GY, GY), jnp.bfloat16)
    table[::2] = half_y_table() * np.array(0.5, jnp.bfloat16)
    table[:, [0, HALF]] *= np.array(0.5, jnp.bfloat16)
    return table


def half_y_inverse():
    cosine, sine = host_tables(GY)
    two = np.array(2.0, jnp.bfloat16)
    real = cosine[:HALF, :] * two
    real[0] = cosine[0]
    imag = -sine[:HALF, :] * two
    imag[0] = cosine[HALF]
    return np.concatenate([real, imag], axis=0)


def mirror_order():
    order = [0, GX // 2]
    for j in range(1, GX // 2):
        order += [j, GX - j]
    return order


def complex_blocks(length, sign):
    cosine, sine = (table.astype(np.float32) for table in host_tables(length))
    return np.array([[cosine, -sign * sine], [sign * sine, cosine]])


def forward_x_table():
    table = np.einsum("oijx,az->joaizx", complex_blocks(GX, -1), np.eye(PLANES))[mirror_order()]
    table = table.reshape(2 * GX * PLANES, 2, PLANES, GX)
    woven = table[:, :, :2].transpose(0, 1, 3, 2).reshape(-1, 2, 2 * GX)
    plain = table[:, :, 2:].reshape(-1, 2, (PLANES - 2) * GX)
    table = np.concatenate([woven, plain], axis=2)
    return table.reshape(2 * GX * PLANES, -1).astype(jnp.bfloat16)


def inverse_x_table():
    table = np.einsum("oijx,az->oaxjiz", complex_blocks(GX, 1), np.eye(PLANES))
    return table.reshape(2 * PLANES * GX, -1).astype(jnp.bfloat16)


def z_rows():
    return np.arange(2 * GZ).reshape(2, GZ // PLANES, PLANES).transpose(1, 0, 2).reshape(-1)


def z_tables():
    forward, inverse = (
        complex_blocks(GZ, sign).transpose(0, 2, 1, 3).reshape(2 * GZ, 2 * GZ) for sign in (-1, 1)
    )
    none = np.zeros((2 * GZ, GZ), np.float32)
    forward_last = np.concatenate([none, forward[:, :GZ]], axis=1)
    inverse_last = np.concatenate([none.T, inverse[:GZ]], axis=0)
    order = z_rows()
    return [
        np.ascontiguousarray(table).astype(jnp.bfloat16)
        for table in (
            forward[:, order],
            inverse[order],
            forward_last[:, order],
            inverse_last[order],
        )
    ]


def imaginary_rows(shape):
    return lax.broadcasted_iota(jnp.int32, shape, 0) % (2 * PLANES) >= PLANES


def first_lane(shape):
    return lax.broadcasted_iota(jnp.int32, shape, 1) == 0


def dot(left, right):
    return jnp.dot(left, right, preferred_element_type=jnp.float32)


def analyse_kernel(
    slots, pairs_ref, extents_ref, tile_ref, *rest
):
    band_refs, (wy_ref, wx_ref, out_ref, crop_ref) = rest[:-4], rest[-4:]
    slot = pl.program_id(0)

    @pl.when(slot == 0)
    def _():
        for p in range(pairs_ref.shape[1]):
            for end in (0, 1):
                named = pairs_ref[2 * end, p] * FACES + pairs_ref[2 * end + 1, p] - tile_ref[0] * slots

                @pl.when((named >= 0) & (named < slots))
                def _():
                    crop_ref[named, 0] = extents_ref[0, p]
                    crop_ref[named, 1] = extents_ref[1, p]

    across, along = crop_ref[slot, 0], crop_ref[slot, 1]

    def live(k, rows):
        lane = lax.broadcasted_iota(jnp.int32, rows.shape, 1)
        return jnp.where((rows < across) & (k * 128 + lane < along), 1.0, 0.0).astype(jnp.bfloat16)

    def halves(rows):
        return (rows + pltpu.roll(rows, 127, 1)).astype(jnp.bfloat16)

    raw_row = lax.broadcasted_iota(jnp.int32, (2 * GX, 128), 0)
    pooled_row = lax.broadcasted_iota(jnp.int32, (GX, 128), 0)
    even = raw_row % 2 == 0
    groups = (2 * GX // 8, 8, 128)
    lives = [
        (live(k, raw_row), live(k, 2 * pooled_row), live(k, 2 * pooled_row + 1))
        for k in range(len(band_refs))
    ]
    block = (2 * PLANES, HALF)
    lane0, imaginary = first_lane(block), imaginary_rows(block)
    sign = jnp.where(imaginary, -1.0, 1.0)
    twice = jnp.where(lane0, 2.0, 1.0)

    def row_pairs(ref, z, mask, shift):
        raw = (ref[0, 0, z] * mask).astype(jnp.float32)
        return raw + pltpu.roll(raw.reshape(groups), shift, 1).reshape(raw.shape)

    def woven(z):
        return [
            halves(jnp.where(even, row_pairs(ref, z, mask, 7), row_pairs(ref, z + 1, mask, 1)))
            for ref, (mask, _, _) in zip(band_refs, lives)
        ]

    def plain(z):
        parts = []
        for ref, (_, *masks) in zip(band_refs, lives):
            rows = [
                (ref[0, 0, z, pl.ds(a, GX, stride=2), :] * masks[a]).astype(jnp.float32) for a in (0, 1)
            ]
            parts.append(halves(rows[0] + rows[1]))
        return parts

    def pool(z):
        return [
            jnp.concatenate(parts, axis=1)
            for parts in (woven(z), *(plain(z + k) for k in range(2, PLANES)))
        ]

    zpart = 4 * PLANES
    zrows = band_refs[0].shape[2]
    planes = sum((pool(z) for z in range(0, zrows, PLANES)), [])
    y = dot(jnp.concatenate(planes, axis=0), wy_ref[...]).astype(jnp.bfloat16)
    y = y.reshape(zrows // PLANES, PLANES * GX, GY)

    def store(start, spectra):
        def at(n):
            rows = spectra[2 * PLANES * n : 2 * PLANES * (n + 1)]
            return [rows[:, k : k + HALF] for k in range(0, rows.shape[1], HALF)]

        def put(j, blocks):
            rows = slice(2 * start, 2 * (start + zpart))
            out_ref[j, 0, rows] = jnp.concatenate(blocks, axis=0).astype(jnp.bfloat16)

        put(0, [a * twice for a in at(0)])
        put(GX // 2, [a * twice for a in at(1)])
        for j in range(1, GX // 2):
            here, mirror = at(2 * j), at(2 * j + 1)
            put(j, [jnp.where(lane0, a + sign * b, a) for a, b in zip(here, mirror)])
            put(
                GX - j,
                [
                    jnp.where(lane0, pltpu.roll(a - sign * b, PLANES, 0), b)
                    for a, b in zip(here, mirror)
                ],
            )

    for start in range(0, zrows, zpart):
        units = [
            jnp.concatenate([y[unit, :, :HALF], y[unit, :, HALF:]], axis=0)
            for unit in range(start // PLANES, (start + zpart) // PLANES)
        ]
        store(start, dot(wx_ref[...], jnp.concatenate(units, axis=1)))


def analyse(band, pairs, extents, tile):
    slots, zrows = band.shape[0] * FACES, band.shape[2]
    tables = (paired_y_table(), forward_x_table())
    whole = [pl.BlockSpec(t.shape, lambda i, *_: (0, 0)) for t in tables]
    lane_blocks = 2 * GY // 128
    return pl.pallas_call(
        functools.partial(analyse_kernel, slots),
        grid_spec=pltpu.PrefetchScalarGridSpec(
            num_scalar_prefetch=3,
            grid=(slots,),
            in_specs=[
                pl.BlockSpec(
                    (1, 1, zrows, 2 * GX, 128),
                    lambda i, *_, k=k: (i // FACES, i % FACES, 0, 0, k),
                )
                for k in range(lane_blocks)
            ]
            + whole,
            out_specs=pl.BlockSpec((GX, 1, 2 * zrows, HALF), lambda i, *_: (0, i, 0, 0)),
            scratch_shapes=[pltpu.SMEM((slots, 2), jnp.int32)],
        ),
        out_shape=jax.ShapeDtypeStruct((GX, slots, 2 * zrows, HALF), jnp.bfloat16),
        compiler_params=pltpu.CompilerParams(vmem_limit_bytes=VMEM_BYTES + VMEM_BYTES * 3 // 4),
        name="analyse",
    )(pairs, extents, tile, *[band] * lane_blocks, *(jnp.asarray(t) for t in tables))


def normalised(a_re, a_im, b_re, b_im):
    cross_re = a_re * b_re + a_im * b_im
    cross_im = a_im * b_re - a_re * b_im
    scale = lax.rsqrt(cross_re * cross_re + cross_im * cross_im + 1.0)
    return (cross_re * scale).astype(jnp.bfloat16), (cross_im * scale).astype(jnp.bfloat16)


def correlate_kernel(
    sizes, tiles_here, pairs_ref, place_ref, in_ref, wz_ref, wzi_ref, wz_last_ref, wzi_last_ref, out_ref
):
    x, y, cores = sizes
    slabs = y * cores

    def place_of(owner, s):
        return owner // x * (cores * x * y) + s % cores * (x * y) + owner % x * y + s // cores

    total = pairs_ref.shape[1]
    pairs_here = out_ref.shape[1]
    slab_rows = out_ref.shape[2]
    both_real = (place_ref[0] == 0) | (place_ref[0] == GX // 2)
    block = (2 * GZ, HALF)
    shared = first_lane(block) & imaginary_rows(block)

    def load(p, end):
        tile = pairs_ref[2 * end, p]
        row = tile // tiles_here
        pos = tile % tiles_here * FACES + pairs_ref[2 * end + 1, p]
        return jnp.concatenate([in_ref[place_of(row, s), pos] for s in range(slabs)], axis=0)

    def phase_of(table_ref, ends):
        spec = dot(table_ref[...], jnp.concatenate(ends, axis=1))
        spec = spec.astype(jnp.bfloat16).astype(jnp.float32)
        parts = [spec[:GZ], spec[GZ:]]
        phases = []
        for k in range(0, spec.shape[1], 2 * HALF):
            a, b = slice(k, k + HALF), slice(k + HALF, k + 2 * HALF)
            phase = normalised(parts[0][:, a], parts[1][:, a], parts[0][:, b], parts[1][:, b])
            phases.append(jnp.concatenate(phase, axis=0))
        return jnp.concatenate(phases, axis=1)

    def join(special):
        if special:
            keep = jnp.where(shared, 0.0, 1.0).astype(jnp.bfloat16)
            lane = lax.broadcasted_iota(jnp.int32, block, 1)
            lasts = [jnp.zeros(block, jnp.bfloat16)] * 2
            for p in range(total):
                for end in (0, 1):
                    lasts[end] = jnp.where(lane == p, load(p, end)[:, 0:1], lasts[end])
            last = dot(wzi_last_ref[...], phase_of(wz_last_ref, lasts)).astype(jnp.bfloat16)
        group = 16 if total % 16 == 0 else 8
        for p in range(0, total, group):
            ends = [load(q, end) for q in range(p, p + group) for end in (0, 1)]
            if special:
                ends = [end * keep for end in ends]
            w = dot(wzi_ref[...], phase_of(wz_ref, ends)).astype(jnp.bfloat16)
            for k, q in enumerate(range(p, p + group)):
                whole = w[:, k * HALF : (k + 1) * HALF]
                if special:
                    whole = jnp.where(shared, last[:, q : q + 1], whole)
                for s in range(slabs):
                    out_ref[place_of(q // pairs_here, s), q % pairs_here] = whole[
                        s * slab_rows : (s + 1) * slab_rows
                    ]

    @pl.when(both_real)
    def _():
        join(True)

    @pl.when(jnp.logical_not(both_real))
    def _():
        join(False)


def correlate(spread, pairs, place, sizes, tiles_here):
    devices, _, slab_rows, _ = spread.shape
    pairs_here = pairs.shape[1] * sizes[1] * sizes[2] // devices
    tables = z_tables()
    vmem = pl.BlockSpec(memory_space=pltpu.VMEM)
    smem = pl.BlockSpec(memory_space=pltpu.SMEM)
    return pl.pallas_call(
        functools.partial(correlate_kernel, sizes, tiles_here),
        in_specs=[smem, smem] + [vmem] * (1 + len(tables)),
        out_specs=vmem,
        out_shape=jax.ShapeDtypeStruct((devices, pairs_here, slab_rows, HALF), jnp.bfloat16),
        compiler_params=pltpu.CompilerParams(vmem_limit_bytes=VMEM_BYTES),
        name="correlate",
    )(pairs, place, spread, *(jnp.asarray(t) for t in tables))


def synthesise_kernel(in_ref, wx_ref, wy_ref, out_ref, maps_ref, sems):
    pairs_here, slab_rows = in_ref.shape[1:3]
    zrows = slab_rows // 2
    units = zrows // PLANES
    block = (slab_rows, HALF)
    lane0, imaginary = first_lane(block), imaginary_rows(block)
    sign = jnp.where(imaginary, -1.0, 1.0)
    groups = (units, 2 * PLANES, HALF)
    zpart = zrows // sems.shape[1]
    rows = PLANES * GX

    def leave(p, part):
        zs = pl.ds(part * zpart, zpart)
        return pltpu.make_async_copy(maps_ref.at[p, zs], out_ref.at[p, zs], sems.at[p, part])

    stacks = []
    for p in range(pairs_here):
        blocks = [None] * GX
        for j in (0, GX // 2):
            blocks[j] = in_ref[j, p].astype(jnp.float32)
        for j in range(1, GX // 2):
            here, mirror = in_ref[j, p].astype(jnp.float32), in_ref[GX - j, p].astype(jnp.float32)
            swapped = pltpu.roll(mirror.reshape(groups), PLANES, 1).reshape(block)
            blocks[j] = jnp.where(lane0, here + swapped, here)
            blocks[GX - j] = jnp.where(lane0, sign * (here - swapped), mirror)
        stacked = jnp.concatenate(
            [
                jnp.concatenate([b[u * 2 * PLANES : (u + 1) * 2 * PLANES] for b in blocks], axis=0)
                for u in range(units)
            ],
            axis=1,
        ).astype(jnp.bfloat16)
        stacks.append(stacked)
    both = dot(wx_ref[...], jnp.concatenate(stacks, axis=1)).astype(jnp.bfloat16)
    for p in range(pairs_here):
        v = both[:, p * units * HALF : (p + 1) * units * HALF]
        cells = [
            jnp.concatenate([v[:rows, k : k + HALF], v[rows:, k : k + HALF]], axis=1)
            for k in range(0, units * HALF, HALF)
        ]
        for part in range(sems.shape[1]):
            of = cells[part * zpart // PLANES : (part + 1) * zpart // PLANES]
            maps = dot(jnp.concatenate(of, axis=0), wy_ref[...])
            maps_ref[p, part * zpart : (part + 1) * zpart] = maps.reshape(zpart, GX, GY)
            leave(p, part).start()
    for p in range(pairs_here):
        for part in range(sems.shape[1]):
            leave(p, part).wait()


def synthesise(returned):
    _, pairs_here, slab_rows, _ = returned.shape
    tables = (inverse_x_table(), half_y_inverse())
    shape = (pairs_here, slab_rows // 2, GX, GY)
    vmem = pl.BlockSpec(memory_space=pltpu.VMEM)
    return pl.pallas_call(
        synthesise_kernel,
        in_specs=[vmem] * (1 + len(tables)),
        out_specs=pl.BlockSpec(memory_space=pl.ANY),
        out_shape=jax.ShapeDtypeStruct(shape, jnp.float32),
        scratch_shapes=[
            pltpu.VMEM(shape, jnp.float32),
            pltpu.SemaphoreType.DMA((pairs_here, slab_rows // (8 * PLANES))),
        ],
        compiler_params=pltpu.CompilerParams(vmem_limit_bytes=VMEM_BYTES),
        name="synthesise",
    )(returned, *(jnp.asarray(t) for t in tables))


ORDER = ("z", "core", "x", "y")


def placed_shards(band, pairs, extents):
    x, y, cores = (lax.axis_size(axis) for axis in ("x", "y", "core"))
    pairs, extents = pairs.T, extents.T
    tile = (lax.axis_index("z") * x + lax.axis_index("x")).astype(jnp.int32)
    device = lax.axis_index(ORDER).astype(jnp.int32)
    spectra = analyse(band, pairs, extents, tile[None])
    spread = lax.all_to_all(spectra, ORDER, split_axis=0, concat_axis=0, tiled=True)
    w = correlate(spread, pairs, device[None], (x, y, cores), band.shape[0])
    returned = lax.all_to_all(w, ORDER, split_axis=0, concat_axis=0, tiled=True)
    return synthesise(returned)


def solution(mesh):
    tiles, slabs = mesh.devices.shape
    cores = 2
    side = max(slabs // cores, 1)
    if tiles * slabs == GX and slabs % cores == 0 and tiles % side == 0:
        over = jax.sharding.Mesh(
            mesh.devices.reshape(tiles // side, side, slabs // cores, cores), ("z", "x", "y", "core")
        )
        tile, slab, body = ("z", "x"), ("y", "core"), placed_shards
    else:
        over, tile, slab, body = mesh, "tile", "zslab", general_shards
    return jax.shard_map(
        body,
        mesh=over,
        in_specs=(P(tile, None, slab, None, None), P(), P()),
        out_specs=P(tile, slab, None, None),
        check_vma=False,
    )
```
